128 devices in a mesh: seq: 16 (over x_hi, z, core), wshard: 8 (over y, x_lo).
Axes of the slice: x: 4 (x_hi: 2, x_lo: 2; x = x_hi * 2 + x_lo), y: 4, z: 4, core: 2. Of those that a mesh axis runs over, the one named last changes fastest.
Arguments:
- tokens: bfloat16 [8, 3584, 1024], P('wshard', 'seq'), may hold values from -6 to 6
- routes: int32 [8, 3584, 8], P('wshard', 'seq'), may hold values from 0 to 31, all different within a row; in each aligned block of 224 rows (0 to 223, 224 to 447, ..., all dimensions but the last counted through in order) at most 70 rows name the same one
- cont_lengths: int32 [8, 6], P('wshard'), may hold values from 1 to 384, 1536 in all within a row
- norm_attn: bfloat16 [1024], P(('seq', 'wshard')), may hold values from 0.3984375 to 1.59375
- w_qkv: bfloat16 [1024, 2048], P(('seq', 'wshard')), may hold values from -0.1875 to 0.1875
- w_out: bfloat16 [1024, 1024], P(('seq', 'wshard')), may hold values from -1.5 to 1.5
- w_router: bfloat16 [1024, 32], P(('seq', 'wshard')), may hold values from -0.09375 to 0.09375
- norm_ffn: bfloat16 [1024], P(('seq', 'wshard')), may hold values from 0.3984375 to 1.59375
- w_gate_up: bfloat16 [32, 1024, 1024], P('seq', 'wshard'), may hold values from -0.1875 to 0.1875
- w_down: bfloat16 [32, 512, 1024], P('seq', 'wshard'), may hold values from -0.75 to 0.75
- cotangent: bfloat16 [8, 3584, 1024], P('wshard', 'seq'), may hold values from -6 to 6
Outputs:
- output: bfloat16 [8, 3584, 1024], P('wshard', 'seq')
- grad_input: float32 [8, 3584, 1024], P('wshard', 'seq')
- grad_norm_attn: float32 [1024], P(('seq', 'wshard'))
- grad_qkv: float32 [1024, 2048], P(('seq', 'wshard'))
- grad_out: float32 [1024, 1024], P(('seq', 'wshard'))
- grad_router: float32 [1024, 32], P(('seq', 'wshard'))
- grad_norm_ffn: float32 [1024], P(('seq', 'wshard'))
- grad_gate_up: float32 [32, 1024, 1024], P('seq', 'wshard')
- grad_down: float32 [32, 512, 1024], P('seq', 'wshard')
The draws below stay inside these ranges and needn't reach their ends.
Inputs may be any that keep to these rules, and one draw needn't show every extreme that they name: `routes`: each row names 8 different experts; in each aligned block of 224 rows (the rows of one device) no expert is named by more than 70 rows, and in some block one expert is named by exactly 70 rows. `cont_lengths`: A group's 6 lengths sum to 1536; the longest is exactly 384.
All inputs are finite; a program needn't handle non-finite values.
Results may differ from the reference program's by a relative error of at most 0.023.
Values may be sent and summed in bfloat16 or wider, within the bound.
No kernel may reach another device: no remote copies, remote signals or barrier semaphores. Data moves between devices by JAX's collectives and lax.ppermute only.
A program may use at most 128 MiB of HBM per device.

```python
import math
import jax
import jax.numpy as jnp
import numpy as np
from jax import lax

D = 1024
HEADS = 16
KV_HEADS = 8
HEAD_DIM = 64
EXPERTS = 32
TOPK = 8
FF = 512
PROMPT = 2048
CONT_LEN = 256
CONTS = 6
CONT_MOST = 384
GROUP = 3584
GROUPS = 8
TOK_DEV = 224
CAP = 70
QDIM = 1024
QKV = 2048
N_SEQ = 16


def levels(key, extent, cuts, smallest, top_value):
    loudness, own = 1.0, jax.random.fold_in(key, 6)
    for dim, blocks in cuts:
        heights = jnp.exp(jax.random.uniform(jax.random.fold_in(own, dim), (blocks,), jnp.float32, smallest / len(cuts), top_value / len(cuts)))
        loudness = loudness * jnp.repeat(heights, extent[dim] // blocks).reshape([-1 if axis == dim else 1 for axis in range(len(extent))])
    return loudness


def length_profile(amount, total, limit, slope):
    portions = [(1 << 20) // math.isqrt(grade ** slope) + 1 for grade in range(2, amount + 1)]
    rest, given = total - limit - (amount - 1), [1] * (amount - 1)
    while rest > 0:
        movable = [i for i in range(amount - 1) if given[i] < limit]
        pool, budget = sum([portions[i] for i in movable]), rest
        for i in movable:
            extra = min(limit - given[i], max(1, budget * portions[i] // pool), rest)
            given[i] = given[i] + extra
            rest = rest - extra
    return np.array([limit] + given)


def uneven(stream_key, amount, total, bound, slope):
    if amount == 2:
        one = jax.random.randint(stream_key, (), max(1, total - bound), min(bound, total - 1) + 1)
        return jnp.stack([one, total - one])
    sizes = jnp.asarray(length_profile(amount, total, bound, slope), jnp.int32)
    couples = (amount - 1) // 2
    donor, taker = sizes[1:1 + 2 * couples:2], sizes[2:2 + 2 * couples:2]
    slack = jnp.minimum(donor - 1, bound - taker)
    shifted = jax.random.randint(jax.random.fold_in(stream_key, 1), (couples,), 0, 1 << 20) % (slack + 1)
    sizes = sizes.at[1:1 + 2 * couples:2].set(donor - shifted).at[2:2 + 2 * couples:2].set(taker + shifted)
    return sizes[jax.random.permutation(jax.random.fold_in(stream_key, 2), amount)]


def assign_block(stream_key, own, number, rows, count, top, limit, lean):
    sequence = jax.random.permutation(stream_key, count)
    heavy_load, common = shares(count, rows * top, limit, lean, True), shares(count, rows * top, limit, lean, False)
    places = jnp.arange(count)

    def named(sizes, rotation):
        used = int((sizes > 0).sum())
        fixed = max(1, used // 4)
        shifted = fixed + (places - fixed + rotation * (used - fixed)) % max(1, count - fixed)
        return jnp.zeros((count,), jnp.int32).at[sequence[jnp.where(places < fixed, places, shifted)]].set(jnp.asarray(sizes, jnp.int32))

    sizes = jnp.where(number % 4 == 0, named(heavy_load, number // 4), named(common, number - number // 4 - 1))
    mixed = jax.random.permutation(jax.random.fold_in(own, 3), count)
    source_of, sink = mixed[0:count // 2 * 2:2], mixed[1:count // 2 * 2:2]
    margin = jnp.minimum(sizes[source_of] - 1, limit - sizes[sink]) // 2
    margin = jnp.where((source_of == sequence[0]) | (sink == sequence[0]) | (sizes[sink] == 0), 0, jnp.maximum(margin, 0))
    shifted = jax.random.randint(jax.random.fold_in(own, 4), (count // 2,), 0, 1 << 20) % (margin + 1)
    sizes = sizes.at[source_of].add(-shifted).at[sink].add(shifted)
    members = jnp.searchsorted(jnp.cumsum(sizes), jnp.arange(rows * top), side="right").astype(jnp.int32)
    table = members.reshape(top, rows).T
    table = table[jax.random.permutation(jax.random.fold_in(own, 1), rows)]
    rotation = jax.random.randint(jax.random.fold_in(own, 2), (rows, 1), 0, top)
    return jnp.take_along_axis(table, (jnp.arange(top)[None, :] + rotation) % top, axis=1)


def shares(count, total, reach, lean, full):
    weights = [(1 << 20) // math.isqrt(rank ** lean) + 1 for rank in range(1, count + 1)]
    largest = reach if full else min(reach, max(-(-total // count), total * weights[0] // sum(weights)))
    least = 1 if total - largest >= count - 1 else 0
    holding, spare = [largest] + [least] * (count - 1), total - largest - least * (count - 1)
    while spare > 0:
        candidates = [i for i in range(1, count) if holding[i] < largest] or [i for i in range(1, count) if holding[i] < reach]
        mass, left = sum([weights[i] for i in candidates]), spare
        for i in candidates:
            addition = min(reach - holding[i], max(1, left * weights[i] // mass), spare)
            holding[i] = holding[i] + addition
            spare = spare - addition
    return np.array(holding)


def gaussian(own_key, dims, width, bound, shards=(), kind=jnp.bfloat16):
    result = width * jax.random.normal(own_key, dims, jnp.float32)
    if shards:
        result = result * levels(own_key, dims, shards, -0.22, 0.18)
    return jnp.clip(result, -bound, bound).astype(kind)


def setup_inputs(seed: int = 0) -> dict:
    splits = jax.random.split(jax.random.key(seed), 12)
    tokens = gaussian(splits[0], (GROUPS, GROUP, D), 1.0, 6.0, ((0, 8), (1, 16)))
    routes_keys = jax.random.split(jax.random.fold_in(splits[1], 1), GROUPS * GROUP // TOK_DEV)
    routes_turns = jax.random.permutation(jax.random.fold_in(splits[1], 3), GROUPS * GROUP // TOK_DEV)
    routes = jax.vmap(lambda own, number: assign_block(jax.random.fold_in(splits[1], 2), own, number, TOK_DEV, EXPERTS, TOPK, CAP, 0))(routes_keys, routes_turns).reshape((GROUPS, GROUP, TOPK))
    cont_lengths = jax.vmap(lambda own: uneven(own, CONTS, CONTS * CONT_LEN, CONT_MOST, 1))(jax.random.split(splits[2], GROUPS)).reshape((GROUPS, CONTS)).astype(jnp.int32)
    norm_attn = jnp.clip(1.0 + 0.12 * jax.random.normal(splits[3], (D,), jnp.float32), 0.3984375, 1.59375).astype(jnp.bfloat16)
    w_qkv = gaussian(splits[4], (D, QKV), D ** -0.5, 0.1875, ((0, 128),))
    w_out = gaussian(splits[5], (QDIM, D), (QDIM // 64) ** -0.5, 1.5, ((0, 128),))
    w_router = gaussian(splits[6], (D, EXPERTS), (4 * D) ** -0.5, 0.09375, ((0, 128),))
    norm_ffn = jnp.clip(1.0 + 0.12 * jax.random.normal(splits[7], (D,), jnp.float32), 0.3984375, 1.59375).astype(jnp.bfloat16)
    w_gate_up = gaussian(splits[8], (EXPERTS, D, 2 * FF), D ** -0.5, 0.1875, ((0, 16), (1, 8)))
    w_down = gaussian(splits[9], (EXPERTS, FF, D), (FF // 8) ** -0.5, 0.75, ((0, 16), (1, 8)))
    cotangent = gaussian(splits[10], (GROUPS, GROUP, D), 1.0, 6.0, ((0, 8), (1, 16)))
    return dict(tokens=tokens, routes=routes, cont_lengths=cont_lengths, norm_attn=norm_attn, w_qkv=w_qkv, w_out=w_out, w_router=w_router, norm_ffn=norm_ffn, w_gate_up=w_gate_up, w_down=w_down, cotangent=cotangent)


@jax.custom_vjp
def low(v):
    return lax.optimization_barrier(v.astype(jnp.bfloat16)).astype(jnp.float32)

@jax.custom_vjp
def low_back(v):
    return v

def low_keep(v):
    return (low(v), None)

def low_pass(kept, grad):
    return (grad,)

def back_keep(v):
    return (v, None)

def back_low(kept, grad):
    return (low(grad),)
low.defvjp(low_keep, low_pass)
low_back.defvjp(back_keep, back_low)
norm_eps = 1e-06
rope_base = 10000.0
masked_score = -1e+30

def rms_norm(values, gain):
    return values * lax.rsqrt(lax.optimization_barrier(jnp.mean(values * values, axis=-1, keepdims=True)) + norm_eps) * gain

def rotary_tables(position):
    half_dim = HEAD_DIM // 2
    inverse = rope_base ** (-(jnp.arange(half_dim, dtype=jnp.float32) * 2.0) / HEAD_DIM)
    angles = position[:, None] * inverse[None, :]
    cosine = jnp.cos(angles)
    sine_table = jnp.sin(angles)
    return (jnp.concatenate([cosine, cosine], axis=-1), jnp.concatenate([sine_table, sine_table], axis=-1))

def rotate(values, cosine, sine_table):
    half_dim = values.shape[-1] // 2
    turned = jnp.concatenate([-values[..., half_dim:], values[..., :half_dim]], axis=-1)
    return values * cosine[:, None, :] + turned * sine_table[:, None, :]

def group_layout(lengths):
    places = jnp.arange(GROUP, dtype=jnp.int32)
    ends = jnp.cumsum(lengths).astype(jnp.int32)
    starts = ends - lengths
    offset_in = places - PROMPT
    segment_id = lax.optimization_barrier(jnp.sum((offset_in[:, None] >= ends[None, :]).astype(jnp.int32), axis=1))
    segment_hot = segment_id[:, None] == jnp.arange(lengths.shape[0], dtype=jnp.int32)[None, :]
    begin = lax.optimization_barrier(jnp.sum(jnp.where(segment_hot, starts[None, :], 0), axis=1)).astype(jnp.int32)
    inside = offset_in >= 0
    position = jnp.where(inside, PROMPT + offset_in - begin, places)
    segment = jnp.where(inside, segment_id, -1)
    return (places, position, segment)

def allowed_mask(query_places, query_segment, places, segment):
    causal = places[None, :] <= query_places[:, None]
    same_doc = (segment[None, :] < 0) | (segment[None, :] == query_segment[:, None])
    return causal & same_doc

def group_forward(tokens_group, lengths, expert_ids, gain_attn, weight_qkv, weight_out, weight_router, gain_ffn, weight_gate_up, weight_down):
    highest = lax.Precision.HIGHEST
    query_width = HEADS * HEAD_DIM
    kv_width = KV_HEADS * HEAD_DIM
    head_share = HEADS // KV_HEADS
    places, position, segment = group_layout(lengths)
    cosine, sine_table = rotary_tables(position.astype(jnp.float32))
    normed = low(rms_norm(tokens_group, gain_attn))
    projected = low_back(jnp.dot(normed, weight_qkv, precision=highest))
    queries = projected[:, :query_width].reshape(GROUP, HEADS, HEAD_DIM)
    keys_part = projected[:, query_width:query_width + kv_width].reshape(GROUP, KV_HEADS, HEAD_DIM)
    values_part = projected[:, query_width + kv_width:].reshape(GROUP, KV_HEADS, HEAD_DIM)
    queries = low(low_back(rotate(queries, cosine, sine_table)))
    keys_wide = low(low_back(jnp.repeat(rotate(keys_part, cosine, sine_table), head_share, axis=1)))
    values_wide = low(low_back(jnp.repeat(values_part, head_share, axis=1)))
    score_scale = HEAD_DIM ** (-0.5)
    block_rows = min(512, GROUP)
    block_count = GROUP // block_rows

    def attend(block_item):
        query_block, query_places, query_segment = block_item
        scores = low_back(jnp.einsum('qhd,khd->hqk', query_block, keys_wide, precision=highest) * score_scale)
        allowed = allowed_mask(query_places, query_segment, places, segment)
        scores = jnp.where(allowed[None], scores, masked_score)
        weights = low(jax.nn.softmax(scores, axis=-1))
        return jnp.einsum('hqk,khd->qhd', weights, values_wide, precision=highest)
    attended = lax.map(jax.checkpoint(attend), (queries.reshape(block_count, block_rows, HEADS, HEAD_DIM), places.reshape(block_count, block_rows), segment.reshape(block_count, block_rows)))
    attended = low(low_back(attended.reshape(GROUP, query_width)))
    branch = low_back(jnp.dot(attended, weight_out, precision=highest))
    hidden = tokens_group + branch
    normed_ffn = low(rms_norm(hidden, gain_ffn))
    logits = low_back(jnp.dot(normed_ffn, weight_router, precision=highest))
    chosen = jnp.take_along_axis(logits, expert_ids, axis=1)
    gate_weights = jax.nn.softmax(chosen, axis=-1)
    expert_flat = expert_ids.reshape(N_SEQ, TOK_DEV * TOPK)
    expert_hot = (expert_flat[:, :, None] == jnp.arange(EXPERTS, dtype=jnp.int32)[None, None, :]).astype(jnp.int32)
    slot_rank = lax.optimization_barrier(jnp.sum((jnp.cumsum(expert_hot, axis=1) - 1) * expert_hot, axis=2))
    slot_index = (expert_flat * (N_SEQ * CAP) + jnp.arange(N_SEQ, dtype=jnp.int32)[:, None] * CAP + slot_rank).reshape(-1).astype(jnp.int32)
    slot_owner = jnp.full((EXPERTS * N_SEQ * CAP,), GROUP * TOPK, jnp.int32).at[slot_index].set(jnp.arange(GROUP * TOPK, dtype=jnp.int32))
    padded = jnp.concatenate([normed_ffn, jnp.zeros((1, D), jnp.float32)], axis=0)
    expert_rows = low_back(padded[slot_owner // TOPK]).reshape(EXPERTS, N_SEQ * CAP, D)
    mixed_rows = low_back(jnp.einsum('erd,edf->erf', expert_rows, weight_gate_up, precision=highest))
    activated = low(jax.nn.silu(mixed_rows[..., :FF]) * mixed_rows[..., FF:])
    returned = low(low_back(jnp.einsum('erf,efd->erd', activated, weight_down, precision=highest)))
    picked = returned.reshape(EXPERTS * N_SEQ * CAP, D)[slot_index].reshape(GROUP, TOPK, D)
    return hidden + lax.optimization_barrier(jnp.sum(gate_weights[..., None] * picked, axis=1))

def reference(tokens, routes, cont_lengths, norm_attn, w_qkv, w_out, w_router, norm_ffn, w_gate_up, w_down, cotangent):

    def forward(inputs, gain_attn, weight_qkv, weight_out, weight_router, gain_ffn, weight_gate_up, weight_down):

        def one_group(group_item):
            tokens_group, lengths, expert_ids = group_item
            return group_forward(tokens_group, lengths, expert_ids, gain_attn, weight_qkv, weight_out, weight_router, gain_ffn, weight_gate_up, weight_down)
        return lax.map(jax.checkpoint(one_group), (inputs, cont_lengths, routes))
    output, pullback = jax.vjp(forward, tokens.astype(jnp.float32), norm_attn.astype(jnp.float32), w_qkv.astype(jnp.float32), w_out.astype(jnp.float32), w_router.astype(jnp.float32), norm_ffn.astype(jnp.float32), w_gate_up.astype(jnp.float32), w_down.astype(jnp.float32))
    gradients = pullback(cotangent.astype(jnp.float32))
    return (output.astype(jnp.bfloat16), gradients[0], gradients[1], gradients[2], gradients[3], gradients[4], gradients[5], gradients[6], gradients[7])
```

```python
import jax
import jax.numpy as jnp
from jax import lax
from jax.sharding import PartitionSpec as P

HEADS = 16
KV_HEADS = 8
HEAD_DIM = 64
EXPERTS = 32
TOPK = 8
FF = 512
PROMPT = 2048
GROUP = 3584
TOK = 224
WIDTH = 1024
SLOTS = 72
N_SEQ = 16

norm_eps = 1e-06
rope_base = 10000.0
masked_score = -1e30
BOTH = ("seq", "wshard")
f32 = jnp.float32
bf16 = jnp.bfloat16


def place_of(x, z, core):
    return x * 8 + z * 2 + core


def shift_perm(a, b):
    return [
        (place_of(x, z, c), place_of(x ^ a, (z + b) % 4, c))
        for x in range(2)
        for z in range(4)
        for c in range(2)
    ]


CORE_PERM = [(i, i ^ 1) for i in range(16)]
CHIPS = [(a, b) for a in range(2) for b in range(4)]


def relative_places(seq_index):
    x, z, c = seq_index // 8, (seq_index // 2) % 4, seq_index % 2
    r = jnp.arange(16, dtype=jnp.int32)
    a, b, k = r // 8, (r // 2) % 4, r % 2
    forward = (a ^ x) * 8 + ((z - b) % 4) * 2 + (k ^ c)
    inverse = (a ^ x) * 8 + ((z - b) % 4) * 2 + (k ^ c)
    return forward, inverse


def seq_gather(rows):
    parts = []
    for a, b in CHIPS:
        got = rows if (a, b) == (0, 0) else lax.ppermute(rows, "seq", shift_perm(a, b))
        parts.append(got)
        parts.append(lax.ppermute(got, "seq", CORE_PERM))
    return jnp.stack(parts)


def seq_scatter_sum(blocks):
    paired = blocks.reshape(8, 2, *blocks.shape[1:])
    mine = paired[:, 0]
    other = lax.ppermute(paired[:, 1], "seq", CORE_PERM)
    chip = (mine.astype(f32) + other.astype(f32)).astype(bf16)
    total = chip[0].astype(f32)
    for i, (a, b) in enumerate(CHIPS):
        if i == 0:
            continue
        total = total + lax.ppermute(chip[i], "seq", shift_perm(a, -b)).astype(f32)
    return total


def inverse_rms(values):
    return lax.rsqrt(jnp.mean(values * values, axis=-1, keepdims=True) + norm_eps)


def rms_pull(values, scale, gain, grad):
    scaled = grad * gain
    return scale * scaled - values * (scale * scale * scale) * jnp.mean(
        scaled * values, axis=-1, keepdims=True
    )


def group_layout(lengths):
    places = jnp.arange(GROUP, dtype=jnp.int32)
    ends = jnp.cumsum(lengths)
    starts = ends - lengths
    offset_in = places - PROMPT
    segment_id = jnp.sum((offset_in[:, None] >= ends[None, :]).astype(jnp.int32), axis=1)
    segment_hot = segment_id[:, None] == jnp.arange(lengths.shape[0], dtype=jnp.int32)[None, :]
    begin = jnp.sum(jnp.where(segment_hot, starts[None, :], 0), axis=1)
    inside = offset_in >= 0
    position = jnp.where(inside, PROMPT + offset_in - begin, places)
    segment = jnp.where(inside, segment_id, -1)
    return (places, position, segment)


def rotary_tables(position):
    half_dim = HEAD_DIM // 2
    inverse = rope_base ** (-(jnp.arange(half_dim, dtype=f32) * 2.0) / HEAD_DIM)
    angles = position[:, None] * inverse[None, :]
    cosine, sine = jnp.cos(angles), jnp.sin(angles)
    return (
        jnp.concatenate([cosine, cosine], axis=-1),
        jnp.concatenate([sine, sine], axis=-1),
    )


def turn(values):
    half_dim = HEAD_DIM // 2
    return jnp.concatenate([-values[..., half_dim:], values[..., :half_dim]], axis=-1)


def turn_back(values):
    half_dim = HEAD_DIM // 2
    return jnp.concatenate([values[..., half_dim:], -values[..., :half_dim]], axis=-1)


def allowed_mask(query_places, query_segment, places, segment):
    causal = places[None, :] <= query_places[:, None]
    same_doc = (segment[None, :] < 0) | (segment[None, :] == query_segment[:, None])
    return causal & same_doc


def attention_forward(q, k, v, places, segment):
    rows = 512
    def block(offset):
        qb = lax.dynamic_slice_in_dim(q, offset, rows, 0)
        query_segment = lax.dynamic_slice_in_dim(segment, offset, rows, 0)
        raw = jnp.einsum("qd,kd->qk", qb, k, preferred_element_type=f32) * HEAD_DIM**-0.5
        allowed = allowed_mask(offset + jnp.arange(rows), query_segment, places, segment)
        scores = jnp.where(allowed, raw, masked_score)
        peak = jnp.max(scores, axis=-1, keepdims=True)
        exponent = jnp.exp(scores - peak)
        total = jnp.sum(exponent, axis=-1, keepdims=True)
        weights = (exponent / total).astype(bf16)
        out = jnp.einsum("qk,kd->qd", weights, v, preferred_element_type=f32)
        return out, peak, total

    offsets = jnp.arange(GROUP // rows, dtype=jnp.int32) * rows
    out, peak, total = lax.map(block, offsets)
    return out.reshape(GROUP, HEAD_DIM), (peak, total)


def attention_backward(q, k, v, attended, stats, grad, places, segment):
    rows = 512
    def block(running, item):
        keys_grad, values_grad = running
        offset, peak, total = item
        qb = lax.dynamic_slice_in_dim(q, offset, rows, 0)
        gb = lax.dynamic_slice_in_dim(grad, offset, rows, 0)
        query_segment = lax.dynamic_slice_in_dim(segment, offset, rows, 0)
        raw = jnp.einsum("qd,kd->qk", qb, k, preferred_element_type=f32) * HEAD_DIM**-0.5
        allowed = allowed_mask(offset + jnp.arange(rows), query_segment, places, segment)
        scores = jnp.where(allowed, raw, masked_score)
        weights = jnp.exp(scores - peak) / total
        wgrad = jnp.einsum("qd,kd->qk", gb, v, preferred_element_type=f32)
        inner = jnp.sum(weights * wgrad, axis=-1, keepdims=True)
        sgrad = (weights * (wgrad - inner)).astype(bf16)
        qgrad = jnp.einsum("qk,kd->qd", sgrad, k, preferred_element_type=f32) * HEAD_DIM**-0.5
        keys_grad = keys_grad + jnp.einsum(
            "qk,qd->kd", sgrad, qb, preferred_element_type=f32
        ) * HEAD_DIM**-0.5
        values_grad = values_grad + jnp.einsum(
            "qk,qd->kd", weights.astype(bf16), gb, preferred_element_type=f32
        )
        return (keys_grad, values_grad), qgrad

    zero = jnp.zeros((GROUP, HEAD_DIM), f32)
    offsets = jnp.arange(GROUP // rows, dtype=jnp.int32) * rows
    (keys_grad, values_grad), qgrad = lax.scan(block, (zero, zero), (offsets, *stats))
    return qgrad.reshape(GROUP, HEAD_DIM), keys_grad, values_grad


def local(
    tokens,
    routes,
    cont_lengths,
    norm_attn,
    w_qkv,
    w_out,
    w_router,
    norm_ffn,
    w_gate_up,
    w_down,
    cotangent,
):
    seq_index = lax.axis_index("seq")
    relative, inverse = relative_places(seq_index)
    rows = tokens[0]
    query_width = HEADS * HEAD_DIM
    kv_width = KV_HEADS * HEAD_DIM

    rows_all = seq_gather(rows)
    head_cols = jnp.concatenate(
        [
            w_qkv[:, :query_width].reshape(8, HEADS, HEAD_DIM),
            jnp.repeat(w_qkv[:, query_width : query_width + kv_width].reshape(8, KV_HEADS, HEAD_DIM), 2, axis=1),
            jnp.repeat(w_qkv[:, query_width + kv_width :].reshape(8, KV_HEADS, HEAD_DIM), 2, axis=1),
            jnp.broadcast_to(norm_attn[:, None, None], (8, HEADS, HEAD_DIM)),
        ],
        axis=2,
    ).transpose(1, 0, 2)
    head_cols = jnp.broadcast_to(head_cols[:, None], (HEADS, 8, 8, 256)).reshape(128, 8, 256)
    head_weights = lax.all_to_all(head_cols, BOTH, 0, 0, tiled=True).reshape(WIDTH, 256)
    weight_head = head_weights[:, :192]
    gain_attn = head_weights[:, 192].astype(f32)

    shared = jnp.concatenate(
        [w_out, w_router, norm_ffn[:, None], jnp.zeros((8, 95), bf16)], axis=1
    )
    shared = lax.all_gather(shared, "wshard", axis=0, tiled=True)
    shared = lax.all_gather(shared, "seq", axis=0, tiled=True)
    weight_out = shared[:, :WIDTH]
    weight_router = shared[:, WIDTH : WIDTH + EXPERTS]
    gain_ffn = shared[:, WIDTH + EXPERTS].astype(f32)

    expert_rows = jnp.concatenate([w_gate_up, w_down], axis=1)
    experts = lax.all_gather(expert_rows, "wshard", axis=0).transpose(1, 0, 2, 3)
    weight_gate_up = experts[:, :, :128].reshape(2, WIDTH, 2 * FF)
    weight_down = experts[:, :, 128:].reshape(2, FF, WIDTH)

    routes_all = jnp.take(lax.all_gather(routes[0], "seq", axis=0), relative, axis=0)
    places, position, segment = group_layout(cont_lengths[0])
    cosine, sine = rotary_tables(position.astype(f32))

    inputs_all = rows_all.astype(f32)
    normed_all = (inputs_all * inverse_rms(inputs_all) * gain_attn).astype(bf16)
    projected = jnp.einsum("btd,df->btf", normed_all, weight_head, preferred_element_type=f32)
    projected = jnp.take(projected, inverse, axis=0).reshape(GROUP, 192)
    q, k, v = projected[:, :64], projected[:, 64:128], projected[:, 128:]
    q = (q * cosine + turn(q) * sine).astype(bf16)
    k = (k * cosine + turn(k) * sine).astype(bf16)
    v = v.astype(bf16)

    attended_head, stats = attention_forward(q, k, v, places, segment)
    attended = lax.all_to_all(
        attended_head.astype(bf16).reshape(16, TOK, HEAD_DIM), "seq", 0, 0, tiled=True
    )
    attended = attended.transpose(1, 0, 2).reshape(TOK, query_width)
    inputs = rows.astype(f32)
    hidden = inputs + jnp.dot(attended, weight_out, preferred_element_type=f32)
    hidden_scale = inverse_rms(hidden)
    normed_ffn = (hidden * hidden_scale * gain_ffn).astype(bf16)

    grad_all = seq_gather(cotangent[0])
    ffn_all = seq_gather(normed_ffn)
    expert_range = jnp.arange(EXPERTS, dtype=jnp.int32)
    chosen = jnp.any(routes_all[..., None] == expert_range, axis=2)
    logits = jnp.einsum("btd,de->bte", ffn_all, weight_router, preferred_element_type=f32)
    peak = jnp.max(jnp.where(chosen, logits, -jnp.inf), axis=-1, keepdims=True)
    raised = jnp.where(chosen, jnp.exp(logits - peak), 0.0)
    gates_all = raised / jnp.sum(raised, axis=-1, keepdims=True)
    gates = gates_all[0]
    chosen_own = lax.dynamic_slice_in_dim(chosen, seq_index * 2, 2, 2).transpose(0, 2, 1)
    gates_own = lax.dynamic_slice_in_dim(gates_all, seq_index * 2, 2, 2).transpose(0, 2, 1)
    rank = jnp.cumsum(chosen_own.astype(jnp.int32), axis=2) - 1
    slot = jnp.arange(SLOTS, dtype=jnp.int32)
    picks = chosen_own[:, :, None, :] & (rank[:, :, None, :] == slot[None, None, :, None])
    slot_gates = jnp.sum(jnp.where(picks, gates_own[:, :, None, :], 0.0), axis=3)
    slot_gates = slot_gates.transpose(1, 0, 2).reshape(2, 16 * SLOTS, 1)
    picks = picks.astype(bf16)

    expert_in = jnp.einsum(
        "best,btd->ebsd", picks, ffn_all, preferred_element_type=f32
    ).astype(bf16).reshape(2, 16 * SLOTS, WIDTH)
    expert_grad = jnp.einsum(
        "best,btd->ebsd", picks, grad_all, preferred_element_type=f32
    ).reshape(2, 16 * SLOTS, WIDTH)
    returned_grad = (slot_gates * expert_grad).astype(bf16)
    mixed = jnp.einsum("erd,edf->erf", expert_in, weight_gate_up, preferred_element_type=f32)
    gate_part, up_part = mixed[..., :FF], mixed[..., FF:]
    sigma = jax.nn.sigmoid(gate_part)
    silu = gate_part * sigma
    activated = (silu * up_part).astype(bf16)
    returned = jnp.einsum(
        "erf,efd->erd", activated, weight_down, preferred_element_type=f32
    ).astype(bf16).astype(f32)
    gate_grad = jnp.sum(returned * expert_grad, axis=-1).reshape(2, 16, SLOTS)
    act_grad = jnp.einsum("erd,efd->erf", returned_grad, weight_down, preferred_element_type=f32)
    mixed_grad = jnp.concatenate(
        [act_grad * up_part * (sigma + silu * (1.0 - sigma)), act_grad * silu], axis=-1
    ).astype(bf16)
    rows_grad = jnp.einsum(
        "erf,edf->erd", mixed_grad, weight_gate_up, preferred_element_type=f32
    ).astype(bf16)
    grad_down = jnp.einsum("erf,erd->efd", activated, returned_grad, preferred_element_type=f32)
    grad_gate_up = jnp.einsum("erd,erf->edf", expert_in, mixed_grad, preferred_element_type=f32)

    routed_part = jnp.einsum(
        "best,ebsd->btd",
        picks,
        rows_grad.reshape(2, 16, SLOTS, WIDTH),
        preferred_element_type=f32,
    ).astype(bf16)
    token_gate_grad = jnp.sum(
        picks.astype(f32) * gate_grad.transpose(1, 0, 2)[..., None], axis=2
    )
    gate_grad_own = lax.all_to_all(
        jnp.take(token_gate_grad, inverse, axis=0), "seq", 0, 0, tiled=True
    ).reshape(EXPERTS, TOK).T
    routed_grad = seq_scatter_sum(routed_part)

    expert_grads = jnp.concatenate(
        [grad_gate_up.reshape(2, 8, 128, 1024), grad_down.reshape(2, 8, 64, 1024)], axis=2
    ).astype(bf16).reshape(2, 8 * 192, 1024)
    expert_grads = lax.psum_scatter(
        expert_grads, "wshard", scatter_dimension=1, tiled=True
    ).astype(f32)

    chosen_grad = gates * (gate_grad_own - jnp.sum(gates * gate_grad_own, axis=-1, keepdims=True))
    logit_grad = chosen_grad.astype(bf16)
    normed_ffn_grad = routed_grad + jnp.einsum(
        "te,de->td", logit_grad, weight_router, preferred_element_type=f32
    )
    grad_router = jnp.einsum("td,te->de", normed_ffn, logit_grad, preferred_element_type=f32)
    upstream = cotangent[0].astype(f32)
    grad_norm_ffn = jnp.sum(normed_ffn_grad * hidden * hidden_scale, axis=0)
    hidden_grad = upstream + rms_pull(hidden, hidden_scale, gain_ffn, normed_ffn_grad)
    branch_grad = hidden_grad.astype(bf16)
    attended_grad = jnp.einsum(
        "td,qd->tq", branch_grad, weight_out, preferred_element_type=f32
    ).astype(bf16)
    head_grad = lax.all_to_all(
        attended_grad.reshape(TOK, HEADS, HEAD_DIM).transpose(1, 0, 2), "seq", 0, 0, tiled=True
    ).reshape(GROUP, HEAD_DIM)

    grad_out = jnp.einsum("tq,td->qd", attended, branch_grad, preferred_element_type=f32)
    shared_grads = jnp.concatenate(
        [grad_out, grad_router, grad_norm_ffn[:, None], jnp.zeros((WIDTH, 95), f32)], axis=1
    ).astype(bf16)
    shared_grads = jnp.sum(
        lax.all_to_all(shared_grads.reshape(128, 8, 1152), BOTH, 0, 0, tiled=True).astype(f32),
        axis=0,
    )

    moved_part = jnp.einsum(
        "best,ebsd->btd",
        picks,
        (slot_gates * returned).astype(bf16).reshape(2, 16, SLOTS, WIDTH),
        preferred_element_type=f32,
    ).astype(bf16)
    output = (hidden + seq_scatter_sum(moved_part)).astype(bf16)

    dq, dk, dv = attention_backward(q, k, v, attended_head, stats, head_grad, places, segment)
    dq = dq.astype(bf16).astype(f32)
    dk = dk.astype(bf16).astype(f32)
    projected_grad = jnp.concatenate(
        [dq * cosine + turn_back(dq * sine), dk * cosine + turn_back(dk * sine), dv], axis=1
    ).astype(bf16)
    projected_grad = jnp.take(projected_grad.reshape(16, TOK, 192), relative, axis=0)
    normed_part = jnp.einsum(
        "btf,df->btd", projected_grad, weight_head, preferred_element_type=f32
    ).astype(bf16)
    normed_grad = seq_scatter_sum(normed_part)
    grad_head = jnp.einsum(
        "btd,btf->df", normed_all, projected_grad, preferred_element_type=f32
    ).astype(bf16)
    grad_heads = jnp.sum(
        lax.all_to_all(grad_head.reshape(128, 8, 192), BOTH, 0, 0, tiled=True)
        .reshape(16, 8, 8, 192)
        .astype(f32),
        axis=1,
    ).transpose(1, 0, 2)
    grad_qkv = jnp.concatenate(
        [
            grad_heads[:, :, :64].reshape(8, query_width),
            jnp.sum(grad_heads[:, :, 64:128].reshape(8, KV_HEADS, 2, 64), axis=2).reshape(8, kv_width),
            jnp.sum(grad_heads[:, :, 128:].reshape(8, KV_HEADS, 2, 64), axis=2).reshape(8, kv_width),
        ],
        axis=1,
    )
    grad_norm_attn = jnp.sum(grad_qkv * w_qkv.astype(f32), axis=1) / norm_attn.astype(f32)
    grad_input = hidden_grad + rms_pull(inputs, inverse_rms(inputs), gain_attn, normed_grad)
    return (
        output[None],
        grad_input[None],
        grad_norm_attn,
        grad_qkv,
        shared_grads[:, :WIDTH],
        shared_grads[:, WIDTH : WIDTH + EXPERTS],
        shared_grads[:, WIDTH + EXPERTS],
        expert_grads[:, :128],
        expert_grads[:, 128:],
    )


def solution(mesh):
    return jax.shard_map(
        local,
        mesh=mesh,
        in_specs=(
            P("wshard", "seq", None),
            P("wshard", "seq", None),
            P("wshard", None),
            P(BOTH),
            P(BOTH, None),
            P(BOTH, None),
            P(BOTH, None),
            P(BOTH),
            P("seq", "wshard", None),
            P("seq", "wshard", None),
            P("wshard", "seq", None),
        ),
        out_specs=(
            P("wshard", "seq", None),
            P("wshard", "seq", None),
            P(BOTH),
            P(BOTH, None),
            P(BOTH, None),
            P(BOTH, None),
            P(BOTH),
            P("seq", "wshard", None),
            P("seq", "wshard", None),
        ),
        check_vma=False,
    )
```

```python
import jax
import jax.numpy as jnp
from jax import lax
from jax.experimental import pallas as pl
from jax.experimental.pallas import tpu as pltpu
from jax.sharding import PartitionSpec as P

HEADS = 16
KV_HEADS = 8
HEAD_DIM = 64
EXPERTS = 32
FF = 512
PROMPT = 2048
GROUP = 3584
TOK = 224
HALF = TOK // 2
WIDTH = 1024
SLOTS = 72
STEP_ROWS = 4 * SLOTS
ALL_ROWS = 16 * SLOTS
BLOCK = 512

norm_eps = 1e-06
rope_base = 10000.0
masked_score = -1e30
BOTH = ("seq", "wshard")
NT = (((1,), (1,)), ((), ()))
TN = (((0,), (0,)), ((), ()))
f32 = jnp.float32
bf16 = jnp.bfloat16
i32 = jnp.int32


def place_of(x, z, core):
    return x * 8 + z * 2 + core


def shift_perm(a, b):
    return [
        (place_of(x, z, c), place_of(x ^ a, (z + b) % 4, c))
        for x in range(2)
        for z in range(4)
        for c in range(2)
    ]


CORE_PERM = [(i, i ^ 1) for i in range(16)]


def send(rows, a, b):
    return lax.ppermute(rows, "seq", shift_perm(a, b))


def swap_cores(rows):
    return lax.ppermute(rows, "seq", CORE_PERM)


def relative_places(seq_index):
    x, z, c = seq_index // 8, (seq_index // 2) % 4, seq_index % 2
    r = jnp.arange(16, dtype=i32)
    a, b, k = r // 8, (r // 2) % 4, r % 2
    return (a ^ x) * 8 + ((z - b) % 4) * 2 + (k ^ c)


def seq_gather(rows):
    near = [rows, send(rows, 0, 1), send(rows, 0, 2), send(rows, 0, 3)]
    across = send(rows, 1, 0)
    mine_near = jnp.stack(near)
    tops = [send(near[b][:HALF], 1, 0) for b in (1, 2, 3)]
    bottoms = [send(across[HALF:], 0, b) for b in (1, 2, 3)]
    far = [across] + [jnp.concatenate([t, u], axis=0) for t, u in zip(tops, bottoms)]
    mine_far = jnp.stack(far)
    return (mine_near, swap_cores(mine_near)), (mine_far, swap_cores(mine_far))


def add_low(*terms):
    return sum([t.astype(f32) for t in terms]).astype(bf16)


def seq_scatter_sum(near, far):
    near_other = swap_cores(near[1])
    far_other = swap_cores(far[1])
    own_near = [(near[0][b], near_other[b]) for b in range(4)]
    own_far = [(far[0][b], far_other[b]) for b in range(4)]
    low = slice(HALF, TOK)
    top = slice(0, HALF)
    near_low = [send(add_low(own_near[b][0][low], own_near[b][1][low]), 0, -b) for b in (1, 2, 3)]
    tops_far = add_low(far[0][:, top], far_other[:, top])
    tops_got = send(tops_far, 1, 0)
    far_low = [send(add_low(own_far[b][0][low], own_far[b][1][low]), 0, -b) for b in (1, 2, 3)]
    crossed = send(add_low(own_far[0][0][low], own_far[0][1][low], *far_low), 1, 0)
    tops = [
        send(add_low(own_near[b][0][top], own_near[b][1][top], tops_got[b]), 0, -b)
        for b in (1, 2, 3)
    ]
    own = [own_near[0][0].astype(f32), own_near[0][1].astype(f32)]
    upper = sum([t.astype(f32) for t in tops], own[0][top] + own[1][top] + tops_got[0].astype(f32))
    lower = sum([t.astype(f32) for t in near_low], own[0][low] + own[1][low] + crossed.astype(f32))
    return jnp.concatenate([upper, lower], axis=0)


def inverse_rms(values):
    return lax.rsqrt(jnp.mean(values * values, axis=-1, keepdims=True) + norm_eps)


def rms_pull(values, scale, gain, grad):
    scaled = grad * gain
    return scale * scaled - values * (scale * scale * scale) * jnp.mean(
        scaled * values, axis=-1, keepdims=True
    )


def group_layout(lengths):
    places = jnp.arange(GROUP, dtype=i32)
    ends = jnp.cumsum(lengths)
    starts = ends - lengths
    offset_in = places - PROMPT
    segment_id = jnp.sum((offset_in[:, None] >= ends[None, :]).astype(i32), axis=1)
    segment_hot = segment_id[:, None] == jnp.arange(lengths.shape[0], dtype=i32)[None, :]
    begin = jnp.sum(jnp.where(segment_hot, starts[None, :], 0), axis=1)
    inside = offset_in >= 0
    position = jnp.where(inside, PROMPT + offset_in - begin, places)
    return position, jnp.where(inside, PROMPT + begin, 0)


def rotary_tables(position):
    half_dim = HEAD_DIM // 2
    inverse = rope_base ** (-(jnp.arange(half_dim, dtype=f32) * 2.0) / HEAD_DIM)
    angles = position[:, None] * inverse[None, :]
    cosine, sine = jnp.cos(angles), jnp.sin(angles)
    return (
        jnp.concatenate([cosine, cosine], axis=-1),
        jnp.concatenate([sine, sine], axis=-1),
    )


def turn(values):
    half_dim = HEAD_DIM // 2
    return jnp.concatenate([-values[:, half_dim:], values[:, :half_dim]], axis=-1)


def turn_back(values):
    half_dim = HEAD_DIM // 2
    return jnp.concatenate([values[:, half_dim:], -values[:, :half_dim]], axis=-1)


def project_kernel(places, mine, other, w, gain, cosine, sine, *refs):
    del places
    normed_ref, q_ref, k_ref, v_ref = refs[-4:]
    rows = jnp.where(pl.program_id(1) == 0, mine[0], other[0])
    values = rows.astype(f32)
    normed = (values * inverse_rms(values) * gain[...]).astype(bf16)
    normed_ref[0] = normed
    projected = jnp.dot(normed, w[...], preferred_element_type=f32)
    c, s = cosine[...], sine[...]
    q, k, v = projected[:, :64], projected[:, 64:128], projected[:, 128:192]
    q_ref[...] = ((q * c + turn(q) * s).astype(bf16).astype(f32) * HEAD_DIM**-0.5).astype(bf16)
    k_ref[...] = (k * c + turn(k) * s).astype(bf16)
    v_ref[...] = v.astype(bf16)


def project(places, gathered, w, gain, cosine, sine, before):
    chip = pl.BlockSpec((1, TOK, WIDTH), lambda j, k, p: (j, 0, 0))
    whole = lambda shape: pl.BlockSpec(shape, lambda j, k, p: (0,) * len(shape))
    at = pl.BlockSpec((TOK, HEAD_DIM), lambda j, k, p: (p[2 * j + k], 0))
    table = jax.ShapeDtypeStruct((GROUP, HEAD_DIM), bf16)
    return pl.pallas_call(
        project_kernel,
        grid_spec=pltpu.PrefetchScalarGridSpec(
            num_scalar_prefetch=1,
            grid=(4, 2),
            in_specs=[chip, chip, whole((WIDTH, 256)), whole((1, WIDTH)), at, at]
            + [pl.BlockSpec(memory_space=pl.ANY)] * len(before),
            out_specs=[pl.BlockSpec((1, TOK, WIDTH), lambda j, k, p: (2 * j + k, 0, 0)), at, at, at],
        ),
        out_shape=[jax.ShapeDtypeStruct((8, TOK, WIDTH), bf16), table, table, table],
        input_output_aliases={7 + i: 1 + i for i in range(len(before))},
        compiler_params=pltpu.CompilerParams(vmem_limit_bytes=32 << 20),
        cost_estimate=pl.CostEstimate(
            flops=2 * 8 * TOK * WIDTH * 256, bytes_accessed=10 << 20, transcendentals=0
        ),
    )(places, *gathered, w, gain, cosine, sine, *before)


def project_back_kernel(places, normed, dq, dk, dv, w, cosine, sine, *refs):
    del places
    mine, other, grad = refs[-3:]
    first = (pl.program_id(0) == 0) & (pl.program_id(1) == 0)

    @pl.when(first)
    def _():
        grad[...] = jnp.zeros_like(grad) if len(refs) == 3 else refs[0][...]

    c, s = cosine[...], sine[...]
    q = dq[...].astype(bf16).astype(f32)
    k = dk[...].astype(bf16).astype(f32)
    projected = jnp.concatenate(
        [q * c + turn_back(q * s), k * c + turn_back(k * s), dv[...], jnp.zeros_like(q)], axis=1
    ).astype(bf16)
    grad[...] += lax.dot_general(normed[0], projected, TN, preferred_element_type=f32)
    part = lax.dot_general(projected, w[...], NT, preferred_element_type=f32).astype(bf16)

    @pl.when(pl.program_id(1) == 0)
    def _():
        mine[0] = part

    @pl.when(pl.program_id(1) == 1)
    def _():
        other[0] = part


def project_back(places, normed, grads, w, cosine, sine, before):
    chip = pl.BlockSpec((1, TOK, WIDTH), lambda j, k, p: (j, 0, 0))
    whole = lambda shape: pl.BlockSpec(shape, lambda j, k, p: (0,) * len(shape))
    at = pl.BlockSpec((TOK, HEAD_DIM), lambda j, k, p: (p[2 * j + k], 0))
    part = jax.ShapeDtypeStruct((4, TOK, WIDTH), bf16)
    return pl.pallas_call(
        project_back_kernel,
        grid_spec=pltpu.PrefetchScalarGridSpec(
            num_scalar_prefetch=1,
            grid=(4, 2),
            in_specs=[
                pl.BlockSpec((1, TOK, WIDTH), lambda j, k, p: (2 * j + k, 0, 0)),
                at,
                at,
                at,
                whole((WIDTH, 256)),
                at,
                at,
            ]
            + [whole((WIDTH, 256))] * len(before),
            out_specs=[chip, chip, whole((WIDTH, 256))],
        ),
        out_shape=[part, part, jax.ShapeDtypeStruct((WIDTH, 256), f32)],
        compiler_params=pltpu.CompilerParams(vmem_limit_bytes=32 << 20),
        cost_estimate=pl.CostEstimate(
            flops=4 * 8 * TOK * WIDTH * 256, bytes_accessed=12 << 20, transcendentals=0
        ),
    )(places, normed, *grads, w, cosine, sine, *before)


def tile_mask(scores, key_start, query_start, begin):
    keys = key_start + lax.broadcasted_iota(i32, scores.shape, 0)
    queries = query_start + lax.broadcasted_iota(i32, scores.shape, 1)
    return jnp.where((keys <= queries) & (keys >= begin), scores, masked_score)


def key_ranges(i):
    first = PROMPT // BLOCK
    return jnp.where(i > first, i - 1, i), jnp.minimum(i, first)


def attend_kernel(q_ref, k_ref, v_ref, begin_ref, o_ref, ot_ref, lse_ref, vt):
    i = pl.program_id(0)

    @pl.when(i == 0)
    def _():
        vt[...] = v_ref[...].T

    q = q_ref[...]
    begin = begin_ref[...]

    def tile(j, carry, masked):
        peak, total, out = carry
        start = pl.multiple_of(j * BLOCK, BLOCK)
        at = pl.ds(start, BLOCK)
        s = lax.dot_general(k_ref[at, :], q, NT, preferred_element_type=f32)
        if masked:
            s = tile_mask(s, start, i * BLOCK, begin)
        higher = jnp.maximum(peak, jnp.max(s, axis=0, keepdims=True))
        p = jnp.exp(s - higher)
        fade = jnp.exp(peak - higher)
        total = total * fade + jnp.sum(p, axis=0, keepdims=True)
        out = out * fade + jnp.dot(vt[:, at], p.astype(bf16), preferred_element_type=f32)
        return higher, total, out

    carry = (
        jnp.full((1, BLOCK), masked_score, f32),
        jnp.zeros((1, BLOCK), f32),
        jnp.zeros((HEAD_DIM, BLOCK), f32),
    )
    carry = tile(i, carry, True)
    window, shared = key_ranges(i)
    carry = lax.fori_loop(window, i, lambda j, c: tile(j, c, True), carry)
    peak, total, out = lax.fori_loop(0, shared, lambda j, c: tile(j, c, False), carry)
    out = out * (1.0 / total)
    ot_ref[...] = out
    o_ref[...] = out.T.astype(bf16)
    lse_ref[...] = peak + jnp.log(total)


def attend(q, k, v, begin):
    whole = pl.BlockSpec((GROUP, HEAD_DIM), lambda i: (0, 0))
    rows = pl.BlockSpec((BLOCK, HEAD_DIM), lambda i: (i, 0))
    cols = lambda n: pl.BlockSpec((n, BLOCK), lambda i: (0, i))
    return pl.pallas_call(
        attend_kernel,
        grid=(GROUP // BLOCK,),
        in_specs=[rows, whole, whole, cols(1)],
        out_specs=[rows, cols(HEAD_DIM), cols(1)],
        out_shape=[
            jax.ShapeDtypeStruct((GROUP, HEAD_DIM), bf16),
            jax.ShapeDtypeStruct((HEAD_DIM, GROUP), f32),
            jax.ShapeDtypeStruct((1, GROUP), f32),
        ],
        scratch_shapes=[pltpu.VMEM((HEAD_DIM, GROUP), bf16)],
        compiler_params=pltpu.CompilerParams(vmem_limit_bytes=32 << 20),
        cost_estimate=pl.CostEstimate(
            flops=2 * 27 * BLOCK * BLOCK * 512, bytes_accessed=4 << 20, transcendentals=27 * BLOCK * BLOCK
        ),
    )(q, k, v, begin)


def attend_back_kernel(
    q_ref, k_ref, v_ref, g_ref, ot_ref, lse_ref, begin_ref, dq_ref, dk_ref, dv_ref, kt
):
    i = pl.program_id(0)

    @pl.when(i == 0)
    def _():
        dk_ref[...] = jnp.zeros_like(dk_ref)
        dv_ref[...] = jnp.zeros_like(dv_ref)
        kt[...] = k_ref[...].T

    q = q_ref[...]
    g = g_ref[...]
    begin = begin_ref[...]
    lse = lse_ref[...]
    inner = jnp.sum(g.T.astype(f32) * ot_ref[...], axis=0, keepdims=True)

    def tile(j, dq, masked):
        start = pl.multiple_of(j * BLOCK, BLOCK)
        at = pl.ds(start, BLOCK)
        s = lax.dot_general(k_ref[at, :], q, NT, preferred_element_type=f32)
        if masked:
            s = tile_mask(s, start, i * BLOCK, begin)
        p = jnp.exp(s - lse)
        dp = lax.dot_general(v_ref[at, :], g, NT, preferred_element_type=f32)
        ds = (p * (dp - inner)).astype(bf16)
        dv_ref[at, :] += jnp.dot(p.astype(bf16), g, preferred_element_type=f32)
        dk_ref[at, :] += jnp.dot(ds, q, preferred_element_type=f32)
        return dq + jnp.dot(kt[:, at], ds, preferred_element_type=f32)

    dq = tile(i, jnp.zeros((HEAD_DIM, BLOCK), f32), True)
    window, shared = key_ranges(i)
    dq = lax.fori_loop(window, i, lambda j, c: tile(j, c, True), dq)
    dq = lax.fori_loop(0, shared, lambda j, c: tile(j, c, False), dq)
    dq_ref[...] = dq.T * HEAD_DIM**-0.5


def attend_back(q, k, v, g, ot, lse, begin):
    whole = pl.BlockSpec((GROUP, HEAD_DIM), lambda i: (0, 0))
    rows = pl.BlockSpec((BLOCK, HEAD_DIM), lambda i: (i, 0))
    cols = lambda n: pl.BlockSpec((n, BLOCK), lambda i: (0, i))
    out = jax.ShapeDtypeStruct((GROUP, HEAD_DIM), f32)
    return pl.pallas_call(
        attend_back_kernel,
        grid=(GROUP // BLOCK,),
        in_specs=[rows, whole, whole, rows, cols(HEAD_DIM), cols(1), cols(1)],
        out_specs=[rows, whole, whole],
        out_shape=[out, out, out],
        scratch_shapes=[pltpu.VMEM((HEAD_DIM, GROUP), bf16)],
        compiler_params=pltpu.CompilerParams(vmem_limit_bytes=48 << 20),
        cost_estimate=pl.CostEstimate(
            flops=5 * 27 * BLOCK * BLOCK * 512, bytes_accessed=8 << 20, transcendentals=27 * BLOCK * BLOCK
        ),
    )(q, k, v, g, ot, lse, begin)


def experts_kernel(
    own_ref, ffn_mine, ffn_other, g_mine, g_other, w_ref, router_ref, chosen_ref, slots_ref, slot_cols_ref, *refs
):
    routed_mine, routed_other, moved_mine, moved_other, gate_grad_ref = refs[-9:-4]
    x_ref, dh_ref, act_ref, dy_ref = refs[-4:]
    own = own_ref[0]
    expert_rows = lax.broadcasted_iota(i32, (EXPERTS, TOK), 0)
    slot_rows = lax.broadcasted_iota(i32, (SLOTS, TOK), 0)
    gate_rows = [[], []]
    picks = [[], []]
    picked_rows = [[], []]
    picked_grads = [[], []]
    blocks = [(ffn_mine, g_mine, 0), (ffn_other, g_other, 0), (ffn_mine, g_mine, 1), (ffn_other, g_other, 1)]
    for b, (rows_ref, grads_ref, n) in enumerate(blocks):
        rows, grads = rows_ref[n], grads_ref[n]
        chosen = chosen_ref[b] > 0
        logits = lax.dot_general(router_ref[...], rows, NT, preferred_element_type=f32)
        peak = jnp.max(jnp.where(chosen, logits, masked_score), axis=0, keepdims=True)
        raised = jnp.where(chosen, jnp.exp(jnp.minimum(logits - peak, 0.0)), 0.0)
        gates = raised / jnp.sum(raised, axis=0, keepdims=True)
        for e in range(2):
            gate_rows[e].append(
                jnp.sum(jnp.where(expert_rows == own + e, gates, 0.0), axis=0, keepdims=True)
            )
            pick = (slots_ref[b, e : e + 1, :] == slot_rows).astype(f32)
            picks[e].append(pick)
            low = pick.astype(bf16)
            picked_rows[e].append(jnp.dot(low, rows, preferred_element_type=f32))
            picked_grads[e].append(jnp.dot(low, grads, preferred_element_type=f32))
    moved, routed = [], []
    for e in range(2):
        w_gate_up = w_ref[:, e, :128, :].reshape(WIDTH, 2 * FF)
        w_down = w_ref[:, e, 128:, :].reshape(FF, WIDTH)
        x = jnp.concatenate(picked_rows[e], axis=0).astype(bf16)
        gate = jnp.concatenate(
            [jnp.sum(p * r, axis=1, keepdims=True) for p, r in zip(picks[e], gate_rows[e])], axis=0
        )
        grads = jnp.concatenate(picked_grads[e], axis=0)
        dy = (gate * grads).astype(bf16)
        mixed = jnp.dot(x, w_gate_up, preferred_element_type=f32)
        dact = lax.dot_general(dy, w_down, NT, preferred_element_type=f32)
        gate_part, up_part = mixed[:, :FF], mixed[:, FF:]
        sigma = 1.0 / (1.0 + jnp.exp(-gate_part))
        silu = gate_part * sigma
        act = (silu * up_part).astype(bf16)
        dh = jnp.concatenate(
            [dact * up_part * (sigma + silu * (1.0 - sigma)), dact * silu], axis=1
        ).astype(bf16)
        x_ref[e] = x
        dy_ref[e] = dy
        act_ref[e] = act
        dh_ref[e] = dh
        returned = jnp.dot(act, w_down, preferred_element_type=f32).astype(bf16).astype(f32)
        dgate = jnp.sum(returned * grads, axis=1, keepdims=True)
        for b in range(4):
            gate_grad_ref[b, e : e + 1, :] = jnp.sum(
                picks[e][b] * dgate[b * SLOTS : (b + 1) * SLOTS], axis=0, keepdims=True
            )
        moved.append(gate * returned)
        routed.append(lax.dot_general(dh, w_gate_up, NT, preferred_element_type=f32))
    columns = lax.broadcasted_iota(i32, (TOK, 2 * SLOTS), 1)
    outs = [(routed_mine, moved_mine, 0), (routed_other, moved_other, 0), (routed_mine, moved_mine, 1), (routed_other, moved_other, 1)]
    for b, (routed_ref, moved_ref, n) in enumerate(outs):
        first, second = slot_cols_ref[b, :, 0:1], slot_cols_ref[b, :, 1:2]
        back = ((columns == first) | ((columns == second + SLOTS) & (second >= 0))).astype(f32).astype(bf16)
        at = slice(b * SLOTS, (b + 1) * SLOTS)
        for terms, ref in ((routed, routed_ref), (moved, moved_ref)):
            joined = jnp.concatenate([terms[0][at], terms[1][at]], axis=0).astype(bf16)
            ref[n] = jnp.dot(back, joined, preferred_element_type=f32).astype(bf16)


def run_experts(half, own, ffn, grads, weights, router, chosen, slots, slot_cols, before):
    pair = pl.BlockSpec((2, TOK, WIDTH), lambda i, o: (i, 0, 0))
    whole = lambda shape: pl.BlockSpec(shape, lambda i, o: (0,) * len(shape))
    four = lambda *shape: pl.BlockSpec((4, *shape), lambda i, o: (i + 2 * half, 0, 0))
    kept = lambda n: pl.BlockSpec((2, STEP_ROWS, n), lambda i, o: (0, i + 2 * half, 0))
    part = jax.ShapeDtypeStruct((4, TOK, WIDTH), bf16)
    keep = lambda n: jax.ShapeDtypeStruct((2, ALL_ROWS, n), bf16)
    return pl.pallas_call(
        experts_kernel,
        grid_spec=pltpu.PrefetchScalarGridSpec(
            num_scalar_prefetch=1,
            grid=(2,),
            in_specs=[
                pair,
                pair,
                pair,
                pair,
                whole((8, 2, 192, 1024)),
                whole((EXPERTS, WIDTH)),
                four(EXPERTS, TOK),
                four(2, TOK),
                four(TOK, 2),
            ]
            + [pl.BlockSpec(memory_space=pl.ANY)] * len(before),
            out_specs=[
                pair,
                pair,
                pair,
                pair,
                pl.BlockSpec((4, 2, TOK), lambda i, o: (i, 0, 0)),
                kept(WIDTH),
                kept(2 * FF),
                kept(FF),
                kept(WIDTH),
            ],
        ),
        out_shape=[
            part,
            part,
            part,
            part,
            jax.ShapeDtypeStruct((8, 2, TOK), f32),
            keep(WIDTH),
            keep(2 * FF),
            keep(FF),
            keep(WIDTH),
        ],
        input_output_aliases={10 + i: 5 + i for i in range(len(before))},
        compiler_params=pltpu.CompilerParams(vmem_limit_bytes=60 << 20),
        cost_estimate=pl.CostEstimate(
            flops=14 << 30, bytes_accessed=24 << 20, transcendentals=8 * SLOTS * 2 * FF
        ),
    )(own, *ffn, *grads, weights, router, chosen, slots, slot_cols, *before)


def expert_grads_kernel(x_ref, dh_ref, act_ref, dy_ref, out_ref):
    up = lax.dot_general(x_ref[0], dh_ref[0], TN, preferred_element_type=f32)
    down = lax.dot_general(act_ref[0], dy_ref[0], TN, preferred_element_type=f32)
    out_ref[:, 0, :128, :] = up.astype(bf16).reshape(2, 128, 2 * FF)
    out_ref[:, 0, 128:, :] = down.astype(bf16).reshape(2, 64, WIDTH)


def expert_weight_grads(x, dh, act, dy):
    return pl.pallas_call(
        expert_grads_kernel,
        grid=(2, 4),
        in_specs=[
            pl.BlockSpec((1, ALL_ROWS, 256), lambda e, i: (e, 0, i)),
            pl.BlockSpec((1, ALL_ROWS, 2 * FF), lambda e, i: (e, 0, 0)),
            pl.BlockSpec((1, ALL_ROWS, 128), lambda e, i: (e, 0, i)),
            pl.BlockSpec((1, ALL_ROWS, WIDTH), lambda e, i: (e, 0, 0)),
        ],
        out_specs=pl.BlockSpec((2, 1, 192, 1024), lambda e, i: (i, e, 0, 0)),
        out_shape=jax.ShapeDtypeStruct((8, 2, 192, 1024), bf16),
        compiler_params=pltpu.CompilerParams(vmem_limit_bytes=48 << 20),
        cost_estimate=pl.CostEstimate(flops=8 << 30, bytes_accessed=14 << 20, transcendentals=0),
    )(x, dh, act, dy)


def local(
    tokens,
    routes,
    cont_lengths,
    norm_attn,
    w_qkv,
    w_out,
    w_router,
    norm_ffn,
    w_gate_up,
    w_down,
    cotangent,
):
    seq_index = lax.axis_index("seq")
    places = relative_places(seq_index)
    rows = tokens[0]
    query_width = HEADS * HEAD_DIM
    kv_width = KV_HEADS * HEAD_DIM

    rows_all = seq_gather(rows)
    kv_heads = lambda start: jnp.repeat(
        w_qkv[:, start : start + kv_width].reshape(8, KV_HEADS, HEAD_DIM), 2, axis=1
    )
    head_cols = jnp.concatenate(
        [
            w_qkv[:, :query_width].reshape(8, HEADS, HEAD_DIM),
            kv_heads(query_width),
            kv_heads(query_width + kv_width),
            jnp.broadcast_to(norm_attn[:, None, None], (8, HEADS, HEAD_DIM)),
        ],
        axis=2,
    ).transpose(1, 0, 2)
    head_cols = jnp.broadcast_to(head_cols[:, None], (HEADS, 8, 8, 256)).reshape(128, 8, 256)
    head_weights = lax.all_to_all(head_cols, BOTH, 0, 0, tiled=True).reshape(WIDTH, 256)
    gain_attn = head_weights[:, 192].astype(f32)[None]
    head_weights = jnp.where(jnp.arange(256)[None] < 192, head_weights, 0.0).astype(bf16)

    routes_t = jnp.broadcast_to(routes[0].T[None], (16, 8, TOK))
    routes_all = jnp.take(lax.all_to_all(routes_t, "seq", 0, 0, tiled=True), places, axis=0)

    shared = jnp.concatenate(
        [w_out, w_router, norm_ffn[:, None], jnp.zeros((8, 95), bf16)], axis=1
    )
    shared = lax.all_to_all(
        jnp.broadcast_to(shared[None], (128, 8, 1152)), BOTH, 0, 0, tiled=True
    ).reshape(WIDTH, 1152)
    weight_out = shared[:, :WIDTH]
    weight_router = shared[:, WIDTH : WIDTH + EXPERTS]
    gain_ffn = shared[:, WIDTH + EXPERTS].astype(f32)

    expert_rows = jnp.concatenate([w_gate_up, w_down], axis=1)
    experts = lax.all_to_all(
        jnp.broadcast_to(expert_rows[None], (8, 2, 192, 1024)), "wshard", 0, 0, tiled=True
    )

    position, begin = group_layout(cont_lengths[0])
    begin = begin[None]
    cosine, sine = rotary_tables(position.astype(f32))

    expert_range = jnp.arange(EXPERTS, dtype=i32)
    chosen = jnp.any(routes_all[:, None] == expert_range[None, :, None, None], axis=2)
    own_first = seq_index * 2
    chosen_own = jnp.any(
        routes_all[:, None] == (own_first + jnp.arange(2, dtype=i32))[None, :, None, None], axis=2
    )
    upto = (jnp.arange(TOK)[:, None] <= jnp.arange(TOK)[None, :]).astype(bf16)
    rank = jnp.einsum("bet,tu->beu", chosen_own.astype(bf16), upto, preferred_element_type=f32)
    slots = jnp.where(chosen_own, rank.astype(i32) - 1, -1)
    slot_cols = slots.transpose(0, 2, 1)
    chosen = chosen.astype(f32)

    normed_near, *qkv = project(places[:8], rows_all[0], head_weights, gain_attn, cosine, sine, ())
    normed_far, q, k, v = project(places[8:], rows_all[1], head_weights, gain_attn, cosine, sine, qkv)
    attended_head, attended_t, lse = attend(q, k, v, begin)
    attended = lax.all_to_all(attended_head.reshape(16, TOK, HEAD_DIM), "seq", 0, 0, tiled=True)
    attended = attended.transpose(1, 0, 2).reshape(TOK, query_width)
    inputs = rows.astype(f32)
    hidden = inputs + jnp.dot(attended, weight_out, preferred_element_type=f32)
    hidden_scale = inverse_rms(hidden)
    normed_ffn = (hidden * hidden_scale * gain_ffn).astype(bf16)

    grad_all = seq_gather(cotangent[0])
    ffn_all = seq_gather(normed_ffn)
    router_t = weight_router.T
    own = own_first[None]
    near = run_experts(
        0, own, ffn_all[0], grad_all[0], experts, router_t, chosen, slots, slot_cols, ()
    )
    far = run_experts(
        1, own, ffn_all[1], grad_all[1], experts, router_t, chosen, slots, slot_cols, near[5:]
    )
    routed_grad = seq_scatter_sum(near[:2], far[:2])
    token_gate_grad = jnp.take(jnp.concatenate([near[4], far[4]], axis=0), places, axis=0)
    gate_grad = lax.all_to_all(token_gate_grad, "seq", 0, 0, tiled=True).reshape(EXPERTS, TOK).T
    expert_grads = lax.all_to_all(expert_weight_grads(*far[5:]), "wshard", 0, 0, tiled=True)
    expert_grads = jnp.sum(expert_grads.astype(f32), axis=0)

    chosen_here = jnp.any(routes[0][:, :, None] == expert_range, axis=1)
    logits = jnp.dot(normed_ffn, weight_router, preferred_element_type=f32)
    peak = jnp.max(jnp.where(chosen_here, logits, -jnp.inf), axis=-1, keepdims=True)
    raised = jnp.where(chosen_here, jnp.exp(logits - peak), 0.0)
    gates = raised / jnp.sum(raised, axis=-1, keepdims=True)
    chosen_grad = gates * (gate_grad - jnp.sum(gates * gate_grad, axis=-1, keepdims=True))
    logit_grad = chosen_grad.astype(bf16)
    normed_ffn_grad = routed_grad + jnp.einsum(
        "te,de->td", logit_grad, weight_router, preferred_element_type=f32
    )
    upstream = cotangent[0].astype(f32)
    hidden_grad = upstream + rms_pull(hidden, hidden_scale, gain_ffn, normed_ffn_grad)
    branch_grad = hidden_grad.astype(bf16)
    attended_grad = jnp.einsum(
        "td,qd->tq", branch_grad, weight_out, preferred_element_type=f32
    ).astype(bf16)
    head_grad = lax.all_to_all(
        attended_grad.reshape(TOK, HEADS, HEAD_DIM).transpose(1, 0, 2), "seq", 0, 0, tiled=True
    ).reshape(GROUP, HEAD_DIM)

    grad_router = jnp.einsum("td,te->de", normed_ffn, logit_grad, preferred_element_type=f32)
    grad_norm_ffn = jnp.sum(normed_ffn_grad * hidden * hidden_scale, axis=0)
    grad_out = jnp.einsum("tq,td->qd", attended, branch_grad, preferred_element_type=f32)
    shared_grads = jnp.concatenate(
        [grad_out, grad_router, grad_norm_ffn[:, None], jnp.zeros((WIDTH, 95), f32)], axis=1
    ).astype(bf16)
    shared_grads = jnp.sum(
        lax.all_to_all(shared_grads.reshape(128, 8, 1152), BOTH, 0, 0, tiled=True).astype(f32),
        axis=0,
    )
    output = (hidden + seq_scatter_sum(near[2:4], far[2:4])).astype(bf16)

    grads = attend_back(q, k, v, head_grad, attended_t, lse, begin)
    *near_part, grad_head = project_back(
        places[:8], normed_near, grads, head_weights, cosine, sine, ()
    )
    *far_part, grad_head = project_back(
        places[8:], normed_far, grads, head_weights, cosine, sine, (grad_head,)
    )
    normed_grad = seq_scatter_sum(near_part, far_part)
    grad_heads = jnp.sum(
        lax.all_to_all(grad_head.astype(bf16).reshape(128, 8, 256), BOTH, 0, 0, tiled=True)
        .reshape(16, 8, 8, 256)
        .astype(f32),
        axis=1,
    ).transpose(1, 0, 2)
    kv_sum = lambda start: jnp.sum(
        grad_heads[:, :, start : start + HEAD_DIM].reshape(8, KV_HEADS, 2, HEAD_DIM), axis=2
    ).reshape(8, kv_width)
    grad_qkv = jnp.concatenate(
        [grad_heads[:, :, :HEAD_DIM].reshape(8, query_width), kv_sum(HEAD_DIM), kv_sum(2 * HEAD_DIM)],
        axis=1,
    )
    grad_norm_attn = jnp.sum(grad_qkv * w_qkv.astype(f32), axis=1) / norm_attn.astype(f32)
    grad_input = hidden_grad + rms_pull(inputs, inverse_rms(inputs), gain_attn, normed_grad)
    return (
        output[None],
        grad_input[None],
        grad_norm_attn,
        grad_qkv,
        shared_grads[:, :WIDTH],
        shared_grads[:, WIDTH : WIDTH + EXPERTS],
        shared_grads[:, WIDTH + EXPERTS],
        expert_grads[:, :128],
        expert_grads[:, 128:],
    )


def solution(mesh):
    return jax.shard_map(
        local,
        mesh=mesh,
        in_specs=(
            P("wshard", "seq", None),
            P("wshard", "seq", None),
            P("wshard", None),
            P(BOTH),
            P(BOTH, None),
            P(BOTH, None),
            P(BOTH, None),
            P(BOTH),
            P("seq", "wshard", None),
            P("seq", "wshard", None),
            P("wshard", "seq", None),
        ),
        out_specs=(
            P("wshard", "seq", None),
            P("wshard", "seq", None),
            P(BOTH),
            P(BOTH, None),
            P(BOTH, None),
            P(BOTH, None),
            P(BOTH),
            P("seq", "wshard", None),
            P("seq", "wshard", None),
        ),
        check_vma=False,
    )
```

```python
import jax
import jax.numpy as jnp
from jax import lax
from jax.experimental import pallas as pl
from jax.experimental.pallas import tpu as pltpu
from jax.sharding import PartitionSpec as P

HEADS = 16
KV_HEADS = 8
HEAD_DIM = 64
EXPERTS = 32
FF = 512
PROMPT = 2048
GROUP = 3584
TOK = 224
WIDTH = 1024
SLOTS = 72
STEP_ROWS = 4 * SLOTS
ALL_ROWS = 16 * SLOTS
BLOCK = 512

norm_eps = 1e-06
rope_base = 10000.0
masked_score = -1e30
BOTH = ("seq", "wshard")
NT = (((1,), (1,)), ((), ()))
TN = (((0,), (0,)), ((), ()))
f32 = jnp.float32
bf16 = jnp.bfloat16
i32 = jnp.int32


def place_of(x, z, core):
    return x * 8 + z * 2 + core


def shift_perm(a, b):
    return [
        (place_of(x, z, c), place_of(x ^ a, (z + b) % 4, c))
        for x in range(2)
        for z in range(4)
        for c in range(2)
    ]


CORE_PERM = [(i, i ^ 1) for i in range(16)]


def send(rows, a, b):
    return lax.ppermute(rows, "seq", shift_perm(a, b))


def swap_cores(rows):
    return lax.ppermute(rows, "seq", CORE_PERM)


def relative_places(seq_index):
    x, z, c = seq_index // 8, (seq_index // 2) % 4, seq_index % 2
    r = jnp.arange(16, dtype=i32)
    a, b, k = r // 8, (r // 2) % 4, r % 2
    return (a ^ x) * 8 + ((z - b) % 4) * 2 + (k ^ c)


def seq_gather(rows):
    across = send(rows, 1, 0)
    near = jnp.stack([rows] + [send(rows, 0, b) for b in (1, 2, 3)])
    far = jnp.stack([across] + [send(across, 0, b) for b in (1, 2, 3)])
    return (near, swap_cores(near)), (far, swap_cores(far))


def add_low(*terms):
    return sum([t.astype(f32) for t in terms]).astype(bf16)


def seq_gather_by_x(rows):
    near = jnp.stack([rows] + [send(rows, 0, b) for b in (1, 2, 3)])
    far = send(near, 1, 0)
    return (near, swap_cores(near)), (far, swap_cores(far))


def seq_sum_by_x(near, far):
    got = swap_cores(far[1])
    crossed = send(add_low(far[0], got), 1, 0)
    got = swap_cores(near[1])
    parts = [add_low(near[0][b], got[b], crossed[b]) for b in range(4)]
    return sum([t.astype(f32) for t in [parts[0]] + [send(parts[b], 0, -b) for b in (1, 2, 3)]])


def sum_along_z(mine, other):
    got = swap_cores(other)
    parts = [add_low(mine[b], got[b]) for b in range(4)]
    return [parts[0]] + [send(parts[b], 0, -b) for b in (1, 2, 3)]


def sum_across(near_terms, far_terms):
    crossed = send(add_low(*far_terms), 1, 0)
    return sum([t.astype(f32) for t in near_terms]) + crossed.astype(f32)


def tie(*values):
    return lax.optimization_barrier(values)


def inverse_rms(values):
    return lax.rsqrt(jnp.mean(values * values, axis=-1, keepdims=True) + norm_eps)


def rms_pull(values, scale, gain, grad):
    scaled = grad * gain
    return scale * scaled - values * (scale * scale * scale) * jnp.mean(
        scaled * values, axis=-1, keepdims=True
    )


def group_layout(lengths):
    places = jnp.arange(GROUP, dtype=i32)
    ends = jnp.cumsum(lengths)
    starts = ends - lengths
    offset_in = places - PROMPT
    segment_id = jnp.sum((offset_in[:, None] >= ends[None, :]).astype(i32), axis=1)
    segment_hot = segment_id[:, None] == jnp.arange(lengths.shape[0], dtype=i32)[None, :]
    begin = jnp.sum(jnp.where(segment_hot, starts[None, :], 0), axis=1)
    inside = offset_in >= 0
    position = jnp.where(inside, PROMPT + offset_in - begin, places)
    return position, jnp.where(inside, PROMPT + begin, 0)


def rotary_tables(position):
    half_dim = HEAD_DIM // 2
    inverse = rope_base ** (-(jnp.arange(half_dim, dtype=f32) * 2.0) / HEAD_DIM)
    angles = position[:, None] * inverse[None, :]
    cosine, sine = jnp.cos(angles), jnp.sin(angles)
    return (
        jnp.concatenate([cosine, cosine], axis=-1),
        jnp.concatenate([sine, sine], axis=-1),
    )


def turn(values):
    half_dim = HEAD_DIM // 2
    return jnp.concatenate([-values[:, half_dim:], values[:, :half_dim]], axis=-1)


def turn_back(values):
    half_dim = HEAD_DIM // 2
    return jnp.concatenate([values[:, half_dim:], -values[:, :half_dim]], axis=-1)


def project_kernel(places, mine, other, w, gain, cosine, sine, *refs):
    del places
    normed_ref, q_ref, k_ref, v_ref = refs[-4:]
    rows = jnp.where(pl.program_id(1) == 0, mine[0], other[0])
    values = rows.astype(f32)
    normed = (values * inverse_rms(values) * gain[...]).astype(bf16)
    normed_ref[0] = normed
    projected = jnp.dot(normed, w[...], preferred_element_type=f32)
    c, s = cosine[...], sine[...]
    q, k, v = projected[:, :64], projected[:, 64:128], projected[:, 128:192]
    q_ref[...] = ((q * c + turn(q) * s).astype(bf16).astype(f32) * HEAD_DIM**-0.5).astype(bf16)
    k_ref[...] = (k * c + turn(k) * s).astype(bf16)
    v_ref[...] = v.astype(bf16)


def project(places, gathered, w, gain, cosine, sine, before):
    chip = pl.BlockSpec((1, TOK, WIDTH), lambda j, k, p: (j, 0, 0))
    whole = lambda shape: pl.BlockSpec(shape, lambda j, k, p: (0,) * len(shape))
    at = pl.BlockSpec((TOK, HEAD_DIM), lambda j, k, p: (p[2 * j + k], 0))
    table = jax.ShapeDtypeStruct((GROUP, HEAD_DIM), bf16)
    return pl.pallas_call(
        project_kernel,
        grid_spec=pltpu.PrefetchScalarGridSpec(
            num_scalar_prefetch=1,
            grid=(4, 2),
            in_specs=[chip, chip, whole((WIDTH, 256)), whole((1, WIDTH)), at, at]
            + [pl.BlockSpec(memory_space=pl.ANY)] * len(before),
            out_specs=[pl.BlockSpec((1, TOK, WIDTH), lambda j, k, p: (2 * j + k, 0, 0)), at, at, at],
        ),
        out_shape=[jax.ShapeDtypeStruct((8, TOK, WIDTH), bf16), table, table, table],
        input_output_aliases={7 + i: 1 + i for i in range(len(before))},
        compiler_params=pltpu.CompilerParams(vmem_limit_bytes=32 << 20),
        cost_estimate=pl.CostEstimate(
            flops=2 * 8 * TOK * WIDTH * 256, bytes_accessed=10 << 20, transcendentals=0
        ),
    )(places, *gathered, w, gain, cosine, sine, *before)


def project_back_kernel(places, normed, dq, dk, dv, w, cosine, sine, *refs):
    del places
    mine, other, grad = refs[-3:]
    first = (pl.program_id(0) == 0) & (pl.program_id(1) == 0)

    @pl.when(first)
    def _():
        grad[...] = jnp.zeros_like(grad) if len(refs) == 3 else refs[0][...]

    c, s = cosine[...], sine[...]
    q = dq[...].astype(bf16).astype(f32)
    k = dk[...].astype(bf16).astype(f32)
    projected = jnp.concatenate(
        [q * c + turn_back(q * s), k * c + turn_back(k * s), dv[...], jnp.zeros_like(q)], axis=1
    ).astype(bf16)
    grad[...] += lax.dot_general(normed[0], projected, TN, preferred_element_type=f32)
    part = lax.dot_general(projected, w[...], NT, preferred_element_type=f32).astype(bf16)

    @pl.when(pl.program_id(1) == 0)
    def _():
        mine[0] = part

    @pl.when(pl.program_id(1) == 1)
    def _():
        other[0] = part


def project_back(places, normed, grads, w, cosine, sine, before):
    chip = pl.BlockSpec((1, TOK, WIDTH), lambda j, k, p: (j, 0, 0))
    whole = lambda shape: pl.BlockSpec(shape, lambda j, k, p: (0,) * len(shape))
    at = pl.BlockSpec((TOK, HEAD_DIM), lambda j, k, p: (p[2 * j + k], 0))
    part = jax.ShapeDtypeStruct((4, TOK, WIDTH), bf16)
    return pl.pallas_call(
        project_back_kernel,
        grid_spec=pltpu.PrefetchScalarGridSpec(
            num_scalar_prefetch=1,
            grid=(4, 2),
            in_specs=[
                pl.BlockSpec((1, TOK, WIDTH), lambda j, k, p: (2 * j + k, 0, 0)),
                at,
                at,
                at,
                whole((WIDTH, 256)),
                at,
                at,
            ]
            + [whole((WIDTH, 256))] * len(before),
            out_specs=[chip, chip, whole((WIDTH, 256))],
        ),
        out_shape=[part, part, jax.ShapeDtypeStruct((WIDTH, 256), f32)],
        compiler_params=pltpu.CompilerParams(vmem_limit_bytes=32 << 20),
        cost_estimate=pl.CostEstimate(
            flops=4 * 8 * TOK * WIDTH * 256, bytes_accessed=12 << 20, transcendentals=0
        ),
    )(places, normed, *grads, w, cosine, sine, *before)


def tile_mask(scores, key_start, query_start, begin):
    keys = key_start + lax.broadcasted_iota(i32, scores.shape, 0)
    queries = query_start + lax.broadcasted_iota(i32, scores.shape, 1)
    return jnp.where((keys <= queries) & (keys >= begin), scores, masked_score)


def key_ranges(i):
    first = PROMPT // BLOCK
    return jnp.where(i > first, i - 1, i), jnp.minimum(i, first)


def attend_kernel(q_ref, k_ref, v_ref, begin_ref, o_ref, ot_ref, lse_ref, vt):
    i = pl.program_id(0)

    @pl.when(i == 0)
    def _():
        vt[...] = v_ref[...].T

    q = q_ref[...]
    begin = begin_ref[...]

    def tile(j, carry, masked):
        peak, total, out = carry
        start = pl.multiple_of(j * BLOCK, BLOCK)
        at = pl.ds(start, BLOCK)
        s = lax.dot_general(k_ref[at, :], q, NT, preferred_element_type=f32)
        if masked:
            s = tile_mask(s, start, i * BLOCK, begin)
        higher = jnp.maximum(peak, jnp.max(s, axis=0, keepdims=True))
        p = jnp.exp(s - higher)
        fade = jnp.exp(peak - higher)
        total = total * fade + jnp.sum(p, axis=0, keepdims=True)
        out = out * fade + jnp.dot(vt[:, at], p.astype(bf16), preferred_element_type=f32)
        return higher, total, out

    carry = (
        jnp.full((1, BLOCK), masked_score, f32),
        jnp.zeros((1, BLOCK), f32),
        jnp.zeros((HEAD_DIM, BLOCK), f32),
    )
    carry = tile(i, carry, True)
    window, shared = key_ranges(i)
    carry = lax.fori_loop(window, i, lambda j, c: tile(j, c, True), carry)
    peak, total, out = lax.fori_loop(0, shared, lambda j, c: tile(j, c, False), carry)
    out = out * (1.0 / total)
    ot_ref[...] = out
    o_ref[...] = out.T.astype(bf16)
    lse_ref[...] = peak + jnp.log(total)


def attend(q, k, v, begin):
    whole = pl.BlockSpec((GROUP, HEAD_DIM), lambda i: (0, 0))
    rows = pl.BlockSpec((BLOCK, HEAD_DIM), lambda i: (i, 0))
    cols = lambda n: pl.BlockSpec((n, BLOCK), lambda i: (0, i))
    return pl.pallas_call(
        attend_kernel,
        grid=(GROUP // BLOCK,),
        in_specs=[rows, whole, whole, cols(1)],
        out_specs=[rows, cols(HEAD_DIM), cols(1)],
        out_shape=[
            jax.ShapeDtypeStruct((GROUP, HEAD_DIM), bf16),
            jax.ShapeDtypeStruct((HEAD_DIM, GROUP), f32),
            jax.ShapeDtypeStruct((1, GROUP), f32),
        ],
        scratch_shapes=[pltpu.VMEM((HEAD_DIM, GROUP), bf16)],
        compiler_params=pltpu.CompilerParams(vmem_limit_bytes=32 << 20),
        cost_estimate=pl.CostEstimate(
            flops=2 * 27 * BLOCK * BLOCK * 512, bytes_accessed=4 << 20, transcendentals=27 * BLOCK * BLOCK
        ),
    )(q, k, v, begin)


def attend_back_kernel(
    q_ref, k_ref, v_ref, g_ref, ot_ref, lse_ref, begin_ref, dq_ref, dk_ref, dv_ref, kt
):
    i = pl.program_id(0)

    @pl.when(i == 0)
    def _():
        dk_ref[...] = jnp.zeros_like(dk_ref)
        dv_ref[...] = jnp.zeros_like(dv_ref)
        kt[...] = k_ref[...].T

    q = q_ref[...]
    g = g_ref[...]
    begin = begin_ref[...]
    lse = lse_ref[...]
    inner = jnp.sum(g.T.astype(f32) * ot_ref[...], axis=0, keepdims=True)

    def tile(j, dq, masked):
        start = pl.multiple_of(j * BLOCK, BLOCK)
        at = pl.ds(start, BLOCK)
        s = lax.dot_general(k_ref[at, :], q, NT, preferred_element_type=f32)
        if masked:
            s = tile_mask(s, start, i * BLOCK, begin)
        p = jnp.exp(s - lse)
        dp = lax.dot_general(v_ref[at, :], g, NT, preferred_element_type=f32)
        ds = (p * (dp - inner)).astype(bf16)
        dv_ref[at, :] += jnp.dot(p.astype(bf16), g, preferred_element_type=f32)
        dk_ref[at, :] += jnp.dot(ds, q, preferred_element_type=f32)
        return dq + jnp.dot(kt[:, at], ds, preferred_element_type=f32)

    dq = tile(i, jnp.zeros((HEAD_DIM, BLOCK), f32), True)
    window, shared = key_ranges(i)
    dq = lax.fori_loop(window, i, lambda j, c: tile(j, c, True), dq)
    dq = lax.fori_loop(0, shared, lambda j, c: tile(j, c, False), dq)
    dq_ref[...] = dq.T * HEAD_DIM**-0.5


def attend_back(q, k, v, g, ot, lse, begin):
    whole = pl.BlockSpec((GROUP, HEAD_DIM), lambda i: (0, 0))
    rows = pl.BlockSpec((BLOCK, HEAD_DIM), lambda i: (i, 0))
    cols = lambda n: pl.BlockSpec((n, BLOCK), lambda i: (0, i))
    out = jax.ShapeDtypeStruct((GROUP, HEAD_DIM), f32)
    return pl.pallas_call(
        attend_back_kernel,
        grid=(GROUP // BLOCK,),
        in_specs=[rows, whole, whole, rows, cols(HEAD_DIM), cols(1), cols(1)],
        out_specs=[rows, whole, whole],
        out_shape=[out, out, out],
        scratch_shapes=[pltpu.VMEM((HEAD_DIM, GROUP), bf16)],
        compiler_params=pltpu.CompilerParams(vmem_limit_bytes=48 << 20),
        cost_estimate=pl.CostEstimate(
            flops=5 * 27 * BLOCK * BLOCK * 512, bytes_accessed=8 << 20, transcendentals=27 * BLOCK * BLOCK
        ),
    )(q, k, v, g, ot, lse, begin)


def experts_kernel(
    own_ref, ffn_mine, ffn_other, g_mine, g_other, w_ref, router_ref, chosen_ref, slots_ref, slot_cols_ref, *refs
):
    routed_mine, routed_other, moved_mine, moved_other, gate_grad_ref = refs[-9:-4]
    x_ref, dh_ref, act_ref, dy_ref = refs[-4:]
    own = own_ref[0]
    expert_rows = lax.broadcasted_iota(i32, (EXPERTS, TOK), 0)
    slot_rows = lax.broadcasted_iota(i32, (SLOTS, TOK), 0)
    gate_rows = [[], []]
    picks = [[], []]
    picked_rows = [[], []]
    picked_grads = [[], []]
    blocks = [(ffn_mine, g_mine, 0), (ffn_other, g_other, 0), (ffn_mine, g_mine, 1), (ffn_other, g_other, 1)]
    for b, (rows_ref, grads_ref, n) in enumerate(blocks):
        rows, grads = rows_ref[n], grads_ref[n]
        chosen = chosen_ref[b] > 0
        logits = lax.dot_general(router_ref[...], rows, NT, preferred_element_type=f32)
        peak = jnp.max(jnp.where(chosen, logits, masked_score), axis=0, keepdims=True)
        raised = jnp.where(chosen, jnp.exp(jnp.minimum(logits - peak, 0.0)), 0.0)
        gates = raised / jnp.sum(raised, axis=0, keepdims=True)
        for e in range(2):
            gate_rows[e].append(
                jnp.sum(jnp.where(expert_rows == own + e, gates, 0.0), axis=0, keepdims=True)
            )
            pick = (slots_ref[b, e : e + 1, :] == slot_rows).astype(f32)
            picks[e].append(pick)
            low = pick.astype(bf16)
            picked_rows[e].append(jnp.dot(low, rows, preferred_element_type=f32))
            picked_grads[e].append(jnp.dot(low, grads, preferred_element_type=f32))
    moved, routed = [], []
    for e in range(2):
        w_gate_up = w_ref[e, :, :128, :].reshape(WIDTH, 2 * FF)
        w_down = w_ref[e, :, 128:, :].reshape(FF, WIDTH)
        x = jnp.concatenate(picked_rows[e], axis=0).astype(bf16)
        gate = jnp.concatenate(
            [jnp.sum(p * r, axis=1, keepdims=True) for p, r in zip(picks[e], gate_rows[e])], axis=0
        )
        grads = jnp.concatenate(picked_grads[e], axis=0)
        dy = (gate * grads).astype(bf16)
        mixed = jnp.dot(x, w_gate_up, preferred_element_type=f32)
        dact = lax.dot_general(dy, w_down, NT, preferred_element_type=f32)
        gate_part, up_part = mixed[:, :FF], mixed[:, FF:]
        sigma = 1.0 / (1.0 + jnp.exp(-gate_part))
        silu = gate_part * sigma
        act = (silu * up_part).astype(bf16)
        dh = jnp.concatenate(
            [dact * up_part * (sigma + silu * (1.0 - sigma)), dact * silu], axis=1
        ).astype(bf16)
        x_ref[e] = x
        dy_ref[e] = dy
        act_ref[e] = act
        dh_ref[e] = dh
        returned = jnp.dot(act, w_down, preferred_element_type=f32).astype(bf16).astype(f32)
        dgate = jnp.sum(returned * grads, axis=1, keepdims=True)
        for b in range(4):
            gate_grad_ref[b, e : e + 1, :] = jnp.sum(
                picks[e][b] * dgate[b * SLOTS : (b + 1) * SLOTS], axis=0, keepdims=True
            )
        moved.append(gate * returned)
        routed.append(lax.dot_general(dh, w_gate_up, NT, preferred_element_type=f32))
    columns = lax.broadcasted_iota(i32, (TOK, 2 * SLOTS), 1)
    outs = [(routed_mine, moved_mine, 0), (routed_other, moved_other, 0), (routed_mine, moved_mine, 1), (routed_other, moved_other, 1)]
    for b, (routed_ref, moved_ref, n) in enumerate(outs):
        first, second = slot_cols_ref[b, :, 0:1], slot_cols_ref[b, :, 1:2]
        back = ((columns == first) | ((columns == second + SLOTS) & (second >= 0))).astype(f32).astype(bf16)
        at = slice(b * SLOTS, (b + 1) * SLOTS)
        for terms, ref in ((routed, routed_ref), (moved, moved_ref)):
            joined = jnp.concatenate([terms[0][at], terms[1][at]], axis=0).astype(bf16)
            ref[n] = jnp.dot(back, joined, preferred_element_type=f32).astype(bf16)


def run_experts(half, own, ffn, grads, weights, router, chosen, slots, slot_cols, before):
    pair = pl.BlockSpec((2, TOK, WIDTH), lambda i, o: (i, 0, 0))
    whole = lambda shape: pl.BlockSpec(shape, lambda i, o: (0,) * len(shape))
    four = lambda *shape: pl.BlockSpec((4, *shape), lambda i, o: (i + 2 * half, 0, 0))
    kept = lambda n: pl.BlockSpec((2, STEP_ROWS, n), lambda i, o: (0, i + 2 * half, 0))
    part = jax.ShapeDtypeStruct((4, TOK, WIDTH), bf16)
    keep = lambda n: jax.ShapeDtypeStruct((2, ALL_ROWS, n), bf16)
    return pl.pallas_call(
        experts_kernel,
        grid_spec=pltpu.PrefetchScalarGridSpec(
            num_scalar_prefetch=1,
            grid=(2,),
            in_specs=[
                pair,
                pair,
                pair,
                pair,
                whole((2, 8, 192, 1024)),
                whole((EXPERTS, WIDTH)),
                four(EXPERTS, TOK),
                four(2, TOK),
                four(TOK, 2),
            ]
            + [pl.BlockSpec(memory_space=pl.ANY)] * len(before),
            out_specs=[
                pair,
                pair,
                pair,
                pair,
                pl.BlockSpec((4, 2, TOK), lambda i, o: (i, 0, 0)),
                kept(WIDTH),
                kept(2 * FF),
                kept(FF),
                kept(WIDTH),
            ],
        ),
        out_shape=[
            part,
            part,
            part,
            part,
            jax.ShapeDtypeStruct((8, 2, TOK), f32),
            keep(WIDTH),
            keep(2 * FF),
            keep(FF),
            keep(WIDTH),
        ],
        input_output_aliases={10 + i: 5 + i for i in range(len(before))},
        compiler_params=pltpu.CompilerParams(vmem_limit_bytes=60 << 20),
        cost_estimate=pl.CostEstimate(
            flops=14 << 30, bytes_accessed=24 << 20, transcendentals=8 * SLOTS * 2 * FF
        ),
    )(own, *ffn, *grads, weights, router, chosen, slots, slot_cols, *before)


def expert_grads_kernel(x_ref, dh_ref, act_ref, dy_ref, out_ref):
    up = lax.dot_general(x_ref[0], dh_ref[0], TN, preferred_element_type=f32)
    down = lax.dot_general(act_ref[0], dy_ref[0], TN, preferred_element_type=f32)
    out_ref[0, :, :128, :] = up.astype(bf16).reshape(2, 128, 2 * FF)
    out_ref[0, :, 128:, :] = down.astype(bf16).reshape(2, 64, WIDTH)


def expert_weight_grads(x, dh, act, dy):
    return pl.pallas_call(
        expert_grads_kernel,
        grid=(2, 4),
        in_specs=[
            pl.BlockSpec((1, ALL_ROWS, 256), lambda e, i: (e, 0, i)),
            pl.BlockSpec((1, ALL_ROWS, 2 * FF), lambda e, i: (e, 0, 0)),
            pl.BlockSpec((1, ALL_ROWS, 128), lambda e, i: (e, 0, i)),
            pl.BlockSpec((1, ALL_ROWS, WIDTH), lambda e, i: (e, 0, 0)),
        ],
        out_specs=pl.BlockSpec((1, 2, 192, 1024), lambda e, i: (e, i, 0, 0)),
        out_shape=jax.ShapeDtypeStruct((2, 8, 192, 1024), bf16),
        compiler_params=pltpu.CompilerParams(vmem_limit_bytes=48 << 20),
        cost_estimate=pl.CostEstimate(flops=8 << 30, bytes_accessed=14 << 20, transcendentals=0),
    )(x, dh, act, dy)


def local(
    tokens,
    routes,
    cont_lengths,
    norm_attn,
    w_qkv,
    w_out,
    w_router,
    norm_ffn,
    w_gate_up,
    w_down,
    cotangent,
):
    seq_index = lax.axis_index("seq")
    places = relative_places(seq_index)
    rows = tokens[0]
    query_width = HEADS * HEAD_DIM
    kv_width = KV_HEADS * HEAD_DIM

    rows_near, rows_far = seq_gather(rows)
    kv_heads = lambda start: jnp.repeat(
        w_qkv[:, start : start + kv_width].reshape(8, KV_HEADS, HEAD_DIM), 2, axis=1
    )
    head_cols = jnp.concatenate(
        [
            w_qkv[:, :query_width].reshape(8, HEADS, HEAD_DIM),
            kv_heads(query_width),
            kv_heads(query_width + kv_width),
            jnp.broadcast_to(norm_attn[:, None, None], (8, HEADS, HEAD_DIM)),
        ],
        axis=2,
    ).transpose(1, 0, 2)
    head_cols = jnp.broadcast_to(head_cols[:, None], (HEADS, 8, 8, 256)).reshape(128, 8, 256)
    head_weights = lax.all_to_all(head_cols, BOTH, 0, 0, tiled=True).reshape(WIDTH, 256)
    gain_attn = head_weights[:, 192].astype(f32)[None]
    head_weights = jnp.where(jnp.arange(256)[None] < 192, head_weights, 0.0).astype(bf16)

    expert_rows = jnp.concatenate([w_gate_up, w_down], axis=1)
    experts = lax.all_gather(expert_rows, "wshard", axis=1, tiled=True).reshape(2, 8, 192, 1024)

    position, begin = group_layout(cont_lengths[0])
    begin = begin[None]
    cosine, sine = rotary_tables(position.astype(f32))

    normed_near, *qkv = project(places[:8], rows_near, head_weights, gain_attn, cosine, sine, ())
    rows_far, normed_near = tie(rows_far, normed_near)

    shared = jnp.concatenate(
        [w_out, w_router, norm_ffn[:, None], jnp.zeros((8, 95), bf16)], axis=1
    )
    shared, _ = tie(shared, head_weights)
    shared = lax.all_to_all(
        jnp.broadcast_to(shared[None], (8, 8, 1152)), "wshard", 0, 0, tiled=True
    ).reshape(64, 1152)
    shared, _ = tie(shared, normed_near)
    in_order = lambda halves: jnp.concatenate(
        [jnp.stack(pair, axis=1).reshape(8, *pair[0].shape[1:]) for pair in halves], axis=0
    )
    shared = jnp.take(in_order(seq_gather_by_x(shared)), places, axis=0).reshape(WIDTH, 1152)
    weight_out = shared[:, :WIDTH]
    weight_router = shared[:, WIDTH : WIDTH + EXPERTS]
    gain_ffn = shared[:, WIDTH + EXPERTS].astype(f32)
    routes_rows = jnp.pad(routes[0].T.astype(bf16), ((0, 8), (0, WIDTH - TOK)))
    upstream_rows, _ = tie(jnp.concatenate([cotangent[0], routes_rows], axis=0), rows_far[1])
    grad_near, grad_far = seq_gather_by_x(upstream_rows)
    routes_all = in_order(
        [tuple(t[:, TOK : TOK + 8, :TOK] for t in half) for half in (grad_near, grad_far)]
    ).astype(i32)

    expert_range = jnp.arange(EXPERTS, dtype=i32)
    chosen = jnp.any(routes_all[:, None] == expert_range[None, :, None, None], axis=2)
    own_first = seq_index * 2
    chosen_own = jnp.any(
        routes_all[:, None] == (own_first + jnp.arange(2, dtype=i32))[None, :, None, None], axis=2
    )
    upto = (jnp.arange(TOK)[:, None] <= jnp.arange(TOK)[None, :]).astype(bf16)
    rank = jnp.einsum("bet,tu->beu", chosen_own.astype(bf16), upto, preferred_element_type=f32)
    slots = jnp.where(chosen_own, rank.astype(i32) - 1, -1)
    slot_cols = slots.transpose(0, 2, 1)
    chosen = chosen.astype(f32)

    normed_far, q, k, v = project(places[8:], rows_far, head_weights, gain_attn, cosine, sine, qkv)
    attended_head, attended_t, lse = attend(q, k, v, begin)
    attended = lax.all_to_all(attended_head.reshape(16, TOK, HEAD_DIM), "seq", 0, 0, tiled=True)
    attended = attended.transpose(1, 0, 2).reshape(TOK, query_width)
    inputs = rows.astype(f32)
    hidden = inputs + jnp.dot(attended, weight_out, preferred_element_type=f32)
    hidden_scale = inverse_rms(hidden)
    normed_ffn = (hidden * hidden_scale * gain_ffn).astype(bf16)
    normed_ffn, grad_near, grad_far, chosen, slots, slot_cols = tie(
        normed_ffn, grad_near, grad_far, chosen, slots, slot_cols
    )

    ffn_near, ffn_far = seq_gather(normed_ffn)
    router_t = weight_router.T
    own = own_first[None]
    near = run_experts(
        0, own, ffn_near, grad_near, experts, router_t, chosen, slots, slot_cols, ()
    )
    near_terms = sum_along_z(near[0], near[1])
    far = run_experts(
        1, own, ffn_far, grad_far, experts, router_t, chosen, slots, slot_cols, near[5:]
    )
    far, near_terms = tie(far, near_terms)
    far_terms = sum_along_z(far[0], far[1])
    expert_grads = expert_weight_grads(*far[5:])
    routed_grad = sum_across(near_terms, far_terms)
    token_gate_grad = jnp.take(jnp.concatenate([near[4], far[4]], axis=0), places, axis=0)
    gate_grad = lax.all_to_all(token_gate_grad, "seq", 0, 0, tiled=True).reshape(EXPERTS, TOK).T
    routed_grad, gate_grad, expert_grads, near, far = tie(
        routed_grad, gate_grad, expert_grads, near, far
    )
    expert_grads = lax.psum_scatter(
        expert_grads.reshape(2, 8 * 192, 1024), "wshard", scatter_dimension=1, tiled=True
    ).astype(f32)

    chosen_here = jnp.any(routes[0][:, :, None] == expert_range, axis=1)
    logits = jnp.dot(normed_ffn, weight_router, preferred_element_type=f32)
    peak = jnp.max(jnp.where(chosen_here, logits, -jnp.inf), axis=-1, keepdims=True)
    raised = jnp.where(chosen_here, jnp.exp(logits - peak), 0.0)
    gates = raised / jnp.sum(raised, axis=-1, keepdims=True)
    chosen_grad = gates * (gate_grad - jnp.sum(gates * gate_grad, axis=-1, keepdims=True))
    logit_grad = chosen_grad.astype(bf16)
    normed_ffn_grad = routed_grad + jnp.einsum(
        "te,de->td", logit_grad, weight_router, preferred_element_type=f32
    )
    upstream = cotangent[0].astype(f32)
    hidden_grad = upstream + rms_pull(hidden, hidden_scale, gain_ffn, normed_ffn_grad)
    branch_grad = hidden_grad.astype(bf16)
    attended_grad = jnp.einsum(
        "td,qd->tq", branch_grad, weight_out, preferred_element_type=f32
    ).astype(bf16)
    head_grad = lax.all_to_all(
        attended_grad.reshape(TOK, HEADS, HEAD_DIM).transpose(1, 0, 2), "seq", 0, 0, tiled=True
    ).reshape(GROUP, HEAD_DIM)

    grad_router = jnp.einsum("td,te->de", normed_ffn, logit_grad, preferred_element_type=f32)
    grad_norm_ffn = jnp.sum(normed_ffn_grad * hidden * hidden_scale, axis=0)
    grad_out = jnp.einsum("tq,td->qd", attended, branch_grad, preferred_element_type=f32)
    shared_grads = jnp.concatenate(
        [grad_out, grad_router, grad_norm_ffn[:, None], jnp.zeros((WIDTH, 95), f32)], axis=1
    ).astype(bf16)
    moved = seq_sum_by_x(near[2:4], far[2:4])
    head_grad, shared_grads = tie(head_grad, shared_grads)
    shared_grads = jnp.sum(
        lax.all_to_all(shared_grads.reshape(128, 8, 1152), BOTH, 0, 0, tiled=True).astype(f32),
        axis=0,
    )
    grads = attend_back(q, k, v, head_grad, attended_t, lse, begin)
    grads, moved = tie(grads, moved)
    output = (hidden + moved).astype(bf16)
    *near_part, grad_head = project_back(
        places[:8], normed_near, grads, head_weights, cosine, sine, ()
    )
    near_terms = sum_along_z(*near_part)
    *far_part, grad_head = project_back(
        places[8:], normed_far, grads, head_weights, cosine, sine, (grad_head,)
    )
    far_terms = sum_along_z(*far_part)
    grad_heads = lax.all_to_all(
        grad_head.astype(bf16).reshape(128, 8, 256), BOTH, 0, 0, tiled=True
    )
    grad_heads, far_terms = tie(grad_heads, far_terms)
    normed_grad = sum_across(near_terms, far_terms)
    grad_heads = jnp.sum(grad_heads.reshape(16, 8, 8, 256).astype(f32), axis=1).transpose(1, 0, 2)
    kv_sum = lambda start: jnp.sum(
        grad_heads[:, :, start : start + HEAD_DIM].reshape(8, KV_HEADS, 2, HEAD_DIM), axis=2
    ).reshape(8, kv_width)
    grad_qkv = jnp.concatenate(
        [grad_heads[:, :, :HEAD_DIM].reshape(8, query_width), kv_sum(HEAD_DIM), kv_sum(2 * HEAD_DIM)],
        axis=1,
    )
    grad_norm_attn = jnp.sum(grad_qkv * w_qkv.astype(f32), axis=1) / norm_attn.astype(f32)
    grad_input = hidden_grad + rms_pull(inputs, inverse_rms(inputs), gain_attn, normed_grad)
    return (
        output[None],
        grad_input[None],
        grad_norm_attn,
        grad_qkv,
        shared_grads[:, :WIDTH],
        shared_grads[:, WIDTH : WIDTH + EXPERTS],
        shared_grads[:, WIDTH + EXPERTS],
        expert_grads[:, :128],
        expert_grads[:, 128:],
    )


def solution(mesh):
    return jax.shard_map(
        local,
        mesh=mesh,
        in_specs=(
            P("wshard", "seq", None),
            P("wshard", "seq", None),
            P("wshard", None),
            P(BOTH),
            P(BOTH, None),
            P(BOTH, None),
            P(BOTH, None),
            P(BOTH),
            P("seq", "wshard", None),
            P("seq", "wshard", None),
            P("wshard", "seq", None),
        ),
        out_specs=(
            P("wshard", "seq", None),
            P("wshard", "seq", None),
            P(BOTH),
            P(BOTH, None),
            P(BOTH, None),
            P(BOTH, None),
            P(BOTH),
            P("seq", "wshard", None),
            P("seq", "wshard", None),
        ),
        check_vma=False,
    )
```

```python
import jax
import jax.numpy as jnp
from jax import lax
from jax.experimental import pallas as pl
from jax.experimental.pallas import tpu as pltpu
from jax.sharding import PartitionSpec as P

HEADS = 16
KV_HEADS = 8
HEAD_DIM = 64
EXPERTS = 32
FF = 512
PROMPT = 2048
GROUP = 3584
TOK = 224
WIDTH = 1024
SLOTS = 72
STEP_ROWS = 4 * SLOTS
ALL_ROWS = 16 * SLOTS
BLOCK = 512

norm_eps = 1e-06
rope_base = 10000.0
masked_score = -1e30
BOTH = ("seq", "wshard")
NT = (((1,), (1,)), ((), ()))
TN = (((0,), (0,)), ((), ()))
f32 = jnp.float32
bf16 = jnp.bfloat16
i32 = jnp.int32


def place_of(x, z, core):
    return x * 8 + z * 2 + core


def shift_perm(a, b):
    return [
        (place_of(x, z, c), place_of(x ^ a, (z + b) % 4, c))
        for x in range(2)
        for z in range(4)
        for c in range(2)
    ]


CORE_PERM = [(i, i ^ 1) for i in range(16)]


def send(rows, a, b):
    return lax.ppermute(rows, "seq", shift_perm(a, b))


def swap_cores(rows):
    return lax.ppermute(rows, "seq", CORE_PERM)


def relative_places(seq_index):
    x, z, c = seq_index // 8, (seq_index // 2) % 4, seq_index % 2
    r = jnp.arange(16, dtype=i32)
    a, i, k = r // 8, (r // 2) % 4, r % 2
    shift = i ^ (i // 2)
    behind = (z - i) % 4
    places = (a ^ x) * 8 + ((z - shift) % 4) * 2 + (k ^ c)
    return places, (a ^ x) * 8 + (behind ^ (behind // 2)) * 2 + (k ^ c)


def gather_near(rows):
    return [rows] + [send(rows, 0, b) for b in (1, 3, 2)], send(rows, 1, 0)


def both_cores(parts):
    mine = jnp.stack(parts)
    return mine, swap_cores(mine)


def gather_far(across):
    return both_cores([across] + [send(across, 0, b) for b in (1, 3, 2)])


def seq_gather(rows):
    near, across = gather_near(rows)
    return both_cores(near), gather_far(across)


def add_low(*terms):
    return sum([t.astype(f32) for t in terms]).astype(bf16)


def sum_along_z(mine, other):
    got = swap_cores(other)
    parts = [add_low(mine[i], got[i]) for i in range(4)]
    return [parts[0]] + [send(parts[i], 0, -b) for i, b in ((1, 1), (2, 3), (3, 2))]


def send_w(rows, a, b):
    pairs = [(y * 2 + x, ((y + b) % 4) * 2 + (x ^ a)) for y in range(4) for x in range(2)]
    return lax.ppermute(rows, "wshard", pairs)


def tie(*values):
    return lax.optimization_barrier(values)


def inverse_rms(values):
    return lax.rsqrt(jnp.mean(values * values, axis=-1, keepdims=True) + norm_eps)


def rms_pull(values, scale, gain, grad):
    scaled = grad * gain
    return scale * scaled - values * (scale * scale * scale) * jnp.mean(
        scaled * values, axis=-1, keepdims=True
    )


def group_layout(lengths):
    places = jnp.arange(GROUP, dtype=i32)
    ends = jnp.cumsum(lengths)
    starts = ends - lengths
    offset_in = places - PROMPT
    segment_id = jnp.sum((offset_in[:, None] >= ends[None, :]).astype(i32), axis=1)
    segment_hot = segment_id[:, None] == jnp.arange(lengths.shape[0], dtype=i32)[None, :]
    begin = jnp.sum(jnp.where(segment_hot, starts[None, :], 0), axis=1)
    inside = offset_in >= 0
    position = jnp.where(inside, PROMPT + offset_in - begin, places)
    return position, jnp.where(inside, PROMPT + begin, 0)


def rotary_tables(position):
    half_dim = HEAD_DIM // 2
    inverse = rope_base ** (-(jnp.arange(half_dim, dtype=f32) * 2.0) / HEAD_DIM)
    angles = position[:, None] * inverse[None, :]
    cosine, sine = jnp.cos(angles), jnp.sin(angles)
    return (
        jnp.concatenate([cosine, cosine], axis=-1),
        jnp.concatenate([sine, sine], axis=-1),
    )


def turn(values):
    half_dim = HEAD_DIM // 2
    return jnp.concatenate([-values[:, half_dim:], values[:, :half_dim]], axis=-1)


def turn_back(values):
    half_dim = HEAD_DIM // 2
    return jnp.concatenate([values[:, half_dim:], -values[:, :half_dim]], axis=-1)


def project_kernel(places, mine, other, w, gain, cosine, sine, *refs):
    del places
    normed_ref, q_ref, k_ref, v_ref = refs[-4:]
    rows = jnp.where(pl.program_id(1) == 0, mine[0], other[0])
    values = rows.astype(f32)
    normed = (values * inverse_rms(values) * gain[...]).astype(bf16)
    normed_ref[0] = normed
    projected = jnp.dot(normed, w[...], preferred_element_type=f32)
    c, s = cosine[...], sine[...]
    q, k, v = projected[:, :64], projected[:, 64:128], projected[:, 128:192]
    q_ref[...] = ((q * c + turn(q) * s).astype(bf16).astype(f32) * HEAD_DIM**-0.5).astype(bf16)
    k_ref[...] = (k * c + turn(k) * s).astype(bf16)
    v_ref[...] = v.astype(bf16)


def project(places, gathered, w, gain, cosine, sine, before):
    chip = pl.BlockSpec((1, TOK, WIDTH), lambda j, k, p: (j, 0, 0))
    whole = lambda shape: pl.BlockSpec(shape, lambda j, k, p: (0,) * len(shape))
    at = pl.BlockSpec((TOK, HEAD_DIM), lambda j, k, p: (p[2 * j + k], 0))
    table = jax.ShapeDtypeStruct((GROUP, HEAD_DIM), bf16)
    return pl.pallas_call(
        project_kernel,
        grid_spec=pltpu.PrefetchScalarGridSpec(
            num_scalar_prefetch=1,
            grid=(4, 2),
            in_specs=[chip, chip, whole((WIDTH, 256)), whole((1, WIDTH)), at, at]
            + [pl.BlockSpec(memory_space=pl.ANY)] * len(before),
            out_specs=[pl.BlockSpec((1, TOK, WIDTH), lambda j, k, p: (2 * j + k, 0, 0)), at, at, at],
        ),
        out_shape=[jax.ShapeDtypeStruct((8, TOK, WIDTH), bf16), table, table, table],
        input_output_aliases={7 + i: 1 + i for i in range(len(before))},
        compiler_params=pltpu.CompilerParams(vmem_limit_bytes=32 << 20),
        cost_estimate=pl.CostEstimate(
            flops=2 * 8 * TOK * WIDTH * 256, bytes_accessed=10 << 20, transcendentals=0
        ),
    )(places, *gathered, w, gain, cosine, sine, *before)


def project_back_kernel(places, normed, dq, dk, dv, w, cosine, sine, *refs):
    del places
    mine, other, grad = refs[-3:]
    first = (pl.program_id(0) == 0) & (pl.program_id(1) == 0)

    @pl.when(first)
    def _():
        grad[...] = jnp.zeros_like(grad) if len(refs) == 3 else refs[0][...]

    c, s = cosine[...], sine[...]
    q = dq[...].astype(bf16).astype(f32)
    k = dk[...].astype(bf16).astype(f32)
    projected = jnp.concatenate(
        [q * c + turn_back(q * s), k * c + turn_back(k * s), dv[...], jnp.zeros_like(q)], axis=1
    ).astype(bf16)
    grad[...] += lax.dot_general(normed[0], projected, TN, preferred_element_type=f32)
    part = lax.dot_general(projected, w[...], NT, preferred_element_type=f32).astype(bf16)

    @pl.when(pl.program_id(1) == 0)
    def _():
        mine[0] = part

    @pl.when(pl.program_id(1) == 1)
    def _():
        other[0] = part


def project_back(places, normed, grads, w, cosine, sine, before):
    chip = pl.BlockSpec((1, TOK, WIDTH), lambda j, k, p: (j, 0, 0))
    whole = lambda shape: pl.BlockSpec(shape, lambda j, k, p: (0,) * len(shape))
    at = pl.BlockSpec((TOK, HEAD_DIM), lambda j, k, p: (p[2 * j + k], 0))
    part = jax.ShapeDtypeStruct((4, TOK, WIDTH), bf16)
    return pl.pallas_call(
        project_back_kernel,
        grid_spec=pltpu.PrefetchScalarGridSpec(
            num_scalar_prefetch=1,
            grid=(4, 2),
            in_specs=[
                pl.BlockSpec((1, TOK, WIDTH), lambda j, k, p: (2 * j + k, 0, 0)),
                at,
                at,
                at,
                whole((WIDTH, 256)),
                at,
                at,
            ]
            + [whole((WIDTH, 256))] * len(before),
            out_specs=[chip, chip, whole((WIDTH, 256))],
        ),
        out_shape=[part, part, jax.ShapeDtypeStruct((WIDTH, 256), f32)],
        compiler_params=pltpu.CompilerParams(vmem_limit_bytes=32 << 20),
        cost_estimate=pl.CostEstimate(
            flops=4 * 8 * TOK * WIDTH * 256, bytes_accessed=12 << 20, transcendentals=0
        ),
    )(places, normed, *grads, w, cosine, sine, *before)


def tile_mask(scores, key_start, query_start, begin):
    keys = key_start + lax.broadcasted_iota(i32, scores.shape, 0)
    queries = query_start + lax.broadcasted_iota(i32, scores.shape, 1)
    return jnp.where((keys <= queries) & (keys >= begin), scores, masked_score)


def key_ranges(i):
    first = PROMPT // BLOCK
    return jnp.where(i > first, i - 1, i), jnp.minimum(i, first)


def attend_kernel(q_ref, k_ref, v_ref, begin_ref, o_ref, ot_ref, lse_ref, vt):
    i = pl.program_id(0)

    @pl.when(i == 0)
    def _():
        vt[...] = v_ref[...].T

    q = q_ref[...]
    begin = begin_ref[...]

    def tile(j, carry, masked):
        peak, total, out = carry
        start = pl.multiple_of(j * BLOCK, BLOCK)
        at = pl.ds(start, BLOCK)
        s = lax.dot_general(k_ref[at, :], q, NT, preferred_element_type=f32)
        if masked:
            s = tile_mask(s, start, i * BLOCK, begin)
        higher = jnp.maximum(peak, jnp.max(s, axis=0, keepdims=True))
        p = jnp.exp(s - higher)
        fade = jnp.exp(peak - higher)
        total = total * fade + jnp.sum(p, axis=0, keepdims=True)
        out = out * fade + jnp.dot(vt[:, at], p.astype(bf16), preferred_element_type=f32)
        return higher, total, out

    carry = (
        jnp.full((1, BLOCK), masked_score, f32),
        jnp.zeros((1, BLOCK), f32),
        jnp.zeros((HEAD_DIM, BLOCK), f32),
    )
    carry = tile(i, carry, True)
    window, shared = key_ranges(i)
    carry = lax.fori_loop(window, i, lambda j, c: tile(j, c, True), carry)
    peak, total, out = lax.fori_loop(0, shared, lambda j, c: tile(j, c, False), carry)
    out = out * (1.0 / total)
    ot_ref[...] = out
    o_ref[...] = out.T.astype(bf16)
    lse_ref[...] = peak + jnp.log(total)


def attend(q, k, v, begin):
    whole = pl.BlockSpec((GROUP, HEAD_DIM), lambda i: (0, 0))
    rows = pl.BlockSpec((BLOCK, HEAD_DIM), lambda i: (i, 0))
    cols = lambda n: pl.BlockSpec((n, BLOCK), lambda i: (0, i))
    return pl.pallas_call(
        attend_kernel,
        grid=(GROUP // BLOCK,),
        in_specs=[rows, whole, whole, cols(1)],
        out_specs=[rows, cols(HEAD_DIM), cols(1)],
        out_shape=[
            jax.ShapeDtypeStruct((GROUP, HEAD_DIM), bf16),
            jax.ShapeDtypeStruct((HEAD_DIM, GROUP), f32),
            jax.ShapeDtypeStruct((1, GROUP), f32),
        ],
        scratch_shapes=[pltpu.VMEM((HEAD_DIM, GROUP), bf16)],
        compiler_params=pltpu.CompilerParams(vmem_limit_bytes=32 << 20),
        cost_estimate=pl.CostEstimate(
            flops=2 * 27 * BLOCK * BLOCK * 512, bytes_accessed=4 << 20, transcendentals=27 * BLOCK * BLOCK
        ),
    )(q, k, v, begin)


def attend_back_kernel(
    q_ref, k_ref, v_ref, g_ref, ot_ref, lse_ref, begin_ref, dq_ref, dk_ref, dv_ref, kt
):
    i = pl.program_id(0)

    @pl.when(i == 0)
    def _():
        dk_ref[...] = jnp.zeros_like(dk_ref)
        dv_ref[...] = jnp.zeros_like(dv_ref)
        kt[...] = k_ref[...].T

    q = q_ref[...]
    g = g_ref[...]
    begin = begin_ref[...]
    lse = lse_ref[...]
    inner = jnp.sum(g.T.astype(f32) * ot_ref[...], axis=0, keepdims=True)

    def tile(j, dq, masked):
        start = pl.multiple_of(j * BLOCK, BLOCK)
        at = pl.ds(start, BLOCK)
        s = lax.dot_general(k_ref[at, :], q, NT, preferred_element_type=f32)
        if masked:
            s = tile_mask(s, start, i * BLOCK, begin)
        p = jnp.exp(s - lse)
        dp = lax.dot_general(v_ref[at, :], g, NT, preferred_element_type=f32)
        ds = (p * (dp - inner)).astype(bf16)
        dv_ref[at, :] += jnp.dot(p.astype(bf16), g, preferred_element_type=f32)
        dk_ref[at, :] += jnp.dot(ds, q, preferred_element_type=f32)
        return dq + jnp.dot(kt[:, at], ds, preferred_element_type=f32)

    dq = tile(i, jnp.zeros((HEAD_DIM, BLOCK), f32), True)
    window, shared = key_ranges(i)
    dq = lax.fori_loop(window, i, lambda j, c: tile(j, c, True), dq)
    dq = lax.fori_loop(0, shared, lambda j, c: tile(j, c, False), dq)
    dq_ref[...] = dq.T * HEAD_DIM**-0.5


def attend_back(q, k, v, g, ot, lse, begin):
    whole = pl.BlockSpec((GROUP, HEAD_DIM), lambda i: (0, 0))
    rows = pl.BlockSpec((BLOCK, HEAD_DIM), lambda i: (i, 0))
    cols = lambda n: pl.BlockSpec((n, BLOCK), lambda i: (0, i))
    out = jax.ShapeDtypeStruct((GROUP, HEAD_DIM), f32)
    return pl.pallas_call(
        attend_back_kernel,
        grid=(GROUP // BLOCK,),
        in_specs=[rows, whole, whole, rows, cols(HEAD_DIM), cols(1), cols(1)],
        out_specs=[rows, whole, whole],
        out_shape=[out, out, out],
        scratch_shapes=[pltpu.VMEM((HEAD_DIM, GROUP), bf16)],
        compiler_params=pltpu.CompilerParams(vmem_limit_bytes=48 << 20),
        cost_estimate=pl.CostEstimate(
            flops=5 * 27 * BLOCK * BLOCK * 512, bytes_accessed=8 << 20, transcendentals=27 * BLOCK * BLOCK
        ),
    )(q, k, v, g, ot, lse, begin)


SHARDS = [(0, 0, 0), (0, 1, 1), (1, 0, 2), (1, 1, 3), (2, 0, 6), (2, 1, 7), (3, None, 4), (4, None, 5)]
N_SHARDS = 5


def experts_kernel(
    own_ref, ffn_mine, ffn_other, g_mine, g_other, router_ref, chosen_ref, slots_ref, slot_cols_ref, *refs
):
    shards = refs[:N_SHARDS]
    routed_mine, routed_other, gate_grad_ref, moved_mine, moved_other = refs[-11:-6]
    x_ref, dh_ref, act_ref, dy_ref, w_ref, sem = refs[-6:]
    own = own_ref[0]

    @pl.when(pl.program_id(0) == 0)
    def _():
        copies = []
        for n, (shard, a, r) in enumerate(SHARDS):
            source = shards[shard] if a is None else shards[shard].at[a]
            for e in range(2):
                place = own_ref[1 + r]
                copies.append(pltpu.make_async_copy(source.at[e], w_ref.at[e, place], sem.at[n, e]))
        for copy in copies:
            copy.start()
        for copy in copies:
            copy.wait()

    expert_rows = lax.broadcasted_iota(i32, (EXPERTS, TOK), 0)
    slot_rows = lax.broadcasted_iota(i32, (SLOTS, TOK), 0)
    gate_rows = [[], []]
    picks = [[], []]
    picked_rows = [[], []]
    picked_grads = [[], []]
    blocks = [(ffn_mine, g_mine, 0), (ffn_other, g_other, 0), (ffn_mine, g_mine, 1), (ffn_other, g_other, 1)]
    for b, (rows_ref, grads_ref, n) in enumerate(blocks):
        rows, grads = rows_ref[n], grads_ref[n]
        chosen = chosen_ref[b] > 0
        logits = lax.dot_general(router_ref[...], rows, NT, preferred_element_type=f32)
        peak = jnp.max(jnp.where(chosen, logits, masked_score), axis=0, keepdims=True)
        raised = jnp.where(chosen, jnp.exp(jnp.minimum(logits - peak, 0.0)), 0.0)
        gates = raised / jnp.sum(raised, axis=0, keepdims=True)
        for e in range(2):
            gate_rows[e].append(
                jnp.sum(jnp.where(expert_rows == own + e, gates, 0.0), axis=0, keepdims=True)
            )
            pick = (slots_ref[b, e : e + 1, :] == slot_rows).astype(f32)
            picks[e].append(pick)
            low = pick.astype(bf16)
            picked_rows[e].append(jnp.dot(low, rows, preferred_element_type=f32))
            picked_grads[e].append(jnp.dot(low, grads, preferred_element_type=f32))
    moved, routed = [], []
    for e in range(2):
        w_gate_up = w_ref[e, :, :128, :].reshape(WIDTH, 2 * FF)
        w_down = w_ref[e, :, 128:, :].reshape(FF, WIDTH)
        x = jnp.concatenate(picked_rows[e], axis=0).astype(bf16)
        gate = jnp.concatenate(
            [jnp.sum(p * r, axis=1, keepdims=True) for p, r in zip(picks[e], gate_rows[e])], axis=0
        )
        grads = jnp.concatenate(picked_grads[e], axis=0)
        dy = (gate * grads).astype(bf16)
        mixed = jnp.dot(x, w_gate_up, preferred_element_type=f32)
        dact = lax.dot_general(dy, w_down, NT, preferred_element_type=f32)
        gate_part, up_part = mixed[:, :FF], mixed[:, FF:]
        sigma = 1.0 / (1.0 + jnp.exp(-gate_part))
        silu = gate_part * sigma
        act = (silu * up_part).astype(bf16)
        dh = jnp.concatenate(
            [dact * up_part * (sigma + silu * (1.0 - sigma)), dact * silu], axis=1
        ).astype(bf16)
        x_ref[e] = x
        dy_ref[e] = dy
        act_ref[e] = act
        dh_ref[e] = dh
        returned = jnp.dot(act, w_down, preferred_element_type=f32).astype(bf16).astype(f32)
        dgate = jnp.sum(returned * grads, axis=1, keepdims=True)
        for b in range(4):
            gate_grad_ref[b, e : e + 1, :] = jnp.sum(
                picks[e][b] * dgate[b * SLOTS : (b + 1) * SLOTS], axis=0, keepdims=True
            )
        moved.append(gate * returned)
        routed.append(lax.dot_general(dh, w_gate_up, NT, preferred_element_type=f32))
    columns = lax.broadcasted_iota(i32, (TOK, 2 * SLOTS), 1)
    outs = [(routed_mine, moved_mine, 0), (routed_other, moved_other, 0), (routed_mine, moved_mine, 1), (routed_other, moved_other, 1)]
    for b, (routed_ref, moved_ref, n) in enumerate(outs):
        first, second = slot_cols_ref[b, :, 0:1], slot_cols_ref[b, :, 1:2]
        back = ((columns == first) | ((columns == second + SLOTS) & (second >= 0))).astype(f32).astype(bf16)
        at = slice(b * SLOTS, (b + 1) * SLOTS)
        for terms, ref in ((routed, routed_ref), (moved, moved_ref)):
            joined = jnp.concatenate([terms[0][at], terms[1][at]], axis=0).astype(bf16)
            ref[n] = jnp.dot(back, joined, preferred_element_type=f32).astype(bf16)


def run_experts(half, own, ffn, grads, weights, router, chosen, slots, slot_cols, before):
    pair = pl.BlockSpec((2, TOK, WIDTH), lambda i, o: (i, 0, 0))
    pair_of_all = pl.BlockSpec((2, TOK, WIDTH), lambda i, o: (i + 2 * half, 0, 0))
    whole = lambda shape: pl.BlockSpec(shape, lambda i, o: (0,) * len(shape))
    four = lambda *shape: pl.BlockSpec((4, *shape), lambda i, o: (i + 2 * half, 0, 0))
    kept = lambda n: pl.BlockSpec((2, STEP_ROWS, n), lambda i, o: (0, i + 2 * half, 0))
    part = jax.ShapeDtypeStruct((4, TOK, WIDTH), bf16)
    keep = lambda n: jax.ShapeDtypeStruct((2, ALL_ROWS, n), bf16)
    return pl.pallas_call(
        experts_kernel,
        grid_spec=pltpu.PrefetchScalarGridSpec(
            num_scalar_prefetch=1,
            grid=(2,),
            in_specs=[
                pair,
                pair,
                pair,
                pair,
                whole((EXPERTS, WIDTH)),
                four(EXPERTS, TOK),
                four(2, TOK),
                four(TOK, 2),
            ]
            + [pl.BlockSpec(memory_space=pl.ANY)] * (N_SHARDS + len(before)),
            out_specs=[
                pair,
                pair,
                pl.BlockSpec((4, 2, TOK), lambda i, o: (i, 0, 0)),
                pair_of_all,
                pair_of_all,
                kept(WIDTH),
                kept(2 * FF),
                kept(FF),
                kept(WIDTH),
            ],
            scratch_shapes=[
                pltpu.VMEM((2, 8, 192, 1024), bf16),
                pltpu.SemaphoreType.DMA((8, 2)),
            ],
        ),
        out_shape=[
            part,
            part,
            jax.ShapeDtypeStruct((8, 2, TOK), f32),
            jax.ShapeDtypeStruct((8, TOK, WIDTH), bf16),
            jax.ShapeDtypeStruct((8, TOK, WIDTH), bf16),
            keep(WIDTH),
            keep(2 * FF),
            keep(FF),
            keep(WIDTH),
        ],
        input_output_aliases={9 + N_SHARDS + i: 3 + i for i in range(len(before))},
        compiler_params=pltpu.CompilerParams(vmem_limit_bytes=60 << 20),
        cost_estimate=pl.CostEstimate(
            flops=14 << 30, bytes_accessed=24 << 20, transcendentals=8 * SLOTS * 2 * FF
        ),
    )(own, *ffn, *grads, router, chosen, slots, slot_cols, *weights, *before)


def expert_grads_kernel(order, x_ref, dh_ref, act_ref, dy_ref, out_ref):
    del order
    up = lax.dot_general(x_ref[0], dh_ref[0], TN, preferred_element_type=f32)
    down = lax.dot_general(act_ref[0], dy_ref[0], TN, preferred_element_type=f32)
    out_ref[0, :, 0, :128, :] = up.astype(bf16).reshape(2, 128, 2 * FF)
    out_ref[0, :, 0, 128:, :] = down.astype(bf16).reshape(2, 64, WIDTH)


def expert_weight_grads(order, x, dh, act, dy):
    return pl.pallas_call(
        expert_grads_kernel,
        grid_spec=pltpu.PrefetchScalarGridSpec(
            num_scalar_prefetch=1,
            grid=(2, 4),
            in_specs=[
                pl.BlockSpec((1, ALL_ROWS, 256), lambda e, i, o: (e, 0, i)),
                pl.BlockSpec((1, ALL_ROWS, 2 * FF), lambda e, i, o: (e, 0, 0)),
                pl.BlockSpec((1, ALL_ROWS, 128), lambda e, i, o: (e, 0, i)),
                pl.BlockSpec((1, ALL_ROWS, WIDTH), lambda e, i, o: (e, 0, 0)),
            ],
            out_specs=pl.BlockSpec((1, 2, 1, 192, 1024), lambda e, i, o: (o[i], 0, e, 0, 0)),
        ),
        out_shape=jax.ShapeDtypeStruct((4, 2, 2, 192, 1024), bf16),
        compiler_params=pltpu.CompilerParams(vmem_limit_bytes=48 << 20),
        cost_estimate=pl.CostEstimate(flops=8 << 30, bytes_accessed=14 << 20, transcendentals=0),
    )(order, x, dh, act, dy)


def hidden_kernel(att_ref, w_ref, rows_ref, gain_ref, hidden_ref, normed_ref, att_rows_ref):
    att = jnp.concatenate([att_ref[h] for h in range(HEADS)], axis=1)
    att_rows_ref[...] = att
    hidden = rows_ref[...].astype(f32) + jnp.dot(att, w_ref[:, :WIDTH], preferred_element_type=f32)
    hidden_ref[...] = hidden
    normed_ref[...] = (hidden * inverse_rms(hidden) * gain_ref[...]).astype(bf16)


def hidden_of(attended, shared, rows, gain):
    return pl.pallas_call(
        hidden_kernel,
        out_shape=[
            jax.ShapeDtypeStruct((TOK, WIDTH), f32),
            jax.ShapeDtypeStruct((TOK, WIDTH), bf16),
            jax.ShapeDtypeStruct((TOK, WIDTH), bf16),
        ],
        compiler_params=pltpu.CompilerParams(vmem_limit_bytes=32 << 20),
        cost_estimate=pl.CostEstimate(
            flops=2 * TOK * WIDTH * WIDTH, bytes_accessed=5 << 20, transcendentals=0
        ),
    )(attended, shared, rows, gain)


def hidden_back_kernel(
    t0, t1, t2, t3, crossed, hidden_ref, normed_ref, gate_grad_ref, chosen_ref, router_ref, g_ref, gain_ref,
    w_ref, hidden_grad_ref, branch_ref, logit_ref, scaled_ref, att_ref
):
    chosen = chosen_ref[...] > 0
    logits = lax.dot_general(router_ref[...], normed_ref[...], NT, preferred_element_type=f32)
    peak = jnp.max(jnp.where(chosen, logits, masked_score), axis=0, keepdims=True)
    raised = jnp.where(chosen, jnp.exp(jnp.minimum(logits - peak, 0.0)), 0.0)
    gates = raised / jnp.sum(raised, axis=0, keepdims=True)
    gate_grad = gate_grad_ref[...]
    logit_grad = gates * (gate_grad - jnp.sum(gates * gate_grad, axis=0, keepdims=True))
    logit_grad = logit_grad.astype(bf16)
    logit_ref[...] = logit_grad
    normed_grad = lax.dot_general(logit_grad, router_ref[...], TN, preferred_element_type=f32)
    for term in (t0, t1, t2, t3, crossed):
        normed_grad = normed_grad + term[...].astype(f32)
    hidden = hidden_ref[...]
    scale = inverse_rms(hidden)
    scaled_ref[...] = (normed_grad * hidden * scale).astype(bf16)
    hidden_grad = g_ref[...].astype(f32) + rms_pull(hidden, scale, gain_ref[...], normed_grad)
    hidden_grad_ref[...] = hidden_grad
    branch = hidden_grad.astype(bf16)
    branch_ref[...] = branch
    att = lax.dot_general(branch, w_ref[:, :WIDTH], NT, preferred_element_type=f32).astype(bf16)
    for h in range(HEADS):
        att_ref[h] = att[:, h * HEAD_DIM : (h + 1) * HEAD_DIM]


def hidden_back(terms, crossed, hidden, normed, gate_grad, chosen, router_t, g, gain, shared):
    wide = lambda t: jax.ShapeDtypeStruct((TOK, WIDTH), t)
    return pl.pallas_call(
        hidden_back_kernel,
        out_shape=[
            wide(f32),
            wide(bf16),
            jax.ShapeDtypeStruct((EXPERTS, TOK), bf16),
            wide(bf16),
            jax.ShapeDtypeStruct((HEADS, TOK, HEAD_DIM), bf16),
        ],
        compiler_params=pltpu.CompilerParams(vmem_limit_bytes=32 << 20),
        cost_estimate=pl.CostEstimate(
            flops=2 * TOK * WIDTH * WIDTH, bytes_accessed=8 << 20, transcendentals=0
        ),
    )(*terms, crossed, hidden, normed, gate_grad, chosen, router_t, g, gain, shared)


def shared_grads_kernel(att_ref, branch_ref, normed_ref, logit_ref, scaled_ref, out_ref):
    out_ref[:, :WIDTH] = lax.dot_general(
        att_ref[...], branch_ref[...], TN, preferred_element_type=f32
    ).astype(bf16)
    over_tokens = (((0,), (1,)), ((), ()))
    logit = jnp.concatenate([logit_ref[...], jnp.zeros((96, TOK), bf16)], axis=0)
    ones = (lax.broadcasted_iota(i32, (128, TOK), 0) == EXPERTS).astype(f32).astype(bf16)
    out_ref[:, WIDTH:] = (
        lax.dot_general(normed_ref[...], logit, over_tokens, preferred_element_type=f32)
        + lax.dot_general(scaled_ref[...], ones, over_tokens, preferred_element_type=f32)
    ).astype(bf16)


def shared_weight_grads(att, branch, normed, logit_grad, scaled):
    return pl.pallas_call(
        shared_grads_kernel,
        out_shape=jax.ShapeDtypeStruct((WIDTH, 1152), bf16),
        compiler_params=pltpu.CompilerParams(vmem_limit_bytes=32 << 20),
        cost_estimate=pl.CostEstimate(
            flops=2 * TOK * WIDTH * 1280, bytes_accessed=5 << 20, transcendentals=0
        ),
    )(att, branch, normed, logit_grad, scaled)


def local(
    tokens,
    routes,
    cont_lengths,
    norm_attn,
    w_qkv,
    w_out,
    w_router,
    norm_ffn,
    w_gate_up,
    w_down,
    cotangent,
):
    seq_index = lax.axis_index("seq")
    places, blocks = relative_places(seq_index)
    rows = tokens[0]
    query_width = HEADS * HEAD_DIM
    kv_width = KV_HEADS * HEAD_DIM

    position, begin = group_layout(cont_lengths[0])
    begin = begin[None]
    cosine, sine = rotary_tables(position.astype(f32))
    kv_heads = lambda start: jnp.repeat(
        w_qkv[:, start : start + kv_width].reshape(8, KV_HEADS, HEAD_DIM), 2, axis=1
    )
    head_cols = jnp.concatenate(
        [
            w_qkv[:, :query_width].reshape(8, HEADS, HEAD_DIM),
            kv_heads(query_width),
            kv_heads(query_width + kv_width),
            jnp.broadcast_to(norm_attn[:, None, None], (8, HEADS, HEAD_DIM)),
        ],
        axis=2,
    ).transpose(1, 0, 2)
    head_cols = jnp.broadcast_to(head_cols[:, None], (HEADS, 8, 8, 256)).reshape(128, 8, 256)
    head_weights = lax.all_to_all(head_cols, BOTH, 0, 0, tiled=True).reshape(WIDTH, 256)
    gain_attn = head_weights[:, 192].astype(f32)[None]
    head_weights = jnp.where(jnp.arange(256)[None] < 192, head_weights, 0.0).astype(bf16)

    rows_near, rows_across = gather_near(rows)
    rows_near, cosine, sine, head_weights = tie(rows_near, cosine, sine, head_weights)
    rows_near = both_cores(rows_near)
    rows_far = [rows_across] + [send(rows_across, 0, b) for b in (1, 3, 2)]

    w_index = lax.axis_index("wshard")
    own_y, own_x = w_index // 2, w_index % 2
    expert_rows = jnp.concatenate([w_gate_up, w_down], axis=1)
    expert_pair = jnp.stack([expert_rows, send_w(expert_rows, 1, 0)])
    pair_before, pair_after = send_w(expert_pair, 0, 1), send_w(expert_pair, 0, -1)
    w_places = [((own_y - b) % 4) * 2 + (own_x ^ a) for b in range(4) for a in range(2)]

    normed_near, *qkv = project(places[:8], rows_near, head_weights, gain_attn, cosine, sine, ())
    shared = jnp.concatenate(
        [w_out, w_router, norm_ffn[:, None], jnp.zeros((8, 95), bf16)], axis=1
    )
    shared, _ = tie(shared, head_weights)
    shared = lax.all_to_all(
        jnp.broadcast_to(shared[None], (8, 8, 1152)), "wshard", 0, 0, tiled=True
    ).reshape(64, 1152)
    rows_far, normed_near, pair_before, pair_after, shared = tie(
        rows_far, normed_near, pair_before, pair_after, shared
    )
    rows_far = both_cores(rows_far)
    experts = (
        expert_pair,
        pair_before,
        pair_after,
        send_w(pair_before[0], 0, 1),
        send_w(pair_after[1], 0, -1),
    )
    normed_far, q, k, v = project(places[8:], rows_far, head_weights, gain_attn, cosine, sine, qkv)

    shared = lax.all_to_all(
        jnp.broadcast_to(shared[None], (16, 64, 1152)), "seq", 0, 0, tiled=True
    ).reshape(WIDTH, 1152)
    router_t = shared[:, WIDTH : WIDTH + EXPERTS].T
    gain_ffn = shared[:, WIDTH + EXPERTS].astype(f32)[None]
    routes_rows = jnp.pad(routes[0].T.astype(bf16), ((0, 8), (0, WIDTH - TOK)))
    upstream_rows, _ = tie(jnp.concatenate([cotangent[0], routes_rows], axis=0), normed_far)
    grad_near, grad_across = gather_near(upstream_rows)
    attended_head, attended_t, lse = attend(q, k, v, begin)
    attended_head, experts, shared, grad_near, grad_across = tie(
        attended_head, experts, shared, grad_near, grad_across
    )
    grad_near, grad_far = both_cores(grad_near), gather_far(grad_across)
    in_order = lambda halves: jnp.concatenate(
        [jnp.stack(pair, axis=1).reshape(8, *pair[0].shape[1:]) for pair in halves], axis=0
    )
    routes_all = in_order(
        [tuple(t[:, TOK : TOK + 8, :TOK] for t in half) for half in (grad_near, grad_far)]
    ).astype(i32)

    expert_range = jnp.arange(EXPERTS, dtype=i32)
    chosen = jnp.any(routes_all[:, None] == expert_range[None, :, None, None], axis=2)
    own_first = seq_index * 2
    chosen_own = jnp.any(
        routes_all[:, None] == (own_first + jnp.arange(2, dtype=i32))[None, :, None, None], axis=2
    )
    upto = (jnp.arange(TOK)[:, None] <= jnp.arange(TOK)[None, :]).astype(bf16)
    rank = jnp.einsum("bet,tu->beu", chosen_own.astype(bf16), upto, preferred_element_type=f32)
    slots = jnp.where(chosen_own, rank.astype(i32) - 1, -1)
    slot_cols = slots.transpose(0, 2, 1)
    chosen = chosen.astype(f32)

    attended = lax.all_to_all(attended_head.reshape(16, TOK, HEAD_DIM), "seq", 0, 0, tiled=True)
    hidden, normed_ffn, attended = hidden_of(attended, shared, rows, gain_ffn)
    normed_ffn, grad_near = tie(normed_ffn, grad_near)

    ffn_near, ffn_far = seq_gather(normed_ffn)
    own = jnp.stack([own_first] + w_places)
    near = run_experts(
        0, own, ffn_near, grad_near, experts, router_t, chosen, slots, slot_cols, ()
    )
    near, saved = near[:3], near[3:]
    near_terms = sum_along_z(near[0], near[1])
    far = run_experts(
        1, own, ffn_far, grad_far, experts, router_t, chosen, slots, slot_cols, saved
    )
    far, saved = far[:3], far[3:]
    moved, saved = saved[:2], saved[2:]
    far, near_terms = tie(far, near_terms)
    far_terms = sum_along_z(far[0], far[1])
    token_gate_grad = jnp.take(jnp.concatenate([near[2], far[2]], axis=0), blocks, axis=0)
    gate_grad = lax.all_to_all(token_gate_grad, "seq", 0, 0, tiled=True).reshape(EXPERTS, TOK)
    along = jnp.arange(4, dtype=i32)
    expert_grads = expert_weight_grads((own_y - along) % 4, *saved)
    far_terms, expert_grads = tie(far_terms, expert_grads)
    crossed = send(add_low(*far_terms), 1, 0)
    crossed, gate_grad, expert_grads, moved = tie(crossed, gate_grad, expert_grads, moved)

    chosen_here = jnp.any(routes[0].T[None] == expert_range[:, None, None], axis=1).astype(f32)
    hidden_grad, branch_grad, logit_grad, scaled_grad, attended_grad = hidden_back(
        near_terms, crossed, hidden, normed_ffn, gate_grad, chosen_here, router_t, cotangent[0], gain_ffn, shared
    )
    head_grad = lax.all_to_all(attended_grad, "seq", 0, 0, tiled=True).reshape(GROUP, HEAD_DIM)
    shared_grads = shared_weight_grads(attended, branch_grad, normed_ffn, logit_grad, scaled_grad)

    far_down, far_up = send_w(expert_grads[2, 0], 0, -1), send_w(expert_grads[2, 1], 0, 1)
    below = jnp.stack([add_low(expert_grads[1, 0], far_down), expert_grads[1, 1]])
    above = jnp.stack([expert_grads[3, 0], add_low(expert_grads[3, 1], far_up)])
    head_grad, shared_grads, below, above = tie(head_grad, shared_grads, below, above)
    expert_terms = (expert_grads[0], send_w(below, 0, -1), send_w(above, 0, 1))

    by_x = [t.reshape(2, 4, TOK, WIDTH).transpose(1, 0, 2, 3) for t in (moved[0], swap_cores(moved[1]))]
    moved_parts = [add_low(by_x[0][i], by_x[1][i]) for i in range(4)]
    moved_terms = [moved_parts[0]] + [
        send(moved_parts[i], 0, -b) for i, b in ((1, 1), (2, 3), (3, 2))
    ]
    shared_grads = lax.all_to_all(shared_grads.reshape(128, 8, 1152), BOTH, 0, 0, tiled=True)
    grads = attend_back(q, k, v, head_grad, attended_t, lse, begin)
    grads, moved_terms = tie(grads, moved_terms)
    moved_crossed = send(add_low(*[t[1] for t in moved_terms]), 1, 0)
    *far_part, grad_head = project_back(
        places[8:], normed_far, grads, head_weights, cosine, sine, ()
    )
    far_part, expert_terms = tie(far_part, expert_terms)
    far_terms = sum_along_z(*far_part)
    *near_part, grad_head = project_back(
        places[:8], normed_near, grads, head_weights, cosine, sine, (grad_head,)
    )
    near_part, shared_grads, moved_crossed = tie(near_part, shared_grads, moved_crossed)
    near_terms = sum_along_z(*near_part)
    grad_heads = lax.all_to_all(
        grad_head.astype(bf16).reshape(128, 8, 256), BOTH, 0, 0, tiled=True
    )
    grad_heads, far_terms = tie(grad_heads, far_terms)
    crossed = send(add_low(*far_terms), 1, 0)
    expert_grads = add_low(*expert_terms)
    kept = lax.dynamic_index_in_dim(expert_grads, own_x, 0, keepdims=False)
    sent = lax.dynamic_index_in_dim(expert_grads, 1 - own_x, 0, keepdims=False)
    expert_grads = kept.astype(f32) + send_w(sent, 1, 0).astype(f32)
    total = lambda terms: sum([t.astype(f32) for t in terms])
    output = (hidden + total([t[0] for t in moved_terms] + [moved_crossed])).astype(bf16)
    normed_grad = total(near_terms + [crossed])
    shared_grads = jnp.sum(shared_grads.astype(f32), axis=0)
    grad_heads = jnp.sum(grad_heads.reshape(16, 8, 8, 256).astype(f32), axis=1).transpose(1, 0, 2)
    kv_sum = lambda start: jnp.sum(
        grad_heads[:, :, start : start + HEAD_DIM].reshape(8, KV_HEADS, 2, HEAD_DIM), axis=2
    ).reshape(8, kv_width)
    grad_qkv = jnp.concatenate(
        [grad_heads[:, :, :HEAD_DIM].reshape(8, query_width), kv_sum(HEAD_DIM), kv_sum(2 * HEAD_DIM)],
        axis=1,
    )
    grad_norm_attn = jnp.sum(grad_qkv * w_qkv.astype(f32), axis=1) / norm_attn.astype(f32)
    inputs = rows.astype(f32)
    grad_input = hidden_grad + rms_pull(inputs, inverse_rms(inputs), gain_attn, normed_grad)
    return (
        output[None],
        grad_input[None],
        grad_norm_attn,
        grad_qkv,
        shared_grads[:, :WIDTH],
        shared_grads[:, WIDTH : WIDTH + EXPERTS],
        shared_grads[:, WIDTH + EXPERTS],
        expert_grads[:, :128],
        expert_grads[:, 128:],
    )


def solution(mesh):
    return jax.shard_map(
        local,
        mesh=mesh,
        in_specs=(
            P("wshard", "seq", None),
            P("wshard", "seq", None),
            P("wshard", None),
            P(BOTH),
            P(BOTH, None),
            P(BOTH, None),
            P(BOTH, None),
            P(BOTH),
            P("seq", "wshard", None),
            P("seq", "wshard", None),
            P("wshard", "seq", None),
        ),
        out_specs=(
            P("wshard", "seq", None),
            P("wshard", "seq", None),
            P(BOTH),
            P(BOTH, None),
            P(BOTH, None),
            P(BOTH, None),
            P(BOTH),
            P("seq", "wshard", None),
            P("seq", "wshard", None),
        ),
        check_vma=False,
    )
```

```python
import jax
import jax.numpy as jnp
from jax import lax
from jax.experimental import pallas as pl
from jax.experimental.pallas import tpu as pltpu
from jax.sharding import PartitionSpec as P

HEADS = 16
KV_HEADS = 8
HEAD_DIM = 64
EXPERTS = 32
FF = 512
PROMPT = 2048
GROUP = 3584
TOK = 224
WIDTH = 1024
SLOTS = 72
STEP_ROWS = 4 * SLOTS
ALL_ROWS = 16 * SLOTS
BLOCK = 512
VMEM_LIMIT = 60 << 20
PAY = TOK + 32

norm_eps = 1e-06
rope_base = 10000.0
masked_score = -1e30
BOTH = ("seq", "wshard")
NT = (((1,), (1,)), ((), ()))
TN = (((0,), (0,)), ((), ()))
f32 = jnp.float32
bf16 = jnp.bfloat16
i32 = jnp.int32


def place_of(x, z, core):
    return x * 8 + z * 2 + core


def shift_perm(a, b):
    return [
        (place_of(x, z, c), place_of(x ^ a, (z + b) % 4, c))
        for x in range(2)
        for z in range(4)
        for c in range(2)
    ]


CORE_PERM = [(i, i ^ 1) for i in range(16)]


def send(rows, a, b):
    return lax.ppermute(rows, "seq", shift_perm(a, b))


def swap_cores(rows):
    return lax.ppermute(rows, "seq", CORE_PERM)


def relative_places(seq_index):
    x, z, c = seq_index // 8, (seq_index // 2) % 4, seq_index % 2
    r = jnp.arange(16, dtype=i32)
    a, i, k = r // 8, (r // 2) % 4, r % 2
    shift = i ^ (i // 2)
    behind = (z - i) % 4
    places = (a ^ x) * 8 + ((z - shift) % 4) * 2 + (k ^ c)
    return places, (a ^ x) * 8 + (behind ^ (behind // 2)) * 2 + (k ^ c)


def gather_near(rows):
    return [rows] + [send(rows, 0, b) for b in (1, 3, 2)], send(rows, 1, 0)


def both_cores(parts):
    mine = jnp.stack(parts)
    return mine, swap_cores(mine)


def gather_far(across):
    return [across] + [send(across, 0, b) for b in (1, 3, 2)]


def add_low(*terms):
    return sum([t.astype(f32) for t in terms]).astype(bf16)


def sum_along_z(mine, other):
    got = swap_cores(other)
    parts = [add_low(mine[i], got[i]) for i in range(4)]
    return [parts[0]] + [send(parts[i], 0, -b) for i, b in ((1, 1), (2, 3), (3, 2))]


def send_w(rows, a, b):
    pairs = [(y * 2 + x, ((y + b) % 4) * 2 + (x ^ a)) for y in range(4) for x in range(2)]
    return lax.ppermute(rows, "wshard", pairs)


def tie(*values):
    return lax.optimization_barrier(values)


def inverse_rms(values):
    return lax.rsqrt(jnp.mean(values * values, axis=-1, keepdims=True) + norm_eps)


def rms_pull(values, scale, gain, grad):
    scaled = grad * gain
    return scale * scaled - values * (scale * scale * scale) * jnp.mean(
        scaled * values, axis=-1, keepdims=True
    )


def group_layout(lengths):
    places = jnp.arange(GROUP, dtype=i32)
    ends = jnp.cumsum(lengths)
    starts = ends - lengths
    offset_in = places - PROMPT
    segment_id = jnp.sum((offset_in[:, None] >= ends[None, :]).astype(i32), axis=1)
    segment_hot = segment_id[:, None] == jnp.arange(lengths.shape[0], dtype=i32)[None, :]
    begin = jnp.sum(jnp.where(segment_hot, starts[None, :], 0), axis=1)
    inside = offset_in >= 0
    position = jnp.where(inside, PROMPT + offset_in - begin, places)
    return position, jnp.where(inside, PROMPT + begin, 0)


def rotary_tables(position):
    half_dim = HEAD_DIM // 2
    inverse = rope_base ** (-(jnp.arange(half_dim, dtype=f32) * 2.0) / HEAD_DIM)
    angles = position[:, None] * inverse[None, :]
    cosine, sine = jnp.cos(angles), jnp.sin(angles)
    return (
        jnp.concatenate([cosine, cosine], axis=-1),
        jnp.concatenate([sine, sine], axis=-1),
    )


def turn(values):
    half_dim = HEAD_DIM // 2
    return jnp.concatenate([-values[:, half_dim:], values[:, :half_dim]], axis=-1)


def turn_back(values):
    half_dim = HEAD_DIM // 2
    return jnp.concatenate([values[:, half_dim:], -values[:, :half_dim]], axis=-1)


def project_kernel(places, mine, other, w, gain, cosine, sine, *refs):
    del places
    normed_ref, q_ref, k_ref, v_ref = refs[-4:]
    rows = jnp.where(pl.program_id(1) == 0, mine[0], other[0])
    values = rows.astype(f32)
    normed = (values * inverse_rms(values) * gain[...]).astype(bf16)
    normed_ref[0] = normed
    projected = jnp.dot(normed, w[...], preferred_element_type=f32)
    c, s = cosine[...], sine[...]
    q, k, v = projected[:, :64], projected[:, 64:128], projected[:, 128:192]
    q_ref[...] = ((q * c + turn(q) * s).astype(bf16).astype(f32) * HEAD_DIM**-0.5).astype(bf16)
    k_ref[...] = (k * c + turn(k) * s).astype(bf16)
    v_ref[...] = v.astype(bf16)


def project(places, gathered, w, gain, cosine, sine, before):
    chip = pl.BlockSpec((1, TOK, WIDTH), lambda j, k, p: (j, 0, 0))
    whole = lambda shape: pl.BlockSpec(shape, lambda j, k, p: (0,) * len(shape))
    at = pl.BlockSpec((TOK, HEAD_DIM), lambda j, k, p: (p[2 * j + k], 0))
    table = jax.ShapeDtypeStruct((GROUP, HEAD_DIM), bf16)
    return pl.pallas_call(
        project_kernel,
        grid_spec=pltpu.PrefetchScalarGridSpec(
            num_scalar_prefetch=1,
            grid=(4, 2),
            in_specs=[chip, chip, whole((WIDTH, 256)), whole((1, WIDTH)), at, at]
            + [pl.BlockSpec(memory_space=pl.ANY)] * len(before),
            out_specs=[pl.BlockSpec((1, TOK, WIDTH), lambda j, k, p: (2 * j + k, 0, 0)), at, at, at],
        ),
        out_shape=[jax.ShapeDtypeStruct((8, TOK, WIDTH), bf16), table, table, table],
        input_output_aliases={7 + i: 1 + i for i in range(len(before))},
        compiler_params=pltpu.CompilerParams(vmem_limit_bytes=VMEM_LIMIT),
        cost_estimate=pl.CostEstimate(
            flops=2 * 8 * TOK * WIDTH * 256, bytes_accessed=10 << 20, transcendentals=0
        ),
    )(places, *gathered, w, gain, cosine, sine, *before)


def project_back_kernel(places, normed, dq, dk, dv, w, cosine, sine, *refs):
    del places
    mine, other, grad = refs[-3:]
    first = (pl.program_id(0) == 0) & (pl.program_id(1) == 0)

    @pl.when(first)
    def _():
        grad[...] = jnp.zeros_like(grad) if len(refs) == 3 else refs[0][...]

    c, s = cosine[...], sine[...]
    q = dq[...].astype(bf16).astype(f32)
    k = dk[...].astype(bf16).astype(f32)
    projected = jnp.concatenate(
        [q * c + turn_back(q * s), k * c + turn_back(k * s), dv[...], jnp.zeros_like(q)], axis=1
    ).astype(bf16)
    grad[...] += lax.dot_general(normed[0], projected, TN, preferred_element_type=f32)
    part = lax.dot_general(projected, w[...], NT, preferred_element_type=f32).astype(bf16)

    @pl.when(pl.program_id(1) == 0)
    def _():
        mine[0] = part

    @pl.when(pl.program_id(1) == 1)
    def _():
        other[0] = part


def project_back(places, normed, grads, w, cosine, sine, before):
    chip = pl.BlockSpec((1, TOK, WIDTH), lambda j, k, p: (j, 0, 0))
    whole = lambda shape: pl.BlockSpec(shape, lambda j, k, p: (0,) * len(shape))
    at = pl.BlockSpec((TOK, HEAD_DIM), lambda j, k, p: (p[2 * j + k], 0))
    part = jax.ShapeDtypeStruct((4, TOK, WIDTH), bf16)
    return pl.pallas_call(
        project_back_kernel,
        grid_spec=pltpu.PrefetchScalarGridSpec(
            num_scalar_prefetch=1,
            grid=(4, 2),
            in_specs=[
                pl.BlockSpec((1, TOK, WIDTH), lambda j, k, p: (2 * j + k, 0, 0)),
                at,
                at,
                at,
                whole((WIDTH, 256)),
                at,
                at,
            ]
            + [whole((WIDTH, 256))] * len(before),
            out_specs=[chip, chip, whole((WIDTH, 256))],
        ),
        out_shape=[part, part, jax.ShapeDtypeStruct((WIDTH, 256), f32)],
        compiler_params=pltpu.CompilerParams(vmem_limit_bytes=VMEM_LIMIT),
        cost_estimate=pl.CostEstimate(
            flops=4 * 8 * TOK * WIDTH * 256, bytes_accessed=12 << 20, transcendentals=0
        ),
    )(places, normed, *grads, w, cosine, sine, *before)


def tile_mask(scores, key_start, query_start, begin):
    keys = key_start + lax.broadcasted_iota(i32, scores.shape, 0)
    queries = query_start + lax.broadcasted_iota(i32, scores.shape, 1)
    return jnp.where((keys <= queries) & (keys >= begin), scores, masked_score)


def key_ranges(i):
    first = PROMPT // BLOCK
    return jnp.where(i > first, i - 1, i), jnp.minimum(i, first)


def attend_kernel(q_ref, k_ref, v_ref, begin_ref, o_ref, ot_ref, lse_ref, vt):
    i = pl.program_id(0)

    @pl.when(i == 0)
    def _():
        vt[...] = v_ref[...].T

    q = q_ref[...]
    begin = begin_ref[...]

    def tile(j, carry, masked, n=1):
        peak, total, out = carry
        start = pl.multiple_of(j * BLOCK, BLOCK)
        at = pl.ds(start, n * BLOCK)
        s = lax.dot_general(k_ref[at, :], q, NT, preferred_element_type=f32)
        if masked:
            s = tile_mask(s, start, i * BLOCK, begin)
        higher = jnp.maximum(peak, jnp.max(s, axis=0, keepdims=True))
        p = jnp.exp(s - higher)
        fade = jnp.exp(peak - higher)
        total = total * fade + jnp.sum(p, axis=0, keepdims=True)
        out = out * fade + jnp.dot(vt[:, at], p.astype(bf16), preferred_element_type=f32)
        return higher, total, out

    carry = (
        jnp.full((1, BLOCK), masked_score, f32),
        jnp.zeros((1, BLOCK), f32),
        jnp.zeros((HEAD_DIM, BLOCK), f32),
    )
    carry = tile(i, carry, True)
    window, shared = key_ranges(i)
    carry = lax.fori_loop(window, i, lambda j, c: tile(j, c, True), carry)
    pairs = shared // 2
    carry = lax.fori_loop(0, pairs, lambda j, c: tile(2 * j, c, False, 2), carry)
    peak, total, out = lax.fori_loop(2 * pairs, shared, lambda j, c: tile(j, c, False), carry)
    ot_ref[:, pl.ds(pl.multiple_of(i * BLOCK, BLOCK), BLOCK)] = out * (1.0 / total)
    lse_ref[...] = peak + jnp.log(total)

    @pl.when(i == GROUP // BLOCK - 1)
    def _():
        for b in range(16):
            o_ref[b] = ot_ref[:, b * TOK : (b + 1) * TOK].astype(bf16)


def attend(q, k, v, begin):
    whole = lambda *shape: pl.BlockSpec(shape, lambda i: (0,) * len(shape))
    rows = pl.BlockSpec((BLOCK, HEAD_DIM), lambda i: (i, 0))
    cols = lambda n: pl.BlockSpec((n, BLOCK), lambda i: (0, i))
    return pl.pallas_call(
        attend_kernel,
        grid=(GROUP // BLOCK,),
        in_specs=[rows, whole(GROUP, HEAD_DIM), whole(GROUP, HEAD_DIM), cols(1)],
        out_specs=[whole(16, HEAD_DIM, TOK), whole(HEAD_DIM, GROUP), cols(1)],
        out_shape=[
            jax.ShapeDtypeStruct((16, HEAD_DIM, TOK), bf16),
            jax.ShapeDtypeStruct((HEAD_DIM, GROUP), f32),
            jax.ShapeDtypeStruct((1, GROUP), f32),
        ],
        scratch_shapes=[pltpu.VMEM((HEAD_DIM, GROUP), bf16)],
        compiler_params=pltpu.CompilerParams(vmem_limit_bytes=VMEM_LIMIT),
        cost_estimate=pl.CostEstimate(
            flops=2 * 27 * BLOCK * BLOCK * 512, bytes_accessed=4 << 20, transcendentals=27 * BLOCK * BLOCK
        ),
    )(q, k, v, begin)


def attend_back_kernel(q_ref, k_ref, v_ref, g_ref, ot_ref, lse_ref, begin_ref, dq_ref, dk_ref, dv_ref, kt, gt):
    i = pl.program_id(0)

    @pl.when(i == 0)
    def _():
        dk_ref[...] = jnp.zeros_like(dk_ref)
        dv_ref[...] = jnp.zeros_like(dv_ref)
        kt[...] = k_ref[...].T
        for b in range(16):
            gt[:, b * TOK : (b + 1) * TOK] = g_ref[b]

    q = q_ref[...]
    g = gt[:, pl.ds(pl.multiple_of(i * BLOCK, BLOCK), BLOCK)]
    begin = begin_ref[...]
    lse = lse_ref[...]
    inner = jnp.sum(g.astype(f32) * ot_ref[...], axis=0, keepdims=True)

    def tile(j, dq, masked, n=1):
        start = pl.multiple_of(j * BLOCK, BLOCK)
        at = pl.ds(start, n * BLOCK)
        s = lax.dot_general(k_ref[at, :], q, NT, preferred_element_type=f32)
        if masked:
            s = tile_mask(s, start, i * BLOCK, begin)
        p = jnp.exp(s - lse)
        dp = jnp.dot(v_ref[at, :], g, preferred_element_type=f32)
        ds = (p * (dp - inner)).astype(bf16)
        dv_ref[at, :] += lax.dot_general(p.astype(bf16), g, NT, preferred_element_type=f32)
        dk_ref[at, :] += jnp.dot(ds, q, preferred_element_type=f32)
        return dq + jnp.dot(kt[:, at], ds, preferred_element_type=f32)

    dq = tile(i, jnp.zeros((HEAD_DIM, BLOCK), f32), True)
    window, shared = key_ranges(i)
    dq = lax.fori_loop(window, i, lambda j, c: tile(j, c, True), dq)
    pairs = shared // 2
    dq = lax.fori_loop(0, pairs, lambda j, c: tile(2 * j, c, False, 2), dq)
    dq = lax.fori_loop(2 * pairs, shared, lambda j, c: tile(j, c, False), dq)
    dq_ref[...] = dq.T * HEAD_DIM**-0.5


def attend_back(q, k, v, g, ot, lse, begin):
    whole = lambda *shape: pl.BlockSpec(shape, lambda i: (0,) * len(shape))
    rows = pl.BlockSpec((BLOCK, HEAD_DIM), lambda i: (i, 0))
    cols = lambda n: pl.BlockSpec((n, BLOCK), lambda i: (0, i))
    out = jax.ShapeDtypeStruct((GROUP, HEAD_DIM), f32)
    return pl.pallas_call(
        attend_back_kernel,
        grid=(GROUP // BLOCK,),
        in_specs=[rows, whole(GROUP, HEAD_DIM), whole(GROUP, HEAD_DIM), whole(16, HEAD_DIM, TOK), cols(HEAD_DIM), cols(1), cols(1)],
        out_specs=[rows, whole(GROUP, HEAD_DIM), whole(GROUP, HEAD_DIM)],
        out_shape=[out, out, out],
        scratch_shapes=[pltpu.VMEM((HEAD_DIM, GROUP), bf16), pltpu.VMEM((HEAD_DIM, GROUP), bf16)],
        compiler_params=pltpu.CompilerParams(vmem_limit_bytes=VMEM_LIMIT),
        cost_estimate=pl.CostEstimate(
            flops=5 * 27 * BLOCK * BLOCK * 512, bytes_accessed=8 << 20, transcendentals=27 * BLOCK * BLOCK
        ),
    )(q, k, v, g, ot, lse, begin)


SHARDS = [(0, 0, 0), (0, 1, 1), (1, 0, 2), (1, 1, 3), (2, 0, 6), (2, 1, 7), (3, None, 4), (4, None, 5)]
N_SHARDS = 5


def experts_kernel(
    own_ref, ffn_mine, ffn_other, g_mine, g_other, routes_mine, routes_other, router_ref, *refs
):
    shards = refs[:N_SHARDS]
    routed_mine, routed_other, moved_mine, moved_other = refs[-10:-6]
    x_ref, dh_ref, act_ref, dy_ref, w_ref, sem = refs[-6:]
    own = own_ref[0]

    @pl.when(pl.program_id(0) == 0)
    def _():
        copies = []
        for n, (shard, a, r) in enumerate(SHARDS):
            source = shards[shard] if a is None else shards[shard].at[a]
            for e in range(2):
                place = own_ref[1 + r]
                copies.append(pltpu.make_async_copy(source.at[e], w_ref.at[e, place], sem.at[n, e]))
        for copy in copies:
            copy.start()
        for copy in copies:
            copy.wait()

    expert_rows = lax.broadcasted_iota(i32, (EXPERTS, TOK), 0)
    slot_rows = lax.broadcasted_iota(i32, (SLOTS, TOK), 0).astype(f32)
    upto = (
        lax.broadcasted_iota(i32, (TOK, TOK), 0) <= lax.broadcasted_iota(i32, (TOK, TOK), 1)
    ).astype(f32).astype(bf16)
    slot_cols = []
    gate_grads = [jnp.zeros((EXPERTS, WIDTH), f32) for _ in range(4)]
    payload_rows = lax.broadcasted_iota(i32, (EXPERTS, WIDTH), 0)
    gate_rows = [[], []]
    picks = [[], []]
    picked_rows = [[], []]
    picked_grads = [[], []]
    blocks = [(ffn_mine, g_mine, routes_mine, 0), (ffn_other, g_other, routes_other, 0)]
    blocks = blocks + [(*refs_of[:3], 1) for refs_of in blocks]
    for rows_ref, grads_ref, routes_ref, n in blocks:
        rows, grads = rows_ref[n], grads_ref[n]
        routes = routes_ref[n][:8, :TOK].astype(f32).astype(i32)
        chosen = expert_rows == routes[0:1]
        for j in range(1, 8):
            chosen = chosen | (expert_rows == routes[j : j + 1])
        named = [jnp.max((routes == own + e).astype(f32), axis=0, keepdims=True) for e in range(2)]
        named = jnp.concatenate(named + [jnp.zeros((6, TOK), f32)], axis=0)
        rank = jnp.dot(named.astype(bf16), upto, preferred_element_type=f32)
        slots = jnp.where(named > 0, rank - 1.0, -1.0)
        slot_cols.append(slots.T)
        logits = lax.dot_general(router_ref[...], rows, NT, preferred_element_type=f32)
        peak = jnp.max(jnp.where(chosen, logits, masked_score), axis=0, keepdims=True)
        raised = jnp.where(chosen, jnp.exp(jnp.minimum(logits - peak, 0.0)), 0.0)
        gates = raised / jnp.sum(raised, axis=0, keepdims=True)
        for e in range(2):
            gate_rows[e].append(
                jnp.sum(jnp.where(expert_rows == own + e, gates, 0.0), axis=0, keepdims=True)
            )
            pick = (slots[e : e + 1] == slot_rows).astype(f32)
            picks[e].append(pick)
            low = pick.astype(bf16)
            picked_rows[e].append(jnp.dot(low, rows, preferred_element_type=f32))
            picked_grads[e].append(jnp.dot(low, grads, preferred_element_type=f32))
    moved, routed = [], []
    for e in range(2):
        w_gate_up = w_ref[e, :, :128, :].reshape(WIDTH, 2 * FF)
        w_down = w_ref[e, :, 128:, :].reshape(FF, WIDTH)
        x = jnp.concatenate(picked_rows[e], axis=0).astype(bf16)
        gate = jnp.concatenate(
            [jnp.sum(p * r, axis=1, keepdims=True) for p, r in zip(picks[e], gate_rows[e])], axis=0
        )
        grads = jnp.concatenate(picked_grads[e], axis=0)
        dy = (gate * grads).astype(bf16)
        mixed = jnp.dot(x, w_gate_up, preferred_element_type=f32)
        dact = lax.dot_general(dy, w_down, NT, preferred_element_type=f32)
        gate_part, up_part = mixed[:, :FF], mixed[:, FF:]
        sigma = 1.0 / (1.0 + jnp.exp(-gate_part))
        silu = gate_part * sigma
        act = (silu * up_part).astype(bf16)
        dh = jnp.concatenate(
            [dact * up_part * (sigma + silu * (1.0 - sigma)), dact * silu], axis=1
        ).astype(bf16)
        x_ref[e] = x
        dy_ref[e] = dy
        act_ref[e] = act
        dh_ref[e] = dh
        returned = jnp.dot(act, w_down, preferred_element_type=f32).astype(bf16).astype(f32)
        dgate = jnp.sum(returned * grads, axis=1, keepdims=True)
        for b in range(4):
            grad = jnp.sum(
                picks[e][b] * dgate[b * SLOTS : (b + 1) * SLOTS], axis=0, keepdims=True
            )
            high = grad.astype(bf16).astype(f32)
            gap = jnp.zeros((1, 256 - TOK), f32)
            wide = jnp.concatenate([high, gap, grad - high, gap, jnp.zeros((1, WIDTH - 512), f32)], axis=1)
            gate_grads[b] = gate_grads[b] + jnp.where(payload_rows == own + e, wide, 0.0)
        moved.append(gate * returned)
        routed.append(lax.dot_general(dh, w_gate_up, NT, preferred_element_type=f32))
    columns = lax.broadcasted_iota(i32, (TOK, 2 * SLOTS), 1).astype(f32)
    outs = [(routed_mine, moved_mine, 0), (routed_other, moved_other, 0), (routed_mine, moved_mine, 1), (routed_other, moved_other, 1)]
    for b, (routed_ref, moved_ref, n) in enumerate(outs):
        first, second = slot_cols[b][:, 0:1], slot_cols[b][:, 1:2]
        back = ((columns == first) | ((columns == second + SLOTS) & (second >= 0))).astype(f32).astype(bf16)
        at = slice(b * SLOTS, (b + 1) * SLOTS)
        for terms, ref in ((routed, routed_ref), (moved, moved_ref)):
            joined = jnp.concatenate([terms[0][at], terms[1][at]], axis=0).astype(bf16)
            ref[n, :TOK, :] = jnp.dot(back, joined, preferred_element_type=f32).astype(bf16)
        routed_ref[n, TOK:, :] = gate_grads[b].astype(bf16)


def run_experts(half, own, ffn, grads, weights, router, before):
    pair = pl.BlockSpec((2, TOK, WIDTH), lambda i, o: (i, 0, 0))
    pair_of_all = pl.BlockSpec((2, TOK, WIDTH), lambda i, o: (i + 2 * half, 0, 0))
    whole = lambda shape: pl.BlockSpec(shape, lambda i, o: (0,) * len(shape))
    routes = pl.BlockSpec((2, 16, 256), lambda i, o: (i, TOK // 16, 0))
    summed = pl.BlockSpec((2, PAY, WIDTH), lambda i, o: (i, 0, 0))
    kept = lambda n: pl.BlockSpec((2, STEP_ROWS, n), lambda i, o: (0, i + 2 * half, 0))
    part = jax.ShapeDtypeStruct((4, PAY, WIDTH), bf16)
    keep = lambda n: jax.ShapeDtypeStruct((2, ALL_ROWS, n), bf16)
    return pl.pallas_call(
        experts_kernel,
        grid_spec=pltpu.PrefetchScalarGridSpec(
            num_scalar_prefetch=1,
            grid=(2,),
            in_specs=[
                pair,
                pair,
                pair,
                pair,
                routes,
                routes,
                whole((EXPERTS, WIDTH)),
            ]
            + [pl.BlockSpec(memory_space=pl.ANY)] * (N_SHARDS + len(before)),
            out_specs=[
                summed,
                summed,
                pair_of_all,
                pair_of_all,
                kept(WIDTH),
                kept(2 * FF),
                kept(FF),
                kept(WIDTH),
            ],
            scratch_shapes=[
                pltpu.VMEM((2, 8, 192, 1024), bf16),
                pltpu.SemaphoreType.DMA((8, 2)),
            ],
        ),
        out_shape=[
            part,
            part,
            jax.ShapeDtypeStruct((8, TOK, WIDTH), bf16),
            jax.ShapeDtypeStruct((8, TOK, WIDTH), bf16),
            keep(WIDTH),
            keep(2 * FF),
            keep(FF),
            keep(WIDTH),
        ],
        input_output_aliases={8 + N_SHARDS + i: 2 + i for i in range(len(before))},
        compiler_params=pltpu.CompilerParams(vmem_limit_bytes=VMEM_LIMIT),
        cost_estimate=pl.CostEstimate(
            flops=14 << 30, bytes_accessed=24 << 20, transcendentals=8 * SLOTS * 2 * FF
        ),
    )(own, *ffn, *grads, *grads, router, *weights, *before)


def expert_grads_kernel(order, x_ref, dh_ref, act_ref, dy_ref, out_ref):
    del order
    up = lax.dot_general(x_ref[0], dh_ref[0], TN, preferred_element_type=f32)
    down = lax.dot_general(act_ref[0], dy_ref[0], TN, preferred_element_type=f32)
    out_ref[0, :, 0, :128, :] = up.astype(bf16).reshape(2, 128, 2 * FF)
    out_ref[0, :, 0, 128:, :] = down.astype(bf16).reshape(2, 64, WIDTH)


def expert_weight_grads(order, x, dh, act, dy):
    return pl.pallas_call(
        expert_grads_kernel,
        grid_spec=pltpu.PrefetchScalarGridSpec(
            num_scalar_prefetch=1,
            grid=(2, 4),
            in_specs=[
                pl.BlockSpec((1, ALL_ROWS, 256), lambda e, i, o: (e, 0, i)),
                pl.BlockSpec((1, ALL_ROWS, 2 * FF), lambda e, i, o: (e, 0, 0)),
                pl.BlockSpec((1, ALL_ROWS, 128), lambda e, i, o: (e, 0, i)),
                pl.BlockSpec((1, ALL_ROWS, WIDTH), lambda e, i, o: (e, 0, 0)),
            ],
            out_specs=pl.BlockSpec((1, 2, 1, 192, 1024), lambda e, i, o: (o[i], 0, e, 0, 0)),
        ),
        out_shape=jax.ShapeDtypeStruct((4, 2, 2, 192, 1024), bf16),
        compiler_params=pltpu.CompilerParams(vmem_limit_bytes=VMEM_LIMIT),
        cost_estimate=pl.CostEstimate(flops=8 << 30, bytes_accessed=14 << 20, transcendentals=0),
    )(order, x, dh, act, dy)


def hidden_kernel(att_ref, w_ref, rows_ref, gain_ref, hidden_ref, normed_ref):
    att = att_ref[...].reshape(WIDTH, TOK)
    hidden = rows_ref[...].astype(f32) + lax.dot_general(
        att, w_ref[:, :WIDTH], TN, preferred_element_type=f32
    )
    hidden_ref[...] = hidden
    normed_ref[...] = (hidden * inverse_rms(hidden) * gain_ref[...]).astype(bf16)


def hidden_of(attended, shared, rows, gain):
    return pl.pallas_call(
        hidden_kernel,
        out_shape=[
            jax.ShapeDtypeStruct((TOK, WIDTH), f32),
            jax.ShapeDtypeStruct((TOK, WIDTH), bf16),
        ],
        compiler_params=pltpu.CompilerParams(vmem_limit_bytes=VMEM_LIMIT),
        cost_estimate=pl.CostEstimate(
            flops=2 * TOK * WIDTH * WIDTH, bytes_accessed=5 << 20, transcendentals=0
        ),
    )(attended, shared, rows, gain)


def hidden_back_kernel(
    t0, t1, t2, t3, crossed, hidden_ref, normed_ref, chosen_ref, router_ref, g_ref, gain_ref,
    w_ref, hidden_grad_ref, branch_ref, logit_ref, scaled_ref, att_ref
):
    chosen = chosen_ref[...] > 0
    logits = lax.dot_general(router_ref[...], normed_ref[...], NT, preferred_element_type=f32)
    peak = jnp.max(jnp.where(chosen, logits, masked_score), axis=0, keepdims=True)
    raised = jnp.where(chosen, jnp.exp(jnp.minimum(logits - peak, 0.0)), 0.0)
    gates = raised / jnp.sum(raised, axis=0, keepdims=True)
    summed = t0[...].astype(f32)
    for term in (t1, t2, t3, crossed):
        summed = summed + term[...].astype(f32)
    gate_grad = summed[TOK:, :TOK] + summed[TOK:, 256 : 256 + TOK]
    logit_grad = gates * (gate_grad - jnp.sum(gates * gate_grad, axis=0, keepdims=True))
    logit_grad = logit_grad.astype(bf16)
    logit_ref[...] = logit_grad
    normed_grad = summed[:TOK] + lax.dot_general(
        logit_grad, router_ref[...], TN, preferred_element_type=f32
    )
    hidden = hidden_ref[...]
    scale = inverse_rms(hidden)
    scaled_ref[...] = (normed_grad * hidden * scale).astype(bf16)
    hidden_grad = g_ref[...].astype(f32) + rms_pull(hidden, scale, gain_ref[...], normed_grad)
    hidden_grad_ref[...] = hidden_grad
    branch = hidden_grad.astype(bf16)
    branch_ref[...] = branch
    att = lax.dot_general(w_ref[:, :WIDTH], branch, NT, preferred_element_type=f32)
    att_ref[...] = att.astype(bf16).reshape(HEADS, HEAD_DIM, TOK)


def hidden_back(terms, crossed, hidden, normed, chosen, router_t, g, gain, shared):
    wide = lambda t: jax.ShapeDtypeStruct((TOK, WIDTH), t)
    return pl.pallas_call(
        hidden_back_kernel,
        out_shape=[
            wide(f32),
            wide(bf16),
            jax.ShapeDtypeStruct((EXPERTS, TOK), bf16),
            wide(bf16),
            jax.ShapeDtypeStruct((HEADS, HEAD_DIM, TOK), bf16),
        ],
        compiler_params=pltpu.CompilerParams(vmem_limit_bytes=VMEM_LIMIT),
        cost_estimate=pl.CostEstimate(
            flops=2 * TOK * WIDTH * WIDTH, bytes_accessed=8 << 20, transcendentals=0
        ),
    )(*terms, crossed, hidden, normed, chosen, router_t, g, gain, shared)


def shared_grads_kernel(att_ref, branch_ref, normed_ref, logit_ref, scaled_ref, out_ref):
    att = att_ref[...].reshape(WIDTH, TOK)
    out_ref[:, :WIDTH] = jnp.dot(att, branch_ref[...], preferred_element_type=f32).astype(bf16)
    over_tokens = (((0,), (1,)), ((), ()))
    logit = jnp.concatenate([logit_ref[...], jnp.zeros((96, TOK), bf16)], axis=0)
    ones = (lax.broadcasted_iota(i32, (128, TOK), 0) == EXPERTS).astype(f32).astype(bf16)
    out_ref[:, WIDTH:] = (
        lax.dot_general(normed_ref[...], logit, over_tokens, preferred_element_type=f32)
        + lax.dot_general(scaled_ref[...], ones, over_tokens, preferred_element_type=f32)
    ).astype(bf16)


def shared_weight_grads(att, branch, normed, logit_grad, scaled):
    return pl.pallas_call(
        shared_grads_kernel,
        out_shape=jax.ShapeDtypeStruct((WIDTH, 1152), bf16),
        compiler_params=pltpu.CompilerParams(vmem_limit_bytes=VMEM_LIMIT),
        cost_estimate=pl.CostEstimate(
            flops=2 * TOK * WIDTH * 1280, bytes_accessed=5 << 20, transcendentals=0
        ),
    )(att, branch, normed, logit_grad, scaled)


def local(
    tokens,
    routes,
    cont_lengths,
    norm_attn,
    w_qkv,
    w_out,
    w_router,
    norm_ffn,
    w_gate_up,
    w_down,
    cotangent,
):
    seq_index = lax.axis_index("seq")
    places, blocks = relative_places(seq_index)
    rows = tokens[0]
    query_width = HEADS * HEAD_DIM
    kv_width = KV_HEADS * HEAD_DIM

    position, begin = group_layout(cont_lengths[0])
    begin = begin[None]
    cosine, sine = rotary_tables(position.astype(f32))
    kv_heads = lambda start: jnp.repeat(
        w_qkv[:, start : start + kv_width].reshape(8, KV_HEADS, HEAD_DIM), 2, axis=1
    )
    head_cols = jnp.concatenate(
        [
            w_qkv[:, :query_width].reshape(8, HEADS, HEAD_DIM),
            kv_heads(query_width),
            kv_heads(query_width + kv_width),
            jnp.broadcast_to(norm_attn[:, None, None], (8, HEADS, HEAD_DIM)),
        ],
        axis=2,
    ).transpose(1, 0, 2)
    head_cols = jnp.broadcast_to(head_cols[:, None], (HEADS, 8, 8, 256)).reshape(128, 8, 256)
    head_weights = lax.all_to_all(head_cols, BOTH, 0, 0, tiled=True).reshape(WIDTH, 256)
    gain_attn = head_weights[:, 192].astype(f32)[None]
    head_weights = jnp.where(jnp.arange(256)[None] < 192, head_weights, 0.0).astype(bf16)

    rows_near, rows_across = gather_near(rows)
    rows_near, _, cosine, sine, head_weights = tie(
        rows_near, rows_across, cosine, sine, head_weights
    )
    rows_near, rows_far = both_cores(rows_near), gather_far(rows_across)

    w_index = lax.axis_index("wshard")
    own_y, own_x = w_index // 2, w_index % 2
    expert_rows = jnp.concatenate([w_gate_up, w_down], axis=1)
    expert_pair = jnp.stack([expert_rows, send_w(expert_rows, 1, 0)])
    pair_before, pair_after = send_w(expert_pair, 0, 1), send_w(expert_pair, 0, -1)
    w_places = [((own_y - b) % 4) * 2 + (own_x ^ a) for b in range(4) for a in range(2)]

    normed_near, *qkv = project(places[:8], rows_near, head_weights, gain_attn, cosine, sine, ())
    shared = jnp.concatenate(
        [w_out, w_router, norm_ffn[:, None], jnp.zeros((8, 95), bf16)], axis=1
    )
    shared, _ = tie(shared, head_weights)
    shared = lax.all_to_all(
        jnp.broadcast_to(shared[None], (8, 8, 1152)), "wshard", 0, 0, tiled=True
    ).reshape(64, 1152)
    rows_far, normed_near, shared = tie(rows_far, normed_near, shared)
    rows_far = both_cores(rows_far)
    normed_far, q, k, v = project(places[8:], rows_far, head_weights, gain_attn, cosine, sine, qkv)

    shared = lax.all_to_all(
        jnp.broadcast_to(shared[None], (16, 64, 1152)), "seq", 0, 0, tiled=True
    ).reshape(WIDTH, 1152)
    router_t = shared[:, WIDTH : WIDTH + EXPERTS].T
    gain_ffn = shared[:, WIDTH + EXPERTS].astype(f32)[None]
    routes_rows = jnp.pad(routes[0].T.astype(bf16), ((0, 8), (0, WIDTH - TOK)))
    upstream_rows, _ = tie(jnp.concatenate([cotangent[0], routes_rows], axis=0), normed_far)
    grad_near, grad_across = gather_near(upstream_rows)
    attended_head, attended_t, lse = attend(q, k, v, begin)
    attended_head, shared, grad_near, grad_across, pair_before, pair_after = tie(
        attended_head, shared, grad_near, grad_across, pair_before, pair_after
    )
    grad_near, grad_far = both_cores(grad_near), gather_far(grad_across)
    experts = (
        expert_pair,
        pair_before,
        pair_after,
        send_w(pair_before[0], 0, 1),
        send_w(pair_after[1], 0, -1),
    )
    attended = lax.all_to_all(attended_head, "seq", 0, 0, tiled=True)
    hidden, normed_ffn = hidden_of(attended, shared, rows, gain_ffn)
    normed_ffn, grad_far, experts = tie(normed_ffn, grad_far, experts)
    grad_far = both_cores(grad_far)

    ffn_near, ffn_across = gather_near(normed_ffn)
    ffn_near, _ = tie(ffn_near, ffn_across)
    ffn_near, ffn_far = both_cores(ffn_near), gather_far(ffn_across)
    own = jnp.stack([seq_index * 2] + w_places)
    near = run_experts(0, own, ffn_near, grad_near, experts, router_t, ())
    near_terms = sum_along_z(*near[:2])
    ffn_far = both_cores(ffn_far)
    far = run_experts(1, own, ffn_far, grad_far, experts, router_t, near[2:])
    far, near_terms = tie(far, near_terms)
    moved, saved = far[2:4], far[4:]
    far_terms = sum_along_z(*far[:2])
    along = jnp.arange(4, dtype=i32)
    expert_grads = expert_weight_grads((own_y - along) % 4, *saved)
    moved_other = swap_cores(moved[1])
    far_terms, expert_grads, moved_other = tie(far_terms, expert_grads, moved_other)
    crossed = send(add_low(*far_terms), 1, 0)
    by_x = [t.reshape(2, 4, TOK, WIDTH) for t in (moved[0], moved_other)]
    moved_parts = [add_low(by_x[0][:, i], by_x[1][:, i]) for i in range(4)]
    moved_terms = [moved_parts[0]] + [
        send(moved_parts[i], 0, -b) for i, b in ((1, 1), (2, 3), (3, 2))
    ]

    expert_range = jnp.arange(EXPERTS, dtype=i32)
    chosen_here = jnp.any(routes[0].T[None] == expert_range[:, None, None], axis=1).astype(f32)
    hidden_grad, branch_grad, logit_grad, scaled_grad, attended_grad = hidden_back(
        near_terms, crossed, hidden, normed_ffn, chosen_here, router_t, cotangent[0], gain_ffn, shared
    )
    branch_grad, expert_grads = tie(branch_grad, expert_grads)
    head_grad = lax.all_to_all(attended_grad, "seq", 0, 0, tiled=True)
    shared_grads = shared_weight_grads(attended, branch_grad, normed_ffn, logit_grad, scaled_grad)

    far_down, far_up = send_w(expert_grads[2, 0], 0, -1), send_w(expert_grads[2, 1], 0, 1)
    below = jnp.stack([add_low(expert_grads[1, 0], far_down), expert_grads[1, 1]])
    above = jnp.stack([expert_grads[3, 0], add_low(expert_grads[3, 1], far_up)])
    head_grad, shared_grads, below, above = tie(head_grad, shared_grads, below, above)
    expert_terms = (expert_grads[0], send_w(below, 0, -1), send_w(above, 0, 1))
    shared_grads = lax.all_to_all(
        shared_grads.reshape(16, 8, 8, 1152), "wshard", 1, 1, tiled=True
    )
    grads = attend_back(q, k, v, head_grad, attended_t, lse, begin)
    grads, moved_terms, expert_terms = tie(grads, moved_terms, expert_terms)
    moved_crossed = send(add_low(*[t[1] for t in moved_terms]), 1, 0)
    *far_part, grad_head = project_back(
        places[8:], normed_far, grads, head_weights, cosine, sine, ()
    )
    far_terms = sum_along_z(*far_part)
    *near_part, grad_head = project_back(
        places[:8], normed_near, grads, head_weights, cosine, sine, (grad_head,)
    )
    near_part, moved_crossed, shared_grads = tie(near_part, moved_crossed, shared_grads)
    near_terms = sum_along_z(*near_part)
    shared_grads = jnp.sum(shared_grads.astype(f32), axis=1).astype(bf16)
    shared_grads = lax.all_to_all(shared_grads, "seq", 0, 0, tiled=True)
    grad_heads = lax.all_to_all(
        grad_head.astype(bf16).reshape(128, 8, 256), BOTH, 0, 0, tiled=True
    )
    crossed = send(add_low(*far_terms), 1, 0)
    crossed, grad_heads = tie(crossed, grad_heads)
    expert_grads = add_low(*expert_terms)
    kept = lax.dynamic_index_in_dim(expert_grads, own_x, 0, keepdims=False)
    sent = lax.dynamic_index_in_dim(expert_grads, 1 - own_x, 0, keepdims=False)
    expert_grads = kept.astype(f32) + send_w(sent, 1, 0).astype(f32)
    total = lambda terms: sum([t.astype(f32) for t in terms])
    output = (hidden + total([t[0] for t in moved_terms] + [moved_crossed])).astype(bf16)
    normed_grad = total(near_terms + [crossed])
    shared_grads = jnp.sum(shared_grads.astype(f32), axis=0)
    grad_heads = jnp.sum(grad_heads.reshape(16, 8, 8, 256).astype(f32), axis=1).transpose(1, 0, 2)
    kv_sum = lambda start: jnp.sum(
        grad_heads[:, :, start : start + HEAD_DIM].reshape(8, KV_HEADS, 2, HEAD_DIM), axis=2
    ).reshape(8, kv_width)
    grad_qkv = jnp.concatenate(
        [grad_heads[:, :, :HEAD_DIM].reshape(8, query_width), kv_sum(HEAD_DIM), kv_sum(2 * HEAD_DIM)],
        axis=1,
    )
    grad_norm_attn = jnp.sum(grad_qkv * w_qkv.astype(f32), axis=1) / norm_attn.astype(f32)
    inputs = rows.astype(f32)
    grad_input = hidden_grad + rms_pull(inputs, inverse_rms(inputs), gain_attn, normed_grad)
    return (
        output[None],
        grad_input[None],
        grad_norm_attn,
        grad_qkv,
        shared_grads[:, :WIDTH],
        shared_grads[:, WIDTH : WIDTH + EXPERTS],
        shared_grads[:, WIDTH + EXPERTS],
        expert_grads[:, :128],
        expert_grads[:, 128:],
    )


def solution(mesh):
    return jax.shard_map(
        local,
        mesh=mesh,
        in_specs=(
            P("wshard", "seq", None),
            P("wshard", "seq", None),
            P("wshard", None),
            P(BOTH),
            P(BOTH, None),
            P(BOTH, None),
            P(BOTH, None),
            P(BOTH),
            P("seq", "wshard", None),
            P("seq", "wshard", None),
            P("wshard", "seq", None),
        ),
        out_specs=(
            P("wshard", "seq", None),
            P("wshard", "seq", None),
            P(BOTH),
            P(BOTH, None),
            P(BOTH, None),
            P(BOTH, None),
            P(BOTH),
            P("seq", "wshard", None),
            P("seq", "wshard", None),
        ),
        check_vma=False,
    )
```

```python
import jax
import jax.numpy as jnp
from jax import lax
from jax.experimental import pallas as pl
from jax.experimental.pallas import tpu as pltpu
from jax.sharding import PartitionSpec as P

HEADS = 16
KV_HEADS = 8
HEAD_DIM = 64
EXPERTS = 32
FF = 512
PROMPT = 2048
GROUP = 3584
TOK = 224
WIDTH = 1024
SLOTS = 72
STEP_ROWS = 4 * SLOTS
ALL_ROWS = 16 * SLOTS
BLOCK = 512
VMEM_LIMIT = 60 << 20
PAY = TOK + 32

norm_eps = 1e-06
rope_base = 10000.0
masked_score = -1e30
BOTH = ("seq", "wshard")
NT = (((1,), (1,)), ((), ()))
TN = (((0,), (0,)), ((), ()))
f32 = jnp.float32
bf16 = jnp.bfloat16
i32 = jnp.int32


def place_of(x, z, core):
    return x * 8 + z * 2 + core


def shift_perm(a, b):
    return [
        (place_of(x, z, c), place_of(x ^ a, (z + b) % 4, c))
        for x in range(2)
        for z in range(4)
        for c in range(2)
    ]


CORE_PERM = [(i, i ^ 1) for i in range(16)]


def send(rows, a, b):
    return lax.ppermute(rows, "seq", shift_perm(a, b))


def swap_cores(rows):
    return lax.ppermute(rows, "seq", CORE_PERM)


def relative_places(seq_index):
    x, z, c = seq_index // 8, (seq_index // 2) % 4, seq_index % 2
    r = jnp.arange(16, dtype=i32)
    a, i, k = r // 8, (r // 2) % 4, r % 2
    shift = i ^ (i // 2)
    behind = (z - i) % 4
    places = (a ^ x) * 8 + ((z - shift) % 4) * 2 + (k ^ c)
    return places, (a ^ x) * 8 + (behind ^ (behind // 2)) * 2 + (k ^ c)


def gather_near(rows):
    return [rows] + [send(rows, 0, b) for b in (1, 3, 2)], send(rows, 1, 0)


def both_cores(parts):
    mine = jnp.stack(parts)
    return mine, swap_cores(mine)


def gather_far(across):
    return [across] + [send(across, 0, b) for b in (1, 3, 2)]


def add_low(*terms):
    return sum([t.astype(f32) for t in terms]).astype(bf16)


def sum_along_z(mine, other):
    return send_along_z(chip_parts(mine, swap_cores(other)))


def chip_parts(mine, got):
    return [add_low(mine[i], got[i]) for i in range(4)]


def send_along_z(parts):
    return [parts[0]] + [send(parts[i], 0, -b) for i, b in ((1, 1), (2, 3), (3, 2))]


def swap_x(rows):
    return lax.ppermute(rows, "wshard", [(w, w ^ 1) for w in range(8)])


ALONG_Y = [[y * 2 + x for y in range(4)] for x in range(2)]


def tie(*values):
    return lax.optimization_barrier(values)


def inverse_rms(values):
    return lax.rsqrt(jnp.mean(values * values, axis=-1, keepdims=True) + norm_eps)


def rms_pull(values, scale, gain, grad):
    scaled = grad * gain
    return scale * scaled - values * (scale * scale * scale) * jnp.mean(
        scaled * values, axis=-1, keepdims=True
    )


def group_layout(lengths):
    places = jnp.arange(GROUP, dtype=i32)
    ends = jnp.cumsum(lengths)
    starts = ends - lengths
    offset_in = places - PROMPT
    segment_id = jnp.sum((offset_in[:, None] >= ends[None, :]).astype(i32), axis=1)
    segment_hot = segment_id[:, None] == jnp.arange(lengths.shape[0], dtype=i32)[None, :]
    begin = jnp.sum(jnp.where(segment_hot, starts[None, :], 0), axis=1)
    inside = offset_in >= 0
    position = jnp.where(inside, PROMPT + offset_in - begin, places)
    return position, jnp.where(inside, PROMPT + begin, 0)


def rotary_table(position):
    half_dim = HEAD_DIM // 2
    inverse = rope_base ** (-(jnp.arange(half_dim, dtype=f32) * 2.0) / HEAD_DIM)
    angles = position[:, None] * inverse[None, :]
    cosine, sine = jnp.cos(angles), jnp.sin(angles)
    return jnp.concatenate([cosine, cosine, sine, sine], axis=-1)


def turn(values):
    half_dim = HEAD_DIM // 2
    return jnp.concatenate([-values[:, half_dim:], values[:, :half_dim]], axis=-1)


def turn_back(values):
    half_dim = HEAD_DIM // 2
    return jnp.concatenate([values[:, half_dim:], -values[:, :half_dim]], axis=-1)


def project_kernel(places, mine, other, w, gain, table, *refs):
    out = refs[-1]
    j = pl.program_id(0)

    if len(refs) > 1:

        @pl.when(j == 0)
        def _():
            out[...] = refs[0][...]

    for k, ref in enumerate((mine, other)):
        at = pl.ds(pl.multiple_of(places[2 * j + k] * TOK, TOK), TOK)
        rows = ref[0].astype(f32)
        normed = (rows * inverse_rms(rows) * gain[...]).astype(bf16)
        projected = jnp.dot(normed, w[...], preferred_element_type=f32)
        c, s = table[at, :HEAD_DIM], table[at, HEAD_DIM:]
        q, k, v = projected[:, :64], projected[:, 64:128], projected[:, 128:]
        q = (q * c + turn(q) * s).astype(bf16).astype(f32) * HEAD_DIM**-0.5
        out[at, :] = jnp.concatenate([q, k * c + turn(k) * s, v], axis=1).astype(bf16)


def project(places, gathered, w, gain, table, before):
    chip = pl.BlockSpec((1, TOK, WIDTH), lambda j, p: (j, 0, 0))
    whole = lambda *shape: pl.BlockSpec(shape, lambda j, p: (0,) * len(shape))
    return pl.pallas_call(
        project_kernel,
        grid_spec=pltpu.PrefetchScalarGridSpec(
            num_scalar_prefetch=1,
            grid=(4,),
            in_specs=[chip, chip, whole(WIDTH, 256), whole(1, WIDTH), whole(GROUP, 128)]
            + [whole(GROUP, 256)] * len(before),
            out_specs=whole(GROUP, 256),
        ),
        out_shape=jax.ShapeDtypeStruct((GROUP, 256), bf16),
        compiler_params=pltpu.CompilerParams(vmem_limit_bytes=VMEM_LIMIT),
        cost_estimate=pl.CostEstimate(
            flops=2 * 8 * TOK * WIDTH * 256, bytes_accessed=10 << 20, transcendentals=0
        ),
    )(places, *gathered, w, gain, table, *before)


def project_back_kernel(places, first, second, w, mine, other):
    del places
    mine[0] = lax.dot_general(first[...], w[...], NT, preferred_element_type=f32).astype(bf16)
    other[0] = lax.dot_general(second[...], w[...], NT, preferred_element_type=f32).astype(bf16)


def project_back(places, projected_grad, w):
    chip = pl.BlockSpec((1, TOK, WIDTH), lambda j, p: (j, 0, 0))
    at = lambda k: pl.BlockSpec((TOK, 256), lambda j, p: (p[2 * j + k], 0))
    part = jax.ShapeDtypeStruct((4, TOK, WIDTH), bf16)
    return pl.pallas_call(
        project_back_kernel,
        grid_spec=pltpu.PrefetchScalarGridSpec(
            num_scalar_prefetch=1,
            grid=(4,),
            in_specs=[at(0), at(1), pl.BlockSpec((WIDTH, 256), lambda j, p: (0, 0))],
            out_specs=[chip, chip],
        ),
        out_shape=[part, part],
        compiler_params=pltpu.CompilerParams(vmem_limit_bytes=VMEM_LIMIT),
        cost_estimate=pl.CostEstimate(
            flops=2 * 8 * TOK * WIDTH * 256, bytes_accessed=5 << 20, transcendentals=0
        ),
    )(places, projected_grad, projected_grad, w)


def head_grad_kernel(places, near_mine, near_other, far_mine, far_other, gain, first, second, out, total):
    del places
    j = pl.program_id(0)

    @pl.when(j == 0)
    def _():
        total[...] = jnp.zeros_like(total)

    for near, far, projected in ((near_mine, far_mine, first), (near_other, far_other, second)):
        rows = jnp.where(j < 4, near[0], far[0]).astype(f32)
        normed = (rows * inverse_rms(rows) * gain[...]).astype(bf16)
        total[...] += lax.dot_general(normed, projected[...], TN, preferred_element_type=f32)

    @pl.when(j == 7)
    def _():
        out[...] = total[...].astype(bf16)


def head_weight_grad(places, near, far, gain, projected_grad):
    near_chip = pl.BlockSpec((1, TOK, WIDTH), lambda j, p: (jnp.minimum(j, 3), 0, 0))
    far_chip = pl.BlockSpec((1, TOK, WIDTH), lambda j, p: (jnp.maximum(j - 4, 0), 0, 0))
    at = lambda k: pl.BlockSpec((TOK, 256), lambda j, p: (p[2 * j + k], 0))
    return pl.pallas_call(
        head_grad_kernel,
        grid_spec=pltpu.PrefetchScalarGridSpec(
            num_scalar_prefetch=1,
            grid=(8,),
            in_specs=[
                near_chip,
                near_chip,
                far_chip,
                far_chip,
                pl.BlockSpec((1, WIDTH), lambda j, p: (0, 0)),
                at(0),
                at(1),
            ],
            out_specs=pl.BlockSpec((WIDTH, 256), lambda j, p: (0, 0)),
            scratch_shapes=[pltpu.VMEM((WIDTH, 256), f32)],
        ),
        out_shape=jax.ShapeDtypeStruct((WIDTH, 256), bf16),
        compiler_params=pltpu.CompilerParams(vmem_limit_bytes=VMEM_LIMIT),
        cost_estimate=pl.CostEstimate(
            flops=2 * 16 * TOK * WIDTH * 256, bytes_accessed=10 << 20, transcendentals=0
        ),
    )(places, *near, *far, gain, projected_grad, projected_grad)


def tile_mask(scores, key_start, query_start, begin):
    keys = key_start + lax.broadcasted_iota(i32, scores.shape, 0)
    queries = query_start + lax.broadcasted_iota(i32, scores.shape, 1)
    return jnp.where((keys <= queries) & (keys >= begin), scores, masked_score)


def key_ranges(i):
    first = PROMPT // BLOCK
    return jnp.where(i > first, i - 1, i), jnp.minimum(i, first)


def attend_kernel(qkv_ref, begin_ref, o_ref, ot_ref, lse_ref, keys, vt):
    i = pl.program_id(0)
    here = pl.ds(pl.multiple_of(i * BLOCK, BLOCK), BLOCK)

    @pl.when(i == 0)
    def _():
        keys[...] = qkv_ref[:, 64:128]
        vt[...] = qkv_ref[:, 128:192].T

    q = qkv_ref[here, :64]
    begin = begin_ref[...]

    def tile(j, carry, masked, n=1):
        peak, total, out = carry
        start = pl.multiple_of(j * BLOCK, BLOCK)
        at = pl.ds(start, n * BLOCK)
        s = lax.dot_general(keys[at, :], q, NT, preferred_element_type=f32)
        if masked:
            s = tile_mask(s, start, i * BLOCK, begin)
        higher = jnp.maximum(peak, jnp.max(s, axis=0, keepdims=True))
        p = jnp.exp(s - higher)
        fade = jnp.exp(peak - higher)
        total = total * fade + jnp.sum(p, axis=0, keepdims=True)
        out = out * fade + jnp.dot(vt[:, at], p.astype(bf16), preferred_element_type=f32)
        return higher, total, out

    carry = (
        jnp.full((1, BLOCK), masked_score, f32),
        jnp.zeros((1, BLOCK), f32),
        jnp.zeros((HEAD_DIM, BLOCK), f32),
    )
    carry = tile(i, carry, True)
    window, shared = key_ranges(i)
    carry = lax.fori_loop(window, i, lambda j, c: tile(j, c, True), carry)
    pairs = shared // 2
    carry = lax.fori_loop(0, pairs, lambda j, c: tile(2 * j, c, False, 2), carry)
    peak, total, out = lax.fori_loop(2 * pairs, shared, lambda j, c: tile(j, c, False), carry)
    ot_ref[:, here] = out * (1.0 / total)
    lse_ref[...] = peak + jnp.log(total)

    @pl.when(i == GROUP // BLOCK - 1)
    def _():
        for b in range(16):
            o_ref[b] = ot_ref[:, b * TOK : (b + 1) * TOK].astype(bf16)


def attend(qkv, begin):
    whole = lambda *shape: pl.BlockSpec(shape, lambda i: (0,) * len(shape))
    cols = lambda n: pl.BlockSpec((n, BLOCK), lambda i: (0, i))
    return pl.pallas_call(
        attend_kernel,
        grid=(GROUP // BLOCK,),
        in_specs=[whole(GROUP, 256), cols(1)],
        out_specs=[whole(16, HEAD_DIM, TOK), whole(HEAD_DIM, GROUP), cols(1)],
        out_shape=[
            jax.ShapeDtypeStruct((16, HEAD_DIM, TOK), bf16),
            jax.ShapeDtypeStruct((HEAD_DIM, GROUP), f32),
            jax.ShapeDtypeStruct((1, GROUP), f32),
        ],
        scratch_shapes=[
            pltpu.VMEM((GROUP, HEAD_DIM), bf16),
            pltpu.VMEM((HEAD_DIM, GROUP), bf16),
        ],
        compiler_params=pltpu.CompilerParams(vmem_limit_bytes=VMEM_LIMIT),
        cost_estimate=pl.CostEstimate(
            flops=2 * 27 * BLOCK * BLOCK * 512, bytes_accessed=4 << 20, transcendentals=27 * BLOCK * BLOCK
        ),
    )(qkv, begin)


def attend_back_kernel(
    qkv_ref, g_ref, ot_ref, lse_ref, begin_ref, table, out_ref, keys, values, kt, gt, dq, dk, dv
):
    i = pl.program_id(0)
    here = pl.ds(pl.multiple_of(i * BLOCK, BLOCK), BLOCK)

    @pl.when(i == 0)
    def _():
        dk[...] = jnp.zeros_like(dk)
        dv[...] = jnp.zeros_like(dv)
        keys[...] = qkv_ref[:, 64:128]
        values[...] = qkv_ref[:, 128:192]
        kt[...] = qkv_ref[:, 64:128].T
        for b in range(16):
            gt[:, b * TOK : (b + 1) * TOK] = g_ref[b]

    q = qkv_ref[here, :64]
    g = gt[:, here]
    begin = begin_ref[...]
    lse = lse_ref[...]
    inner = jnp.sum(g.astype(f32) * ot_ref[...], axis=0, keepdims=True)

    def tile(j, dq, masked, n=1):
        start = pl.multiple_of(j * BLOCK, BLOCK)
        at = pl.ds(start, n * BLOCK)
        s = lax.dot_general(keys[at, :], q, NT, preferred_element_type=f32)
        if masked:
            s = tile_mask(s, start, i * BLOCK, begin)
        p = jnp.exp(s - lse)
        dp = jnp.dot(values[at, :], g, preferred_element_type=f32)
        ds = (p * (dp - inner)).astype(bf16)
        dv[at, :] += lax.dot_general(p.astype(bf16), g, NT, preferred_element_type=f32)
        dk[at, :] += jnp.dot(ds, q, preferred_element_type=f32)
        return dq + jnp.dot(kt[:, at], ds, preferred_element_type=f32)

    dqt = tile(i, jnp.zeros((HEAD_DIM, BLOCK), f32), True)
    window, shared = key_ranges(i)
    dqt = lax.fori_loop(window, i, lambda j, c: tile(j, c, True), dqt)
    pairs = shared // 2
    dqt = lax.fori_loop(0, pairs, lambda j, c: tile(2 * j, c, False, 2), dqt)
    dqt = lax.fori_loop(2 * pairs, shared, lambda j, c: tile(j, c, False), dqt)
    dq[here, :] = dqt.T * HEAD_DIM**-0.5

    @pl.when(i == GROUP // BLOCK - 1)
    def _():
        def back(b, _):
            at = pl.ds(pl.multiple_of(b * BLOCK, BLOCK), BLOCK)
            c, s = table[at, :HEAD_DIM], table[at, HEAD_DIM:]
            q, k = dq[at, :].astype(bf16).astype(f32), dk[at, :].astype(bf16).astype(f32)
            parts = [q * c + turn_back(q * s), k * c + turn_back(k * s), dv[at, :], jnp.zeros_like(q)]
            out_ref[at, :] = jnp.concatenate(parts, axis=1).astype(bf16)
            return 0

        lax.fori_loop(0, GROUP // BLOCK, back, 0)


def attend_back(qkv, g, ot, lse, begin, table):
    whole = lambda *shape: pl.BlockSpec(shape, lambda i: (0,) * len(shape))
    cols = lambda n: pl.BlockSpec((n, BLOCK), lambda i: (0, i))
    return pl.pallas_call(
        attend_back_kernel,
        grid=(GROUP // BLOCK,),
        in_specs=[
            whole(GROUP, 256),
            whole(16, HEAD_DIM, TOK),
            cols(HEAD_DIM),
            cols(1),
            cols(1),
            whole(GROUP, 128),
        ],
        out_specs=whole(GROUP, 256),
        out_shape=jax.ShapeDtypeStruct((GROUP, 256), bf16),
        scratch_shapes=[
            pltpu.VMEM((GROUP, HEAD_DIM), bf16),
            pltpu.VMEM((GROUP, HEAD_DIM), bf16),
            pltpu.VMEM((HEAD_DIM, GROUP), bf16),
            pltpu.VMEM((HEAD_DIM, GROUP), bf16),
            pltpu.VMEM((GROUP, HEAD_DIM), f32),
            pltpu.VMEM((GROUP, HEAD_DIM), f32),
            pltpu.VMEM((GROUP, HEAD_DIM), f32),
        ],
        compiler_params=pltpu.CompilerParams(vmem_limit_bytes=VMEM_LIMIT),
        cost_estimate=pl.CostEstimate(
            flops=5 * 27 * BLOCK * BLOCK * 512, bytes_accessed=8 << 20, transcendentals=27 * BLOCK * BLOCK
        ),
    )(qkv, g, ot, lse, begin, table)


def experts_kernel(
    own_ref, ffn_mine, ffn_other, g_mine, g_other, routes_mine, routes_other, router_ref, own_w, across_w, *refs
):
    routed_mine, routed_other, moved_mine, moved_other = refs[-10:-6]
    x_ref, dh_ref, act_ref, dy_ref, w_ref, sem = refs[-6:]
    own = own_ref[0]

    @pl.when(pl.program_id(0) == 0)
    def _():
        copies = [
            pltpu.make_async_copy(shards.at[y, e], w_ref.at[e, 2 * y + (own_ref[1] ^ a)], sem.at[a, y, e])
            for a, shards in enumerate((own_w, across_w))
            for y in range(4)
            for e in range(2)
        ]
        for copy in copies:
            copy.start()
        for copy in copies:
            copy.wait()

    expert_rows = lax.broadcasted_iota(i32, (EXPERTS, TOK), 0)
    slot_rows = lax.broadcasted_iota(i32, (SLOTS, TOK), 0).astype(f32)
    upto = (
        lax.broadcasted_iota(i32, (TOK, TOK), 0) <= lax.broadcasted_iota(i32, (TOK, TOK), 1)
    ).astype(f32).astype(bf16)
    slot_cols = []
    gate_grads = [jnp.zeros((EXPERTS, WIDTH), f32) for _ in range(4)]
    payload_rows = lax.broadcasted_iota(i32, (EXPERTS, WIDTH), 0)
    gate_rows = [[], []]
    picks = [[], []]
    picked_rows = [[], []]
    picked_grads = [[], []]
    blocks = [(ffn_mine, g_mine, routes_mine, 0), (ffn_other, g_other, routes_other, 0)]
    blocks = blocks + [(*refs_of[:3], 1) for refs_of in blocks]
    for rows_ref, grads_ref, routes_ref, n in blocks:
        rows, grads = rows_ref[n], grads_ref[n]
        routes = routes_ref[n][:8, :TOK].astype(f32).astype(i32)
        chosen = expert_rows == routes[0:1]
        for j in range(1, 8):
            chosen = chosen | (expert_rows == routes[j : j + 1])
        named = [jnp.max((routes == own + e).astype(f32), axis=0, keepdims=True) for e in range(2)]
        named = jnp.concatenate(named + [jnp.zeros((6, TOK), f32)], axis=0)
        rank = jnp.dot(named.astype(bf16), upto, preferred_element_type=f32)
        slots = jnp.where(named > 0, rank - 1.0, -1.0)
        slot_cols.append(slots.T)
        logits = lax.dot_general(router_ref[...], rows, NT, preferred_element_type=f32)
        peak = jnp.max(jnp.where(chosen, logits, masked_score), axis=0, keepdims=True)
        raised = jnp.where(chosen, jnp.exp(jnp.minimum(logits - peak, 0.0)), 0.0)
        gates = raised / jnp.sum(raised, axis=0, keepdims=True)
        for e in range(2):
            gate_rows[e].append(
                jnp.sum(jnp.where(expert_rows == own + e, gates, 0.0), axis=0, keepdims=True)
            )
            pick = (slots[e : e + 1] == slot_rows).astype(f32)
            picks[e].append(pick)
            low = pick.astype(bf16)
            picked_rows[e].append(jnp.dot(low, rows, preferred_element_type=f32))
            picked_grads[e].append(jnp.dot(low, grads, preferred_element_type=f32))
    moved, routed = [], []
    for e in range(2):
        w_gate_up = w_ref[e, :, :128, :].reshape(WIDTH, 2 * FF)
        w_down = w_ref[e, :, 128:, :].reshape(FF, WIDTH)
        x = jnp.concatenate(picked_rows[e], axis=0).astype(bf16)
        gate = jnp.concatenate(
            [jnp.sum(p * r, axis=1, keepdims=True) for p, r in zip(picks[e], gate_rows[e])], axis=0
        )
        grads = jnp.concatenate(picked_grads[e], axis=0)
        dy = (gate * grads).astype(bf16)
        mixed = jnp.dot(x, w_gate_up, preferred_element_type=f32)
        dact = lax.dot_general(dy, w_down, NT, preferred_element_type=f32)
        gate_part, up_part = mixed[:, :FF], mixed[:, FF:]
        sigma = 1.0 / (1.0 + jnp.exp(-gate_part))
        silu = gate_part * sigma
        act = (silu * up_part).astype(bf16)
        dh = jnp.concatenate(
            [dact * up_part * (sigma + silu * (1.0 - sigma)), dact * silu], axis=1
        ).astype(bf16)
        x_ref[e] = x
        dy_ref[e] = dy
        act_ref[e] = act
        dh_ref[e] = dh
        returned = jnp.dot(act, w_down, preferred_element_type=f32).astype(bf16).astype(f32)
        dgate = jnp.sum(returned * grads, axis=1, keepdims=True)
        for b in range(4):
            grad = jnp.sum(
                picks[e][b] * dgate[b * SLOTS : (b + 1) * SLOTS], axis=0, keepdims=True
            )
            high = grad.astype(bf16).astype(f32)
            gap = jnp.zeros((1, 256 - TOK), f32)
            wide = jnp.concatenate([high, gap, grad - high, gap, jnp.zeros((1, WIDTH - 512), f32)], axis=1)
            gate_grads[b] = gate_grads[b] + jnp.where(payload_rows == own + e, wide, 0.0)
        moved.append(gate * returned)
        routed.append(lax.dot_general(dh, w_gate_up, NT, preferred_element_type=f32))
    columns = lax.broadcasted_iota(i32, (TOK, 2 * SLOTS), 1).astype(f32)
    outs = [(routed_mine, moved_mine, 0), (routed_other, moved_other, 0), (routed_mine, moved_mine, 1), (routed_other, moved_other, 1)]
    for b, (routed_ref, moved_ref, n) in enumerate(outs):
        first, second = slot_cols[b][:, 0:1], slot_cols[b][:, 1:2]
        back = ((columns == first) | ((columns == second + SLOTS) & (second >= 0))).astype(f32).astype(bf16)
        at = slice(b * SLOTS, (b + 1) * SLOTS)
        for terms, ref in ((routed, routed_ref), (moved, moved_ref)):
            joined = jnp.concatenate([terms[0][at], terms[1][at]], axis=0).astype(bf16)
            ref[n, :TOK, :] = jnp.dot(back, joined, preferred_element_type=f32).astype(bf16)
        routed_ref[n, TOK:, :] = gate_grads[b].astype(bf16)


def run_experts(half, own, ffn, grads, weights, router, before):
    pair = pl.BlockSpec((2, TOK, WIDTH), lambda i, o: (i, 0, 0))
    pair_of_all = pl.BlockSpec((2, TOK, WIDTH), lambda i, o: (i + 2 * half, 0, 0))
    whole = lambda shape: pl.BlockSpec(shape, lambda i, o: (0,) * len(shape))
    routes = pl.BlockSpec((2, 16, 256), lambda i, o: (i, TOK // 16, 0))
    summed = pl.BlockSpec((2, PAY, WIDTH), lambda i, o: (i, 0, 0))
    kept = lambda n: pl.BlockSpec((2, STEP_ROWS, n), lambda i, o: (0, i + 2 * half, 0))
    part = jax.ShapeDtypeStruct((4, PAY, WIDTH), bf16)
    keep = lambda n: jax.ShapeDtypeStruct((2, ALL_ROWS, n), bf16)
    return pl.pallas_call(
        experts_kernel,
        grid_spec=pltpu.PrefetchScalarGridSpec(
            num_scalar_prefetch=1,
            grid=(2,),
            in_specs=[
                pair,
                pair,
                pair,
                pair,
                routes,
                routes,
                whole((EXPERTS, WIDTH)),
            ]
            + [pl.BlockSpec(memory_space=pl.ANY)] * (2 + len(before)),
            out_specs=[
                summed,
                summed,
                pair_of_all,
                pair_of_all,
                kept(WIDTH),
                kept(2 * FF),
                kept(FF),
                kept(WIDTH),
            ],
            scratch_shapes=[
                pltpu.VMEM((2, 8, 192, 1024), bf16),
                pltpu.SemaphoreType.DMA((2, 4, 2)),
            ],
        ),
        out_shape=[
            part,
            part,
            jax.ShapeDtypeStruct((8, TOK, WIDTH), bf16),
            jax.ShapeDtypeStruct((8, TOK, WIDTH), bf16),
            keep(WIDTH),
            keep(2 * FF),
            keep(FF),
            keep(WIDTH),
        ],
        input_output_aliases={10 + i: 2 + i for i in range(len(before))},
        compiler_params=pltpu.CompilerParams(vmem_limit_bytes=VMEM_LIMIT),
        cost_estimate=pl.CostEstimate(
            flops=14 << 30, bytes_accessed=24 << 20, transcendentals=8 * SLOTS * 2 * FF
        ),
    )(own, *ffn, *grads, *grads, router, *weights, *before)


def expert_grads_kernel(x_ref, dh_ref, act_ref, dy_ref, out_ref):
    up = lax.dot_general(x_ref[0], dh_ref[0], TN, preferred_element_type=f32)
    down = lax.dot_general(act_ref[0], dy_ref[0], TN, preferred_element_type=f32)
    out_ref[0, :, 0, :128, :] = up.astype(bf16).reshape(2, 128, 2 * FF)
    out_ref[0, :, 0, 128:, :] = down.astype(bf16).reshape(2, 64, WIDTH)


def expert_weight_grads(x, dh, act, dy):
    return pl.pallas_call(
        expert_grads_kernel,
        grid=(2, 4),
        in_specs=[
            pl.BlockSpec((1, ALL_ROWS, 256), lambda e, i: (e, 0, i)),
            pl.BlockSpec((1, ALL_ROWS, 2 * FF), lambda e, i: (e, 0, 0)),
            pl.BlockSpec((1, ALL_ROWS, 128), lambda e, i: (e, 0, i)),
            pl.BlockSpec((1, ALL_ROWS, WIDTH), lambda e, i: (e, 0, 0)),
        ],
        out_specs=pl.BlockSpec((1, 2, 1, 192, 1024), lambda e, i: (i, 0, e, 0, 0)),
        out_shape=jax.ShapeDtypeStruct((4, 2, 2, 192, 1024), bf16),
        compiler_params=pltpu.CompilerParams(vmem_limit_bytes=VMEM_LIMIT),
        cost_estimate=pl.CostEstimate(flops=8 << 30, bytes_accessed=14 << 20, transcendentals=0),
    )(x, dh, act, dy)


def hidden_kernel(att_ref, w_ref, rows_ref, gain_ref, hidden_ref, normed_ref):
    att = att_ref[...].reshape(WIDTH, TOK)
    hidden = rows_ref[...].astype(f32) + lax.dot_general(
        att, w_ref[:, :WIDTH], TN, preferred_element_type=f32
    )
    hidden_ref[...] = hidden
    normed_ref[...] = (hidden * inverse_rms(hidden) * gain_ref[...]).astype(bf16)


def hidden_of(attended, shared, rows, gain):
    return pl.pallas_call(
        hidden_kernel,
        out_shape=[
            jax.ShapeDtypeStruct((TOK, WIDTH), f32),
            jax.ShapeDtypeStruct((TOK, WIDTH), bf16),
        ],
        compiler_params=pltpu.CompilerParams(vmem_limit_bytes=VMEM_LIMIT),
        cost_estimate=pl.CostEstimate(
            flops=2 * TOK * WIDTH * WIDTH, bytes_accessed=5 << 20, transcendentals=0
        ),
    )(attended, shared, rows, gain)


def hidden_back_kernel(
    t0, t1, t2, t3, crossed, hidden_ref, normed_ref, chosen_ref, router_ref, g_ref, gain_ref,
    w_ref, hidden_grad_ref, branch_ref, logit_ref, scaled_ref, att_ref
):
    chosen = chosen_ref[...] > 0
    logits = lax.dot_general(router_ref[...], normed_ref[...], NT, preferred_element_type=f32)
    peak = jnp.max(jnp.where(chosen, logits, masked_score), axis=0, keepdims=True)
    raised = jnp.where(chosen, jnp.exp(jnp.minimum(logits - peak, 0.0)), 0.0)
    gates = raised / jnp.sum(raised, axis=0, keepdims=True)
    summed = t0[...].astype(f32)
    for term in (t1, t2, t3, crossed):
        summed = summed + term[...].astype(f32)
    gate_grad = summed[TOK:, :TOK] + summed[TOK:, 256 : 256 + TOK]
    logit_grad = gates * (gate_grad - jnp.sum(gates * gate_grad, axis=0, keepdims=True))
    logit_grad = logit_grad.astype(bf16)
    logit_ref[...] = logit_grad
    normed_grad = summed[:TOK] + lax.dot_general(
        logit_grad, router_ref[...], TN, preferred_element_type=f32
    )
    hidden = hidden_ref[...]
    scale = inverse_rms(hidden)
    scaled_ref[...] = (normed_grad * hidden * scale).astype(bf16)
    hidden_grad = g_ref[...].astype(f32) + rms_pull(hidden, scale, gain_ref[...], normed_grad)
    hidden_grad_ref[...] = hidden_grad
    branch = hidden_grad.astype(bf16)
    branch_ref[...] = branch
    att = lax.dot_general(w_ref[:, :WIDTH], branch, NT, preferred_element_type=f32)
    att_ref[...] = att.astype(bf16).reshape(HEADS, HEAD_DIM, TOK)


def hidden_back(terms, crossed, hidden, normed, chosen, router_t, g, gain, shared):
    wide = lambda t: jax.ShapeDtypeStruct((TOK, WIDTH), t)
    return pl.pallas_call(
        hidden_back_kernel,
        out_shape=[
            wide(f32),
            wide(bf16),
            jax.ShapeDtypeStruct((EXPERTS, TOK), bf16),
            wide(bf16),
            jax.ShapeDtypeStruct((HEADS, HEAD_DIM, TOK), bf16),
        ],
        compiler_params=pltpu.CompilerParams(vmem_limit_bytes=VMEM_LIMIT),
        cost_estimate=pl.CostEstimate(
            flops=2 * TOK * WIDTH * WIDTH, bytes_accessed=8 << 20, transcendentals=0
        ),
    )(*terms, crossed, hidden, normed, chosen, router_t, g, gain, shared)


def shared_grads_kernel(att_ref, branch_ref, normed_ref, logit_ref, scaled_ref, out_ref):
    att = att_ref[...].reshape(WIDTH, TOK)
    out_ref[:, :WIDTH] = jnp.dot(att, branch_ref[...], preferred_element_type=f32).astype(bf16)
    over_tokens = (((0,), (1,)), ((), ()))
    logit = jnp.concatenate([logit_ref[...], jnp.zeros((96, TOK), bf16)], axis=0)
    ones = (lax.broadcasted_iota(i32, (128, TOK), 0) == EXPERTS).astype(f32).astype(bf16)
    out_ref[:, WIDTH:] = (
        lax.dot_general(normed_ref[...], logit, over_tokens, preferred_element_type=f32)
        + lax.dot_general(scaled_ref[...], ones, over_tokens, preferred_element_type=f32)
    ).astype(bf16)


def shared_weight_grads(att, branch, normed, logit_grad, scaled):
    return pl.pallas_call(
        shared_grads_kernel,
        out_shape=jax.ShapeDtypeStruct((WIDTH, 1152), bf16),
        compiler_params=pltpu.CompilerParams(vmem_limit_bytes=VMEM_LIMIT),
        cost_estimate=pl.CostEstimate(
            flops=2 * TOK * WIDTH * 1280, bytes_accessed=5 << 20, transcendentals=0
        ),
    )(att, branch, normed, logit_grad, scaled)


def local(
    tokens,
    routes,
    cont_lengths,
    norm_attn,
    w_qkv,
    w_out,
    w_router,
    norm_ffn,
    w_gate_up,
    w_down,
    cotangent,
):
    seq_index = lax.axis_index("seq")
    places, blocks = relative_places(seq_index)
    rows = tokens[0]
    query_width = HEADS * HEAD_DIM
    kv_width = KV_HEADS * HEAD_DIM

    position, begin = group_layout(cont_lengths[0])
    begin = begin[None]
    table = rotary_table(position.astype(f32))
    kv_heads = lambda start: jnp.repeat(
        w_qkv[:, start : start + kv_width].reshape(8, KV_HEADS, HEAD_DIM), 2, axis=1
    )
    head_cols = jnp.concatenate(
        [
            w_qkv[:, :query_width].reshape(8, HEADS, HEAD_DIM),
            kv_heads(query_width),
            kv_heads(query_width + kv_width),
            jnp.broadcast_to(norm_attn[:, None, None], (8, HEADS, HEAD_DIM)),
        ],
        axis=2,
    ).transpose(1, 0, 2)
    head_cols = jnp.broadcast_to(head_cols[:, None], (HEADS, 8, 8, 256)).reshape(128, 8, 256)
    head_weights = lax.all_to_all(head_cols, BOTH, 0, 0, tiled=True).reshape(WIDTH, 256)
    gain_attn = head_weights[:, 192].astype(f32)[None]
    head_weights = jnp.where(jnp.arange(256)[None] < 192, head_weights, 0.0).astype(bf16)

    rows_near, rows_across = gather_near(rows)
    rows_near, _, table, head_weights = tie(rows_near, rows_across, table, head_weights)
    rows_near, rows_far = both_cores(rows_near), gather_far(rows_across)

    own_x = lax.axis_index("wshard") % 2
    expert_rows = jnp.concatenate([w_gate_up, w_down], axis=1)
    along_y = lambda t: lax.all_gather(t, "wshard", axis_index_groups=ALONG_Y, axis=0)
    experts, expert_rows = along_y(expert_rows), swap_x(expert_rows)

    qkv = project(places[:8], rows_near, head_weights, gain_attn, table, ())
    shared = jnp.concatenate(
        [w_out, w_router, norm_ffn[:, None], jnp.zeros((8, 95), bf16)], axis=1
    )
    shared, _ = tie(shared, head_weights)
    shared = lax.all_to_all(
        jnp.broadcast_to(shared[None], (8, 8, 1152)), "wshard", 0, 0, tiled=True
    ).reshape(64, 1152)
    routes_rows = jnp.pad(routes[0].T.astype(bf16), ((0, 8), (0, WIDTH - TOK)))
    upstream_rows = jnp.concatenate([cotangent[0], routes_rows], axis=0)
    rows_far, qkv, shared, upstream_rows, expert_rows = tie(
        rows_far, qkv, shared, upstream_rows, expert_rows
    )
    experts = [experts, along_y(expert_rows)]
    rows_far = both_cores(rows_far)
    grad_near = [upstream_rows] + [send(upstream_rows, 0, b) for b in (1, 3, 2)]
    qkv = project(places[8:], rows_far, head_weights, gain_attn, table, (qkv,))

    shared = lax.all_to_all(
        jnp.broadcast_to(shared[None], (16, 64, 1152)), "seq", 0, 0, tiled=True
    ).reshape(WIDTH, 1152)
    router_t = shared[:, WIDTH : WIDTH + EXPERTS].T
    gain_ffn = shared[:, WIDTH + EXPERTS].astype(f32)[None]
    attended_head, attended_t, lse = attend(qkv, begin)
    attended_head, shared, grad_near = tie(attended_head, shared, grad_near)
    grad_near = jnp.stack(grad_near)
    grad_far = send(grad_near, 1, 0)
    attended = lax.all_to_all(attended_head, "seq", 0, 0, tiled=True)
    hidden, normed_ffn = hidden_of(attended, shared, rows, gain_ffn)
    grad_near = (grad_near, swap_cores(grad_near))

    ffn_near, ffn_across = gather_near(normed_ffn)
    ffn_near, _, grad_far = tie(ffn_near, ffn_across, grad_far)
    ffn_near, ffn_far = both_cores(ffn_near), gather_far(ffn_across)
    own = jnp.stack([seq_index * 2, own_x])
    near = run_experts(0, own, ffn_near, grad_near, experts, router_t, ())
    near_terms = sum_along_z(*near[:2])
    ffn_far = both_cores(ffn_far)
    grad_far = (grad_far, swap_cores(grad_far))
    far = run_experts(1, own, ffn_far, grad_far, experts, router_t, near[2:])
    far, near_terms = tie(far, near_terms)
    moved, saved = far[2:4], far[4:]
    far_other, moved_other = tie(swap_cores(far[1]), moved[1])
    far_terms = send_along_z(chip_parts(far[0], far_other))
    expert_grads = expert_weight_grads(*saved)
    moved_other = swap_cores(moved_other)
    far_terms, expert_grads, moved_other = tie(far_terms, expert_grads, moved_other)
    crossed = send(add_low(*far_terms), 1, 0)
    by_x = [t.reshape(2, 4, TOK, WIDTH) for t in (moved[0], moved_other)]
    moved_parts = [add_low(by_x[0][:, i], by_x[1][:, i]) for i in range(4)]
    crossed, moved_parts = tie(crossed, moved_parts)

    expert_range = jnp.arange(EXPERTS, dtype=i32)
    chosen_here = jnp.any(routes[0].T[None] == expert_range[:, None, None], axis=1).astype(f32)
    hidden_grad, branch_grad, logit_grad, scaled_grad, attended_grad = hidden_back(
        near_terms, crossed, hidden, normed_ffn, chosen_here, router_t, cotangent[0], gain_ffn, shared
    )
    expert_grads = lax.psum_scatter(
        expert_grads.reshape(8, 2, 192, 1024),
        "wshard",
        axis_index_groups=ALONG_Y,
        scatter_dimension=0,
        tiled=True,
    )
    head_grad = lax.all_to_all(attended_grad, "seq", 0, 0, tiled=True)
    shared_grads = shared_weight_grads(attended, branch_grad, normed_ffn, logit_grad, scaled_grad)
    head_grad, shared_grads, moved_parts = tie(head_grad, shared_grads, moved_parts)
    moved_terms = [moved_parts[0]] + [
        send(moved_parts[i], 0, -b) for i, b in ((1, 1), (2, 3), (3, 2))
    ]

    shared_grads = lax.all_to_all(
        shared_grads.reshape(16, 8, 8, 1152), "wshard", 1, 1, tiled=True
    )
    projected_grad = attend_back(qkv, head_grad, attended_t, lse, begin, table)
    far_part = project_back(places[8:], projected_grad, head_weights)
    far_part, shared_grads, moved_terms = tie(far_part, shared_grads, moved_terms)
    far_parts = chip_parts(far_part[0], swap_cores(far_part[1]))
    near_part = project_back(places[:8], projected_grad, head_weights)
    near_part, expert_grads = tie(near_part, expert_grads)
    far_parts, projected_grad = tie(far_parts, projected_grad)
    far_terms = send_along_z(far_parts)
    near_terms = sum_along_z(*near_part)
    moved_crossed = send(add_low(*[t[1] for t in moved_terms]), 1, 0)
    shared_grads = jnp.sum(shared_grads.astype(f32), axis=1).astype(bf16)
    shared_grads = lax.all_to_all(shared_grads, "seq", 0, 0, tiled=True)
    grad_head = head_weight_grad(places, rows_near, rows_far, gain_attn, projected_grad)
    grad_heads = lax.all_to_all(grad_head.reshape(128, 8, 256), BOTH, 0, 0, tiled=True)
    crossed = send(add_low(*far_terms), 1, 0)
    crossed, near_terms, grad_heads = tie(crossed, near_terms, grad_heads)
    kept = lax.dynamic_index_in_dim(expert_grads, own_x, 0, keepdims=False)
    sent = lax.dynamic_index_in_dim(expert_grads, 1 - own_x, 0, keepdims=False)
    expert_grads = kept.astype(f32) + swap_x(sent).astype(f32)
    total = lambda terms: sum([t.astype(f32) for t in terms])
    output = (hidden + total([t[0] for t in moved_terms] + [moved_crossed])).astype(bf16)
    normed_grad = total(near_terms + [crossed])
    shared_grads = jnp.sum(shared_grads.astype(f32), axis=0)
    grad_heads = jnp.sum(grad_heads.reshape(16, 8, 8, 256).astype(f32), axis=1).transpose(1, 0, 2)
    kv_sum = lambda start: jnp.sum(
        grad_heads[:, :, start : start + HEAD_DIM].reshape(8, KV_HEADS, 2, HEAD_DIM), axis=2
    ).reshape(8, kv_width)
    grad_qkv = jnp.concatenate(
        [grad_heads[:, :, :HEAD_DIM].reshape(8, query_width), kv_sum(HEAD_DIM), kv_sum(2 * HEAD_DIM)],
        axis=1,
    )
    grad_norm_attn = jnp.sum(grad_qkv * w_qkv.astype(f32), axis=1) / norm_attn.astype(f32)
    inputs = rows.astype(f32)
    grad_input = hidden_grad + rms_pull(inputs, inverse_rms(inputs), gain_attn, normed_grad)
    return (
        output[None],
        grad_input[None],
        grad_norm_attn,
        grad_qkv,
        shared_grads[:, :WIDTH],
        shared_grads[:, WIDTH : WIDTH + EXPERTS],
        shared_grads[:, WIDTH + EXPERTS],
        expert_grads[:, :128],
        expert_grads[:, 128:],
    )


def solution(mesh):
    return jax.shard_map(
        local,
        mesh=mesh,
        in_specs=(
            P("wshard", "seq", None),
            P("wshard", "seq", None),
            P("wshard", None),
            P(BOTH),
            P(BOTH, None),
            P(BOTH, None),
            P(BOTH, None),
            P(BOTH),
            P("seq", "wshard", None),
            P("seq", "wshard", None),
            P("wshard", "seq", None),
        ),
        out_specs=(
            P("wshard", "seq", None),
            P("wshard", "seq", None),
            P(BOTH),
            P(BOTH, None),
            P(BOTH, None),
            P(BOTH, None),
            P(BOTH),
            P("seq", "wshard", None),
            P("seq", "wshard", None),
        ),
        check_vma=False,
    )
```

```python
import jax
import jax.numpy as jnp
from jax import lax
from jax.experimental import pallas as pl
from jax.experimental.pallas import tpu as pltpu
from jax.sharding import PartitionSpec as P

HEADS = 16
KV_HEADS = 8
HEAD_DIM = 64
EXPERTS = 32
FF = 512
PROMPT = 2048
GROUP = 3584
TOK = 224
WIDTH = 1024
SLOTS = 72
STEP_ROWS = 4 * SLOTS
ALL_ROWS = 16 * SLOTS
BLOCK = 512
VMEM_LIMIT = 60 << 20
PAY = TOK + 32

norm_eps = 1e-06
rope_base = 10000.0
masked_score = -1e30
BOTH = ("seq", "wshard")
NT = (((1,), (1,)), ((), ()))
TN = (((0,), (0,)), ((), ()))
f32 = jnp.float32
bf16 = jnp.bfloat16
i32 = jnp.int32


def place_of(x, z, core):
    return x * 8 + z * 2 + core


def shift_perm(a, b):
    return [
        (place_of(x, z, c), place_of(x ^ a, (z + b) % 4, c))
        for x in range(2)
        for z in range(4)
        for c in range(2)
    ]


CORE_PERM = [(i, i ^ 1) for i in range(16)]


def send(rows, a, b):
    return lax.ppermute(rows, "seq", shift_perm(a, b))


def swap_cores(rows):
    return lax.ppermute(rows, "seq", CORE_PERM)


def relative_places(seq_index):
    x, z, c = seq_index // 8, (seq_index // 2) % 4, seq_index % 2
    r = jnp.arange(16, dtype=i32)
    a, i, k = r // 8, (r // 2) % 4, r % 2
    shift = i ^ (i // 2)
    behind = (z - i) % 4
    places = (a ^ x) * 8 + ((z - shift) % 4) * 2 + (k ^ c)
    return places, (a ^ x) * 8 + (behind ^ (behind // 2)) * 2 + (k ^ c)


def gather_near(rows):
    return [rows] + [send(rows, 0, b) for b in (1, 3, 2)], send(rows, 1, 0)


def both_cores(parts):
    mine = jnp.stack(parts)
    return mine, swap_cores(mine)


def gather_far(across):
    return [across] + [send(across, 0, b) for b in (1, 3, 2)]


def add_low(*terms):
    return sum([t.astype(f32) for t in terms]).astype(bf16)


def sum_along_z(mine, other):
    return send_along_z(chip_parts(mine, swap_cores(other)))


def chip_parts(mine, got):
    return [add_low(mine[i], got[i]) for i in range(4)]


def send_along_z(parts):
    return [parts[0]] + [send(parts[i], 0, -b) for i, b in ((1, 1), (2, 3), (3, 2))]


def swap_x(rows):
    return lax.ppermute(rows, "wshard", [(w, w ^ 1) for w in range(8)])


ALONG_Y = [[y * 2 + x for y in range(4)] for x in range(2)]


def tie(*values):
    return lax.optimization_barrier(values)


def inverse_rms(values):
    return lax.rsqrt(jnp.mean(values * values, axis=-1, keepdims=True) + norm_eps)


def rms_pull(values, scale, gain, grad):
    scaled = grad * gain
    return scale * scaled - values * (scale * scale * scale) * jnp.mean(
        scaled * values, axis=-1, keepdims=True
    )


def group_layout(lengths):
    places = jnp.arange(GROUP, dtype=i32)
    ends = jnp.cumsum(lengths)
    starts = ends - lengths
    offset_in = places - PROMPT
    segment_id = jnp.sum((offset_in[:, None] >= ends[None, :]).astype(i32), axis=1)
    segment_hot = segment_id[:, None] == jnp.arange(lengths.shape[0], dtype=i32)[None, :]
    begin = jnp.sum(jnp.where(segment_hot, starts[None, :], 0), axis=1)
    inside = offset_in >= 0
    position = jnp.where(inside, PROMPT + offset_in - begin, places)
    return position, jnp.where(inside, PROMPT + begin, 0)


def rotary_table(position):
    half_dim = HEAD_DIM // 2
    inverse = rope_base ** (-((jnp.arange(2 * HEAD_DIM) % half_dim).astype(f32) * 2.0) / HEAD_DIM)
    back = jnp.where(jnp.arange(2 * HEAD_DIM) < HEAD_DIM, 0.0, 0.5 * jnp.pi).astype(f32)
    return jnp.cos(position[:, None] * inverse[None, :] - back[None, :])


def turn(values):
    half_dim = HEAD_DIM // 2
    return jnp.concatenate([-values[:, half_dim:], values[:, :half_dim]], axis=-1)


def turn_back(values):
    half_dim = HEAD_DIM // 2
    return jnp.concatenate([values[:, half_dim:], -values[:, :half_dim]], axis=-1)


def project_kernel(places, mine, other, w, gain, table, *refs):
    out = refs[-1]
    j = pl.program_id(0)

    if len(refs) > 1:

        @pl.when(j == 0)
        def _():
            out[...] = refs[0][...]

    for k, ref in enumerate((mine, other)):
        at = pl.ds(pl.multiple_of(places[2 * j + k] * TOK, TOK), TOK)
        rows = ref[0].astype(f32)
        normed = (rows * inverse_rms(rows) * gain[...]).astype(bf16)
        projected = jnp.dot(normed, w[...], preferred_element_type=f32)
        c, s = table[at, :HEAD_DIM], table[at, HEAD_DIM:]
        q, k, v = projected[:, :64], projected[:, 64:128], projected[:, 128:]
        q = (q * c + turn(q) * s).astype(bf16).astype(f32) * HEAD_DIM**-0.5
        out[at, :] = jnp.concatenate([q, k * c + turn(k) * s, v], axis=1).astype(bf16)


def project(places, gathered, w, gain, table, before):
    chip = pl.BlockSpec((1, TOK, WIDTH), lambda j, p: (j, 0, 0))
    whole = lambda *shape: pl.BlockSpec(shape, lambda j, p: (0,) * len(shape))
    return pl.pallas_call(
        project_kernel,
        grid_spec=pltpu.PrefetchScalarGridSpec(
            num_scalar_prefetch=1,
            grid=(4,),
            in_specs=[chip, chip, whole(WIDTH, 256), whole(1, WIDTH), whole(GROUP, 128)]
            + [whole(GROUP, 256)] * len(before),
            out_specs=whole(GROUP, 256),
        ),
        out_shape=jax.ShapeDtypeStruct((GROUP, 256), bf16),
        compiler_params=pltpu.CompilerParams(vmem_limit_bytes=VMEM_LIMIT),
        cost_estimate=pl.CostEstimate(
            flops=2 * 8 * TOK * WIDTH * 256, bytes_accessed=10 << 20, transcendentals=0
        ),
    )(places, *gathered, w, gain, table, *before)


def project_back_kernel(places, first, second, w, mine, other):
    del places
    mine[0] = lax.dot_general(first[...], w[...], NT, preferred_element_type=f32).astype(bf16)
    other[0] = lax.dot_general(second[...], w[...], NT, preferred_element_type=f32).astype(bf16)


def project_back(places, projected_grad, w):
    chip = pl.BlockSpec((1, TOK, WIDTH), lambda j, p: (j, 0, 0))
    at = lambda k: pl.BlockSpec((TOK, 256), lambda j, p: (p[2 * j + k], 0))
    part = jax.ShapeDtypeStruct((4, TOK, WIDTH), bf16)
    return pl.pallas_call(
        project_back_kernel,
        grid_spec=pltpu.PrefetchScalarGridSpec(
            num_scalar_prefetch=1,
            grid=(4,),
            in_specs=[at(0), at(1), pl.BlockSpec((WIDTH, 256), lambda j, p: (0, 0))],
            out_specs=[chip, chip],
        ),
        out_shape=[part, part],
        compiler_params=pltpu.CompilerParams(vmem_limit_bytes=VMEM_LIMIT),
        cost_estimate=pl.CostEstimate(
            flops=2 * 8 * TOK * WIDTH * 256, bytes_accessed=5 << 20, transcendentals=0
        ),
    )(places, projected_grad, projected_grad, w)


def head_grad_kernel(places, near_mine, near_other, far_mine, far_other, gain, first, second, out, total):
    del places
    j = pl.program_id(0)

    @pl.when(j == 0)
    def _():
        total[...] = jnp.zeros_like(total)

    for near, far, projected in ((near_mine, far_mine, first), (near_other, far_other, second)):
        rows = jnp.where(j < 4, near[0], far[0]).astype(f32)
        normed = (rows * inverse_rms(rows) * gain[...]).astype(bf16)
        total[...] += lax.dot_general(normed, projected[...], TN, preferred_element_type=f32)

    @pl.when(j == 7)
    def _():
        out[...] = total[...].astype(bf16)


def head_weight_grad(places, near, far, gain, projected_grad):
    near_chip = pl.BlockSpec((1, TOK, WIDTH), lambda j, p: (jnp.minimum(j, 3), 0, 0))
    far_chip = pl.BlockSpec((1, TOK, WIDTH), lambda j, p: (jnp.maximum(j - 4, 0), 0, 0))
    at = lambda k: pl.BlockSpec((TOK, 256), lambda j, p: (p[2 * j + k], 0))
    return pl.pallas_call(
        head_grad_kernel,
        grid_spec=pltpu.PrefetchScalarGridSpec(
            num_scalar_prefetch=1,
            grid=(8,),
            in_specs=[
                near_chip,
                near_chip,
                far_chip,
                far_chip,
                pl.BlockSpec((1, WIDTH), lambda j, p: (0, 0)),
                at(0),
                at(1),
            ],
            out_specs=pl.BlockSpec((WIDTH, 256), lambda j, p: (0, 0)),
            scratch_shapes=[pltpu.VMEM((WIDTH, 256), f32)],
        ),
        out_shape=jax.ShapeDtypeStruct((WIDTH, 256), bf16),
        compiler_params=pltpu.CompilerParams(vmem_limit_bytes=VMEM_LIMIT),
        cost_estimate=pl.CostEstimate(
            flops=2 * 16 * TOK * WIDTH * 256, bytes_accessed=10 << 20, transcendentals=0
        ),
    )(places, *near, *far, gain, projected_grad, projected_grad)


def tile_mask(scores, key_start, query_start, begin):
    keys = key_start + lax.broadcasted_iota(i32, scores.shape, 0)
    queries = query_start + lax.broadcasted_iota(i32, scores.shape, 1)
    return jnp.where((keys <= queries) & (keys >= begin), scores, masked_score)


def key_ranges(i):
    first = PROMPT // BLOCK
    return jnp.where(i > first, i - 1, i), jnp.minimum(i, first)


def attend_kernel(qkv_ref, begin_ref, o_ref, ot_ref, lse_ref, keys, vt):
    i = pl.program_id(0)
    here = pl.ds(pl.multiple_of(i * BLOCK, BLOCK), BLOCK)

    @pl.when(i == 0)
    def _():
        keys[...] = qkv_ref[:, 64:128]
        vt[...] = qkv_ref[:, 128:192].T

    q = qkv_ref[here, :64]
    begin = begin_ref[...]

    def tile(j, carry, masked, n=1):
        peak, total, out = carry
        start = pl.multiple_of(j * BLOCK, BLOCK)
        at = pl.ds(start, n * BLOCK)
        s = lax.dot_general(keys[at, :], q, NT, preferred_element_type=f32)
        if masked:
            s = tile_mask(s, start, i * BLOCK, begin)
        higher = jnp.maximum(peak, jnp.max(s, axis=0, keepdims=True))
        p = jnp.exp(s - higher)
        fade = jnp.exp(peak - higher)
        total = total * fade + jnp.sum(p, axis=0, keepdims=True)
        out = out * fade + jnp.dot(vt[:, at], p.astype(bf16), preferred_element_type=f32)
        return higher, total, out

    carry = (
        jnp.full((1, BLOCK), masked_score, f32),
        jnp.zeros((1, BLOCK), f32),
        jnp.zeros((HEAD_DIM, BLOCK), f32),
    )
    carry = tile(i, carry, True)
    window, shared = key_ranges(i)
    carry = lax.fori_loop(window, i, lambda j, c: tile(j, c, True), carry)
    pairs = shared // 2
    carry = lax.fori_loop(0, pairs, lambda j, c: tile(2 * j, c, False, 2), carry)
    peak, total, out = lax.fori_loop(2 * pairs, shared, lambda j, c: tile(j, c, False), carry)
    ot_ref[:, here] = out * (1.0 / total)
    lse_ref[...] = peak + jnp.log(total)

    @pl.when(i == GROUP // BLOCK - 1)
    def _():
        for b in range(16):
            o_ref[b] = ot_ref[:, b * TOK : (b + 1) * TOK].astype(bf16)


def attend(qkv, begin):
    whole = lambda *shape: pl.BlockSpec(shape, lambda i: (0,) * len(shape))
    cols = lambda n: pl.BlockSpec((n, BLOCK), lambda i: (0, i))
    return pl.pallas_call(
        attend_kernel,
        grid=(GROUP // BLOCK,),
        in_specs=[whole(GROUP, 256), cols(1)],
        out_specs=[whole(16, HEAD_DIM, TOK), whole(HEAD_DIM, GROUP), cols(1)],
        out_shape=[
            jax.ShapeDtypeStruct((16, HEAD_DIM, TOK), bf16),
            jax.ShapeDtypeStruct((HEAD_DIM, GROUP), f32),
            jax.ShapeDtypeStruct((1, GROUP), f32),
        ],
        scratch_shapes=[
            pltpu.VMEM((GROUP, HEAD_DIM), bf16),
            pltpu.VMEM((HEAD_DIM, GROUP), bf16),
        ],
        compiler_params=pltpu.CompilerParams(vmem_limit_bytes=VMEM_LIMIT),
        cost_estimate=pl.CostEstimate(
            flops=2 * 27 * BLOCK * BLOCK * 512, bytes_accessed=4 << 20, transcendentals=27 * BLOCK * BLOCK
        ),
    )(qkv, begin)


def attend_back_kernel(
    qkv_ref, g_ref, ot_ref, lse_ref, begin_ref, table, out_ref, keys, values, kt, gt, dq, dk, dv
):
    i = pl.program_id(0)
    here = pl.ds(pl.multiple_of(i * BLOCK, BLOCK), BLOCK)

    @pl.when(i == 0)
    def _():
        dk[...] = jnp.zeros_like(dk)
        dv[...] = jnp.zeros_like(dv)
        keys[...] = qkv_ref[:, 64:128]
        values[...] = qkv_ref[:, 128:192]
        kt[...] = qkv_ref[:, 64:128].T
        for b in range(16):
            gt[:, b * TOK : (b + 1) * TOK] = g_ref[b]

    q = qkv_ref[here, :64]
    g = gt[:, here]
    begin = begin_ref[...]
    lse = lse_ref[...]
    inner = jnp.sum(g.astype(f32) * ot_ref[...], axis=0, keepdims=True)

    def tile(j, dq, masked, n=1):
        start = pl.multiple_of(j * BLOCK, BLOCK)
        at = pl.ds(start, n * BLOCK)
        s = lax.dot_general(keys[at, :], q, NT, preferred_element_type=f32)
        if masked:
            s = tile_mask(s, start, i * BLOCK, begin)
        p = jnp.exp(s - lse)
        dp = jnp.dot(values[at, :], g, preferred_element_type=f32)
        ds = (p * (dp - inner)).astype(bf16)
        dv[at, :] += lax.dot_general(p.astype(bf16), g, NT, preferred_element_type=f32)
        dk[at, :] += jnp.dot(ds, q, preferred_element_type=f32)
        return dq + jnp.dot(kt[:, at], ds, preferred_element_type=f32)

    dqt = tile(i, jnp.zeros((HEAD_DIM, BLOCK), f32), True)
    window, shared = key_ranges(i)
    dqt = lax.fori_loop(window, i, lambda j, c: tile(j, c, True), dqt)
    pairs = shared // 2
    dqt = lax.fori_loop(0, pairs, lambda j, c: tile(2 * j, c, False, 2), dqt)
    dqt = lax.fori_loop(2 * pairs, shared, lambda j, c: tile(j, c, False), dqt)
    dq[here, :] = dqt.T * HEAD_DIM**-0.5

    @pl.when(i == GROUP // BLOCK - 1)
    def _():
        def back(b, _):
            at = pl.ds(pl.multiple_of(b * BLOCK, BLOCK), BLOCK)
            c, s = table[at, :HEAD_DIM], table[at, HEAD_DIM:]
            q, k = dq[at, :].astype(bf16).astype(f32), dk[at, :].astype(bf16).astype(f32)
            parts = [q * c + turn_back(q * s), k * c + turn_back(k * s), dv[at, :], jnp.zeros_like(q)]
            out_ref[at, :] = jnp.concatenate(parts, axis=1).astype(bf16)
            return 0

        lax.fori_loop(0, GROUP // BLOCK, back, 0)


def attend_back(qkv, g, ot, lse, begin, table):
    whole = lambda *shape: pl.BlockSpec(shape, lambda i: (0,) * len(shape))
    cols = lambda n: pl.BlockSpec((n, BLOCK), lambda i: (0, i))
    return pl.pallas_call(
        attend_back_kernel,
        grid=(GROUP // BLOCK,),
        in_specs=[
            whole(GROUP, 256),
            whole(16, HEAD_DIM, TOK),
            cols(HEAD_DIM),
            cols(1),
            cols(1),
            whole(GROUP, 128),
        ],
        out_specs=whole(GROUP, 256),
        out_shape=jax.ShapeDtypeStruct((GROUP, 256), bf16),
        scratch_shapes=[
            pltpu.VMEM((GROUP, HEAD_DIM), bf16),
            pltpu.VMEM((GROUP, HEAD_DIM), bf16),
            pltpu.VMEM((HEAD_DIM, GROUP), bf16),
            pltpu.VMEM((HEAD_DIM, GROUP), bf16),
            pltpu.VMEM((GROUP, HEAD_DIM), f32),
            pltpu.VMEM((GROUP, HEAD_DIM), f32),
            pltpu.VMEM((GROUP, HEAD_DIM), f32),
        ],
        compiler_params=pltpu.CompilerParams(vmem_limit_bytes=VMEM_LIMIT),
        cost_estimate=pl.CostEstimate(
            flops=5 * 27 * BLOCK * BLOCK * 512, bytes_accessed=8 << 20, transcendentals=27 * BLOCK * BLOCK
        ),
    )(qkv, g, ot, lse, begin, table)


def experts_kernel(
    own_ref, ffn_mine, ffn_other, g_mine, g_other, routes_mine, routes_other, router_ref, own_w, across_w, *refs
):
    routed_mine, routed_other, moved_mine, moved_other = refs[-10:-6]
    x_ref, dh_ref, act_ref, dy_ref, w_ref, sem = refs[-6:]
    own = own_ref[0]

    @pl.when(pl.program_id(0) == 0)
    def _():
        copies = [
            pltpu.make_async_copy(shards.at[y, e], w_ref.at[e, 2 * y + (own_ref[1] ^ a)], sem.at[a, y, e])
            for a, shards in enumerate((own_w, across_w))
            for y in range(4)
            for e in range(2)
        ]
        for copy in copies:
            copy.start()
        for copy in copies:
            copy.wait()

    expert_rows = lax.broadcasted_iota(i32, (EXPERTS, TOK), 0)
    slot_rows = lax.broadcasted_iota(i32, (SLOTS, TOK), 0).astype(f32)
    upto = (
        lax.broadcasted_iota(i32, (TOK, TOK), 0) <= lax.broadcasted_iota(i32, (TOK, TOK), 1)
    ).astype(f32).astype(bf16)
    slot_cols = []
    gate_grads = [jnp.zeros((EXPERTS, WIDTH), f32) for _ in range(4)]
    payload_rows = lax.broadcasted_iota(i32, (EXPERTS, WIDTH), 0)
    gate_rows = [[], []]
    picks = [[], []]
    picked_rows = [[], []]
    picked_grads = [[], []]
    blocks = [(ffn_mine, g_mine, routes_mine, 0), (ffn_other, g_other, routes_other, 0)]
    blocks = blocks + [(*refs_of[:3], 1) for refs_of in blocks]
    for rows_ref, grads_ref, routes_ref, n in blocks:
        rows, grads = rows_ref[n], grads_ref[n]
        routes = routes_ref[n][:8, :TOK].astype(f32).astype(i32)
        chosen = expert_rows == routes[0:1]
        for j in range(1, 8):
            chosen = chosen | (expert_rows == routes[j : j + 1])
        named = [jnp.max((routes == own + e).astype(f32), axis=0, keepdims=True) for e in range(2)]
        named = jnp.concatenate(named + [jnp.zeros((6, TOK), f32)], axis=0)
        rank = jnp.dot(named.astype(bf16), upto, preferred_element_type=f32)
        slots = jnp.where(named > 0, rank - 1.0, -1.0)
        slot_cols.append(slots.T)
        logits = lax.dot_general(router_ref[...], rows, NT, preferred_element_type=f32)
        peak = jnp.max(jnp.where(chosen, logits, masked_score), axis=0, keepdims=True)
        raised = jnp.where(chosen, jnp.exp(jnp.minimum(logits - peak, 0.0)), 0.0)
        gates = raised / jnp.sum(raised, axis=0, keepdims=True)
        for e in range(2):
            gate_rows[e].append(
                jnp.sum(jnp.where(expert_rows == own + e, gates, 0.0), axis=0, keepdims=True)
            )
            pick = (slots[e : e + 1] == slot_rows).astype(f32)
            picks[e].append(pick)
            low = pick.astype(bf16)
            picked_rows[e].append(jnp.dot(low, rows, preferred_element_type=f32))
            picked_grads[e].append(jnp.dot(low, grads, preferred_element_type=f32))
    moved, routed = [], []
    for e in range(2):
        w_gate_up = w_ref[e, :, :128, :].reshape(WIDTH, 2 * FF)
        w_down = w_ref[e, :, 128:, :].reshape(FF, WIDTH)
        x = jnp.concatenate(picked_rows[e], axis=0).astype(bf16)
        gate = jnp.concatenate(
            [jnp.sum(p * r, axis=1, keepdims=True) for p, r in zip(picks[e], gate_rows[e])], axis=0
        )
        grads = jnp.concatenate(picked_grads[e], axis=0)
        dy = (gate * grads).astype(bf16)
        mixed = jnp.dot(x, w_gate_up, preferred_element_type=f32)
        dact = lax.dot_general(dy, w_down, NT, preferred_element_type=f32)
        gate_part, up_part = mixed[:, :FF], mixed[:, FF:]
        sigma = 1.0 / (1.0 + jnp.exp(-gate_part))
        silu = gate_part * sigma
        act = (silu * up_part).astype(bf16)
        dh = jnp.concatenate(
            [dact * up_part * (sigma + silu * (1.0 - sigma)), dact * silu], axis=1
        ).astype(bf16)
        x_ref[e] = x
        dy_ref[e] = dy
        act_ref[e] = act
        dh_ref[e] = dh
        returned = jnp.dot(act, w_down, preferred_element_type=f32).astype(bf16).astype(f32)
        dgate = jnp.sum(returned * grads, axis=1, keepdims=True)
        for b in range(4):
            grad = jnp.sum(
                picks[e][b] * dgate[b * SLOTS : (b + 1) * SLOTS], axis=0, keepdims=True
            )
            high = grad.astype(bf16).astype(f32)
            gap = jnp.zeros((1, 256 - TOK), f32)
            wide = jnp.concatenate([high, gap, grad - high, gap, jnp.zeros((1, WIDTH - 512), f32)], axis=1)
            gate_grads[b] = gate_grads[b] + jnp.where(payload_rows == own + e, wide, 0.0)
        moved.append(gate * returned)
        routed.append(lax.dot_general(dh, w_gate_up, NT, preferred_element_type=f32))
    columns = lax.broadcasted_iota(i32, (TOK, 2 * SLOTS), 1).astype(f32)
    outs = [(routed_mine, moved_mine, 0), (routed_other, moved_other, 0), (routed_mine, moved_mine, 1), (routed_other, moved_other, 1)]
    for b, (routed_ref, moved_ref, n) in enumerate(outs):
        first, second = slot_cols[b][:, 0:1], slot_cols[b][:, 1:2]
        back = ((columns == first) | ((columns == second + SLOTS) & (second >= 0))).astype(f32).astype(bf16)
        at = slice(b * SLOTS, (b + 1) * SLOTS)
        for terms, ref in ((routed, routed_ref), (moved, moved_ref)):
            joined = jnp.concatenate([terms[0][at], terms[1][at]], axis=0).astype(bf16)
            ref[n, :TOK, :] = jnp.dot(back, joined, preferred_element_type=f32).astype(bf16)
        routed_ref[n, TOK:, :] = gate_grads[b].astype(bf16)


def run_experts(half, own, ffn, grads, weights, router, before):
    pair = pl.BlockSpec((2, TOK, WIDTH), lambda i, o: (i, 0, 0))
    pair_of_all = pl.BlockSpec((2, TOK, WIDTH), lambda i, o: (i + 2 * half, 0, 0))
    whole = lambda shape: pl.BlockSpec(shape, lambda i, o: (0,) * len(shape))
    routes = pl.BlockSpec((2, 16, 256), lambda i, o: (i, TOK // 16, 0))
    summed = pl.BlockSpec((2, PAY, WIDTH), lambda i, o: (i, 0, 0))
    kept = lambda n: pl.BlockSpec((2, STEP_ROWS, n), lambda i, o: (0, i + 2 * half, 0))
    part = jax.ShapeDtypeStruct((4, PAY, WIDTH), bf16)
    keep = lambda n: jax.ShapeDtypeStruct((2, ALL_ROWS, n), bf16)
    return pl.pallas_call(
        experts_kernel,
        grid_spec=pltpu.PrefetchScalarGridSpec(
            num_scalar_prefetch=1,
            grid=(2,),
            in_specs=[
                pair,
                pair,
                pair,
                pair,
                routes,
                routes,
                whole((EXPERTS, WIDTH)),
            ]
            + [pl.BlockSpec(memory_space=pl.ANY)] * (2 + len(before)),
            out_specs=[
                summed,
                summed,
                pair_of_all,
                pair_of_all,
                kept(WIDTH),
                kept(2 * FF),
                kept(FF),
                kept(WIDTH),
            ],
            scratch_shapes=[
                pltpu.VMEM((2, 8, 192, 1024), bf16),
                pltpu.SemaphoreType.DMA((2, 4, 2)),
            ],
        ),
        out_shape=[
            part,
            part,
            jax.ShapeDtypeStruct((8, TOK, WIDTH), bf16),
            jax.ShapeDtypeStruct((8, TOK, WIDTH), bf16),
            keep(WIDTH),
            keep(2 * FF),
            keep(FF),
            keep(WIDTH),
        ],
        input_output_aliases={10 + i: 2 + i for i in range(len(before))},
        compiler_params=pltpu.CompilerParams(vmem_limit_bytes=VMEM_LIMIT),
        cost_estimate=pl.CostEstimate(
            flops=14 << 30, bytes_accessed=24 << 20, transcendentals=8 * SLOTS * 2 * FF
        ),
    )(own, *ffn, *grads, *grads, router, *weights, *before)


def expert_grads_kernel(x_ref, dh_ref, act_ref, dy_ref, out_ref):
    up = lax.dot_general(x_ref[0], dh_ref[0], TN, preferred_element_type=f32)
    down = lax.dot_general(act_ref[0], dy_ref[0], TN, preferred_element_type=f32)
    out_ref[0, :, 0, :128, :] = up.astype(bf16).reshape(2, 128, 2 * FF)
    out_ref[0, :, 0, 128:, :] = down.astype(bf16).reshape(2, 64, WIDTH)


def expert_weight_grads(x, dh, act, dy):
    return pl.pallas_call(
        expert_grads_kernel,
        grid=(2, 4),
        in_specs=[
            pl.BlockSpec((1, ALL_ROWS, 256), lambda e, i: (e, 0, i)),
            pl.BlockSpec((1, ALL_ROWS, 2 * FF), lambda e, i: (e, 0, 0)),
            pl.BlockSpec((1, ALL_ROWS, 128), lambda e, i: (e, 0, i)),
            pl.BlockSpec((1, ALL_ROWS, WIDTH), lambda e, i: (e, 0, 0)),
        ],
        out_specs=pl.BlockSpec((1, 2, 1, 192, 1024), lambda e, i: (i, 0, e, 0, 0)),
        out_shape=jax.ShapeDtypeStruct((4, 2, 2, 192, 1024), bf16),
        compiler_params=pltpu.CompilerParams(vmem_limit_bytes=VMEM_LIMIT),
        cost_estimate=pl.CostEstimate(flops=8 << 30, bytes_accessed=14 << 20, transcendentals=0),
    )(x, dh, act, dy)


def hidden_kernel(att_ref, w_ref, rows_ref, gain_ref, hidden_ref, normed_ref):
    att = att_ref[...].reshape(WIDTH, TOK)
    hidden = rows_ref[...].astype(f32) + lax.dot_general(
        att, w_ref[:, :WIDTH], TN, preferred_element_type=f32
    )
    hidden_ref[...] = hidden
    normed_ref[...] = (hidden * inverse_rms(hidden) * gain_ref[...]).astype(bf16)


def hidden_of(attended, shared, rows, gain):
    return pl.pallas_call(
        hidden_kernel,
        out_shape=[
            jax.ShapeDtypeStruct((TOK, WIDTH), f32),
            jax.ShapeDtypeStruct((TOK, WIDTH), bf16),
        ],
        compiler_params=pltpu.CompilerParams(vmem_limit_bytes=VMEM_LIMIT),
        cost_estimate=pl.CostEstimate(
            flops=2 * TOK * WIDTH * WIDTH, bytes_accessed=5 << 20, transcendentals=0
        ),
    )(attended, shared, rows, gain)


def hidden_back_kernel(
    t0, t1, t2, t3, crossed, hidden_ref, normed_ref, chosen_ref, router_ref, g_ref, gain_ref,
    w_ref, hidden_grad_ref, branch_ref, logit_ref, scaled_ref, att_ref
):
    chosen = chosen_ref[...] > 0
    logits = lax.dot_general(router_ref[...], normed_ref[...], NT, preferred_element_type=f32)
    peak = jnp.max(jnp.where(chosen, logits, masked_score), axis=0, keepdims=True)
    raised = jnp.where(chosen, jnp.exp(jnp.minimum(logits - peak, 0.0)), 0.0)
    gates = raised / jnp.sum(raised, axis=0, keepdims=True)
    summed = t0[...].astype(f32)
    for term in (t1, t2, t3, crossed):
        summed = summed + term[...].astype(f32)
    gate_grad = summed[TOK:, :TOK] + summed[TOK:, 256 : 256 + TOK]
    logit_grad = gates * (gate_grad - jnp.sum(gates * gate_grad, axis=0, keepdims=True))
    logit_grad = logit_grad.astype(bf16)
    logit_ref[...] = logit_grad
    normed_grad = summed[:TOK] + lax.dot_general(
        logit_grad, router_ref[...], TN, preferred_element_type=f32
    )
    hidden = hidden_ref[...]
    scale = inverse_rms(hidden)
    scaled_ref[...] = (normed_grad * hidden * scale).astype(bf16)
    hidden_grad = g_ref[...].astype(f32) + rms_pull(hidden, scale, gain_ref[...], normed_grad)
    hidden_grad_ref[...] = hidden_grad
    branch = hidden_grad.astype(bf16)
    branch_ref[...] = branch
    att = lax.dot_general(w_ref[:, :WIDTH], branch, NT, preferred_element_type=f32)
    att_ref[...] = att.astype(bf16).reshape(HEADS, HEAD_DIM, TOK)


def hidden_back(terms, crossed, hidden, normed, chosen, router_t, g, gain, shared):
    wide = lambda t: jax.ShapeDtypeStruct((TOK, WIDTH), t)
    return pl.pallas_call(
        hidden_back_kernel,
        out_shape=[
            wide(f32),
            wide(bf16),
            jax.ShapeDtypeStruct((EXPERTS, TOK), bf16),
            wide(bf16),
            jax.ShapeDtypeStruct((HEADS, HEAD_DIM, TOK), bf16),
        ],
        compiler_params=pltpu.CompilerParams(vmem_limit_bytes=VMEM_LIMIT),
        cost_estimate=pl.CostEstimate(
            flops=2 * TOK * WIDTH * WIDTH, bytes_accessed=8 << 20, transcendentals=0
        ),
    )(*terms, crossed, hidden, normed, chosen, router_t, g, gain, shared)


def shared_grads_kernel(att_ref, branch_ref, normed_ref, logit_ref, scaled_ref, out_ref):
    over_tokens = (((0,), (1,)), ((), ()))
    logit = jnp.concatenate([logit_ref[...], jnp.zeros((96, TOK), bf16)], axis=0)
    ones = (lax.broadcasted_iota(i32, (128, TOK), 0) == EXPERTS).astype(f32).astype(bf16)
    att = att_ref[...].reshape(WIDTH, TOK)
    grads = [
        jnp.dot(att, branch_ref[...], preferred_element_type=f32),
        lax.dot_general(normed_ref[...], logit, over_tokens, preferred_element_type=f32)
        + lax.dot_general(scaled_ref[...], ones, over_tokens, preferred_element_type=f32),
    ]
    for w in range(8):
        for part, at in zip(grads, (slice(0, WIDTH), slice(WIDTH, None))):
            rows = [part[s * 64 + w * 8 : s * 64 + w * 8 + 8] for s in range(16)]
            out_ref[w, :, at] = jnp.concatenate(rows, axis=0).astype(bf16)


def shared_weight_grads(att, branch, normed, logit_grad, scaled):
    return pl.pallas_call(
        shared_grads_kernel,
        out_shape=jax.ShapeDtypeStruct((8, 128, 1152), bf16),
        compiler_params=pltpu.CompilerParams(vmem_limit_bytes=VMEM_LIMIT),
        cost_estimate=pl.CostEstimate(
            flops=2 * TOK * WIDTH * 1280, bytes_accessed=5 << 20, transcendentals=0
        ),
    )(att, branch, normed, logit_grad, scaled)


def local(
    tokens,
    routes,
    cont_lengths,
    norm_attn,
    w_qkv,
    w_out,
    w_router,
    norm_ffn,
    w_gate_up,
    w_down,
    cotangent,
):
    seq_index = lax.axis_index("seq")
    places, blocks = relative_places(seq_index)
    rows = tokens[0]
    query_width = HEADS * HEAD_DIM
    kv_width = KV_HEADS * HEAD_DIM

    position, begin = group_layout(cont_lengths[0])
    begin = begin[None]
    table = rotary_table(position.astype(f32))
    kv_heads = lambda start: jnp.repeat(
        w_qkv[:, start : start + kv_width].reshape(8, KV_HEADS, HEAD_DIM), 2, axis=1
    )
    head_cols = jnp.concatenate(
        [
            w_qkv[:, :query_width].reshape(8, HEADS, HEAD_DIM),
            kv_heads(query_width),
            kv_heads(query_width + kv_width),
            jnp.broadcast_to(norm_attn[:, None, None], (8, HEADS, HEAD_DIM)),
        ],
        axis=2,
    ).transpose(1, 0, 2)
    head_cols = jnp.broadcast_to(head_cols[:, None], (HEADS, 8, 8, 256)).reshape(128, 8, 256)
    head_weights = lax.all_to_all(head_cols, BOTH, 0, 0, tiled=True).reshape(WIDTH, 256)
    gain_attn = head_weights[:, 192].astype(f32)[None]
    head_weights = jnp.where(jnp.arange(256)[None] < 192, head_weights, 0.0).astype(bf16)

    rows_near, rows_across = gather_near(rows)
    rows_near, _, table, head_weights = tie(rows_near, rows_across, table, head_weights)
    rows_near, rows_far = both_cores(rows_near), gather_far(rows_across)

    own_x = lax.axis_index("wshard") % 2
    expert_rows = jnp.concatenate([w_gate_up, w_down], axis=1)
    along_y = lambda t: lax.all_gather(t, "wshard", axis_index_groups=ALONG_Y, axis=0)
    experts, expert_rows = along_y(expert_rows), swap_x(expert_rows)

    qkv = project(places[:8], rows_near, head_weights, gain_attn, table, ())
    shared = jnp.concatenate(
        [w_out, w_router, norm_ffn[:, None], jnp.zeros((8, 95), bf16)], axis=1
    )
    shared, qkv = tie(shared, qkv)
    shared = lax.all_to_all(
        jnp.broadcast_to(shared[None], (128, 8, 1152)), BOTH, 0, 0, tiled=True
    ).reshape(WIDTH, 1152)
    routes_rows = jnp.pad(routes[0].T.astype(bf16), ((0, 8), (0, WIDTH - TOK)))
    upstream_rows = jnp.concatenate([cotangent[0], routes_rows], axis=0)
    rows_far, qkv, upstream_rows, expert_rows = tie(rows_far, qkv, upstream_rows, expert_rows)
    experts = [experts, along_y(expert_rows)]
    rows_far = both_cores(rows_far)
    grad_near = [upstream_rows] + [send(upstream_rows, 0, b) for b in (1, 3, 2)]
    qkv = project(places[8:], rows_far, head_weights, gain_attn, table, (qkv,))

    router_t = shared[:, WIDTH : WIDTH + EXPERTS].T
    gain_ffn = shared[:, WIDTH + EXPERTS].astype(f32)[None]
    attended_head, attended_t, lse = attend(qkv, begin)
    attended_head, shared = tie(attended_head, shared)
    attended = lax.all_to_all(attended_head, "seq", 0, 0, tiled=True)
    attended, grad_near = tie(attended, grad_near)
    grad_near = jnp.stack(grad_near)
    grad_far = send(grad_near, 1, 0)
    hidden, normed_ffn = hidden_of(attended, shared, rows, gain_ffn)
    grad_near = (grad_near, swap_cores(grad_near))

    ffn_near, ffn_across = gather_near(normed_ffn)
    ffn_near, _, grad_far = tie(ffn_near, ffn_across, grad_far)
    ffn_near, ffn_far = both_cores(ffn_near), gather_far(ffn_across)
    own = jnp.stack([seq_index * 2, own_x])
    near = run_experts(0, own, ffn_near, grad_near, experts, router_t, ())
    near_terms = sum_along_z(*near[:2])
    ffn_far = both_cores(ffn_far)
    grad_far = (grad_far, swap_cores(grad_far))
    far = run_experts(1, own, ffn_far, grad_far, experts, router_t, near[2:])
    far, near_terms = tie(far, near_terms)
    moved, saved = far[2:4], far[4:]
    far_other, moved_other = tie(swap_cores(far[1]), moved[1])
    far_terms = send_along_z(chip_parts(far[0], far_other))
    expert_grads = expert_weight_grads(*saved)
    moved_other = swap_cores(moved_other)
    far_terms, expert_grads, moved_other = tie(far_terms, expert_grads, moved_other)
    crossed = send(add_low(*far_terms), 1, 0)
    by_x = [t.reshape(2, 4, TOK, WIDTH) for t in (moved[0], moved_other)]
    moved_parts = [add_low(by_x[0][:, i], by_x[1][:, i]) for i in range(4)]
    crossed, moved_parts = tie(crossed, moved_parts)

    expert_range = jnp.arange(EXPERTS, dtype=i32)
    chosen_here = jnp.any(routes[0].T[None] == expert_range[:, None, None], axis=1).astype(f32)
    hidden_grad, branch_grad, logit_grad, scaled_grad, attended_grad = hidden_back(
        near_terms, crossed, hidden, normed_ffn, chosen_here, router_t, cotangent[0], gain_ffn, shared
    )
    expert_grads = lax.psum_scatter(
        expert_grads.reshape(8, 2, 192, 1024),
        "wshard",
        axis_index_groups=ALONG_Y,
        scatter_dimension=0,
        tiled=True,
    )
    head_grad = lax.all_to_all(attended_grad, "seq", 0, 0, tiled=True)
    shared_grads = shared_weight_grads(attended, branch_grad, normed_ffn, logit_grad, scaled_grad)
    head_grad, shared_grads, moved_parts = tie(head_grad, shared_grads, moved_parts)
    moved_terms = [moved_parts[0]] + [
        send(moved_parts[i], 0, -b) for i, b in ((1, 1), (2, 3), (3, 2))
    ]

    shared_grads = lax.all_to_all(shared_grads, "wshard", 0, 0, tiled=True)
    projected_grad = attend_back(qkv, head_grad, attended_t, lse, begin, table)
    far_part = project_back(places[8:], projected_grad, head_weights)
    far_part, shared_grads, moved_terms = tie(far_part, shared_grads, moved_terms)
    far_parts = chip_parts(far_part[0], swap_cores(far_part[1]))
    near_part = project_back(places[:8], projected_grad, head_weights)
    near_part, expert_grads = tie(near_part, expert_grads)
    far_parts, projected_grad, shared_grads, moved_terms, expert_grads = tie(
        far_parts, projected_grad, shared_grads, moved_terms, expert_grads
    )
    far_terms = send_along_z(far_parts)
    near_parts = chip_parts(near_part[0], swap_cores(near_part[1]))
    near_parts, projected_grad = tie(near_parts, projected_grad)
    near_terms = send_along_z(near_parts)
    moved_crossed = send(add_low(*[t[1] for t in moved_terms]), 1, 0)
    shared_grads = jnp.sum(shared_grads.astype(f32), axis=0).astype(bf16).reshape(16, 8, 1152)
    shared_grads = lax.all_to_all(shared_grads, "seq", 0, 0, tiled=True)
    grad_head = head_weight_grad(places, rows_near, rows_far, gain_attn, projected_grad)
    grad_heads = lax.all_to_all(grad_head.reshape(128, 8, 256), BOTH, 0, 0, tiled=True)
    crossed = send(add_low(*far_terms), 1, 0)
    crossed, near_terms, grad_heads = tie(crossed, near_terms, grad_heads)
    kept = lax.dynamic_index_in_dim(expert_grads, own_x, 0, keepdims=False)
    sent = lax.dynamic_index_in_dim(expert_grads, 1 - own_x, 0, keepdims=False)
    expert_grads = kept.astype(f32) + swap_x(sent).astype(f32)
    total = lambda terms: sum([t.astype(f32) for t in terms])
    output = (hidden + total([t[0] for t in moved_terms] + [moved_crossed])).astype(bf16)
    normed_grad = total(near_terms + [crossed])
    shared_grads = jnp.sum(shared_grads.astype(f32), axis=0)
    grad_heads = jnp.sum(grad_heads.reshape(16, 8, 8, 256).astype(f32), axis=1).transpose(1, 0, 2)
    kv_sum = lambda start: jnp.sum(
        grad_heads[:, :, start : start + HEAD_DIM].reshape(8, KV_HEADS, 2, HEAD_DIM), axis=2
    ).reshape(8, kv_width)
    grad_qkv = jnp.concatenate(
        [grad_heads[:, :, :HEAD_DIM].reshape(8, query_width), kv_sum(HEAD_DIM), kv_sum(2 * HEAD_DIM)],
        axis=1,
    )
    grad_norm_attn = jnp.sum(grad_qkv * w_qkv.astype(f32), axis=1) / norm_attn.astype(f32)
    inputs = rows.astype(f32)
    grad_input = hidden_grad + rms_pull(inputs, inverse_rms(inputs), gain_attn, normed_grad)
    return (
        output[None],
        grad_input[None],
        grad_norm_attn,
        grad_qkv,
        shared_grads[:, :WIDTH],
        shared_grads[:, WIDTH : WIDTH + EXPERTS],
        shared_grads[:, WIDTH + EXPERTS],
        expert_grads[:, :128],
        expert_grads[:, 128:],
    )


def solution(mesh):
    return jax.shard_map(
        local,
        mesh=mesh,
        in_specs=(
            P("wshard", "seq", None),
            P("wshard", "seq", None),
            P("wshard", None),
            P(BOTH),
            P(BOTH, None),
            P(BOTH, None),
            P(BOTH, None),
            P(BOTH),
            P("seq", "wshard", None),
            P("seq", "wshard", None),
            P("wshard", "seq", None),
        ),
        out_specs=(
            P("wshard", "seq", None),
            P("wshard", "seq", None),
            P(BOTH),
            P(BOTH, None),
            P(BOTH, None),
            P(BOTH, None),
            P(BOTH),
            P("seq", "wshard", None),
            P("seq", "wshard", None),
        ),
        check_vma=False,
    )
```

```python
import jax
import jax.numpy as jnp
from jax import lax
from jax.experimental import pallas as pl
from jax.experimental.pallas import tpu as pltpu
from jax.sharding import PartitionSpec as P

HEADS = 16
KV_HEADS = 8
HEAD_DIM = 64
EXPERTS = 32
FF = 512
PROMPT = 2048
GROUP = 3584
TOK = 224
WIDTH = 1024
SLOTS = 72
STEP_ROWS = 4 * SLOTS
ALL_ROWS = 16 * SLOTS
BLOCK = 512
VMEM_LIMIT = 60 << 20
PAY = TOK + 32

norm_eps = 1e-06
rope_base = 10000.0
masked_score = -1e30
BOTH = ("seq", "wshard")
NT = (((1,), (1,)), ((), ()))
TN = (((0,), (0,)), ((), ()))
f32 = jnp.float32
bf16 = jnp.bfloat16
i32 = jnp.int32


def place_of(x, z, core):
    return x * 8 + z * 2 + core


def shift_perm(a, b):
    return [
        (place_of(x, z, c), place_of(x ^ a, (z + b) % 4, c))
        for x in range(2)
        for z in range(4)
        for c in range(2)
    ]


CORE_PERM = [(i, i ^ 1) for i in range(16)]


def send(rows, a, b):
    return lax.ppermute(rows, "seq", shift_perm(a, b))


def swap_cores(rows):
    return lax.ppermute(rows, "seq", CORE_PERM)


def relative_places(seq_index):
    x, z, c = seq_index // 8, (seq_index // 2) % 4, seq_index % 2
    r = jnp.arange(16, dtype=i32)
    a, i, k = r // 8, (r // 2) % 4, r % 2
    shift = i ^ (i // 2)
    behind = (z - i) % 4
    places = (a ^ x) * 8 + ((z - shift) % 4) * 2 + (k ^ c)
    return places, (a ^ x) * 8 + (behind ^ (behind // 2)) * 2 + (k ^ c)


def gather_near(rows):
    return [rows] + [send(rows, 0, b) for b in (1, 3, 2)], send(rows, 1, 0)


def both_cores(parts):
    mine = jnp.stack(parts)
    return mine, swap_cores(mine)


def gather_far(across):
    return [across] + [send(across, 0, b) for b in (1, 3, 2)]


def add_low(*terms):
    return sum([t.astype(f32) for t in terms]).astype(bf16)


def sum_along_z(mine, other):
    return send_along_z(chip_parts(mine, swap_cores(other)))


def chip_parts(mine, got):
    return [add_low(mine[i], got[i]) for i in range(4)]


def send_along_z(parts):
    return [parts[0]] + [send(parts[i], 0, -b) for i, b in ((1, 1), (2, 3), (3, 2))]


def swap_x(rows):
    return lax.ppermute(rows, "wshard", [(w, w ^ 1) for w in range(8)])


ALONG_Y = [[y * 2 + x for y in range(4)] for x in range(2)]


def tie(*values):
    return lax.optimization_barrier(values)


def inverse_rms(values):
    return lax.rsqrt(jnp.mean(values * values, axis=-1, keepdims=True) + norm_eps)


def rms_pull(values, scale, gain, grad):
    scaled = grad * gain
    return scale * scaled - values * (scale * scale * scale) * jnp.mean(
        scaled * values, axis=-1, keepdims=True
    )


def group_layout(lengths):
    places = jnp.arange(GROUP, dtype=i32)
    ends = jnp.cumsum(lengths)
    starts = ends - lengths
    offset_in = places - PROMPT
    segment_id = jnp.sum((offset_in[:, None] >= ends[None, :]).astype(i32), axis=1)
    segment_hot = segment_id[:, None] == jnp.arange(lengths.shape[0], dtype=i32)[None, :]
    begin = jnp.sum(jnp.where(segment_hot, starts[None, :], 0), axis=1)
    inside = offset_in >= 0
    position = jnp.where(inside, PROMPT + offset_in - begin, places)
    return position, jnp.where(inside, PROMPT + begin, 0)


def rotary_table(position):
    half_dim = HEAD_DIM // 2
    inverse = rope_base ** (-((jnp.arange(2 * HEAD_DIM) % half_dim).astype(f32) * 2.0) / HEAD_DIM)
    back = jnp.where(jnp.arange(2 * HEAD_DIM) < HEAD_DIM, 0.0, 0.5 * jnp.pi).astype(f32)
    return jnp.cos(position[:, None] * inverse[None, :] - back[None, :])


def turn(values):
    half_dim = HEAD_DIM // 2
    return jnp.concatenate([-values[:, half_dim:], values[:, :half_dim]], axis=-1)


def turn_back(values):
    half_dim = HEAD_DIM // 2
    return jnp.concatenate([values[:, half_dim:], -values[:, :half_dim]], axis=-1)


def project_kernel(places, mine, other, w, gain, table, *refs):
    out = refs[-1]
    j = pl.program_id(0)

    if len(refs) > 1:

        @pl.when(j == 0)
        def _():
            out[...] = refs[0][...]

    for k, ref in enumerate((mine, other)):
        at = pl.ds(pl.multiple_of(places[2 * j + k] * TOK, TOK), TOK)
        rows = ref[0].astype(f32)
        normed = (rows * inverse_rms(rows) * gain[...]).astype(bf16)
        projected = jnp.dot(normed, w[...], preferred_element_type=f32)
        c, s = table[at, :HEAD_DIM], table[at, HEAD_DIM:]
        q, k, v = projected[:, :64], projected[:, 64:128], projected[:, 128:]
        q = (q * c + turn(q) * s).astype(bf16).astype(f32) * HEAD_DIM**-0.5
        out[at, :] = jnp.concatenate([q, k * c + turn(k) * s, v], axis=1).astype(bf16)


def project(places, gathered, w, gain, table, before):
    chip = pl.BlockSpec((1, TOK, WIDTH), lambda j, p: (j, 0, 0))
    whole = lambda *shape: pl.BlockSpec(shape, lambda j, p: (0,) * len(shape))
    return pl.pallas_call(
        project_kernel,
        grid_spec=pltpu.PrefetchScalarGridSpec(
            num_scalar_prefetch=1,
            grid=(4,),
            in_specs=[chip, chip, whole(WIDTH, 256), whole(1, WIDTH), whole(GROUP, 128)]
            + [whole(GROUP, 256)] * len(before),
            out_specs=whole(GROUP, 256),
        ),
        out_shape=jax.ShapeDtypeStruct((GROUP, 256), bf16),
        compiler_params=pltpu.CompilerParams(vmem_limit_bytes=VMEM_LIMIT),
        cost_estimate=pl.CostEstimate(
            flops=2 * 8 * TOK * WIDTH * 256, bytes_accessed=10 << 20, transcendentals=0
        ),
    )(places, *gathered, w, gain, table, *before)


def project_back_kernel(places, first, second, w, mine, other):
    del places
    mine[0] = lax.dot_general(first[...], w[...], NT, preferred_element_type=f32).astype(bf16)
    other[0] = lax.dot_general(second[...], w[...], NT, preferred_element_type=f32).astype(bf16)


def project_back(places, projected_grad, w):
    chip = pl.BlockSpec((1, TOK, WIDTH), lambda j, p: (j, 0, 0))
    at = lambda k: pl.BlockSpec((TOK, 256), lambda j, p: (p[2 * j + k], 0))
    part = jax.ShapeDtypeStruct((4, TOK, WIDTH), bf16)
    return pl.pallas_call(
        project_back_kernel,
        grid_spec=pltpu.PrefetchScalarGridSpec(
            num_scalar_prefetch=1,
            grid=(4,),
            in_specs=[at(0), at(1), pl.BlockSpec((WIDTH, 256), lambda j, p: (0, 0))],
            out_specs=[chip, chip],
        ),
        out_shape=[part, part],
        compiler_params=pltpu.CompilerParams(vmem_limit_bytes=VMEM_LIMIT),
        cost_estimate=pl.CostEstimate(
            flops=2 * 8 * TOK * WIDTH * 256, bytes_accessed=5 << 20, transcendentals=0
        ),
    )(places, projected_grad, projected_grad, w)


def head_grad_kernel(places, near_mine, near_other, far_mine, far_other, gain, first, second, out, total):
    del places
    j = pl.program_id(0)

    @pl.when(j == 0)
    def _():
        total[...] = jnp.zeros_like(total)

    for near, far, projected in ((near_mine, far_mine, first), (near_other, far_other, second)):
        rows = jnp.where(j < 4, near[0], far[0]).astype(f32)
        normed = (rows * inverse_rms(rows) * gain[...]).astype(bf16)
        total[...] += lax.dot_general(normed, projected[...], TN, preferred_element_type=f32)

    @pl.when(j == 7)
    def _():
        out[...] = total[...].astype(bf16)


def head_weight_grad(places, near, far, gain, projected_grad):
    near_chip = pl.BlockSpec((1, TOK, WIDTH), lambda j, p: (jnp.minimum(j, 3), 0, 0))
    far_chip = pl.BlockSpec((1, TOK, WIDTH), lambda j, p: (jnp.maximum(j - 4, 0), 0, 0))
    at = lambda k: pl.BlockSpec((TOK, 256), lambda j, p: (p[2 * j + k], 0))
    return pl.pallas_call(
        head_grad_kernel,
        grid_spec=pltpu.PrefetchScalarGridSpec(
            num_scalar_prefetch=1,
            grid=(8,),
            in_specs=[
                near_chip,
                near_chip,
                far_chip,
                far_chip,
                pl.BlockSpec((1, WIDTH), lambda j, p: (0, 0)),
                at(0),
                at(1),
            ],
            out_specs=pl.BlockSpec((WIDTH, 256), lambda j, p: (0, 0)),
            scratch_shapes=[pltpu.VMEM((WIDTH, 256), f32)],
        ),
        out_shape=jax.ShapeDtypeStruct((WIDTH, 256), bf16),
        compiler_params=pltpu.CompilerParams(vmem_limit_bytes=VMEM_LIMIT),
        cost_estimate=pl.CostEstimate(
            flops=2 * 16 * TOK * WIDTH * 256, bytes_accessed=10 << 20, transcendentals=0
        ),
    )(places, *near, *far, gain, projected_grad, projected_grad)


def tile_mask(scores, key_start, query_start, begin):
    keys = key_start + lax.broadcasted_iota(i32, scores.shape, 0)
    queries = query_start + lax.broadcasted_iota(i32, scores.shape, 1)
    return jnp.where((keys <= queries) & (keys >= begin), scores, masked_score)


def key_ranges(i):
    first = PROMPT // BLOCK
    return jnp.where(i > first, i - 1, i), jnp.minimum(i, first)


def attend_kernel(qkv_ref, begin_ref, o_ref, ot_ref, lse_ref, keys, vt):
    i = pl.program_id(0)
    here = pl.ds(pl.multiple_of(i * BLOCK, BLOCK), BLOCK)

    @pl.when(i == 0)
    def _():
        keys[...] = qkv_ref[:, 64:128]
        vt[...] = qkv_ref[:, 128:192].T

    q = qkv_ref[here, :64]
    begin = begin_ref[...]

    def tile(j, carry, masked, n=1):
        peak, total, out = carry
        start = pl.multiple_of(j * BLOCK, BLOCK)
        at = pl.ds(start, n * BLOCK)
        s = lax.dot_general(keys[at, :], q, NT, preferred_element_type=f32)
        if masked:
            s = tile_mask(s, start, i * BLOCK, begin)
        higher = jnp.maximum(peak, jnp.max(s, axis=0, keepdims=True))
        p = jnp.exp(s - higher)
        fade = jnp.exp(peak - higher)
        total = total * fade + jnp.sum(p, axis=0, keepdims=True)
        out = out * fade + jnp.dot(vt[:, at], p.astype(bf16), preferred_element_type=f32)
        return higher, total, out

    carry = (
        jnp.full((1, BLOCK), masked_score, f32),
        jnp.zeros((1, BLOCK), f32),
        jnp.zeros((HEAD_DIM, BLOCK), f32),
    )
    carry = tile(i, carry, True)
    window, shared = key_ranges(i)
    carry = lax.fori_loop(window, i, lambda j, c: tile(j, c, True), carry)
    pairs = shared // 2
    carry = lax.fori_loop(0, pairs, lambda j, c: tile(2 * j, c, False, 2), carry)
    peak, total, out = lax.fori_loop(2 * pairs, shared, lambda j, c: tile(j, c, False), carry)
    ot_ref[:, here] = out * (1.0 / total)
    lse_ref[...] = peak + jnp.log(total)

    @pl.when(i == GROUP // BLOCK - 1)
    def _():
        for b in range(16):
            o_ref[b] = ot_ref[:, b * TOK : (b + 1) * TOK].astype(bf16)


def attend(qkv, begin):
    whole = lambda *shape: pl.BlockSpec(shape, lambda i: (0,) * len(shape))
    cols = lambda n: pl.BlockSpec((n, BLOCK), lambda i: (0, i))
    return pl.pallas_call(
        attend_kernel,
        grid=(GROUP // BLOCK,),
        in_specs=[whole(GROUP, 256), cols(1)],
        out_specs=[whole(16, HEAD_DIM, TOK), whole(HEAD_DIM, GROUP), cols(1)],
        out_shape=[
            jax.ShapeDtypeStruct((16, HEAD_DIM, TOK), bf16),
            jax.ShapeDtypeStruct((HEAD_DIM, GROUP), f32),
            jax.ShapeDtypeStruct((1, GROUP), f32),
        ],
        scratch_shapes=[
            pltpu.VMEM((GROUP, HEAD_DIM), bf16),
            pltpu.VMEM((HEAD_DIM, GROUP), bf16),
        ],
        compiler_params=pltpu.CompilerParams(vmem_limit_bytes=VMEM_LIMIT),
        cost_estimate=pl.CostEstimate(
            flops=2 * 27 * BLOCK * BLOCK * 512, bytes_accessed=4 << 20, transcendentals=27 * BLOCK * BLOCK
        ),
    )(qkv, begin)


def attend_back_kernel(
    qkv_ref, g_ref, ot_ref, lse_ref, begin_ref, table, out_ref, keys, values, kt, gt, dq, dk, dv
):
    i = pl.program_id(0)
    here = pl.ds(pl.multiple_of(i * BLOCK, BLOCK), BLOCK)

    @pl.when(i == 0)
    def _():
        dk[...] = jnp.zeros_like(dk)
        dv[...] = jnp.zeros_like(dv)
        keys[...] = qkv_ref[:, 64:128]
        values[...] = qkv_ref[:, 128:192]
        kt[...] = qkv_ref[:, 64:128].T
        for b in range(16):
            gt[:, b * TOK : (b + 1) * TOK] = g_ref[b]

    q = qkv_ref[here, :64]
    g = gt[:, here]
    begin = begin_ref[...]
    lse = lse_ref[...]
    inner = jnp.sum(g.astype(f32) * ot_ref[...], axis=0, keepdims=True)

    def tile(j, dq, masked, n=1):
        start = pl.multiple_of(j * BLOCK, BLOCK)
        at = pl.ds(start, n * BLOCK)
        s = lax.dot_general(keys[at, :], q, NT, preferred_element_type=f32)
        if masked:
            s = tile_mask(s, start, i * BLOCK, begin)
        p = jnp.exp(s - lse)
        dp = jnp.dot(values[at, :], g, preferred_element_type=f32)
        ds = (p * (dp - inner)).astype(bf16)
        dv[at, :] += lax.dot_general(p.astype(bf16), g, NT, preferred_element_type=f32)
        dk[at, :] += jnp.dot(ds, q, preferred_element_type=f32)
        return dq + jnp.dot(kt[:, at], ds, preferred_element_type=f32)

    dqt = tile(i, jnp.zeros((HEAD_DIM, BLOCK), f32), True)
    window, shared = key_ranges(i)
    dqt = lax.fori_loop(window, i, lambda j, c: tile(j, c, True), dqt)
    pairs = shared // 2
    dqt = lax.fori_loop(0, pairs, lambda j, c: tile(2 * j, c, False, 2), dqt)
    dqt = lax.fori_loop(2 * pairs, shared, lambda j, c: tile(j, c, False), dqt)
    dq[here, :] = dqt.T * HEAD_DIM**-0.5

    @pl.when(i == GROUP // BLOCK - 1)
    def _():
        def back(b, _):
            at = pl.ds(pl.multiple_of(b * BLOCK, BLOCK), BLOCK)
            c, s = table[at, :HEAD_DIM], table[at, HEAD_DIM:]
            q, k = dq[at, :].astype(bf16).astype(f32), dk[at, :].astype(bf16).astype(f32)
            parts = [q * c + turn_back(q * s), k * c + turn_back(k * s), dv[at, :], jnp.zeros_like(q)]
            out_ref[at, :] = jnp.concatenate(parts, axis=1).astype(bf16)
            return 0

        lax.fori_loop(0, GROUP // BLOCK, back, 0)


def attend_back(qkv, g, ot, lse, begin, table):
    whole = lambda *shape: pl.BlockSpec(shape, lambda i: (0,) * len(shape))
    cols = lambda n: pl.BlockSpec((n, BLOCK), lambda i: (0, i))
    return pl.pallas_call(
        attend_back_kernel,
        grid=(GROUP // BLOCK,),
        in_specs=[
            whole(GROUP, 256),
            whole(16, HEAD_DIM, TOK),
            cols(HEAD_DIM),
            cols(1),
            cols(1),
            whole(GROUP, 128),
        ],
        out_specs=whole(GROUP, 256),
        out_shape=jax.ShapeDtypeStruct((GROUP, 256), bf16),
        scratch_shapes=[
            pltpu.VMEM((GROUP, HEAD_DIM), bf16),
            pltpu.VMEM((GROUP, HEAD_DIM), bf16),
            pltpu.VMEM((HEAD_DIM, GROUP), bf16),
            pltpu.VMEM((HEAD_DIM, GROUP), bf16),
            pltpu.VMEM((GROUP, HEAD_DIM), f32),
            pltpu.VMEM((GROUP, HEAD_DIM), f32),
            pltpu.VMEM((GROUP, HEAD_DIM), f32),
        ],
        compiler_params=pltpu.CompilerParams(vmem_limit_bytes=VMEM_LIMIT),
        cost_estimate=pl.CostEstimate(
            flops=5 * 27 * BLOCK * BLOCK * 512, bytes_accessed=8 << 20, transcendentals=27 * BLOCK * BLOCK
        ),
    )(qkv, g, ot, lse, begin, table)


def experts_kernel(
    own_ref, ffn_mine, ffn_other, g_mine, g_other, routes_mine, routes_other, router_ref, own_w, across_w, *refs
):
    routed_mine, routed_other, moved_mine, moved_other = refs[-10:-6]
    x_ref, dh_ref, act_ref, dy_ref, w_ref, sem = refs[-6:]
    own = own_ref[0]

    @pl.when(pl.program_id(0) == 0)
    def _():
        copies = [
            pltpu.make_async_copy(shards.at[y, e], w_ref.at[e, 2 * y + (own_ref[1] ^ a)], sem.at[a, y, e])
            for a, shards in enumerate((own_w, across_w))
            for y in range(4)
            for e in range(2)
        ]
        for copy in copies:
            copy.start()
        for copy in copies:
            copy.wait()

    expert_rows = lax.broadcasted_iota(i32, (EXPERTS, TOK), 0)
    slot_rows = lax.broadcasted_iota(i32, (SLOTS, TOK), 0).astype(f32)
    upto = (
        lax.broadcasted_iota(i32, (TOK, TOK), 0) <= lax.broadcasted_iota(i32, (TOK, TOK), 1)
    ).astype(f32).astype(bf16)
    slot_cols = []
    gate_grads = [jnp.zeros((EXPERTS, WIDTH), f32) for _ in range(4)]
    payload_rows = lax.broadcasted_iota(i32, (EXPERTS, WIDTH), 0)
    gate_rows = [[], []]
    picks = [[], []]
    picked_rows = [[], []]
    picked_grads = [[], []]
    blocks = [(ffn_mine, g_mine, routes_mine, 0), (ffn_other, g_other, routes_other, 0)]
    blocks = blocks + [(*refs_of[:3], 1) for refs_of in blocks]
    for rows_ref, grads_ref, routes_ref, n in blocks:
        rows, grads = rows_ref[n], grads_ref[n]
        routes = routes_ref[n][:8, :TOK].astype(f32).astype(i32)
        chosen = expert_rows == routes[0:1]
        for j in range(1, 8):
            chosen = chosen | (expert_rows == routes[j : j + 1])
        named = [jnp.max((routes == own + e).astype(f32), axis=0, keepdims=True) for e in range(2)]
        named = jnp.concatenate(named + [jnp.zeros((6, TOK), f32)], axis=0)
        rank = jnp.dot(named.astype(bf16), upto, preferred_element_type=f32)
        slots = jnp.where(named > 0, rank - 1.0, -1.0)
        slot_cols.append(slots.T)
        logits = lax.dot_general(router_ref[...], rows, NT, preferred_element_type=f32)
        peak = jnp.max(jnp.where(chosen, logits, masked_score), axis=0, keepdims=True)
        raised = jnp.where(chosen, jnp.exp(jnp.minimum(logits - peak, 0.0)), 0.0)
        gates = raised / jnp.sum(raised, axis=0, keepdims=True)
        for e in range(2):
            gate_rows[e].append(
                jnp.sum(jnp.where(expert_rows == own + e, gates, 0.0), axis=0, keepdims=True)
            )
            pick = (slots[e : e + 1] == slot_rows).astype(f32)
            picks[e].append(pick)
            low = pick.astype(bf16)
            picked_rows[e].append(jnp.dot(low, rows, preferred_element_type=f32))
            picked_grads[e].append(jnp.dot(low, grads, preferred_element_type=f32))
    moved, routed = [], []
    for e in range(2):
        w_gate_up = w_ref[e, :, :128, :].reshape(WIDTH, 2 * FF)
        w_down = w_ref[e, :, 128:, :].reshape(FF, WIDTH)
        x = jnp.concatenate(picked_rows[e], axis=0).astype(bf16)
        gate = jnp.concatenate(
            [jnp.sum(p * r, axis=1, keepdims=True) for p, r in zip(picks[e], gate_rows[e])], axis=0
        )
        grads = jnp.concatenate(picked_grads[e], axis=0)
        dy = (gate * grads).astype(bf16)
        mixed = jnp.dot(x, w_gate_up, preferred_element_type=f32)
        dact = lax.dot_general(dy, w_down, NT, preferred_element_type=f32)
        gate_part, up_part = mixed[:, :FF], mixed[:, FF:]
        sigma = 1.0 / (1.0 + jnp.exp(-gate_part))
        silu = gate_part * sigma
        act = (silu * up_part).astype(bf16)
        dh = jnp.concatenate(
            [dact * up_part * (sigma + silu * (1.0 - sigma)), dact * silu], axis=1
        ).astype(bf16)
        x_ref[e] = x
        dy_ref[e] = dy
        act_ref[e] = act
        dh_ref[e] = dh
        returned = jnp.dot(act, w_down, preferred_element_type=f32).astype(bf16).astype(f32)
        dgate = jnp.sum(returned * grads, axis=1, keepdims=True)
        for b in range(4):
            grad = jnp.sum(
                picks[e][b] * dgate[b * SLOTS : (b + 1) * SLOTS], axis=0, keepdims=True
            )
            high = grad.astype(bf16).astype(f32)
            gap = jnp.zeros((1, 256 - TOK), f32)
            wide = jnp.concatenate([high, gap, grad - high, gap, jnp.zeros((1, WIDTH - 512), f32)], axis=1)
            gate_grads[b] = gate_grads[b] + jnp.where(payload_rows == own + e, wide, 0.0)
        moved.append(gate * returned)
        routed.append(lax.dot_general(dh, w_gate_up, NT, preferred_element_type=f32))
    columns = lax.broadcasted_iota(i32, (TOK, 2 * SLOTS), 1).astype(f32)
    outs = [(routed_mine, moved_mine, 0), (routed_other, moved_other, 0), (routed_mine, moved_mine, 1), (routed_other, moved_other, 1)]
    for b, (routed_ref, moved_ref, n) in enumerate(outs):
        first, second = slot_cols[b][:, 0:1], slot_cols[b][:, 1:2]
        back = ((columns == first) | ((columns == second + SLOTS) & (second >= 0))).astype(f32).astype(bf16)
        at = slice(b * SLOTS, (b + 1) * SLOTS)
        for terms, ref in ((routed, routed_ref), (moved, moved_ref)):
            joined = jnp.concatenate([terms[0][at], terms[1][at]], axis=0).astype(bf16)
            ref[n, :TOK, :] = jnp.dot(back, joined, preferred_element_type=f32).astype(bf16)
        routed_ref[n, TOK:, :] = gate_grads[b].astype(bf16)


def run_experts(half, own, ffn, grads, weights, router, before):
    pair = pl.BlockSpec((2, TOK, WIDTH), lambda i, o: (i, 0, 0))
    pair_of_all = pl.BlockSpec((2, TOK, WIDTH), lambda i, o: (i + 2 * half, 0, 0))
    whole = lambda shape: pl.BlockSpec(shape, lambda i, o: (0,) * len(shape))
    routes = pl.BlockSpec((2, 16, 256), lambda i, o: (i, TOK // 16, 0))
    summed = pl.BlockSpec((2, PAY, WIDTH), lambda i, o: (i, 0, 0))
    kept = lambda n: pl.BlockSpec((2, STEP_ROWS, n), lambda i, o: (0, i + 2 * half, 0))
    part = jax.ShapeDtypeStruct((4, PAY, WIDTH), bf16)
    keep = lambda n: jax.ShapeDtypeStruct((2, ALL_ROWS, n), bf16)
    return pl.pallas_call(
        experts_kernel,
        grid_spec=pltpu.PrefetchScalarGridSpec(
            num_scalar_prefetch=1,
            grid=(2,),
            in_specs=[
                pair,
                pair,
                pair,
                pair,
                routes,
                routes,
                whole((EXPERTS, WIDTH)),
            ]
            + [pl.BlockSpec(memory_space=pl.ANY)] * (2 + len(before)),
            out_specs=[
                summed,
                summed,
                pair_of_all,
                pair_of_all,
                kept(WIDTH),
                kept(2 * FF),
                kept(FF),
                kept(WIDTH),
            ],
            scratch_shapes=[
                pltpu.VMEM((2, 8, 192, 1024), bf16),
                pltpu.SemaphoreType.DMA((2, 4, 2)),
            ],
        ),
        out_shape=[
            part,
            part,
            jax.ShapeDtypeStruct((8, TOK, WIDTH), bf16),
            jax.ShapeDtypeStruct((8, TOK, WIDTH), bf16),
            keep(WIDTH),
            keep(2 * FF),
            keep(FF),
            keep(WIDTH),
        ],
        input_output_aliases={10 + i: 2 + i for i in range(len(before))},
        compiler_params=pltpu.CompilerParams(vmem_limit_bytes=VMEM_LIMIT),
        cost_estimate=pl.CostEstimate(
            flops=14 << 30, bytes_accessed=24 << 20, transcendentals=8 * SLOTS * 2 * FF
        ),
    )(own, *ffn, *grads, *grads, router, *weights, *before)


def expert_grads_kernel(x_ref, dh_ref, act_ref, dy_ref, out_ref):
    up = lax.dot_general(x_ref[0], dh_ref[0], TN, preferred_element_type=f32)
    down = lax.dot_general(act_ref[0], dy_ref[0], TN, preferred_element_type=f32)
    out_ref[0, :, 0, :128, :] = up.astype(bf16).reshape(2, 128, 2 * FF)
    out_ref[0, :, 0, 128:, :] = down.astype(bf16).reshape(2, 64, WIDTH)


def expert_weight_grads(x, dh, act, dy):
    return pl.pallas_call(
        expert_grads_kernel,
        grid=(2, 4),
        in_specs=[
            pl.BlockSpec((1, ALL_ROWS, 256), lambda e, i: (e, 0, i)),
            pl.BlockSpec((1, ALL_ROWS, 2 * FF), lambda e, i: (e, 0, 0)),
            pl.BlockSpec((1, ALL_ROWS, 128), lambda e, i: (e, 0, i)),
            pl.BlockSpec((1, ALL_ROWS, WIDTH), lambda e, i: (e, 0, 0)),
        ],
        out_specs=pl.BlockSpec((1, 2, 1, 192, 1024), lambda e, i: (i, 0, e, 0, 0)),
        out_shape=jax.ShapeDtypeStruct((4, 2, 2, 192, 1024), bf16),
        compiler_params=pltpu.CompilerParams(vmem_limit_bytes=VMEM_LIMIT),
        cost_estimate=pl.CostEstimate(flops=8 << 30, bytes_accessed=14 << 20, transcendentals=0),
    )(x, dh, act, dy)


def hidden_kernel(att_ref, w_ref, rows_ref, gain_ref, hidden_ref, normed_ref):
    att = att_ref[...].reshape(WIDTH, TOK)
    hidden = rows_ref[...].astype(f32) + lax.dot_general(
        att, w_ref[:, :WIDTH], TN, preferred_element_type=f32
    )
    hidden_ref[...] = hidden
    normed_ref[...] = (hidden * inverse_rms(hidden) * gain_ref[...]).astype(bf16)


def hidden_of(attended, shared, rows, gain):
    return pl.pallas_call(
        hidden_kernel,
        out_shape=[
            jax.ShapeDtypeStruct((TOK, WIDTH), f32),
            jax.ShapeDtypeStruct((TOK, WIDTH), bf16),
        ],
        compiler_params=pltpu.CompilerParams(vmem_limit_bytes=VMEM_LIMIT),
        cost_estimate=pl.CostEstimate(
            flops=2 * TOK * WIDTH * WIDTH, bytes_accessed=5 << 20, transcendentals=0
        ),
    )(attended, shared, rows, gain)


def hidden_back_kernel(
    t0, t1, t2, t3, crossed, hidden_ref, normed_ref, chosen_ref, router_ref, g_ref, gain_ref,
    w_ref, hidden_grad_ref, branch_ref, logit_ref, scaled_ref, att_ref
):
    chosen = chosen_ref[...] > 0
    logits = lax.dot_general(router_ref[...], normed_ref[...], NT, preferred_element_type=f32)
    peak = jnp.max(jnp.where(chosen, logits, masked_score), axis=0, keepdims=True)
    raised = jnp.where(chosen, jnp.exp(jnp.minimum(logits - peak, 0.0)), 0.0)
    gates = raised / jnp.sum(raised, axis=0, keepdims=True)
    summed = t0[...].astype(f32)
    for term in (t1, t2, t3, crossed):
        summed = summed + term[...].astype(f32)
    gate_grad = summed[TOK:, :TOK] + summed[TOK:, 256 : 256 + TOK]
    logit_grad = gates * (gate_grad - jnp.sum(gates * gate_grad, axis=0, keepdims=True))
    logit_grad = logit_grad.astype(bf16)
    logit_ref[...] = logit_grad
    normed_grad = summed[:TOK] + lax.dot_general(
        logit_grad, router_ref[...], TN, preferred_element_type=f32
    )
    hidden = hidden_ref[...]
    scale = inverse_rms(hidden)
    scaled_ref[...] = (normed_grad * hidden * scale).astype(bf16)
    hidden_grad = g_ref[...].astype(f32) + rms_pull(hidden, scale, gain_ref[...], normed_grad)
    hidden_grad_ref[...] = hidden_grad
    branch = hidden_grad.astype(bf16)
    branch_ref[...] = branch
    att = lax.dot_general(w_ref[:, :WIDTH], branch, NT, preferred_element_type=f32)
    att_ref[...] = att.astype(bf16).reshape(HEADS, HEAD_DIM, TOK)


def hidden_back(terms, crossed, hidden, normed, chosen, router_t, g, gain, shared):
    wide = lambda t: jax.ShapeDtypeStruct((TOK, WIDTH), t)
    return pl.pallas_call(
        hidden_back_kernel,
        out_shape=[
            wide(f32),
            wide(bf16),
            jax.ShapeDtypeStruct((EXPERTS, TOK), bf16),
            wide(bf16),
            jax.ShapeDtypeStruct((HEADS, HEAD_DIM, TOK), bf16),
        ],
        compiler_params=pltpu.CompilerParams(vmem_limit_bytes=VMEM_LIMIT),
        cost_estimate=pl.CostEstimate(
            flops=2 * TOK * WIDTH * WIDTH, bytes_accessed=8 << 20, transcendentals=0
        ),
    )(*terms, crossed, hidden, normed, chosen, router_t, g, gain, shared)


def shared_grads_kernel(att_ref, branch_ref, normed_ref, logit_ref, scaled_ref, out_ref):
    over_tokens = (((0,), (1,)), ((), ()))
    logit = jnp.concatenate([logit_ref[...], jnp.zeros((96, TOK), bf16)], axis=0)
    ones = (lax.broadcasted_iota(i32, (128, TOK), 0) == EXPERTS).astype(f32).astype(bf16)
    att = att_ref[...].reshape(WIDTH, TOK)
    grads = [
        jnp.dot(att, branch_ref[...], preferred_element_type=f32),
        lax.dot_general(normed_ref[...], logit, over_tokens, preferred_element_type=f32)
        + lax.dot_general(scaled_ref[...], ones, over_tokens, preferred_element_type=f32),
    ]
    for w in range(8):
        for part, at in zip(grads, (slice(0, WIDTH), slice(WIDTH, None))):
            rows = [part[s * 64 + w * 8 : s * 64 + w * 8 + 8] for s in range(16)]
            out_ref[w, :, at] = jnp.concatenate(rows, axis=0).astype(bf16)


def shared_weight_grads(att, branch, normed, logit_grad, scaled):
    return pl.pallas_call(
        shared_grads_kernel,
        out_shape=jax.ShapeDtypeStruct((8, 128, 1152), bf16),
        compiler_params=pltpu.CompilerParams(vmem_limit_bytes=VMEM_LIMIT),
        cost_estimate=pl.CostEstimate(
            flops=2 * TOK * WIDTH * 1280, bytes_accessed=5 << 20, transcendentals=0
        ),
    )(att, branch, normed, logit_grad, scaled)


def local(
    tokens,
    routes,
    cont_lengths,
    norm_attn,
    w_qkv,
    w_out,
    w_router,
    norm_ffn,
    w_gate_up,
    w_down,
    cotangent,
):
    seq_index = lax.axis_index("seq")
    places, blocks = relative_places(seq_index)
    rows = tokens[0]
    query_width = HEADS * HEAD_DIM
    kv_width = KV_HEADS * HEAD_DIM

    position, begin = group_layout(cont_lengths[0])
    begin = begin[None]
    table = rotary_table(position.astype(f32))
    kv_heads = lambda start: jnp.repeat(
        w_qkv[:, start : start + kv_width].reshape(8, KV_HEADS, HEAD_DIM), 2, axis=1
    )
    head_cols = jnp.concatenate(
        [
            w_qkv[:, :query_width].reshape(8, HEADS, HEAD_DIM),
            kv_heads(query_width),
            kv_heads(query_width + kv_width),
            jnp.broadcast_to(norm_attn[:, None, None], (8, HEADS, HEAD_DIM)),
        ],
        axis=2,
    ).transpose(1, 0, 2)
    head_cols = jnp.broadcast_to(head_cols[:, None], (HEADS, 8, 8, 256)).reshape(128, 8, 256)
    head_weights = lax.all_to_all(head_cols, BOTH, 0, 0, tiled=True).reshape(WIDTH, 256)
    gain_attn = head_weights[:, 192].astype(f32)[None]
    head_weights = jnp.where(jnp.arange(256)[None] < 192, head_weights, 0.0).astype(bf16)

    rows_near, rows_across = gather_near(rows)
    rows_near, _, table, head_weights = tie(rows_near, rows_across, table, head_weights)
    rows_near, rows_far = both_cores(rows_near), gather_far(rows_across)

    own_x = lax.axis_index("wshard") % 2
    expert_rows = jnp.concatenate([w_gate_up, w_down], axis=1)
    along_y = lambda t: lax.all_gather(t, "wshard", axis_index_groups=ALONG_Y, axis=0)
    experts, expert_rows = along_y(expert_rows), swap_x(expert_rows)

    qkv = project(places[:8], rows_near, head_weights, gain_attn, table, ())
    shared = jnp.concatenate(
        [w_out, w_router, norm_ffn[:, None], jnp.zeros((8, 95), bf16)], axis=1
    )
    shared, qkv = tie(shared, qkv)
    shared = lax.all_to_all(
        jnp.broadcast_to(shared[None], (128, 8, 1152)), BOTH, 0, 0, tiled=True
    ).reshape(WIDTH, 1152)
    routes_rows = jnp.pad(routes[0].T.astype(bf16), ((0, 8), (0, WIDTH - TOK)))
    upstream_rows = jnp.concatenate([cotangent[0], routes_rows], axis=0)
    grad_across = send(upstream_rows, 1, 0)
    rows_far, qkv, upstream_rows, grad_across = tie(rows_far, qkv, upstream_rows, grad_across)
    rows_far = both_cores(rows_far)
    grad_near = [upstream_rows] + [send(upstream_rows, 0, b) for b in (1, 3, 2)]
    qkv = project(places[8:], rows_far, head_weights, gain_attn, table, (qkv,))

    router_t = shared[:, WIDTH : WIDTH + EXPERTS].T
    gain_ffn = shared[:, WIDTH + EXPERTS].astype(f32)[None]
    grad_far = [grad_across, send(grad_across, 0, 1), send(grad_across, 0, 3)]
    attended_head, attended_t, lse = attend(qkv, begin)
    grad_across, expert_rows, _ = tie(grad_across, expert_rows, attended_head)
    experts = [experts, along_y(expert_rows)]
    grad_far = grad_far + [send(grad_across, 0, 2)]
    attended_head, shared = tie(attended_head, shared)
    attended = lax.all_to_all(attended_head, "seq", 0, 0, tiled=True)
    attended, grad_near, grad_far = tie(attended, grad_near, grad_far)
    hidden, normed_ffn = hidden_of(attended, shared, rows, gain_ffn)

    ffn_near, ffn_across = gather_near(normed_ffn)
    ffn_near, _ = tie(ffn_near, ffn_across)
    ffn_near, ffn_far = both_cores(ffn_near), gather_far(ffn_across)
    grad_near = both_cores(grad_near)
    own = jnp.stack([seq_index * 2, own_x])
    near = run_experts(0, own, ffn_near, grad_near, experts, router_t, ())
    near_terms = sum_along_z(*near[:2])
    ffn_far = both_cores(ffn_far)
    grad_far = both_cores(grad_far)
    far = run_experts(1, own, ffn_far, grad_far, experts, router_t, near[2:])
    far, near_terms = tie(far, near_terms)
    moved, saved = far[2:4], far[4:]
    far_other, moved_other = tie(swap_cores(far[1]), moved[1])
    far_terms = send_along_z(chip_parts(far[0], far_other))
    expert_grads = expert_weight_grads(*saved)
    moved_other = swap_cores(moved_other)
    far_terms, expert_grads, moved_other = tie(far_terms, expert_grads, moved_other)
    crossed = send(add_low(*far_terms), 1, 0)
    by_x = [t.reshape(2, 4, TOK, WIDTH) for t in (moved[0], moved_other)]
    moved_parts = [add_low(by_x[0][:, i], by_x[1][:, i]) for i in range(4)]
    crossed, moved_parts = tie(crossed, moved_parts)

    expert_range = jnp.arange(EXPERTS, dtype=i32)
    chosen_here = jnp.any(routes[0].T[None] == expert_range[:, None, None], axis=1).astype(f32)
    hidden_grad, branch_grad, logit_grad, scaled_grad, attended_grad = hidden_back(
        near_terms, crossed, hidden, normed_ffn, chosen_here, router_t, cotangent[0], gain_ffn, shared
    )
    expert_grads = lax.psum_scatter(
        expert_grads.reshape(8, 2, 192, 1024),
        "wshard",
        axis_index_groups=ALONG_Y,
        scatter_dimension=0,
        tiled=True,
    )
    head_grad = lax.all_to_all(attended_grad, "seq", 0, 0, tiled=True)
    shared_grads = shared_weight_grads(attended, branch_grad, normed_ffn, logit_grad, scaled_grad)
    head_grad, shared_grads, moved_parts = tie(head_grad, shared_grads, moved_parts)
    moved_terms = [moved_parts[0]] + [
        send(moved_parts[i], 0, -b) for i, b in ((1, 1), (2, 3), (3, 2))
    ]

    shared_grads = lax.all_to_all(shared_grads, "wshard", 0, 0, tiled=True)
    projected_grad = attend_back(qkv, head_grad, attended_t, lse, begin, table)
    far_part = project_back(places[8:], projected_grad, head_weights)
    far_part, shared_grads, moved_terms = tie(far_part, shared_grads, moved_terms)
    far_parts = chip_parts(far_part[0], swap_cores(far_part[1]))
    near_part = project_back(places[:8], projected_grad, head_weights)
    near_part, expert_grads = tie(near_part, expert_grads)
    far_parts, projected_grad, shared_grads, moved_terms, expert_grads = tie(
        far_parts, projected_grad, shared_grads, moved_terms, expert_grads
    )
    far_terms = send_along_z(far_parts)
    near_parts = chip_parts(near_part[0], swap_cores(near_part[1]))
    moved_crossed = send(add_low(*[t[1] for t in moved_terms]), 1, 0)
    shared_grads = jnp.sum(shared_grads.astype(f32), axis=0).astype(bf16).reshape(16, 8, 1152)
    shared_grads = lax.all_to_all(shared_grads, "seq", 0, 0, tiled=True)
    grad_head = head_weight_grad(places, rows_near, rows_far, gain_attn, projected_grad)
    far_terms, near_parts, grad_head = tie(far_terms, near_parts, grad_head)
    near_terms = send_along_z(near_parts)
    grad_heads = lax.all_to_all(grad_head.reshape(128, 8, 256), BOTH, 0, 0, tiled=True)
    crossed = send(add_low(*far_terms), 1, 0)
    crossed, near_terms, grad_heads = tie(crossed, near_terms, grad_heads)
    kept = lax.dynamic_index_in_dim(expert_grads, own_x, 0, keepdims=False)
    sent = lax.dynamic_index_in_dim(expert_grads, 1 - own_x, 0, keepdims=False)
    expert_grads = kept.astype(f32) + swap_x(sent).astype(f32)
    total = lambda terms: sum([t.astype(f32) for t in terms])
    output = (hidden + total([t[0] for t in moved_terms] + [moved_crossed])).astype(bf16)
    normed_grad = total(near_terms + [crossed])
    shared_grads = jnp.sum(shared_grads.astype(f32), axis=0)
    grad_heads = jnp.sum(grad_heads.reshape(16, 8, 8, 256).astype(f32), axis=1).transpose(1, 0, 2)
    kv_sum = lambda start: jnp.sum(
        grad_heads[:, :, start : start + HEAD_DIM].reshape(8, KV_HEADS, 2, HEAD_DIM), axis=2
    ).reshape(8, kv_width)
    grad_qkv = jnp.concatenate(
        [grad_heads[:, :, :HEAD_DIM].reshape(8, query_width), kv_sum(HEAD_DIM), kv_sum(2 * HEAD_DIM)],
        axis=1,
    )
    grad_norm_attn = jnp.sum(grad_qkv * w_qkv.astype(f32), axis=1) / norm_attn.astype(f32)
    inputs = rows.astype(f32)
    grad_input = hidden_grad + rms_pull(inputs, inverse_rms(inputs), gain_attn, normed_grad)
    return (
        output[None],
        grad_input[None],
        grad_norm_attn,
        grad_qkv,
        shared_grads[:, :WIDTH],
        shared_grads[:, WIDTH : WIDTH + EXPERTS],
        shared_grads[:, WIDTH + EXPERTS],
        expert_grads[:, :128],
        expert_grads[:, 128:],
    )


def solution(mesh):
    return jax.shard_map(
        local,
        mesh=mesh,
        in_specs=(
            P("wshard", "seq", None),
            P("wshard", "seq", None),
            P("wshard", None),
            P(BOTH),
            P(BOTH, None),
            P(BOTH, None),
            P(BOTH, None),
            P(BOTH),
            P("seq", "wshard", None),
            P("seq", "wshard", None),
            P("wshard", "seq", None),
        ),
        out_specs=(
            P("wshard", "seq", None),
            P("wshard", "seq", None),
            P(BOTH),
            P(BOTH, None),
            P(BOTH, None),
            P(BOTH, None),
            P(BOTH),
            P("seq", "wshard", None),
            P("seq", "wshard", None),
        ),
        check_vma=False,
    )
```

```python
import jax
import jax.numpy as jnp
from jax import lax
from jax.experimental import pallas as pl
from jax.experimental.pallas import tpu as pltpu
from jax.sharding import PartitionSpec as P

HEADS = 16
KV_HEADS = 8
HEAD_DIM = 64
EXPERTS = 32
FF = 512
PROMPT = 2048
GROUP = 3584
TOK = 224
WIDTH = 1024
SLOTS = 72
STEP_ROWS = 4 * SLOTS
ALL_ROWS = 16 * SLOTS
BLOCK = 512
VMEM_LIMIT = 60 << 20
PAY = TOK + 32

norm_eps = 1e-06
rope_base = 10000.0
masked_score = -1e30
BOTH = ("seq", "wshard")
NT = (((1,), (1,)), ((), ()))
TN = (((0,), (0,)), ((), ()))
f32 = jnp.float32
bf16 = jnp.bfloat16
i32 = jnp.int32


def place_of(x, z, core):
    return x * 8 + z * 2 + core


def shift_perm(a, b):
    return [
        (place_of(x, z, c), place_of(x ^ a, (z + b) % 4, c))
        for x in range(2)
        for z in range(4)
        for c in range(2)
    ]


CORE_PERM = [(i, i ^ 1) for i in range(16)]


def send(rows, a, b):
    return lax.ppermute(rows, "seq", shift_perm(a, b))


def swap_cores(rows):
    return lax.ppermute(rows, "seq", CORE_PERM)


def relative_places(seq_index):
    x, z, c = seq_index // 8, (seq_index // 2) % 4, seq_index % 2
    r = jnp.arange(16, dtype=i32)
    a, i, k = r // 8, (r // 2) % 4, r % 2
    shift = i ^ (i // 2)
    behind = (z - i) % 4
    places = (a ^ x) * 8 + ((z - shift) % 4) * 2 + (k ^ c)
    return places, (a ^ x) * 8 + (behind ^ (behind // 2)) * 2 + (k ^ c)


def gather_near(rows):
    return [rows] + [send(rows, 0, b) for b in (1, 3, 2)], send(rows, 1, 0)


def both_cores(parts):
    mine = jnp.stack(parts)
    return mine, swap_cores(mine)


def gather_far(across):
    return [across] + [send(across, 0, b) for b in (1, 3, 2)]


def add_low(*terms):
    return sum([t.astype(f32) for t in terms]).astype(bf16)


def sum_along_z(mine, other):
    return send_along_z(chip_parts(mine, swap_cores(other)))


def chip_parts(mine, got):
    return [add_low(mine[i], got[i]) for i in range(4)]


def send_along_z(parts):
    return [parts[0]] + [send(parts[i], 0, -b) for i, b in ((1, 1), (2, 3), (3, 2))]


def swap_x(rows):
    return lax.ppermute(rows, "wshard", [(w, w ^ 1) for w in range(8)])


ALONG_Y = [[y * 2 + x for y in range(4)] for x in range(2)]


def tie(*values):
    return lax.optimization_barrier(values)


def inverse_rms(values):
    return lax.rsqrt(jnp.mean(values * values, axis=-1, keepdims=True) + norm_eps)


def rms_pull(values, scale, gain, grad):
    scaled = grad * gain
    return scale * scaled - values * (scale * scale * scale) * jnp.mean(
        scaled * values, axis=-1, keepdims=True
    )


def group_layout(lengths):
    places = jnp.arange(GROUP, dtype=i32)
    ends = jnp.cumsum(lengths)
    starts = ends - lengths
    offset_in = places - PROMPT
    segment_id = jnp.sum((offset_in[:, None] >= ends[None, :]).astype(i32), axis=1)
    segment_hot = segment_id[:, None] == jnp.arange(lengths.shape[0], dtype=i32)[None, :]
    begin = jnp.sum(jnp.where(segment_hot, starts[None, :], 0), axis=1)
    inside = offset_in >= 0
    position = jnp.where(inside, PROMPT + offset_in - begin, places)
    return position, jnp.where(inside, PROMPT + begin, 0)


def rotary_table(position):
    half_dim = HEAD_DIM // 2
    inverse = rope_base ** (-((jnp.arange(2 * HEAD_DIM) % half_dim).astype(f32) * 2.0) / HEAD_DIM)
    back = jnp.where(jnp.arange(2 * HEAD_DIM) < HEAD_DIM, 0.0, 0.5 * jnp.pi).astype(f32)
    return jnp.cos(position[:, None] * inverse[None, :] - back[None, :])


def turn(values):
    half_dim = HEAD_DIM // 2
    return jnp.concatenate([-values[:, half_dim:], values[:, :half_dim]], axis=-1)


def turn_back(values):
    half_dim = HEAD_DIM // 2
    return jnp.concatenate([values[:, half_dim:], -values[:, :half_dim]], axis=-1)


def project_kernel(places, mine, other, w, gain, table, *refs):
    out = refs[-1]
    j = pl.program_id(0)

    if len(refs) > 1:

        @pl.when(j == 0)
        def _():
            out[...] = refs[0][...]

    for k, ref in enumerate((mine, other)):
        at = pl.ds(pl.multiple_of(places[2 * j + k] * TOK, TOK), TOK)
        rows = ref[0].astype(f32)
        normed = (rows * inverse_rms(rows) * gain[...]).astype(bf16)
        projected = jnp.dot(normed, w[...], preferred_element_type=f32)
        c, s = table[at, :HEAD_DIM], table[at, HEAD_DIM:]
        q, k, v = projected[:, :64], projected[:, 64:128], projected[:, 128:]
        q = (q * c + turn(q) * s).astype(bf16).astype(f32) * HEAD_DIM**-0.5
        out[at, :] = jnp.concatenate([q, k * c + turn(k) * s, v], axis=1).astype(bf16)


def project(places, gathered, w, gain, table, before):
    chip = pl.BlockSpec((1, TOK, WIDTH), lambda j, p: (j, 0, 0))
    whole = lambda *shape: pl.BlockSpec(shape, lambda j, p: (0,) * len(shape))
    return pl.pallas_call(
        project_kernel,
        grid_spec=pltpu.PrefetchScalarGridSpec(
            num_scalar_prefetch=1,
            grid=(4,),
            in_specs=[chip, chip, whole(WIDTH, 256), whole(1, WIDTH), whole(GROUP, 128)]
            + [whole(GROUP, 256)] * len(before),
            out_specs=whole(GROUP, 256),
        ),
        out_shape=jax.ShapeDtypeStruct((GROUP, 256), bf16),
        compiler_params=pltpu.CompilerParams(vmem_limit_bytes=VMEM_LIMIT),
        cost_estimate=pl.CostEstimate(
            flops=2 * 8 * TOK * WIDTH * 256, bytes_accessed=10 << 20, transcendentals=0
        ),
    )(places, *gathered, w, gain, table, *before)


def project_back_kernel(places, first, second, w, mine, other):
    del places
    mine[0] = lax.dot_general(first[...], w[...], NT, preferred_element_type=f32).astype(bf16)
    other[0] = lax.dot_general(second[...], w[...], NT, preferred_element_type=f32).astype(bf16)


def project_back(places, projected_grad, w):
    chip = pl.BlockSpec((1, TOK, WIDTH), lambda j, p: (j, 0, 0))
    at = lambda k: pl.BlockSpec((TOK, 256), lambda j, p: (p[2 * j + k], 0))
    part = jax.ShapeDtypeStruct((4, TOK, WIDTH), bf16)
    return pl.pallas_call(
        project_back_kernel,
        grid_spec=pltpu.PrefetchScalarGridSpec(
            num_scalar_prefetch=1,
            grid=(4,),
            in_specs=[at(0), at(1), pl.BlockSpec((WIDTH, 256), lambda j, p: (0, 0))],
            out_specs=[chip, chip],
        ),
        out_shape=[part, part],
        compiler_params=pltpu.CompilerParams(vmem_limit_bytes=VMEM_LIMIT),
        cost_estimate=pl.CostEstimate(
            flops=2 * 8 * TOK * WIDTH * 256, bytes_accessed=5 << 20, transcendentals=0
        ),
    )(places, projected_grad, projected_grad, w)


def head_grad_kernel(places, near_mine, near_other, far_mine, far_other, gain, first, second, out, total):
    del places
    j = pl.program_id(0)

    @pl.when(j == 0)
    def _():
        total[...] = jnp.zeros_like(total)

    for near, far, projected in ((near_mine, far_mine, first), (near_other, far_other, second)):
        rows = jnp.where(j < 4, near[0], far[0]).astype(f32)
        normed = (rows * inverse_rms(rows) * gain[...]).astype(bf16)
        total[...] += lax.dot_general(normed, projected[...], TN, preferred_element_type=f32)

    @pl.when(j == 7)
    def _():
        out[...] = total[...].astype(bf16)


def head_weight_grad(places, near, far, gain, projected_grad):
    near_chip = pl.BlockSpec((1, TOK, WIDTH), lambda j, p: (jnp.minimum(j, 3), 0, 0))
    far_chip = pl.BlockSpec((1, TOK, WIDTH), lambda j, p: (jnp.maximum(j - 4, 0), 0, 0))
    at = lambda k: pl.BlockSpec((TOK, 256), lambda j, p: (p[2 * j + k], 0))
    return pl.pallas_call(
        head_grad_kernel,
        grid_spec=pltpu.PrefetchScalarGridSpec(
            num_scalar_prefetch=1,
            grid=(8,),
            in_specs=[
                near_chip,
                near_chip,
                far_chip,
                far_chip,
                pl.BlockSpec((1, WIDTH), lambda j, p: (0, 0)),
                at(0),
                at(1),
            ],
            out_specs=pl.BlockSpec((WIDTH, 256), lambda j, p: (0, 0)),
            scratch_shapes=[pltpu.VMEM((WIDTH, 256), f32)],
        ),
        out_shape=jax.ShapeDtypeStruct((WIDTH, 256), bf16),
        compiler_params=pltpu.CompilerParams(vmem_limit_bytes=VMEM_LIMIT),
        cost_estimate=pl.CostEstimate(
            flops=2 * 16 * TOK * WIDTH * 256, bytes_accessed=10 << 20, transcendentals=0
        ),
    )(places, *near, *far, gain, projected_grad, projected_grad)


def tile_mask(scores, key_start, query_start, begin):
    keys = key_start + lax.broadcasted_iota(i32, scores.shape, 0)
    queries = query_start + lax.broadcasted_iota(i32, scores.shape, 1)
    return jnp.where((keys <= queries) & (keys >= begin), scores, masked_score)


def key_ranges(i):
    first = PROMPT // BLOCK
    return jnp.where(i > first, i - 1, i), jnp.minimum(i, first)


def attend_kernel(qkv_ref, begin_ref, o_ref, ot_ref, lse_ref, keys, vt):
    i = pl.program_id(0)
    here = pl.ds(pl.multiple_of(i * BLOCK, BLOCK), BLOCK)

    @pl.when(i == 0)
    def _():
        keys[...] = qkv_ref[:, 64:128]
        vt[...] = qkv_ref[:, 128:192].T

    q = qkv_ref[here, :64]
    begin = begin_ref[...]

    def tile(j, carry, masked, n=1):
        peak, total, out = carry
        start = pl.multiple_of(j * BLOCK, BLOCK)
        at = pl.ds(start, n * BLOCK)
        s = lax.dot_general(keys[at, :], q, NT, preferred_element_type=f32)
        if masked:
            s = tile_mask(s, start, i * BLOCK, begin)
        higher = jnp.maximum(peak, jnp.max(s, axis=0, keepdims=True))
        p = jnp.exp(s - higher)
        fade = jnp.exp(peak - higher)
        total = total * fade + jnp.sum(p, axis=0, keepdims=True)
        out = out * fade + jnp.dot(vt[:, at], p.astype(bf16), preferred_element_type=f32)
        return higher, total, out

    carry = (
        jnp.full((1, BLOCK), masked_score, f32),
        jnp.zeros((1, BLOCK), f32),
        jnp.zeros((HEAD_DIM, BLOCK), f32),
    )
    carry = tile(i, carry, True)
    window, shared = key_ranges(i)
    carry = lax.fori_loop(window, i, lambda j, c: tile(j, c, True), carry)
    pairs = shared // 2
    carry = lax.fori_loop(0, pairs, lambda j, c: tile(2 * j, c, False, 2), carry)
    peak, total, out = lax.fori_loop(2 * pairs, shared, lambda j, c: tile(j, c, False), carry)
    ot_ref[:, here] = out * (1.0 / total)
    lse_ref[...] = peak + jnp.log(total)

    @pl.when(i == GROUP // BLOCK - 1)
    def _():
        for b in range(16):
            o_ref[b] = ot_ref[:, b * TOK : (b + 1) * TOK].astype(bf16)


def attend(qkv, begin):
    whole = lambda *shape: pl.BlockSpec(shape, lambda i: (0,) * len(shape))
    cols = lambda n: pl.BlockSpec((n, BLOCK), lambda i: (0, i))
    return pl.pallas_call(
        attend_kernel,
        grid=(GROUP // BLOCK,),
        in_specs=[whole(GROUP, 256), cols(1)],
        out_specs=[whole(16, HEAD_DIM, TOK), whole(HEAD_DIM, GROUP), cols(1)],
        out_shape=[
            jax.ShapeDtypeStruct((16, HEAD_DIM, TOK), bf16),
            jax.ShapeDtypeStruct((HEAD_DIM, GROUP), f32),
            jax.ShapeDtypeStruct((1, GROUP), f32),
        ],
        scratch_shapes=[
            pltpu.VMEM((GROUP, HEAD_DIM), bf16),
            pltpu.VMEM((HEAD_DIM, GROUP), bf16),
        ],
        compiler_params=pltpu.CompilerParams(vmem_limit_bytes=VMEM_LIMIT),
        cost_estimate=pl.CostEstimate(
            flops=2 * 27 * BLOCK * BLOCK * 512, bytes_accessed=4 << 20, transcendentals=27 * BLOCK * BLOCK
        ),
    )(qkv, begin)


def attend_back_kernel(
    qkv_ref, g_ref, ot_ref, lse_ref, begin_ref, table, out_ref, keys, values, kt, gt, dq, dk, dv
):
    i = pl.program_id(0)
    here = pl.ds(pl.multiple_of(i * BLOCK, BLOCK), BLOCK)

    @pl.when(i == 0)
    def _():
        dk[...] = jnp.zeros_like(dk)
        dv[...] = jnp.zeros_like(dv)
        keys[...] = qkv_ref[:, 64:128]
        values[...] = qkv_ref[:, 128:192]
        kt[...] = qkv_ref[:, 64:128].T
        for b in range(16):
            gt[:, b * TOK : (b + 1) * TOK] = g_ref[b]

    q = qkv_ref[here, :64]
    g = gt[:, here]
    begin = begin_ref[...]
    lse = lse_ref[...]
    inner = jnp.sum(g.astype(f32) * ot_ref[...], axis=0, keepdims=True)

    def tile(j, dq, masked, n=1):
        start = pl.multiple_of(j * BLOCK, BLOCK)
        at = pl.ds(start, n * BLOCK)
        s = lax.dot_general(keys[at, :], q, NT, preferred_element_type=f32)
        if masked:
            s = tile_mask(s, start, i * BLOCK, begin)
        p = jnp.exp(s - lse)
        dp = jnp.dot(values[at, :], g, preferred_element_type=f32)
        ds = (p * (dp - inner)).astype(bf16)
        dv[at, :] += lax.dot_general(p.astype(bf16), g, NT, preferred_element_type=f32)
        dk[at, :] += jnp.dot(ds, q, preferred_element_type=f32)
        return dq + jnp.dot(kt[:, at], ds, preferred_element_type=f32)

    dqt = tile(i, jnp.zeros((HEAD_DIM, BLOCK), f32), True)
    window, shared = key_ranges(i)
    dqt = lax.fori_loop(window, i, lambda j, c: tile(j, c, True), dqt)
    pairs = shared // 2
    dqt = lax.fori_loop(0, pairs, lambda j, c: tile(2 * j, c, False, 2), dqt)
    dqt = lax.fori_loop(2 * pairs, shared, lambda j, c: tile(j, c, False), dqt)
    dq[here, :] = dqt.T * HEAD_DIM**-0.5

    @pl.when(i == GROUP // BLOCK - 1)
    def _():
        def back(b, _):
            at = pl.ds(pl.multiple_of(b * BLOCK, BLOCK), BLOCK)
            c, s = table[at, :HEAD_DIM], table[at, HEAD_DIM:]
            q, k = dq[at, :].astype(bf16).astype(f32), dk[at, :].astype(bf16).astype(f32)
            parts = [q * c + turn_back(q * s), k * c + turn_back(k * s), dv[at, :], jnp.zeros_like(q)]
            out_ref[at, :] = jnp.concatenate(parts, axis=1).astype(bf16)
            return 0

        lax.fori_loop(0, GROUP // BLOCK, back, 0)


def attend_back(qkv, g, ot, lse, begin, table):
    whole = lambda *shape: pl.BlockSpec(shape, lambda i: (0,) * len(shape))
    cols = lambda n: pl.BlockSpec((n, BLOCK), lambda i: (0, i))
    return pl.pallas_call(
        attend_back_kernel,
        grid=(GROUP // BLOCK,),
        in_specs=[
            whole(GROUP, 256),
            whole(16, HEAD_DIM, TOK),
            cols(HEAD_DIM),
            cols(1),
            cols(1),
            whole(GROUP, 128),
        ],
        out_specs=whole(GROUP, 256),
        out_shape=jax.ShapeDtypeStruct((GROUP, 256), bf16),
        scratch_shapes=[
            pltpu.VMEM((GROUP, HEAD_DIM), bf16),
            pltpu.VMEM((GROUP, HEAD_DIM), bf16),
            pltpu.VMEM((HEAD_DIM, GROUP), bf16),
            pltpu.VMEM((HEAD_DIM, GROUP), bf16),
            pltpu.VMEM((GROUP, HEAD_DIM), f32),
            pltpu.VMEM((GROUP, HEAD_DIM), f32),
            pltpu.VMEM((GROUP, HEAD_DIM), f32),
        ],
        compiler_params=pltpu.CompilerParams(vmem_limit_bytes=VMEM_LIMIT),
        cost_estimate=pl.CostEstimate(
            flops=5 * 27 * BLOCK * BLOCK * 512, bytes_accessed=8 << 20, transcendentals=27 * BLOCK * BLOCK
        ),
    )(qkv, g, ot, lse, begin, table)


def experts_kernel(
    own_ref, ffn_mine, ffn_other, g_mine, g_other, routes_mine, routes_other, router_ref, own_w, across_w, *refs
):
    routed_mine, routed_other, moved_mine, moved_other = refs[-10:-6]
    x_ref, dh_ref, act_ref, dy_ref, w_ref, sem = refs[-6:]
    own = own_ref[0]

    copies = [
        [
            pltpu.make_async_copy(shards.at[y, e], w_ref.at[e, 2 * y + (own_ref[1] ^ a)], sem.at[a, y, e])
            for a, shards in enumerate((own_w, across_w))
            for y in range(4)
        ]
        for e in range(2)
    ]

    @pl.when(pl.program_id(0) == 0)
    def _():
        for copy in copies[0] + copies[1]:
            copy.start()

    expert_rows = lax.broadcasted_iota(i32, (EXPERTS, TOK), 0)
    slot_rows = lax.broadcasted_iota(i32, (SLOTS, TOK), 0).astype(f32)
    upto = (
        lax.broadcasted_iota(i32, (TOK, TOK), 0) <= lax.broadcasted_iota(i32, (TOK, TOK), 1)
    ).astype(f32).astype(bf16)
    slot_cols = []
    gate_grads = [jnp.zeros((EXPERTS, WIDTH), f32) for _ in range(4)]
    payload_rows = lax.broadcasted_iota(i32, (EXPERTS, WIDTH), 0)
    gate_rows = [[], []]
    picks = [[], []]
    picked_rows = [[], []]
    picked_grads = [[], []]
    blocks = [(ffn_mine, g_mine, routes_mine, 0), (ffn_other, g_other, routes_other, 0)]
    blocks = blocks + [(*refs_of[:3], 1) for refs_of in blocks]
    for rows_ref, grads_ref, routes_ref, n in blocks:
        rows, grads = rows_ref[n], grads_ref[n]
        routes = routes_ref[n][:8, :TOK].astype(f32).astype(i32)
        chosen = expert_rows == routes[0:1]
        for j in range(1, 8):
            chosen = chosen | (expert_rows == routes[j : j + 1])
        named = [jnp.max((routes == own + e).astype(f32), axis=0, keepdims=True) for e in range(2)]
        named = jnp.concatenate(named + [jnp.zeros((6, TOK), f32)], axis=0)
        rank = jnp.dot(named.astype(bf16), upto, preferred_element_type=f32)
        slots = jnp.where(named > 0, rank - 1.0, -1.0)
        slot_cols.append(slots.T)
        logits = lax.dot_general(router_ref[...], rows, NT, preferred_element_type=f32)
        peak = jnp.max(jnp.where(chosen, logits, masked_score), axis=0, keepdims=True)
        raised = jnp.where(chosen, jnp.exp(jnp.minimum(logits - peak, 0.0)), 0.0)
        gates = raised / jnp.sum(raised, axis=0, keepdims=True)
        for e in range(2):
            gate_rows[e].append(
                jnp.sum(jnp.where(expert_rows == own + e, gates, 0.0), axis=0, keepdims=True)
            )
            picks[e].append((slots[e : e + 1] == slot_rows).astype(f32))
        low = jnp.concatenate([picks[0][-1], picks[1][-1]], axis=0).astype(bf16)
        for source, kept in ((rows, picked_rows), (grads, picked_grads)):
            both = jnp.dot(low, source, preferred_element_type=f32)
            kept[0].append(both[:SLOTS])
            kept[1].append(both[SLOTS:])
    moved, routed = [], []
    for e in range(2):

        @pl.when(pl.program_id(0) == 0)
        def _():
            for copy in copies[e]:
                copy.wait()

        w_gate_up = w_ref[e, :, :128, :].reshape(WIDTH, 2 * FF)
        w_down = w_ref[e, :, 128:, :].reshape(FF, WIDTH)
        x = jnp.concatenate(picked_rows[e], axis=0).astype(bf16)
        gate = jnp.concatenate(
            [jnp.sum(p * r, axis=1, keepdims=True) for p, r in zip(picks[e], gate_rows[e])], axis=0
        )
        grads = jnp.concatenate(picked_grads[e], axis=0)
        dy = (gate * grads).astype(bf16)
        mixed = jnp.dot(x, w_gate_up, preferred_element_type=f32)
        dact = lax.dot_general(dy, w_down, NT, preferred_element_type=f32)
        gate_part, up_part = mixed[:, :FF], mixed[:, FF:]
        sigma = 1.0 / (1.0 + jnp.exp(-gate_part))
        silu = gate_part * sigma
        act = (silu * up_part).astype(bf16)
        dh = jnp.concatenate(
            [dact * up_part * (sigma + silu * (1.0 - sigma)), dact * silu], axis=1
        ).astype(bf16)
        x_ref[e] = x
        dy_ref[e] = dy
        act_ref[e] = act
        dh_ref[e] = dh
        returned = jnp.dot(act, w_down, preferred_element_type=f32).astype(bf16).astype(f32)
        dgate = jnp.sum(returned * grads, axis=1, keepdims=True)
        for b in range(4):
            grad = jnp.sum(
                picks[e][b] * dgate[b * SLOTS : (b + 1) * SLOTS], axis=0, keepdims=True
            )
            high = grad.astype(bf16).astype(f32)
            gap = jnp.zeros((1, 256 - TOK), f32)
            wide = jnp.concatenate([high, gap, grad - high, gap, jnp.zeros((1, WIDTH - 512), f32)], axis=1)
            gate_grads[b] = gate_grads[b] + jnp.where(payload_rows == own + e, wide, 0.0)
        moved.append(gate * returned)
        routed.append(lax.dot_general(dh, w_gate_up, NT, preferred_element_type=f32))
    columns = lax.broadcasted_iota(i32, (TOK, 2 * SLOTS), 1).astype(f32)
    outs = [(routed_mine, moved_mine, 0), (routed_other, moved_other, 0), (routed_mine, moved_mine, 1), (routed_other, moved_other, 1)]
    for b, (routed_ref, moved_ref, n) in enumerate(outs):
        first, second = slot_cols[b][:, 0:1], slot_cols[b][:, 1:2]
        back = ((columns == first) | ((columns == second + SLOTS) & (second >= 0))).astype(f32).astype(bf16)
        at = slice(b * SLOTS, (b + 1) * SLOTS)
        for terms, ref in ((routed, routed_ref), (moved, moved_ref)):
            joined = jnp.concatenate([terms[0][at], terms[1][at]], axis=0).astype(bf16)
            ref[n, :TOK, :] = jnp.dot(back, joined, preferred_element_type=f32).astype(bf16)
        routed_ref[n, TOK:, :] = gate_grads[b].astype(bf16)


def run_experts(half, own, ffn, grads, weights, router, before):
    pair = pl.BlockSpec((2, TOK, WIDTH), lambda i, o: (i, 0, 0))
    pair_of_all = pl.BlockSpec((2, TOK, WIDTH), lambda i, o: (i + 2 * half, 0, 0))
    whole = lambda shape: pl.BlockSpec(shape, lambda i, o: (0,) * len(shape))
    routes = pl.BlockSpec((2, 16, 256), lambda i, o: (i + 2 * half, TOK // 16, 0))
    summed = pl.BlockSpec((2, PAY, WIDTH), lambda i, o: (i, 0, 0))
    kept = lambda n: pl.BlockSpec((2, STEP_ROWS, n), lambda i, o: (0, i + 2 * half, 0))
    part = jax.ShapeDtypeStruct((4, PAY, WIDTH), bf16)
    keep = lambda n: jax.ShapeDtypeStruct((2, ALL_ROWS, n), bf16)
    return pl.pallas_call(
        experts_kernel,
        grid_spec=pltpu.PrefetchScalarGridSpec(
            num_scalar_prefetch=1,
            grid=(2,),
            in_specs=[
                pair,
                pair,
                pair_of_all,
                pair_of_all,
                routes,
                routes,
                whole((EXPERTS, WIDTH)),
            ]
            + [pl.BlockSpec(memory_space=pl.ANY)] * (2 + len(before)),
            out_specs=[
                summed,
                summed,
                pair_of_all,
                pair_of_all,
                kept(WIDTH),
                kept(2 * FF),
                kept(FF),
                kept(WIDTH),
            ],
            scratch_shapes=[
                pltpu.VMEM((2, 8, 192, 1024), bf16),
                pltpu.SemaphoreType.DMA((2, 4, 2)),
            ],
        ),
        out_shape=[
            part,
            part,
            jax.ShapeDtypeStruct((8, TOK, WIDTH), bf16),
            jax.ShapeDtypeStruct((8, TOK, WIDTH), bf16),
            keep(WIDTH),
            keep(2 * FF),
            keep(FF),
            keep(WIDTH),
        ],
        input_output_aliases={10 + i: 2 + i for i in range(len(before))},
        compiler_params=pltpu.CompilerParams(vmem_limit_bytes=VMEM_LIMIT),
        cost_estimate=pl.CostEstimate(
            flops=14 << 30, bytes_accessed=24 << 20, transcendentals=8 * SLOTS * 2 * FF
        ),
    )(own, *ffn, *grads, *grads, router, *weights, *before)


def expert_grads_kernel(x_ref, dh_ref, act_ref, dy_ref, out_ref):
    up = lax.dot_general(x_ref[0], dh_ref[0], TN, preferred_element_type=f32)
    down = lax.dot_general(act_ref[0], dy_ref[0], TN, preferred_element_type=f32)
    out_ref[0, :, 0, :128, :] = up.astype(bf16).reshape(2, 128, 2 * FF)
    out_ref[0, :, 0, 128:, :] = down.astype(bf16).reshape(2, 64, WIDTH)


def expert_weight_grads(x, dh, act, dy):
    return pl.pallas_call(
        expert_grads_kernel,
        grid=(2, 4),
        in_specs=[
            pl.BlockSpec((1, ALL_ROWS, 256), lambda e, i: (e, 0, i)),
            pl.BlockSpec((1, ALL_ROWS, 2 * FF), lambda e, i: (e, 0, 0)),
            pl.BlockSpec((1, ALL_ROWS, 128), lambda e, i: (e, 0, i)),
            pl.BlockSpec((1, ALL_ROWS, WIDTH), lambda e, i: (e, 0, 0)),
        ],
        out_specs=pl.BlockSpec((1, 2, 1, 192, 1024), lambda e, i: (i, 0, e, 0, 0)),
        out_shape=jax.ShapeDtypeStruct((4, 2, 2, 192, 1024), bf16),
        compiler_params=pltpu.CompilerParams(vmem_limit_bytes=VMEM_LIMIT),
        cost_estimate=pl.CostEstimate(flops=8 << 30, bytes_accessed=14 << 20, transcendentals=0),
    )(x, dh, act, dy)


def hidden_kernel(att_ref, w_ref, rows_ref, gain_ref, hidden_ref, normed_ref):
    att = att_ref[...].reshape(WIDTH, TOK)
    hidden = rows_ref[...].astype(f32) + lax.dot_general(
        att, w_ref[:, :WIDTH], TN, preferred_element_type=f32
    )
    hidden_ref[...] = hidden
    normed_ref[...] = (hidden * inverse_rms(hidden) * gain_ref[...]).astype(bf16)


def hidden_of(attended, shared, rows, gain):
    return pl.pallas_call(
        hidden_kernel,
        out_shape=[
            jax.ShapeDtypeStruct((TOK, WIDTH), f32),
            jax.ShapeDtypeStruct((TOK, WIDTH), bf16),
        ],
        compiler_params=pltpu.CompilerParams(vmem_limit_bytes=VMEM_LIMIT),
        cost_estimate=pl.CostEstimate(
            flops=2 * TOK * WIDTH * WIDTH, bytes_accessed=5 << 20, transcendentals=0
        ),
    )(attended, shared, rows, gain)


def hidden_back_kernel(
    t0, t1, t2, t3, crossed, hidden_ref, normed_ref, chosen_ref, router_ref, g_ref, gain_ref,
    w_ref, hidden_grad_ref, branch_ref, logit_ref, scaled_ref, att_ref
):
    chosen = chosen_ref[...] > 0
    logits = lax.dot_general(router_ref[...], normed_ref[...], NT, preferred_element_type=f32)
    peak = jnp.max(jnp.where(chosen, logits, masked_score), axis=0, keepdims=True)
    raised = jnp.where(chosen, jnp.exp(jnp.minimum(logits - peak, 0.0)), 0.0)
    gates = raised / jnp.sum(raised, axis=0, keepdims=True)
    summed = t0[...].astype(f32)
    for term in (t1, t2, t3, crossed):
        summed = summed + term[...].astype(f32)
    gate_grad = summed[TOK:, :TOK] + summed[TOK:, 256 : 256 + TOK]
    logit_grad = gates * (gate_grad - jnp.sum(gates * gate_grad, axis=0, keepdims=True))
    logit_grad = logit_grad.astype(bf16)
    logit_ref[...] = logit_grad
    normed_grad = summed[:TOK] + lax.dot_general(
        logit_grad, router_ref[...], TN, preferred_element_type=f32
    )
    hidden = hidden_ref[...]
    scale = inverse_rms(hidden)
    scaled_ref[...] = (normed_grad * hidden * scale).astype(bf16)
    hidden_grad = g_ref[...].astype(f32) + rms_pull(hidden, scale, gain_ref[...], normed_grad)
    hidden_grad_ref[...] = hidden_grad
    branch = hidden_grad.astype(bf16)
    branch_ref[...] = branch
    att = lax.dot_general(w_ref[:, :WIDTH], branch, NT, preferred_element_type=f32)
    att_ref[...] = att.astype(bf16).reshape(HEADS, HEAD_DIM, TOK)


def hidden_back(terms, crossed, hidden, normed, chosen, router_t, g, gain, shared):
    wide = lambda t: jax.ShapeDtypeStruct((TOK, WIDTH), t)
    return pl.pallas_call(
        hidden_back_kernel,
        out_shape=[
            wide(f32),
            wide(bf16),
            jax.ShapeDtypeStruct((EXPERTS, TOK), bf16),
            wide(bf16),
            jax.ShapeDtypeStruct((HEADS, HEAD_DIM, TOK), bf16),
        ],
        compiler_params=pltpu.CompilerParams(vmem_limit_bytes=VMEM_LIMIT),
        cost_estimate=pl.CostEstimate(
            flops=2 * TOK * WIDTH * WIDTH, bytes_accessed=8 << 20, transcendentals=0
        ),
    )(*terms, crossed, hidden, normed, chosen, router_t, g, gain, shared)


def shared_grads_kernel(att_ref, branch_ref, normed_ref, logit_ref, scaled_ref, out_ref):
    over_tokens = (((0,), (1,)), ((), ()))
    logit = jnp.concatenate([logit_ref[...], jnp.zeros((96, TOK), bf16)], axis=0)
    ones = (lax.broadcasted_iota(i32, (128, TOK), 0) == EXPERTS).astype(f32).astype(bf16)
    att = att_ref[...].reshape(WIDTH, TOK)
    grads = [
        jnp.dot(att, branch_ref[...], preferred_element_type=f32),
        lax.dot_general(normed_ref[...], logit, over_tokens, preferred_element_type=f32)
        + lax.dot_general(scaled_ref[...], ones, over_tokens, preferred_element_type=f32),
    ]
    for w in range(8):
        for part, at in zip(grads, (slice(0, WIDTH), slice(WIDTH, None))):
            rows = [part[s * 64 + w * 8 : s * 64 + w * 8 + 8] for s in range(16)]
            out_ref[w, :, at] = jnp.concatenate(rows, axis=0).astype(bf16)


def shared_weight_grads(att, branch, normed, logit_grad, scaled):
    return pl.pallas_call(
        shared_grads_kernel,
        out_shape=jax.ShapeDtypeStruct((8, 128, 1152), bf16),
        compiler_params=pltpu.CompilerParams(vmem_limit_bytes=VMEM_LIMIT),
        cost_estimate=pl.CostEstimate(
            flops=2 * TOK * WIDTH * 1280, bytes_accessed=5 << 20, transcendentals=0
        ),
    )(att, branch, normed, logit_grad, scaled)


def local(
    tokens,
    routes,
    cont_lengths,
    norm_attn,
    w_qkv,
    w_out,
    w_router,
    norm_ffn,
    w_gate_up,
    w_down,
    cotangent,
):
    seq_index = lax.axis_index("seq")
    places, blocks = relative_places(seq_index)
    rows = tokens[0]
    query_width = HEADS * HEAD_DIM
    kv_width = KV_HEADS * HEAD_DIM

    position, begin = group_layout(cont_lengths[0])
    begin = begin[None]
    table = rotary_table(position.astype(f32))
    kv_heads = lambda start: jnp.repeat(
        w_qkv[:, start : start + kv_width].reshape(8, KV_HEADS, HEAD_DIM), 2, axis=1
    )
    head_cols = jnp.concatenate(
        [
            w_qkv[:, :query_width].reshape(8, HEADS, HEAD_DIM),
            kv_heads(query_width),
            kv_heads(query_width + kv_width),
            jnp.broadcast_to(norm_attn[:, None, None], (8, HEADS, HEAD_DIM)),
        ],
        axis=2,
    ).transpose(1, 0, 2)
    head_cols = jnp.broadcast_to(head_cols[:, None], (HEADS, 8, 8, 256)).reshape(128, 8, 256)
    head_weights = lax.all_to_all(head_cols, BOTH, 0, 0, tiled=True).reshape(WIDTH, 256)
    gain_attn = head_weights[:, 192].astype(f32)[None]
    head_weights = jnp.where(jnp.arange(256)[None] < 192, head_weights, 0.0).astype(bf16)

    rows_near, rows_across = gather_near(rows)
    rows_near, _, table, head_weights = tie(rows_near, rows_across, table, head_weights)
    rows_near, rows_far = both_cores(rows_near), gather_far(rows_across)

    own_x = lax.axis_index("wshard") % 2
    expert_rows = jnp.concatenate([w_gate_up, w_down], axis=1)
    along_y = lambda t: lax.all_gather(t, "wshard", axis_index_groups=ALONG_Y, axis=0)
    experts, expert_rows = along_y(expert_rows), swap_x(expert_rows)

    qkv = project(places[:8], rows_near, head_weights, gain_attn, table, ())
    shared = jnp.concatenate(
        [w_out, w_router, norm_ffn[:, None], jnp.zeros((8, 95), bf16)], axis=1
    )
    shared, qkv = tie(shared, qkv)
    shared = lax.all_to_all(
        jnp.broadcast_to(shared[None], (128, 8, 1152)), BOTH, 0, 0, tiled=True
    ).reshape(WIDTH, 1152)
    routes_rows = jnp.pad(routes[0].T.astype(bf16), ((0, 8), (0, WIDTH - TOK)))
    upstream_rows = jnp.concatenate([cotangent[0], routes_rows], axis=0)
    grad_across = send(upstream_rows, 1, 0)
    rows_far, qkv, upstream_rows, grad_across, expert_rows = tie(
        rows_far, qkv, upstream_rows, grad_across, expert_rows
    )
    experts = [experts, along_y(expert_rows)]
    rows_far = both_cores(rows_far)
    grad_near = [upstream_rows] + [send(upstream_rows, 0, b) for b in (1, 3, 2)]
    qkv = project(places[8:], rows_far, head_weights, gain_attn, table, (qkv,))

    router_t = shared[:, WIDTH : WIDTH + EXPERTS].T
    gain_ffn = shared[:, WIDTH + EXPERTS].astype(f32)[None]
    grad_far = [grad_across, send(grad_across, 0, 1), send(grad_across, 0, 3)]
    attended_head, attended_t, lse = attend(qkv, begin)
    grad_across, _ = tie(grad_across, attended_head)
    grad_far = grad_far + [send(grad_across, 0, 2)]
    attended_head, shared = tie(attended_head, shared)
    attended = lax.all_to_all(attended_head, "seq", 0, 0, tiled=True)
    attended, grad_near, grad_far = tie(attended, grad_near, grad_far)
    hidden, normed_ffn = hidden_of(attended, shared, rows, gain_ffn)

    ffn_near, ffn_across = gather_near(normed_ffn)
    grad_all = both_cores(grad_near + grad_far)
    ffn_near, _, grad_all = tie(ffn_near, ffn_across, grad_all)
    ffn_near, ffn_far = both_cores(ffn_near), gather_far(ffn_across)
    own = jnp.stack([seq_index * 2, own_x])
    near = run_experts(0, own, ffn_near, grad_all, experts, router_t, ())
    near_terms = sum_along_z(*near[:2])
    ffn_far = both_cores(ffn_far)
    far = run_experts(1, own, ffn_far, grad_all, experts, router_t, near[2:])
    far, near_terms = tie(far, near_terms)
    moved, saved = far[2:4], far[4:]
    far_other, moved_other = tie(swap_cores(far[1]), moved[1])
    far_terms = send_along_z(chip_parts(far[0], far_other))
    expert_grads = expert_weight_grads(*saved)
    moved_other = swap_cores(moved_other)
    far_terms, expert_grads, moved_other = tie(far_terms, expert_grads, moved_other)
    crossed = send(add_low(*far_terms), 1, 0)
    by_x = [t.reshape(2, 4, TOK, WIDTH) for t in (moved[0], moved_other)]
    moved_parts = [add_low(by_x[0][:, i], by_x[1][:, i]) for i in range(4)]
    crossed, moved_parts = tie(crossed, moved_parts)

    expert_range = jnp.arange(EXPERTS, dtype=i32)
    chosen_here = jnp.any(routes[0].T[None] == expert_range[:, None, None], axis=1).astype(f32)
    hidden_grad, branch_grad, logit_grad, scaled_grad, attended_grad = hidden_back(
        near_terms, crossed, hidden, normed_ffn, chosen_here, router_t, cotangent[0], gain_ffn, shared
    )
    expert_grads = lax.psum_scatter(
        expert_grads.reshape(8, 2, 192, 1024),
        "wshard",
        axis_index_groups=ALONG_Y,
        scatter_dimension=0,
        tiled=True,
    )
    head_grad = lax.all_to_all(attended_grad, "seq", 0, 0, tiled=True)
    shared_grads = shared_weight_grads(attended, branch_grad, normed_ffn, logit_grad, scaled_grad)
    head_grad, shared_grads, moved_parts = tie(head_grad, shared_grads, moved_parts)
    moved_terms = [moved_parts[0]] + [
        send(moved_parts[i], 0, -b) for i, b in ((1, 1), (2, 3), (3, 2))
    ]

    shared_grads = lax.all_to_all(shared_grads, "wshard", 0, 0, tiled=True)
    projected_grad = attend_back(qkv, head_grad, attended_t, lse, begin, table)
    far_part = project_back(places[8:], projected_grad, head_weights)
    far_part, shared_grads, moved_terms = tie(far_part, shared_grads, moved_terms)
    far_parts = chip_parts(far_part[0], swap_cores(far_part[1]))
    near_part = project_back(places[:8], projected_grad, head_weights)
    near_part, expert_grads = tie(near_part, expert_grads)
    far_parts, projected_grad, shared_grads, moved_terms, expert_grads = tie(
        far_parts, projected_grad, shared_grads, moved_terms, expert_grads
    )
    far_terms = send_along_z(far_parts)
    near_parts = chip_parts(near_part[0], swap_cores(near_part[1]))
    moved_crossed = send(add_low(*[t[1] for t in moved_terms]), 1, 0)
    shared_grads = jnp.sum(shared_grads.astype(f32), axis=0).astype(bf16).reshape(16, 8, 1152)
    shared_grads = lax.all_to_all(shared_grads, "seq", 0, 0, tiled=True)
    grad_head = head_weight_grad(places, rows_near, rows_far, gain_attn, projected_grad)
    far_terms, near_parts, grad_head = tie(far_terms, near_parts, grad_head)
    near_terms = send_along_z(near_parts)
    grad_heads = lax.all_to_all(grad_head.reshape(128, 8, 256), BOTH, 0, 0, tiled=True)
    crossed = send(add_low(*far_terms), 1, 0)
    crossed, near_terms, grad_heads = tie(crossed, near_terms, grad_heads)
    kept = lax.dynamic_index_in_dim(expert_grads, own_x, 0, keepdims=False)
    sent = lax.dynamic_index_in_dim(expert_grads, 1 - own_x, 0, keepdims=False)
    expert_grads = kept.astype(f32) + swap_x(sent).astype(f32)
    total = lambda terms: sum([t.astype(f32) for t in terms])
    output = (hidden + total([t[0] for t in moved_terms] + [moved_crossed])).astype(bf16)
    normed_grad = total(near_terms + [crossed])
    shared_grads = jnp.sum(shared_grads.astype(f32), axis=0)
    grad_heads = jnp.sum(grad_heads.reshape(16, 8, 8, 256).astype(f32), axis=1).transpose(1, 0, 2)
    kv_sum = lambda start: jnp.sum(
        grad_heads[:, :, start : start + HEAD_DIM].reshape(8, KV_HEADS, 2, HEAD_DIM), axis=2
    ).reshape(8, kv_width)
    grad_qkv = jnp.concatenate(
        [grad_heads[:, :, :HEAD_DIM].reshape(8, query_width), kv_sum(HEAD_DIM), kv_sum(2 * HEAD_DIM)],
        axis=1,
    )
    grad_norm_attn = jnp.sum(grad_qkv * w_qkv.astype(f32), axis=1) / norm_attn.astype(f32)
    inputs = rows.astype(f32)
    grad_input = hidden_grad + rms_pull(inputs, inverse_rms(inputs), gain_attn, normed_grad)
    return (
        output[None],
        grad_input[None],
        grad_norm_attn,
        grad_qkv,
        shared_grads[:, :WIDTH],
        shared_grads[:, WIDTH : WIDTH + EXPERTS],
        shared_grads[:, WIDTH + EXPERTS],
        expert_grads[:, :128],
        expert_grads[:, 128:],
    )


def solution(mesh):
    return jax.shard_map(
        local,
        mesh=mesh,
        in_specs=(
            P("wshard", "seq", None),
            P("wshard", "seq", None),
            P("wshard", None),
            P(BOTH),
            P(BOTH, None),
            P(BOTH, None),
            P(BOTH, None),
            P(BOTH),
            P("seq", "wshard", None),
            P("seq", "wshard", None),
            P("wshard", "seq", None),
        ),
        out_specs=(
            P("wshard", "seq", None),
            P("wshard", "seq", None),
            P(BOTH),
            P(BOTH, None),
            P(BOTH, None),
            P(BOTH, None),
            P(BOTH),
            P("seq", "wshard", None),
            P("seq", "wshard", None),
        ),
        check_vma=False,
    )
```

```python
import jax
import jax.numpy as jnp
from jax import lax
from jax.experimental import pallas as pl
from jax.experimental.pallas import tpu as pltpu
from jax.sharding import PartitionSpec as P

HEADS = 16
KV_HEADS = 8
HEAD_DIM = 64
EXPERTS = 32
FF = 512
PROMPT = 2048
GROUP = 3584
TOK = 224
WIDTH = 1024
SLOTS = 72
STEP_ROWS = 4 * SLOTS
ALL_ROWS = 16 * SLOTS
BLOCK = 512
VMEM_LIMIT = 60 << 20
PAY = TOK + 32

norm_eps = 1e-06
rope_base = 10000.0
masked_score = -1e30
BOTH = ("seq", "wshard")
NT = (((1,), (1,)), ((), ()))
TN = (((0,), (0,)), ((), ()))
f32 = jnp.float32
bf16 = jnp.bfloat16
i32 = jnp.int32


def place_of(x, z, core):
    return x * 8 + z * 2 + core


def shift_perm(a, b):
    return [
        (place_of(x, z, c), place_of(x ^ a, (z + b) % 4, c))
        for x in range(2)
        for z in range(4)
        for c in range(2)
    ]


CORE_PERM = [(i, i ^ 1) for i in range(16)]


def send(rows, a, b):
    return lax.ppermute(rows, "seq", shift_perm(a, b))


def swap_cores(rows):
    return lax.ppermute(rows, "seq", CORE_PERM)


def relative_places(seq_index):
    x, z, c = seq_index // 8, (seq_index // 2) % 4, seq_index % 2
    r = jnp.arange(16, dtype=i32)
    a, i, k = r // 8, (r // 2) % 4, r % 2
    shift = i ^ (i // 2)
    behind = (z - i) % 4
    places = (a ^ x) * 8 + ((z - shift) % 4) * 2 + (k ^ c)
    return places, (a ^ x) * 8 + (behind ^ (behind // 2)) * 2 + (k ^ c)


def gather_near(rows):
    return [rows] + [send(rows, 0, b) for b in (1, 3, 2)], send(rows, 1, 0)


def both_cores(parts):
    mine = jnp.stack(parts)
    return mine, swap_cores(mine)


def gather_far(across):
    return [across] + [send(across, 0, b) for b in (1, 3, 2)]


def add_low(*terms):
    return sum([t.astype(f32) for t in terms]).astype(bf16)


def sum_along_z(mine, other):
    return send_along_z(chip_parts(mine, swap_cores(other)))


def chip_parts(mine, got):
    return [add_low(mine[i], got[i]) for i in range(4)]


def send_along_z(parts):
    return [parts[0]] + [send(parts[i], 0, -b) for i, b in ((1, 1), (2, 3), (3, 2))]


def swap_x(rows):
    return lax.ppermute(rows, "wshard", [(w, w ^ 1) for w in range(8)])


ALONG_Y = [[y * 2 + x for y in range(4)] for x in range(2)]


def tie(*values):
    return lax.optimization_barrier(values)


def inverse_rms(values):
    return lax.rsqrt(jnp.mean(values * values, axis=-1, keepdims=True) + norm_eps)


def rms_pull(values, scale, gain, grad):
    scaled = grad * gain
    return scale * scaled - values * (scale * scale * scale) * jnp.mean(
        scaled * values, axis=-1, keepdims=True
    )


def group_layout(lengths):
    places = jnp.arange(GROUP, dtype=i32)
    ends = jnp.cumsum(lengths)
    starts = ends - lengths
    offset_in = places - PROMPT
    segment_id = jnp.sum((offset_in[:, None] >= ends[None, :]).astype(i32), axis=1)
    segment_hot = segment_id[:, None] == jnp.arange(lengths.shape[0], dtype=i32)[None, :]
    begin = jnp.sum(jnp.where(segment_hot, starts[None, :], 0), axis=1)
    inside = offset_in >= 0
    position = jnp.where(inside, PROMPT + offset_in - begin, places)
    return position, jnp.where(inside, PROMPT + begin, 0)


def rotary_table(position):
    half_dim = HEAD_DIM // 2
    inverse = rope_base ** (-((jnp.arange(2 * HEAD_DIM) % half_dim).astype(f32) * 2.0) / HEAD_DIM)
    back = jnp.where(jnp.arange(2 * HEAD_DIM) < HEAD_DIM, 0.0, 0.5 * jnp.pi).astype(f32)
    return jnp.cos(position[:, None] * inverse[None, :] - back[None, :])


def turn(values):
    half_dim = HEAD_DIM // 2
    return jnp.concatenate([-values[:, half_dim:], values[:, :half_dim]], axis=-1)


def turn_back(values):
    half_dim = HEAD_DIM // 2
    return jnp.concatenate([values[:, half_dim:], -values[:, :half_dim]], axis=-1)


def project_kernel(places, mine, other, w, gain, table, *refs):
    out = refs[-1]
    j = pl.program_id(0)

    if len(refs) > 1:

        @pl.when(j == 0)
        def _():
            out[...] = refs[0][...]

    for k, ref in enumerate((mine, other)):
        at = pl.ds(pl.multiple_of(places[2 * j + k] * TOK, TOK), TOK)
        rows = ref[0].astype(f32)
        normed = (rows * inverse_rms(rows) * gain[...]).astype(bf16)
        projected = jnp.dot(normed, w[...], preferred_element_type=f32)
        c, s = table[at, :HEAD_DIM], table[at, HEAD_DIM:]
        q, k, v = projected[:, :64], projected[:, 64:128], projected[:, 128:]
        q = (q * c + turn(q) * s).astype(bf16).astype(f32) * HEAD_DIM**-0.5
        out[at, :] = jnp.concatenate([q, k * c + turn(k) * s, v], axis=1).astype(bf16)


def project(places, gathered, w, gain, table, before):
    chip = pl.BlockSpec((1, TOK, WIDTH), lambda j, p: (j, 0, 0))
    whole = lambda *shape: pl.BlockSpec(shape, lambda j, p: (0,) * len(shape))
    return pl.pallas_call(
        project_kernel,
        grid_spec=pltpu.PrefetchScalarGridSpec(
            num_scalar_prefetch=1,
            grid=(4,),
            in_specs=[chip, chip, whole(WIDTH, 256), whole(1, WIDTH), whole(GROUP, 128)]
            + [whole(GROUP, 256)] * len(before),
            out_specs=whole(GROUP, 256),
        ),
        out_shape=jax.ShapeDtypeStruct((GROUP, 256), bf16),
        compiler_params=pltpu.CompilerParams(vmem_limit_bytes=VMEM_LIMIT),
        cost_estimate=pl.CostEstimate(
            flops=2 * 8 * TOK * WIDTH * 256, bytes_accessed=10 << 20, transcendentals=0
        ),
    )(places, *gathered, w, gain, table, *before)


def project_back_kernel(places, first, second, w, mine, other):
    del places
    mine[0] = lax.dot_general(first[...], w[...], NT, preferred_element_type=f32).astype(bf16)
    other[0] = lax.dot_general(second[...], w[...], NT, preferred_element_type=f32).astype(bf16)


def project_back(places, projected_grad, w):
    chip = pl.BlockSpec((1, TOK, WIDTH), lambda j, p: (j, 0, 0))
    at = lambda k: pl.BlockSpec((TOK, 256), lambda j, p: (p[2 * j + k], 0))
    part = jax.ShapeDtypeStruct((4, TOK, WIDTH), bf16)
    return pl.pallas_call(
        project_back_kernel,
        grid_spec=pltpu.PrefetchScalarGridSpec(
            num_scalar_prefetch=1,
            grid=(4,),
            in_specs=[at(0), at(1), pl.BlockSpec((WIDTH, 256), lambda j, p: (0, 0))],
            out_specs=[chip, chip],
        ),
        out_shape=[part, part],
        compiler_params=pltpu.CompilerParams(vmem_limit_bytes=VMEM_LIMIT),
        cost_estimate=pl.CostEstimate(
            flops=2 * 8 * TOK * WIDTH * 256, bytes_accessed=5 << 20, transcendentals=0
        ),
    )(places, projected_grad, projected_grad, w)


def head_grad_kernel(places, near_mine, near_other, far_mine, far_other, gain, first, second, out, total):
    del places
    j = pl.program_id(0)

    @pl.when(j == 0)
    def _():
        total[...] = jnp.zeros_like(total)

    for near, far, projected in ((near_mine, far_mine, first), (near_other, far_other, second)):
        rows = jnp.where(j < 4, near[0], far[0]).astype(f32)
        normed = (rows * inverse_rms(rows) * gain[...]).astype(bf16)
        total[...] += lax.dot_general(normed, projected[...], TN, preferred_element_type=f32)

    @pl.when(j == 7)
    def _():
        out[...] = total[...].astype(bf16)


def head_weight_grad(places, near, far, gain, projected_grad):
    near_chip = pl.BlockSpec((1, TOK, WIDTH), lambda j, p: (jnp.minimum(j, 3), 0, 0))
    far_chip = pl.BlockSpec((1, TOK, WIDTH), lambda j, p: (jnp.maximum(j - 4, 0), 0, 0))
    at = lambda k: pl.BlockSpec((TOK, 256), lambda j, p: (p[2 * j + k], 0))
    return pl.pallas_call(
        head_grad_kernel,
        grid_spec=pltpu.PrefetchScalarGridSpec(
            num_scalar_prefetch=1,
            grid=(8,),
            in_specs=[
                near_chip,
                near_chip,
                far_chip,
                far_chip,
                pl.BlockSpec((1, WIDTH), lambda j, p: (0, 0)),
                at(0),
                at(1),
            ],
            out_specs=pl.BlockSpec((WIDTH, 256), lambda j, p: (0, 0)),
            scratch_shapes=[pltpu.VMEM((WIDTH, 256), f32)],
        ),
        out_shape=jax.ShapeDtypeStruct((WIDTH, 256), bf16),
        compiler_params=pltpu.CompilerParams(vmem_limit_bytes=VMEM_LIMIT),
        cost_estimate=pl.CostEstimate(
            flops=2 * 16 * TOK * WIDTH * 256, bytes_accessed=10 << 20, transcendentals=0
        ),
    )(places, *near, *far, gain, projected_grad, projected_grad)


def tile_mask(scores, key_start, query_start, begin):
    keys = key_start + lax.broadcasted_iota(i32, scores.shape, 0)
    queries = query_start + lax.broadcasted_iota(i32, scores.shape, 1)
    return jnp.where((keys <= queries) & (keys >= begin), scores, masked_score)


def key_ranges(i):
    first = PROMPT // BLOCK
    return jnp.where(i > first, i - 1, i), jnp.minimum(i, first)


def attend_kernel(qkv_ref, begin_ref, o_ref, ot_ref, lse_ref, keys, vt):
    i = pl.program_id(0)
    here = pl.ds(pl.multiple_of(i * BLOCK, BLOCK), BLOCK)

    @pl.when(i == 0)
    def _():
        keys[...] = qkv_ref[:, 64:128]
        vt[...] = qkv_ref[:, 128:192].T

    q = qkv_ref[here, :64]
    begin = begin_ref[...]

    def tile(j, carry, masked, n=1):
        peak, total, out = carry
        start = pl.multiple_of(j * BLOCK, BLOCK)
        at = pl.ds(start, n * BLOCK)
        s = lax.dot_general(keys[at, :], q, NT, preferred_element_type=f32)
        if masked:
            s = tile_mask(s, start, i * BLOCK, begin)
        higher = jnp.maximum(peak, jnp.max(s, axis=0, keepdims=True))
        p = jnp.exp(s - higher)
        fade = jnp.exp(peak - higher)
        total = total * fade + jnp.sum(p, axis=0, keepdims=True)
        out = out * fade + jnp.dot(vt[:, at], p.astype(bf16), preferred_element_type=f32)
        return higher, total, out

    carry = (
        jnp.full((1, BLOCK), masked_score, f32),
        jnp.zeros((1, BLOCK), f32),
        jnp.zeros((HEAD_DIM, BLOCK), f32),
    )
    carry = tile(i, carry, True)
    window, shared = key_ranges(i)
    carry = lax.fori_loop(window, i, lambda j, c: tile(j, c, True), carry)
    pairs = shared // 2
    carry = lax.fori_loop(0, pairs, lambda j, c: tile(2 * j, c, False, 2), carry)
    peak, total, out = lax.fori_loop(2 * pairs, shared, lambda j, c: tile(j, c, False), carry)
    ot_ref[:, here] = out * (1.0 / total)
    lse_ref[...] = peak + jnp.log(total)

    @pl.when(i == GROUP // BLOCK - 1)
    def _():
        for b in range(16):
            o_ref[b] = ot_ref[:, b * TOK : (b + 1) * TOK].astype(bf16)


def attend(qkv, begin):
    whole = lambda *shape: pl.BlockSpec(shape, lambda i: (0,) * len(shape))
    cols = lambda n: pl.BlockSpec((n, BLOCK), lambda i: (0, i))
    return pl.pallas_call(
        attend_kernel,
        grid=(GROUP // BLOCK,),
        in_specs=[whole(GROUP, 256), cols(1)],
        out_specs=[whole(16, HEAD_DIM, TOK), whole(HEAD_DIM, GROUP), cols(1)],
        out_shape=[
            jax.ShapeDtypeStruct((16, HEAD_DIM, TOK), bf16),
            jax.ShapeDtypeStruct((HEAD_DIM, GROUP), f32),
            jax.ShapeDtypeStruct((1, GROUP), f32),
        ],
        scratch_shapes=[
            pltpu.VMEM((GROUP, HEAD_DIM), bf16),
            pltpu.VMEM((HEAD_DIM, GROUP), bf16),
        ],
        compiler_params=pltpu.CompilerParams(vmem_limit_bytes=VMEM_LIMIT),
        cost_estimate=pl.CostEstimate(
            flops=2 * 27 * BLOCK * BLOCK * 512, bytes_accessed=4 << 20, transcendentals=27 * BLOCK * BLOCK
        ),
    )(qkv, begin)


def attend_back_kernel(
    qkv_ref, g_ref, ot_ref, lse_ref, begin_ref, table, out_ref, keys, values, kt, gt, dq, dk, dv
):
    i = pl.program_id(0)
    here = pl.ds(pl.multiple_of(i * BLOCK, BLOCK), BLOCK)

    @pl.when(i == 0)
    def _():
        dk[...] = jnp.zeros_like(dk)
        dv[...] = jnp.zeros_like(dv)
        keys[...] = qkv_ref[:, 64:128]
        values[...] = qkv_ref[:, 128:192]
        kt[...] = qkv_ref[:, 64:128].T
        for b in range(16):
            gt[:, b * TOK : (b + 1) * TOK] = g_ref[b]

    q = qkv_ref[here, :64]
    g = gt[:, here]
    begin = begin_ref[...]
    lse = lse_ref[...]
    inner = jnp.sum(g.astype(f32) * ot_ref[...], axis=0, keepdims=True)

    def tile(j, dq, masked, n=1):
        start = pl.multiple_of(j * BLOCK, BLOCK)
        at = pl.ds(start, n * BLOCK)
        s = lax.dot_general(keys[at, :], q, NT, preferred_element_type=f32)
        if masked:
            s = tile_mask(s, start, i * BLOCK, begin)
        p = jnp.exp(s - lse)
        dp = jnp.dot(values[at, :], g, preferred_element_type=f32)
        ds = (p * (dp - inner)).astype(bf16)
        dv[at, :] += lax.dot_general(p.astype(bf16), g, NT, preferred_element_type=f32)
        dk[at, :] += jnp.dot(ds, q, preferred_element_type=f32)
        return dq + jnp.dot(kt[:, at], ds, preferred_element_type=f32)

    dqt = tile(i, jnp.zeros((HEAD_DIM, BLOCK), f32), True)
    window, shared = key_ranges(i)
    dqt = lax.fori_loop(window, i, lambda j, c: tile(j, c, True), dqt)
    pairs = shared // 2
    dqt = lax.fori_loop(0, pairs, lambda j, c: tile(2 * j, c, False, 2), dqt)
    dqt = lax.fori_loop(2 * pairs, shared, lambda j, c: tile(j, c, False), dqt)
    dq[here, :] = dqt.T * HEAD_DIM**-0.5

    @pl.when(i == GROUP // BLOCK - 1)
    def _():
        def back(b, _):
            at = pl.ds(pl.multiple_of(b * BLOCK, BLOCK), BLOCK)
            c, s = table[at, :HEAD_DIM], table[at, HEAD_DIM:]
            q, k = dq[at, :].astype(bf16).astype(f32), dk[at, :].astype(bf16).astype(f32)
            parts = [q * c + turn_back(q * s), k * c + turn_back(k * s), dv[at, :], jnp.zeros_like(q)]
            out_ref[at, :] = jnp.concatenate(parts, axis=1).astype(bf16)
            return 0

        lax.fori_loop(0, GROUP // BLOCK, back, 0)


def attend_back(qkv, g, ot, lse, begin, table):
    whole = lambda *shape: pl.BlockSpec(shape, lambda i: (0,) * len(shape))
    cols = lambda n: pl.BlockSpec((n, BLOCK), lambda i: (0, i))
    return pl.pallas_call(
        attend_back_kernel,
        grid=(GROUP // BLOCK,),
        in_specs=[
            whole(GROUP, 256),
            whole(16, HEAD_DIM, TOK),
            cols(HEAD_DIM),
            cols(1),
            cols(1),
            whole(GROUP, 128),
        ],
        out_specs=whole(GROUP, 256),
        out_shape=jax.ShapeDtypeStruct((GROUP, 256), bf16),
        scratch_shapes=[
            pltpu.VMEM((GROUP, HEAD_DIM), bf16),
            pltpu.VMEM((GROUP, HEAD_DIM), bf16),
            pltpu.VMEM((HEAD_DIM, GROUP), bf16),
            pltpu.VMEM((HEAD_DIM, GROUP), bf16),
            pltpu.VMEM((GROUP, HEAD_DIM), f32),
            pltpu.VMEM((GROUP, HEAD_DIM), f32),
            pltpu.VMEM((GROUP, HEAD_DIM), f32),
        ],
        compiler_params=pltpu.CompilerParams(vmem_limit_bytes=VMEM_LIMIT),
        cost_estimate=pl.CostEstimate(
            flops=5 * 27 * BLOCK * BLOCK * 512, bytes_accessed=8 << 20, transcendentals=27 * BLOCK * BLOCK
        ),
    )(qkv, g, ot, lse, begin, table)


def experts_kernel(
    own_ref, ffn_mine, ffn_other, g_mine, g_other, routes_mine, routes_other, router_ref, own_w, across_w, *refs
):
    routed_mine, routed_other, moved_mine, moved_other = refs[-10:-6]
    x_ref, dh_ref, act_ref, dy_ref, w_ref, sem = refs[-6:]
    own = own_ref[0]

    copies = [
        [
            pltpu.make_async_copy(shards.at[y, e], w_ref.at[e, 2 * y + (own_ref[1] ^ a)], sem.at[a, y, e])
            for a, shards in enumerate((own_w, across_w))
            for y in range(4)
        ]
        for e in range(2)
    ]

    @pl.when(pl.program_id(0) == 0)
    def _():
        for copy in copies[0] + copies[1]:
            copy.start()

    expert_rows = lax.broadcasted_iota(i32, (EXPERTS, TOK), 0)
    slot_rows = lax.broadcasted_iota(i32, (SLOTS, TOK), 0).astype(f32)
    upto = (
        lax.broadcasted_iota(i32, (TOK, TOK), 0) <= lax.broadcasted_iota(i32, (TOK, TOK), 1)
    ).astype(f32).astype(bf16)
    slot_cols = []
    gate_grads = [jnp.zeros((EXPERTS, WIDTH), f32) for _ in range(4)]
    payload_rows = lax.broadcasted_iota(i32, (EXPERTS, WIDTH), 0)
    gate_rows = [[], []]
    picks = [[], []]
    picked_rows = [[], []]
    picked_grads = [[], []]
    blocks = [(ffn_mine, g_mine, routes_mine, 0), (ffn_other, g_other, routes_other, 0)]
    blocks = blocks + [(*refs_of[:3], 1) for refs_of in blocks]
    for rows_ref, grads_ref, routes_ref, n in blocks:
        rows, grads = rows_ref[n], grads_ref[n]
        routes = routes_ref[n][:8, :TOK].astype(f32).astype(i32)
        chosen = expert_rows == routes[0:1]
        for j in range(1, 8):
            chosen = chosen | (expert_rows == routes[j : j + 1])
        named = [jnp.max((routes == own + e).astype(f32), axis=0, keepdims=True) for e in range(2)]
        named = jnp.concatenate(named + [jnp.zeros((6, TOK), f32)], axis=0)
        rank = jnp.dot(named.astype(bf16), upto, preferred_element_type=f32)
        slots = jnp.where(named > 0, rank - 1.0, -1.0)
        slot_cols.append(slots.T)
        logits = lax.dot_general(router_ref[...], rows, NT, preferred_element_type=f32)
        peak = jnp.max(jnp.where(chosen, logits, masked_score), axis=0, keepdims=True)
        raised = jnp.where(chosen, jnp.exp(jnp.minimum(logits - peak, 0.0)), 0.0)
        gates = raised / jnp.sum(raised, axis=0, keepdims=True)
        for e in range(2):
            gate_rows[e].append(
                jnp.sum(jnp.where(expert_rows == own + e, gates, 0.0), axis=0, keepdims=True)
            )
            picks[e].append((slots[e : e + 1] == slot_rows).astype(f32))
        low = jnp.concatenate([picks[0][-1], picks[1][-1]], axis=0).astype(bf16)
        for source, kept in ((rows, picked_rows), (grads, picked_grads)):
            both = jnp.dot(low, source, preferred_element_type=f32)
            kept[0].append(both[:SLOTS])
            kept[1].append(both[SLOTS:])
    moved, routed = [], []
    for e in range(2):

        @pl.when(pl.program_id(0) == 0)
        def _():
            for copy in copies[e]:
                copy.wait()

        w_gate_up = w_ref[e, :, :128, :].reshape(WIDTH, 2 * FF)
        w_down = w_ref[e, :, 128:, :].reshape(FF, WIDTH)
        x = jnp.concatenate(picked_rows[e], axis=0).astype(bf16)
        gate = jnp.concatenate(
            [jnp.sum(p * r, axis=1, keepdims=True) for p, r in zip(picks[e], gate_rows[e])], axis=0
        )
        grads = jnp.concatenate(picked_grads[e], axis=0)
        dy = (gate * grads).astype(bf16)
        mixed = jnp.dot(x, w_gate_up, preferred_element_type=f32)
        dact = lax.dot_general(dy, w_down, NT, preferred_element_type=f32)
        gate_part, up_part = mixed[:, :FF], mixed[:, FF:]
        sigma = 1.0 / (1.0 + jnp.exp(-gate_part))
        silu = gate_part * sigma
        act = (silu * up_part).astype(bf16)
        dh = jnp.concatenate(
            [dact * up_part * (sigma + silu * (1.0 - sigma)), dact * silu], axis=1
        ).astype(bf16)
        x_ref[e] = x
        dy_ref[e] = dy
        act_ref[e] = act
        dh_ref[e] = dh
        returned = jnp.dot(act, w_down, preferred_element_type=f32).astype(bf16).astype(f32)
        dgate = jnp.sum(returned * grads, axis=1, keepdims=True)
        for b in range(4):
            grad = jnp.sum(
                picks[e][b] * dgate[b * SLOTS : (b + 1) * SLOTS], axis=0, keepdims=True
            )
            high = grad.astype(bf16).astype(f32)
            gap = jnp.zeros((1, 256 - TOK), f32)
            wide = jnp.concatenate([high, gap, grad - high, gap, jnp.zeros((1, WIDTH - 512), f32)], axis=1)
            gate_grads[b] = gate_grads[b] + jnp.where(payload_rows == own + e, wide, 0.0)
        moved.append(gate * returned)
        routed.append(lax.dot_general(dh, w_gate_up, NT, preferred_element_type=f32))
    columns = lax.broadcasted_iota(i32, (TOK, 2 * SLOTS), 1).astype(f32)
    outs = [(routed_mine, moved_mine, 0), (routed_other, moved_other, 0), (routed_mine, moved_mine, 1), (routed_other, moved_other, 1)]
    for b, (routed_ref, moved_ref, n) in enumerate(outs):
        first, second = slot_cols[b][:, 0:1], slot_cols[b][:, 1:2]
        back = ((columns == first) | ((columns == second + SLOTS) & (second >= 0))).astype(f32).astype(bf16)
        at = slice(b * SLOTS, (b + 1) * SLOTS)
        for terms, ref in ((routed, routed_ref), (moved, moved_ref)):
            joined = jnp.concatenate([terms[0][at], terms[1][at]], axis=0).astype(bf16)
            ref[n, :TOK, :] = jnp.dot(back, joined, preferred_element_type=f32).astype(bf16)
        routed_ref[n, TOK:, :] = gate_grads[b].astype(bf16)


def run_experts(half, own, ffn, grads, weights, router, before):
    pair = pl.BlockSpec((2, TOK, WIDTH), lambda i, o: (i, 0, 0))
    pair_of_all = pl.BlockSpec((2, TOK, WIDTH), lambda i, o: (i + 2 * half, 0, 0))
    whole = lambda shape: pl.BlockSpec(shape, lambda i, o: (0,) * len(shape))
    routes = pl.BlockSpec((2, 16, 256), lambda i, o: (i, TOK // 16, 0))
    summed = pl.BlockSpec((2, PAY, WIDTH), lambda i, o: (i, 0, 0))
    kept = lambda n: pl.BlockSpec((2, STEP_ROWS, n), lambda i, o: (0, i + 2 * half, 0))
    part = jax.ShapeDtypeStruct((4, PAY, WIDTH), bf16)
    keep = lambda n: jax.ShapeDtypeStruct((2, ALL_ROWS, n), bf16)
    return pl.pallas_call(
        experts_kernel,
        grid_spec=pltpu.PrefetchScalarGridSpec(
            num_scalar_prefetch=1,
            grid=(2,),
            in_specs=[
                pair,
                pair,
                pair,
                pair,
                routes,
                routes,
                whole((EXPERTS, WIDTH)),
            ]
            + [pl.BlockSpec(memory_space=pl.ANY)] * (2 + len(before)),
            out_specs=[
                summed,
                summed,
                pair_of_all,
                pair_of_all,
                kept(WIDTH),
                kept(2 * FF),
                kept(FF),
                kept(WIDTH),
            ],
            scratch_shapes=[
                pltpu.VMEM((2, 8, 192, 1024), bf16),
                pltpu.SemaphoreType.DMA((2, 4, 2)),
            ],
        ),
        out_shape=[
            part,
            part,
            jax.ShapeDtypeStruct((8, TOK, WIDTH), bf16),
            jax.ShapeDtypeStruct((8, TOK, WIDTH), bf16),
            keep(WIDTH),
            keep(2 * FF),
            keep(FF),
            keep(WIDTH),
        ],
        input_output_aliases={10 + i: 2 + i for i in range(len(before))},
        compiler_params=pltpu.CompilerParams(vmem_limit_bytes=VMEM_LIMIT),
        cost_estimate=pl.CostEstimate(
            flops=14 << 30, bytes_accessed=24 << 20, transcendentals=8 * SLOTS * 2 * FF
        ),
    )(own, *ffn, *grads, *grads, router, *weights, *before)


def expert_grads_kernel(x_ref, dh_ref, act_ref, dy_ref, out_ref):
    up = lax.dot_general(x_ref[0], dh_ref[0], TN, preferred_element_type=f32)
    down = lax.dot_general(act_ref[0], dy_ref[0], TN, preferred_element_type=f32)
    out_ref[0, :, 0, :128, :] = up.astype(bf16).reshape(2, 128, 2 * FF)
    out_ref[0, :, 0, 128:, :] = down.astype(bf16).reshape(2, 64, WIDTH)


def expert_weight_grads(x, dh, act, dy):
    return pl.pallas_call(
        expert_grads_kernel,
        grid=(2, 4),
        in_specs=[
            pl.BlockSpec((1, ALL_ROWS, 256), lambda e, i: (e, 0, i)),
            pl.BlockSpec((1, ALL_ROWS, 2 * FF), lambda e, i: (e, 0, 0)),
            pl.BlockSpec((1, ALL_ROWS, 128), lambda e, i: (e, 0, i)),
            pl.BlockSpec((1, ALL_ROWS, WIDTH), lambda e, i: (e, 0, 0)),
        ],
        out_specs=pl.BlockSpec((1, 2, 1, 192, 1024), lambda e, i: (i, 0, e, 0, 0)),
        out_shape=jax.ShapeDtypeStruct((4, 2, 2, 192, 1024), bf16),
        compiler_params=pltpu.CompilerParams(vmem_limit_bytes=VMEM_LIMIT),
        cost_estimate=pl.CostEstimate(flops=8 << 30, bytes_accessed=14 << 20, transcendentals=0),
    )(x, dh, act, dy)


def hidden_kernel(att_ref, w_ref, rows_ref, gain_ref, hidden_ref, normed_ref):
    att = att_ref[...].reshape(WIDTH, TOK)
    hidden = rows_ref[...].astype(f32) + lax.dot_general(
        att, w_ref[:, :WIDTH], TN, preferred_element_type=f32
    )
    hidden_ref[...] = hidden
    normed_ref[...] = (hidden * inverse_rms(hidden) * gain_ref[...]).astype(bf16)


def hidden_of(attended, shared, rows, gain):
    return pl.pallas_call(
        hidden_kernel,
        out_shape=[
            jax.ShapeDtypeStruct((TOK, WIDTH), f32),
            jax.ShapeDtypeStruct((TOK, WIDTH), bf16),
        ],
        compiler_params=pltpu.CompilerParams(vmem_limit_bytes=VMEM_LIMIT),
        cost_estimate=pl.CostEstimate(
            flops=2 * TOK * WIDTH * WIDTH, bytes_accessed=5 << 20, transcendentals=0
        ),
    )(attended, shared, rows, gain)


def hidden_back_kernel(
    t0, t1, t2, t3, crossed, hidden_ref, normed_ref, chosen_ref, router_ref, g_ref, gain_ref,
    w_ref, hidden_grad_ref, branch_ref, logit_ref, scaled_ref, att_ref
):
    chosen = chosen_ref[...] > 0
    logits = lax.dot_general(router_ref[...], normed_ref[...], NT, preferred_element_type=f32)
    peak = jnp.max(jnp.where(chosen, logits, masked_score), axis=0, keepdims=True)
    raised = jnp.where(chosen, jnp.exp(jnp.minimum(logits - peak, 0.0)), 0.0)
    gates = raised / jnp.sum(raised, axis=0, keepdims=True)
    summed = t0[...].astype(f32)
    for term in (t1, t2, t3, crossed):
        summed = summed + term[...].astype(f32)
    gate_grad = summed[TOK:, :TOK] + summed[TOK:, 256 : 256 + TOK]
    logit_grad = gates * (gate_grad - jnp.sum(gates * gate_grad, axis=0, keepdims=True))
    logit_grad = logit_grad.astype(bf16)
    logit_ref[...] = logit_grad
    normed_grad = summed[:TOK] + lax.dot_general(
        logit_grad, router_ref[...], TN, preferred_element_type=f32
    )
    hidden = hidden_ref[...]
    scale = inverse_rms(hidden)
    scaled_ref[...] = (normed_grad * hidden * scale).astype(bf16)
    hidden_grad = g_ref[...].astype(f32) + rms_pull(hidden, scale, gain_ref[...], normed_grad)
    hidden_grad_ref[...] = hidden_grad
    branch = hidden_grad.astype(bf16)
    branch_ref[...] = branch
    att = lax.dot_general(w_ref[:, :WIDTH], branch, NT, preferred_element_type=f32)
    att_ref[...] = att.astype(bf16).reshape(HEADS, HEAD_DIM, TOK)


def hidden_back(terms, crossed, hidden, normed, chosen, router_t, g, gain, shared):
    wide = lambda t: jax.ShapeDtypeStruct((TOK, WIDTH), t)
    return pl.pallas_call(
        hidden_back_kernel,
        out_shape=[
            wide(f32),
            wide(bf16),
            jax.ShapeDtypeStruct((EXPERTS, TOK), bf16),
            wide(bf16),
            jax.ShapeDtypeStruct((HEADS, HEAD_DIM, TOK), bf16),
        ],
        compiler_params=pltpu.CompilerParams(vmem_limit_bytes=VMEM_LIMIT),
        cost_estimate=pl.CostEstimate(
            flops=2 * TOK * WIDTH * WIDTH, bytes_accessed=8 << 20, transcendentals=0
        ),
    )(*terms, crossed, hidden, normed, chosen, router_t, g, gain, shared)


def shared_grads_kernel(att_ref, branch_ref, normed_ref, logit_ref, scaled_ref, out_ref):
    over_tokens = (((0,), (1,)), ((), ()))
    logit = jnp.concatenate([logit_ref[...], jnp.zeros((96, TOK), bf16)], axis=0)
    ones = (lax.broadcasted_iota(i32, (128, TOK), 0) == EXPERTS).astype(f32).astype(bf16)
    att = att_ref[...].reshape(WIDTH, TOK)
    grads = [
        jnp.dot(att, branch_ref[...], preferred_element_type=f32),
        lax.dot_general(normed_ref[...], logit, over_tokens, preferred_element_type=f32)
        + lax.dot_general(scaled_ref[...], ones, over_tokens, preferred_element_type=f32),
    ]
    for w in range(8):
        for part, at in zip(grads, (slice(0, WIDTH), slice(WIDTH, None))):
            rows = [part[s * 64 + w * 8 : s * 64 + w * 8 + 8] for s in range(16)]
            out_ref[w, :, at] = jnp.concatenate(rows, axis=0).astype(bf16)


def shared_weight_grads(att, branch, normed, logit_grad, scaled):
    return pl.pallas_call(
        shared_grads_kernel,
        out_shape=jax.ShapeDtypeStruct((8, 128, 1152), bf16),
        compiler_params=pltpu.CompilerParams(vmem_limit_bytes=VMEM_LIMIT),
        cost_estimate=pl.CostEstimate(
            flops=2 * TOK * WIDTH * 1280, bytes_accessed=5 << 20, transcendentals=0
        ),
    )(att, branch, normed, logit_grad, scaled)


def local(
    tokens,
    routes,
    cont_lengths,
    norm_attn,
    w_qkv,
    w_out,
    w_router,
    norm_ffn,
    w_gate_up,
    w_down,
    cotangent,
):
    seq_index = lax.axis_index("seq")
    places, blocks = relative_places(seq_index)
    rows = tokens[0]
    query_width = HEADS * HEAD_DIM
    kv_width = KV_HEADS * HEAD_DIM

    position, begin = group_layout(cont_lengths[0])
    begin = begin[None]
    table = rotary_table(position.astype(f32))
    kv_heads = lambda start: jnp.repeat(
        w_qkv[:, start : start + kv_width].reshape(8, KV_HEADS, HEAD_DIM), 2, axis=1
    )
    head_cols = jnp.concatenate(
        [
            w_qkv[:, :query_width].reshape(8, HEADS, HEAD_DIM),
            kv_heads(query_width),
            kv_heads(query_width + kv_width),
            jnp.broadcast_to(norm_attn[:, None, None], (8, HEADS, HEAD_DIM)),
        ],
        axis=2,
    ).transpose(1, 0, 2)
    head_cols = jnp.broadcast_to(head_cols[:, None], (HEADS, 8, 8, 256)).reshape(128, 8, 256)
    head_weights = lax.all_to_all(head_cols, BOTH, 0, 0, tiled=True).reshape(WIDTH, 256)
    gain_attn = head_weights[:, 192].astype(f32)[None]
    head_weights = jnp.where(jnp.arange(256)[None] < 192, head_weights, 0.0).astype(bf16)

    rows_near, rows_across = gather_near(rows)
    rows_near, _, table, head_weights = tie(rows_near, rows_across, table, head_weights)
    rows_near, rows_far = both_cores(rows_near), gather_far(rows_across)

    own_x = lax.axis_index("wshard") % 2
    expert_rows = jnp.concatenate([w_gate_up, w_down], axis=1)
    along_y = lambda t: lax.all_gather(t, "wshard", axis_index_groups=ALONG_Y, axis=0)
    experts, expert_rows = along_y(expert_rows), swap_x(expert_rows)

    qkv = project(places[:8], rows_near, head_weights, gain_attn, table, ())
    shared = jnp.concatenate(
        [w_out, w_router, norm_ffn[:, None], jnp.zeros((8, 95), bf16)], axis=1
    )
    shared, qkv = tie(shared, qkv)
    shared = lax.all_to_all(
        jnp.broadcast_to(shared[None], (128, 8, 1152)), BOTH, 0, 0, tiled=True
    ).reshape(WIDTH, 1152)
    routes_rows = jnp.pad(routes[0].T.astype(bf16), ((0, 8), (0, WIDTH - TOK)))
    upstream_rows = jnp.concatenate([cotangent[0], routes_rows], axis=0)
    rows_far, qkv, upstream_rows, expert_rows = tie(rows_far, qkv, upstream_rows, expert_rows)
    experts = [experts, along_y(expert_rows)]
    rows_far = both_cores(rows_far)
    grad_near = [upstream_rows] + [send(upstream_rows, 0, b) for b in (1, 3, 2)]
    qkv = project(places[8:], rows_far, head_weights, gain_attn, table, (qkv,))

    router_t = shared[:, WIDTH : WIDTH + EXPERTS].T
    gain_ffn = shared[:, WIDTH + EXPERTS].astype(f32)[None]
    attended_head, attended_t, lse = attend(qkv, begin)
    attended_head, shared = tie(attended_head, shared)
    attended = lax.all_to_all(attended_head, "seq", 0, 0, tiled=True)
    attended, grad_near = tie(attended, grad_near)
    grad_near = jnp.stack(grad_near)
    hidden, normed_ffn = hidden_of(attended, shared, rows, gain_ffn)
    ffn_near, ffn_across = gather_near(normed_ffn)
    ffn_near, _ = tie(ffn_near, ffn_across)
    grad_near_mine, _ = tie(grad_near, ffn_across)
    grad_far = send(grad_near_mine, 1, 0)
    grad_near = (grad_near, swap_cores(grad_near))
    ffn_near, ffn_far = both_cores(ffn_near), gather_far(ffn_across)
    own = jnp.stack([seq_index * 2, own_x])
    near = run_experts(0, own, ffn_near, grad_near, experts, router_t, ())
    near_terms = sum_along_z(*near[:2])
    ffn_far = both_cores(ffn_far)
    grad_far = (grad_far, swap_cores(grad_far))
    far = run_experts(1, own, ffn_far, grad_far, experts, router_t, near[2:])
    far, near_terms = tie(far, near_terms)
    moved, saved = far[2:4], far[4:]
    far_other, moved_other = tie(swap_cores(far[1]), moved[1])
    far_terms = send_along_z(chip_parts(far[0], far_other))
    expert_grads = expert_weight_grads(*saved)
    moved_other = swap_cores(moved_other)
    far_terms, expert_grads, moved_other = tie(far_terms, expert_grads, moved_other)
    crossed = send(add_low(*far_terms), 1, 0)
    by_x = [t.reshape(2, 4, TOK, WIDTH) for t in (moved[0], moved_other)]
    moved_parts = [add_low(by_x[0][:, i], by_x[1][:, i]) for i in range(4)]
    crossed, moved_parts = tie(crossed, moved_parts)

    expert_range = jnp.arange(EXPERTS, dtype=i32)
    chosen_here = jnp.any(routes[0].T[None] == expert_range[:, None, None], axis=1).astype(f32)
    hidden_grad, branch_grad, logit_grad, scaled_grad, attended_grad = hidden_back(
        near_terms, crossed, hidden, normed_ffn, chosen_here, router_t, cotangent[0], gain_ffn, shared
    )
    expert_grads = lax.psum_scatter(
        expert_grads.reshape(8, 2, 192, 1024),
        "wshard",
        axis_index_groups=ALONG_Y,
        scatter_dimension=0,
        tiled=True,
    )
    head_grad = lax.all_to_all(attended_grad, "seq", 0, 0, tiled=True)
    shared_grads = shared_weight_grads(attended, branch_grad, normed_ffn, logit_grad, scaled_grad)
    head_grad, shared_grads, moved_parts = tie(head_grad, shared_grads, moved_parts)
    moved_terms = [moved_parts[0]] + [
        send(moved_parts[i], 0, -b) for i, b in ((1, 1), (2, 3), (3, 2))
    ]

    shared_grads = lax.all_to_all(shared_grads, "wshard", 0, 0, tiled=True)
    projected_grad = attend_back(qkv, head_grad, attended_t, lse, begin, table)
    far_part = project_back(places[8:], projected_grad, head_weights)
    far_part, shared_grads, moved_terms = tie(far_part, shared_grads, moved_terms)
    far_parts = chip_parts(far_part[0], swap_cores(far_part[1]))
    near_part = project_back(places[:8], projected_grad, head_weights)
    near_part, expert_grads = tie(near_part, expert_grads)
    far_parts, projected_grad, shared_grads, moved_terms, expert_grads = tie(
        far_parts, projected_grad, shared_grads, moved_terms, expert_grads
    )
    far_terms = send_along_z(far_parts)
    near_parts = chip_parts(near_part[0], swap_cores(near_part[1]))
    moved_crossed = send(add_low(*[t[1] for t in moved_terms]), 1, 0)
    shared_grads = jnp.sum(shared_grads.astype(f32), axis=0).astype(bf16).reshape(16, 8, 1152)
    shared_grads = lax.all_to_all(shared_grads, "seq", 0, 0, tiled=True)
    grad_head = head_weight_grad(places, rows_near, rows_far, gain_attn, projected_grad)
    far_terms, near_parts, grad_head = tie(far_terms, near_parts, grad_head)
    near_terms = send_along_z(near_parts)
    grad_heads = lax.all_to_all(grad_head.reshape(128, 8, 256), BOTH, 0, 0, tiled=True)
    crossed = send(add_low(*far_terms), 1, 0)
    crossed, near_terms, grad_heads, shared_grads = tie(
        crossed, near_terms, grad_heads, shared_grads
    )
    kept = lax.dynamic_index_in_dim(expert_grads, own_x, 0, keepdims=False)
    sent = lax.dynamic_index_in_dim(expert_grads, 1 - own_x, 0, keepdims=False)
    expert_grads = kept.astype(f32) + swap_x(sent).astype(f32)
    total = lambda terms: sum([t.astype(f32) for t in terms])
    output = (hidden + total([t[0] for t in moved_terms] + [moved_crossed])).astype(bf16)
    normed_grad = total(near_terms + [crossed])
    shared_grads = jnp.sum(shared_grads.astype(f32), axis=0)
    grad_heads = jnp.sum(grad_heads.reshape(16, 8, 8, 256).astype(f32), axis=1).transpose(1, 0, 2)
    kv_sum = lambda start: jnp.sum(
        grad_heads[:, :, start : start + HEAD_DIM].reshape(8, KV_HEADS, 2, HEAD_DIM), axis=2
    ).reshape(8, kv_width)
    grad_qkv = jnp.concatenate(
        [grad_heads[:, :, :HEAD_DIM].reshape(8, query_width), kv_sum(HEAD_DIM), kv_sum(2 * HEAD_DIM)],
        axis=1,
    )
    grad_norm_attn = jnp.sum(grad_qkv * w_qkv.astype(f32), axis=1) / norm_attn.astype(f32)
    inputs = rows.astype(f32)
    grad_input = hidden_grad + rms_pull(inputs, inverse_rms(inputs), gain_attn, normed_grad)
    return (
        output[None],
        grad_input[None],
        grad_norm_attn,
        grad_qkv,
        shared_grads[:, :WIDTH],
        shared_grads[:, WIDTH : WIDTH + EXPERTS],
        shared_grads[:, WIDTH + EXPERTS],
        expert_grads[:, :128],
        expert_grads[:, 128:],
    )


def solution(mesh):
    return jax.shard_map(
        local,
        mesh=mesh,
        in_specs=(
            P("wshard", "seq", None),
            P("wshard", "seq", None),
            P("wshard", None),
            P(BOTH),
            P(BOTH, None),
            P(BOTH, None),
            P(BOTH, None),
            P(BOTH),
            P("seq", "wshard", None),
            P("seq", "wshard", None),
            P("wshard", "seq", None),
        ),
        out_specs=(
            P("wshard", "seq", None),
            P("wshard", "seq", None),
            P(BOTH),
            P(BOTH, None),
            P(BOTH, None),
            P(BOTH, None),
            P(BOTH),
            P("seq", "wshard", None),
            P("seq", "wshard", None),
        ),
        check_vma=False,
    )
```

```python
import jax
import jax.numpy as jnp
from jax import lax
from jax.experimental import pallas as pl
from jax.experimental.pallas import tpu as pltpu
from jax.sharding import PartitionSpec as P

HEADS = 16
KV_HEADS = 8
HEAD_DIM = 64
EXPERTS = 32
FF = 512
PROMPT = 2048
GROUP = 3584
TOK = 224
WIDTH = 1024
SLOTS = 72
STEP_ROWS = 4 * SLOTS
ALL_ROWS = 16 * SLOTS
BLOCK = 512
VMEM_LIMIT = 60 << 20
PAY = TOK + 32

norm_eps = 1e-06
rope_base = 10000.0
masked_score = -1e30
BOTH = ("seq", "wshard")
NT = (((1,), (1,)), ((), ()))
TN = (((0,), (0,)), ((), ()))
f32 = jnp.float32
bf16 = jnp.bfloat16
i32 = jnp.int32


def place_of(x, z, core):
    return x * 8 + z * 2 + core


def shift_perm(a, b):
    return [
        (place_of(x, z, c), place_of(x ^ a, (z + b) % 4, c))
        for x in range(2)
        for z in range(4)
        for c in range(2)
    ]


CORE_PERM = [(i, i ^ 1) for i in range(16)]


def send(rows, a, b):
    return lax.ppermute(rows, "seq", shift_perm(a, b))


def swap_cores(rows):
    return lax.ppermute(rows, "seq", CORE_PERM)


def relative_places(seq_index):
    x, z, c = seq_index // 8, (seq_index // 2) % 4, seq_index % 2
    r = jnp.arange(16, dtype=i32)
    a, i, k = r // 8, (r // 2) % 4, r % 2
    shift = i ^ (i // 2)
    behind = (z - i) % 4
    places = (a ^ x) * 8 + ((z - shift) % 4) * 2 + (k ^ c)
    return places, (a ^ x) * 8 + (behind ^ (behind // 2)) * 2 + (k ^ c)


def gather_near(rows):
    return [rows] + [send(rows, 0, b) for b in (1, 3, 2)], send(rows, 1, 0)


def both_cores(parts):
    mine = jnp.stack(parts)
    return mine, swap_cores(mine)


def gather_far(across):
    return [across] + [send(across, 0, b) for b in (1, 3, 2)]


def add_low(*terms):
    return sum([t.astype(f32) for t in terms]).astype(bf16)


def sum_along_z(mine, other):
    return send_along_z(chip_parts(mine, swap_cores(other)))


def chip_parts(mine, got):
    return [add_low(mine[i], got[i]) for i in range(4)]


def send_along_z(parts):
    return [parts[0]] + [send(parts[i], 0, -b) for i, b in ((1, 1), (2, 3), (3, 2))]


def swap_x(rows):
    return lax.ppermute(rows, "wshard", [(w, w ^ 1) for w in range(8)])


ALONG_Y = [[y * 2 + x for y in range(4)] for x in range(2)]


def tie(*values):
    return lax.optimization_barrier(values)


def inverse_rms(values):
    return lax.rsqrt(jnp.mean(values * values, axis=-1, keepdims=True) + norm_eps)


def rms_pull(values, scale, gain, grad):
    scaled = grad * gain
    return scale * scaled - values * (scale * scale * scale) * jnp.mean(
        scaled * values, axis=-1, keepdims=True
    )


def group_layout(lengths):
    places = jnp.arange(GROUP, dtype=i32)
    ends = jnp.cumsum(lengths)
    starts = ends - lengths
    offset_in = places - PROMPT
    segment_id = jnp.sum((offset_in[:, None] >= ends[None, :]).astype(i32), axis=1)
    segment_hot = segment_id[:, None] == jnp.arange(lengths.shape[0], dtype=i32)[None, :]
    begin = jnp.sum(jnp.where(segment_hot, starts[None, :], 0), axis=1)
    inside = offset_in >= 0
    position = jnp.where(inside, PROMPT + offset_in - begin, places)
    return position, jnp.where(inside, PROMPT + begin, 0)


def rotary_table(position):
    half_dim = HEAD_DIM // 2
    inverse = rope_base ** (-((jnp.arange(2 * HEAD_DIM) % half_dim).astype(f32) * 2.0) / HEAD_DIM)
    back = jnp.where(jnp.arange(2 * HEAD_DIM) < HEAD_DIM, 0.0, 0.5 * jnp.pi).astype(f32)
    return jnp.cos(position[:, None] * inverse[None, :] - back[None, :])


def turn(values):
    half_dim = HEAD_DIM // 2
    return jnp.concatenate([-values[:, half_dim:], values[:, :half_dim]], axis=-1)


def turn_back(values):
    half_dim = HEAD_DIM // 2
    return jnp.concatenate([values[:, half_dim:], -values[:, :half_dim]], axis=-1)


def project_kernel(places, mine, other, w, gain, table, *refs):
    out = refs[-1]
    j = pl.program_id(0)

    if len(refs) > 1:

        @pl.when(j == 0)
        def _():
            out[...] = refs[0][...]

    for k, ref in enumerate((mine, other)):
        at = pl.ds(pl.multiple_of(places[2 * j + k] * TOK, TOK), TOK)
        rows = ref[0].astype(f32)
        normed = (rows * inverse_rms(rows) * gain[...]).astype(bf16)
        projected = jnp.dot(normed, w[...], preferred_element_type=f32)
        c, s = table[at, :HEAD_DIM], table[at, HEAD_DIM:]
        q, k, v = projected[:, :64], projected[:, 64:128], projected[:, 128:]
        q = (q * c + turn(q) * s).astype(bf16).astype(f32) * HEAD_DIM**-0.5
        out[at, :] = jnp.concatenate([q, k * c + turn(k) * s, v], axis=1).astype(bf16)


def project(places, gathered, w, gain, table, before):
    chip = pl.BlockSpec((1, TOK, WIDTH), lambda j, p: (j, 0, 0))
    whole = lambda *shape: pl.BlockSpec(shape, lambda j, p: (0,) * len(shape))
    return pl.pallas_call(
        project_kernel,
        grid_spec=pltpu.PrefetchScalarGridSpec(
            num_scalar_prefetch=1,
            grid=(4,),
            in_specs=[chip, chip, whole(WIDTH, 256), whole(1, WIDTH), whole(GROUP, 128)]
            + [whole(GROUP, 256)] * len(before),
            out_specs=whole(GROUP, 256),
        ),
        out_shape=jax.ShapeDtypeStruct((GROUP, 256), bf16),
        compiler_params=pltpu.CompilerParams(vmem_limit_bytes=VMEM_LIMIT),
        cost_estimate=pl.CostEstimate(
            flops=2 * 8 * TOK * WIDTH * 256, bytes_accessed=10 << 20, transcendentals=0
        ),
    )(places, *gathered, w, gain, table, *before)


def project_back_kernel(places, first, second, w, mine, other):
    del places
    mine[0] = lax.dot_general(first[...], w[...], NT, preferred_element_type=f32).astype(bf16)
    other[0] = lax.dot_general(second[...], w[...], NT, preferred_element_type=f32).astype(bf16)


def project_back(places, projected_grad, w):
    chip = pl.BlockSpec((1, TOK, WIDTH), lambda j, p: (j, 0, 0))
    at = lambda k: pl.BlockSpec((TOK, 256), lambda j, p: (p[2 * j + k], 0))
    part = jax.ShapeDtypeStruct((4, TOK, WIDTH), bf16)
    return pl.pallas_call(
        project_back_kernel,
        grid_spec=pltpu.PrefetchScalarGridSpec(
            num_scalar_prefetch=1,
            grid=(4,),
            in_specs=[at(0), at(1), pl.BlockSpec((WIDTH, 256), lambda j, p: (0, 0))],
            out_specs=[chip, chip],
        ),
        out_shape=[part, part],
        compiler_params=pltpu.CompilerParams(vmem_limit_bytes=VMEM_LIMIT),
        cost_estimate=pl.CostEstimate(
            flops=2 * 8 * TOK * WIDTH * 256, bytes_accessed=5 << 20, transcendentals=0
        ),
    )(places, projected_grad, projected_grad, w)


def head_grad_kernel(places, near_mine, near_other, far_mine, far_other, gain, first, second, out, total):
    del places
    j = pl.program_id(0)

    @pl.when(j == 0)
    def _():
        total[...] = jnp.zeros_like(total)

    for near, far, projected in ((near_mine, far_mine, first), (near_other, far_other, second)):
        rows = jnp.where(j < 4, near[0], far[0]).astype(f32)
        normed = (rows * inverse_rms(rows) * gain[...]).astype(bf16)
        total[...] += lax.dot_general(normed, projected[...], TN, preferred_element_type=f32)

    @pl.when(j == 7)
    def _():
        out[...] = total[...].astype(bf16)


def head_weight_grad(places, near, far, gain, projected_grad):
    near_chip = pl.BlockSpec((1, TOK, WIDTH), lambda j, p: (jnp.minimum(j, 3), 0, 0))
    far_chip = pl.BlockSpec((1, TOK, WIDTH), lambda j, p: (jnp.maximum(j - 4, 0), 0, 0))
    at = lambda k: pl.BlockSpec((TOK, 256), lambda j, p: (p[2 * j + k], 0))
    return pl.pallas_call(
        head_grad_kernel,
        grid_spec=pltpu.PrefetchScalarGridSpec(
            num_scalar_prefetch=1,
            grid=(8,),
            in_specs=[
                near_chip,
                near_chip,
                far_chip,
                far_chip,
                pl.BlockSpec((1, WIDTH), lambda j, p: (0, 0)),
                at(0),
                at(1),
            ],
            out_specs=pl.BlockSpec((WIDTH, 256), lambda j, p: (0, 0)),
            scratch_shapes=[pltpu.VMEM((WIDTH, 256), f32)],
        ),
        out_shape=jax.ShapeDtypeStruct((WIDTH, 256), bf16),
        compiler_params=pltpu.CompilerParams(vmem_limit_bytes=VMEM_LIMIT),
        cost_estimate=pl.CostEstimate(
            flops=2 * 16 * TOK * WIDTH * 256, bytes_accessed=10 << 20, transcendentals=0
        ),
    )(places, *near, *far, gain, projected_grad, projected_grad)


def tile_mask(scores, key_start, query_start, begin):
    keys = key_start + lax.broadcasted_iota(i32, scores.shape, 0)
    queries = query_start + lax.broadcasted_iota(i32, scores.shape, 1)
    return jnp.where((keys <= queries) & (keys >= begin), scores, masked_score)


def key_ranges(i):
    first = PROMPT // BLOCK
    return jnp.where(i > first, i - 1, i), jnp.minimum(i, first)


def attend_kernel(qkv_ref, begin_ref, o_ref, ot_ref, lse_ref, keys, vt):
    i = pl.program_id(0)
    here = pl.ds(pl.multiple_of(i * BLOCK, BLOCK), BLOCK)

    @pl.when(i == 0)
    def _():
        keys[...] = qkv_ref[:, 64:128]
        vt[...] = qkv_ref[:, 128:192].T

    q = qkv_ref[here, :64]
    begin = begin_ref[...]

    def tile(j, carry, masked, n=1):
        peak, total, out = carry
        start = pl.multiple_of(j * BLOCK, BLOCK)
        at = pl.ds(start, n * BLOCK)
        s = lax.dot_general(keys[at, :], q, NT, preferred_element_type=f32)
        if masked:
            s = tile_mask(s, start, i * BLOCK, begin)
        higher = jnp.maximum(peak, jnp.max(s, axis=0, keepdims=True))
        p = jnp.exp(s - higher)
        fade = jnp.exp(peak - higher)
        total = total * fade + jnp.sum(p, axis=0, keepdims=True)
        out = out * fade + jnp.dot(vt[:, at], p.astype(bf16), preferred_element_type=f32)
        return higher, total, out

    carry = (
        jnp.full((1, BLOCK), masked_score, f32),
        jnp.zeros((1, BLOCK), f32),
        jnp.zeros((HEAD_DIM, BLOCK), f32),
    )
    carry = tile(i, carry, True)
    window, shared = key_ranges(i)
    carry = lax.fori_loop(window, i, lambda j, c: tile(j, c, True), carry)
    pairs = shared // 2
    carry = lax.fori_loop(0, pairs, lambda j, c: tile(2 * j, c, False, 2), carry)
    peak, total, out = lax.fori_loop(2 * pairs, shared, lambda j, c: tile(j, c, False), carry)
    ot_ref[:, here] = out * (1.0 / total)
    lse_ref[...] = peak + jnp.log(total)

    @pl.when(i == GROUP // BLOCK - 1)
    def _():
        for b in range(16):
            o_ref[b] = ot_ref[:, b * TOK : (b + 1) * TOK].astype(bf16)


def attend(qkv, begin):
    whole = lambda *shape: pl.BlockSpec(shape, lambda i: (0,) * len(shape))
    cols = lambda n: pl.BlockSpec((n, BLOCK), lambda i: (0, i))
    return pl.pallas_call(
        attend_kernel,
        grid=(GROUP // BLOCK,),
        in_specs=[whole(GROUP, 256), cols(1)],
        out_specs=[whole(16, HEAD_DIM, TOK), whole(HEAD_DIM, GROUP), cols(1)],
        out_shape=[
            jax.ShapeDtypeStruct((16, HEAD_DIM, TOK), bf16),
            jax.ShapeDtypeStruct((HEAD_DIM, GROUP), f32),
            jax.ShapeDtypeStruct((1, GROUP), f32),
        ],
        scratch_shapes=[
            pltpu.VMEM((GROUP, HEAD_DIM), bf16),
            pltpu.VMEM((HEAD_DIM, GROUP), bf16),
        ],
        compiler_params=pltpu.CompilerParams(vmem_limit_bytes=VMEM_LIMIT),
        cost_estimate=pl.CostEstimate(
            flops=2 * 27 * BLOCK * BLOCK * 512, bytes_accessed=4 << 20, transcendentals=27 * BLOCK * BLOCK
        ),
    )(qkv, begin)


def attend_back_kernel(
    qkv_ref, g_ref, ot_ref, lse_ref, begin_ref, table, out_ref, keys, values, kt, gt, dq, dk, dv
):
    i = pl.program_id(0)
    here = pl.ds(pl.multiple_of(i * BLOCK, BLOCK), BLOCK)

    @pl.when(i == 0)
    def _():
        dk[...] = jnp.zeros_like(dk)
        dv[...] = jnp.zeros_like(dv)
        keys[...] = qkv_ref[:, 64:128]
        values[...] = qkv_ref[:, 128:192]
        kt[...] = qkv_ref[:, 64:128].T
        for b in range(16):
            gt[:, b * TOK : (b + 1) * TOK] = g_ref[b]

    q = qkv_ref[here, :64]
    g = gt[:, here]
    begin = begin_ref[...]
    lse = lse_ref[...]
    inner = jnp.sum(g.astype(f32) * ot_ref[...], axis=0, keepdims=True)

    def tile(j, dq, masked, n=1):
        start = pl.multiple_of(j * BLOCK, BLOCK)
        at = pl.ds(start, n * BLOCK)
        s = lax.dot_general(keys[at, :], q, NT, preferred_element_type=f32)
        if masked:
            s = tile_mask(s, start, i * BLOCK, begin)
        p = jnp.exp(s - lse)
        dp = jnp.dot(values[at, :], g, preferred_element_type=f32)
        ds = (p * (dp - inner)).astype(bf16)
        dv[at, :] += lax.dot_general(p.astype(bf16), g, NT, preferred_element_type=f32)
        dk[at, :] += jnp.dot(ds, q, preferred_element_type=f32)
        return dq + jnp.dot(kt[:, at], ds, preferred_element_type=f32)

    dqt = tile(i, jnp.zeros((HEAD_DIM, BLOCK), f32), True)
    window, shared = key_ranges(i)
    dqt = lax.fori_loop(window, i, lambda j, c: tile(j, c, True), dqt)
    pairs = shared // 2
    dqt = lax.fori_loop(0, pairs, lambda j, c: tile(2 * j, c, False, 2), dqt)
    dqt = lax.fori_loop(2 * pairs, shared, lambda j, c: tile(j, c, False), dqt)
    dq[here, :] = dqt.T * HEAD_DIM**-0.5

    @pl.when(i == GROUP // BLOCK - 1)
    def _():
        def back(b, _):
            at = pl.ds(pl.multiple_of(b * BLOCK, BLOCK), BLOCK)
            c, s = table[at, :HEAD_DIM], table[at, HEAD_DIM:]
            q, k = dq[at, :].astype(bf16).astype(f32), dk[at, :].astype(bf16).astype(f32)
            parts = [q * c + turn_back(q * s), k * c + turn_back(k * s), dv[at, :], jnp.zeros_like(q)]
            out_ref[at, :] = jnp.concatenate(parts, axis=1).astype(bf16)
            return 0

        lax.fori_loop(0, GROUP // BLOCK, back, 0)


def attend_back(qkv, g, ot, lse, begin, table):
    whole = lambda *shape: pl.BlockSpec(shape, lambda i: (0,) * len(shape))
    cols = lambda n: pl.BlockSpec((n, BLOCK), lambda i: (0, i))
    return pl.pallas_call(
        attend_back_kernel,
        grid=(GROUP // BLOCK,),
        in_specs=[
            whole(GROUP, 256),
            whole(16, HEAD_DIM, TOK),
            cols(HEAD_DIM),
            cols(1),
            cols(1),
            whole(GROUP, 128),
        ],
        out_specs=whole(GROUP, 256),
        out_shape=jax.ShapeDtypeStruct((GROUP, 256), bf16),
        scratch_shapes=[
            pltpu.VMEM((GROUP, HEAD_DIM), bf16),
            pltpu.VMEM((GROUP, HEAD_DIM), bf16),
            pltpu.VMEM((HEAD_DIM, GROUP), bf16),
            pltpu.VMEM((HEAD_DIM, GROUP), bf16),
            pltpu.VMEM((GROUP, HEAD_DIM), f32),
            pltpu.VMEM((GROUP, HEAD_DIM), f32),
            pltpu.VMEM((GROUP, HEAD_DIM), f32),
        ],
        compiler_params=pltpu.CompilerParams(vmem_limit_bytes=VMEM_LIMIT),
        cost_estimate=pl.CostEstimate(
            flops=5 * 27 * BLOCK * BLOCK * 512, bytes_accessed=8 << 20, transcendentals=27 * BLOCK * BLOCK
        ),
    )(qkv, g, ot, lse, begin, table)


def experts_kernel(
    own_ref, ffn_mine, ffn_other, g_mine, g_other, routes_mine, routes_other, router_ref, own_w, across_w, *refs
):
    routed_mine, routed_other, moved_mine, moved_other = refs[-10:-6]
    x_ref, dh_ref, act_ref, dy_ref, w_ref, sem = refs[-6:]
    own = own_ref[0]

    copies = [
        [
            pltpu.make_async_copy(shards.at[y, e], w_ref.at[e, 2 * y + (own_ref[1] ^ a)], sem.at[a, y, e])
            for a, shards in enumerate((own_w, across_w))
            for y in range(4)
        ]
        for e in range(2)
    ]

    @pl.when(pl.program_id(0) == 0)
    def _():
        for copy in copies[0] + copies[1]:
            copy.start()

    expert_rows = lax.broadcasted_iota(i32, (EXPERTS, TOK), 0)
    slot_rows = lax.broadcasted_iota(i32, (SLOTS, TOK), 0).astype(f32)
    upto = (
        lax.broadcasted_iota(i32, (TOK, TOK), 0) <= lax.broadcasted_iota(i32, (TOK, TOK), 1)
    ).astype(f32).astype(bf16)
    slot_cols = []
    gate_grads = [jnp.zeros((EXPERTS, WIDTH), f32) for _ in range(4)]
    payload_rows = lax.broadcasted_iota(i32, (EXPERTS, WIDTH), 0)
    gate_rows = [[], []]
    picks = [[], []]
    picked_rows = [[], []]
    picked_grads = [[], []]
    blocks = [(ffn_mine, g_mine, routes_mine, 0), (ffn_other, g_other, routes_other, 0)]
    blocks = blocks + [(*refs_of[:3], 1) for refs_of in blocks]
    for rows_ref, grads_ref, routes_ref, n in blocks:
        rows, grads = rows_ref[n], grads_ref[n]
        routes = routes_ref[n][:8, :TOK].astype(f32).astype(i32)
        chosen = expert_rows == routes[0:1]
        for j in range(1, 8):
            chosen = chosen | (expert_rows == routes[j : j + 1])
        named = [jnp.max((routes == own + e).astype(f32), axis=0, keepdims=True) for e in range(2)]
        named = jnp.concatenate(named + [jnp.zeros((6, TOK), f32)], axis=0)
        rank = jnp.dot(named.astype(bf16), upto, preferred_element_type=f32)
        slots = jnp.where(named > 0, rank - 1.0, -1.0)
        slot_cols.append(slots.T)
        logits = lax.dot_general(router_ref[...], rows, NT, preferred_element_type=f32)
        peak = jnp.max(jnp.where(chosen, logits, masked_score), axis=0, keepdims=True)
        raised = jnp.where(chosen, jnp.exp(jnp.minimum(logits - peak, 0.0)), 0.0)
        gates = raised / jnp.sum(raised, axis=0, keepdims=True)
        for e in range(2):
            gate_rows[e].append(
                jnp.sum(jnp.where(expert_rows == own + e, gates, 0.0), axis=0, keepdims=True)
            )
            picks[e].append((slots[e : e + 1] == slot_rows).astype(f32))
        low = jnp.concatenate([picks[0][-1], picks[1][-1]], axis=0).astype(bf16)
        for source, kept in ((rows, picked_rows), (grads, picked_grads)):
            both = jnp.dot(low, source, preferred_element_type=f32)
            kept[0].append(both[:SLOTS])
            kept[1].append(both[SLOTS:])
    moved, routed = [], []
    for e in range(2):

        @pl.when(pl.program_id(0) == 0)
        def _():
            for copy in copies[e]:
                copy.wait()

        w_gate_up = w_ref[e, :, :128, :].reshape(WIDTH, 2 * FF)
        w_down = w_ref[e, :, 128:, :].reshape(FF, WIDTH)
        x = jnp.concatenate(picked_rows[e], axis=0).astype(bf16)
        gate = jnp.concatenate(
            [jnp.sum(p * r, axis=1, keepdims=True) for p, r in zip(picks[e], gate_rows[e])], axis=0
        )
        grads = jnp.concatenate(picked_grads[e], axis=0)
        dy = (gate * grads).astype(bf16)
        mixed = jnp.dot(x, w_gate_up, preferred_element_type=f32)
        dact = lax.dot_general(dy, w_down, NT, preferred_element_type=f32)
        gate_part, up_part = mixed[:, :FF], mixed[:, FF:]
        sigma = 1.0 / (1.0 + jnp.exp(-gate_part))
        silu = gate_part * sigma
        act = (silu * up_part).astype(bf16)
        dh = jnp.concatenate(
            [dact * up_part * (sigma + silu * (1.0 - sigma)), dact * silu], axis=1
        ).astype(bf16)
        x_ref[e] = x
        dy_ref[e] = dy
        act_ref[e] = act
        dh_ref[e] = dh
        returned = jnp.dot(act, w_down, preferred_element_type=f32).astype(bf16).astype(f32)
        dgate = jnp.sum(returned * grads, axis=1, keepdims=True)
        for b in range(4):
            grad = jnp.sum(
                picks[e][b] * dgate[b * SLOTS : (b + 1) * SLOTS], axis=0, keepdims=True
            )
            high = grad.astype(bf16).astype(f32)
            gap = jnp.zeros((1, 256 - TOK), f32)
            wide = jnp.concatenate([high, gap, grad - high, gap, jnp.zeros((1, WIDTH - 512), f32)], axis=1)
            gate_grads[b] = gate_grads[b] + jnp.where(payload_rows == own + e, wide, 0.0)
        moved.append(gate * returned)
        routed.append(lax.dot_general(dh, w_gate_up, NT, preferred_element_type=f32))
    columns = lax.broadcasted_iota(i32, (TOK, 2 * SLOTS), 1).astype(f32)
    outs = [(routed_mine, moved_mine, 0), (routed_other, moved_other, 0), (routed_mine, moved_mine, 1), (routed_other, moved_other, 1)]
    for b, (routed_ref, moved_ref, n) in enumerate(outs):
        first, second = slot_cols[b][:, 0:1], slot_cols[b][:, 1:2]
        back = ((columns == first) | ((columns == second + SLOTS) & (second >= 0))).astype(f32).astype(bf16)
        at = slice(b * SLOTS, (b + 1) * SLOTS)
        for terms, ref in ((routed, routed_ref), (moved, moved_ref)):
            joined = jnp.concatenate([terms[0][at], terms[1][at]], axis=0).astype(bf16)
            ref[n, :TOK, :] = jnp.dot(back, joined, preferred_element_type=f32).astype(bf16)
        routed_ref[n, TOK:, :] = gate_grads[b].astype(bf16)


def run_experts(half, own, ffn, grads, weights, router, before):
    pair = pl.BlockSpec((2, TOK, WIDTH), lambda i, o: (i, 0, 0))
    pair_of_all = pl.BlockSpec((2, TOK, WIDTH), lambda i, o: (i + 2 * half, 0, 0))
    whole = lambda shape: pl.BlockSpec(shape, lambda i, o: (0,) * len(shape))
    routes = pl.BlockSpec((2, 16, 256), lambda i, o: (i, TOK // 16, 0))
    summed = pl.BlockSpec((2, PAY, WIDTH), lambda i, o: (i, 0, 0))
    kept = lambda n: pl.BlockSpec((2, STEP_ROWS, n), lambda i, o: (0, i + 2 * half, 0))
    part = jax.ShapeDtypeStruct((4, PAY, WIDTH), bf16)
    keep = lambda n: jax.ShapeDtypeStruct((2, ALL_ROWS, n), bf16)
    return pl.pallas_call(
        experts_kernel,
        grid_spec=pltpu.PrefetchScalarGridSpec(
            num_scalar_prefetch=1,
            grid=(2,),
            in_specs=[
                pair,
                pair,
                pair,
                pair,
                routes,
                routes,
                whole((EXPERTS, WIDTH)),
            ]
            + [pl.BlockSpec(memory_space=pl.ANY)] * (2 + len(before)),
            out_specs=[
                summed,
                summed,
                pair_of_all,
                pair_of_all,
                kept(WIDTH),
                kept(2 * FF),
                kept(FF),
                kept(WIDTH),
            ],
            scratch_shapes=[
                pltpu.VMEM((2, 8, 192, 1024), bf16),
                pltpu.SemaphoreType.DMA((2, 4, 2)),
            ],
        ),
        out_shape=[
            part,
            part,
            jax.ShapeDtypeStruct((8, TOK, WIDTH), bf16),
            jax.ShapeDtypeStruct((8, TOK, WIDTH), bf16),
            keep(WIDTH),
            keep(2 * FF),
            keep(FF),
            keep(WIDTH),
        ],
        input_output_aliases={10 + i: 2 + i for i in range(len(before))},
        compiler_params=pltpu.CompilerParams(vmem_limit_bytes=VMEM_LIMIT),
        cost_estimate=pl.CostEstimate(
            flops=14 << 30, bytes_accessed=24 << 20, transcendentals=8 * SLOTS * 2 * FF
        ),
    )(own, *ffn, *grads, *grads, router, *weights, *before)


def expert_grads_kernel(x_ref, dh_ref, act_ref, dy_ref, out_ref):
    up = lax.dot_general(x_ref[0], dh_ref[0], TN, preferred_element_type=f32)
    down = lax.dot_general(act_ref[0], dy_ref[0], TN, preferred_element_type=f32)
    out_ref[0, :, 0, :128, :] = up.astype(bf16).reshape(2, 128, 2 * FF)
    out_ref[0, :, 0, 128:, :] = down.astype(bf16).reshape(2, 64, WIDTH)


def expert_weight_grads(x, dh, act, dy):
    return pl.pallas_call(
        expert_grads_kernel,
        grid=(2, 4),
        in_specs=[
            pl.BlockSpec((1, ALL_ROWS, 256), lambda e, i: (e, 0, i)),
            pl.BlockSpec((1, ALL_ROWS, 2 * FF), lambda e, i: (e, 0, 0)),
            pl.BlockSpec((1, ALL_ROWS, 128), lambda e, i: (e, 0, i)),
            pl.BlockSpec((1, ALL_ROWS, WIDTH), lambda e, i: (e, 0, 0)),
        ],
        out_specs=pl.BlockSpec((1, 2, 1, 192, 1024), lambda e, i: (i, 0, e, 0, 0)),
        out_shape=jax.ShapeDtypeStruct((4, 2, 2, 192, 1024), bf16),
        compiler_params=pltpu.CompilerParams(vmem_limit_bytes=VMEM_LIMIT),
        cost_estimate=pl.CostEstimate(flops=8 << 30, bytes_accessed=14 << 20, transcendentals=0),
    )(x, dh, act, dy)


def hidden_kernel(att_ref, w_ref, rows_ref, gain_ref, hidden_ref, normed_ref):
    att = att_ref[...].reshape(WIDTH, TOK)
    hidden = rows_ref[...].astype(f32) + lax.dot_general(
        att, w_ref[:, :WIDTH], TN, preferred_element_type=f32
    )
    hidden_ref[...] = hidden
    normed_ref[...] = (hidden * inverse_rms(hidden) * gain_ref[...]).astype(bf16)


def hidden_of(attended, shared, rows, gain):
    return pl.pallas_call(
        hidden_kernel,
        out_shape=[
            jax.ShapeDtypeStruct((TOK, WIDTH), f32),
            jax.ShapeDtypeStruct((TOK, WIDTH), bf16),
        ],
        compiler_params=pltpu.CompilerParams(vmem_limit_bytes=VMEM_LIMIT),
        cost_estimate=pl.CostEstimate(
            flops=2 * TOK * WIDTH * WIDTH, bytes_accessed=5 << 20, transcendentals=0
        ),
    )(attended, shared, rows, gain)


def hidden_back_kernel(
    t0, t1, t2, t3, crossed, hidden_ref, normed_ref, chosen_ref, router_ref, g_ref, gain_ref,
    w_ref, hidden_grad_ref, branch_ref, logit_ref, scaled_ref, att_ref
):
    chosen = chosen_ref[...] > 0
    logits = lax.dot_general(router_ref[...], normed_ref[...], NT, preferred_element_type=f32)
    peak = jnp.max(jnp.where(chosen, logits, masked_score), axis=0, keepdims=True)
    raised = jnp.where(chosen, jnp.exp(jnp.minimum(logits - peak, 0.0)), 0.0)
    gates = raised / jnp.sum(raised, axis=0, keepdims=True)
    summed = t0[...].astype(f32)
    for term in (t1, t2, t3, crossed):
        summed = summed + term[...].astype(f32)
    gate_grad = summed[TOK:, :TOK] + summed[TOK:, 256 : 256 + TOK]
    logit_grad = gates * (gate_grad - jnp.sum(gates * gate_grad, axis=0, keepdims=True))
    logit_grad = logit_grad.astype(bf16)
    logit_ref[...] = logit_grad
    normed_grad = summed[:TOK] + lax.dot_general(
        logit_grad, router_ref[...], TN, preferred_element_type=f32
    )
    hidden = hidden_ref[...]
    scale = inverse_rms(hidden)
    scaled_ref[...] = (normed_grad * hidden * scale).astype(bf16)
    hidden_grad = g_ref[...].astype(f32) + rms_pull(hidden, scale, gain_ref[...], normed_grad)
    hidden_grad_ref[...] = hidden_grad
    branch = hidden_grad.astype(bf16)
    branch_ref[...] = branch
    att = lax.dot_general(w_ref[:, :WIDTH], branch, NT, preferred_element_type=f32)
    att_ref[...] = att.astype(bf16).reshape(HEADS, HEAD_DIM, TOK)


def hidden_back(terms, crossed, hidden, normed, chosen, router_t, g, gain, shared):
    wide = lambda t: jax.ShapeDtypeStruct((TOK, WIDTH), t)
    return pl.pallas_call(
        hidden_back_kernel,
        out_shape=[
            wide(f32),
            wide(bf16),
            jax.ShapeDtypeStruct((EXPERTS, TOK), bf16),
            wide(bf16),
            jax.ShapeDtypeStruct((HEADS, HEAD_DIM, TOK), bf16),
        ],
        compiler_params=pltpu.CompilerParams(vmem_limit_bytes=VMEM_LIMIT),
        cost_estimate=pl.CostEstimate(
            flops=2 * TOK * WIDTH * WIDTH, bytes_accessed=8 << 20, transcendentals=0
        ),
    )(*terms, crossed, hidden, normed, chosen, router_t, g, gain, shared)


def shared_grads_kernel(att_ref, branch_ref, normed_ref, logit_ref, scaled_ref, out_ref):
    over_tokens = (((0,), (1,)), ((), ()))
    logit = jnp.concatenate([logit_ref[...], jnp.zeros((96, TOK), bf16)], axis=0)
    ones = (lax.broadcasted_iota(i32, (128, TOK), 0) == EXPERTS).astype(f32).astype(bf16)
    att = att_ref[...].reshape(WIDTH, TOK)
    grads = [
        jnp.dot(att, branch_ref[...], preferred_element_type=f32),
        lax.dot_general(normed_ref[...], logit, over_tokens, preferred_element_type=f32)
        + lax.dot_general(scaled_ref[...], ones, over_tokens, preferred_element_type=f32),
    ]
    for w in range(8):
        for part, at in zip(grads, (slice(0, WIDTH), slice(WIDTH, None))):
            rows = [part[s * 64 + w * 8 : s * 64 + w * 8 + 8] for s in range(16)]
            out_ref[w, :, at] = jnp.concatenate(rows, axis=0).astype(bf16)


def shared_weight_grads(att, branch, normed, logit_grad, scaled):
    return pl.pallas_call(
        shared_grads_kernel,
        out_shape=jax.ShapeDtypeStruct((8, 128, 1152), bf16),
        compiler_params=pltpu.CompilerParams(vmem_limit_bytes=VMEM_LIMIT),
        cost_estimate=pl.CostEstimate(
            flops=2 * TOK * WIDTH * 1280, bytes_accessed=5 << 20, transcendentals=0
        ),
    )(att, branch, normed, logit_grad, scaled)


def local(
    tokens,
    routes,
    cont_lengths,
    norm_attn,
    w_qkv,
    w_out,
    w_router,
    norm_ffn,
    w_gate_up,
    w_down,
    cotangent,
):
    seq_index = lax.axis_index("seq")
    places, blocks = relative_places(seq_index)
    rows = tokens[0]
    query_width = HEADS * HEAD_DIM
    kv_width = KV_HEADS * HEAD_DIM

    position, begin = group_layout(cont_lengths[0])
    begin = begin[None]
    table = rotary_table(position.astype(f32))
    kv_heads = lambda start: jnp.repeat(
        w_qkv[:, start : start + kv_width].reshape(8, KV_HEADS, HEAD_DIM), 2, axis=1
    )
    head_cols = jnp.concatenate(
        [
            w_qkv[:, :query_width].reshape(8, HEADS, HEAD_DIM),
            kv_heads(query_width),
            kv_heads(query_width + kv_width),
            jnp.broadcast_to(norm_attn[:, None, None], (8, HEADS, HEAD_DIM)),
        ],
        axis=2,
    ).transpose(1, 0, 2)
    head_cols = jnp.broadcast_to(head_cols[:, None], (HEADS, 8, 8, 256)).reshape(128, 8, 256)
    head_weights = lax.all_to_all(head_cols, BOTH, 0, 0, tiled=True).reshape(WIDTH, 256)
    gain_attn = head_weights[:, 192].astype(f32)[None]
    head_weights = jnp.where(jnp.arange(256)[None] < 192, head_weights, 0.0).astype(bf16)

    rows_near, rows_across = gather_near(rows)
    rows_near, _, table, head_weights = tie(rows_near, rows_across, table, head_weights)
    rows_near, rows_far = both_cores(rows_near), gather_far(rows_across)

    own_x = lax.axis_index("wshard") % 2
    expert_rows = jnp.concatenate([w_gate_up, w_down], axis=1)
    along_y = lambda t: lax.all_gather(t, "wshard", axis_index_groups=ALONG_Y, axis=0)
    experts, expert_rows = along_y(expert_rows), swap_x(expert_rows)

    qkv = project(places[:8], rows_near, head_weights, gain_attn, table, ())
    shared = jnp.concatenate(
        [w_out, w_router, norm_ffn[:, None], jnp.zeros((8, 95), bf16)], axis=1
    )
    shared, qkv = tie(shared, qkv)
    shared = lax.all_to_all(
        jnp.broadcast_to(shared[None], (128, 8, 1152)), BOTH, 0, 0, tiled=True
    ).reshape(WIDTH, 1152)
    routes_rows = jnp.pad(routes[0].T.astype(bf16), ((0, 8), (0, WIDTH - TOK)))
    upstream_rows = jnp.concatenate([cotangent[0], routes_rows], axis=0)
    rows_far, qkv, upstream_rows, expert_rows = tie(rows_far, qkv, upstream_rows, expert_rows)
    experts = [experts, along_y(expert_rows)]
    rows_far = both_cores(rows_far)
    grad_near = [upstream_rows] + [send(upstream_rows, 0, b) for b in (1, 3, 2)]
    qkv = project(places[8:], rows_far, head_weights, gain_attn, table, (qkv,))

    router_t = shared[:, WIDTH : WIDTH + EXPERTS].T
    gain_ffn = shared[:, WIDTH + EXPERTS].astype(f32)[None]
    attended_head, attended_t, lse = attend(qkv, begin)
    attended_head, shared = tie(attended_head, shared)
    attended = lax.all_to_all(attended_head, "seq", 0, 0, tiled=True)
    attended, grad_near = tie(attended, grad_near)
    grad_near = jnp.stack(grad_near)
    hidden, normed_ffn = hidden_of(attended, shared, rows, gain_ffn)
    ffn_near, ffn_across = gather_near(normed_ffn)
    ffn_near, _ = tie(ffn_near, ffn_across)
    grad_near_mine, _ = tie(grad_near, ffn_across)
    grad_far = send(grad_near_mine, 1, 0)
    grad_near = (grad_near, swap_cores(grad_near))
    ffn_near, ffn_far = both_cores(ffn_near), gather_far(ffn_across)
    own = jnp.stack([seq_index * 2, own_x])
    near = run_experts(0, own, ffn_near, grad_near, experts, router_t, ())
    near_terms = sum_along_z(*near[:2])
    ffn_far = both_cores(ffn_far)
    grad_far = (grad_far, swap_cores(grad_far))
    far = run_experts(1, own, ffn_far, grad_far, experts, router_t, near[2:])
    far, near_terms = tie(far, near_terms)
    moved, saved = far[2:4], far[4:]
    far_other, moved_other = tie(swap_cores(far[1]), moved[1])
    far_terms = send_along_z(chip_parts(far[0], far_other))
    expert_grads = expert_weight_grads(*saved)
    moved_other = swap_cores(moved_other)
    far_terms, expert_grads, moved_other = tie(far_terms, expert_grads, moved_other)
    crossed = send(add_low(*far_terms), 1, 0)
    by_x = [t.reshape(2, 4, TOK, WIDTH) for t in (moved[0], moved_other)]
    moved_parts = [add_low(by_x[0][:, i], by_x[1][:, i]) for i in range(4)]
    crossed, moved_parts = tie(crossed, moved_parts)

    expert_range = jnp.arange(EXPERTS, dtype=i32)
    chosen_here = jnp.any(routes[0].T[None] == expert_range[:, None, None], axis=1).astype(f32)
    hidden_grad, branch_grad, logit_grad, scaled_grad, attended_grad = hidden_back(
        near_terms, crossed, hidden, normed_ffn, chosen_here, router_t, cotangent[0], gain_ffn, shared
    )
    expert_grads = lax.psum_scatter(
        expert_grads.reshape(8, 2, 192, 1024),
        "wshard",
        axis_index_groups=ALONG_Y,
        scatter_dimension=0,
        tiled=True,
    )
    head_grad = lax.all_to_all(attended_grad, "seq", 0, 0, tiled=True)
    shared_grads = shared_weight_grads(attended, branch_grad, normed_ffn, logit_grad, scaled_grad)
    head_grad, shared_grads, moved_parts = tie(head_grad, shared_grads, moved_parts)
    moved_terms = [moved_parts[0]] + [
        send(moved_parts[i], 0, -b) for i, b in ((1, 1), (2, 3), (3, 2))
    ]

    shared_grads = lax.all_to_all(shared_grads, "wshard", 0, 0, tiled=True)
    projected_grad = attend_back(qkv, head_grad, attended_t, lse, begin, table)
    far_part = project_back(places[8:], projected_grad, head_weights)
    far_part, shared_grads, moved_terms = tie(far_part, shared_grads, moved_terms)
    near_part = project_back(places[:8], projected_grad, head_weights)
    shared_grads = jnp.sum(shared_grads.astype(f32), axis=0).astype(bf16).reshape(16, 8, 1152)
    upper, lower = slice(0, TOK // 2), slice(TOK // 2, TOK)
    far_got, near_got = swap_cores(far_part[1]), swap_cores(near_part[1])
    far_upper = add_low(far_part[0][:, upper], far_got[:, upper])
    lower_parts = [
        jnp.stack(
            [
                add_low(near_part[0][i, lower], near_got[i, lower]),
                add_low(far_part[0][i, lower], far_got[i, lower]),
            ]
        )
        for i in range(4)
    ]
    far_upper, lower_parts, projected_grad, shared_grads = tie(
        far_upper, lower_parts, projected_grad, shared_grads
    )
    far_upper = send(far_upper, 1, 0)
    lower_terms = [lower_parts[0]] + [
        send(lower_parts[i], 0, -b) for i, b in ((1, 1), (2, 3), (3, 2))
    ]
    shared_grads = lax.all_to_all(shared_grads, "seq", 0, 0, tiled=True)
    grad_head = head_weight_grad(places, rows_near, rows_far, gain_attn, projected_grad)
    far_upper, lower_terms, moved_terms, expert_grads = tie(
        far_upper, lower_terms, moved_terms, expert_grads
    )
    grad_heads = lax.all_to_all(grad_head.reshape(128, 8, 256), BOTH, 0, 0, tiled=True)
    crossed = send(add_low(*[t[1] for t in lower_terms]), 1, 0)
    upper_parts = [
        add_low(near_part[0][i, upper], near_got[i, upper], far_upper[i]) for i in range(4)
    ]
    upper_terms = [upper_parts[0]] + [
        send(upper_parts[i], 0, -b) for i, b in ((1, 1), (2, 3), (3, 2))
    ]
    moved_crossed = send(add_low(*[t[1] for t in moved_terms]), 1, 0)
    crossed, grad_heads = tie(crossed, grad_heads)
    kept = lax.dynamic_index_in_dim(expert_grads, own_x, 0, keepdims=False)
    sent = lax.dynamic_index_in_dim(expert_grads, 1 - own_x, 0, keepdims=False)
    expert_grads = kept.astype(f32) + swap_x(sent).astype(f32)
    total = lambda terms: sum([t.astype(f32) for t in terms])
    output = (hidden + total([t[0] for t in moved_terms] + [moved_crossed])).astype(bf16)
    normed_grad = jnp.concatenate(
        [total(upper_terms), total([t[0] for t in lower_terms] + [crossed])], axis=0
    )
    shared_grads = jnp.sum(shared_grads.astype(f32), axis=0)
    grad_heads = jnp.sum(grad_heads.reshape(16, 8, 8, 256).astype(f32), axis=1).transpose(1, 0, 2)
    kv_sum = lambda start: jnp.sum(
        grad_heads[:, :, start : start + HEAD_DIM].reshape(8, KV_HEADS, 2, HEAD_DIM), axis=2
    ).reshape(8, kv_width)
    grad_qkv = jnp.concatenate(
        [grad_heads[:, :, :HEAD_DIM].reshape(8, query_width), kv_sum(HEAD_DIM), kv_sum(2 * HEAD_DIM)],
        axis=1,
    )
    grad_norm_attn = jnp.sum(grad_qkv * w_qkv.astype(f32), axis=1) / norm_attn.astype(f32)
    inputs = rows.astype(f32)
    grad_input = hidden_grad + rms_pull(inputs, inverse_rms(inputs), gain_attn, normed_grad)
    return (
        output[None],
        grad_input[None],
        grad_norm_attn,
        grad_qkv,
        shared_grads[:, :WIDTH],
        shared_grads[:, WIDTH : WIDTH + EXPERTS],
        shared_grads[:, WIDTH + EXPERTS],
        expert_grads[:, :128],
        expert_grads[:, 128:],
    )


def solution(mesh):
    return jax.shard_map(
        local,
        mesh=mesh,
        in_specs=(
            P("wshard", "seq", None),
            P("wshard", "seq", None),
            P("wshard", None),
            P(BOTH),
            P(BOTH, None),
            P(BOTH, None),
            P(BOTH, None),
            P(BOTH),
            P("seq", "wshard", None),
            P("seq", "wshard", None),
            P("wshard", "seq", None),
        ),
        out_specs=(
            P("wshard", "seq", None),
            P("wshard", "seq", None),
            P(BOTH),
            P(BOTH, None),
            P(BOTH, None),
            P(BOTH, None),
            P(BOTH),
            P("seq", "wshard", None),
            P("seq", "wshard", None),
        ),
        check_vma=False,
    )
```

```python
import jax
import jax.numpy as jnp
from jax import lax
from jax.experimental import pallas as pl
from jax.experimental.pallas import tpu as pltpu
from jax.sharding import PartitionSpec as P

HEADS = 16
KV_HEADS = 8
HEAD_DIM = 64
EXPERTS = 32
FF = 512
PROMPT = 2048
GROUP = 3584
TOK = 224
WIDTH = 1024
SLOTS = 72
STEP_ROWS = 4 * SLOTS
ALL_ROWS = 16 * SLOTS
BLOCK = 512
VMEM_LIMIT = 60 << 20
PAY = TOK + 32

norm_eps = 1e-06
rope_base = 10000.0
masked_score = -1e30
BOTH = ("seq", "wshard")
NT = (((1,), (1,)), ((), ()))
TN = (((0,), (0,)), ((), ()))
f32 = jnp.float32
bf16 = jnp.bfloat16
i32 = jnp.int32


def place_of(x, z, core):
    return x * 8 + z * 2 + core


def shift_perm(a, b):
    return [
        (place_of(x, z, c), place_of(x ^ a, (z + b) % 4, c))
        for x in range(2)
        for z in range(4)
        for c in range(2)
    ]


CORE_PERM = [(i, i ^ 1) for i in range(16)]


def send(rows, a, b):
    return lax.ppermute(rows, "seq", shift_perm(a, b))


def swap_cores(rows):
    return lax.ppermute(rows, "seq", CORE_PERM)


def relative_places(seq_index):
    x, z, c = seq_index // 8, (seq_index // 2) % 4, seq_index % 2
    r = jnp.arange(16, dtype=i32)
    a, i, k = r // 8, (r // 2) % 4, r % 2
    shift = i ^ (i // 2)
    behind = (z - i) % 4
    places = (a ^ x) * 8 + ((z - shift) % 4) * 2 + (k ^ c)
    return places, (a ^ x) * 8 + (behind ^ (behind // 2)) * 2 + (k ^ c)


def gather_near(rows):
    return [rows] + [send(rows, 0, b) for b in (1, 3, 2)], send(rows, 1, 0)


def both_cores(parts):
    mine = jnp.stack(parts)
    return mine, swap_cores(mine)


def gather_far(across):
    return [across] + [send(across, 0, b) for b in (1, 3, 2)]


def add_low(*terms):
    return sum([t.astype(f32) for t in terms]).astype(bf16)


def sum_along_z(mine, other):
    return send_along_z(chip_parts(mine, swap_cores(other)))


def chip_parts(mine, got):
    return [add_low(mine[i], got[i]) for i in range(4)]


def send_along_z(parts):
    return [parts[0]] + [send(parts[i], 0, -b) for i, b in ((1, 1), (2, 3), (3, 2))]


def swap_x(rows):
    return lax.ppermute(rows, "wshard", [(w, w ^ 1) for w in range(8)])


ALONG_Y = [[y * 2 + x for y in range(4)] for x in range(2)]


def tie(*values):
    return lax.optimization_barrier(values)


def inverse_rms(values):
    return lax.rsqrt(jnp.mean(values * values, axis=-1, keepdims=True) + norm_eps)


def rms_pull(values, scale, gain, grad):
    scaled = grad * gain
    return scale * scaled - values * (scale * scale * scale) * jnp.mean(
        scaled * values, axis=-1, keepdims=True
    )


def group_layout(lengths):
    places = jnp.arange(GROUP, dtype=i32)
    ends = jnp.cumsum(lengths)
    starts = ends - lengths
    offset_in = places - PROMPT
    segment_id = jnp.sum((offset_in[:, None] >= ends[None, :]).astype(i32), axis=1)
    segment_hot = segment_id[:, None] == jnp.arange(lengths.shape[0], dtype=i32)[None, :]
    begin = jnp.sum(jnp.where(segment_hot, starts[None, :], 0), axis=1)
    inside = offset_in >= 0
    position = jnp.where(inside, PROMPT + offset_in - begin, places)
    return position, jnp.where(inside, PROMPT + begin, 0)


def rotary_table(position):
    half_dim = HEAD_DIM // 2
    inverse = rope_base ** (-((jnp.arange(2 * HEAD_DIM) % half_dim).astype(f32) * 2.0) / HEAD_DIM)
    back = jnp.where(jnp.arange(2 * HEAD_DIM) < HEAD_DIM, 0.0, 0.5 * jnp.pi).astype(f32)
    return jnp.cos(position[:, None] * inverse[None, :] - back[None, :])


def turn(values):
    half_dim = HEAD_DIM // 2
    return jnp.concatenate([-values[:, half_dim:], values[:, :half_dim]], axis=-1)


def turn_back(values):
    half_dim = HEAD_DIM // 2
    return jnp.concatenate([values[:, half_dim:], -values[:, :half_dim]], axis=-1)


def project_kernel(places, mine, other, w, gain, table, *refs):
    out = refs[-1]
    j = pl.program_id(0)

    if len(refs) > 1:

        @pl.when(j == 0)
        def _():
            out[...] = refs[0][...]

    for k, ref in enumerate((mine, other)):
        at = pl.ds(pl.multiple_of(places[2 * j + k] * TOK, TOK), TOK)
        rows = ref[0].astype(f32)
        normed = (rows * inverse_rms(rows) * gain[...]).astype(bf16)
        projected = jnp.dot(normed, w[...], preferred_element_type=f32)
        c, s = table[at, :HEAD_DIM], table[at, HEAD_DIM:]
        q, k, v = projected[:, :64], projected[:, 64:128], projected[:, 128:]
        q = (q * c + turn(q) * s).astype(bf16).astype(f32) * HEAD_DIM**-0.5
        out[at, :] = jnp.concatenate([q, k * c + turn(k) * s, v], axis=1).astype(bf16)


def project(places, gathered, w, gain, table, before):
    chip = pl.BlockSpec((1, TOK, WIDTH), lambda j, p: (j, 0, 0))
    whole = lambda *shape: pl.BlockSpec(shape, lambda j, p: (0,) * len(shape))
    return pl.pallas_call(
        project_kernel,
        grid_spec=pltpu.PrefetchScalarGridSpec(
            num_scalar_prefetch=1,
            grid=(4,),
            in_specs=[chip, chip, whole(WIDTH, 256), whole(1, WIDTH), whole(GROUP, 128)]
            + [whole(GROUP, 256)] * len(before),
            out_specs=whole(GROUP, 256),
        ),
        out_shape=jax.ShapeDtypeStruct((GROUP, 256), bf16),
        compiler_params=pltpu.CompilerParams(vmem_limit_bytes=VMEM_LIMIT),
        cost_estimate=pl.CostEstimate(
            flops=2 * 8 * TOK * WIDTH * 256, bytes_accessed=10 << 20, transcendentals=0
        ),
    )(places, *gathered, w, gain, table, *before)


def project_back_kernel(places, first, second, w, mine, other):
    del places
    mine[0] = lax.dot_general(first[...], w[...], NT, preferred_element_type=f32).astype(bf16)
    other[0] = lax.dot_general(second[...], w[...], NT, preferred_element_type=f32).astype(bf16)


def project_back(places, projected_grad, w):
    chip = pl.BlockSpec((1, TOK, WIDTH), lambda j, p: (j, 0, 0))
    at = lambda k: pl.BlockSpec((TOK, 256), lambda j, p: (p[2 * j + k], 0))
    part = jax.ShapeDtypeStruct((4, TOK, WIDTH), bf16)
    return pl.pallas_call(
        project_back_kernel,
        grid_spec=pltpu.PrefetchScalarGridSpec(
            num_scalar_prefetch=1,
            grid=(4,),
            in_specs=[at(0), at(1), pl.BlockSpec((WIDTH, 256), lambda j, p: (0, 0))],
            out_specs=[chip, chip],
        ),
        out_shape=[part, part],
        compiler_params=pltpu.CompilerParams(vmem_limit_bytes=VMEM_LIMIT),
        cost_estimate=pl.CostEstimate(
            flops=2 * 8 * TOK * WIDTH * 256, bytes_accessed=5 << 20, transcendentals=0
        ),
    )(places, projected_grad, projected_grad, w)


def head_grad_kernel(places, near_mine, near_other, far_mine, far_other, gain, first, second, out, total):
    del places
    j = pl.program_id(0)

    @pl.when(j == 0)
    def _():
        total[...] = jnp.zeros_like(total)

    for near, far, projected in ((near_mine, far_mine, first), (near_other, far_other, second)):
        rows = jnp.where(j < 4, near[0], far[0]).astype(f32)
        normed = (rows * inverse_rms(rows) * gain[...]).astype(bf16)
        total[...] += lax.dot_general(normed, projected[...], TN, preferred_element_type=f32)

    @pl.when(j == 7)
    def _():
        out[...] = total[...].astype(bf16)


def head_weight_grad(places, near, far, gain, projected_grad):
    near_chip = pl.BlockSpec((1, TOK, WIDTH), lambda j, p: (jnp.minimum(j, 3), 0, 0))
    far_chip = pl.BlockSpec((1, TOK, WIDTH), lambda j, p: (jnp.maximum(j - 4, 0), 0, 0))
    at = lambda k: pl.BlockSpec((TOK, 256), lambda j, p: (p[2 * j + k], 0))
    return pl.pallas_call(
        head_grad_kernel,
        grid_spec=pltpu.PrefetchScalarGridSpec(
            num_scalar_prefetch=1,
            grid=(8,),
            in_specs=[
                near_chip,
                near_chip,
                far_chip,
                far_chip,
                pl.BlockSpec((1, WIDTH), lambda j, p: (0, 0)),
                at(0),
                at(1),
            ],
            out_specs=pl.BlockSpec((WIDTH, 256), lambda j, p: (0, 0)),
            scratch_shapes=[pltpu.VMEM((WIDTH, 256), f32)],
        ),
        out_shape=jax.ShapeDtypeStruct((WIDTH, 256), bf16),
        compiler_params=pltpu.CompilerParams(vmem_limit_bytes=VMEM_LIMIT),
        cost_estimate=pl.CostEstimate(
            flops=2 * 16 * TOK * WIDTH * 256, bytes_accessed=10 << 20, transcendentals=0
        ),
    )(places, *near, *far, gain, projected_grad, projected_grad)


def tile_mask(scores, key_start, query_start, begin):
    keys = key_start + lax.broadcasted_iota(i32, scores.shape, 0)
    queries = query_start + lax.broadcasted_iota(i32, scores.shape, 1)
    return jnp.where((keys <= queries) & (keys >= begin), scores, masked_score)


def key_ranges(i):
    first = PROMPT // BLOCK
    return jnp.where(i > first, i - 1, i), jnp.minimum(i, first)


def attend_kernel(qkv_ref, begin_ref, o_ref, ot_ref, lse_ref, keys, vt):
    i = pl.program_id(0)
    here = pl.ds(pl.multiple_of(i * BLOCK, BLOCK), BLOCK)

    @pl.when(i == 0)
    def _():
        keys[...] = qkv_ref[:, 64:128]
        vt[...] = qkv_ref[:, 128:192].T

    q = qkv_ref[here, :64]
    begin = begin_ref[...]

    def tile(j, carry, masked, n=1):
        peak, total, out = carry
        start = pl.multiple_of(j * BLOCK, BLOCK)
        at = pl.ds(start, n * BLOCK)
        s = lax.dot_general(keys[at, :], q, NT, preferred_element_type=f32)
        if masked:
            s = tile_mask(s, start, i * BLOCK, begin)
        higher = jnp.maximum(peak, jnp.max(s, axis=0, keepdims=True))
        p = jnp.exp(s - higher)
        fade = jnp.exp(peak - higher)
        total = total * fade + jnp.sum(p, axis=0, keepdims=True)
        out = out * fade + jnp.dot(vt[:, at], p.astype(bf16), preferred_element_type=f32)
        return higher, total, out

    carry = (
        jnp.full((1, BLOCK), masked_score, f32),
        jnp.zeros((1, BLOCK), f32),
        jnp.zeros((HEAD_DIM, BLOCK), f32),
    )
    carry = tile(i, carry, True)
    window, shared = key_ranges(i)
    carry = lax.fori_loop(window, i, lambda j, c: tile(j, c, True), carry)
    pairs = shared // 2
    carry = lax.fori_loop(0, pairs, lambda j, c: tile(2 * j, c, False, 2), carry)
    peak, total, out = lax.fori_loop(2 * pairs, shared, lambda j, c: tile(j, c, False), carry)
    ot_ref[:, here] = out * (1.0 / total)
    lse_ref[...] = peak + jnp.log(total)

    @pl.when(i == GROUP // BLOCK - 1)
    def _():
        for b in range(16):
            o_ref[b] = ot_ref[:, b * TOK : (b + 1) * TOK].astype(bf16)


def attend(qkv, begin):
    whole = lambda *shape: pl.BlockSpec(shape, lambda i: (0,) * len(shape))
    cols = lambda n: pl.BlockSpec((n, BLOCK), lambda i: (0, i))
    return pl.pallas_call(
        attend_kernel,
        grid=(GROUP // BLOCK,),
        in_specs=[whole(GROUP, 256), cols(1)],
        out_specs=[whole(16, HEAD_DIM, TOK), whole(HEAD_DIM, GROUP), cols(1)],
        out_shape=[
            jax.ShapeDtypeStruct((16, HEAD_DIM, TOK), bf16),
            jax.ShapeDtypeStruct((HEAD_DIM, GROUP), f32),
            jax.ShapeDtypeStruct((1, GROUP), f32),
        ],
        scratch_shapes=[
            pltpu.VMEM((GROUP, HEAD_DIM), bf16),
            pltpu.VMEM((HEAD_DIM, GROUP), bf16),
        ],
        compiler_params=pltpu.CompilerParams(vmem_limit_bytes=VMEM_LIMIT),
        cost_estimate=pl.CostEstimate(
            flops=2 * 27 * BLOCK * BLOCK * 512, bytes_accessed=4 << 20, transcendentals=27 * BLOCK * BLOCK
        ),
    )(qkv, begin)


def attend_back_kernel(
    qkv_ref, g_ref, ot_ref, lse_ref, begin_ref, table, out_ref, keys, values, kt, gt, dq, dk, dv
):
    i = pl.program_id(0)
    here = pl.ds(pl.multiple_of(i * BLOCK, BLOCK), BLOCK)

    @pl.when(i == 0)
    def _():
        dk[...] = jnp.zeros_like(dk)
        dv[...] = jnp.zeros_like(dv)
        keys[...] = qkv_ref[:, 64:128]
        values[...] = qkv_ref[:, 128:192]
        kt[...] = qkv_ref[:, 64:128].T
        for b in range(16):
            gt[:, b * TOK : (b + 1) * TOK] = g_ref[b]

    q = qkv_ref[here, :64]
    g = gt[:, here]
    begin = begin_ref[...]
    lse = lse_ref[...]
    inner = jnp.sum(g.astype(f32) * ot_ref[...], axis=0, keepdims=True)

    def tile(j, dq, masked, n=1):
        start = pl.multiple_of(j * BLOCK, BLOCK)
        at = pl.ds(start, n * BLOCK)
        s = lax.dot_general(keys[at, :], q, NT, preferred_element_type=f32)
        if masked:
            s = tile_mask(s, start, i * BLOCK, begin)
        p = jnp.exp(s - lse)
        dp = jnp.dot(values[at, :], g, preferred_element_type=f32)
        ds = (p * (dp - inner)).astype(bf16)
        dv[at, :] += lax.dot_general(p.astype(bf16), g, NT, preferred_element_type=f32)
        dk[at, :] += jnp.dot(ds, q, preferred_element_type=f32)
        return dq + jnp.dot(kt[:, at], ds, preferred_element_type=f32)

    dqt = tile(i, jnp.zeros((HEAD_DIM, BLOCK), f32), True)
    window, shared = key_ranges(i)
    dqt = lax.fori_loop(window, i, lambda j, c: tile(j, c, True), dqt)
    pairs = shared // 2
    dqt = lax.fori_loop(0, pairs, lambda j, c: tile(2 * j, c, False, 2), dqt)
    dqt = lax.fori_loop(2 * pairs, shared, lambda j, c: tile(j, c, False), dqt)
    dq[here, :] = dqt.T * HEAD_DIM**-0.5

    @pl.when(i == GROUP // BLOCK - 1)
    def _():
        def back(b, _):
            at = pl.ds(pl.multiple_of(b * BLOCK, BLOCK), BLOCK)
            c, s = table[at, :HEAD_DIM], table[at, HEAD_DIM:]
            q, k = dq[at, :].astype(bf16).astype(f32), dk[at, :].astype(bf16).astype(f32)
            parts = [q * c + turn_back(q * s), k * c + turn_back(k * s), dv[at, :], jnp.zeros_like(q)]
            out_ref[at, :] = jnp.concatenate(parts, axis=1).astype(bf16)
            return 0

        lax.fori_loop(0, GROUP // BLOCK, back, 0)


def attend_back(qkv, g, ot, lse, begin, table):
    whole = lambda *shape: pl.BlockSpec(shape, lambda i: (0,) * len(shape))
    cols = lambda n: pl.BlockSpec((n, BLOCK), lambda i: (0, i))
    return pl.pallas_call(
        attend_back_kernel,
        grid=(GROUP // BLOCK,),
        in_specs=[
            whole(GROUP, 256),
            whole(16, HEAD_DIM, TOK),
            cols(HEAD_DIM),
            cols(1),
            cols(1),
            whole(GROUP, 128),
        ],
        out_specs=whole(GROUP, 256),
        out_shape=jax.ShapeDtypeStruct((GROUP, 256), bf16),
        scratch_shapes=[
            pltpu.VMEM((GROUP, HEAD_DIM), bf16),
            pltpu.VMEM((GROUP, HEAD_DIM), bf16),
            pltpu.VMEM((HEAD_DIM, GROUP), bf16),
            pltpu.VMEM((HEAD_DIM, GROUP), bf16),
            pltpu.VMEM((GROUP, HEAD_DIM), f32),
            pltpu.VMEM((GROUP, HEAD_DIM), f32),
            pltpu.VMEM((GROUP, HEAD_DIM), f32),
        ],
        compiler_params=pltpu.CompilerParams(vmem_limit_bytes=VMEM_LIMIT),
        cost_estimate=pl.CostEstimate(
            flops=5 * 27 * BLOCK * BLOCK * 512, bytes_accessed=8 << 20, transcendentals=27 * BLOCK * BLOCK
        ),
    )(qkv, g, ot, lse, begin, table)


def experts_kernel(
    own_ref, ffn_mine, ffn_other, g_mine, g_other, routes_mine, routes_other, router_ref, own_w, across_w, *refs
):
    routed_mine, routed_other, moved_mine, moved_other = refs[-10:-6]
    x_ref, dh_ref, act_ref, dy_ref, w_ref, sem = refs[-6:]
    own = own_ref[0]

    copies = [
        [
            pltpu.make_async_copy(shards.at[y, e], w_ref.at[e, 2 * y + (own_ref[1] ^ a)], sem.at[a, y, e])
            for a, shards in enumerate((own_w, across_w))
            for y in range(4)
        ]
        for e in range(2)
    ]

    @pl.when(pl.program_id(0) == 0)
    def _():
        for copy in copies[0] + copies[1]:
            copy.start()

    expert_rows = lax.broadcasted_iota(i32, (EXPERTS, TOK), 0)
    slot_rows = lax.broadcasted_iota(i32, (SLOTS, TOK), 0).astype(f32)
    upto = (
        lax.broadcasted_iota(i32, (TOK, TOK), 0) <= lax.broadcasted_iota(i32, (TOK, TOK), 1)
    ).astype(f32).astype(bf16)
    slot_cols = []
    gate_grads = [jnp.zeros((EXPERTS, WIDTH), f32) for _ in range(4)]
    payload_rows = lax.broadcasted_iota(i32, (EXPERTS, WIDTH), 0)
    gate_rows = [[], []]
    picks = [[], []]
    picked_rows = [[], []]
    picked_grads = [[], []]
    blocks = [(ffn_mine, g_mine, routes_mine, 0), (ffn_other, g_other, routes_other, 0)]
    blocks = blocks + [(*refs_of[:3], 1) for refs_of in blocks]
    for rows_ref, grads_ref, routes_ref, n in blocks:
        rows, grads = rows_ref[n], grads_ref[n]
        routes = routes_ref[n][:8, :TOK].astype(f32).astype(i32)
        chosen = expert_rows == routes[0:1]
        for j in range(1, 8):
            chosen = chosen | (expert_rows == routes[j : j + 1])
        named = [jnp.max((routes == own + e).astype(f32), axis=0, keepdims=True) for e in range(2)]
        named = jnp.concatenate(named + [jnp.zeros((6, TOK), f32)], axis=0)
        rank = jnp.dot(named.astype(bf16), upto, preferred_element_type=f32)
        slots = jnp.where(named > 0, rank - 1.0, -1.0)
        slot_cols.append(slots.T)
        logits = lax.dot_general(router_ref[...], rows, NT, preferred_element_type=f32)
        peak = jnp.max(jnp.where(chosen, logits, masked_score), axis=0, keepdims=True)
        raised = jnp.where(chosen, jnp.exp(jnp.minimum(logits - peak, 0.0)), 0.0)
        gates = raised / jnp.sum(raised, axis=0, keepdims=True)
        for e in range(2):
            gate_rows[e].append(
                jnp.sum(jnp.where(expert_rows == own + e, gates, 0.0), axis=0, keepdims=True)
            )
            picks[e].append((slots[e : e + 1] == slot_rows).astype(f32))
        low = jnp.concatenate([picks[0][-1], picks[1][-1]], axis=0).astype(bf16)
        for source, kept in ((rows, picked_rows), (grads, picked_grads)):
            both = jnp.dot(low, source, preferred_element_type=f32)
            kept[0].append(both[:SLOTS])
            kept[1].append(both[SLOTS:])
    moved, routed = [], []
    for e in range(2):

        @pl.when(pl.program_id(0) == 0)
        def _():
            for copy in copies[e]:
                copy.wait()

        w_gate_up = w_ref[e, :, :128, :].reshape(WIDTH, 2 * FF)
        w_down = w_ref[e, :, 128:, :].reshape(FF, WIDTH)
        x = jnp.concatenate(picked_rows[e], axis=0).astype(bf16)
        gate = jnp.concatenate(
            [jnp.sum(p * r, axis=1, keepdims=True) for p, r in zip(picks[e], gate_rows[e])], axis=0
        )
        grads = jnp.concatenate(picked_grads[e], axis=0)
        dy = (gate * grads).astype(bf16)
        mixed = jnp.dot(x, w_gate_up, preferred_element_type=f32)
        dact = lax.dot_general(dy, w_down, NT, preferred_element_type=f32)
        gate_part, up_part = mixed[:, :FF], mixed[:, FF:]
        sigma = 1.0 / (1.0 + jnp.exp(-gate_part))
        silu = gate_part * sigma
        act = (silu * up_part).astype(bf16)
        dh = jnp.concatenate(
            [dact * up_part * (sigma + silu * (1.0 - sigma)), dact * silu], axis=1
        ).astype(bf16)
        x_ref[e] = x
        dy_ref[e] = dy
        act_ref[e] = act
        dh_ref[e] = dh
        returned = jnp.dot(act, w_down, preferred_element_type=f32).astype(bf16).astype(f32)
        dgate = jnp.sum(returned * grads, axis=1, keepdims=True)
        for b in range(4):
            grad = jnp.sum(
                picks[e][b] * dgate[b * SLOTS : (b + 1) * SLOTS], axis=0, keepdims=True
            )
            high = grad.astype(bf16).astype(f32)
            gap = jnp.zeros((1, 256 - TOK), f32)
            wide = jnp.concatenate([high, gap, grad - high, gap, jnp.zeros((1, WIDTH - 512), f32)], axis=1)
            gate_grads[b] = gate_grads[b] + jnp.where(payload_rows == own + e, wide, 0.0)
        moved.append(gate * returned)
        routed.append(lax.dot_general(dh, w_gate_up, NT, preferred_element_type=f32))
    columns = lax.broadcasted_iota(i32, (TOK, 2 * SLOTS), 1).astype(f32)
    outs = [(routed_mine, moved_mine, 0), (routed_other, moved_other, 0), (routed_mine, moved_mine, 1), (routed_other, moved_other, 1)]
    for b, (routed_ref, moved_ref, n) in enumerate(outs):
        first, second = slot_cols[b][:, 0:1], slot_cols[b][:, 1:2]
        back = ((columns == first) | ((columns == second + SLOTS) & (second >= 0))).astype(f32).astype(bf16)
        at = slice(b * SLOTS, (b + 1) * SLOTS)
        for terms, ref in ((routed, routed_ref), (moved, moved_ref)):
            joined = jnp.concatenate([terms[0][at], terms[1][at]], axis=0).astype(bf16)
            ref[n, :TOK, :] = jnp.dot(back, joined, preferred_element_type=f32).astype(bf16)
        routed_ref[n, TOK:, :] = gate_grads[b].astype(bf16)


def run_experts(half, own, ffn, grads, weights, router, before):
    pair = pl.BlockSpec((2, TOK, WIDTH), lambda i, o: (i, 0, 0))
    pair_of_all = pl.BlockSpec((2, TOK, WIDTH), lambda i, o: (i + 2 * half, 0, 0))
    whole = lambda shape: pl.BlockSpec(shape, lambda i, o: (0,) * len(shape))
    routes = pl.BlockSpec((2, 16, 256), lambda i, o: (i, TOK // 16, 0))
    summed = pl.BlockSpec((2, PAY, WIDTH), lambda i, o: (i, 0, 0))
    kept = lambda n: pl.BlockSpec((2, STEP_ROWS, n), lambda i, o: (0, i + 2 * half, 0))
    part = jax.ShapeDtypeStruct((4, PAY, WIDTH), bf16)
    keep = lambda n: jax.ShapeDtypeStruct((2, ALL_ROWS, n), bf16)
    return pl.pallas_call(
        experts_kernel,
        grid_spec=pltpu.PrefetchScalarGridSpec(
            num_scalar_prefetch=1,
            grid=(2,),
            in_specs=[
                pair,
                pair,
                pair,
                pair,
                routes,
                routes,
                whole((EXPERTS, WIDTH)),
            ]
            + [pl.BlockSpec(memory_space=pl.ANY)] * (2 + len(before)),
            out_specs=[
                summed,
                summed,
                pair_of_all,
                pair_of_all,
                kept(WIDTH),
                kept(2 * FF),
                kept(FF),
                kept(WIDTH),
            ],
            scratch_shapes=[
                pltpu.VMEM((2, 8, 192, 1024), bf16),
                pltpu.SemaphoreType.DMA((2, 4, 2)),
            ],
        ),
        out_shape=[
            part,
            part,
            jax.ShapeDtypeStruct((8, TOK, WIDTH), bf16),
            jax.ShapeDtypeStruct((8, TOK, WIDTH), bf16),
            keep(WIDTH),
            keep(2 * FF),
            keep(FF),
            keep(WIDTH),
        ],
        input_output_aliases={10 + i: 2 + i for i in range(len(before))},
        compiler_params=pltpu.CompilerParams(vmem_limit_bytes=VMEM_LIMIT),
        cost_estimate=pl.CostEstimate(
            flops=14 << 30, bytes_accessed=24 << 20, transcendentals=8 * SLOTS * 2 * FF
        ),
    )(own, *ffn, *grads, *grads, router, *weights, *before)


def expert_grads_kernel(x_ref, dh_ref, act_ref, dy_ref, out_ref):
    up = lax.dot_general(x_ref[0], dh_ref[0], TN, preferred_element_type=f32)
    down = lax.dot_general(act_ref[0], dy_ref[0], TN, preferred_element_type=f32)
    out_ref[0, :, 0, :128, :] = up.astype(bf16).reshape(2, 128, 2 * FF)
    out_ref[0, :, 0, 128:, :] = down.astype(bf16).reshape(2, 64, WIDTH)


def expert_weight_grads(x, dh, act, dy):
    return pl.pallas_call(
        expert_grads_kernel,
        grid=(2, 4),
        in_specs=[
            pl.BlockSpec((1, ALL_ROWS, 256), lambda e, i: (e, 0, i)),
            pl.BlockSpec((1, ALL_ROWS, 2 * FF), lambda e, i: (e, 0, 0)),
            pl.BlockSpec((1, ALL_ROWS, 128), lambda e, i: (e, 0, i)),
            pl.BlockSpec((1, ALL_ROWS, WIDTH), lambda e, i: (e, 0, 0)),
        ],
        out_specs=pl.BlockSpec((1, 2, 1, 192, 1024), lambda e, i: (i, 0, e, 0, 0)),
        out_shape=jax.ShapeDtypeStruct((4, 2, 2, 192, 1024), bf16),
        compiler_params=pltpu.CompilerParams(vmem_limit_bytes=VMEM_LIMIT),
        cost_estimate=pl.CostEstimate(flops=8 << 30, bytes_accessed=14 << 20, transcendentals=0),
    )(x, dh, act, dy)


def hidden_kernel(att_ref, w_ref, rows_ref, gain_ref, hidden_ref, normed_ref):
    att = att_ref[...].reshape(WIDTH, TOK)
    hidden = rows_ref[...].astype(f32) + lax.dot_general(
        att, w_ref[:, :WIDTH], TN, preferred_element_type=f32
    )
    hidden_ref[...] = hidden
    normed_ref[...] = (hidden * inverse_rms(hidden) * gain_ref[...]).astype(bf16)


def hidden_of(attended, shared, rows, gain):
    return pl.pallas_call(
        hidden_kernel,
        out_shape=[
            jax.ShapeDtypeStruct((TOK, WIDTH), f32),
            jax.ShapeDtypeStruct((TOK, WIDTH), bf16),
        ],
        compiler_params=pltpu.CompilerParams(vmem_limit_bytes=VMEM_LIMIT),
        cost_estimate=pl.CostEstimate(
            flops=2 * TOK * WIDTH * WIDTH, bytes_accessed=5 << 20, transcendentals=0
        ),
    )(attended, shared, rows, gain)


def hidden_back_kernel(
    t0, t1, t2, t3, crossed, hidden_ref, normed_ref, chosen_ref, router_ref, g_ref, gain_ref,
    w_ref, hidden_grad_ref, branch_ref, logit_ref, scaled_ref, att_ref
):
    chosen = chosen_ref[...] > 0
    logits = lax.dot_general(router_ref[...], normed_ref[...], NT, preferred_element_type=f32)
    peak = jnp.max(jnp.where(chosen, logits, masked_score), axis=0, keepdims=True)
    raised = jnp.where(chosen, jnp.exp(jnp.minimum(logits - peak, 0.0)), 0.0)
    gates = raised / jnp.sum(raised, axis=0, keepdims=True)
    summed = t0[...].astype(f32)
    for term in (t1, t2, t3, crossed):
        summed = summed + term[...].astype(f32)
    gate_grad = summed[TOK:, :TOK] + summed[TOK:, 256 : 256 + TOK]
    logit_grad = gates * (gate_grad - jnp.sum(gates * gate_grad, axis=0, keepdims=True))
    logit_grad = logit_grad.astype(bf16)
    logit_ref[...] = logit_grad
    normed_grad = summed[:TOK] + lax.dot_general(
        logit_grad, router_ref[...], TN, preferred_element_type=f32
    )
    hidden = hidden_ref[...]
    scale = inverse_rms(hidden)
    scaled_ref[...] = (normed_grad * hidden * scale).astype(bf16)
    hidden_grad = g_ref[...].astype(f32) + rms_pull(hidden, scale, gain_ref[...], normed_grad)
    hidden_grad_ref[...] = hidden_grad
    branch = hidden_grad.astype(bf16)
    branch_ref[...] = branch
    att = lax.dot_general(w_ref[:, :WIDTH], branch, NT, preferred_element_type=f32)
    att_ref[...] = att.astype(bf16).reshape(HEADS, HEAD_DIM, TOK)


def hidden_back(terms, crossed, hidden, normed, chosen, router_t, g, gain, shared):
    wide = lambda t: jax.ShapeDtypeStruct((TOK, WIDTH), t)
    return pl.pallas_call(
        hidden_back_kernel,
        out_shape=[
            wide(f32),
            wide(bf16),
            jax.ShapeDtypeStruct((EXPERTS, TOK), bf16),
            wide(bf16),
            jax.ShapeDtypeStruct((HEADS, HEAD_DIM, TOK), bf16),
        ],
        compiler_params=pltpu.CompilerParams(vmem_limit_bytes=VMEM_LIMIT),
        cost_estimate=pl.CostEstimate(
            flops=2 * TOK * WIDTH * WIDTH, bytes_accessed=8 << 20, transcendentals=0
        ),
    )(*terms, crossed, hidden, normed, chosen, router_t, g, gain, shared)


def shared_grads_kernel(att_ref, branch_ref, normed_ref, logit_ref, scaled_ref, out_ref):
    over_tokens = (((0,), (1,)), ((), ()))
    logit = jnp.concatenate([logit_ref[...], jnp.zeros((96, TOK), bf16)], axis=0)
    ones = (lax.broadcasted_iota(i32, (128, TOK), 0) == EXPERTS).astype(f32).astype(bf16)
    att = att_ref[...].reshape(WIDTH, TOK)
    grads = [
        jnp.dot(att, branch_ref[...], preferred_element_type=f32),
        lax.dot_general(normed_ref[...], logit, over_tokens, preferred_element_type=f32)
        + lax.dot_general(scaled_ref[...], ones, over_tokens, preferred_element_type=f32),
    ]
    for w in range(8):
        for part, at in zip(grads, (slice(0, WIDTH), slice(WIDTH, None))):
            rows = [part[s * 64 + w * 8 : s * 64 + w * 8 + 8] for s in range(16)]
            out_ref[w, :, at] = jnp.concatenate(rows, axis=0).astype(bf16)


def shared_weight_grads(att, branch, normed, logit_grad, scaled):
    return pl.pallas_call(
        shared_grads_kernel,
        out_shape=jax.ShapeDtypeStruct((8, 128, 1152), bf16),
        compiler_params=pltpu.CompilerParams(vmem_limit_bytes=VMEM_LIMIT),
        cost_estimate=pl.CostEstimate(
            flops=2 * TOK * WIDTH * 1280, bytes_accessed=5 << 20, transcendentals=0
        ),
    )(att, branch, normed, logit_grad, scaled)


def local(
    tokens,
    routes,
    cont_lengths,
    norm_attn,
    w_qkv,
    w_out,
    w_router,
    norm_ffn,
    w_gate_up,
    w_down,
    cotangent,
):
    seq_index = lax.axis_index("seq")
    places, blocks = relative_places(seq_index)
    rows = tokens[0]
    query_width = HEADS * HEAD_DIM
    kv_width = KV_HEADS * HEAD_DIM

    position, begin = group_layout(cont_lengths[0])
    begin = begin[None]
    table = rotary_table(position.astype(f32))
    kv_heads = lambda start: jnp.repeat(
        w_qkv[:, start : start + kv_width].reshape(8, KV_HEADS, HEAD_DIM), 2, axis=1
    )
    head_cols = jnp.concatenate(
        [
            w_qkv[:, :query_width].reshape(8, HEADS, HEAD_DIM),
            kv_heads(query_width),
            kv_heads(query_width + kv_width),
            jnp.broadcast_to(norm_attn[:, None, None], (8, HEADS, HEAD_DIM)),
        ],
        axis=2,
    ).transpose(1, 0, 2)
    head_cols = jnp.broadcast_to(head_cols[:, None], (HEADS, 8, 8, 256)).reshape(128, 8, 256)
    head_weights = lax.all_to_all(head_cols, BOTH, 0, 0, tiled=True).reshape(WIDTH, 256)
    gain_attn = head_weights[:, 192].astype(f32)[None]
    head_weights = jnp.where(jnp.arange(256)[None] < 192, head_weights, 0.0).astype(bf16)

    rows_near = [rows] + [send(rows, 0, b) for b in (1, 3, 2)]
    rows_near, table, head_weights = tie(rows_near, table, head_weights)
    rows_near = both_cores(rows_near)
    rows_far = send(rows_near[0], 1, 0)

    own_x = lax.axis_index("wshard") % 2
    expert_rows = jnp.concatenate([w_gate_up, w_down], axis=1)
    along_y = lambda t: lax.all_gather(t, "wshard", axis_index_groups=ALONG_Y, axis=0)
    experts, expert_rows = along_y(expert_rows), swap_x(expert_rows)

    qkv = project(places[:8], rows_near, head_weights, gain_attn, table, ())
    shared = jnp.concatenate(
        [w_out, w_router, norm_ffn[:, None], jnp.zeros((8, 95), bf16)], axis=1
    )
    shared, qkv = tie(shared, qkv)
    shared = lax.all_to_all(
        jnp.broadcast_to(shared[None], (128, 8, 1152)), BOTH, 0, 0, tiled=True
    ).reshape(WIDTH, 1152)
    routes_rows = jnp.pad(routes[0].T.astype(bf16), ((0, 8), (0, WIDTH - TOK)))
    upstream_rows = jnp.concatenate([cotangent[0], routes_rows], axis=0)
    upstream_rows, _ = tie(upstream_rows, rows_near[0])
    grad_near = [upstream_rows] + [send(upstream_rows, 0, b) for b in (1, 3, 2)]
    rows_far, qkv, grad_near, upstream_rows = tie(rows_far, qkv, grad_near, upstream_rows)
    grad_across = send(upstream_rows, 1, 0)
    rows_far = (rows_far, swap_cores(rows_far))
    qkv = project(places[8:], rows_far, head_weights, gain_attn, table, (qkv,))
    qkv, grad_across = tie(qkv, grad_across)
    grad_far = gather_far(grad_across)

    router_t = shared[:, WIDTH : WIDTH + EXPERTS].T
    gain_ffn = shared[:, WIDTH + EXPERTS].astype(f32)[None]
    attended_head, attended_t, lse = attend(qkv, begin)
    attended_head, shared, expert_rows = tie(attended_head, shared, expert_rows)
    experts = [experts, along_y(expert_rows)]
    attended = lax.all_to_all(attended_head, "seq", 0, 0, tiled=True)
    hidden, normed_ffn = hidden_of(attended, shared, rows, gain_ffn)
    normed_ffn, grad_far = tie(normed_ffn, grad_far)

    ffn_near, ffn_across = gather_near(normed_ffn)
    ffn_near, _ = tie(ffn_near, ffn_across)
    grad_near = both_cores(grad_near)
    ffn_near, ffn_far = both_cores(ffn_near), gather_far(ffn_across)
    own = jnp.stack([seq_index * 2, own_x])
    near = run_experts(0, own, ffn_near, grad_near, experts, router_t, ())
    near_terms = sum_along_z(*near[:2])
    ffn_far = both_cores(ffn_far)
    grad_far = both_cores(grad_far)
    far = run_experts(1, own, ffn_far, grad_far, experts, router_t, near[2:])
    far, near_terms = tie(far, near_terms)
    moved, saved = far[2:4], far[4:]
    far_other, moved_other = tie(swap_cores(far[1]), moved[1])
    far_terms = send_along_z(chip_parts(far[0], far_other))
    expert_grads = expert_weight_grads(*saved)
    moved_other = swap_cores(moved_other)
    far_terms, expert_grads, moved_other = tie(far_terms, expert_grads, moved_other)
    crossed = send(add_low(*far_terms), 1, 0)
    by_x = [t.reshape(2, 4, TOK, WIDTH) for t in (moved[0], moved_other)]
    moved_parts = [add_low(by_x[0][:, i], by_x[1][:, i]) for i in range(4)]
    crossed, moved_parts = tie(crossed, moved_parts)

    expert_range = jnp.arange(EXPERTS, dtype=i32)
    chosen_here = jnp.any(routes[0].T[None] == expert_range[:, None, None], axis=1).astype(f32)
    hidden_grad, branch_grad, logit_grad, scaled_grad, attended_grad = hidden_back(
        near_terms, crossed, hidden, normed_ffn, chosen_here, router_t, cotangent[0], gain_ffn, shared
    )
    expert_grads = lax.psum_scatter(
        expert_grads.reshape(8, 2, 192, 1024),
        "wshard",
        axis_index_groups=ALONG_Y,
        scatter_dimension=0,
        tiled=True,
    )
    head_grad = lax.all_to_all(attended_grad, "seq", 0, 0, tiled=True)
    shared_grads = shared_weight_grads(attended, branch_grad, normed_ffn, logit_grad, scaled_grad)
    head_grad, shared_grads, moved_parts = tie(head_grad, shared_grads, moved_parts)
    moved_terms = [moved_parts[0]] + [
        send(moved_parts[i], 0, -b) for i, b in ((1, 1), (2, 3), (3, 2))
    ]

    shared_grads = lax.all_to_all(shared_grads, "wshard", 0, 0, tiled=True)
    projected_grad = attend_back(qkv, head_grad, attended_t, lse, begin, table)
    far_part = project_back(places[8:], projected_grad, head_weights)
    far_part, shared_grads, moved_terms = tie(far_part, shared_grads, moved_terms)
    far_parts = chip_parts(far_part[0], swap_cores(far_part[1]))
    near_part = project_back(places[:8], projected_grad, head_weights)
    near_part, expert_grads = tie(near_part, expert_grads)
    far_parts, projected_grad, shared_grads, moved_terms, expert_grads = tie(
        far_parts, projected_grad, shared_grads, moved_terms, expert_grads
    )
    far_terms = send_along_z(far_parts)
    near_parts = chip_parts(near_part[0], swap_cores(near_part[1]))
    moved_crossed = send(add_low(*[t[1] for t in moved_terms]), 1, 0)
    shared_grads = jnp.sum(shared_grads.astype(f32), axis=0).astype(bf16).reshape(16, 8, 1152)
    shared_grads = lax.all_to_all(shared_grads, "seq", 0, 0, tiled=True)
    grad_head = head_weight_grad(places, rows_near, rows_far, gain_attn, projected_grad)
    far_terms, near_parts, grad_head = tie(far_terms, near_parts, grad_head)
    near_terms = send_along_z(near_parts)
    grad_heads = lax.all_to_all(grad_head.reshape(128, 8, 256), BOTH, 0, 0, tiled=True)
    crossed = send(add_low(*far_terms), 1, 0)
    crossed, near_terms, grad_heads, shared_grads = tie(
        crossed, near_terms, grad_heads, shared_grads
    )
    kept = lax.dynamic_index_in_dim(expert_grads, own_x, 0, keepdims=False)
    sent = lax.dynamic_index_in_dim(expert_grads, 1 - own_x, 0, keepdims=False)
    expert_grads = kept.astype(f32) + swap_x(sent).astype(f32)
    total = lambda terms: sum([t.astype(f32) for t in terms])
    output = (hidden + total([t[0] for t in moved_terms] + [moved_crossed])).astype(bf16)
    normed_grad = total(near_terms + [crossed])
    shared_grads = jnp.sum(shared_grads.astype(f32), axis=0)
    grad_heads = jnp.sum(grad_heads.reshape(16, 8, 8, 256).astype(f32), axis=1).transpose(1, 0, 2)
    kv_sum = lambda start: jnp.sum(
        grad_heads[:, :, start : start + HEAD_DIM].reshape(8, KV_HEADS, 2, HEAD_DIM), axis=2
    ).reshape(8, kv_width)
    grad_qkv = jnp.concatenate(
        [grad_heads[:, :, :HEAD_DIM].reshape(8, query_width), kv_sum(HEAD_DIM), kv_sum(2 * HEAD_DIM)],
        axis=1,
    )
    grad_norm_attn = jnp.sum(grad_qkv * w_qkv.astype(f32), axis=1) / norm_attn.astype(f32)
    inputs = rows.astype(f32)
    grad_input = hidden_grad + rms_pull(inputs, inverse_rms(inputs), gain_attn, normed_grad)
    return (
        output[None],
        grad_input[None],
        grad_norm_attn,
        grad_qkv,
        shared_grads[:, :WIDTH],
        shared_grads[:, WIDTH : WIDTH + EXPERTS],
        shared_grads[:, WIDTH + EXPERTS],
        expert_grads[:, :128],
        expert_grads[:, 128:],
    )


def solution(mesh):
    return jax.shard_map(
        local,
        mesh=mesh,
        in_specs=(
            P("wshard", "seq", None),
            P("wshard", "seq", None),
            P("wshard", None),
            P(BOTH),
            P(BOTH, None),
            P(BOTH, None),
            P(BOTH, None),
            P(BOTH),
            P("seq", "wshard", None),
            P("seq", "wshard", None),
            P("wshard", "seq", None),
        ),
        out_specs=(
            P("wshard", "seq", None),
            P("wshard", "seq", None),
            P(BOTH),
            P(BOTH, None),
            P(BOTH, None),
            P(BOTH, None),
            P(BOTH),
            P("seq", "wshard", None),
            P("seq", "wshard", None),
        ),
        check_vma=False,
    )
```

```python
import jax
import jax.numpy as jnp
from jax import lax
from jax.experimental import pallas as pl
from jax.experimental.pallas import tpu as pltpu
from jax.sharding import PartitionSpec as P

HEADS = 16
KV_HEADS = 8
HEAD_DIM = 64
EXPERTS = 32
FF = 512
PROMPT = 2048
GROUP = 3584
TOK = 224
WIDTH = 1024
SLOTS = 72
STEP_ROWS = 4 * SLOTS
ALL_ROWS = 16 * SLOTS
BLOCK = 512
VMEM_LIMIT = 60 << 20
PAY = TOK + 32

norm_eps = 1e-06
rope_base = 10000.0
masked_score = -1e30
BOTH = ("seq", "wshard")
NT = (((1,), (1,)), ((), ()))
TN = (((0,), (0,)), ((), ()))
f32 = jnp.float32
bf16 = jnp.bfloat16
i32 = jnp.int32


def place_of(x, z, core):
    return x * 8 + z * 2 + core


def shift_perm(a, b):
    return [
        (place_of(x, z, c), place_of(x ^ a, (z + b) % 4, c))
        for x in range(2)
        for z in range(4)
        for c in range(2)
    ]


CORE_PERM = [(i, i ^ 1) for i in range(16)]


def send(rows, a, b):
    return lax.ppermute(rows, "seq", shift_perm(a, b))


def swap_cores(rows):
    return lax.ppermute(rows, "seq", CORE_PERM)


def relative_places(seq_index):
    x, z, c = seq_index // 8, (seq_index // 2) % 4, seq_index % 2
    r = jnp.arange(16, dtype=i32)
    a, i, k = r // 8, (r // 2) % 4, r % 2
    shift = i ^ (i // 2)
    behind = (z - i) % 4
    places = (a ^ x) * 8 + ((z - shift) % 4) * 2 + (k ^ c)
    return places, (a ^ x) * 8 + (behind ^ (behind // 2)) * 2 + (k ^ c)


def gather_near(rows):
    return [rows] + [send(rows, 0, b) for b in (1, 3, 2)], send(rows, 1, 0)


def both_cores(parts):
    mine = jnp.stack(parts)
    return mine, swap_cores(mine)


def gather_far(across):
    return [across] + [send(across, 0, b) for b in (1, 3, 2)]


def add_low(*terms):
    return sum([t.astype(f32) for t in terms]).astype(bf16)


def sum_along_z(mine, other):
    return send_along_z(chip_parts(mine, swap_cores(other)))


def chip_parts(mine, got):
    return [add_low(mine[i], got[i]) for i in range(4)]


def send_along_z(parts):
    return [parts[0]] + [send(parts[i], 0, -b) for i, b in ((1, 1), (2, 3), (3, 2))]


def swap_x(rows):
    return lax.ppermute(rows, "wshard", [(w, w ^ 1) for w in range(8)])


ALONG_Y = [[y * 2 + x for y in range(4)] for x in range(2)]


def tie(*values):
    return lax.optimization_barrier(values)


def inverse_rms(values):
    return lax.rsqrt(jnp.mean(values * values, axis=-1, keepdims=True) + norm_eps)


def rms_pull(values, scale, gain, grad):
    scaled = grad * gain
    return scale * scaled - values * (scale * scale * scale) * jnp.mean(
        scaled * values, axis=-1, keepdims=True
    )


def group_layout(lengths):
    places = jnp.arange(GROUP, dtype=i32)
    ends = jnp.cumsum(lengths)
    starts = ends - lengths
    offset_in = places - PROMPT
    segment_id = jnp.sum((offset_in[:, None] >= ends[None, :]).astype(i32), axis=1)
    segment_hot = segment_id[:, None] == jnp.arange(lengths.shape[0], dtype=i32)[None, :]
    begin = jnp.sum(jnp.where(segment_hot, starts[None, :], 0), axis=1)
    inside = offset_in >= 0
    position = jnp.where(inside, PROMPT + offset_in - begin, places)
    return position, jnp.where(inside, PROMPT + begin, 0)


def rotary_table(position):
    half_dim = HEAD_DIM // 2
    inverse = rope_base ** (-((jnp.arange(2 * HEAD_DIM) % half_dim).astype(f32) * 2.0) / HEAD_DIM)
    back = jnp.where(jnp.arange(2 * HEAD_DIM) < HEAD_DIM, 0.0, 0.5 * jnp.pi).astype(f32)
    return jnp.cos(position[:, None] * inverse[None, :] - back[None, :])


def turn(values):
    half_dim = HEAD_DIM // 2
    return jnp.concatenate([-values[:, half_dim:], values[:, :half_dim]], axis=-1)


def turn_back(values):
    half_dim = HEAD_DIM // 2
    return jnp.concatenate([values[:, half_dim:], -values[:, :half_dim]], axis=-1)


def project_kernel(places, mine, other, w, gain, table, *refs):
    out = refs[-1]
    j = pl.program_id(0)

    if len(refs) > 1:

        @pl.when(j == 0)
        def _():
            out[...] = refs[0][...]

    for k, ref in enumerate((mine, other)):
        at = pl.ds(pl.multiple_of(places[2 * j + k] * TOK, TOK), TOK)
        rows = ref[0].astype(f32)
        normed = (rows * inverse_rms(rows) * gain[...]).astype(bf16)
        projected = jnp.dot(normed, w[...], preferred_element_type=f32)
        c, s = table[at, :HEAD_DIM], table[at, HEAD_DIM:]
        q, k, v = projected[:, :64], projected[:, 64:128], projected[:, 128:]
        q = (q * c + turn(q) * s).astype(bf16).astype(f32) * HEAD_DIM**-0.5
        out[at, :] = jnp.concatenate([q, k * c + turn(k) * s, v], axis=1).astype(bf16)


def project(places, gathered, w, gain, table, before):
    chip = pl.BlockSpec((1, TOK, WIDTH), lambda j, p: (j, 0, 0))
    whole = lambda *shape: pl.BlockSpec(shape, lambda j, p: (0,) * len(shape))
    return pl.pallas_call(
        project_kernel,
        grid_spec=pltpu.PrefetchScalarGridSpec(
            num_scalar_prefetch=1,
            grid=(4,),
            in_specs=[chip, chip, whole(WIDTH, 256), whole(1, WIDTH), whole(GROUP, 128)]
            + [whole(GROUP, 256)] * len(before),
            out_specs=whole(GROUP, 256),
        ),
        out_shape=jax.ShapeDtypeStruct((GROUP, 256), bf16),
        compiler_params=pltpu.CompilerParams(vmem_limit_bytes=VMEM_LIMIT),
        cost_estimate=pl.CostEstimate(
            flops=2 * 8 * TOK * WIDTH * 256, bytes_accessed=10 << 20, transcendentals=0
        ),
    )(places, *gathered, w, gain, table, *before)


def project_back_kernel(places, first, second, w, mine, other):
    del places
    mine[0] = lax.dot_general(first[...], w[...], NT, preferred_element_type=f32).astype(bf16)
    other[0] = lax.dot_general(second[...], w[...], NT, preferred_element_type=f32).astype(bf16)


def project_back(places, projected_grad, w):
    chip = pl.BlockSpec((1, TOK, WIDTH), lambda j, p: (j, 0, 0))
    at = lambda k: pl.BlockSpec((TOK, 256), lambda j, p: (p[2 * j + k], 0))
    part = jax.ShapeDtypeStruct((4, TOK, WIDTH), bf16)
    return pl.pallas_call(
        project_back_kernel,
        grid_spec=pltpu.PrefetchScalarGridSpec(
            num_scalar_prefetch=1,
            grid=(4,),
            in_specs=[at(0), at(1), pl.BlockSpec((WIDTH, 256), lambda j, p: (0, 0))],
            out_specs=[chip, chip],
        ),
        out_shape=[part, part],
        compiler_params=pltpu.CompilerParams(vmem_limit_bytes=VMEM_LIMIT),
        cost_estimate=pl.CostEstimate(
            flops=2 * 8 * TOK * WIDTH * 256, bytes_accessed=5 << 20, transcendentals=0
        ),
    )(places, projected_grad, projected_grad, w)


def head_grad_kernel(places, near_mine, near_other, far_mine, far_other, gain, first, second, out, total):
    del places
    j = pl.program_id(0)

    @pl.when(j == 0)
    def _():
        total[...] = jnp.zeros_like(total)

    for near, far, projected in ((near_mine, far_mine, first), (near_other, far_other, second)):
        rows = jnp.where(j < 4, near[0], far[0]).astype(f32)
        normed = (rows * inverse_rms(rows) * gain[...]).astype(bf16)
        total[...] += lax.dot_general(normed, projected[...], TN, preferred_element_type=f32)

    @pl.when(j == 7)
    def _():
        out[...] = total[...].astype(bf16)


def head_weight_grad(places, near, far, gain, projected_grad):
    near_chip = pl.BlockSpec((1, TOK, WIDTH), lambda j, p: (jnp.minimum(j, 3), 0, 0))
    far_chip = pl.BlockSpec((1, TOK, WIDTH), lambda j, p: (jnp.maximum(j - 4, 0), 0, 0))
    at = lambda k: pl.BlockSpec((TOK, 256), lambda j, p: (p[2 * j + k], 0))
    return pl.pallas_call(
        head_grad_kernel,
        grid_spec=pltpu.PrefetchScalarGridSpec(
            num_scalar_prefetch=1,
            grid=(8,),
            in_specs=[
                near_chip,
                near_chip,
                far_chip,
                far_chip,
                pl.BlockSpec((1, WIDTH), lambda j, p: (0, 0)),
                at(0),
                at(1),
            ],
            out_specs=pl.BlockSpec((WIDTH, 256), lambda j, p: (0, 0)),
            scratch_shapes=[pltpu.VMEM((WIDTH, 256), f32)],
        ),
        out_shape=jax.ShapeDtypeStruct((WIDTH, 256), bf16),
        compiler_params=pltpu.CompilerParams(vmem_limit_bytes=VMEM_LIMIT),
        cost_estimate=pl.CostEstimate(
            flops=2 * 16 * TOK * WIDTH * 256, bytes_accessed=10 << 20, transcendentals=0
        ),
    )(places, *near, *far, gain, projected_grad, projected_grad)


def tile_mask(scores, key_start, query_start, begin):
    keys = key_start + lax.broadcasted_iota(i32, scores.shape, 0)
    queries = query_start + lax.broadcasted_iota(i32, scores.shape, 1)
    return jnp.where((keys <= queries) & (keys >= begin), scores, masked_score)


def key_ranges(i):
    first = PROMPT // BLOCK
    return jnp.where(i > first, i - 1, i), jnp.minimum(i, first)


def attend_kernel(qkv_ref, begin_ref, o_ref, ot_ref, lse_ref, keys, vt):
    i = pl.program_id(0)
    here = pl.ds(pl.multiple_of(i * BLOCK, BLOCK), BLOCK)

    @pl.when(i == 0)
    def _():
        keys[...] = qkv_ref[:, 64:128]
        vt[...] = qkv_ref[:, 128:192].T

    q = qkv_ref[here, :64]
    begin = begin_ref[...]

    def tile(j, carry, masked, n=1):
        peak, total, out = carry
        start = pl.multiple_of(j * BLOCK, BLOCK)
        at = pl.ds(start, n * BLOCK)
        s = lax.dot_general(keys[at, :], q, NT, preferred_element_type=f32)
        if masked:
            s = tile_mask(s, start, i * BLOCK, begin)
        higher = jnp.maximum(peak, jnp.max(s, axis=0, keepdims=True))
        p = jnp.exp(s - higher)
        fade = jnp.exp(peak - higher)
        total = total * fade + jnp.sum(p, axis=0, keepdims=True)
        out = out * fade + jnp.dot(vt[:, at], p.astype(bf16), preferred_element_type=f32)
        return higher, total, out

    carry = (
        jnp.full((1, BLOCK), masked_score, f32),
        jnp.zeros((1, BLOCK), f32),
        jnp.zeros((HEAD_DIM, BLOCK), f32),
    )
    carry = tile(i, carry, True)
    window, shared = key_ranges(i)
    carry = lax.fori_loop(window, i, lambda j, c: tile(j, c, True), carry)
    pairs = shared // 2
    carry = lax.fori_loop(0, pairs, lambda j, c: tile(2 * j, c, False, 2), carry)
    peak, total, out = lax.fori_loop(2 * pairs, shared, lambda j, c: tile(j, c, False), carry)
    ot_ref[:, here] = out * (1.0 / total)
    lse_ref[...] = peak + jnp.log(total)

    @pl.when(i == GROUP // BLOCK - 1)
    def _():
        for b in range(16):
            o_ref[b] = ot_ref[:, b * TOK : (b + 1) * TOK].astype(bf16)


def attend(qkv, begin):
    whole = lambda *shape: pl.BlockSpec(shape, lambda i: (0,) * len(shape))
    cols = lambda n: pl.BlockSpec((n, BLOCK), lambda i: (0, i))
    return pl.pallas_call(
        attend_kernel,
        grid=(GROUP // BLOCK,),
        in_specs=[whole(GROUP, 256), cols(1)],
        out_specs=[whole(16, HEAD_DIM, TOK), whole(HEAD_DIM, GROUP), cols(1)],
        out_shape=[
            jax.ShapeDtypeStruct((16, HEAD_DIM, TOK), bf16),
            jax.ShapeDtypeStruct((HEAD_DIM, GROUP), f32),
            jax.ShapeDtypeStruct((1, GROUP), f32),
        ],
        scratch_shapes=[
            pltpu.VMEM((GROUP, HEAD_DIM), bf16),
            pltpu.VMEM((HEAD_DIM, GROUP), bf16),
        ],
        compiler_params=pltpu.CompilerParams(vmem_limit_bytes=VMEM_LIMIT),
        cost_estimate=pl.CostEstimate(
            flops=2 * 27 * BLOCK * BLOCK * 512, bytes_accessed=4 << 20, transcendentals=27 * BLOCK * BLOCK
        ),
    )(qkv, begin)


def attend_back_kernel(
    qkv_ref, g_ref, ot_ref, lse_ref, begin_ref, table, out_ref, keys, values, kt, gt, dq, dk, dv
):
    i = pl.program_id(0)
    here = pl.ds(pl.multiple_of(i * BLOCK, BLOCK), BLOCK)

    @pl.when(i == 0)
    def _():
        dk[...] = jnp.zeros_like(dk)
        dv[...] = jnp.zeros_like(dv)
        keys[...] = qkv_ref[:, 64:128]
        values[...] = qkv_ref[:, 128:192]
        kt[...] = qkv_ref[:, 64:128].T
        for b in range(16):
            gt[:, b * TOK : (b + 1) * TOK] = g_ref[b]

    q = qkv_ref[here, :64]
    g = gt[:, here]
    begin = begin_ref[...]
    lse = lse_ref[...]
    inner = jnp.sum(g.astype(f32) * ot_ref[...], axis=0, keepdims=True)

    def tile(j, dq, masked, n=1):
        start = pl.multiple_of(j * BLOCK, BLOCK)
        at = pl.ds(start, n * BLOCK)
        s = lax.dot_general(keys[at, :], q, NT, preferred_element_type=f32)
        if masked:
            s = tile_mask(s, start, i * BLOCK, begin)
        p = jnp.exp(s - lse)
        dp = jnp.dot(values[at, :], g, preferred_element_type=f32)
        ds = (p * (dp - inner)).astype(bf16)
        dv[at, :] += lax.dot_general(p.astype(bf16), g, NT, preferred_element_type=f32)
        dk[at, :] += jnp.dot(ds, q, preferred_element_type=f32)
        return dq + jnp.dot(kt[:, at], ds, preferred_element_type=f32)

    dqt = tile(i, jnp.zeros((HEAD_DIM, BLOCK), f32), True)
    window, shared = key_ranges(i)
    dqt = lax.fori_loop(window, i, lambda j, c: tile(j, c, True), dqt)
    pairs = shared // 2
    dqt = lax.fori_loop(0, pairs, lambda j, c: tile(2 * j, c, False, 2), dqt)
    dqt = lax.fori_loop(2 * pairs, shared, lambda j, c: tile(j, c, False), dqt)
    dq[here, :] = dqt.T * HEAD_DIM**-0.5

    @pl.when(i == GROUP // BLOCK - 1)
    def _():
        def back(b, _):
            at = pl.ds(pl.multiple_of(b * BLOCK, BLOCK), BLOCK)
            c, s = table[at, :HEAD_DIM], table[at, HEAD_DIM:]
            q, k = dq[at, :].astype(bf16).astype(f32), dk[at, :].astype(bf16).astype(f32)
            parts = [q * c + turn_back(q * s), k * c + turn_back(k * s), dv[at, :], jnp.zeros_like(q)]
            out_ref[at, :] = jnp.concatenate(parts, axis=1).astype(bf16)
            return 0

        lax.fori_loop(0, GROUP // BLOCK, back, 0)


def attend_back(qkv, g, ot, lse, begin, table):
    whole = lambda *shape: pl.BlockSpec(shape, lambda i: (0,) * len(shape))
    cols = lambda n: pl.BlockSpec((n, BLOCK), lambda i: (0, i))
    return pl.pallas_call(
        attend_back_kernel,
        grid=(GROUP // BLOCK,),
        in_specs=[
            whole(GROUP, 256),
            whole(16, HEAD_DIM, TOK),
            cols(HEAD_DIM),
            cols(1),
            cols(1),
            whole(GROUP, 128),
        ],
        out_specs=whole(GROUP, 256),
        out_shape=jax.ShapeDtypeStruct((GROUP, 256), bf16),
        scratch_shapes=[
            pltpu.VMEM((GROUP, HEAD_DIM), bf16),
            pltpu.VMEM((GROUP, HEAD_DIM), bf16),
            pltpu.VMEM((HEAD_DIM, GROUP), bf16),
            pltpu.VMEM((HEAD_DIM, GROUP), bf16),
            pltpu.VMEM((GROUP, HEAD_DIM), f32),
            pltpu.VMEM((GROUP, HEAD_DIM), f32),
            pltpu.VMEM((GROUP, HEAD_DIM), f32),
        ],
        compiler_params=pltpu.CompilerParams(vmem_limit_bytes=VMEM_LIMIT),
        cost_estimate=pl.CostEstimate(
            flops=5 * 27 * BLOCK * BLOCK * 512, bytes_accessed=8 << 20, transcendentals=27 * BLOCK * BLOCK
        ),
    )(qkv, g, ot, lse, begin, table)


def experts_kernel(
    own_ref, ffn_mine, ffn_other, g_mine, g_other, routes_mine, routes_other, router_ref, own_w, across_w, *refs
):
    routed_mine, routed_other, moved_mine, moved_other = refs[-10:-6]
    x_ref, dh_ref, act_ref, dy_ref, w_ref, sem = refs[-6:]
    own = own_ref[0]

    copies = [
        [
            pltpu.make_async_copy(shards.at[y, e], w_ref.at[e, 2 * y + (own_ref[1] ^ a)], sem.at[a, y, e])
            for a, shards in enumerate((own_w, across_w))
            for y in range(4)
        ]
        for e in range(2)
    ]

    @pl.when(pl.program_id(0) == 0)
    def _():
        for copy in copies[0] + copies[1]:
            copy.start()

    expert_rows = lax.broadcasted_iota(i32, (EXPERTS, TOK), 0)
    slot_rows = lax.broadcasted_iota(i32, (SLOTS, TOK), 0).astype(f32)
    upto = (
        lax.broadcasted_iota(i32, (TOK, TOK), 0) <= lax.broadcasted_iota(i32, (TOK, TOK), 1)
    ).astype(f32).astype(bf16)
    slot_cols = []
    gate_grads = [jnp.zeros((EXPERTS, WIDTH), f32) for _ in range(4)]
    payload_rows = lax.broadcasted_iota(i32, (EXPERTS, WIDTH), 0)
    gate_rows = [[], []]
    picks = [[], []]
    picked_rows = [[], []]
    picked_grads = [[], []]
    blocks = [(ffn_mine, g_mine, routes_mine, 0), (ffn_other, g_other, routes_other, 0)]
    blocks = blocks + [(*refs_of[:3], 1) for refs_of in blocks]
    for rows_ref, grads_ref, routes_ref, n in blocks:
        rows, grads = rows_ref[n], grads_ref[n]
        routes = routes_ref[n][:8, :TOK].astype(f32).astype(i32)
        chosen = expert_rows == routes[0:1]
        for j in range(1, 8):
            chosen = chosen | (expert_rows == routes[j : j + 1])
        named = [jnp.max((routes == own + e).astype(f32), axis=0, keepdims=True) for e in range(2)]
        named = jnp.concatenate(named + [jnp.zeros((6, TOK), f32)], axis=0)
        rank = jnp.dot(named.astype(bf16), upto, preferred_element_type=f32)
        slots = jnp.where(named > 0, rank - 1.0, -1.0)
        slot_cols.append(slots.T)
        logits = lax.dot_general(router_ref[...], rows, NT, preferred_element_type=f32)
        peak = jnp.max(jnp.where(chosen, logits, masked_score), axis=0, keepdims=True)
        raised = jnp.where(chosen, jnp.exp(jnp.minimum(logits - peak, 0.0)), 0.0)
        gates = raised / jnp.sum(raised, axis=0, keepdims=True)
        for e in range(2):
            gate_rows[e].append(
                jnp.sum(jnp.where(expert_rows == own + e, gates, 0.0), axis=0, keepdims=True)
            )
            picks[e].append((slots[e : e + 1] == slot_rows).astype(f32))
        low = jnp.concatenate([picks[0][-1], picks[1][-1]], axis=0).astype(bf16)
        for source, kept in ((rows, picked_rows), (grads, picked_grads)):
            both = jnp.dot(low, source, preferred_element_type=f32)
            kept[0].append(both[:SLOTS])
            kept[1].append(both[SLOTS:])
    moved, routed = [], []
    for e in range(2):

        @pl.when(pl.program_id(0) == 0)
        def _():
            for copy in copies[e]:
                copy.wait()

        w_gate_up = w_ref[e, :, :128, :].reshape(WIDTH, 2 * FF)
        w_down = w_ref[e, :, 128:, :].reshape(FF, WIDTH)
        x = jnp.concatenate(picked_rows[e], axis=0).astype(bf16)
        gate = jnp.concatenate(
            [jnp.sum(p * r, axis=1, keepdims=True) for p, r in zip(picks[e], gate_rows[e])], axis=0
        )
        grads = jnp.concatenate(picked_grads[e], axis=0)
        dy = (gate * grads).astype(bf16)
        mixed = jnp.dot(x, w_gate_up, preferred_element_type=f32)
        dact = lax.dot_general(dy, w_down, NT, preferred_element_type=f32)
        gate_part, up_part = mixed[:, :FF], mixed[:, FF:]
        sigma = 1.0 / (1.0 + jnp.exp(-gate_part))
        silu = gate_part * sigma
        act = (silu * up_part).astype(bf16)
        dh = jnp.concatenate(
            [dact * up_part * (sigma + silu * (1.0 - sigma)), dact * silu], axis=1
        ).astype(bf16)
        x_ref[e] = x
        dy_ref[e] = dy
        act_ref[e] = act
        dh_ref[e] = dh
        returned = jnp.dot(act, w_down, preferred_element_type=f32).astype(bf16).astype(f32)
        dgate = jnp.sum(returned * grads, axis=1, keepdims=True)
        for b in range(4):
            grad = jnp.sum(
                picks[e][b] * dgate[b * SLOTS : (b + 1) * SLOTS], axis=0, keepdims=True
            )
            high = grad.astype(bf16).astype(f32)
            gap = jnp.zeros((1, 256 - TOK), f32)
            wide = jnp.concatenate([high, gap, grad - high, gap, jnp.zeros((1, WIDTH - 512), f32)], axis=1)
            gate_grads[b] = gate_grads[b] + jnp.where(payload_rows == own + e, wide, 0.0)
        moved.append(gate * returned)
        routed.append(lax.dot_general(dh, w_gate_up, NT, preferred_element_type=f32))
    columns = lax.broadcasted_iota(i32, (TOK, 2 * SLOTS), 1).astype(f32)
    outs = [(routed_mine, moved_mine, 0), (routed_other, moved_other, 0), (routed_mine, moved_mine, 1), (routed_other, moved_other, 1)]
    for b, (routed_ref, moved_ref, n) in enumerate(outs):
        first, second = slot_cols[b][:, 0:1], slot_cols[b][:, 1:2]
        back = ((columns == first) | ((columns == second + SLOTS) & (second >= 0))).astype(f32).astype(bf16)
        at = slice(b * SLOTS, (b + 1) * SLOTS)
        for terms, ref in ((routed, routed_ref), (moved, moved_ref)):
            joined = jnp.concatenate([terms[0][at], terms[1][at]], axis=0).astype(bf16)
            ref[n, :TOK, :] = jnp.dot(back, joined, preferred_element_type=f32).astype(bf16)
        routed_ref[n, TOK:, :] = gate_grads[b].astype(bf16)


def run_experts(half, own, ffn, grads, weights, router, before):
    pair = pl.BlockSpec((2, TOK, WIDTH), lambda i, o: (i, 0, 0))
    pair_of_all = pl.BlockSpec((2, TOK, WIDTH), lambda i, o: (i + 2 * half, 0, 0))
    whole = lambda shape: pl.BlockSpec(shape, lambda i, o: (0,) * len(shape))
    routes = pl.BlockSpec((2, 16, 256), lambda i, o: (i, TOK // 16, 0))
    summed = pl.BlockSpec((2, PAY, WIDTH), lambda i, o: (i, 0, 0))
    kept = lambda n: pl.BlockSpec((2, STEP_ROWS, n), lambda i, o: (0, i + 2 * half, 0))
    part = jax.ShapeDtypeStruct((4, PAY, WIDTH), bf16)
    keep = lambda n: jax.ShapeDtypeStruct((2, ALL_ROWS, n), bf16)
    return pl.pallas_call(
        experts_kernel,
        grid_spec=pltpu.PrefetchScalarGridSpec(
            num_scalar_prefetch=1,
            grid=(2,),
            in_specs=[
                pair,
                pair,
                pair,
                pair,
                routes,
                routes,
                whole((EXPERTS, WIDTH)),
            ]
            + [pl.BlockSpec(memory_space=pl.ANY)] * (2 + len(before)),
            out_specs=[
                summed,
                summed,
                pair_of_all,
                pair_of_all,
                kept(WIDTH),
                kept(2 * FF),
                kept(FF),
                kept(WIDTH),
            ],
            scratch_shapes=[
                pltpu.VMEM((2, 8, 192, 1024), bf16),
                pltpu.SemaphoreType.DMA((2, 4, 2)),
            ],
        ),
        out_shape=[
            part,
            part,
            jax.ShapeDtypeStruct((8, TOK, WIDTH), bf16),
            jax.ShapeDtypeStruct((8, TOK, WIDTH), bf16),
            keep(WIDTH),
            keep(2 * FF),
            keep(FF),
            keep(WIDTH),
        ],
        input_output_aliases={10 + i: 2 + i for i in range(len(before))},
        compiler_params=pltpu.CompilerParams(vmem_limit_bytes=VMEM_LIMIT),
        cost_estimate=pl.CostEstimate(
            flops=14 << 30, bytes_accessed=24 << 20, transcendentals=8 * SLOTS * 2 * FF
        ),
    )(own, *ffn, *grads, *grads, router, *weights, *before)


def expert_grads_kernel(x_ref, dh_ref, act_ref, dy_ref, out_ref):
    up = lax.dot_general(x_ref[0], dh_ref[0], TN, preferred_element_type=f32)
    down = lax.dot_general(act_ref[0], dy_ref[0], TN, preferred_element_type=f32)
    out_ref[0, :, 0, :128, :] = up.astype(bf16).reshape(2, 128, 2 * FF)
    out_ref[0, :, 0, 128:, :] = down.astype(bf16).reshape(2, 64, WIDTH)


def expert_weight_grads(x, dh, act, dy):
    return pl.pallas_call(
        expert_grads_kernel,
        grid=(2, 4),
        in_specs=[
            pl.BlockSpec((1, ALL_ROWS, 256), lambda e, i: (e, 0, i)),
            pl.BlockSpec((1, ALL_ROWS, 2 * FF), lambda e, i: (e, 0, 0)),
            pl.BlockSpec((1, ALL_ROWS, 128), lambda e, i: (e, 0, i)),
            pl.BlockSpec((1, ALL_ROWS, WIDTH), lambda e, i: (e, 0, 0)),
        ],
        out_specs=pl.BlockSpec((1, 2, 1, 192, 1024), lambda e, i: (i, 0, e, 0, 0)),
        out_shape=jax.ShapeDtypeStruct((4, 2, 2, 192, 1024), bf16),
        compiler_params=pltpu.CompilerParams(vmem_limit_bytes=VMEM_LIMIT),
        cost_estimate=pl.CostEstimate(flops=8 << 30, bytes_accessed=14 << 20, transcendentals=0),
    )(x, dh, act, dy)


def hidden_kernel(att_ref, w_ref, rows_ref, gain_ref, hidden_ref, normed_ref):
    att = att_ref[...].reshape(WIDTH, TOK)
    hidden = rows_ref[...].astype(f32) + lax.dot_general(
        att, w_ref[:, :WIDTH], TN, preferred_element_type=f32
    )
    hidden_ref[...] = hidden
    normed_ref[...] = (hidden * inverse_rms(hidden) * gain_ref[...]).astype(bf16)


def hidden_of(attended, shared, rows, gain):
    return pl.pallas_call(
        hidden_kernel,
        out_shape=[
            jax.ShapeDtypeStruct((TOK, WIDTH), f32),
            jax.ShapeDtypeStruct((TOK, WIDTH), bf16),
        ],
        compiler_params=pltpu.CompilerParams(vmem_limit_bytes=VMEM_LIMIT),
        cost_estimate=pl.CostEstimate(
            flops=2 * TOK * WIDTH * WIDTH, bytes_accessed=5 << 20, transcendentals=0
        ),
    )(attended, shared, rows, gain)


def hidden_back_kernel(
    t0, t1, t2, t3, crossed, hidden_ref, normed_ref, chosen_ref, router_ref, g_ref, gain_ref,
    w_ref, hidden_grad_ref, branch_ref, logit_ref, scaled_ref, att_ref
):
    chosen = chosen_ref[...] > 0
    logits = lax.dot_general(router_ref[...], normed_ref[...], NT, preferred_element_type=f32)
    peak = jnp.max(jnp.where(chosen, logits, masked_score), axis=0, keepdims=True)
    raised = jnp.where(chosen, jnp.exp(jnp.minimum(logits - peak, 0.0)), 0.0)
    gates = raised / jnp.sum(raised, axis=0, keepdims=True)
    summed = t0[...].astype(f32)
    for term in (t1, t2, t3, crossed):
        summed = summed + term[...].astype(f32)
    gate_grad = summed[TOK:, :TOK] + summed[TOK:, 256 : 256 + TOK]
    logit_grad = gates * (gate_grad - jnp.sum(gates * gate_grad, axis=0, keepdims=True))
    logit_grad = logit_grad.astype(bf16)
    logit_ref[...] = logit_grad
    normed_grad = summed[:TOK] + lax.dot_general(
        logit_grad, router_ref[...], TN, preferred_element_type=f32
    )
    hidden = hidden_ref[...]
    scale = inverse_rms(hidden)
    scaled_ref[...] = (normed_grad * hidden * scale).astype(bf16)
    hidden_grad = g_ref[...].astype(f32) + rms_pull(hidden, scale, gain_ref[...], normed_grad)
    hidden_grad_ref[...] = hidden_grad
    branch = hidden_grad.astype(bf16)
    branch_ref[...] = branch
    att = lax.dot_general(w_ref[:, :WIDTH], branch, NT, preferred_element_type=f32)
    att_ref[...] = att.astype(bf16).reshape(HEADS, HEAD_DIM, TOK)


def hidden_back(terms, crossed, hidden, normed, chosen, router_t, g, gain, shared):
    wide = lambda t: jax.ShapeDtypeStruct((TOK, WIDTH), t)
    return pl.pallas_call(
        hidden_back_kernel,
        out_shape=[
            wide(f32),
            wide(bf16),
            jax.ShapeDtypeStruct((EXPERTS, TOK), bf16),
            wide(bf16),
            jax.ShapeDtypeStruct((HEADS, HEAD_DIM, TOK), bf16),
        ],
        compiler_params=pltpu.CompilerParams(vmem_limit_bytes=VMEM_LIMIT),
        cost_estimate=pl.CostEstimate(
            flops=2 * TOK * WIDTH * WIDTH, bytes_accessed=8 << 20, transcendentals=0
        ),
    )(*terms, crossed, hidden, normed, chosen, router_t, g, gain, shared)


def shared_grads_kernel(att_ref, branch_ref, normed_ref, logit_ref, scaled_ref, out_ref):
    over_tokens = (((0,), (1,)), ((), ()))
    logit = jnp.concatenate([logit_ref[...], jnp.zeros((96, TOK), bf16)], axis=0)
    ones = (lax.broadcasted_iota(i32, (128, TOK), 0) == EXPERTS).astype(f32).astype(bf16)
    att = att_ref[...].reshape(WIDTH, TOK)
    grads = [
        jnp.dot(att, branch_ref[...], preferred_element_type=f32),
        lax.dot_general(normed_ref[...], logit, over_tokens, preferred_element_type=f32)
        + lax.dot_general(scaled_ref[...], ones, over_tokens, preferred_element_type=f32),
    ]
    for w in range(8):
        for part, at in zip(grads, (slice(0, WIDTH), slice(WIDTH, None))):
            rows = [part[s * 64 + w * 8 : s * 64 + w * 8 + 8] for s in range(16)]
            out_ref[w, :, at] = jnp.concatenate(rows, axis=0).astype(bf16)


def shared_weight_grads(att, branch, normed, logit_grad, scaled):
    return pl.pallas_call(
        shared_grads_kernel,
        out_shape=jax.ShapeDtypeStruct((8, 128, 1152), bf16),
        compiler_params=pltpu.CompilerParams(vmem_limit_bytes=VMEM_LIMIT),
        cost_estimate=pl.CostEstimate(
            flops=2 * TOK * WIDTH * 1280, bytes_accessed=5 << 20, transcendentals=0
        ),
    )(att, branch, normed, logit_grad, scaled)


def local(
    tokens,
    routes,
    cont_lengths,
    norm_attn,
    w_qkv,
    w_out,
    w_router,
    norm_ffn,
    w_gate_up,
    w_down,
    cotangent,
):
    seq_index = lax.axis_index("seq")
    places, blocks = relative_places(seq_index)
    rows = tokens[0]
    query_width = HEADS * HEAD_DIM
    kv_width = KV_HEADS * HEAD_DIM

    position, begin = group_layout(cont_lengths[0])
    begin = begin[None]
    table = rotary_table(position.astype(f32))
    kv_heads = lambda start: jnp.repeat(
        w_qkv[:, start : start + kv_width].reshape(8, KV_HEADS, HEAD_DIM), 2, axis=1
    )
    head_cols = jnp.concatenate(
        [
            w_qkv[:, :query_width].reshape(8, HEADS, HEAD_DIM),
            kv_heads(query_width),
            kv_heads(query_width + kv_width),
            jnp.broadcast_to(norm_attn[:, None, None], (8, HEADS, HEAD_DIM)),
        ],
        axis=2,
    ).transpose(1, 0, 2)
    head_cols = jnp.broadcast_to(head_cols[:, None], (HEADS, 8, 8, 256)).reshape(128, 8, 256)
    head_weights = lax.all_to_all(head_cols, BOTH, 0, 0, tiled=True).reshape(WIDTH, 256)
    gain_attn = head_weights[:, 192].astype(f32)[None]
    head_weights = jnp.where(jnp.arange(256)[None] < 192, head_weights, 0.0).astype(bf16)

    rows_near, rows_across = gather_near(rows)
    rows_near, _, table, head_weights = tie(rows_near, rows_across, table, head_weights)
    rows_near, rows_far = both_cores(rows_near), gather_far(rows_across)

    own_x = lax.axis_index("wshard") % 2
    expert_rows = jnp.concatenate([w_gate_up, w_down], axis=1)
    along_y = lambda t: lax.all_gather(t, "wshard", axis_index_groups=ALONG_Y, axis=0)
    experts, expert_rows = along_y(expert_rows), swap_x(expert_rows)

    qkv = project(places[:8], rows_near, head_weights, gain_attn, table, ())
    shared = jnp.concatenate(
        [w_out, w_router, norm_ffn[:, None], jnp.zeros((8, 95), bf16)], axis=1
    )
    shared, qkv = tie(shared, qkv)
    shared = lax.all_to_all(
        jnp.broadcast_to(shared[None], (128, 8, 1152)), BOTH, 0, 0, tiled=True
    ).reshape(WIDTH, 1152)
    routes_rows = jnp.pad(routes[0].T.astype(bf16), ((0, 8), (0, WIDTH - TOK)))
    upstream_rows = jnp.concatenate([cotangent[0], routes_rows], axis=0)
    rows_far, qkv, upstream_rows, expert_rows = tie(rows_far, qkv, upstream_rows, expert_rows)
    experts = [experts, along_y(expert_rows)]
    rows_far = both_cores(rows_far)
    grad_near = [upstream_rows] + [send(upstream_rows, 0, b) for b in (1, 3, 2)]
    qkv = project(places[8:], rows_far, head_weights, gain_attn, table, (qkv,))

    router_t = shared[:, WIDTH : WIDTH + EXPERTS].T
    gain_ffn = shared[:, WIDTH + EXPERTS].astype(f32)[None]
    attended_head, attended_t, lse = attend(qkv, begin)
    attended_head, shared = tie(attended_head, shared)
    attended = lax.all_to_all(attended_head, "seq", 0, 0, tiled=True)
    attended, grad_near = tie(attended, grad_near)
    grad_near = jnp.stack(grad_near)
    grad_far = [send(grad_near[:2], 1, 0)]
    hidden, normed_ffn = hidden_of(attended, shared, rows, gain_ffn)
    ffn_near, ffn_across = gather_near(normed_ffn)
    grad_near_mine, _ = tie(grad_near, ffn_across)
    ffn_near, _, grad_far[0] = tie(ffn_near, ffn_across, grad_far[0])
    grad_far.append(send(grad_near_mine[2:], 1, 0))
    grad_near = (grad_near, swap_cores(grad_near))
    ffn_near, ffn_far = both_cores(ffn_near), gather_far(ffn_across)
    own = jnp.stack([seq_index * 2, own_x])
    near = run_experts(0, own, ffn_near, grad_near, experts, router_t, ())
    near_terms = sum_along_z(*near[:2])
    ffn_far = both_cores(ffn_far)
    grad_far = jnp.concatenate(grad_far, axis=0)
    grad_far = (grad_far, swap_cores(grad_far))
    far = run_experts(1, own, ffn_far, grad_far, experts, router_t, near[2:])
    far, near_terms = tie(far, near_terms)
    moved, saved = far[2:4], far[4:]
    far_other, moved_other = tie(swap_cores(far[1]), moved[1])
    far_terms = send_along_z(chip_parts(far[0], far_other))
    expert_grads = expert_weight_grads(*saved)
    moved_other = swap_cores(moved_other)
    far_terms, expert_grads, moved_other = tie(far_terms, expert_grads, moved_other)
    crossed = send(add_low(*far_terms), 1, 0)
    by_x = [t.reshape(2, 4, TOK, WIDTH) for t in (moved[0], moved_other)]
    moved_parts = [add_low(by_x[0][:, i], by_x[1][:, i]) for i in range(4)]
    crossed, moved_parts = tie(crossed, moved_parts)

    expert_range = jnp.arange(EXPERTS, dtype=i32)
    chosen_here = jnp.any(routes[0].T[None] == expert_range[:, None, None], axis=1).astype(f32)
    hidden_grad, branch_grad, logit_grad, scaled_grad, attended_grad = hidden_back(
        near_terms, crossed, hidden, normed_ffn, chosen_here, router_t, cotangent[0], gain_ffn, shared
    )
    expert_grads = lax.psum_scatter(
        expert_grads.reshape(8, 2, 192, 1024),
        "wshard",
        axis_index_groups=ALONG_Y,
        scatter_dimension=0,
        tiled=True,
    )
    head_grad = lax.all_to_all(attended_grad, "seq", 0, 0, tiled=True)
    shared_grads = shared_weight_grads(attended, branch_grad, normed_ffn, logit_grad, scaled_grad)
    head_grad, shared_grads, moved_parts = tie(head_grad, shared_grads, moved_parts)
    moved_terms = [moved_parts[0]] + [
        send(moved_parts[i], 0, -b) for i, b in ((1, 1), (2, 3), (3, 2))
    ]

    shared_grads = lax.all_to_all(shared_grads, "wshard", 0, 0, tiled=True)
    projected_grad = attend_back(qkv, head_grad, attended_t, lse, begin, table)
    far_part = project_back(places[8:], projected_grad, head_weights)
    far_parts = chip_parts(far_part[0], swap_cores(far_part[1]))
    near_part = project_back(places[:8], projected_grad, head_weights)
    near_part, expert_grads, shared_grads, moved_terms = tie(
        near_part, expert_grads, shared_grads, moved_terms
    )
    near_parts = chip_parts(near_part[0], swap_cores(near_part[1]))
    far_parts, near_parts, projected_grad, shared_grads, moved_terms = tie(
        far_parts, near_parts, projected_grad, shared_grads, moved_terms
    )
    far_terms = send_along_z(far_parts)
    moved_crossed = send(add_low(*[t[1] for t in moved_terms]), 1, 0)
    shared_grads = jnp.sum(shared_grads.astype(f32), axis=0).astype(bf16).reshape(16, 8, 1152)
    shared_grads = lax.all_to_all(shared_grads, "seq", 0, 0, tiled=True)
    grad_head = head_weight_grad(places, rows_near, rows_far, gain_attn, projected_grad)
    near_terms = send_along_z(near_parts)
    far_terms, grad_head, expert_grads = tie(far_terms, grad_head, expert_grads)
    grad_heads = lax.all_to_all(grad_head.reshape(128, 8, 256), BOTH, 0, 0, tiled=True)
    crossed = send(add_low(*far_terms), 1, 0)
    crossed, near_terms, grad_heads, shared_grads = tie(
        crossed, near_terms, grad_heads, shared_grads
    )
    kept = lax.dynamic_index_in_dim(expert_grads, own_x, 0, keepdims=False)
    sent = lax.dynamic_index_in_dim(expert_grads, 1 - own_x, 0, keepdims=False)
    expert_grads = kept.astype(f32) + swap_x(sent).astype(f32)
    total = lambda terms: sum([t.astype(f32) for t in terms])
    output = (hidden + total([t[0] for t in moved_terms] + [moved_crossed])).astype(bf16)
    normed_grad = total(near_terms + [crossed])
    shared_grads = jnp.sum(shared_grads.astype(f32), axis=0)
    grad_heads = jnp.sum(grad_heads.reshape(16, 8, 8, 256).astype(f32), axis=1).transpose(1, 0, 2)
    kv_sum = lambda start: jnp.sum(
        grad_heads[:, :, start : start + HEAD_DIM].reshape(8, KV_HEADS, 2, HEAD_DIM), axis=2
    ).reshape(8, kv_width)
    grad_qkv = jnp.concatenate(
        [grad_heads[:, :, :HEAD_DIM].reshape(8, query_width), kv_sum(HEAD_DIM), kv_sum(2 * HEAD_DIM)],
        axis=1,
    )
    grad_norm_attn = jnp.sum(grad_qkv * w_qkv.astype(f32), axis=1) / norm_attn.astype(f32)
    inputs = rows.astype(f32)
    grad_input = hidden_grad + rms_pull(inputs, inverse_rms(inputs), gain_attn, normed_grad)
    return (
        output[None],
        grad_input[None],
        grad_norm_attn,
        grad_qkv,
        shared_grads[:, :WIDTH],
        shared_grads[:, WIDTH : WIDTH + EXPERTS],
        shared_grads[:, WIDTH + EXPERTS],
        expert_grads[:, :128],
        expert_grads[:, 128:],
    )


def solution(mesh):
    return jax.shard_map(
        local,
        mesh=mesh,
        in_specs=(
            P("wshard", "seq", None),
            P("wshard", "seq", None),
            P("wshard", None),
            P(BOTH),
            P(BOTH, None),
            P(BOTH, None),
            P(BOTH, None),
            P(BOTH),
            P("seq", "wshard", None),
            P("seq", "wshard", None),
            P("wshard", "seq", None),
        ),
        out_specs=(
            P("wshard", "seq", None),
            P("wshard", "seq", None),
            P(BOTH),
            P(BOTH, None),
            P(BOTH, None),
            P(BOTH, None),
            P(BOTH),
            P("seq", "wshard", None),
            P("seq", "wshard", None),
        ),
        check_vma=False,
    )
```

```python
import jax
import jax.numpy as jnp
from jax import lax
from jax.experimental import pallas as pl
from jax.experimental.pallas import tpu as pltpu
from jax.sharding import PartitionSpec as P

HEADS = 16
KV_HEADS = 8
HEAD_DIM = 64
EXPERTS = 32
FF = 512
PROMPT = 2048
GROUP = 3584
TOK = 224
WIDTH = 1024
SLOTS = 72
STEP_ROWS = 4 * SLOTS
ALL_ROWS = 16 * SLOTS
BLOCK = 512
VMEM_LIMIT = 60 << 20
LAST = TOK + 16
PAY = TOK + 32

norm_eps = 1e-06
rope_base = 10000.0
masked_score = -1e30
BOTH = ("seq", "wshard")
NT = (((1,), (1,)), ((), ()))
TN = (((0,), (0,)), ((), ()))
f32 = jnp.float32
bf16 = jnp.bfloat16
i32 = jnp.int32


def place_of(x, z, core):
    return x * 8 + z * 2 + core


def shift_perm(a, b):
    return [
        (place_of(x, z, c), place_of(x ^ a, (z + b) % 4, c))
        for x in range(2)
        for z in range(4)
        for c in range(2)
    ]


CORE_PERM = [(i, i ^ 1) for i in range(16)]


def send(rows, a, b):
    return lax.ppermute(rows, "seq", shift_perm(a, b))


def swap_cores(rows):
    return lax.ppermute(rows, "seq", CORE_PERM)


def relative_places(seq_index):
    x, z, c = seq_index // 8, (seq_index // 2) % 4, seq_index % 2
    r = jnp.arange(16, dtype=i32)
    a, i, k = r // 8, (r // 2) % 4, r % 2
    shift = i ^ (i // 2)
    behind = (z - i) % 4
    places = (a ^ x) * 8 + ((z - shift) % 4) * 2 + (k ^ c)
    return places, (a ^ x) * 8 + (behind ^ (behind // 2)) * 2 + (k ^ c)


def gather_near(rows):
    return [rows] + [send(rows, 0, b) for b in (1, 3, 2)], send(rows, 1, 0)


def both_cores(parts):
    mine = jnp.stack(parts)
    return mine, swap_cores(mine)


def gather_far(across):
    return [across] + [send(across, 0, b) for b in (1, 3, 2)]


def add_low(*terms):
    return sum([t.astype(f32) for t in terms]).astype(bf16)


def sum_along_z(mine, other):
    return send_along_z(chip_parts(mine, swap_cores(other)))


def chip_parts(mine, got):
    return [add_low(mine[i], got[i]) for i in range(4)]


def send_along_z(parts):
    return [parts[0]] + [send(parts[i], 0, -b) for i, b in ((1, 1), (2, 3), (3, 2))]


def swap_x(rows):
    return lax.ppermute(rows, "wshard", [(w, w ^ 1) for w in range(8)])


ALONG_Y = [[y * 2 + x for y in range(4)] for x in range(2)]


def tie(*values):
    return lax.optimization_barrier(values)


def inverse_rms(values):
    return lax.rsqrt(jnp.mean(values * values, axis=-1, keepdims=True) + norm_eps)


def rms_pull(values, scale, gain, grad):
    scaled = grad * gain
    return scale * scaled - values * (scale * scale * scale) * jnp.mean(
        scaled * values, axis=-1, keepdims=True
    )


def group_layout(lengths):
    places = jnp.arange(GROUP, dtype=i32)
    ends = jnp.cumsum(lengths)
    starts = ends - lengths
    offset_in = places - PROMPT
    segment_id = jnp.sum((offset_in[:, None] >= ends[None, :]).astype(i32), axis=1)
    segment_hot = segment_id[:, None] == jnp.arange(lengths.shape[0], dtype=i32)[None, :]
    begin = jnp.sum(jnp.where(segment_hot, starts[None, :], 0), axis=1)
    inside = offset_in >= 0
    position = jnp.where(inside, PROMPT + offset_in - begin, places)
    return position, jnp.where(inside, PROMPT + begin, 0)


def rotary_table(position):
    half_dim = HEAD_DIM // 2
    inverse = rope_base ** (-((jnp.arange(2 * HEAD_DIM) % half_dim).astype(f32) * 2.0) / HEAD_DIM)
    back = jnp.where(jnp.arange(2 * HEAD_DIM) < HEAD_DIM, 0.0, 0.5 * jnp.pi).astype(f32)
    return jnp.cos(position[:, None] * inverse[None, :] - back[None, :])


def turn(values):
    half_dim = HEAD_DIM // 2
    return jnp.concatenate([-values[:, half_dim:], values[:, :half_dim]], axis=-1)


def turn_back(values):
    half_dim = HEAD_DIM // 2
    return jnp.concatenate([values[:, half_dim:], -values[:, :half_dim]], axis=-1)


def project_kernel(places, mine, other, w, gain, table, *refs):
    out = refs[-1]
    j = pl.program_id(0)

    if len(refs) > 1:

        @pl.when(j == 0)
        def _():
            out[...] = refs[0][...]

    for k, ref in enumerate((mine, other)):
        at = pl.ds(pl.multiple_of(places[2 * j + k] * TOK, TOK), TOK)
        rows = ref[0].astype(f32)
        normed = (rows * inverse_rms(rows) * gain[...]).astype(bf16)
        projected = jnp.dot(normed, w[...], preferred_element_type=f32)
        c, s = table[at, :HEAD_DIM], table[at, HEAD_DIM:]
        q, k, v = projected[:, :64], projected[:, 64:128], projected[:, 128:]
        q = (q * c + turn(q) * s).astype(bf16).astype(f32) * HEAD_DIM**-0.5
        out[at, :] = jnp.concatenate([q, k * c + turn(k) * s, v], axis=1).astype(bf16)


def project(places, gathered, w, gain, table, before):
    chip = pl.BlockSpec((1, TOK, WIDTH), lambda j, p: (j, 0, 0))
    whole = lambda *shape: pl.BlockSpec(shape, lambda j, p: (0,) * len(shape))
    return pl.pallas_call(
        project_kernel,
        grid_spec=pltpu.PrefetchScalarGridSpec(
            num_scalar_prefetch=1,
            grid=(4,),
            in_specs=[chip, chip, whole(WIDTH, 256), whole(1, WIDTH), whole(GROUP, 128)]
            + [whole(GROUP, 256)] * len(before),
            out_specs=whole(GROUP, 256),
        ),
        out_shape=jax.ShapeDtypeStruct((GROUP, 256), bf16),
        compiler_params=pltpu.CompilerParams(vmem_limit_bytes=VMEM_LIMIT),
        cost_estimate=pl.CostEstimate(
            flops=2 * 8 * TOK * WIDTH * 256, bytes_accessed=10 << 20, transcendentals=0
        ),
    )(places, *gathered, w, gain, table, *before)


def project_back_kernel(places, first, second, w, first_shared, second_shared, mine, other):
    del places
    for projected, shared, out in ((first, first_shared, mine), (second, second_shared, other)):
        out[0, :TOK, :] = lax.dot_general(
            projected[...], w[...], NT, preferred_element_type=f32
        ).astype(bf16)
        rest = jnp.concatenate([shared[:, WIDTH:], jnp.zeros((8, WIDTH - 128), f32)], axis=1)
        out[0, TOK:, :] = jnp.concatenate([shared[:, :WIDTH], rest], axis=0).astype(bf16)


def project_back(places, projected_grad, w, shared):
    chip = pl.BlockSpec((1, LAST, WIDTH), lambda j, p: (j, 0, 0))
    at = lambda k, rows, n: pl.BlockSpec((rows, n), lambda j, p: (p[2 * j + k], 0))
    part = jax.ShapeDtypeStruct((4, LAST, WIDTH), bf16)
    return pl.pallas_call(
        project_back_kernel,
        grid_spec=pltpu.PrefetchScalarGridSpec(
            num_scalar_prefetch=1,
            grid=(4,),
            in_specs=[
                at(0, TOK, 256),
                at(1, TOK, 256),
                pl.BlockSpec((WIDTH, 256), lambda j, p: (0, 0)),
                at(0, 8, 1152),
                at(1, 8, 1152),
            ],
            out_specs=[chip, chip],
        ),
        out_shape=[part, part],
        compiler_params=pltpu.CompilerParams(vmem_limit_bytes=VMEM_LIMIT),
        cost_estimate=pl.CostEstimate(
            flops=2 * 8 * TOK * WIDTH * 256, bytes_accessed=5 << 20, transcendentals=0
        ),
    )(places, projected_grad, projected_grad, w, shared, shared)


def head_grad_kernel(places, near_mine, near_other, far_mine, far_other, gain, first, second, out, total):
    del places
    j = pl.program_id(0)

    @pl.when(j == 0)
    def _():
        total[...] = jnp.zeros_like(total)

    for near, far, projected in ((near_mine, far_mine, first), (near_other, far_other, second)):
        rows = jnp.where(j < 4, near[0], far[0]).astype(f32)
        normed = (rows * inverse_rms(rows) * gain[...]).astype(bf16)
        total[...] += lax.dot_general(normed, projected[...], TN, preferred_element_type=f32)

    @pl.when(j == 7)
    def _():
        out[...] = total[...].astype(bf16)


def head_weight_grad(places, near, far, gain, projected_grad):
    near_chip = pl.BlockSpec((1, TOK, WIDTH), lambda j, p: (jnp.minimum(j, 3), 0, 0))
    far_chip = pl.BlockSpec((1, TOK, WIDTH), lambda j, p: (jnp.maximum(j - 4, 0), 0, 0))
    at = lambda k: pl.BlockSpec((TOK, 256), lambda j, p: (p[2 * j + k], 0))
    return pl.pallas_call(
        head_grad_kernel,
        grid_spec=pltpu.PrefetchScalarGridSpec(
            num_scalar_prefetch=1,
            grid=(8,),
            in_specs=[
                near_chip,
                near_chip,
                far_chip,
                far_chip,
                pl.BlockSpec((1, WIDTH), lambda j, p: (0, 0)),
                at(0),
                at(1),
            ],
            out_specs=pl.BlockSpec((WIDTH, 256), lambda j, p: (0, 0)),
            scratch_shapes=[pltpu.VMEM((WIDTH, 256), f32)],
        ),
        out_shape=jax.ShapeDtypeStruct((WIDTH, 256), bf16),
        compiler_params=pltpu.CompilerParams(vmem_limit_bytes=VMEM_LIMIT),
        cost_estimate=pl.CostEstimate(
            flops=2 * 16 * TOK * WIDTH * 256, bytes_accessed=10 << 20, transcendentals=0
        ),
    )(places, *near, *far, gain, projected_grad, projected_grad)


def tile_mask(scores, key_start, query_start, begin):
    keys = key_start + lax.broadcasted_iota(i32, scores.shape, 0)
    queries = query_start + lax.broadcasted_iota(i32, scores.shape, 1)
    return jnp.where((keys <= queries) & (keys >= begin), scores, masked_score)


def key_ranges(i):
    first = PROMPT // BLOCK
    return jnp.where(i > first, i - 1, i), jnp.minimum(i, first)


def attend_kernel(qkv_ref, begin_ref, o_ref, ot_ref, lse_ref, keys, vt):
    i = pl.program_id(0)
    here = pl.ds(pl.multiple_of(i * BLOCK, BLOCK), BLOCK)

    @pl.when(i == 0)
    def _():
        keys[...] = qkv_ref[:, 64:128]
        vt[...] = qkv_ref[:, 128:192].T

    q = qkv_ref[here, :64]
    begin = begin_ref[...]

    def tile(j, carry, masked, n=1):
        peak, total, out = carry
        start = pl.multiple_of(j * BLOCK, BLOCK)
        at = pl.ds(start, n * BLOCK)
        s = lax.dot_general(keys[at, :], q, NT, preferred_element_type=f32)
        if masked:
            s = tile_mask(s, start, i * BLOCK, begin)
        higher = jnp.maximum(peak, jnp.max(s, axis=0, keepdims=True))
        p = jnp.exp(s - higher)
        fade = jnp.exp(peak - higher)
        total = total * fade + jnp.sum(p, axis=0, keepdims=True)
        out = out * fade + jnp.dot(vt[:, at], p.astype(bf16), preferred_element_type=f32)
        return higher, total, out

    carry = (
        jnp.full((1, BLOCK), masked_score, f32),
        jnp.zeros((1, BLOCK), f32),
        jnp.zeros((HEAD_DIM, BLOCK), f32),
    )
    carry = tile(i, carry, True)
    window, shared = key_ranges(i)
    carry = lax.fori_loop(window, i, lambda j, c: tile(j, c, True), carry)
    pairs = shared // 2
    carry = lax.fori_loop(0, pairs, lambda j, c: tile(2 * j, c, False, 2), carry)
    peak, total, out = lax.fori_loop(2 * pairs, shared, lambda j, c: tile(j, c, False), carry)
    ot_ref[:, here] = out * (1.0 / total)
    lse_ref[...] = peak + jnp.log(total)

    @pl.when(i == GROUP // BLOCK - 1)
    def _():
        for b in range(16):
            o_ref[b] = ot_ref[:, b * TOK : (b + 1) * TOK].astype(bf16)


def attend(qkv, begin):
    whole = lambda *shape: pl.BlockSpec(shape, lambda i: (0,) * len(shape))
    cols = lambda n: pl.BlockSpec((n, BLOCK), lambda i: (0, i))
    return pl.pallas_call(
        attend_kernel,
        grid=(GROUP // BLOCK,),
        in_specs=[whole(GROUP, 256), cols(1)],
        out_specs=[whole(16, HEAD_DIM, TOK), whole(HEAD_DIM, GROUP), cols(1)],
        out_shape=[
            jax.ShapeDtypeStruct((16, HEAD_DIM, TOK), bf16),
            jax.ShapeDtypeStruct((HEAD_DIM, GROUP), f32),
            jax.ShapeDtypeStruct((1, GROUP), f32),
        ],
        scratch_shapes=[
            pltpu.VMEM((GROUP, HEAD_DIM), bf16),
            pltpu.VMEM((HEAD_DIM, GROUP), bf16),
        ],
        compiler_params=pltpu.CompilerParams(vmem_limit_bytes=VMEM_LIMIT),
        cost_estimate=pl.CostEstimate(
            flops=2 * 27 * BLOCK * BLOCK * 512, bytes_accessed=4 << 20, transcendentals=27 * BLOCK * BLOCK
        ),
    )(qkv, begin)


def attend_back_kernel(
    qkv_ref, g_ref, ot_ref, lse_ref, begin_ref, table, out_ref, keys, values, kt, gt, dq, dk, dv
):
    i = pl.program_id(0)
    here = pl.ds(pl.multiple_of(i * BLOCK, BLOCK), BLOCK)

    @pl.when(i == 0)
    def _():
        dk[...] = jnp.zeros_like(dk)
        dv[...] = jnp.zeros_like(dv)
        keys[...] = qkv_ref[:, 64:128]
        values[...] = qkv_ref[:, 128:192]
        kt[...] = qkv_ref[:, 64:128].T
        for b in range(16):
            gt[:, b * TOK : (b + 1) * TOK] = g_ref[b]

    q = qkv_ref[here, :64]
    g = gt[:, here]
    begin = begin_ref[...]
    lse = lse_ref[...]
    inner = jnp.sum(g.astype(f32) * ot_ref[...], axis=0, keepdims=True)

    def tile(j, dq, masked, n=1):
        start = pl.multiple_of(j * BLOCK, BLOCK)
        at = pl.ds(start, n * BLOCK)
        s = lax.dot_general(keys[at, :], q, NT, preferred_element_type=f32)
        if masked:
            s = tile_mask(s, start, i * BLOCK, begin)
        p = jnp.exp(s - lse)
        dp = jnp.dot(values[at, :], g, preferred_element_type=f32)
        ds = (p * (dp - inner)).astype(bf16)
        dv[at, :] += lax.dot_general(p.astype(bf16), g, NT, preferred_element_type=f32)
        dk[at, :] += jnp.dot(ds, q, preferred_element_type=f32)
        return dq + jnp.dot(kt[:, at], ds, preferred_element_type=f32)

    dqt = tile(i, jnp.zeros((HEAD_DIM, BLOCK), f32), True)
    window, shared = key_ranges(i)
    dqt = lax.fori_loop(window, i, lambda j, c: tile(j, c, True), dqt)
    pairs = shared // 2
    dqt = lax.fori_loop(0, pairs, lambda j, c: tile(2 * j, c, False, 2), dqt)
    dqt = lax.fori_loop(2 * pairs, shared, lambda j, c: tile(j, c, False), dqt)
    dq[here, :] = dqt.T * HEAD_DIM**-0.5

    @pl.when(i == GROUP // BLOCK - 1)
    def _():
        def back(b, _):
            at = pl.ds(pl.multiple_of(b * BLOCK, BLOCK), BLOCK)
            c, s = table[at, :HEAD_DIM], table[at, HEAD_DIM:]
            q, k = dq[at, :].astype(bf16).astype(f32), dk[at, :].astype(bf16).astype(f32)
            parts = [q * c + turn_back(q * s), k * c + turn_back(k * s), dv[at, :], jnp.zeros_like(q)]
            out_ref[at, :] = jnp.concatenate(parts, axis=1).astype(bf16)
            return 0

        lax.fori_loop(0, GROUP // BLOCK, back, 0)


def attend_back(qkv, g, ot, lse, begin, table):
    whole = lambda *shape: pl.BlockSpec(shape, lambda i: (0,) * len(shape))
    cols = lambda n: pl.BlockSpec((n, BLOCK), lambda i: (0, i))
    return pl.pallas_call(
        attend_back_kernel,
        grid=(GROUP // BLOCK,),
        in_specs=[
            whole(GROUP, 256),
            whole(16, HEAD_DIM, TOK),
            cols(HEAD_DIM),
            cols(1),
            cols(1),
            whole(GROUP, 128),
        ],
        out_specs=whole(GROUP, 256),
        out_shape=jax.ShapeDtypeStruct((GROUP, 256), bf16),
        scratch_shapes=[
            pltpu.VMEM((GROUP, HEAD_DIM), bf16),
            pltpu.VMEM((GROUP, HEAD_DIM), bf16),
            pltpu.VMEM((HEAD_DIM, GROUP), bf16),
            pltpu.VMEM((HEAD_DIM, GROUP), bf16),
            pltpu.VMEM((GROUP, HEAD_DIM), f32),
            pltpu.VMEM((GROUP, HEAD_DIM), f32),
            pltpu.VMEM((GROUP, HEAD_DIM), f32),
        ],
        compiler_params=pltpu.CompilerParams(vmem_limit_bytes=VMEM_LIMIT),
        cost_estimate=pl.CostEstimate(
            flops=5 * 27 * BLOCK * BLOCK * 512, bytes_accessed=8 << 20, transcendentals=27 * BLOCK * BLOCK
        ),
    )(qkv, g, ot, lse, begin, table)


def experts_kernel(
    own_ref, ffn_mine, ffn_other, g_mine, g_other, routes_mine, routes_other, router_ref, own_w, across_w, *refs
):
    routed_mine, routed_other, moved_mine, moved_other = refs[-10:-6]
    x_ref, dh_ref, act_ref, dy_ref, w_ref, sem = refs[-6:]
    own = own_ref[0]

    copies = [
        [
            pltpu.make_async_copy(shards.at[y, e], w_ref.at[e, 2 * y + (own_ref[1] ^ a)], sem.at[a, y, e])
            for a, shards in enumerate((own_w, across_w))
            for y in range(4)
        ]
        for e in range(2)
    ]

    @pl.when(pl.program_id(0) == 0)
    def _():
        for copy in copies[0] + copies[1]:
            copy.start()

    expert_rows = lax.broadcasted_iota(i32, (EXPERTS, TOK), 0)
    slot_rows = lax.broadcasted_iota(i32, (SLOTS, TOK), 0).astype(f32)
    upto = (
        lax.broadcasted_iota(i32, (TOK, TOK), 0) <= lax.broadcasted_iota(i32, (TOK, TOK), 1)
    ).astype(f32).astype(bf16)
    slot_cols = []
    gate_grads = [jnp.zeros((EXPERTS, WIDTH), f32) for _ in range(4)]
    payload_rows = lax.broadcasted_iota(i32, (EXPERTS, WIDTH), 0)
    gate_rows = [[], []]
    picks = [[], []]
    picked_rows = [[], []]
    picked_grads = [[], []]
    blocks = [(ffn_mine, g_mine, routes_mine, 0), (ffn_other, g_other, routes_other, 0)]
    blocks = blocks + [(*refs_of[:3], 1) for refs_of in blocks]
    for rows_ref, grads_ref, routes_ref, n in blocks:
        rows, grads = rows_ref[n], grads_ref[n]
        routes = routes_ref[n][:8, :TOK].astype(f32).astype(i32)
        chosen = expert_rows == routes[0:1]
        for j in range(1, 8):
            chosen = chosen | (expert_rows == routes[j : j + 1])
        named = [jnp.max((routes == own + e).astype(f32), axis=0, keepdims=True) for e in range(2)]
        named = jnp.concatenate(named + [jnp.zeros((6, TOK), f32)], axis=0)
        rank = jnp.dot(named.astype(bf16), upto, preferred_element_type=f32)
        slots = jnp.where(named > 0, rank - 1.0, -1.0)
        slot_cols.append(slots.T)
        logits = lax.dot_general(router_ref[...], rows, NT, preferred_element_type=f32)
        peak = jnp.max(jnp.where(chosen, logits, masked_score), axis=0, keepdims=True)
        raised = jnp.where(chosen, jnp.exp(jnp.minimum(logits - peak, 0.0)), 0.0)
        gates = raised / jnp.sum(raised, axis=0, keepdims=True)
        for e in range(2):
            gate_rows[e].append(
                jnp.sum(jnp.where(expert_rows == own + e, gates, 0.0), axis=0, keepdims=True)
            )
            picks[e].append((slots[e : e + 1] == slot_rows).astype(f32))
        low = jnp.concatenate([picks[0][-1], picks[1][-1]], axis=0).astype(bf16)
        for source, kept in ((rows, picked_rows), (grads, picked_grads)):
            both = jnp.dot(low, source, preferred_element_type=f32)
            kept[0].append(both[:SLOTS])
            kept[1].append(both[SLOTS:])
    moved, routed = [], []
    for e in range(2):

        @pl.when(pl.program_id(0) == 0)
        def _():
            for copy in copies[e]:
                copy.wait()

        w_gate_up = w_ref[e, :, :128, :].reshape(WIDTH, 2 * FF)
        w_down = w_ref[e, :, 128:, :].reshape(FF, WIDTH)
        x = jnp.concatenate(picked_rows[e], axis=0).astype(bf16)
        gate = jnp.concatenate(
            [jnp.sum(p * r, axis=1, keepdims=True) for p, r in zip(picks[e], gate_rows[e])], axis=0
        )
        grads = jnp.concatenate(picked_grads[e], axis=0)
        dy = (gate * grads).astype(bf16)
        mixed = jnp.dot(x, w_gate_up, preferred_element_type=f32)
        dact = lax.dot_general(dy, w_down, NT, preferred_element_type=f32)
        gate_part, up_part = mixed[:, :FF], mixed[:, FF:]
        sigma = 1.0 / (1.0 + jnp.exp(-gate_part))
        silu = gate_part * sigma
        act = (silu * up_part).astype(bf16)
        dh = jnp.concatenate(
            [dact * up_part * (sigma + silu * (1.0 - sigma)), dact * silu], axis=1
        ).astype(bf16)
        x_ref[e] = x
        dy_ref[e] = dy
        act_ref[e] = act
        dh_ref[e] = dh
        returned = jnp.dot(act, w_down, preferred_element_type=f32).astype(bf16).astype(f32)
        dgate = jnp.sum(returned * grads, axis=1, keepdims=True)
        for b in range(4):
            grad = jnp.sum(
                picks[e][b] * dgate[b * SLOTS : (b + 1) * SLOTS], axis=0, keepdims=True
            )
            high = grad.astype(bf16).astype(f32)
            gap = jnp.zeros((1, 256 - TOK), f32)
            wide = jnp.concatenate([high, gap, grad - high, gap, jnp.zeros((1, WIDTH - 512), f32)], axis=1)
            gate_grads[b] = gate_grads[b] + jnp.where(payload_rows == own + e, wide, 0.0)
        moved.append(gate * returned)
        routed.append(lax.dot_general(dh, w_gate_up, NT, preferred_element_type=f32))
    columns = lax.broadcasted_iota(i32, (TOK, 2 * SLOTS), 1).astype(f32)
    outs = [(routed_mine, moved_mine, 0), (routed_other, moved_other, 0), (routed_mine, moved_mine, 1), (routed_other, moved_other, 1)]
    for b, (routed_ref, moved_ref, n) in enumerate(outs):
        first, second = slot_cols[b][:, 0:1], slot_cols[b][:, 1:2]
        back = ((columns == first) | ((columns == second + SLOTS) & (second >= 0))).astype(f32).astype(bf16)
        at = slice(b * SLOTS, (b + 1) * SLOTS)
        for terms, ref in ((routed, routed_ref), (moved, moved_ref)):
            joined = jnp.concatenate([terms[0][at], terms[1][at]], axis=0).astype(bf16)
            ref[n, :TOK, :] = jnp.dot(back, joined, preferred_element_type=f32).astype(bf16)
        routed_ref[n, TOK:, :] = gate_grads[b].astype(bf16)


def run_experts(half, own, ffn, grads, weights, router, before):
    pair = pl.BlockSpec((2, TOK, WIDTH), lambda i, o: (i, 0, 0))
    pair_of_all = pl.BlockSpec((2, TOK, WIDTH), lambda i, o: (i + 2 * half, 0, 0))
    whole = lambda shape: pl.BlockSpec(shape, lambda i, o: (0,) * len(shape))
    routes = pl.BlockSpec((2, 16, 256), lambda i, o: (i, TOK // 16, 0))
    summed = pl.BlockSpec((2, PAY, WIDTH), lambda i, o: (i, 0, 0))
    kept = lambda n: pl.BlockSpec((2, STEP_ROWS, n), lambda i, o: (0, i + 2 * half, 0))
    part = jax.ShapeDtypeStruct((4, PAY, WIDTH), bf16)
    keep = lambda n: jax.ShapeDtypeStruct((2, ALL_ROWS, n), bf16)
    return pl.pallas_call(
        experts_kernel,
        grid_spec=pltpu.PrefetchScalarGridSpec(
            num_scalar_prefetch=1,
            grid=(2,),
            in_specs=[
                pair,
                pair,
                pair,
                pair,
                routes,
                routes,
                whole((EXPERTS, WIDTH)),
            ]
            + [pl.BlockSpec(memory_space=pl.ANY)] * (2 + len(before)),
            out_specs=[
                summed,
                summed,
                pair_of_all,
                pair_of_all,
                kept(WIDTH),
                kept(2 * FF),
                kept(FF),
                kept(WIDTH),
            ],
            scratch_shapes=[
                pltpu.VMEM((2, 8, 192, 1024), bf16),
                pltpu.SemaphoreType.DMA((2, 4, 2)),
            ],
        ),
        out_shape=[
            part,
            part,
            jax.ShapeDtypeStruct((8, TOK, WIDTH), bf16),
            jax.ShapeDtypeStruct((8, TOK, WIDTH), bf16),
            keep(WIDTH),
            keep(2 * FF),
            keep(FF),
            keep(WIDTH),
        ],
        input_output_aliases={10 + i: 2 + i for i in range(len(before))},
        compiler_params=pltpu.CompilerParams(vmem_limit_bytes=VMEM_LIMIT),
        cost_estimate=pl.CostEstimate(
            flops=14 << 30, bytes_accessed=24 << 20, transcendentals=8 * SLOTS * 2 * FF
        ),
    )(own, *ffn, *grads, *grads, router, *weights, *before)


def expert_grads_kernel(x_ref, dh_ref, act_ref, dy_ref, out_ref):
    up = lax.dot_general(x_ref[0], dh_ref[0], TN, preferred_element_type=f32)
    down = lax.dot_general(act_ref[0], dy_ref[0], TN, preferred_element_type=f32)
    out_ref[0, :, 0, :128, :] = up.astype(bf16).reshape(2, 128, 2 * FF)
    out_ref[0, :, 0, 128:, :] = down.astype(bf16).reshape(2, 64, WIDTH)


def expert_weight_grads(x, dh, act, dy):
    return pl.pallas_call(
        expert_grads_kernel,
        grid=(2, 4),
        in_specs=[
            pl.BlockSpec((1, ALL_ROWS, 256), lambda e, i: (e, 0, i)),
            pl.BlockSpec((1, ALL_ROWS, 2 * FF), lambda e, i: (e, 0, 0)),
            pl.BlockSpec((1, ALL_ROWS, 128), lambda e, i: (e, 0, i)),
            pl.BlockSpec((1, ALL_ROWS, WIDTH), lambda e, i: (e, 0, 0)),
        ],
        out_specs=pl.BlockSpec((1, 2, 1, 192, 1024), lambda e, i: (i, 0, e, 0, 0)),
        out_shape=jax.ShapeDtypeStruct((4, 2, 2, 192, 1024), bf16),
        compiler_params=pltpu.CompilerParams(vmem_limit_bytes=VMEM_LIMIT),
        cost_estimate=pl.CostEstimate(flops=8 << 30, bytes_accessed=14 << 20, transcendentals=0),
    )(x, dh, act, dy)


def hidden_kernel(att_ref, w_ref, rows_ref, gain_ref, hidden_ref, normed_ref):
    att = att_ref[...].reshape(WIDTH, TOK)
    hidden = rows_ref[...].astype(f32) + lax.dot_general(
        att, w_ref[:, :WIDTH], TN, preferred_element_type=f32
    )
    hidden_ref[...] = hidden
    normed_ref[...] = (hidden * inverse_rms(hidden) * gain_ref[...]).astype(bf16)


def hidden_of(attended, shared, rows, gain):
    return pl.pallas_call(
        hidden_kernel,
        out_shape=[
            jax.ShapeDtypeStruct((TOK, WIDTH), f32),
            jax.ShapeDtypeStruct((TOK, WIDTH), bf16),
        ],
        compiler_params=pltpu.CompilerParams(vmem_limit_bytes=VMEM_LIMIT),
        cost_estimate=pl.CostEstimate(
            flops=2 * TOK * WIDTH * WIDTH, bytes_accessed=5 << 20, transcendentals=0
        ),
    )(attended, shared, rows, gain)


def hidden_back_kernel(
    t0, t1, t2, t3, crossed, hidden_ref, normed_ref, chosen_ref, router_ref, g_ref, gain_ref,
    w_ref, hidden_grad_ref, branch_ref, logit_ref, scaled_ref, att_ref
):
    chosen = chosen_ref[...] > 0
    logits = lax.dot_general(router_ref[...], normed_ref[...], NT, preferred_element_type=f32)
    peak = jnp.max(jnp.where(chosen, logits, masked_score), axis=0, keepdims=True)
    raised = jnp.where(chosen, jnp.exp(jnp.minimum(logits - peak, 0.0)), 0.0)
    gates = raised / jnp.sum(raised, axis=0, keepdims=True)
    summed = t0[...].astype(f32)
    for term in (t1, t2, t3, crossed):
        summed = summed + term[...].astype(f32)
    gate_grad = summed[TOK:, :TOK] + summed[TOK:, 256 : 256 + TOK]
    logit_grad = gates * (gate_grad - jnp.sum(gates * gate_grad, axis=0, keepdims=True))
    logit_grad = logit_grad.astype(bf16)
    logit_ref[...] = logit_grad
    normed_grad = summed[:TOK] + lax.dot_general(
        logit_grad, router_ref[...], TN, preferred_element_type=f32
    )
    hidden = hidden_ref[...]
    scale = inverse_rms(hidden)
    scaled_ref[...] = (normed_grad * hidden * scale).astype(bf16)
    hidden_grad = g_ref[...].astype(f32) + rms_pull(hidden, scale, gain_ref[...], normed_grad)
    hidden_grad_ref[...] = hidden_grad
    branch = hidden_grad.astype(bf16)
    branch_ref[...] = branch
    att = lax.dot_general(w_ref[:, :WIDTH], branch, NT, preferred_element_type=f32)
    att_ref[...] = att.astype(bf16).reshape(HEADS, HEAD_DIM, TOK)


def hidden_back(terms, crossed, hidden, normed, chosen, router_t, g, gain, shared):
    wide = lambda t: jax.ShapeDtypeStruct((TOK, WIDTH), t)
    return pl.pallas_call(
        hidden_back_kernel,
        out_shape=[
            wide(f32),
            wide(bf16),
            jax.ShapeDtypeStruct((EXPERTS, TOK), bf16),
            wide(bf16),
            jax.ShapeDtypeStruct((HEADS, HEAD_DIM, TOK), bf16),
        ],
        compiler_params=pltpu.CompilerParams(vmem_limit_bytes=VMEM_LIMIT),
        cost_estimate=pl.CostEstimate(
            flops=2 * TOK * WIDTH * WIDTH, bytes_accessed=8 << 20, transcendentals=0
        ),
    )(*terms, crossed, hidden, normed, chosen, router_t, g, gain, shared)


def shared_grads_kernel(att_ref, branch_ref, normed_ref, logit_ref, scaled_ref, out_ref):
    over_tokens = (((0,), (1,)), ((), ()))
    logit = jnp.concatenate([logit_ref[...], jnp.zeros((96, TOK), bf16)], axis=0)
    ones = (lax.broadcasted_iota(i32, (128, TOK), 0) == EXPERTS).astype(f32).astype(bf16)
    att = att_ref[...].reshape(WIDTH, TOK)
    grads = [
        jnp.dot(att, branch_ref[...], preferred_element_type=f32),
        lax.dot_general(normed_ref[...], logit, over_tokens, preferred_element_type=f32)
        + lax.dot_general(scaled_ref[...], ones, over_tokens, preferred_element_type=f32),
    ]
    for w in range(8):
        for part, at in zip(grads, (slice(0, WIDTH), slice(WIDTH, None))):
            rows = [part[s * 64 + w * 8 : s * 64 + w * 8 + 8] for s in range(16)]
            out_ref[w, :, at] = jnp.concatenate(rows, axis=0).astype(bf16)


def shared_weight_grads(att, branch, normed, logit_grad, scaled):
    return pl.pallas_call(
        shared_grads_kernel,
        out_shape=jax.ShapeDtypeStruct((8, 128, 1152), bf16),
        compiler_params=pltpu.CompilerParams(vmem_limit_bytes=VMEM_LIMIT),
        cost_estimate=pl.CostEstimate(
            flops=2 * TOK * WIDTH * 1280, bytes_accessed=5 << 20, transcendentals=0
        ),
    )(att, branch, normed, logit_grad, scaled)


def local(
    tokens,
    routes,
    cont_lengths,
    norm_attn,
    w_qkv,
    w_out,
    w_router,
    norm_ffn,
    w_gate_up,
    w_down,
    cotangent,
):
    seq_index = lax.axis_index("seq")
    places, blocks = relative_places(seq_index)
    rows = tokens[0]
    query_width = HEADS * HEAD_DIM
    kv_width = KV_HEADS * HEAD_DIM

    position, begin = group_layout(cont_lengths[0])
    begin = begin[None]
    table = rotary_table(position.astype(f32))
    kv_heads = lambda start: jnp.repeat(
        w_qkv[:, start : start + kv_width].reshape(8, KV_HEADS, HEAD_DIM), 2, axis=1
    )
    head_cols = jnp.concatenate(
        [
            w_qkv[:, :query_width].reshape(8, HEADS, HEAD_DIM),
            kv_heads(query_width),
            kv_heads(query_width + kv_width),
            jnp.broadcast_to(norm_attn[:, None, None], (8, HEADS, HEAD_DIM)),
        ],
        axis=2,
    ).transpose(1, 0, 2)
    head_cols = jnp.broadcast_to(head_cols[:, None], (HEADS, 8, 8, 256)).reshape(128, 8, 256)
    head_weights = lax.all_to_all(head_cols, BOTH, 0, 0, tiled=True).reshape(WIDTH, 256)
    gain_attn = head_weights[:, 192].astype(f32)[None]
    head_weights = jnp.where(jnp.arange(256)[None] < 192, head_weights, 0.0).astype(bf16)

    rows_near, rows_across = gather_near(rows)
    rows_near, _, table, head_weights = tie(rows_near, rows_across, table, head_weights)
    rows_near, rows_far = both_cores(rows_near), gather_far(rows_across)

    own_x = lax.axis_index("wshard") % 2
    expert_rows = jnp.concatenate([w_gate_up, w_down], axis=1)
    along_y = lambda t: lax.all_gather(t, "wshard", axis_index_groups=ALONG_Y, axis=0)
    experts, expert_rows = along_y(expert_rows), swap_x(expert_rows)

    qkv = project(places[:8], rows_near, head_weights, gain_attn, table, ())
    shared = jnp.concatenate(
        [w_out, w_router, norm_ffn[:, None], jnp.zeros((8, 95), bf16)], axis=1
    )
    shared, qkv = tie(shared, qkv)
    shared = lax.all_to_all(
        jnp.broadcast_to(shared[None], (128, 8, 1152)), BOTH, 0, 0, tiled=True
    ).reshape(WIDTH, 1152)
    routes_rows = jnp.pad(routes[0].T.astype(bf16), ((0, 8), (0, WIDTH - TOK)))
    upstream_rows = jnp.concatenate([cotangent[0], routes_rows], axis=0)
    rows_far, qkv, upstream_rows, expert_rows = tie(rows_far, qkv, upstream_rows, expert_rows)
    experts = [experts, along_y(expert_rows)]
    rows_far = both_cores(rows_far)
    grad_near = [upstream_rows] + [send(upstream_rows, 0, b) for b in (1, 3, 2)]
    qkv = project(places[8:], rows_far, head_weights, gain_attn, table, (qkv,))

    router_t = shared[:, WIDTH : WIDTH + EXPERTS].T
    gain_ffn = shared[:, WIDTH + EXPERTS].astype(f32)[None]
    attended_head, attended_t, lse = attend(qkv, begin)
    attended_head, shared = tie(attended_head, shared)
    attended = lax.all_to_all(attended_head, "seq", 0, 0, tiled=True)
    attended, grad_near = tie(attended, grad_near)
    grad_near = jnp.stack(grad_near)
    grad_far = [send(grad_near[:2], 1, 0)]
    hidden, normed_ffn = hidden_of(attended, shared, rows, gain_ffn)
    ffn_near, ffn_across = gather_near(normed_ffn)
    grad_near_mine, _ = tie(grad_near, ffn_across)
    ffn_near, _, grad_far[0] = tie(ffn_near, ffn_across, grad_far[0])
    grad_far.append(send(grad_near_mine[2:], 1, 0))
    grad_near = (grad_near, swap_cores(grad_near))
    ffn_near, ffn_far = both_cores(ffn_near), gather_far(ffn_across)
    own = jnp.stack([seq_index * 2, own_x])
    near = run_experts(0, own, ffn_near, grad_near, experts, router_t, ())
    near_terms = sum_along_z(*near[:2])
    ffn_far = both_cores(ffn_far)
    grad_far = jnp.concatenate(grad_far, axis=0)
    grad_far = (grad_far, swap_cores(grad_far))
    far = run_experts(1, own, ffn_far, grad_far, experts, router_t, near[2:])
    far, near_terms = tie(far, near_terms)
    moved, saved = far[2:4], far[4:]
    far_other, moved_other = tie(swap_cores(far[1]), moved[1])
    far_terms = send_along_z(chip_parts(far[0], far_other))
    expert_grads = expert_weight_grads(*saved)
    moved_other = swap_cores(moved_other)
    far_terms, expert_grads, moved_other = tie(far_terms, expert_grads, moved_other)
    crossed = send(add_low(*far_terms), 1, 0)
    by_x = [t.reshape(2, 4, TOK, WIDTH) for t in (moved[0], moved_other)]
    moved_parts = [add_low(by_x[0][:, i], by_x[1][:, i]) for i in range(4)]
    crossed, moved_parts = tie(crossed, moved_parts)

    expert_range = jnp.arange(EXPERTS, dtype=i32)
    chosen_here = jnp.any(routes[0].T[None] == expert_range[:, None, None], axis=1).astype(f32)
    hidden_grad, branch_grad, logit_grad, scaled_grad, attended_grad = hidden_back(
        near_terms, crossed, hidden, normed_ffn, chosen_here, router_t, cotangent[0], gain_ffn, shared
    )
    expert_grads = lax.psum_scatter(
        expert_grads.reshape(8, 2, 192, 1024),
        "wshard",
        axis_index_groups=ALONG_Y,
        scatter_dimension=0,
        tiled=True,
    )
    head_grad = lax.all_to_all(attended_grad, "seq", 0, 0, tiled=True)
    shared_grads = shared_weight_grads(attended, branch_grad, normed_ffn, logit_grad, scaled_grad)
    head_grad, shared_grads, moved_parts = tie(head_grad, shared_grads, moved_parts)
    moved_terms = [moved_parts[0]] + [
        send(moved_parts[i], 0, -b) for i, b in ((1, 1), (2, 3), (3, 2))
    ]

    shared_grads = lax.all_to_all(shared_grads, "wshard", 0, 0, tiled=True)
    projected_grad = attend_back(qkv, head_grad, attended_t, lse, begin, table)
    shared_grads = jnp.sum(shared_grads.astype(f32), axis=0)
    far_part = project_back(places[8:], projected_grad, head_weights, shared_grads)
    near_part = project_back(places[:8], projected_grad, head_weights, shared_grads)
    far_parts = chip_parts(far_part[0], swap_cores(far_part[1]))
    near_part, moved_terms, expert_grads = tie(near_part, moved_terms, expert_grads)
    near_parts = chip_parts(near_part[0], swap_cores(near_part[1]))
    far_parts, near_parts, projected_grad, moved_terms, expert_grads = tie(
        far_parts, near_parts, projected_grad, moved_terms, expert_grads
    )
    far_terms = send_along_z(far_parts)
    near_terms = send_along_z(near_parts)
    moved_crossed = send(add_low(*[t[1] for t in moved_terms]), 1, 0)
    grad_head = head_weight_grad(places, rows_near, rows_far, gain_attn, projected_grad)
    grad_heads = lax.all_to_all(grad_head.reshape(128, 8, 256), BOTH, 0, 0, tiled=True)
    crossed = send(add_low(*far_terms), 1, 0)
    crossed, near_terms, grad_heads = tie(crossed, near_terms, grad_heads)
    kept = lax.dynamic_index_in_dim(expert_grads, own_x, 0, keepdims=False)
    sent = lax.dynamic_index_in_dim(expert_grads, 1 - own_x, 0, keepdims=False)
    expert_grads = kept.astype(f32) + swap_x(sent).astype(f32)
    total = lambda terms: sum([t.astype(f32) for t in terms])
    output = (hidden + total([t[0] for t in moved_terms] + [moved_crossed])).astype(bf16)
    last_sum = total(near_terms + [crossed])
    normed_grad, shared_grads = last_sum[:TOK], last_sum[TOK:]
    grad_heads = jnp.sum(grad_heads.reshape(16, 8, 8, 256).astype(f32), axis=1).transpose(1, 0, 2)
    kv_sum = lambda start: jnp.sum(
        grad_heads[:, :, start : start + HEAD_DIM].reshape(8, KV_HEADS, 2, HEAD_DIM), axis=2
    ).reshape(8, kv_width)
    grad_qkv = jnp.concatenate(
        [grad_heads[:, :, :HEAD_DIM].reshape(8, query_width), kv_sum(HEAD_DIM), kv_sum(2 * HEAD_DIM)],
        axis=1,
    )
    grad_norm_attn = jnp.sum(grad_qkv * w_qkv.astype(f32), axis=1) / norm_attn.astype(f32)
    inputs = rows.astype(f32)
    grad_input = hidden_grad + rms_pull(inputs, inverse_rms(inputs), gain_attn, normed_grad)
    return (
        output[None],
        grad_input[None],
        grad_norm_attn,
        grad_qkv,
        shared_grads[:8],
        shared_grads[8:, :EXPERTS],
        shared_grads[8:, EXPERTS],
        expert_grads[:, :128],
        expert_grads[:, 128:],
    )


def solution(mesh):
    return jax.shard_map(
        local,
        mesh=mesh,
        in_specs=(
            P("wshard", "seq", None),
            P("wshard", "seq", None),
            P("wshard", None),
            P(BOTH),
            P(BOTH, None),
            P(BOTH, None),
            P(BOTH, None),
            P(BOTH),
            P("seq", "wshard", None),
            P("seq", "wshard", None),
            P("wshard", "seq", None),
        ),
        out_specs=(
            P("wshard", "seq", None),
            P("wshard", "seq", None),
            P(BOTH),
            P(BOTH, None),
            P(BOTH, None),
            P(BOTH, None),
            P(BOTH),
            P("seq", "wshard", None),
            P("seq", "wshard", None),
        ),
        check_vma=False,
    )
```

```python
import jax
import jax.numpy as jnp
from jax import lax
from jax.experimental import pallas as pl
from jax.experimental.pallas import tpu as pltpu
from jax.sharding import PartitionSpec as P

HEADS = 16
KV_HEADS = 8
HEAD_DIM = 64
EXPERTS = 32
FF = 512
PROMPT = 2048
GROUP = 3584
TOK = 224
WIDTH = 1024
SLOTS = 72
STEP_ROWS = 4 * SLOTS
ALL_ROWS = 16 * SLOTS
BLOCK = 512
VMEM_LIMIT = 60 << 20
LAST = TOK + 16
PAY = TOK + 32

norm_eps = 1e-06
rope_base = 10000.0
masked_score = -1e30
BOTH = ("seq", "wshard")
NT = (((1,), (1,)), ((), ()))
TN = (((0,), (0,)), ((), ()))
f32 = jnp.float32
bf16 = jnp.bfloat16
i32 = jnp.int32


def place_of(x, z, core):
    return x * 8 + z * 2 + core


def shift_perm(a, b):
    return [
        (place_of(x, z, c), place_of(x ^ a, (z + b) % 4, c))
        for x in range(2)
        for z in range(4)
        for c in range(2)
    ]


CORE_PERM = [(i, i ^ 1) for i in range(16)]


def send(rows, a, b):
    return lax.ppermute(rows, "seq", shift_perm(a, b))


def swap_cores(rows):
    return lax.ppermute(rows, "seq", CORE_PERM)


def relative_places(seq_index):
    x, z, c = seq_index // 8, (seq_index // 2) % 4, seq_index % 2
    r = jnp.arange(16, dtype=i32)
    a, i, k = r // 8, (r // 2) % 4, r % 2
    shift = i ^ (i // 2)
    behind = (z - i) % 4
    places = (a ^ x) * 8 + ((z - shift) % 4) * 2 + (k ^ c)
    return places, (a ^ x) * 8 + (behind ^ (behind // 2)) * 2 + (k ^ c)


def gather_near(rows):
    return [rows] + [send(rows, 0, b) for b in (1, 3, 2)], send(rows, 1, 0)


def both_cores(parts):
    mine = jnp.stack(parts)
    return mine, swap_cores(mine)


def gather_far(across):
    return [across] + [send(across, 0, b) for b in (1, 3, 2)]


def add_low(*terms):
    return sum([t.astype(f32) for t in terms]).astype(bf16)


def sum_along_z(mine, other):
    return send_along_z(chip_parts(mine, swap_cores(other)))


def chip_parts(mine, got):
    return [add_low(mine[i], got[i]) for i in range(4)]


def send_along_z(parts):
    return [parts[0]] + [send(parts[i], 0, -b) for i, b in ((1, 1), (2, 3), (3, 2))]


def swap_x(rows):
    return lax.ppermute(rows, "wshard", [(w, w ^ 1) for w in range(8)])


ALONG_Y = [[y * 2 + x for y in range(4)] for x in range(2)]


def tie(*values):
    return lax.optimization_barrier(values)


def inverse_rms(values):
    return lax.rsqrt(jnp.mean(values * values, axis=-1, keepdims=True) + norm_eps)


def rms_pull(values, scale, gain, grad):
    scaled = grad * gain
    return scale * scaled - values * (scale * scale * scale) * jnp.mean(
        scaled * values, axis=-1, keepdims=True
    )


def group_layout(lengths):
    places = jnp.arange(GROUP, dtype=i32)
    ends = jnp.cumsum(lengths)
    starts = ends - lengths
    offset_in = places - PROMPT
    segment_id = jnp.sum((offset_in[:, None] >= ends[None, :]).astype(i32), axis=1)
    segment_hot = segment_id[:, None] == jnp.arange(lengths.shape[0], dtype=i32)[None, :]
    begin = jnp.sum(jnp.where(segment_hot, starts[None, :], 0), axis=1)
    inside = offset_in >= 0
    position = jnp.where(inside, PROMPT + offset_in - begin, places)
    return position, jnp.where(inside, PROMPT + begin, 0)


def rotary_table(position):
    half_dim = HEAD_DIM // 2
    inverse = rope_base ** (-((jnp.arange(2 * HEAD_DIM) % half_dim).astype(f32) * 2.0) / HEAD_DIM)
    back = jnp.where(jnp.arange(2 * HEAD_DIM) < HEAD_DIM, 0.0, 0.5 * jnp.pi).astype(f32)
    return jnp.cos(position[:, None] * inverse[None, :] - back[None, :])


def turn(values):
    half_dim = HEAD_DIM // 2
    return jnp.concatenate([-values[:, half_dim:], values[:, :half_dim]], axis=-1)


def turn_back(values):
    half_dim = HEAD_DIM // 2
    return jnp.concatenate([values[:, half_dim:], -values[:, :half_dim]], axis=-1)


def project_kernel(places, mine, other, w, gain, table, *refs):
    out = refs[-1]
    j = pl.program_id(0)

    if len(refs) > 1:

        @pl.when(j == 0)
        def _():
            out[...] = refs[0][...]

    for k, ref in enumerate((mine, other)):
        at = pl.ds(pl.multiple_of(places[2 * j + k] * TOK, TOK), TOK)
        rows = ref[0].astype(f32)
        normed = (rows * inverse_rms(rows) * gain[...]).astype(bf16)
        projected = jnp.dot(normed, w[...], preferred_element_type=f32)
        c, s = table[at, :HEAD_DIM], table[at, HEAD_DIM:]
        q, k, v = projected[:, :64], projected[:, 64:128], projected[:, 128:]
        q = (q * c + turn(q) * s).astype(bf16).astype(f32) * HEAD_DIM**-0.5
        out[at, :] = jnp.concatenate([q, k * c + turn(k) * s, v], axis=1).astype(bf16)


def project(places, gathered, w, gain, table, before):
    chip = pl.BlockSpec((1, TOK, WIDTH), lambda j, p: (j, 0, 0))
    whole = lambda *shape: pl.BlockSpec(shape, lambda j, p: (0,) * len(shape))
    return pl.pallas_call(
        project_kernel,
        grid_spec=pltpu.PrefetchScalarGridSpec(
            num_scalar_prefetch=1,
            grid=(4,),
            in_specs=[chip, chip, whole(WIDTH, 256), whole(1, WIDTH), whole(GROUP, 128)]
            + [whole(GROUP, 256)] * len(before),
            out_specs=whole(GROUP, 256),
        ),
        out_shape=jax.ShapeDtypeStruct((GROUP, 256), bf16),
        compiler_params=pltpu.CompilerParams(vmem_limit_bytes=VMEM_LIMIT),
        cost_estimate=pl.CostEstimate(
            flops=2 * 8 * TOK * WIDTH * 256, bytes_accessed=10 << 20, transcendentals=0
        ),
    )(places, *gathered, w, gain, table, *before)


def project_back_kernel(places, first, second, w, first_shared, second_shared, mine, other):
    del places
    for projected, shared, out in ((first, first_shared, mine), (second, second_shared, other)):
        out[0, :TOK, :] = lax.dot_general(
            projected[...], w[...], NT, preferred_element_type=f32
        ).astype(bf16)
        rest = jnp.concatenate([shared[:, WIDTH:], jnp.zeros((8, WIDTH - 128), f32)], axis=1)
        out[0, TOK:, :] = jnp.concatenate([shared[:, :WIDTH], rest], axis=0).astype(bf16)


def project_back(places, projected_grad, w, shared):
    chip = pl.BlockSpec((1, LAST, WIDTH), lambda j, p: (j, 0, 0))
    at = lambda k, rows, n: pl.BlockSpec((rows, n), lambda j, p: (p[2 * j + k], 0))
    part = jax.ShapeDtypeStruct((4, LAST, WIDTH), bf16)
    return pl.pallas_call(
        project_back_kernel,
        grid_spec=pltpu.PrefetchScalarGridSpec(
            num_scalar_prefetch=1,
            grid=(4,),
            in_specs=[
                at(0, TOK, 256),
                at(1, TOK, 256),
                pl.BlockSpec((WIDTH, 256), lambda j, p: (0, 0)),
                at(0, 8, 1152),
                at(1, 8, 1152),
            ],
            out_specs=[chip, chip],
        ),
        out_shape=[part, part],
        compiler_params=pltpu.CompilerParams(vmem_limit_bytes=VMEM_LIMIT),
        cost_estimate=pl.CostEstimate(
            flops=2 * 8 * TOK * WIDTH * 256, bytes_accessed=5 << 20, transcendentals=0
        ),
    )(places, projected_grad, projected_grad, w, shared, shared)


def head_grad_kernel(places, near_mine, near_other, far_mine, far_other, gain, first, second, out, total):
    del places
    j = pl.program_id(0)

    @pl.when(j == 0)
    def _():
        total[...] = jnp.zeros_like(total)

    for near, far, projected in ((near_mine, far_mine, first), (near_other, far_other, second)):
        rows = jnp.where(j < 4, near[0], far[0]).astype(f32)
        normed = (rows * inverse_rms(rows) * gain[...]).astype(bf16)
        total[...] += lax.dot_general(normed, projected[...], TN, preferred_element_type=f32)

    @pl.when(j == 7)
    def _():
        out[...] = total[...].astype(bf16)


def head_weight_grad(places, near, far, gain, projected_grad):
    near_chip = pl.BlockSpec((1, TOK, WIDTH), lambda j, p: (jnp.minimum(j, 3), 0, 0))
    far_chip = pl.BlockSpec((1, TOK, WIDTH), lambda j, p: (jnp.maximum(j - 4, 0), 0, 0))
    at = lambda k: pl.BlockSpec((TOK, 256), lambda j, p: (p[2 * j + k], 0))
    return pl.pallas_call(
        head_grad_kernel,
        grid_spec=pltpu.PrefetchScalarGridSpec(
            num_scalar_prefetch=1,
            grid=(8,),
            in_specs=[
                near_chip,
                near_chip,
                far_chip,
                far_chip,
                pl.BlockSpec((1, WIDTH), lambda j, p: (0, 0)),
                at(0),
                at(1),
            ],
            out_specs=pl.BlockSpec((WIDTH, 256), lambda j, p: (0, 0)),
            scratch_shapes=[pltpu.VMEM((WIDTH, 256), f32)],
        ),
        out_shape=jax.ShapeDtypeStruct((WIDTH, 256), bf16),
        compiler_params=pltpu.CompilerParams(vmem_limit_bytes=VMEM_LIMIT),
        cost_estimate=pl.CostEstimate(
            flops=2 * 16 * TOK * WIDTH * 256, bytes_accessed=10 << 20, transcendentals=0
        ),
    )(places, *near, *far, gain, projected_grad, projected_grad)


def tile_mask(scores, key_start, query_start, begin):
    keys = key_start + lax.broadcasted_iota(i32, scores.shape, 0)
    queries = query_start + lax.broadcasted_iota(i32, scores.shape, 1)
    return jnp.where((keys <= queries) & (keys >= begin), scores, masked_score)


def key_ranges(i):
    first = PROMPT // BLOCK
    return jnp.where(i > first, i - 1, i), jnp.minimum(i, first)


def attend_kernel(qkv_ref, begin_ref, o_ref, ot_ref, lse_ref, keys, vt):
    i = pl.program_id(0)
    here = pl.ds(pl.multiple_of(i * BLOCK, BLOCK), BLOCK)

    @pl.when(i == 0)
    def _():
        keys[...] = qkv_ref[:, 64:128]
        vt[...] = qkv_ref[:, 128:192].T

    q = qkv_ref[here, :64]
    begin = begin_ref[...]

    def tile(j, carry, masked, n=1):
        peak, total, out = carry
        start = pl.multiple_of(j * BLOCK, BLOCK)
        at = pl.ds(start, n * BLOCK)
        s = lax.dot_general(keys[at, :], q, NT, preferred_element_type=f32)
        if masked:
            s = tile_mask(s, start, i * BLOCK, begin)
        higher = jnp.maximum(peak, jnp.max(s, axis=0, keepdims=True))
        p = jnp.exp(s - higher)
        fade = jnp.exp(peak - higher)
        total = total * fade + jnp.sum(p, axis=0, keepdims=True)
        out = out * fade + jnp.dot(vt[:, at], p.astype(bf16), preferred_element_type=f32)
        return higher, total, out

    carry = (
        jnp.full((1, BLOCK), masked_score, f32),
        jnp.zeros((1, BLOCK), f32),
        jnp.zeros((HEAD_DIM, BLOCK), f32),
    )
    carry = tile(i, carry, True)
    window, shared = key_ranges(i)
    carry = lax.fori_loop(window, i, lambda j, c: tile(j, c, True), carry)
    pairs = shared // 2
    carry = lax.fori_loop(0, pairs, lambda j, c: tile(2 * j, c, False, 2), carry)
    peak, total, out = lax.fori_loop(2 * pairs, shared, lambda j, c: tile(j, c, False), carry)
    ot_ref[:, here] = out * (1.0 / total)
    lse_ref[...] = peak + jnp.log(total)

    @pl.when(i == GROUP // BLOCK - 1)
    def _():
        for b in range(16):
            o_ref[b] = ot_ref[:, b * TOK : (b + 1) * TOK].astype(bf16)


def attend(qkv, begin):
    whole = lambda *shape: pl.BlockSpec(shape, lambda i: (0,) * len(shape))
    cols = lambda n: pl.BlockSpec((n, BLOCK), lambda i: (0, i))
    return pl.pallas_call(
        attend_kernel,
        grid=(GROUP // BLOCK,),
        in_specs=[whole(GROUP, 256), cols(1)],
        out_specs=[whole(16, HEAD_DIM, TOK), whole(HEAD_DIM, GROUP), cols(1)],
        out_shape=[
            jax.ShapeDtypeStruct((16, HEAD_DIM, TOK), bf16),
            jax.ShapeDtypeStruct((HEAD_DIM, GROUP), f32),
            jax.ShapeDtypeStruct((1, GROUP), f32),
        ],
        scratch_shapes=[
            pltpu.VMEM((GROUP, HEAD_DIM), bf16),
            pltpu.VMEM((HEAD_DIM, GROUP), bf16),
        ],
        compiler_params=pltpu.CompilerParams(vmem_limit_bytes=VMEM_LIMIT),
        cost_estimate=pl.CostEstimate(
            flops=2 * 27 * BLOCK * BLOCK * 512, bytes_accessed=4 << 20, transcendentals=27 * BLOCK * BLOCK
        ),
    )(qkv, begin)


def attend_back_kernel(
    qkv_ref, g_ref, ot_ref, lse_ref, begin_ref, table, out_ref, keys, values, kt, gt, dq, dk, dv
):
    i = pl.program_id(0)
    here = pl.ds(pl.multiple_of(i * BLOCK, BLOCK), BLOCK)

    @pl.when(i == 0)
    def _():
        dk[...] = jnp.zeros_like(dk)
        dv[...] = jnp.zeros_like(dv)
        keys[...] = qkv_ref[:, 64:128]
        values[...] = qkv_ref[:, 128:192]
        kt[...] = qkv_ref[:, 64:128].T
        for b in range(16):
            gt[:, b * TOK : (b + 1) * TOK] = g_ref[b]

    q = qkv_ref[here, :64]
    g = gt[:, here]
    begin = begin_ref[...]
    lse = lse_ref[...]
    inner = jnp.sum(g.astype(f32) * ot_ref[...], axis=0, keepdims=True)

    def tile(j, dq, masked, n=1):
        start = pl.multiple_of(j * BLOCK, BLOCK)
        at = pl.ds(start, n * BLOCK)
        s = lax.dot_general(keys[at, :], q, NT, preferred_element_type=f32)
        if masked:
            s = tile_mask(s, start, i * BLOCK, begin)
        p = jnp.exp(s - lse)
        dp = jnp.dot(values[at, :], g, preferred_element_type=f32)
        ds = (p * (dp - inner)).astype(bf16)
        dv[at, :] += lax.dot_general(p.astype(bf16), g, NT, preferred_element_type=f32)
        dk[at, :] += jnp.dot(ds, q, preferred_element_type=f32)
        return dq + jnp.dot(kt[:, at], ds, preferred_element_type=f32)

    dqt = tile(i, jnp.zeros((HEAD_DIM, BLOCK), f32), True)
    window, shared = key_ranges(i)
    dqt = lax.fori_loop(window, i, lambda j, c: tile(j, c, True), dqt)
    pairs = shared // 2
    dqt = lax.fori_loop(0, pairs, lambda j, c: tile(2 * j, c, False, 2), dqt)
    dqt = lax.fori_loop(2 * pairs, shared, lambda j, c: tile(j, c, False), dqt)
    dq[here, :] = dqt.T * HEAD_DIM**-0.5

    @pl.when(i == GROUP // BLOCK - 1)
    def _():
        def back(b, _):
            at = pl.ds(pl.multiple_of(b * BLOCK, BLOCK), BLOCK)
            c, s = table[at, :HEAD_DIM], table[at, HEAD_DIM:]
            q, k = dq[at, :].astype(bf16).astype(f32), dk[at, :].astype(bf16).astype(f32)
            parts = [q * c + turn_back(q * s), k * c + turn_back(k * s), dv[at, :], jnp.zeros_like(q)]
            out_ref[at, :] = jnp.concatenate(parts, axis=1).astype(bf16)
            return 0

        lax.fori_loop(0, GROUP // BLOCK, back, 0)


def attend_back(qkv, g, ot, lse, begin, table):
    whole = lambda *shape: pl.BlockSpec(shape, lambda i: (0,) * len(shape))
    cols = lambda n: pl.BlockSpec((n, BLOCK), lambda i: (0, i))
    return pl.pallas_call(
        attend_back_kernel,
        grid=(GROUP // BLOCK,),
        in_specs=[
            whole(GROUP, 256),
            whole(16, HEAD_DIM, TOK),
            cols(HEAD_DIM),
            cols(1),
            cols(1),
            whole(GROUP, 128),
        ],
        out_specs=whole(GROUP, 256),
        out_shape=jax.ShapeDtypeStruct((GROUP, 256), bf16),
        scratch_shapes=[
            pltpu.VMEM((GROUP, HEAD_DIM), bf16),
            pltpu.VMEM((GROUP, HEAD_DIM), bf16),
            pltpu.VMEM((HEAD_DIM, GROUP), bf16),
            pltpu.VMEM((HEAD_DIM, GROUP), bf16),
            pltpu.VMEM((GROUP, HEAD_DIM), f32),
            pltpu.VMEM((GROUP, HEAD_DIM), f32),
            pltpu.VMEM((GROUP, HEAD_DIM), f32),
        ],
        compiler_params=pltpu.CompilerParams(vmem_limit_bytes=VMEM_LIMIT),
        cost_estimate=pl.CostEstimate(
            flops=5 * 27 * BLOCK * BLOCK * 512, bytes_accessed=8 << 20, transcendentals=27 * BLOCK * BLOCK
        ),
    )(qkv, g, ot, lse, begin, table)


def up_to():
    return (
        lax.broadcasted_iota(i32, (TOK, TOK), 0) <= lax.broadcasted_iota(i32, (TOK, TOK), 1)
    ).astype(f32).astype(bf16)


def slots_of(routes, own, upto):
    named = [jnp.max((routes == own + e).astype(f32), axis=0, keepdims=True) for e in range(2)]
    named = jnp.concatenate(named + [jnp.zeros((6, TOK), f32)], axis=0)
    rank = jnp.dot(named.astype(bf16), upto, preferred_element_type=f32)
    return jnp.where(named > 0, rank - 1.0, -1.0)


def back_to_tokens(slot_cols):
    columns = lax.broadcasted_iota(i32, (TOK, 2 * SLOTS), 1).astype(f32)
    first, second = slot_cols[:, 0:1], slot_cols[:, 1:2]
    back = (columns == first) | ((columns == second + SLOTS) & (second >= 0))
    return back.astype(f32).astype(bf16)


def experts_kernel(
    own_ref, ffn_mine, ffn_other, g_mine, g_other, routes_mine, routes_other, router_ref, own_w, across_w, *refs
):
    routed_mine, routed_other, z_ref = refs[-9:-6]
    x_ref, dh_ref, act_ref, dy_ref, w_ref, sem = refs[-6:]
    own = own_ref[0]

    copies = [
        [
            pltpu.make_async_copy(shards.at[y, e], w_ref.at[e, 2 * y + (own_ref[1] ^ a)], sem.at[a, y, e])
            for a, shards in enumerate((own_w, across_w))
            for y in range(4)
        ]
        for e in range(2)
    ]

    @pl.when(pl.program_id(0) == 0)
    def _():
        for copy in copies[0] + copies[1]:
            copy.start()

    expert_rows = lax.broadcasted_iota(i32, (EXPERTS, TOK), 0)
    slot_rows = lax.broadcasted_iota(i32, (SLOTS, TOK), 0).astype(f32)
    upto = up_to()
    slot_cols = []
    gate_grads = [jnp.zeros((EXPERTS, WIDTH), f32) for _ in range(4)]
    payload_rows = lax.broadcasted_iota(i32, (EXPERTS, WIDTH), 0)
    gate_rows = [[], []]
    picks = [[], []]
    picked_rows = [[], []]
    picked_grads = [[], []]
    blocks = [(ffn_mine, g_mine, routes_mine, 0), (ffn_other, g_other, routes_other, 0)]
    blocks = blocks + [(*refs_of[:3], 1) for refs_of in blocks]
    for rows_ref, grads_ref, routes_ref, n in blocks:
        rows, grads = rows_ref[n], grads_ref[n]
        routes = routes_ref[n][:8, :TOK].astype(f32).astype(i32)
        chosen = expert_rows == routes[0:1]
        for j in range(1, 8):
            chosen = chosen | (expert_rows == routes[j : j + 1])
        slots = slots_of(routes, own, upto)
        slot_cols.append(slots.T)
        logits = lax.dot_general(router_ref[...], rows, NT, preferred_element_type=f32)
        peak = jnp.max(jnp.where(chosen, logits, masked_score), axis=0, keepdims=True)
        raised = jnp.where(chosen, jnp.exp(jnp.minimum(logits - peak, 0.0)), 0.0)
        gates = raised / jnp.sum(raised, axis=0, keepdims=True)
        for e in range(2):
            gate_rows[e].append(
                jnp.sum(jnp.where(expert_rows == own + e, gates, 0.0), axis=0, keepdims=True)
            )
            picks[e].append((slots[e : e + 1] == slot_rows).astype(f32))
        low = jnp.concatenate([picks[0][-1], picks[1][-1]], axis=0).astype(bf16)
        for source, kept in ((rows, picked_rows), (grads, picked_grads)):
            both = jnp.dot(low, source, preferred_element_type=f32)
            kept[0].append(both[:SLOTS])
            kept[1].append(both[SLOTS:])
    moved, routed = [], []
    for e in range(2):

        @pl.when(pl.program_id(0) == 0)
        def _():
            for copy in copies[e]:
                copy.wait()

        w_gate_up = w_ref[e, :, :128, :].reshape(WIDTH, 2 * FF)
        w_down = w_ref[e, :, 128:, :].reshape(FF, WIDTH)
        x = jnp.concatenate(picked_rows[e], axis=0).astype(bf16)
        gate = jnp.concatenate(
            [jnp.sum(p * r, axis=1, keepdims=True) for p, r in zip(picks[e], gate_rows[e])], axis=0
        )
        grads = jnp.concatenate(picked_grads[e], axis=0)
        dy = (gate * grads).astype(bf16)
        mixed = jnp.dot(x, w_gate_up, preferred_element_type=f32)
        dact = lax.dot_general(dy, w_down, NT, preferred_element_type=f32)
        gate_part, up_part = mixed[:, :FF], mixed[:, FF:]
        sigma = 1.0 / (1.0 + jnp.exp(-gate_part))
        silu = gate_part * sigma
        act = (silu * up_part).astype(bf16)
        dh = jnp.concatenate(
            [dact * up_part * (sigma + silu * (1.0 - sigma)), dact * silu], axis=1
        ).astype(bf16)
        x_ref[e] = x
        dy_ref[e] = dy
        act_ref[e] = act
        dh_ref[e] = dh
        returned = jnp.dot(act, w_down, preferred_element_type=f32).astype(bf16).astype(f32)
        dgate = jnp.sum(returned * grads, axis=1, keepdims=True)
        for b in range(4):
            grad = jnp.sum(
                picks[e][b] * dgate[b * SLOTS : (b + 1) * SLOTS], axis=0, keepdims=True
            )
            high = grad.astype(bf16).astype(f32)
            gap = jnp.zeros((1, 256 - TOK), f32)
            wide = jnp.concatenate([high, gap, grad - high, gap, jnp.zeros((1, WIDTH - 512), f32)], axis=1)
            gate_grads[b] = gate_grads[b] + jnp.where(payload_rows == own + e, wide, 0.0)
        moved.append(gate * returned)
        routed.append(lax.dot_general(dh, w_gate_up, NT, preferred_element_type=f32))
    outs = [(routed_mine, 0), (routed_other, 0), (routed_mine, 1), (routed_other, 1)]
    for b, (routed_ref, n) in enumerate(outs):
        at = slice(b * SLOTS, (b + 1) * SLOTS)
        joined = jnp.concatenate([routed[0][at], routed[1][at]], axis=0).astype(bf16)
        back = back_to_tokens(slot_cols[b])
        routed_ref[n, :TOK, :] = jnp.dot(back, joined, preferred_element_type=f32).astype(bf16)
        routed_ref[n, TOK:, :] = gate_grads[b].astype(bf16)
        z_ref[b] = jnp.concatenate([moved[0][at], moved[1][at]], axis=0).astype(bf16)


def moved_kernel(own_ref, routes_mine, routes_other, z_ref, moved_mine, moved_other):
    upto = up_to()
    outs = [(routes_mine, moved_mine, 0), (routes_other, moved_other, 0)]
    outs = outs + [(*refs_of[:2], 1) for refs_of in outs]
    for b, (routes_ref, moved_ref, n) in enumerate(outs):
        routes = routes_ref[n][:8, :TOK].astype(f32).astype(i32)
        back = back_to_tokens(slots_of(routes, own_ref[0], upto).T)
        moved_ref[n] = jnp.dot(back, z_ref[b], preferred_element_type=f32).astype(bf16)


def moved_rows(half, own, grads, z):
    routes = pl.BlockSpec((2, 16, 256), lambda i, o: (i, TOK // 16, 0))
    pair = pl.BlockSpec((2, TOK, WIDTH), lambda i, o: (i, 0, 0))
    part = jax.ShapeDtypeStruct((4, TOK, WIDTH), bf16)
    return pl.pallas_call(
        moved_kernel,
        grid_spec=pltpu.PrefetchScalarGridSpec(
            num_scalar_prefetch=1,
            grid=(2,),
            in_specs=[
                routes,
                routes,
                pl.BlockSpec((4, 2 * SLOTS, WIDTH), lambda i, o: (i + 2 * half, 0, 0)),
            ],
            out_specs=[pair, pair],
        ),
        out_shape=[part, part],
        compiler_params=pltpu.CompilerParams(vmem_limit_bytes=VMEM_LIMIT),
        cost_estimate=pl.CostEstimate(flops=1 << 30, bytes_accessed=6 << 20, transcendentals=0),
    )(own, *grads, z)


def run_experts(half, own, ffn, grads, weights, router, before):
    pair = pl.BlockSpec((2, TOK, WIDTH), lambda i, o: (i, 0, 0))
    whole = lambda shape: pl.BlockSpec(shape, lambda i, o: (0,) * len(shape))
    routes = pl.BlockSpec((2, 16, 256), lambda i, o: (i, TOK // 16, 0))
    summed = pl.BlockSpec((2, PAY, WIDTH), lambda i, o: (i, 0, 0))
    kept = lambda n: pl.BlockSpec((2, STEP_ROWS, n), lambda i, o: (0, i + 2 * half, 0))
    part = jax.ShapeDtypeStruct((4, PAY, WIDTH), bf16)
    keep = lambda n: jax.ShapeDtypeStruct((2, ALL_ROWS, n), bf16)
    return pl.pallas_call(
        experts_kernel,
        grid_spec=pltpu.PrefetchScalarGridSpec(
            num_scalar_prefetch=1,
            grid=(2,),
            in_specs=[
                pair,
                pair,
                pair,
                pair,
                routes,
                routes,
                whole((EXPERTS, WIDTH)),
            ]
            + [pl.BlockSpec(memory_space=pl.ANY)] * (2 + len(before)),
            out_specs=[
                summed,
                summed,
                pl.BlockSpec((4, 2 * SLOTS, WIDTH), lambda i, o: (i + 2 * half, 0, 0)),
                kept(WIDTH),
                kept(2 * FF),
                kept(FF),
                kept(WIDTH),
            ],
            scratch_shapes=[
                pltpu.VMEM((2, 8, 192, 1024), bf16),
                pltpu.SemaphoreType.DMA((2, 4, 2)),
            ],
        ),
        out_shape=[
            part,
            part,
            jax.ShapeDtypeStruct((16, 2 * SLOTS, WIDTH), bf16),
            keep(WIDTH),
            keep(2 * FF),
            keep(FF),
            keep(WIDTH),
        ],
        input_output_aliases={10 + i: 2 + i for i in range(len(before))},
        compiler_params=pltpu.CompilerParams(vmem_limit_bytes=VMEM_LIMIT),
        cost_estimate=pl.CostEstimate(
            flops=14 << 30, bytes_accessed=24 << 20, transcendentals=8 * SLOTS * 2 * FF
        ),
    )(own, *ffn, *grads, *grads, router, *weights, *before)


def expert_grads_kernel(x_ref, dh_ref, act_ref, dy_ref, out_ref):
    up = lax.dot_general(x_ref[0], dh_ref[0], TN, preferred_element_type=f32)
    down = lax.dot_general(act_ref[0], dy_ref[0], TN, preferred_element_type=f32)
    out_ref[0, :, 0, :128, :] = up.astype(bf16).reshape(2, 128, 2 * FF)
    out_ref[0, :, 0, 128:, :] = down.astype(bf16).reshape(2, 64, WIDTH)


def expert_weight_grads(x, dh, act, dy):
    return pl.pallas_call(
        expert_grads_kernel,
        grid=(2, 4),
        in_specs=[
            pl.BlockSpec((1, ALL_ROWS, 256), lambda e, i: (e, 0, i)),
            pl.BlockSpec((1, ALL_ROWS, 2 * FF), lambda e, i: (e, 0, 0)),
            pl.BlockSpec((1, ALL_ROWS, 128), lambda e, i: (e, 0, i)),
            pl.BlockSpec((1, ALL_ROWS, WIDTH), lambda e, i: (e, 0, 0)),
        ],
        out_specs=pl.BlockSpec((1, 2, 1, 192, 1024), lambda e, i: (i, 0, e, 0, 0)),
        out_shape=jax.ShapeDtypeStruct((4, 2, 2, 192, 1024), bf16),
        compiler_params=pltpu.CompilerParams(vmem_limit_bytes=VMEM_LIMIT),
        cost_estimate=pl.CostEstimate(flops=8 << 30, bytes_accessed=14 << 20, transcendentals=0),
    )(x, dh, act, dy)


def hidden_kernel(att_ref, w_ref, rows_ref, gain_ref, hidden_ref, normed_ref):
    att = att_ref[...].reshape(WIDTH, TOK)
    hidden = rows_ref[...].astype(f32) + lax.dot_general(
        att, w_ref[:, :WIDTH], TN, preferred_element_type=f32
    )
    hidden_ref[...] = hidden
    normed_ref[...] = (hidden * inverse_rms(hidden) * gain_ref[...]).astype(bf16)


def hidden_of(attended, shared, rows, gain):
    return pl.pallas_call(
        hidden_kernel,
        out_shape=[
            jax.ShapeDtypeStruct((TOK, WIDTH), f32),
            jax.ShapeDtypeStruct((TOK, WIDTH), bf16),
        ],
        compiler_params=pltpu.CompilerParams(vmem_limit_bytes=VMEM_LIMIT),
        cost_estimate=pl.CostEstimate(
            flops=2 * TOK * WIDTH * WIDTH, bytes_accessed=5 << 20, transcendentals=0
        ),
    )(attended, shared, rows, gain)


def hidden_back_kernel(
    t0, t1, t2, t3, crossed, hidden_ref, normed_ref, chosen_ref, router_ref, g_ref, gain_ref,
    w_ref, hidden_grad_ref, branch_ref, logit_ref, scaled_ref, att_ref
):
    chosen = chosen_ref[...] > 0
    logits = lax.dot_general(router_ref[...], normed_ref[...], NT, preferred_element_type=f32)
    peak = jnp.max(jnp.where(chosen, logits, masked_score), axis=0, keepdims=True)
    raised = jnp.where(chosen, jnp.exp(jnp.minimum(logits - peak, 0.0)), 0.0)
    gates = raised / jnp.sum(raised, axis=0, keepdims=True)
    summed = t0[...].astype(f32)
    for term in (t1, t2, t3, crossed):
        summed = summed + term[...].astype(f32)
    gate_grad = summed[TOK:, :TOK] + summed[TOK:, 256 : 256 + TOK]
    logit_grad = gates * (gate_grad - jnp.sum(gates * gate_grad, axis=0, keepdims=True))
    logit_grad = logit_grad.astype(bf16)
    logit_ref[...] = logit_grad
    normed_grad = summed[:TOK] + lax.dot_general(
        logit_grad, router_ref[...], TN, preferred_element_type=f32
    )
    hidden = hidden_ref[...]
    scale = inverse_rms(hidden)
    scaled_ref[...] = (normed_grad * hidden * scale).astype(bf16)
    hidden_grad = g_ref[...].astype(f32) + rms_pull(hidden, scale, gain_ref[...], normed_grad)
    hidden_grad_ref[...] = hidden_grad
    branch = hidden_grad.astype(bf16)
    branch_ref[...] = branch
    att = lax.dot_general(w_ref[:, :WIDTH], branch, NT, preferred_element_type=f32)
    att_ref[...] = att.astype(bf16).reshape(HEADS, HEAD_DIM, TOK)


def hidden_back(terms, crossed, hidden, normed, chosen, router_t, g, gain, shared):
    wide = lambda t: jax.ShapeDtypeStruct((TOK, WIDTH), t)
    return pl.pallas_call(
        hidden_back_kernel,
        out_shape=[
            wide(f32),
            wide(bf16),
            jax.ShapeDtypeStruct((EXPERTS, TOK), bf16),
            wide(bf16),
            jax.ShapeDtypeStruct((HEADS, HEAD_DIM, TOK), bf16),
        ],
        compiler_params=pltpu.CompilerParams(vmem_limit_bytes=VMEM_LIMIT),
        cost_estimate=pl.CostEstimate(
            flops=2 * TOK * WIDTH * WIDTH, bytes_accessed=8 << 20, transcendentals=0
        ),
    )(*terms, crossed, hidden, normed, chosen, router_t, g, gain, shared)


def shared_grads_kernel(att_ref, branch_ref, normed_ref, logit_ref, scaled_ref, out_ref):
    over_tokens = (((0,), (1,)), ((), ()))
    logit = jnp.concatenate([logit_ref[...], jnp.zeros((96, TOK), bf16)], axis=0)
    ones = (lax.broadcasted_iota(i32, (128, TOK), 0) == EXPERTS).astype(f32).astype(bf16)
    att = att_ref[...].reshape(WIDTH, TOK)
    grads = [
        jnp.dot(att, branch_ref[...], preferred_element_type=f32),
        lax.dot_general(normed_ref[...], logit, over_tokens, preferred_element_type=f32)
        + lax.dot_general(scaled_ref[...], ones, over_tokens, preferred_element_type=f32),
    ]
    for w in range(8):
        for part, at in zip(grads, (slice(0, WIDTH), slice(WIDTH, None))):
            rows = [part[s * 64 + w * 8 : s * 64 + w * 8 + 8] for s in range(16)]
            out_ref[w, :, at] = jnp.concatenate(rows, axis=0).astype(bf16)


def shared_weight_grads(att, branch, normed, logit_grad, scaled):
    return pl.pallas_call(
        shared_grads_kernel,
        out_shape=jax.ShapeDtypeStruct((8, 128, 1152), bf16),
        compiler_params=pltpu.CompilerParams(vmem_limit_bytes=VMEM_LIMIT),
        cost_estimate=pl.CostEstimate(
            flops=2 * TOK * WIDTH * 1280, bytes_accessed=5 << 20, transcendentals=0
        ),
    )(att, branch, normed, logit_grad, scaled)


def local(
    tokens,
    routes,
    cont_lengths,
    norm_attn,
    w_qkv,
    w_out,
    w_router,
    norm_ffn,
    w_gate_up,
    w_down,
    cotangent,
):
    seq_index = lax.axis_index("seq")
    places, blocks = relative_places(seq_index)
    rows = tokens[0]
    query_width = HEADS * HEAD_DIM
    kv_width = KV_HEADS * HEAD_DIM

    position, begin = group_layout(cont_lengths[0])
    begin = begin[None]
    table = rotary_table(position.astype(f32))
    kv_heads = lambda start: jnp.repeat(
        w_qkv[:, start : start + kv_width].reshape(8, KV_HEADS, HEAD_DIM), 2, axis=1
    )
    head_cols = jnp.concatenate(
        [
            w_qkv[:, :query_width].reshape(8, HEADS, HEAD_DIM),
            kv_heads(query_width),
            kv_heads(query_width + kv_width),
            jnp.broadcast_to(norm_attn[:, None, None], (8, HEADS, HEAD_DIM)),
        ],
        axis=2,
    ).transpose(1, 0, 2)
    head_cols = jnp.broadcast_to(head_cols[:, None], (HEADS, 8, 8, 256)).reshape(128, 8, 256)
    head_weights = lax.all_to_all(head_cols, BOTH, 0, 0, tiled=True).reshape(WIDTH, 256)
    gain_attn = head_weights[:, 192].astype(f32)[None]
    head_weights = jnp.where(jnp.arange(256)[None] < 192, head_weights, 0.0).astype(bf16)

    rows_near, rows_across = gather_near(rows)
    rows_near, _, table, head_weights = tie(rows_near, rows_across, table, head_weights)
    rows_near, rows_far = both_cores(rows_near), gather_far(rows_across)

    own_x = lax.axis_index("wshard") % 2
    expert_rows = jnp.concatenate([w_gate_up, w_down], axis=1)
    along_y = lambda t: lax.all_gather(t, "wshard", axis_index_groups=ALONG_Y, axis=0)
    experts, expert_rows = along_y(expert_rows), swap_x(expert_rows)

    qkv = project(places[:8], rows_near, head_weights, gain_attn, table, ())
    shared = jnp.concatenate(
        [w_out, w_router, norm_ffn[:, None], jnp.zeros((8, 95), bf16)], axis=1
    )
    shared, qkv = tie(shared, qkv)
    shared = lax.all_to_all(
        jnp.broadcast_to(shared[None], (128, 8, 1152)), BOTH, 0, 0, tiled=True
    ).reshape(WIDTH, 1152)
    routes_rows = jnp.pad(routes[0].T.astype(bf16), ((0, 8), (0, WIDTH - TOK)))
    upstream_rows = jnp.concatenate([cotangent[0], routes_rows], axis=0)
    rows_far, qkv, upstream_rows, expert_rows = tie(rows_far, qkv, upstream_rows, expert_rows)
    experts = [experts, along_y(expert_rows)]
    rows_far = both_cores(rows_far)
    grad_near = [upstream_rows] + [send(upstream_rows, 0, b) for b in (1, 3, 2)]
    qkv = project(places[8:], rows_far, head_weights, gain_attn, table, (qkv,))

    router_t = shared[:, WIDTH : WIDTH + EXPERTS].T
    gain_ffn = shared[:, WIDTH + EXPERTS].astype(f32)[None]
    attended_head, attended_t, lse = attend(qkv, begin)
    attended_head, shared = tie(attended_head, shared)
    attended = lax.all_to_all(attended_head, "seq", 0, 0, tiled=True)
    attended, grad_near = tie(attended, grad_near)
    grad_near = jnp.stack(grad_near)
    grad_far = [send(grad_near[:1], 1, 0)]
    hidden, normed_ffn = hidden_of(attended, shared, rows, gain_ffn)
    ffn_near, ffn_across = gather_near(normed_ffn)
    grad_near_mine, _ = tie(grad_near, ffn_across)
    ffn_near, _, grad_far[0] = tie(ffn_near, ffn_across, grad_far[0])
    grad_far.append(send(grad_near_mine[1:], 1, 0))
    grad_near = (grad_near, swap_cores(grad_near))
    ffn_near, ffn_far = both_cores(ffn_near), gather_far(ffn_across)
    own = jnp.stack([seq_index * 2, own_x])
    near = run_experts(0, own, ffn_near, grad_near, experts, router_t, ())
    near_terms = sum_along_z(*near[:2])
    ffn_far = both_cores(ffn_far)
    grad_far = jnp.concatenate(grad_far, axis=0)
    grad_far = (grad_far, swap_cores(grad_far))
    far = run_experts(1, own, ffn_far, grad_far, experts, router_t, near[2:])
    far, near_terms = tie(far, near_terms)
    moved, saved = far[2], far[3:]
    far_other, moved = tie(swap_cores(far[1]), moved)
    far_terms = send_along_z(chip_parts(far[0], far_other))
    expert_grads = expert_weight_grads(*saved)
    moved_near = moved_rows(0, own, grad_near, moved)
    moved_far = moved_rows(1, own, grad_far, moved)
    far_terms, expert_grads, moved_near, moved_far = tie(
        far_terms, expert_grads, moved_near, moved_far
    )
    crossed = send(add_low(*far_terms), 1, 0)
    near_got, far_got = swap_cores(moved_near[1]), swap_cores(moved_far[1])
    moved_parts = [
        jnp.stack([add_low(moved_near[0][i], near_got[i]), add_low(moved_far[0][i], far_got[i])])
        for i in range(4)
    ]
    crossed, moved_parts = tie(crossed, moved_parts)

    expert_range = jnp.arange(EXPERTS, dtype=i32)
    chosen_here = jnp.any(routes[0].T[None] == expert_range[:, None, None], axis=1).astype(f32)
    hidden_grad, branch_grad, logit_grad, scaled_grad, attended_grad = hidden_back(
        near_terms, crossed, hidden, normed_ffn, chosen_here, router_t, cotangent[0], gain_ffn, shared
    )
    expert_grads = lax.psum_scatter(
        expert_grads.reshape(8, 2, 192, 1024),
        "wshard",
        axis_index_groups=ALONG_Y,
        scatter_dimension=0,
        tiled=True,
    )
    head_grad = lax.all_to_all(attended_grad, "seq", 0, 0, tiled=True)
    shared_grads = shared_weight_grads(attended, branch_grad, normed_ffn, logit_grad, scaled_grad)
    head_grad, shared_grads, moved_parts = tie(head_grad, shared_grads, moved_parts)
    moved_terms = [moved_parts[0]] + [
        send(moved_parts[i], 0, -b) for i, b in ((1, 1), (2, 3), (3, 2))
    ]

    shared_grads = lax.all_to_all(shared_grads, "wshard", 0, 0, tiled=True)
    projected_grad = attend_back(qkv, head_grad, attended_t, lse, begin, table)
    shared_grads = jnp.sum(shared_grads.astype(f32), axis=0)
    far_part = project_back(places[8:], projected_grad, head_weights, shared_grads)
    near_part = project_back(places[:8], projected_grad, head_weights, shared_grads)
    far_parts = chip_parts(far_part[0], swap_cores(far_part[1]))
    near_part, moved_terms, expert_grads = tie(near_part, moved_terms, expert_grads)
    near_parts = chip_parts(near_part[0], swap_cores(near_part[1]))
    far_parts, near_parts, projected_grad, moved_terms, expert_grads = tie(
        far_parts, near_parts, projected_grad, moved_terms, expert_grads
    )
    far_terms = send_along_z(far_parts)
    near_terms = send_along_z(near_parts)
    moved_crossed = send(add_low(*[t[1] for t in moved_terms]), 1, 0)
    grad_head = head_weight_grad(places, rows_near, rows_far, gain_attn, projected_grad)
    grad_heads = lax.all_to_all(grad_head.reshape(128, 8, 256), BOTH, 0, 0, tiled=True)
    crossed = send(add_low(*far_terms), 1, 0)
    crossed, near_terms, grad_heads = tie(crossed, near_terms, grad_heads)
    kept = lax.dynamic_index_in_dim(expert_grads, own_x, 0, keepdims=False)
    sent = lax.dynamic_index_in_dim(expert_grads, 1 - own_x, 0, keepdims=False)
    expert_grads = kept.astype(f32) + swap_x(sent).astype(f32)
    total = lambda terms: sum([t.astype(f32) for t in terms])
    output = (hidden + total([t[0] for t in moved_terms] + [moved_crossed])).astype(bf16)
    last_sum = total(near_terms + [crossed])
    normed_grad, shared_grads = last_sum[:TOK], last_sum[TOK:]
    grad_heads = jnp.sum(grad_heads.reshape(16, 8, 8, 256).astype(f32), axis=1).transpose(1, 0, 2)
    kv_sum = lambda start: jnp.sum(
        grad_heads[:, :, start : start + HEAD_DIM].reshape(8, KV_HEADS, 2, HEAD_DIM), axis=2
    ).reshape(8, kv_width)
    grad_qkv = jnp.concatenate(
        [grad_heads[:, :, :HEAD_DIM].reshape(8, query_width), kv_sum(HEAD_DIM), kv_sum(2 * HEAD_DIM)],
        axis=1,
    )
    grad_norm_attn = jnp.sum(grad_qkv * w_qkv.astype(f32), axis=1) / norm_attn.astype(f32)
    inputs = rows.astype(f32)
    grad_input = hidden_grad + rms_pull(inputs, inverse_rms(inputs), gain_attn, normed_grad)
    return (
        output[None],
        grad_input[None],
        grad_norm_attn,
        grad_qkv,
        shared_grads[:8],
        shared_grads[8:, :EXPERTS],
        shared_grads[8:, EXPERTS],
        expert_grads[:, :128],
        expert_grads[:, 128:],
    )


def solution(mesh):
    return jax.shard_map(
        local,
        mesh=mesh,
        in_specs=(
            P("wshard", "seq", None),
            P("wshard", "seq", None),
            P("wshard", None),
            P(BOTH),
            P(BOTH, None),
            P(BOTH, None),
            P(BOTH, None),
            P(BOTH),
            P("seq", "wshard", None),
            P("seq", "wshard", None),
            P("wshard", "seq", None),
        ),
        out_specs=(
            P("wshard", "seq", None),
            P("wshard", "seq", None),
            P(BOTH),
            P(BOTH, None),
            P(BOTH, None),
            P(BOTH, None),
            P(BOTH),
            P("seq", "wshard", None),
            P("seq", "wshard", None),
        ),
        check_vma=False,
    )
```

```python
import jax
import jax.numpy as jnp
from jax import lax
from jax.experimental import pallas as pl
from jax.experimental.pallas import tpu as pltpu
from jax.sharding import PartitionSpec as P

HEADS = 16
KV_HEADS = 8
HEAD_DIM = 64
EXPERTS = 32
FF = 512
PROMPT = 2048
GROUP = 3584
TOK = 224
WIDTH = 1024
SLOTS = 72
STEP_ROWS = 4 * SLOTS
ALL_ROWS = 16 * SLOTS
BLOCK = 512
VMEM_LIMIT = 60 << 20
LAST = TOK + 16
EARLY = 352
PAY = TOK + 32

norm_eps = 1e-06
rope_base = 10000.0
masked_score = -1e30
BOTH = ("seq", "wshard")
NT = (((1,), (1,)), ((), ()))
TN = (((0,), (0,)), ((), ()))
f32 = jnp.float32
bf16 = jnp.bfloat16
i32 = jnp.int32


def place_of(x, z, core):
    return x * 8 + z * 2 + core


def shift_perm(a, b):
    return [
        (place_of(x, z, c), place_of(x ^ a, (z + b) % 4, c))
        for x in range(2)
        for z in range(4)
        for c in range(2)
    ]


CORE_PERM = [(i, i ^ 1) for i in range(16)]


def send(rows, a, b):
    return lax.ppermute(rows, "seq", shift_perm(a, b))


def swap_cores(rows):
    return lax.ppermute(rows, "seq", CORE_PERM)


def relative_places(seq_index):
    x, z, c = seq_index // 8, (seq_index // 2) % 4, seq_index % 2
    r = jnp.arange(16, dtype=i32)
    a, i, k = r // 8, (r // 2) % 4, r % 2
    shift = i ^ (i // 2)
    behind = (z - i) % 4
    places = (a ^ x) * 8 + ((z - shift) % 4) * 2 + (k ^ c)
    return places, (a ^ x) * 8 + (behind ^ (behind // 2)) * 2 + (k ^ c)


def gather_near(rows):
    return [rows] + [send(rows, 0, b) for b in (1, 3, 2)], send(rows, 1, 0)


def both_cores(parts):
    mine = jnp.stack(parts)
    return mine, swap_cores(mine)


def gather_far(across):
    return [across] + [send(across, 0, b) for b in (1, 3, 2)]


def add_low(*terms):
    return sum([t.astype(f32) for t in terms]).astype(bf16)


def sum_along_z(mine, other):
    return send_along_z(chip_parts(mine, swap_cores(other)))


def chip_parts(mine, got):
    return [add_low(mine[i], got[i]) for i in range(4)]


def send_along_z(parts):
    return [parts[0]] + [send(parts[i], 0, -b) for i, b in ((1, 1), (2, 3), (3, 2))]


def swap_x(rows):
    return lax.ppermute(rows, "wshard", [(w, w ^ 1) for w in range(8)])


ALONG_Y = [[y * 2 + x for y in range(4)] for x in range(2)]


def tie(*values):
    return lax.optimization_barrier(values)


def inverse_rms(values):
    return lax.rsqrt(jnp.mean(values * values, axis=-1, keepdims=True) + norm_eps)


def rms_pull(values, scale, gain, grad):
    scaled = grad * gain
    return scale * scaled - values * (scale * scale * scale) * jnp.mean(
        scaled * values, axis=-1, keepdims=True
    )


def group_layout(lengths):
    places = jnp.arange(GROUP, dtype=i32)
    ends = jnp.cumsum(lengths)
    starts = ends - lengths
    offset_in = places - PROMPT
    segment_id = jnp.sum((offset_in[:, None] >= ends[None, :]).astype(i32), axis=1)
    segment_hot = segment_id[:, None] == jnp.arange(lengths.shape[0], dtype=i32)[None, :]
    begin = jnp.sum(jnp.where(segment_hot, starts[None, :], 0), axis=1)
    inside = offset_in >= 0
    position = jnp.where(inside, PROMPT + offset_in - begin, places)
    return position, jnp.where(inside, PROMPT + begin, 0)


def rotary_table(position):
    half_dim = HEAD_DIM // 2
    inverse = rope_base ** (-((jnp.arange(2 * HEAD_DIM) % half_dim).astype(f32) * 2.0) / HEAD_DIM)
    back = jnp.where(jnp.arange(2 * HEAD_DIM) < HEAD_DIM, 0.0, 0.5 * jnp.pi).astype(f32)
    return jnp.cos(position[:, None] * inverse[None, :] - back[None, :])


def turn(values):
    half_dim = HEAD_DIM // 2
    return jnp.concatenate([-values[:, half_dim:], values[:, :half_dim]], axis=-1)


def turn_back(values):
    half_dim = HEAD_DIM // 2
    return jnp.concatenate([values[:, half_dim:], -values[:, :half_dim]], axis=-1)


def project_kernel(places, mine, other, w, gain, table, *refs):
    out = refs[-1]
    j = pl.program_id(0)

    if len(refs) > 1:

        @pl.when(j == 0)
        def _():
            out[...] = refs[0][...]

    for k, ref in enumerate((mine, other)):
        at = pl.ds(pl.multiple_of(places[2 * j + k] * TOK, TOK), TOK)
        rows = ref[0].astype(f32)
        normed = (rows * inverse_rms(rows) * gain[...]).astype(bf16)
        projected = jnp.dot(normed, w[...], preferred_element_type=f32)
        c, s = table[at, :HEAD_DIM], table[at, HEAD_DIM:]
        q, k, v = projected[:, :64], projected[:, 64:128], projected[:, 128:]
        q = (q * c + turn(q) * s).astype(bf16).astype(f32) * HEAD_DIM**-0.5
        out[at, :] = jnp.concatenate([q, k * c + turn(k) * s, v], axis=1).astype(bf16)


def project(places, gathered, w, gain, table, before):
    chip = pl.BlockSpec((1, TOK, WIDTH), lambda j, p: (j, 0, 0))
    whole = lambda *shape: pl.BlockSpec(shape, lambda j, p: (0,) * len(shape))
    return pl.pallas_call(
        project_kernel,
        grid_spec=pltpu.PrefetchScalarGridSpec(
            num_scalar_prefetch=1,
            grid=(4,),
            in_specs=[chip, chip, whole(WIDTH, 256), whole(1, WIDTH), whole(GROUP, 128)]
            + [whole(GROUP, 256)] * len(before),
            out_specs=whole(GROUP, 256),
        ),
        out_shape=jax.ShapeDtypeStruct((GROUP, 256), bf16),
        compiler_params=pltpu.CompilerParams(vmem_limit_bytes=VMEM_LIMIT),
        cost_estimate=pl.CostEstimate(
            flops=2 * 8 * TOK * WIDTH * 256, bytes_accessed=10 << 20, transcendentals=0
        ),
    )(places, *gathered, w, gain, table, *before)


def project_back_kernel(places, first, second, w, first_shared, second_shared, mine, other):
    del places
    for projected, shared, out in ((first, first_shared, mine), (second, second_shared, other)):
        out[0, :TOK, :] = lax.dot_general(
            projected[...], w[...], NT, preferred_element_type=f32
        ).astype(bf16)
        rest = jnp.concatenate([shared[:, WIDTH:], jnp.zeros((8, WIDTH - 128), f32)], axis=1)
        out[0, TOK:, :] = jnp.concatenate([shared[:, :WIDTH], rest], axis=0).astype(bf16)


def project_back(places, projected_grad, w, shared):
    chip = pl.BlockSpec((1, LAST, WIDTH), lambda j, p: (j, 0, 0))
    at = lambda k, rows, n: pl.BlockSpec((rows, n), lambda j, p: (p[2 * j + k], 0))
    part = jax.ShapeDtypeStruct((4, LAST, WIDTH), bf16)
    return pl.pallas_call(
        project_back_kernel,
        grid_spec=pltpu.PrefetchScalarGridSpec(
            num_scalar_prefetch=1,
            grid=(4,),
            in_specs=[
                at(0, TOK, 256),
                at(1, TOK, 256),
                pl.BlockSpec((WIDTH, 256), lambda j, p: (0, 0)),
                at(0, 8, 1152),
                at(1, 8, 1152),
            ],
            out_specs=[chip, chip],
        ),
        out_shape=[part, part],
        compiler_params=pltpu.CompilerParams(vmem_limit_bytes=VMEM_LIMIT),
        cost_estimate=pl.CostEstimate(
            flops=2 * 8 * TOK * WIDTH * 256, bytes_accessed=5 << 20, transcendentals=0
        ),
    )(places, projected_grad, projected_grad, w, shared, shared)


def head_grad_kernel(places, near_mine, near_other, far_mine, far_other, gain, first, second, out, total):
    del places
    j = pl.program_id(0)

    @pl.when(j == 0)
    def _():
        total[...] = jnp.zeros_like(total)

    for near, far, projected in ((near_mine, far_mine, first), (near_other, far_other, second)):
        rows = jnp.where(j < 4, near[0], far[0]).astype(f32)
        normed = (rows * inverse_rms(rows) * gain[...]).astype(bf16)
        total[...] += lax.dot_general(normed, projected[...], TN, preferred_element_type=f32)

    @pl.when(j == 7)
    def _():
        out[...] = total[...].astype(bf16)


def head_weight_grad(places, near, far, gain, projected_grad):
    near_chip = pl.BlockSpec((1, TOK, WIDTH), lambda j, p: (jnp.minimum(j, 3), 0, 0))
    far_chip = pl.BlockSpec((1, TOK, WIDTH), lambda j, p: (jnp.maximum(j - 4, 0), 0, 0))
    at = lambda k: pl.BlockSpec((TOK, 256), lambda j, p: (p[2 * j + k], 0))
    return pl.pallas_call(
        head_grad_kernel,
        grid_spec=pltpu.PrefetchScalarGridSpec(
            num_scalar_prefetch=1,
            grid=(8,),
            in_specs=[
                near_chip,
                near_chip,
                far_chip,
                far_chip,
                pl.BlockSpec((1, WIDTH), lambda j, p: (0, 0)),
                at(0),
                at(1),
            ],
            out_specs=pl.BlockSpec((WIDTH, 256), lambda j, p: (0, 0)),
            scratch_shapes=[pltpu.VMEM((WIDTH, 256), f32)],
        ),
        out_shape=jax.ShapeDtypeStruct((WIDTH, 256), bf16),
        compiler_params=pltpu.CompilerParams(vmem_limit_bytes=VMEM_LIMIT),
        cost_estimate=pl.CostEstimate(
            flops=2 * 16 * TOK * WIDTH * 256, bytes_accessed=10 << 20, transcendentals=0
        ),
    )(places, *near, *far, gain, projected_grad, projected_grad)


def tile_mask(scores, key_start, query_start, begin):
    keys = key_start + lax.broadcasted_iota(i32, scores.shape, 0)
    queries = query_start + lax.broadcasted_iota(i32, scores.shape, 1)
    return jnp.where((keys <= queries) & (keys >= begin), scores, masked_score)


def key_ranges(i):
    first = PROMPT // BLOCK
    return jnp.where(i > first, i - 1, i), jnp.minimum(i, first)


def attend_kernel(qkv_ref, begin_ref, o_ref, ot_ref, lse_ref, keys, vt):
    i = pl.program_id(0)
    here = pl.ds(pl.multiple_of(i * BLOCK, BLOCK), BLOCK)

    @pl.when(i == 0)
    def _():
        keys[...] = qkv_ref[:, 64:128]
        vt[...] = qkv_ref[:, 128:192].T

    q = qkv_ref[here, :64]
    begin = begin_ref[...]

    def tile(j, carry, masked, n=1):
        peak, total, out = carry
        start = pl.multiple_of(j * BLOCK, BLOCK)
        at = pl.ds(start, n * BLOCK)
        s = lax.dot_general(keys[at, :], q, NT, preferred_element_type=f32)
        if masked:
            s = tile_mask(s, start, i * BLOCK, begin)
        higher = jnp.maximum(peak, jnp.max(s, axis=0, keepdims=True))
        p = jnp.exp(s - higher)
        fade = jnp.exp(peak - higher)
        total = total * fade + jnp.sum(p, axis=0, keepdims=True)
        out = out * fade + jnp.dot(vt[:, at], p.astype(bf16), preferred_element_type=f32)
        return higher, total, out

    carry = (
        jnp.full((1, BLOCK), masked_score, f32),
        jnp.zeros((1, BLOCK), f32),
        jnp.zeros((HEAD_DIM, BLOCK), f32),
    )
    carry = tile(i, carry, True)
    window, shared = key_ranges(i)
    carry = lax.fori_loop(window, i, lambda j, c: tile(j, c, True), carry)
    pairs = shared // 2
    carry = lax.fori_loop(0, pairs, lambda j, c: tile(2 * j, c, False, 2), carry)
    peak, total, out = lax.fori_loop(2 * pairs, shared, lambda j, c: tile(j, c, False), carry)
    ot_ref[:, here] = out * (1.0 / total)
    lse_ref[...] = peak + jnp.log(total)

    @pl.when(i == GROUP // BLOCK - 1)
    def _():
        for b in range(16):
            o_ref[b] = ot_ref[:, b * TOK : (b + 1) * TOK].astype(bf16)


def attend(qkv, begin):
    whole = lambda *shape: pl.BlockSpec(shape, lambda i: (0,) * len(shape))
    cols = lambda n: pl.BlockSpec((n, BLOCK), lambda i: (0, i))
    return pl.pallas_call(
        attend_kernel,
        grid=(GROUP // BLOCK,),
        in_specs=[whole(GROUP, 256), cols(1)],
        out_specs=[whole(16, HEAD_DIM, TOK), whole(HEAD_DIM, GROUP), cols(1)],
        out_shape=[
            jax.ShapeDtypeStruct((16, HEAD_DIM, TOK), bf16),
            jax.ShapeDtypeStruct((HEAD_DIM, GROUP), f32),
            jax.ShapeDtypeStruct((1, GROUP), f32),
        ],
        scratch_shapes=[
            pltpu.VMEM((GROUP, HEAD_DIM), bf16),
            pltpu.VMEM((HEAD_DIM, GROUP), bf16),
        ],
        compiler_params=pltpu.CompilerParams(vmem_limit_bytes=VMEM_LIMIT),
        cost_estimate=pl.CostEstimate(
            flops=2 * 27 * BLOCK * BLOCK * 512, bytes_accessed=4 << 20, transcendentals=27 * BLOCK * BLOCK
        ),
    )(qkv, begin)


def attend_back_kernel(
    qkv_ref, g_ref, ot_ref, lse_ref, begin_ref, table, out_ref, keys, values, kt, gt, dq, dk, dv
):
    i = pl.program_id(0)
    here = pl.ds(pl.multiple_of(i * BLOCK, BLOCK), BLOCK)

    @pl.when(i == 0)
    def _():
        dk[...] = jnp.zeros_like(dk)
        dv[...] = jnp.zeros_like(dv)
        keys[...] = qkv_ref[:, 64:128]
        values[...] = qkv_ref[:, 128:192]
        kt[...] = qkv_ref[:, 64:128].T
        for b in range(16):
            gt[:, b * TOK : (b + 1) * TOK] = g_ref[b]

    q = qkv_ref[here, :64]
    g = gt[:, here]
    begin = begin_ref[...]
    lse = lse_ref[...]
    inner = jnp.sum(g.astype(f32) * ot_ref[...], axis=0, keepdims=True)

    def tile(j, dq, masked, n=1):
        start = pl.multiple_of(j * BLOCK, BLOCK)
        at = pl.ds(start, n * BLOCK)
        s = lax.dot_general(keys[at, :], q, NT, preferred_element_type=f32)
        if masked:
            s = tile_mask(s, start, i * BLOCK, begin)
        p = jnp.exp(s - lse)
        dp = jnp.dot(values[at, :], g, preferred_element_type=f32)
        ds = (p * (dp - inner)).astype(bf16)
        dv[at, :] += lax.dot_general(p.astype(bf16), g, NT, preferred_element_type=f32)
        dk[at, :] += jnp.dot(ds, q, preferred_element_type=f32)
        return dq + jnp.dot(kt[:, at], ds, preferred_element_type=f32)

    dqt = tile(i, jnp.zeros((HEAD_DIM, BLOCK), f32), True)
    window, shared = key_ranges(i)
    dqt = lax.fori_loop(window, i, lambda j, c: tile(j, c, True), dqt)
    pairs = shared // 2
    dqt = lax.fori_loop(0, pairs, lambda j, c: tile(2 * j, c, False, 2), dqt)
    dqt = lax.fori_loop(2 * pairs, shared, lambda j, c: tile(j, c, False), dqt)
    dq[here, :] = dqt.T * HEAD_DIM**-0.5

    @pl.when(i == GROUP // BLOCK - 1)
    def _():
        def back(b, _):
            at = pl.ds(pl.multiple_of(b * BLOCK, BLOCK), BLOCK)
            c, s = table[at, :HEAD_DIM], table[at, HEAD_DIM:]
            q, k = dq[at, :].astype(bf16).astype(f32), dk[at, :].astype(bf16).astype(f32)
            parts = [q * c + turn_back(q * s), k * c + turn_back(k * s), dv[at, :], jnp.zeros_like(q)]
            out_ref[at, :] = jnp.concatenate(parts, axis=1).astype(bf16)
            return 0

        lax.fori_loop(0, GROUP // BLOCK, back, 0)


def attend_back(qkv, g, ot, lse, begin, table):
    whole = lambda *shape: pl.BlockSpec(shape, lambda i: (0,) * len(shape))
    cols = lambda n: pl.BlockSpec((n, BLOCK), lambda i: (0, i))
    return pl.pallas_call(
        attend_back_kernel,
        grid=(GROUP // BLOCK,),
        in_specs=[
            whole(GROUP, 256),
            whole(16, HEAD_DIM, TOK),
            cols(HEAD_DIM),
            cols(1),
            cols(1),
            whole(GROUP, 128),
        ],
        out_specs=whole(GROUP, 256),
        out_shape=jax.ShapeDtypeStruct((GROUP, 256), bf16),
        scratch_shapes=[
            pltpu.VMEM((GROUP, HEAD_DIM), bf16),
            pltpu.VMEM((GROUP, HEAD_DIM), bf16),
            pltpu.VMEM((HEAD_DIM, GROUP), bf16),
            pltpu.VMEM((HEAD_DIM, GROUP), bf16),
            pltpu.VMEM((GROUP, HEAD_DIM), f32),
            pltpu.VMEM((GROUP, HEAD_DIM), f32),
            pltpu.VMEM((GROUP, HEAD_DIM), f32),
        ],
        compiler_params=pltpu.CompilerParams(vmem_limit_bytes=VMEM_LIMIT),
        cost_estimate=pl.CostEstimate(
            flops=5 * 27 * BLOCK * BLOCK * 512, bytes_accessed=8 << 20, transcendentals=27 * BLOCK * BLOCK
        ),
    )(qkv, g, ot, lse, begin, table)


def experts_kernel(
    own_ref, ffn_mine, ffn_other, g_mine, g_other, routes_mine, routes_other, router_ref, own_w, across_w, *refs
):
    routed_mine, routed_other, moved_mine, moved_other = refs[-10:-6]
    x_ref, dh_ref, act_ref, dy_ref, w_ref, sem = refs[-6:]
    own = own_ref[0]

    copies = [
        [
            pltpu.make_async_copy(shards.at[y, e], w_ref.at[e, 2 * y + (own_ref[1] ^ a)], sem.at[a, y, e])
            for a, shards in enumerate((own_w, across_w))
            for y in range(4)
        ]
        for e in range(2)
    ]

    @pl.when(pl.program_id(0) == 0)
    def _():
        for copy in copies[0] + copies[1]:
            copy.start()

    expert_rows = lax.broadcasted_iota(i32, (EXPERTS, TOK), 0)
    slot_rows = lax.broadcasted_iota(i32, (SLOTS, TOK), 0).astype(f32)
    upto = (
        lax.broadcasted_iota(i32, (TOK, TOK), 0) <= lax.broadcasted_iota(i32, (TOK, TOK), 1)
    ).astype(f32).astype(bf16)
    slot_cols = []
    gate_grads = [jnp.zeros((EXPERTS, WIDTH), f32) for _ in range(4)]
    payload_rows = lax.broadcasted_iota(i32, (EXPERTS, WIDTH), 0)
    gate_rows = [[], []]
    picks = [[], []]
    picked_rows = [[], []]
    picked_grads = [[], []]
    blocks = [(ffn_mine, g_mine, routes_mine, 0), (ffn_other, g_other, routes_other, 0)]
    blocks = blocks + [(*refs_of[:3], 1) for refs_of in blocks]
    for rows_ref, grads_ref, routes_ref, n in blocks:
        rows, grads = rows_ref[n], grads_ref[n]
        routes = routes_ref[n][:8, :TOK].astype(f32).astype(i32)
        chosen = expert_rows == routes[0:1]
        for j in range(1, 8):
            chosen = chosen | (expert_rows == routes[j : j + 1])
        named = [jnp.max((routes == own + e).astype(f32), axis=0, keepdims=True) for e in range(2)]
        named = jnp.concatenate(named + [jnp.zeros((6, TOK), f32)], axis=0)
        rank = jnp.dot(named.astype(bf16), upto, preferred_element_type=f32)
        slots = jnp.where(named > 0, rank - 1.0, -1.0)
        slot_cols.append(slots.T)
        logits = lax.dot_general(router_ref[...], rows, NT, preferred_element_type=f32)
        peak = jnp.max(jnp.where(chosen, logits, masked_score), axis=0, keepdims=True)
        raised = jnp.where(chosen, jnp.exp(jnp.minimum(logits - peak, 0.0)), 0.0)
        gates = raised / jnp.sum(raised, axis=0, keepdims=True)
        for e in range(2):
            gate_rows[e].append(
                jnp.sum(jnp.where(expert_rows == own + e, gates, 0.0), axis=0, keepdims=True)
            )
            picks[e].append((slots[e : e + 1] == slot_rows).astype(f32))
        low = jnp.concatenate([picks[0][-1], picks[1][-1]], axis=0).astype(bf16)
        for source, kept in ((rows, picked_rows), (grads, picked_grads)):
            both = jnp.dot(low, source, preferred_element_type=f32)
            kept[0].append(both[:SLOTS])
            kept[1].append(both[SLOTS:])
    moved, routed = [], []
    for e in range(2):

        @pl.when(pl.program_id(0) == 0)
        def _():
            for copy in copies[e]:
                copy.wait()

        w_gate_up = w_ref[e, :, :128, :].reshape(WIDTH, 2 * FF)
        w_down = w_ref[e, :, 128:, :].reshape(FF, WIDTH)
        x = jnp.concatenate(picked_rows[e], axis=0).astype(bf16)
        gate = jnp.concatenate(
            [jnp.sum(p * r, axis=1, keepdims=True) for p, r in zip(picks[e], gate_rows[e])], axis=0
        )
        grads = jnp.concatenate(picked_grads[e], axis=0)
        dy = (gate * grads).astype(bf16)
        mixed = jnp.dot(x, w_gate_up, preferred_element_type=f32)
        dact = lax.dot_general(dy, w_down, NT, preferred_element_type=f32)
        gate_part, up_part = mixed[:, :FF], mixed[:, FF:]
        sigma = 1.0 / (1.0 + jnp.exp(-gate_part))
        silu = gate_part * sigma
        act = (silu * up_part).astype(bf16)
        dh = jnp.concatenate(
            [dact * up_part * (sigma + silu * (1.0 - sigma)), dact * silu], axis=1
        ).astype(bf16)
        x_ref[e] = x
        dy_ref[e] = dy
        act_ref[e] = act
        dh_ref[e] = dh
        returned = jnp.dot(act, w_down, preferred_element_type=f32).astype(bf16).astype(f32)
        dgate = jnp.sum(returned * grads, axis=1, keepdims=True)
        for b in range(4):
            grad = jnp.sum(
                picks[e][b] * dgate[b * SLOTS : (b + 1) * SLOTS], axis=0, keepdims=True
            )
            high = grad.astype(bf16).astype(f32)
            gap = jnp.zeros((1, 256 - TOK), f32)
            wide = jnp.concatenate([high, gap, grad - high, gap, jnp.zeros((1, WIDTH - 512), f32)], axis=1)
            gate_grads[b] = gate_grads[b] + jnp.where(payload_rows == own + e, wide, 0.0)
        moved.append(gate * returned)
        routed.append(lax.dot_general(dh, w_gate_up, NT, preferred_element_type=f32))
    columns = lax.broadcasted_iota(i32, (TOK, 2 * SLOTS), 1).astype(f32)
    outs = [(routed_mine, moved_mine, 0), (routed_other, moved_other, 0), (routed_mine, moved_mine, 1), (routed_other, moved_other, 1)]
    for b, (routed_ref, moved_ref, n) in enumerate(outs):
        first, second = slot_cols[b][:, 0:1], slot_cols[b][:, 1:2]
        back = ((columns == first) | ((columns == second + SLOTS) & (second >= 0))).astype(f32).astype(bf16)
        at = slice(b * SLOTS, (b + 1) * SLOTS)
        for terms, ref in ((routed, routed_ref), (moved, moved_ref)):
            joined = jnp.concatenate([terms[0][at], terms[1][at]], axis=0).astype(bf16)
            ref[n, :TOK, :] = jnp.dot(back, joined, preferred_element_type=f32).astype(bf16)
        routed_ref[n, TOK:, :] = gate_grads[b].astype(bf16)


def run_experts(half, own, ffn, grads, weights, router, before):
    pair = pl.BlockSpec((2, TOK, WIDTH), lambda i, o: (i, 0, 0))
    pair_of_all = pl.BlockSpec((2, TOK, WIDTH), lambda i, o: (i + 2 * half, 0, 0))
    whole = lambda shape: pl.BlockSpec(shape, lambda i, o: (0,) * len(shape))
    routes = pl.BlockSpec((2, 16, 256), lambda i, o: (i, TOK // 16, 0))
    summed = pl.BlockSpec((2, PAY, WIDTH), lambda i, o: (i, 0, 0))
    kept = lambda n: pl.BlockSpec((2, STEP_ROWS, n), lambda i, o: (0, i + 2 * half, 0))
    part = jax.ShapeDtypeStruct((4, PAY, WIDTH), bf16)
    keep = lambda n: jax.ShapeDtypeStruct((2, ALL_ROWS, n), bf16)
    return pl.pallas_call(
        experts_kernel,
        grid_spec=pltpu.PrefetchScalarGridSpec(
            num_scalar_prefetch=1,
            grid=(2,),
            in_specs=[
                pair,
                pair,
                pair,
                pair,
                routes,
                routes,
                whole((EXPERTS, WIDTH)),
            ]
            + [pl.BlockSpec(memory_space=pl.ANY)] * (2 + len(before)),
            out_specs=[
                summed,
                summed,
                pair_of_all,
                pair_of_all,
                kept(WIDTH),
                kept(2 * FF),
                kept(FF),
                kept(WIDTH),
            ],
            scratch_shapes=[
                pltpu.VMEM((2, 8, 192, 1024), bf16),
                pltpu.SemaphoreType.DMA((2, 4, 2)),
            ],
        ),
        out_shape=[
            part,
            part,
            jax.ShapeDtypeStruct((8, TOK, WIDTH), bf16),
            jax.ShapeDtypeStruct((8, TOK, WIDTH), bf16),
            keep(WIDTH),
            keep(2 * FF),
            keep(FF),
            keep(WIDTH),
        ],
        input_output_aliases={10 + i: 2 + i for i in range(len(before))},
        compiler_params=pltpu.CompilerParams(vmem_limit_bytes=VMEM_LIMIT),
        cost_estimate=pl.CostEstimate(
            flops=14 << 30, bytes_accessed=24 << 20, transcendentals=8 * SLOTS * 2 * FF
        ),
    )(own, *ffn, *grads, *grads, router, *weights, *before)


def expert_grads_kernel(x_ref, dh_ref, act_ref, dy_ref, out_ref):
    up = lax.dot_general(x_ref[0], dh_ref[0], TN, preferred_element_type=f32)
    down = lax.dot_general(act_ref[0], dy_ref[0], TN, preferred_element_type=f32)
    out_ref[0, :, 0, :128, :] = up.astype(bf16).reshape(2, 128, 2 * FF)
    out_ref[0, :, 0, 128:, :] = down.astype(bf16).reshape(2, 64, WIDTH)


def expert_weight_grads(x, dh, act, dy):
    return pl.pallas_call(
        expert_grads_kernel,
        grid=(2, 4),
        in_specs=[
            pl.BlockSpec((1, ALL_ROWS, 256), lambda e, i: (e, 0, i)),
            pl.BlockSpec((1, ALL_ROWS, 2 * FF), lambda e, i: (e, 0, 0)),
            pl.BlockSpec((1, ALL_ROWS, 128), lambda e, i: (e, 0, i)),
            pl.BlockSpec((1, ALL_ROWS, WIDTH), lambda e, i: (e, 0, 0)),
        ],
        out_specs=pl.BlockSpec((1, 2, 1, 192, 1024), lambda e, i: (i, 0, e, 0, 0)),
        out_shape=jax.ShapeDtypeStruct((4, 2, 2, 192, 1024), bf16),
        compiler_params=pltpu.CompilerParams(vmem_limit_bytes=VMEM_LIMIT),
        cost_estimate=pl.CostEstimate(flops=8 << 30, bytes_accessed=14 << 20, transcendentals=0),
    )(x, dh, act, dy)


def hidden_kernel(att_ref, w_ref, rows_ref, gain_ref, hidden_ref, normed_ref):
    att = att_ref[...].reshape(WIDTH, TOK)
    hidden = rows_ref[...].astype(f32) + lax.dot_general(
        att, w_ref[:, :WIDTH], TN, preferred_element_type=f32
    )
    hidden_ref[...] = hidden
    normed_ref[...] = (hidden * inverse_rms(hidden) * gain_ref[...]).astype(bf16)


def hidden_of(attended, shared, rows, gain):
    return pl.pallas_call(
        hidden_kernel,
        out_shape=[
            jax.ShapeDtypeStruct((TOK, WIDTH), f32),
            jax.ShapeDtypeStruct((TOK, WIDTH), bf16),
        ],
        compiler_params=pltpu.CompilerParams(vmem_limit_bytes=VMEM_LIMIT),
        cost_estimate=pl.CostEstimate(
            flops=2 * TOK * WIDTH * WIDTH, bytes_accessed=5 << 20, transcendentals=0
        ),
    )(attended, shared, rows, gain)


def hidden_back_kernel(
    t0, t1, t2, t3, crossed, hidden_ref, normed_ref, chosen_ref, router_ref, g_ref, gain_ref,
    w_ref, hidden_grad_ref, branch_ref, logit_ref, scaled_ref, att_ref
):
    chosen = chosen_ref[...] > 0
    logits = lax.dot_general(router_ref[...], normed_ref[...], NT, preferred_element_type=f32)
    peak = jnp.max(jnp.where(chosen, logits, masked_score), axis=0, keepdims=True)
    raised = jnp.where(chosen, jnp.exp(jnp.minimum(logits - peak, 0.0)), 0.0)
    gates = raised / jnp.sum(raised, axis=0, keepdims=True)
    summed = t0[...].astype(f32)
    for term in (t1, t2, t3, crossed):
        summed = summed + term[...].astype(f32)
    gate_grad = summed[TOK:, :TOK] + summed[TOK:, 256 : 256 + TOK]
    logit_grad = gates * (gate_grad - jnp.sum(gates * gate_grad, axis=0, keepdims=True))
    logit_grad = logit_grad.astype(bf16)
    logit_ref[...] = logit_grad
    normed_grad = summed[:TOK] + lax.dot_general(
        logit_grad, router_ref[...], TN, preferred_element_type=f32
    )
    hidden = hidden_ref[...]
    scale = inverse_rms(hidden)
    scaled_ref[...] = (normed_grad * hidden * scale).astype(bf16)
    hidden_grad = g_ref[...].astype(f32) + rms_pull(hidden, scale, gain_ref[...], normed_grad)
    hidden_grad_ref[...] = hidden_grad
    branch = hidden_grad.astype(bf16)
    branch_ref[...] = branch
    att = lax.dot_general(w_ref[:, :WIDTH], branch, NT, preferred_element_type=f32)
    att_ref[...] = att.astype(bf16).reshape(HEADS, HEAD_DIM, TOK)


def hidden_back(terms, crossed, hidden, normed, chosen, router_t, g, gain, shared):
    wide = lambda t: jax.ShapeDtypeStruct((TOK, WIDTH), t)
    return pl.pallas_call(
        hidden_back_kernel,
        out_shape=[
            wide(f32),
            wide(bf16),
            jax.ShapeDtypeStruct((EXPERTS, TOK), bf16),
            wide(bf16),
            jax.ShapeDtypeStruct((HEADS, HEAD_DIM, TOK), bf16),
        ],
        compiler_params=pltpu.CompilerParams(vmem_limit_bytes=VMEM_LIMIT),
        cost_estimate=pl.CostEstimate(
            flops=2 * TOK * WIDTH * WIDTH, bytes_accessed=8 << 20, transcendentals=0
        ),
    )(*terms, crossed, hidden, normed, chosen, router_t, g, gain, shared)


def shared_grads_kernel(att_ref, branch_ref, normed_ref, logit_ref, scaled_ref, out_ref):
    over_tokens = (((0,), (1,)), ((), ()))
    logit = jnp.concatenate([logit_ref[...], jnp.zeros((96, TOK), bf16)], axis=0)
    ones = (lax.broadcasted_iota(i32, (128, TOK), 0) == EXPERTS).astype(f32).astype(bf16)
    att = att_ref[...].reshape(WIDTH, TOK)
    grads = [
        jnp.dot(att, branch_ref[...], preferred_element_type=f32),
        lax.dot_general(normed_ref[...], logit, over_tokens, preferred_element_type=f32)
        + lax.dot_general(scaled_ref[...], ones, over_tokens, preferred_element_type=f32),
    ]
    for w in range(8):
        for part, at in zip(grads, (slice(0, WIDTH), slice(WIDTH, None))):
            rows = [part[s * 64 + w * 8 : s * 64 + w * 8 + 8] for s in range(16)]
            out_ref[w, :, at] = jnp.concatenate(rows, axis=0).astype(bf16)


def shared_weight_grads(att, branch, normed, logit_grad, scaled):
    return pl.pallas_call(
        shared_grads_kernel,
        out_shape=jax.ShapeDtypeStruct((8, 128, 1152), bf16),
        compiler_params=pltpu.CompilerParams(vmem_limit_bytes=VMEM_LIMIT),
        cost_estimate=pl.CostEstimate(
            flops=2 * TOK * WIDTH * 1280, bytes_accessed=5 << 20, transcendentals=0
        ),
    )(att, branch, normed, logit_grad, scaled)


def local(
    tokens,
    routes,
    cont_lengths,
    norm_attn,
    w_qkv,
    w_out,
    w_router,
    norm_ffn,
    w_gate_up,
    w_down,
    cotangent,
):
    seq_index = lax.axis_index("seq")
    places, blocks = relative_places(seq_index)
    rows = tokens[0]
    query_width = HEADS * HEAD_DIM
    kv_width = KV_HEADS * HEAD_DIM

    position, begin = group_layout(cont_lengths[0])
    begin = begin[None]
    table = rotary_table(position.astype(f32))
    kv_heads = lambda start: jnp.repeat(
        w_qkv[:, start : start + kv_width].reshape(8, KV_HEADS, HEAD_DIM), 2, axis=1
    )
    head_cols = jnp.concatenate(
        [
            w_qkv[:, :query_width].reshape(8, HEADS, HEAD_DIM),
            kv_heads(query_width),
            kv_heads(query_width + kv_width),
            jnp.broadcast_to(norm_attn[:, None, None], (8, HEADS, HEAD_DIM)),
        ],
        axis=2,
    ).transpose(1, 0, 2)
    head_cols = jnp.broadcast_to(head_cols[:, None], (HEADS, 8, 8, 256)).reshape(128, 8, 256)
    head_weights = lax.all_to_all(head_cols, BOTH, 0, 0, tiled=True).reshape(WIDTH, 256)
    gain_attn = head_weights[:, 192].astype(f32)[None]
    head_weights = jnp.where(jnp.arange(256)[None] < 192, head_weights, 0.0).astype(bf16)

    rows_near, rows_across = gather_near(rows)
    rows_near, _, table, head_weights = tie(rows_near, rows_across, table, head_weights)
    rows_near, rows_far = both_cores(rows_near), gather_far(rows_across)

    own_x = lax.axis_index("wshard") % 2
    expert_rows = jnp.concatenate([w_gate_up, w_down], axis=1)
    along_y = lambda t: lax.all_gather(t, "wshard", axis_index_groups=ALONG_Y, axis=0)
    experts, expert_rows = along_y(expert_rows), swap_x(expert_rows)

    qkv = project(places[:8], rows_near, head_weights, gain_attn, table, ())
    shared = jnp.concatenate(
        [w_out, w_router, norm_ffn[:, None], jnp.zeros((8, 95), bf16)], axis=1
    )
    shared, qkv = tie(shared, qkv)
    shared = lax.all_to_all(
        jnp.broadcast_to(shared[None], (128, 8, 1152)), BOTH, 0, 0, tiled=True
    ).reshape(WIDTH, 1152)
    routes_rows = jnp.pad(routes[0].T.astype(bf16), ((0, 8), (0, WIDTH - TOK)))
    upstream_rows = jnp.concatenate([cotangent[0], routes_rows], axis=0)
    rows_far, qkv, upstream_rows, expert_rows = tie(rows_far, qkv, upstream_rows, expert_rows)
    experts = [experts, along_y(expert_rows)]
    rows_far = both_cores(rows_far)
    grad_near = [upstream_rows] + [send(upstream_rows, 0, b) for b in (1, 3, 2)]
    qkv = project(places[8:], rows_far, head_weights, gain_attn, table, (qkv,))

    router_t = shared[:, WIDTH : WIDTH + EXPERTS].T
    gain_ffn = shared[:, WIDTH + EXPERTS].astype(f32)[None]
    attended_head, attended_t, lse = attend(qkv, begin)
    attended_head, shared = tie(attended_head, shared)
    attended = lax.all_to_all(attended_head, "seq", 0, 0, tiled=True)
    attended, grad_near = tie(attended, grad_near)
    grad_near = jnp.stack(grad_near)
    grad_rows = grad_near.reshape(-1, WIDTH)
    grad_far = [send(grad_rows[:EARLY], 1, 0)]
    hidden, normed_ffn = hidden_of(attended, shared, rows, gain_ffn)
    ffn_near, ffn_across = gather_near(normed_ffn)
    grad_rows, _ = tie(grad_rows, ffn_across)
    ffn_near, _, grad_far[0] = tie(ffn_near, ffn_across, grad_far[0])
    grad_far.append(send(grad_rows[EARLY:], 1, 0))
    grad_near = (grad_near, swap_cores(grad_near))
    ffn_near, ffn_far = both_cores(ffn_near), gather_far(ffn_across)
    own = jnp.stack([seq_index * 2, own_x])
    near = run_experts(0, own, ffn_near, grad_near, experts, router_t, ())
    near_terms = sum_along_z(*near[:2])
    ffn_far = both_cores(ffn_far)
    grad_far = jnp.concatenate(grad_far, axis=0).reshape(grad_near[0].shape)
    grad_far = (grad_far, swap_cores(grad_far))
    far = run_experts(1, own, ffn_far, grad_far, experts, router_t, near[2:])
    far, near_terms = tie(far, near_terms)
    moved, saved = far[2:4], far[4:]
    far_other, moved_other = tie(swap_cores(far[1]), moved[1])
    far_terms = send_along_z(chip_parts(far[0], far_other))
    expert_grads = expert_weight_grads(*saved)
    moved_other = swap_cores(moved_other)
    far_terms, expert_grads, moved_other = tie(far_terms, expert_grads, moved_other)
    crossed = send(add_low(*far_terms), 1, 0)
    by_x = [t.reshape(2, 4, TOK, WIDTH) for t in (moved[0], moved_other)]
    moved_parts = [add_low(by_x[0][:, i], by_x[1][:, i]) for i in range(4)]
    crossed, moved_parts = tie(crossed, moved_parts)

    expert_range = jnp.arange(EXPERTS, dtype=i32)
    chosen_here = jnp.any(routes[0].T[None] == expert_range[:, None, None], axis=1).astype(f32)
    hidden_grad, branch_grad, logit_grad, scaled_grad, attended_grad = hidden_back(
        near_terms, crossed, hidden, normed_ffn, chosen_here, router_t, cotangent[0], gain_ffn, shared
    )
    expert_grads = lax.psum_scatter(
        expert_grads.reshape(8, 2, 192, 1024),
        "wshard",
        axis_index_groups=ALONG_Y,
        scatter_dimension=0,
        tiled=True,
    )
    head_grad = lax.all_to_all(attended_grad, "seq", 0, 0, tiled=True)
    shared_grads = shared_weight_grads(attended, branch_grad, normed_ffn, logit_grad, scaled_grad)
    head_grad, shared_grads, moved_parts = tie(head_grad, shared_grads, moved_parts)
    moved_terms = [moved_parts[0]] + [
        send(moved_parts[i], 0, -b) for i, b in ((1, 1), (2, 3), (3, 2))
    ]

    shared_grads = lax.all_to_all(shared_grads, "wshard", 0, 0, tiled=True)
    projected_grad = attend_back(qkv, head_grad, attended_t, lse, begin, table)
    grad_head = head_weight_grad(places, rows_near, rows_far, gain_attn, projected_grad)
    shared_grads, grad_head, projected_grad = tie(shared_grads, grad_head, projected_grad)
    shared_grads = jnp.sum(shared_grads.astype(f32), axis=0)
    far_part = project_back(places[8:], projected_grad, head_weights, shared_grads)
    near_part = project_back(places[:8], projected_grad, head_weights, shared_grads)
    far_parts = chip_parts(far_part[0], swap_cores(far_part[1]))
    near_part, moved_terms, expert_grads = tie(near_part, moved_terms, expert_grads)
    near_parts = chip_parts(near_part[0], swap_cores(near_part[1]))
    far_parts, near_parts, grad_head, moved_terms, expert_grads = tie(
        far_parts, near_parts, grad_head, moved_terms, expert_grads
    )
    far_terms = send_along_z(far_parts)
    near_terms = send_along_z(near_parts)
    moved_crossed = send(add_low(*[t[1] for t in moved_terms]), 1, 0)
    grad_heads = lax.all_to_all(grad_head.reshape(128, 8, 256), BOTH, 0, 0, tiled=True)
    crossed = send(add_low(*far_terms), 1, 0)
    crossed, near_terms, grad_heads = tie(crossed, near_terms, grad_heads)
    kept = lax.dynamic_index_in_dim(expert_grads, own_x, 0, keepdims=False)
    sent = lax.dynamic_index_in_dim(expert_grads, 1 - own_x, 0, keepdims=False)
    expert_grads = kept.astype(f32) + swap_x(sent).astype(f32)
    total = lambda terms: sum([t.astype(f32) for t in terms])
    output = (hidden + total([t[0] for t in moved_terms] + [moved_crossed])).astype(bf16)
    last_sum = total(near_terms + [crossed])
    normed_grad, shared_grads = last_sum[:TOK], last_sum[TOK:]
    grad_heads = jnp.sum(grad_heads.reshape(16, 8, 8, 256).astype(f32), axis=1).transpose(1, 0, 2)
    kv_sum = lambda start: jnp.sum(
        grad_heads[:, :, start : start + HEAD_DIM].reshape(8, KV_HEADS, 2, HEAD_DIM), axis=2
    ).reshape(8, kv_width)
    grad_qkv = jnp.concatenate(
        [grad_heads[:, :, :HEAD_DIM].reshape(8, query_width), kv_sum(HEAD_DIM), kv_sum(2 * HEAD_DIM)],
        axis=1,
    )
    grad_norm_attn = jnp.sum(grad_qkv * w_qkv.astype(f32), axis=1) / norm_attn.astype(f32)
    inputs = rows.astype(f32)
    grad_input = hidden_grad + rms_pull(inputs, inverse_rms(inputs), gain_attn, normed_grad)
    return (
        output[None],
        grad_input[None],
        grad_norm_attn,
        grad_qkv,
        shared_grads[:8],
        shared_grads[8:, :EXPERTS],
        shared_grads[8:, EXPERTS],
        expert_grads[:, :128],
        expert_grads[:, 128:],
    )


def solution(mesh):
    return jax.shard_map(
        local,
        mesh=mesh,
        in_specs=(
            P("wshard", "seq", None),
            P("wshard", "seq", None),
            P("wshard", None),
            P(BOTH),
            P(BOTH, None),
            P(BOTH, None),
            P(BOTH, None),
            P(BOTH),
            P("seq", "wshard", None),
            P("seq", "wshard", None),
            P("wshard", "seq", None),
        ),
        out_specs=(
            P("wshard", "seq", None),
            P("wshard", "seq", None),
            P(BOTH),
            P(BOTH, None),
            P(BOTH, None),
            P(BOTH, None),
            P(BOTH),
            P("seq", "wshard", None),
            P("seq", "wshard", None),
        ),
        check_vma=False,
    )
```

```python
import jax
import jax.numpy as jnp
from jax import lax
from jax.experimental import pallas as pl
from jax.experimental.pallas import tpu as pltpu
from jax.sharding import PartitionSpec as P

HEADS = 16
KV_HEADS = 8
HEAD_DIM = 64
EXPERTS = 32
FF = 512
PROMPT = 2048
GROUP = 3584
TOK = 224
WIDTH = 1024
SLOTS = 72
STEP_ROWS = 4 * SLOTS
ALL_ROWS = 16 * SLOTS
BLOCK = 512
VMEM_LIMIT = 60 << 20
LAST = TOK + 16
EARLY = 352
PAY = TOK + 32

norm_eps = 1e-06
rope_base = 10000.0
masked_score = -1e30
BOTH = ("seq", "wshard")
NT = (((1,), (1,)), ((), ()))
TN = (((0,), (0,)), ((), ()))
f32 = jnp.float32
bf16 = jnp.bfloat16
i32 = jnp.int32


def place_of(x, z, core):
    return x * 8 + z * 2 + core


def shift_perm(a, b):
    return [
        (place_of(x, z, c), place_of(x ^ a, (z + b) % 4, c))
        for x in range(2)
        for z in range(4)
        for c in range(2)
    ]


CORE_PERM = [(i, i ^ 1) for i in range(16)]


def send(rows, a, b):
    return lax.ppermute(rows, "seq", shift_perm(a, b))


def swap_cores(rows):
    return lax.ppermute(rows, "seq", CORE_PERM)


def relative_places(seq_index):
    x, z, c = seq_index // 8, (seq_index // 2) % 4, seq_index % 2
    r = jnp.arange(16, dtype=i32)
    a, i, k = r // 8, (r // 2) % 4, r % 2
    shift = i ^ (i // 2)
    behind = (z - i) % 4
    places = (a ^ x) * 8 + ((z - shift) % 4) * 2 + (k ^ c)
    return places, (a ^ x) * 8 + (behind ^ (behind // 2)) * 2 + (k ^ c)


def gather_near(rows):
    return [rows] + [send(rows, 0, b) for b in (1, 3, 2)], send(rows, 1, 0)


def both_cores(parts):
    mine = jnp.stack(parts)
    return mine, swap_cores(mine)


def gather_far(across):
    return [across] + [send(across, 0, b) for b in (1, 3, 2)]


def add_low(*terms):
    return sum([t.astype(f32) for t in terms]).astype(bf16)


def sum_along_z(mine, other):
    return send_along_z(chip_parts(mine, swap_cores(other)))


def chip_parts(mine, got):
    return [add_low(mine[i], got[i]) for i in range(4)]


def send_along_z(parts):
    return [parts[0]] + [send(parts[i], 0, -b) for i, b in ((1, 1), (2, 3), (3, 2))]


def swap_x(rows):
    return lax.ppermute(rows, "wshard", [(w, w ^ 1) for w in range(8)])


ALONG_Y = [[y * 2 + x for y in range(4)] for x in range(2)]


def tie(*values):
    return lax.optimization_barrier(values)


def inverse_rms(values):
    return lax.rsqrt(jnp.mean(values * values, axis=-1, keepdims=True) + norm_eps)


def rms_pull(values, scale, gain, grad):
    scaled = grad * gain
    return scale * scaled - values * (scale * scale * scale) * jnp.mean(
        scaled * values, axis=-1, keepdims=True
    )


def group_layout(lengths):
    places = jnp.arange(GROUP, dtype=i32)
    ends = jnp.cumsum(lengths)
    starts = ends - lengths
    offset_in = places - PROMPT
    segment_id = jnp.sum((offset_in[:, None] >= ends[None, :]).astype(i32), axis=1)
    segment_hot = segment_id[:, None] == jnp.arange(lengths.shape[0], dtype=i32)[None, :]
    begin = jnp.sum(jnp.where(segment_hot, starts[None, :], 0), axis=1)
    inside = offset_in >= 0
    position = jnp.where(inside, PROMPT + offset_in - begin, places)
    return position, jnp.where(inside, PROMPT + begin, 0)


def rotary_table(position):
    half_dim = HEAD_DIM // 2
    inverse = rope_base ** (-((jnp.arange(2 * HEAD_DIM) % half_dim).astype(f32) * 2.0) / HEAD_DIM)
    back = jnp.where(jnp.arange(2 * HEAD_DIM) < HEAD_DIM, 0.0, 0.5 * jnp.pi).astype(f32)
    return jnp.cos(position[:, None] * inverse[None, :] - back[None, :])


def turn(values):
    half_dim = HEAD_DIM // 2
    return jnp.concatenate([-values[:, half_dim:], values[:, :half_dim]], axis=-1)


def turn_back(values):
    half_dim = HEAD_DIM // 2
    return jnp.concatenate([values[:, half_dim:], -values[:, :half_dim]], axis=-1)


def project_kernel(places, mine, other, w, gain, table, *refs):
    out = refs[-1]
    j = pl.program_id(0)

    if len(refs) > 1:

        @pl.when(j == 0)
        def _():
            out[...] = refs[0][...]

    for k, ref in enumerate((mine, other)):
        at = pl.ds(pl.multiple_of(places[2 * j + k] * TOK, TOK), TOK)
        rows = ref[0].astype(f32)
        normed = (rows * inverse_rms(rows) * gain[...]).astype(bf16)
        projected = jnp.dot(normed, w[...], preferred_element_type=f32)
        c, s = table[at, :HEAD_DIM], table[at, HEAD_DIM:]
        q, k, v = projected[:, :64], projected[:, 64:128], projected[:, 128:]
        q = (q * c + turn(q) * s).astype(bf16).astype(f32) * HEAD_DIM**-0.5
        out[at, :] = jnp.concatenate([q, k * c + turn(k) * s, v], axis=1).astype(bf16)


def project(places, gathered, w, gain, table, before):
    chip = pl.BlockSpec((1, TOK, WIDTH), lambda j, p: (j, 0, 0))
    whole = lambda *shape: pl.BlockSpec(shape, lambda j, p: (0,) * len(shape))
    return pl.pallas_call(
        project_kernel,
        grid_spec=pltpu.PrefetchScalarGridSpec(
            num_scalar_prefetch=1,
            grid=(4,),
            in_specs=[chip, chip, whole(WIDTH, 256), whole(1, WIDTH), whole(GROUP, 128)]
            + [whole(GROUP, 256)] * len(before),
            out_specs=whole(GROUP, 256),
        ),
        out_shape=jax.ShapeDtypeStruct((GROUP, 256), bf16),
        compiler_params=pltpu.CompilerParams(vmem_limit_bytes=VMEM_LIMIT),
        cost_estimate=pl.CostEstimate(
            flops=2 * 8 * TOK * WIDTH * 256, bytes_accessed=10 << 20, transcendentals=0
        ),
    )(places, *gathered, w, gain, table, *before)


def project_back_kernel(places, first, second, w, first_shared, second_shared, mine, other):
    del places
    for projected, shared, out in ((first, first_shared, mine), (second, second_shared, other)):
        out[0, :TOK, :] = lax.dot_general(
            projected[...], w[...], NT, preferred_element_type=f32
        ).astype(bf16)
        rest = jnp.concatenate([shared[:, WIDTH:], jnp.zeros((8, WIDTH - 128), f32)], axis=1)
        out[0, TOK:, :] = jnp.concatenate([shared[:, :WIDTH], rest], axis=0).astype(bf16)


def project_back(places, projected_grad, w, shared):
    chip = pl.BlockSpec((1, LAST, WIDTH), lambda j, p: (j, 0, 0))
    at = lambda k, rows, n: pl.BlockSpec((rows, n), lambda j, p: (p[2 * j + k], 0))
    part = jax.ShapeDtypeStruct((4, LAST, WIDTH), bf16)
    return pl.pallas_call(
        project_back_kernel,
        grid_spec=pltpu.PrefetchScalarGridSpec(
            num_scalar_prefetch=1,
            grid=(4,),
            in_specs=[
                at(0, TOK, 256),
                at(1, TOK, 256),
                pl.BlockSpec((WIDTH, 256), lambda j, p: (0, 0)),
                at(0, 8, 1152),
                at(1, 8, 1152),
            ],
            out_specs=[chip, chip],
        ),
        out_shape=[part, part],
        compiler_params=pltpu.CompilerParams(vmem_limit_bytes=VMEM_LIMIT),
        cost_estimate=pl.CostEstimate(
            flops=2 * 8 * TOK * WIDTH * 256, bytes_accessed=5 << 20, transcendentals=0
        ),
    )(places, projected_grad, projected_grad, w, shared, shared)


def head_grad_kernel(places, near_mine, near_other, far_mine, far_other, gain, first, second, out, total):
    del places
    j = pl.program_id(0)

    @pl.when(j == 0)
    def _():
        total[...] = jnp.zeros_like(total)

    for near, far, projected in ((near_mine, far_mine, first), (near_other, far_other, second)):
        rows = jnp.where(j < 4, near[0], far[0]).astype(f32)
        normed = (rows * inverse_rms(rows) * gain[...]).astype(bf16)
        total[...] += lax.dot_general(normed, projected[...], TN, preferred_element_type=f32)

    @pl.when(j == 7)
    def _():
        out[...] = total[...].astype(bf16)


def head_weight_grad(places, near, far, gain, projected_grad):
    near_chip = pl.BlockSpec((1, TOK, WIDTH), lambda j, p: (jnp.minimum(j, 3), 0, 0))
    far_chip = pl.BlockSpec((1, TOK, WIDTH), lambda j, p: (jnp.maximum(j - 4, 0), 0, 0))
    at = lambda k: pl.BlockSpec((TOK, 256), lambda j, p: (p[2 * j + k], 0))
    return pl.pallas_call(
        head_grad_kernel,
        grid_spec=pltpu.PrefetchScalarGridSpec(
            num_scalar_prefetch=1,
            grid=(8,),
            in_specs=[
                near_chip,
                near_chip,
                far_chip,
                far_chip,
                pl.BlockSpec((1, WIDTH), lambda j, p: (0, 0)),
                at(0),
                at(1),
            ],
            out_specs=pl.BlockSpec((WIDTH, 256), lambda j, p: (0, 0)),
            scratch_shapes=[pltpu.VMEM((WIDTH, 256), f32)],
        ),
        out_shape=jax.ShapeDtypeStruct((WIDTH, 256), bf16),
        compiler_params=pltpu.CompilerParams(vmem_limit_bytes=VMEM_LIMIT),
        cost_estimate=pl.CostEstimate(
            flops=2 * 16 * TOK * WIDTH * 256, bytes_accessed=10 << 20, transcendentals=0
        ),
    )(places, *near, *far, gain, projected_grad, projected_grad)


def tile_mask(scores, key_start, query_start, begin):
    keys = key_start + lax.broadcasted_iota(i32, scores.shape, 0)
    queries = query_start + lax.broadcasted_iota(i32, scores.shape, 1)
    return jnp.where((keys <= queries) & (keys >= begin), scores, masked_score)


def key_ranges(i):
    first = PROMPT // BLOCK
    return jnp.where(i > first, i - 1, i), jnp.minimum(i, first)


def attend_kernel(qkv_ref, begin_ref, o_ref, ot_ref, lse_ref, keys, vt):
    i = pl.program_id(0)
    here = pl.ds(pl.multiple_of(i * BLOCK, BLOCK), BLOCK)

    @pl.when(i == 0)
    def _():
        keys[...] = qkv_ref[:, 64:128]
        vt[...] = qkv_ref[:, 128:192].T

    q = qkv_ref[here, :64]
    begin = begin_ref[...]

    def tile(j, carry, masked, n=1):
        peak, total, out = carry
        start = pl.multiple_of(j * BLOCK, BLOCK)
        at = pl.ds(start, n * BLOCK)
        s = lax.dot_general(keys[at, :], q, NT, preferred_element_type=f32)
        if masked:
            s = tile_mask(s, start, i * BLOCK, begin)
        higher = jnp.maximum(peak, jnp.max(s, axis=0, keepdims=True))
        p = jnp.exp(s - higher)
        fade = jnp.exp(peak - higher)
        total = total * fade + jnp.sum(p, axis=0, keepdims=True)
        out = out * fade + jnp.dot(vt[:, at], p.astype(bf16), preferred_element_type=f32)
        return higher, total, out

    carry = (
        jnp.full((1, BLOCK), masked_score, f32),
        jnp.zeros((1, BLOCK), f32),
        jnp.zeros((HEAD_DIM, BLOCK), f32),
    )
    carry = tile(i, carry, True)
    window, shared = key_ranges(i)
    carry = lax.fori_loop(window, i, lambda j, c: tile(j, c, True), carry)
    pairs = shared // 2
    carry = lax.fori_loop(0, pairs, lambda j, c: tile(2 * j, c, False, 2), carry)
    peak, total, out = lax.fori_loop(2 * pairs, shared, lambda j, c: tile(j, c, False), carry)
    ot_ref[:, here] = out * (1.0 / total)
    lse_ref[...] = peak + jnp.log(total)

    @pl.when(i == GROUP // BLOCK - 1)
    def _():
        for b in range(16):
            o_ref[b] = ot_ref[:, b * TOK : (b + 1) * TOK].astype(bf16)


def attend(qkv, begin):
    whole = lambda *shape: pl.BlockSpec(shape, lambda i: (0,) * len(shape))
    cols = lambda n: pl.BlockSpec((n, BLOCK), lambda i: (0, i))
    return pl.pallas_call(
        attend_kernel,
        grid=(GROUP // BLOCK,),
        in_specs=[whole(GROUP, 256), cols(1)],
        out_specs=[whole(16, HEAD_DIM, TOK), whole(HEAD_DIM, GROUP), cols(1)],
        out_shape=[
            jax.ShapeDtypeStruct((16, HEAD_DIM, TOK), bf16),
            jax.ShapeDtypeStruct((HEAD_DIM, GROUP), f32),
            jax.ShapeDtypeStruct((1, GROUP), f32),
        ],
        scratch_shapes=[
            pltpu.VMEM((GROUP, HEAD_DIM), bf16),
            pltpu.VMEM((HEAD_DIM, GROUP), bf16),
        ],
        compiler_params=pltpu.CompilerParams(vmem_limit_bytes=VMEM_LIMIT),
        cost_estimate=pl.CostEstimate(
            flops=2 * 27 * BLOCK * BLOCK * 512, bytes_accessed=4 << 20, transcendentals=27 * BLOCK * BLOCK
        ),
    )(qkv, begin)


def attend_back_kernel(
    qkv_ref, g_ref, ot_ref, lse_ref, begin_ref, table, out_ref, keys, values, kt, gt, dq, dk, dv
):
    i = pl.program_id(0)
    here = pl.ds(pl.multiple_of(i * BLOCK, BLOCK), BLOCK)

    @pl.when(i == 0)
    def _():
        dk[...] = jnp.zeros_like(dk)
        dv[...] = jnp.zeros_like(dv)
        keys[...] = qkv_ref[:, 64:128]
        values[...] = qkv_ref[:, 128:192]
        kt[...] = qkv_ref[:, 64:128].T
        for b in range(16):
            gt[:, b * TOK : (b + 1) * TOK] = g_ref[b]

    q = qkv_ref[here, :64]
    g = gt[:, here]
    begin = begin_ref[...]
    lse = lse_ref[...]
    inner = jnp.sum(g.astype(f32) * ot_ref[...], axis=0, keepdims=True)

    def tile(j, dq, masked, n=1):
        start = pl.multiple_of(j * BLOCK, BLOCK)
        at = pl.ds(start, n * BLOCK)
        s = lax.dot_general(keys[at, :], q, NT, preferred_element_type=f32)
        if masked:
            s = tile_mask(s, start, i * BLOCK, begin)
        p = jnp.exp(s - lse)
        dp = jnp.dot(values[at, :], g, preferred_element_type=f32)
        ds = (p * (dp - inner)).astype(bf16)
        dv[at, :] += lax.dot_general(p.astype(bf16), g, NT, preferred_element_type=f32)
        dk[at, :] += jnp.dot(ds, q, preferred_element_type=f32)
        return dq + jnp.dot(kt[:, at], ds, preferred_element_type=f32)

    dqt = tile(i, jnp.zeros((HEAD_DIM, BLOCK), f32), True)
    window, shared = key_ranges(i)
    dqt = lax.fori_loop(window, i, lambda j, c: tile(j, c, True), dqt)
    pairs = shared // 2
    dqt = lax.fori_loop(0, pairs, lambda j, c: tile(2 * j, c, False, 2), dqt)
    dqt = lax.fori_loop(2 * pairs, shared, lambda j, c: tile(j, c, False), dqt)
    dq[here, :] = dqt.T * HEAD_DIM**-0.5

    @pl.when(i == GROUP // BLOCK - 1)
    def _():
        def back(b, _):
            at = pl.ds(pl.multiple_of(b * BLOCK, BLOCK), BLOCK)
            c, s = table[at, :HEAD_DIM], table[at, HEAD_DIM:]
            q, k = dq[at, :].astype(bf16).astype(f32), dk[at, :].astype(bf16).astype(f32)
            parts = [q * c + turn_back(q * s), k * c + turn_back(k * s), dv[at, :], jnp.zeros_like(q)]
            out_ref[at, :] = jnp.concatenate(parts, axis=1).astype(bf16)
            return 0

        lax.fori_loop(0, GROUP // BLOCK, back, 0)


def attend_back(qkv, g, ot, lse, begin, table):
    whole = lambda *shape: pl.BlockSpec(shape, lambda i: (0,) * len(shape))
    cols = lambda n: pl.BlockSpec((n, BLOCK), lambda i: (0, i))
    return pl.pallas_call(
        attend_back_kernel,
        grid=(GROUP // BLOCK,),
        in_specs=[
            whole(GROUP, 256),
            whole(16, HEAD_DIM, TOK),
            cols(HEAD_DIM),
            cols(1),
            cols(1),
            whole(GROUP, 128),
        ],
        out_specs=whole(GROUP, 256),
        out_shape=jax.ShapeDtypeStruct((GROUP, 256), bf16),
        scratch_shapes=[
            pltpu.VMEM((GROUP, HEAD_DIM), bf16),
            pltpu.VMEM((GROUP, HEAD_DIM), bf16),
            pltpu.VMEM((HEAD_DIM, GROUP), bf16),
            pltpu.VMEM((HEAD_DIM, GROUP), bf16),
            pltpu.VMEM((GROUP, HEAD_DIM), f32),
            pltpu.VMEM((GROUP, HEAD_DIM), f32),
            pltpu.VMEM((GROUP, HEAD_DIM), f32),
        ],
        compiler_params=pltpu.CompilerParams(vmem_limit_bytes=VMEM_LIMIT),
        cost_estimate=pl.CostEstimate(
            flops=5 * 27 * BLOCK * BLOCK * 512, bytes_accessed=8 << 20, transcendentals=27 * BLOCK * BLOCK
        ),
    )(qkv, g, ot, lse, begin, table)


def experts_kernel(
    own_ref, ffn_mine, ffn_other, g_mine, g_other, routes_mine, routes_other, router_ref, own_w, across_w, *refs
):
    routed_mine, routed_other, moved_mine, moved_other = refs[-10:-6]
    x_ref, dh_ref, act_ref, dy_ref, w_ref, sem = refs[-6:]
    own = own_ref[0]

    copies = [
        [
            pltpu.make_async_copy(shards.at[y, e], w_ref.at[e, 2 * y + (own_ref[1] ^ a)], sem.at[a, y, e])
            for a, shards in enumerate((own_w, across_w))
            for y in range(4)
        ]
        for e in range(2)
    ]

    @pl.when(pl.program_id(0) == 0)
    def _():
        for copy in copies[0] + copies[1]:
            copy.start()

    expert_rows = lax.broadcasted_iota(i32, (EXPERTS, TOK), 0)
    slot_rows = lax.broadcasted_iota(i32, (SLOTS, TOK), 0).astype(f32)
    upto = (
        lax.broadcasted_iota(i32, (TOK, TOK), 0) <= lax.broadcasted_iota(i32, (TOK, TOK), 1)
    ).astype(f32).astype(bf16)
    slot_cols = []
    gate_grads = [jnp.zeros((EXPERTS, WIDTH), f32) for _ in range(4)]
    payload_rows = lax.broadcasted_iota(i32, (EXPERTS, WIDTH), 0)
    gate_rows = [[], []]
    picks = [[], []]
    picked_rows = [[], []]
    picked_grads = [[], []]
    blocks = [(ffn_mine, g_mine, routes_mine, 0), (ffn_other, g_other, routes_other, 0)]
    blocks = blocks + [(*refs_of[:3], 1) for refs_of in blocks]
    for rows_ref, grads_ref, routes_ref, n in blocks:
        rows, grads = rows_ref[n], grads_ref[n]
        routes = routes_ref[n][:8, :TOK].astype(f32).astype(i32)
        chosen = expert_rows == routes[0:1]
        for j in range(1, 8):
            chosen = chosen | (expert_rows == routes[j : j + 1])
        named = [jnp.max((routes == own + e).astype(f32), axis=0, keepdims=True) for e in range(2)]
        named = jnp.concatenate(named + [jnp.zeros((6, TOK), f32)], axis=0)
        rank = jnp.dot(named.astype(bf16), upto, preferred_element_type=f32)
        slots = jnp.where(named > 0, rank - 1.0, -1.0)
        slot_cols.append(slots.T)
        logits = lax.dot_general(router_ref[...], rows, NT, preferred_element_type=f32)
        peak = jnp.max(jnp.where(chosen, logits, masked_score), axis=0, keepdims=True)
        raised = jnp.where(chosen, jnp.exp(jnp.minimum(logits - peak, 0.0)), 0.0)
        gates = raised / jnp.sum(raised, axis=0, keepdims=True)
        for e in range(2):
            gate_rows[e].append(
                jnp.sum(jnp.where(expert_rows == own + e, gates, 0.0), axis=0, keepdims=True)
            )
            picks[e].append((slots[e : e + 1] == slot_rows).astype(f32))
        low = jnp.concatenate([picks[0][-1], picks[1][-1]], axis=0).astype(bf16)
        for source, kept in ((rows, picked_rows), (grads, picked_grads)):
            both = jnp.dot(low, source, preferred_element_type=f32)
            kept[0].append(both[:SLOTS])
            kept[1].append(both[SLOTS:])
    moved, routed = [], []
    for e in range(2):

        @pl.when(pl.program_id(0) == 0)
        def _():
            for copy in copies[e]:
                copy.wait()

        w_gate_up = w_ref[e, :, :128, :].reshape(WIDTH, 2 * FF)
        w_down = w_ref[e, :, 128:, :].reshape(FF, WIDTH)
        x = jnp.concatenate(picked_rows[e], axis=0).astype(bf16)
        gate = jnp.concatenate(
            [jnp.sum(p * r, axis=1, keepdims=True) for p, r in zip(picks[e], gate_rows[e])], axis=0
        )
        grads = jnp.concatenate(picked_grads[e], axis=0)
        dy = (gate * grads).astype(bf16)
        mixed = jnp.dot(x, w_gate_up, preferred_element_type=f32)
        dact = lax.dot_general(dy, w_down, NT, preferred_element_type=f32)
        gate_part, up_part = mixed[:, :FF], mixed[:, FF:]
        sigma = 1.0 / (1.0 + jnp.exp(-gate_part))
        silu = gate_part * sigma
        act = (silu * up_part).astype(bf16)
        dh = jnp.concatenate(
            [dact * up_part * (sigma + silu * (1.0 - sigma)), dact * silu], axis=1
        ).astype(bf16)
        x_ref[e] = x
        dy_ref[e] = dy
        act_ref[e] = act
        dh_ref[e] = dh
        returned = jnp.dot(act, w_down, preferred_element_type=f32).astype(bf16).astype(f32)
        dgate = jnp.sum(returned * grads, axis=1, keepdims=True)
        for b in range(4):
            grad = jnp.sum(
                picks[e][b] * dgate[b * SLOTS : (b + 1) * SLOTS], axis=0, keepdims=True
            )
            high = grad.astype(bf16).astype(f32)
            gap = jnp.zeros((1, 256 - TOK), f32)
            wide = jnp.concatenate([high, gap, grad - high, gap, jnp.zeros((1, WIDTH - 512), f32)], axis=1)
            gate_grads[b] = gate_grads[b] + jnp.where(payload_rows == own + e, wide, 0.0)
        moved.append(gate * returned)
        routed.append(lax.dot_general(dh, w_gate_up, NT, preferred_element_type=f32))
    columns = lax.broadcasted_iota(i32, (TOK, 2 * SLOTS), 1).astype(f32)
    outs = [(routed_mine, moved_mine, 0), (routed_other, moved_other, 0), (routed_mine, moved_mine, 1), (routed_other, moved_other, 1)]
    for b, (routed_ref, moved_ref, n) in enumerate(outs):
        first, second = slot_cols[b][:, 0:1], slot_cols[b][:, 1:2]
        back = ((columns == first) | ((columns == second + SLOTS) & (second >= 0))).astype(f32).astype(bf16)
        at = slice(b * SLOTS, (b + 1) * SLOTS)
        for terms, ref in ((routed, routed_ref), (moved, moved_ref)):
            joined = jnp.concatenate([terms[0][at], terms[1][at]], axis=0).astype(bf16)
            ref[n, :TOK, :] = jnp.dot(back, joined, preferred_element_type=f32).astype(bf16)
        routed_ref[n, TOK:, :] = gate_grads[b].astype(bf16)


def run_experts(half, own, ffn, grads, weights, router, before):
    pair = pl.BlockSpec((2, TOK, WIDTH), lambda i, o: (i, 0, 0))
    pair_of_all = pl.BlockSpec((2, TOK, WIDTH), lambda i, o: (i + 2 * half, 0, 0))
    whole = lambda shape: pl.BlockSpec(shape, lambda i, o: (0,) * len(shape))
    routes = pl.BlockSpec((2, 16, 256), lambda i, o: (i, TOK // 16, 0))
    summed = pl.BlockSpec((2, PAY, WIDTH), lambda i, o: (i, 0, 0))
    kept = lambda n: pl.BlockSpec((2, STEP_ROWS, n), lambda i, o: (0, i + 2 * half, 0))
    part = jax.ShapeDtypeStruct((4, PAY, WIDTH), bf16)
    keep = lambda n: jax.ShapeDtypeStruct((2, ALL_ROWS, n), bf16)
    return pl.pallas_call(
        experts_kernel,
        grid_spec=pltpu.PrefetchScalarGridSpec(
            num_scalar_prefetch=1,
            grid=(2,),
            in_specs=[
                pair,
                pair,
                pair,
                pair,
                routes,
                routes,
                whole((EXPERTS, WIDTH)),
            ]
            + [pl.BlockSpec(memory_space=pl.ANY)] * (2 + len(before)),
            out_specs=[
                summed,
                summed,
                pair_of_all,
                pair_of_all,
                kept(WIDTH),
                kept(2 * FF),
                kept(FF),
                kept(WIDTH),
            ],
            scratch_shapes=[
                pltpu.VMEM((2, 8, 192, 1024), bf16),
                pltpu.SemaphoreType.DMA((2, 4, 2)),
            ],
        ),
        out_shape=[
            part,
            part,
            jax.ShapeDtypeStruct((8, TOK, WIDTH), bf16),
            jax.ShapeDtypeStruct((8, TOK, WIDTH), bf16),
            keep(WIDTH),
            keep(2 * FF),
            keep(FF),
            keep(WIDTH),
        ],
        input_output_aliases={10 + i: 2 + i for i in range(len(before))},
        compiler_params=pltpu.CompilerParams(vmem_limit_bytes=VMEM_LIMIT),
        cost_estimate=pl.CostEstimate(
            flops=14 << 30, bytes_accessed=24 << 20, transcendentals=8 * SLOTS * 2 * FF
        ),
    )(own, *ffn, *grads, *grads, router, *weights, *before)


def expert_grads_kernel(x_ref, dh_ref, act_ref, dy_ref, out_ref):
    up = lax.dot_general(x_ref[0], dh_ref[0], TN, preferred_element_type=f32)
    down = lax.dot_general(act_ref[0], dy_ref[0], TN, preferred_element_type=f32)
    out_ref[0, :, 0, :128, :] = up.astype(bf16).reshape(2, 128, 2 * FF)
    out_ref[0, :, 0, 128:, :] = down.astype(bf16).reshape(2, 64, WIDTH)


def expert_weight_grads(x, dh, act, dy):
    return pl.pallas_call(
        expert_grads_kernel,
        grid=(2, 4),
        in_specs=[
            pl.BlockSpec((1, ALL_ROWS, 256), lambda e, i: (e, 0, i)),
            pl.BlockSpec((1, ALL_ROWS, 2 * FF), lambda e, i: (e, 0, 0)),
            pl.BlockSpec((1, ALL_ROWS, 128), lambda e, i: (e, 0, i)),
            pl.BlockSpec((1, ALL_ROWS, WIDTH), lambda e, i: (e, 0, 0)),
        ],
        out_specs=pl.BlockSpec((1, 2, 1, 192, 1024), lambda e, i: (i, 0, e, 0, 0)),
        out_shape=jax.ShapeDtypeStruct((4, 2, 2, 192, 1024), bf16),
        compiler_params=pltpu.CompilerParams(vmem_limit_bytes=VMEM_LIMIT),
        cost_estimate=pl.CostEstimate(flops=8 << 30, bytes_accessed=14 << 20, transcendentals=0),
    )(x, dh, act, dy)


def hidden_kernel(att_ref, w_ref, rows_ref, gain_ref, hidden_ref, normed_ref):
    att = att_ref[...].reshape(WIDTH, TOK)
    hidden = rows_ref[...].astype(f32) + lax.dot_general(
        att, w_ref[:, :WIDTH], TN, preferred_element_type=f32
    )
    hidden_ref[...] = hidden
    normed_ref[...] = (hidden * inverse_rms(hidden) * gain_ref[...]).astype(bf16)


def hidden_of(attended, shared, rows, gain):
    return pl.pallas_call(
        hidden_kernel,
        out_shape=[
            jax.ShapeDtypeStruct((TOK, WIDTH), f32),
            jax.ShapeDtypeStruct((TOK, WIDTH), bf16),
        ],
        compiler_params=pltpu.CompilerParams(vmem_limit_bytes=VMEM_LIMIT),
        cost_estimate=pl.CostEstimate(
            flops=2 * TOK * WIDTH * WIDTH, bytes_accessed=5 << 20, transcendentals=0
        ),
    )(attended, shared, rows, gain)


def hidden_back_kernel(
    t0, t1, t2, t3, crossed, hidden_ref, normed_ref, chosen_ref, router_ref, g_ref, gain_ref,
    w_ref, hidden_grad_ref, branch_ref, logit_ref, scaled_ref, att_ref
):
    chosen = chosen_ref[...] > 0
    logits = lax.dot_general(router_ref[...], normed_ref[...], NT, preferred_element_type=f32)
    peak = jnp.max(jnp.where(chosen, logits, masked_score), axis=0, keepdims=True)
    raised = jnp.where(chosen, jnp.exp(jnp.minimum(logits - peak, 0.0)), 0.0)
    gates = raised / jnp.sum(raised, axis=0, keepdims=True)
    summed = t0[...].astype(f32)
    for term in (t1, t2, t3, crossed):
        summed = summed + term[...].astype(f32)
    gate_grad = summed[TOK:, :TOK] + summed[TOK:, 256 : 256 + TOK]
    logit_grad = gates * (gate_grad - jnp.sum(gates * gate_grad, axis=0, keepdims=True))
    logit_grad = logit_grad.astype(bf16)
    logit_ref[...] = logit_grad
    normed_grad = summed[:TOK] + lax.dot_general(
        logit_grad, router_ref[...], TN, preferred_element_type=f32
    )
    hidden = hidden_ref[...]
    scale = inverse_rms(hidden)
    scaled_ref[...] = (normed_grad * hidden * scale).astype(bf16)
    hidden_grad = g_ref[...].astype(f32) + rms_pull(hidden, scale, gain_ref[...], normed_grad)
    hidden_grad_ref[...] = hidden_grad
    branch = hidden_grad.astype(bf16)
    branch_ref[...] = branch
    att = lax.dot_general(w_ref[:, :WIDTH], branch, NT, preferred_element_type=f32)
    att_ref[...] = att.astype(bf16).reshape(HEADS, HEAD_DIM, TOK)


def hidden_back(terms, crossed, hidden, normed, chosen, router_t, g, gain, shared):
    wide = lambda t: jax.ShapeDtypeStruct((TOK, WIDTH), t)
    return pl.pallas_call(
        hidden_back_kernel,
        out_shape=[
            wide(f32),
            wide(bf16),
            jax.ShapeDtypeStruct((EXPERTS, TOK), bf16),
            wide(bf16),
            jax.ShapeDtypeStruct((HEADS, HEAD_DIM, TOK), bf16),
        ],
        compiler_params=pltpu.CompilerParams(vmem_limit_bytes=VMEM_LIMIT),
        cost_estimate=pl.CostEstimate(
            flops=2 * TOK * WIDTH * WIDTH, bytes_accessed=8 << 20, transcendentals=0
        ),
    )(*terms, crossed, hidden, normed, chosen, router_t, g, gain, shared)


def shared_grads_kernel(att_ref, branch_ref, normed_ref, logit_ref, scaled_ref, out_ref):
    over_tokens = (((0,), (1,)), ((), ()))
    logit = jnp.concatenate([logit_ref[...], jnp.zeros((96, TOK), bf16)], axis=0)
    ones = (lax.broadcasted_iota(i32, (128, TOK), 0) == EXPERTS).astype(f32).astype(bf16)
    att = att_ref[...].reshape(WIDTH, TOK)
    grads = [
        jnp.dot(att, branch_ref[...], preferred_element_type=f32),
        lax.dot_general(normed_ref[...], logit, over_tokens, preferred_element_type=f32)
        + lax.dot_general(scaled_ref[...], ones, over_tokens, preferred_element_type=f32),
    ]
    for w in range(8):
        for part, at in zip(grads, (slice(0, WIDTH), slice(WIDTH, None))):
            rows = [part[s * 64 + w * 8 : s * 64 + w * 8 + 8] for s in range(16)]
            out_ref[w, :, at] = jnp.concatenate(rows, axis=0).astype(bf16)


def shared_weight_grads(att, branch, normed, logit_grad, scaled):
    return pl.pallas_call(
        shared_grads_kernel,
        out_shape=jax.ShapeDtypeStruct((8, 128, 1152), bf16),
        compiler_params=pltpu.CompilerParams(vmem_limit_bytes=VMEM_LIMIT),
        cost_estimate=pl.CostEstimate(
            flops=2 * TOK * WIDTH * 1280, bytes_accessed=5 << 20, transcendentals=0
        ),
    )(att, branch, normed, logit_grad, scaled)


def local(
    tokens,
    routes,
    cont_lengths,
    norm_attn,
    w_qkv,
    w_out,
    w_router,
    norm_ffn,
    w_gate_up,
    w_down,
    cotangent,
):
    seq_index = lax.axis_index("seq")
    places, blocks = relative_places(seq_index)
    rows = tokens[0]
    query_width = HEADS * HEAD_DIM
    kv_width = KV_HEADS * HEAD_DIM

    position, begin = group_layout(cont_lengths[0])
    begin = begin[None]
    table = rotary_table(position.astype(f32))
    kv_heads = lambda start: jnp.repeat(
        w_qkv[:, start : start + kv_width].reshape(8, KV_HEADS, HEAD_DIM), 2, axis=1
    )
    head_cols = jnp.concatenate(
        [
            w_qkv[:, :query_width].reshape(8, HEADS, HEAD_DIM),
            kv_heads(query_width),
            kv_heads(query_width + kv_width),
            jnp.broadcast_to(norm_attn[:, None, None], (8, HEADS, HEAD_DIM)),
        ],
        axis=2,
    ).transpose(1, 0, 2)
    head_cols = jnp.broadcast_to(head_cols[:, None], (HEADS, 8, 8, 256)).reshape(128, 8, 256)
    head_weights = lax.all_to_all(head_cols, BOTH, 0, 0, tiled=True).reshape(WIDTH, 256)
    gain_attn = head_weights[:, 192].astype(f32)[None]
    head_weights = jnp.where(jnp.arange(256)[None] < 192, head_weights, 0.0).astype(bf16)

    rows_near, rows_across = gather_near(rows)
    rows_near, _, table, head_weights = tie(rows_near, rows_across, table, head_weights)
    rows_near, rows_far = both_cores(rows_near), gather_far(rows_across)

    own_x = lax.axis_index("wshard") % 2
    expert_rows = jnp.concatenate([w_gate_up, w_down], axis=1)
    along_y = lambda t: lax.all_gather(t, "wshard", axis_index_groups=ALONG_Y, axis=0)
    experts, expert_rows = along_y(expert_rows), swap_x(expert_rows)

    qkv = project(places[:8], rows_near, head_weights, gain_attn, table, ())
    shared = jnp.concatenate(
        [w_out, w_router, norm_ffn[:, None], jnp.zeros((8, 95), bf16)], axis=1
    )
    shared, qkv = tie(shared, qkv)
    shared = lax.all_to_all(
        jnp.broadcast_to(shared[None], (128, 8, 1152)), BOTH, 0, 0, tiled=True
    ).reshape(WIDTH, 1152)
    routes_rows = jnp.pad(routes[0].T.astype(bf16), ((0, 8), (0, WIDTH - TOK)))
    upstream_rows = jnp.concatenate([cotangent[0], routes_rows], axis=0)
    rows_far, qkv, upstream_rows, expert_rows = tie(rows_far, qkv, upstream_rows, expert_rows)
    experts = [experts, along_y(expert_rows)]
    rows_far = both_cores(rows_far)
    grad_near = [upstream_rows] + [send(upstream_rows, 0, b) for b in (1, 3, 2)]
    qkv = project(places[8:], rows_far, head_weights, gain_attn, table, (qkv,))

    router_t = shared[:, WIDTH : WIDTH + EXPERTS].T
    gain_ffn = shared[:, WIDTH + EXPERTS].astype(f32)[None]
    attended_head, attended_t, lse = attend(qkv, begin)
    attended_head, shared = tie(attended_head, shared)
    attended = lax.all_to_all(attended_head, "seq", 0, 0, tiled=True)
    attended, grad_near = tie(attended, grad_near)
    grad_near = jnp.stack(grad_near)
    grad_rows = grad_near.reshape(-1, WIDTH)
    grad_far = [send(grad_rows[:EARLY], 1, 0)]
    hidden, normed_ffn = hidden_of(attended, shared, rows, gain_ffn)
    ffn_near, ffn_across = gather_near(normed_ffn)
    grad_rows, _ = tie(grad_rows, ffn_across)
    ffn_near, _, grad_far[0] = tie(ffn_near, ffn_across, grad_far[0])
    grad_far.append(send(grad_rows[EARLY:], 1, 0))
    grad_near = (grad_near, swap_cores(grad_near))
    ffn_near, ffn_far = both_cores(ffn_near), gather_far(ffn_across)
    own = jnp.stack([seq_index * 2, own_x])
    near = run_experts(0, own, ffn_near, grad_near, experts, router_t, ())
    near_terms = sum_along_z(*near[:2])
    ffn_far = both_cores(ffn_far)
    grad_far = jnp.concatenate(grad_far, axis=0).reshape(grad_near[0].shape)
    grad_far = (grad_far, swap_cores(grad_far))
    far = run_experts(1, own, ffn_far, grad_far, experts, router_t, near[2:])
    far, near_terms = tie(far, near_terms)
    moved, saved = far[2:4], far[4:]
    far_other, moved_other = tie(swap_cores(far[1]), moved[1])
    far_terms = send_along_z(chip_parts(far[0], far_other))
    expert_grads = expert_weight_grads(*saved)
    moved_other = swap_cores(moved_other)
    far_terms, expert_grads, moved_other = tie(far_terms, expert_grads, moved_other)
    crossed = send(add_low(*far_terms), 1, 0)
    by_x = [t.reshape(2, 4, TOK, WIDTH) for t in (moved[0], moved_other)]
    moved_parts = [add_low(by_x[0][:, i], by_x[1][:, i]) for i in range(4)]
    crossed, moved_parts = tie(crossed, moved_parts)

    expert_range = jnp.arange(EXPERTS, dtype=i32)
    chosen_here = jnp.any(routes[0].T[None] == expert_range[:, None, None], axis=1).astype(f32)
    hidden_grad, branch_grad, logit_grad, scaled_grad, attended_grad = hidden_back(
        near_terms, crossed, hidden, normed_ffn, chosen_here, router_t, cotangent[0], gain_ffn, shared
    )
    expert_grads = lax.psum_scatter(
        expert_grads.reshape(8, 2, 192, 1024),
        "wshard",
        axis_index_groups=ALONG_Y,
        scatter_dimension=0,
        tiled=True,
    )
    head_grad = lax.all_to_all(attended_grad, "seq", 0, 0, tiled=True)
    shared_grads = shared_weight_grads(attended, branch_grad, normed_ffn, logit_grad, scaled_grad)
    head_grad, shared_grads, moved_parts = tie(head_grad, shared_grads, moved_parts)
    moved_terms = [moved_parts[0]] + [
        send(moved_parts[i], 0, -b) for i, b in ((1, 1), (2, 3), (3, 2))
    ]

    shared_grads = lax.all_to_all(shared_grads, "wshard", 0, 0, tiled=True)
    projected_grad = attend_back(qkv, head_grad, attended_t, lse, begin, table)
    shared_grads, moved_terms = tie(shared_grads, moved_terms)
    shared_grads = jnp.sum(shared_grads.astype(f32), axis=0)
    moved_crossed = add_low(*[t[1] for t in moved_terms])
    shared_grads, moved_crossed = tie(shared_grads, moved_crossed)
    moved_crossed = send(moved_crossed, 1, 0)
    far_part = project_back(places[8:], projected_grad, head_weights, shared_grads)
    near_part = project_back(places[:8], projected_grad, head_weights, shared_grads)
    far_parts = chip_parts(far_part[0], swap_cores(far_part[1]))
    near_part, expert_grads = tie(near_part, expert_grads)
    near_parts = chip_parts(near_part[0], swap_cores(near_part[1]))
    far_parts, near_parts, projected_grad, expert_grads = tie(
        far_parts, near_parts, projected_grad, expert_grads
    )
    far_terms, moved_crossed = tie(send_along_z(far_parts), moved_crossed)
    near_terms = send_along_z(near_parts)
    grad_head = head_weight_grad(places, rows_near, rows_far, gain_attn, projected_grad)
    grad_heads = lax.all_to_all(grad_head.reshape(128, 8, 256), BOTH, 0, 0, tiled=True)
    crossed = send(add_low(*far_terms), 1, 0)
    crossed, near_terms, grad_heads = tie(crossed, near_terms, grad_heads)
    kept = lax.dynamic_index_in_dim(expert_grads, own_x, 0, keepdims=False)
    sent = lax.dynamic_index_in_dim(expert_grads, 1 - own_x, 0, keepdims=False)
    expert_grads = kept.astype(f32) + swap_x(sent).astype(f32)
    total = lambda terms: sum([t.astype(f32) for t in terms])
    output = (hidden + total([t[0] for t in moved_terms] + [moved_crossed])).astype(bf16)
    last_sum = total(near_terms + [crossed])
    normed_grad, shared_grads = last_sum[:TOK], last_sum[TOK:]
    grad_heads = jnp.sum(grad_heads.reshape(16, 8, 8, 256).astype(f32), axis=1).transpose(1, 0, 2)
    kv_sum = lambda start: jnp.sum(
        grad_heads[:, :, start : start + HEAD_DIM].reshape(8, KV_HEADS, 2, HEAD_DIM), axis=2
    ).reshape(8, kv_width)
    grad_qkv = jnp.concatenate(
        [grad_heads[:, :, :HEAD_DIM].reshape(8, query_width), kv_sum(HEAD_DIM), kv_sum(2 * HEAD_DIM)],
        axis=1,
    )
    grad_norm_attn = jnp.sum(grad_qkv * w_qkv.astype(f32), axis=1) / norm_attn.astype(f32)
    inputs = rows.astype(f32)
    grad_input = hidden_grad + rms_pull(inputs, inverse_rms(inputs), gain_attn, normed_grad)
    return (
        output[None],
        grad_input[None],
        grad_norm_attn,
        grad_qkv,
        shared_grads[:8],
        shared_grads[8:, :EXPERTS],
        shared_grads[8:, EXPERTS],
        expert_grads[:, :128],
        expert_grads[:, 128:],
    )


def solution(mesh):
    return jax.shard_map(
        local,
        mesh=mesh,
        in_specs=(
            P("wshard", "seq", None),
            P("wshard", "seq", None),
            P("wshard", None),
            P(BOTH),
            P(BOTH, None),
            P(BOTH, None),
            P(BOTH, None),
            P(BOTH),
            P("seq", "wshard", None),
            P("seq", "wshard", None),
            P("wshard", "seq", None),
        ),
        out_specs=(
            P("wshard", "seq", None),
            P("wshard", "seq", None),
            P(BOTH),
            P(BOTH, None),
            P(BOTH, None),
            P(BOTH, None),
            P(BOTH),
            P("seq", "wshard", None),
            P("seq", "wshard", None),
        ),
        check_vma=False,
    )
```

```python
import jax
import jax.numpy as jnp
from jax import lax
from jax.experimental import pallas as pl
from jax.experimental.pallas import tpu as pltpu
from jax.sharding import PartitionSpec as P

HEADS = 16
KV_HEADS = 8
HEAD_DIM = 64
EXPERTS = 32
FF = 512
PROMPT = 2048
GROUP = 3584
TOK = 224
WIDTH = 1024
SLOTS = 72
STEP_ROWS = 4 * SLOTS
ALL_ROWS = 16 * SLOTS
BLOCK = 512
VMEM_LIMIT = 60 << 20
LAST = TOK + 16
EARLY = 352
PAY = TOK + 32

norm_eps = 1e-06
rope_base = 10000.0
masked_score = -1e30
BOTH = ("seq", "wshard")
NT = (((1,), (1,)), ((), ()))
TN = (((0,), (0,)), ((), ()))
f32 = jnp.float32
bf16 = jnp.bfloat16
i32 = jnp.int32


def place_of(x, z, core):
    return x * 8 + z * 2 + core


def shift_perm(a, b):
    return [
        (place_of(x, z, c), place_of(x ^ a, (z + b) % 4, c))
        for x in range(2)
        for z in range(4)
        for c in range(2)
    ]


CORE_PERM = [(i, i ^ 1) for i in range(16)]


def send(rows, a, b):
    return lax.ppermute(rows, "seq", shift_perm(a, b))


def swap_cores(rows):
    return lax.ppermute(rows, "seq", CORE_PERM)


def relative_places(seq_index):
    x, z, c = seq_index // 8, (seq_index // 2) % 4, seq_index % 2
    r = jnp.arange(16, dtype=i32)
    a, i, k = r // 8, (r // 2) % 4, r % 2
    shift = i ^ (i // 2)
    behind = (z - i) % 4
    places = (a ^ x) * 8 + ((z - shift) % 4) * 2 + (k ^ c)
    return places, (a ^ x) * 8 + (behind ^ (behind // 2)) * 2 + (k ^ c)


def gather_near(rows):
    return [rows] + [send(rows, 0, b) for b in (1, 3, 2)], send(rows, 1, 0)


def both_cores(parts):
    mine = jnp.stack(parts)
    return mine, swap_cores(mine)


def gather_far(across):
    return [across] + [send(across, 0, b) for b in (1, 3, 2)]


def add_low(*terms):
    return sum([t.astype(f32) for t in terms]).astype(bf16)


def sum_along_z(mine, other):
    return send_along_z(chip_parts(mine, swap_cores(other)))


def chip_parts(mine, got):
    return [add_low(mine[i], got[i]) for i in range(4)]


def send_along_z(parts):
    return [parts[0]] + [send(parts[i], 0, -b) for i, b in ((1, 1), (2, 3), (3, 2))]


def swap_x(rows):
    return lax.ppermute(rows, "wshard", [(w, w ^ 1) for w in range(8)])


ALONG_Y = [[y * 2 + x for y in range(4)] for x in range(2)]


def tie(*values):
    return lax.optimization_barrier(values)


def inverse_rms(values):
    return lax.rsqrt(jnp.mean(values * values, axis=-1, keepdims=True) + norm_eps)


def rms_pull(values, scale, gain, grad):
    scaled = grad * gain
    return scale * scaled - values * (scale * scale * scale) * jnp.mean(
        scaled * values, axis=-1, keepdims=True
    )


def group_layout(lengths):
    places = jnp.arange(GROUP, dtype=i32)
    ends = jnp.cumsum(lengths)
    starts = ends - lengths
    offset_in = places - PROMPT
    segment_id = jnp.sum((offset_in[:, None] >= ends[None, :]).astype(i32), axis=1)
    segment_hot = segment_id[:, None] == jnp.arange(lengths.shape[0], dtype=i32)[None, :]
    begin = jnp.sum(jnp.where(segment_hot, starts[None, :], 0), axis=1)
    inside = offset_in >= 0
    position = jnp.where(inside, PROMPT + offset_in - begin, places)
    return position, jnp.where(inside, PROMPT + begin, 0)


def rotary_table(position):
    half_dim = HEAD_DIM // 2
    inverse = rope_base ** (-((jnp.arange(2 * HEAD_DIM) % half_dim).astype(f32) * 2.0) / HEAD_DIM)
    back = jnp.where(jnp.arange(2 * HEAD_DIM) < HEAD_DIM, 0.0, 0.5 * jnp.pi).astype(f32)
    return jnp.cos(position[:, None] * inverse[None, :] - back[None, :])


def turn(values):
    half_dim = HEAD_DIM // 2
    return jnp.concatenate([-values[:, half_dim:], values[:, :half_dim]], axis=-1)


def turn_back(values):
    half_dim = HEAD_DIM // 2
    return jnp.concatenate([values[:, half_dim:], -values[:, :half_dim]], axis=-1)


def project_kernel(places, mine, other, w, gain, table, *refs):
    out = refs[-1]
    j = pl.program_id(0)

    if len(refs) > 1:

        @pl.when(j == 0)
        def _():
            out[...] = refs[0][...]

    for k, ref in enumerate((mine, other)):
        at = pl.ds(pl.multiple_of(places[2 * j + k] * TOK, TOK), TOK)
        rows = ref[0].astype(f32)
        normed = (rows * inverse_rms(rows) * gain[...]).astype(bf16)
        projected = jnp.dot(normed, w[...], preferred_element_type=f32)
        c, s = table[at, :HEAD_DIM], table[at, HEAD_DIM:]
        q, k, v = projected[:, :64], projected[:, 64:128], projected[:, 128:]
        q = (q * c + turn(q) * s).astype(bf16).astype(f32) * HEAD_DIM**-0.5
        out[at, :] = jnp.concatenate([q, k * c + turn(k) * s, v], axis=1).astype(bf16)


def project(places, gathered, w, gain, table, before):
    chip = pl.BlockSpec((1, TOK, WIDTH), lambda j, p: (j, 0, 0))
    whole = lambda *shape: pl.BlockSpec(shape, lambda j, p: (0,) * len(shape))
    return pl.pallas_call(
        project_kernel,
        grid_spec=pltpu.PrefetchScalarGridSpec(
            num_scalar_prefetch=1,
            grid=(4,),
            in_specs=[chip, chip, whole(WIDTH, 256), whole(1, WIDTH), whole(GROUP, 128)]
            + [whole(GROUP, 256)] * len(before),
            out_specs=whole(GROUP, 256),
        ),
        out_shape=jax.ShapeDtypeStruct((GROUP, 256), bf16),
        compiler_params=pltpu.CompilerParams(vmem_limit_bytes=VMEM_LIMIT),
        cost_estimate=pl.CostEstimate(
            flops=2 * 8 * TOK * WIDTH * 256, bytes_accessed=10 << 20, transcendentals=0
        ),
    )(places, *gathered, w, gain, table, *before)


def project_back_kernel(places, first, second, w, first_shared, second_shared, mine, other):
    del places
    for projected, shared, out in ((first, first_shared, mine), (second, second_shared, other)):
        out[0, :TOK, :] = lax.dot_general(
            projected[...], w[...], NT, preferred_element_type=f32
        ).astype(bf16)
        rest = jnp.concatenate([shared[:, WIDTH:], jnp.zeros((8, WIDTH - 128), f32)], axis=1)
        out[0, TOK:, :] = jnp.concatenate([shared[:, :WIDTH], rest], axis=0).astype(bf16)


def project_back(places, projected_grad, w, shared):
    chip = pl.BlockSpec((1, LAST, WIDTH), lambda j, p: (j, 0, 0))
    at = lambda k, rows, n: pl.BlockSpec((rows, n), lambda j, p: (p[2 * j + k], 0))
    part = jax.ShapeDtypeStruct((4, LAST, WIDTH), bf16)
    return pl.pallas_call(
        project_back_kernel,
        grid_spec=pltpu.PrefetchScalarGridSpec(
            num_scalar_prefetch=1,
            grid=(4,),
            in_specs=[
                at(0, TOK, 256),
                at(1, TOK, 256),
                pl.BlockSpec((WIDTH, 256), lambda j, p: (0, 0)),
                at(0, 8, 1152),
                at(1, 8, 1152),
            ],
            out_specs=[chip, chip],
        ),
        out_shape=[part, part],
        compiler_params=pltpu.CompilerParams(vmem_limit_bytes=VMEM_LIMIT),
        cost_estimate=pl.CostEstimate(
            flops=2 * 8 * TOK * WIDTH * 256, bytes_accessed=5 << 20, transcendentals=0
        ),
    )(places, projected_grad, projected_grad, w, shared, shared)


def head_grad_kernel(places, near_mine, near_other, far_mine, far_other, gain, first, second, out, total):
    del places
    j = pl.program_id(0)

    @pl.when(j == 0)
    def _():
        total[...] = jnp.zeros_like(total)

    for near, far, projected in ((near_mine, far_mine, first), (near_other, far_other, second)):
        rows = jnp.where(j < 4, near[0], far[0]).astype(f32)
        normed = (rows * inverse_rms(rows) * gain[...]).astype(bf16)
        total[...] += lax.dot_general(normed, projected[...], TN, preferred_element_type=f32)

    @pl.when(j == 7)
    def _():
        out[...] = total[...].astype(bf16)


def head_weight_grad(places, near, far, gain, projected_grad):
    near_chip = pl.BlockSpec((1, TOK, WIDTH), lambda j, p: (jnp.minimum(j, 3), 0, 0))
    far_chip = pl.BlockSpec((1, TOK, WIDTH), lambda j, p: (jnp.maximum(j - 4, 0), 0, 0))
    at = lambda k: pl.BlockSpec((TOK, 256), lambda j, p: (p[2 * j + k], 0))
    return pl.pallas_call(
        head_grad_kernel,
        grid_spec=pltpu.PrefetchScalarGridSpec(
            num_scalar_prefetch=1,
            grid=(8,),
            in_specs=[
                near_chip,
                near_chip,
                far_chip,
                far_chip,
                pl.BlockSpec((1, WIDTH), lambda j, p: (0, 0)),
                at(0),
                at(1),
            ],
            out_specs=pl.BlockSpec((WIDTH, 256), lambda j, p: (0, 0)),
            scratch_shapes=[pltpu.VMEM((WIDTH, 256), f32)],
        ),
        out_shape=jax.ShapeDtypeStruct((WIDTH, 256), bf16),
        compiler_params=pltpu.CompilerParams(vmem_limit_bytes=VMEM_LIMIT),
        cost_estimate=pl.CostEstimate(
            flops=2 * 16 * TOK * WIDTH * 256, bytes_accessed=10 << 20, transcendentals=0
        ),
    )(places, *near, *far, gain, projected_grad, projected_grad)


def tile_mask(scores, key_start, query_start, begin):
    keys = key_start + lax.broadcasted_iota(i32, scores.shape, 0)
    queries = query_start + lax.broadcasted_iota(i32, scores.shape, 1)
    return jnp.where((keys <= queries) & (keys >= begin), scores, masked_score)


def key_ranges(i):
    first = PROMPT // BLOCK
    return jnp.where(i > first, i - 1, i), jnp.minimum(i, first)


def attend_kernel(qkv_ref, begin_ref, o_ref, ot_ref, lse_ref, keys, vt):
    i = pl.program_id(0)
    here = pl.ds(pl.multiple_of(i * BLOCK, BLOCK), BLOCK)

    @pl.when(i == 0)
    def _():
        keys[...] = qkv_ref[:, 64:128]
        vt[...] = qkv_ref[:, 128:192].T

    q = qkv_ref[here, :64]
    begin = begin_ref[...]

    def tile(j, carry, masked, n=1):
        peak, total, out = carry
        start = pl.multiple_of(j * BLOCK, BLOCK)
        at = pl.ds(start, n * BLOCK)
        s = lax.dot_general(keys[at, :], q, NT, preferred_element_type=f32)
        if masked:
            s = tile_mask(s, start, i * BLOCK, begin)
        higher = jnp.maximum(peak, jnp.max(s, axis=0, keepdims=True))
        p = jnp.exp(s - higher)
        fade = jnp.exp(peak - higher)
        total = total * fade + jnp.sum(p, axis=0, keepdims=True)
        out = out * fade + jnp.dot(vt[:, at], p.astype(bf16), preferred_element_type=f32)
        return higher, total, out

    carry = (
        jnp.full((1, BLOCK), masked_score, f32),
        jnp.zeros((1, BLOCK), f32),
        jnp.zeros((HEAD_DIM, BLOCK), f32),
    )
    carry = tile(i, carry, True)
    window, shared = key_ranges(i)
    carry = lax.fori_loop(window, i, lambda j, c: tile(j, c, True), carry)
    pairs = shared // 2
    carry = lax.fori_loop(0, pairs, lambda j, c: tile(2 * j, c, False, 2), carry)
    peak, total, out = lax.fori_loop(2 * pairs, shared, lambda j, c: tile(j, c, False), carry)
    ot_ref[:, here] = out * (1.0 / total)
    lse_ref[...] = peak + jnp.log(total)

    @pl.when(i == GROUP // BLOCK - 1)
    def _():
        for b in range(16):
            o_ref[b] = ot_ref[:, b * TOK : (b + 1) * TOK].astype(bf16)


def attend(qkv, begin):
    whole = lambda *shape: pl.BlockSpec(shape, lambda i: (0,) * len(shape))
    cols = lambda n: pl.BlockSpec((n, BLOCK), lambda i: (0, i))
    return pl.pallas_call(
        attend_kernel,
        grid=(GROUP // BLOCK,),
        in_specs=[whole(GROUP, 256), cols(1)],
        out_specs=[whole(16, HEAD_DIM, TOK), whole(HEAD_DIM, GROUP), cols(1)],
        out_shape=[
            jax.ShapeDtypeStruct((16, HEAD_DIM, TOK), bf16),
            jax.ShapeDtypeStruct((HEAD_DIM, GROUP), f32),
            jax.ShapeDtypeStruct((1, GROUP), f32),
        ],
        scratch_shapes=[
            pltpu.VMEM((GROUP, HEAD_DIM), bf16),
            pltpu.VMEM((HEAD_DIM, GROUP), bf16),
        ],
        compiler_params=pltpu.CompilerParams(vmem_limit_bytes=VMEM_LIMIT),
        cost_estimate=pl.CostEstimate(
            flops=2 * 27 * BLOCK * BLOCK * 512, bytes_accessed=4 << 20, transcendentals=27 * BLOCK * BLOCK
        ),
    )(qkv, begin)


def attend_back_kernel(
    qkv_ref, g_ref, ot_ref, lse_ref, begin_ref, table, out_ref, keys, values, kt, gt, dq, dk, dv
):
    i = pl.program_id(0)
    here = pl.ds(pl.multiple_of(i * BLOCK, BLOCK), BLOCK)

    @pl.when(i == 0)
    def _():
        dk[...] = jnp.zeros_like(dk)
        dv[...] = jnp.zeros_like(dv)
        keys[...] = qkv_ref[:, 64:128]
        values[...] = qkv_ref[:, 128:192]
        kt[...] = qkv_ref[:, 64:128].T
        for b in range(16):
            gt[:, b * TOK : (b + 1) * TOK] = g_ref[b]

    q = qkv_ref[here, :64]
    g = gt[:, here]
    begin = begin_ref[...]
    lse = lse_ref[...]
    inner = jnp.sum(g.astype(f32) * ot_ref[...], axis=0, keepdims=True)

    def tile(j, dq, masked, n=1):
        start = pl.multiple_of(j * BLOCK, BLOCK)
        at = pl.ds(start, n * BLOCK)
        s = lax.dot_general(keys[at, :], q, NT, preferred_element_type=f32)
        if masked:
            s = tile_mask(s, start, i * BLOCK, begin)
        p = jnp.exp(s - lse)
        dp = jnp.dot(values[at, :], g, preferred_element_type=f32)
        ds = (p * (dp - inner)).astype(bf16)
        dv[at, :] += lax.dot_general(p.astype(bf16), g, NT, preferred_element_type=f32)
        dk[at, :] += jnp.dot(ds, q, preferred_element_type=f32)
        return dq + jnp.dot(kt[:, at], ds, preferred_element_type=f32)

    dqt = tile(i, jnp.zeros((HEAD_DIM, BLOCK), f32), True)
    window, shared = key_ranges(i)
    dqt = lax.fori_loop(window, i, lambda j, c: tile(j, c, True), dqt)
    pairs = shared // 2
    dqt = lax.fori_loop(0, pairs, lambda j, c: tile(2 * j, c, False, 2), dqt)
    dqt = lax.fori_loop(2 * pairs, shared, lambda j, c: tile(j, c, False), dqt)
    dq[here, :] = dqt.T * HEAD_DIM**-0.5

    @pl.when(i == GROUP // BLOCK - 1)
    def _():
        def back(b, _):
            at = pl.ds(pl.multiple_of(b * BLOCK, BLOCK), BLOCK)
            c, s = table[at, :HEAD_DIM], table[at, HEAD_DIM:]
            q, k = dq[at, :].astype(bf16).astype(f32), dk[at, :].astype(bf16).astype(f32)
            parts = [q * c + turn_back(q * s), k * c + turn_back(k * s), dv[at, :], jnp.zeros_like(q)]
            out_ref[at, :] = jnp.concatenate(parts, axis=1).astype(bf16)
            return 0

        lax.fori_loop(0, GROUP // BLOCK, back, 0)


def attend_back(qkv, g, ot, lse, begin, table):
    whole = lambda *shape: pl.BlockSpec(shape, lambda i: (0,) * len(shape))
    cols = lambda n: pl.BlockSpec((n, BLOCK), lambda i: (0, i))
    return pl.pallas_call(
        attend_back_kernel,
        grid=(GROUP // BLOCK,),
        in_specs=[
            whole(GROUP, 256),
            whole(16, HEAD_DIM, TOK),
            cols(HEAD_DIM),
            cols(1),
            cols(1),
            whole(GROUP, 128),
        ],
        out_specs=whole(GROUP, 256),
        out_shape=jax.ShapeDtypeStruct((GROUP, 256), bf16),
        scratch_shapes=[
            pltpu.VMEM((GROUP, HEAD_DIM), bf16),
            pltpu.VMEM((GROUP, HEAD_DIM), bf16),
            pltpu.VMEM((HEAD_DIM, GROUP), bf16),
            pltpu.VMEM((HEAD_DIM, GROUP), bf16),
            pltpu.VMEM((GROUP, HEAD_DIM), f32),
            pltpu.VMEM((GROUP, HEAD_DIM), f32),
            pltpu.VMEM((GROUP, HEAD_DIM), f32),
        ],
        compiler_params=pltpu.CompilerParams(vmem_limit_bytes=VMEM_LIMIT),
        cost_estimate=pl.CostEstimate(
            flops=5 * 27 * BLOCK * BLOCK * 512, bytes_accessed=8 << 20, transcendentals=27 * BLOCK * BLOCK
        ),
    )(qkv, g, ot, lse, begin, table)


def experts_kernel(
    own_ref, ffn_mine, ffn_other, g_mine, g_other, routes_mine, routes_other, router_ref, own_w, across_w, *refs
):
    routed_mine, routed_other, moved_mine, moved_other = refs[-10:-6]
    x_ref, dh_ref, act_ref, dy_ref, w_ref, sem = refs[-6:]
    own = own_ref[0]

    copies = [
        [
            pltpu.make_async_copy(shards.at[y, e], w_ref.at[e, 2 * y + (own_ref[1] ^ a)], sem.at[a, y, e])
            for a, shards in enumerate((own_w, across_w))
            for y in range(4)
        ]
        for e in range(2)
    ]

    @pl.when(pl.program_id(0) == 0)
    def _():
        for copy in copies[0] + copies[1]:
            copy.start()

    expert_rows = lax.broadcasted_iota(i32, (EXPERTS, TOK), 0)
    slot_rows = lax.broadcasted_iota(i32, (SLOTS, TOK), 0).astype(f32)
    upto = (
        lax.broadcasted_iota(i32, (TOK, TOK), 0) <= lax.broadcasted_iota(i32, (TOK, TOK), 1)
    ).astype(f32).astype(bf16)
    slot_cols = []
    gate_grads = [jnp.zeros((EXPERTS, WIDTH), f32) for _ in range(4)]
    payload_rows = lax.broadcasted_iota(i32, (EXPERTS, WIDTH), 0)
    gate_rows = [[], []]
    picks = [[], []]
    picked_rows = [[], []]
    picked_grads = [[], []]
    blocks = [(ffn_mine, g_mine, routes_mine, 0), (ffn_other, g_other, routes_other, 0)]
    blocks = blocks + [(*refs_of[:3], 1) for refs_of in blocks]
    for rows_ref, grads_ref, routes_ref, n in blocks:
        rows, grads = rows_ref[n], grads_ref[n]
        routes = routes_ref[n][:8, :TOK].astype(f32).astype(i32)
        chosen = expert_rows == routes[0:1]
        for j in range(1, 8):
            chosen = chosen | (expert_rows == routes[j : j + 1])
        named = [jnp.max((routes == own + e).astype(f32), axis=0, keepdims=True) for e in range(2)]
        named = jnp.concatenate(named + [jnp.zeros((6, TOK), f32)], axis=0)
        rank = jnp.dot(named.astype(bf16), upto, preferred_element_type=f32)
        slots = jnp.where(named > 0, rank - 1.0, -1.0)
        slot_cols.append(slots.T)
        logits = lax.dot_general(router_ref[...], rows, NT, preferred_element_type=f32)
        peak = jnp.max(jnp.where(chosen, logits, masked_score), axis=0, keepdims=True)
        raised = jnp.where(chosen, jnp.exp(jnp.minimum(logits - peak, 0.0)), 0.0)
        gates = raised / jnp.sum(raised, axis=0, keepdims=True)
        for e in range(2):
            gate_rows[e].append(
                jnp.sum(jnp.where(expert_rows == own + e, gates, 0.0), axis=0, keepdims=True)
            )
            picks[e].append((slots[e : e + 1] == slot_rows).astype(f32))
        low = jnp.concatenate([picks[0][-1], picks[1][-1]], axis=0).astype(bf16)
        for source, kept in ((rows, picked_rows), (grads, picked_grads)):
            both = jnp.dot(low, source, preferred_element_type=f32)
            kept[0].append(both[:SLOTS])
            kept[1].append(both[SLOTS:])
    moved, routed = [], []
    for e in range(2):

        @pl.when(pl.program_id(0) == 0)
        def _():
            for copy in copies[e]:
                copy.wait()

        w_gate_up = w_ref[e, :, :128, :].reshape(WIDTH, 2 * FF)
        w_down = w_ref[e, :, 128:, :].reshape(FF, WIDTH)
        x = jnp.concatenate(picked_rows[e], axis=0).astype(bf16)
        gate = jnp.concatenate(
            [jnp.sum(p * r, axis=1, keepdims=True) for p, r in zip(picks[e], gate_rows[e])], axis=0
        )
        grads = jnp.concatenate(picked_grads[e], axis=0)
        dy = (gate * grads).astype(bf16)
        mixed = jnp.dot(x, w_gate_up, preferred_element_type=f32)
        dact = lax.dot_general(dy, w_down, NT, preferred_element_type=f32)
        gate_part, up_part = mixed[:, :FF], mixed[:, FF:]
        sigma = 1.0 / (1.0 + jnp.exp(-gate_part))
        silu = gate_part * sigma
        act = (silu * up_part).astype(bf16)
        dh = jnp.concatenate(
            [dact * up_part * (sigma + silu * (1.0 - sigma)), dact * silu], axis=1
        ).astype(bf16)
        x_ref[e] = x
        dy_ref[e] = dy
        act_ref[e] = act
        dh_ref[e] = dh
        returned = jnp.dot(act, w_down, preferred_element_type=f32).astype(bf16).astype(f32)
        dgate = jnp.sum(returned * grads, axis=1, keepdims=True)
        for b in range(4):
            grad = jnp.sum(
                picks[e][b] * dgate[b * SLOTS : (b + 1) * SLOTS], axis=0, keepdims=True
            )
            high = grad.astype(bf16).astype(f32)
            gap = jnp.zeros((1, 256 - TOK), f32)
            wide = jnp.concatenate([high, gap, grad - high, gap, jnp.zeros((1, WIDTH - 512), f32)], axis=1)
            gate_grads[b] = gate_grads[b] + jnp.where(payload_rows == own + e, wide, 0.0)
        moved.append(gate * returned)
        routed.append(lax.dot_general(dh, w_gate_up, NT, preferred_element_type=f32))
    columns = lax.broadcasted_iota(i32, (TOK, 2 * SLOTS), 1).astype(f32)
    outs = [(routed_mine, moved_mine, 0), (routed_other, moved_other, 0), (routed_mine, moved_mine, 1), (routed_other, moved_other, 1)]
    for b, (routed_ref, moved_ref, n) in enumerate(outs):
        first, second = slot_cols[b][:, 0:1], slot_cols[b][:, 1:2]
        back = ((columns == first) | ((columns == second + SLOTS) & (second >= 0))).astype(f32).astype(bf16)
        at = slice(b * SLOTS, (b + 1) * SLOTS)
        for terms, ref in ((routed, routed_ref), (moved, moved_ref)):
            joined = jnp.concatenate([terms[0][at], terms[1][at]], axis=0).astype(bf16)
            ref[n, :TOK, :] = jnp.dot(back, joined, preferred_element_type=f32).astype(bf16)
        routed_ref[n, TOK:, :] = gate_grads[b].astype(bf16)


def run_experts(half, own, ffn, grads, weights, router, before):
    pair = pl.BlockSpec((2, TOK, WIDTH), lambda i, o: (i, 0, 0))
    pair_of_all = pl.BlockSpec((2, TOK, WIDTH), lambda i, o: (i + 2 * half, 0, 0))
    whole = lambda shape: pl.BlockSpec(shape, lambda i, o: (0,) * len(shape))
    routes = pl.BlockSpec((2, 16, 256), lambda i, o: (i, TOK // 16, 0))
    summed = pl.BlockSpec((2, PAY, WIDTH), lambda i, o: (i, 0, 0))
    kept = lambda n: pl.BlockSpec((2, STEP_ROWS, n), lambda i, o: (0, i + 2 * half, 0))
    part = jax.ShapeDtypeStruct((4, PAY, WIDTH), bf16)
    keep = lambda n: jax.ShapeDtypeStruct((2, ALL_ROWS, n), bf16)
    return pl.pallas_call(
        experts_kernel,
        grid_spec=pltpu.PrefetchScalarGridSpec(
            num_scalar_prefetch=1,
            grid=(2,),
            in_specs=[
                pair,
                pair,
                pair,
                pair,
                routes,
                routes,
                whole((EXPERTS, WIDTH)),
            ]
            + [pl.BlockSpec(memory_space=pl.ANY)] * (2 + len(before)),
            out_specs=[
                summed,
                summed,
                pair_of_all,
                pair_of_all,
                kept(WIDTH),
                kept(2 * FF),
                kept(FF),
                kept(WIDTH),
            ],
            scratch_shapes=[
                pltpu.VMEM((2, 8, 192, 1024), bf16),
                pltpu.SemaphoreType.DMA((2, 4, 2)),
            ],
        ),
        out_shape=[
            part,
            part,
            jax.ShapeDtypeStruct((8, TOK, WIDTH), bf16),
            jax.ShapeDtypeStruct((8, TOK, WIDTH), bf16),
            keep(WIDTH),
            keep(2 * FF),
            keep(FF),
            keep(WIDTH),
        ],
        input_output_aliases={10 + i: 2 + i for i in range(len(before))},
        compiler_params=pltpu.CompilerParams(vmem_limit_bytes=VMEM_LIMIT),
        cost_estimate=pl.CostEstimate(
            flops=14 << 30, bytes_accessed=24 << 20, transcendentals=8 * SLOTS * 2 * FF
        ),
    )(own, *ffn, *grads, *grads, router, *weights, *before)


def expert_grads_kernel(x_ref, dh_ref, act_ref, dy_ref, out_ref):
    up = lax.dot_general(x_ref[0], dh_ref[0], TN, preferred_element_type=f32)
    down = lax.dot_general(act_ref[0], dy_ref[0], TN, preferred_element_type=f32)
    out_ref[0, :, 0, :128, :] = up.astype(bf16).reshape(2, 128, 2 * FF)
    out_ref[0, :, 0, 128:, :] = down.astype(bf16).reshape(2, 64, WIDTH)


def expert_weight_grads(x, dh, act, dy):
    return pl.pallas_call(
        expert_grads_kernel,
        grid=(2, 4),
        in_specs=[
            pl.BlockSpec((1, ALL_ROWS, 256), lambda e, i: (e, 0, i)),
            pl.BlockSpec((1, ALL_ROWS, 2 * FF), lambda e, i: (e, 0, 0)),
            pl.BlockSpec((1, ALL_ROWS, 128), lambda e, i: (e, 0, i)),
            pl.BlockSpec((1, ALL_ROWS, WIDTH), lambda e, i: (e, 0, 0)),
        ],
        out_specs=pl.BlockSpec((1, 2, 1, 192, 1024), lambda e, i: (i, 0, e, 0, 0)),
        out_shape=jax.ShapeDtypeStruct((4, 2, 2, 192, 1024), bf16),
        compiler_params=pltpu.CompilerParams(vmem_limit_bytes=VMEM_LIMIT),
        cost_estimate=pl.CostEstimate(flops=8 << 30, bytes_accessed=14 << 20, transcendentals=0),
    )(x, dh, act, dy)


def hidden_kernel(att_ref, w_ref, rows_ref, gain_ref, hidden_ref, normed_ref):
    att = att_ref[...].reshape(WIDTH, TOK)
    hidden = rows_ref[...].astype(f32) + lax.dot_general(
        att, w_ref[:, :WIDTH], TN, preferred_element_type=f32
    )
    hidden_ref[...] = hidden
    normed_ref[...] = (hidden * inverse_rms(hidden) * gain_ref[...]).astype(bf16)


def hidden_of(attended, shared, rows, gain):
    return pl.pallas_call(
        hidden_kernel,
        out_shape=[
            jax.ShapeDtypeStruct((TOK, WIDTH), f32),
            jax.ShapeDtypeStruct((TOK, WIDTH), bf16),
        ],
        compiler_params=pltpu.CompilerParams(vmem_limit_bytes=VMEM_LIMIT),
        cost_estimate=pl.CostEstimate(
            flops=2 * TOK * WIDTH * WIDTH, bytes_accessed=5 << 20, transcendentals=0
        ),
    )(attended, shared, rows, gain)


def hidden_back_kernel(
    t0, t1, t2, t3, crossed, hidden_ref, normed_ref, chosen_ref, router_ref, g_ref, gain_ref,
    w_ref, hidden_grad_ref, branch_ref, logit_ref, scaled_ref, att_ref
):
    chosen = chosen_ref[...] > 0
    logits = lax.dot_general(router_ref[...], normed_ref[...], NT, preferred_element_type=f32)
    peak = jnp.max(jnp.where(chosen, logits, masked_score), axis=0, keepdims=True)
    raised = jnp.where(chosen, jnp.exp(jnp.minimum(logits - peak, 0.0)), 0.0)
    gates = raised / jnp.sum(raised, axis=0, keepdims=True)
    summed = t0[...].astype(f32)
    for term in (t1, t2, t3, crossed):
        summed = summed + term[...].astype(f32)
    gate_grad = summed[TOK:, :TOK] + summed[TOK:, 256 : 256 + TOK]
    logit_grad = gates * (gate_grad - jnp.sum(gates * gate_grad, axis=0, keepdims=True))
    logit_grad = logit_grad.astype(bf16)
    logit_ref[...] = logit_grad
    normed_grad = summed[:TOK] + lax.dot_general(
        logit_grad, router_ref[...], TN, preferred_element_type=f32
    )
    hidden = hidden_ref[...]
    scale = inverse_rms(hidden)
    scaled_ref[...] = (normed_grad * hidden * scale).astype(bf16)
    hidden_grad = g_ref[...].astype(f32) + rms_pull(hidden, scale, gain_ref[...], normed_grad)
    hidden_grad_ref[...] = hidden_grad
    branch = hidden_grad.astype(bf16)
    branch_ref[...] = branch
    att = lax.dot_general(w_ref[:, :WIDTH], branch, NT, preferred_element_type=f32)
    att_ref[...] = att.astype(bf16).reshape(HEADS, HEAD_DIM, TOK)


def hidden_back(terms, crossed, hidden, normed, chosen, router_t, g, gain, shared):
    wide = lambda t: jax.ShapeDtypeStruct((TOK, WIDTH), t)
    return pl.pallas_call(
        hidden_back_kernel,
        out_shape=[
            wide(f32),
            wide(bf16),
            jax.ShapeDtypeStruct((EXPERTS, TOK), bf16),
            wide(bf16),
            jax.ShapeDtypeStruct((HEADS, HEAD_DIM, TOK), bf16),
        ],
        compiler_params=pltpu.CompilerParams(vmem_limit_bytes=VMEM_LIMIT),
        cost_estimate=pl.CostEstimate(
            flops=2 * TOK * WIDTH * WIDTH, bytes_accessed=8 << 20, transcendentals=0
        ),
    )(*terms, crossed, hidden, normed, chosen, router_t, g, gain, shared)


def shared_grads_kernel(att_ref, branch_ref, normed_ref, logit_ref, scaled_ref, out_ref):
    over_tokens = (((0,), (1,)), ((), ()))
    logit = jnp.concatenate([logit_ref[...], jnp.zeros((96, TOK), bf16)], axis=0)
    ones = (lax.broadcasted_iota(i32, (128, TOK), 0) == EXPERTS).astype(f32).astype(bf16)
    att = att_ref[...].reshape(WIDTH, TOK)
    grads = [
        jnp.dot(att, branch_ref[...], preferred_element_type=f32),
        lax.dot_general(normed_ref[...], logit, over_tokens, preferred_element_type=f32)
        + lax.dot_general(scaled_ref[...], ones, over_tokens, preferred_element_type=f32),
    ]
    for w in range(8):
        for part, at in zip(grads, (slice(0, WIDTH), slice(WIDTH, None))):
            rows = [part[s * 64 + w * 8 : s * 64 + w * 8 + 8] for s in range(16)]
            out_ref[w, :, at] = jnp.concatenate(rows, axis=0).astype(bf16)


def shared_weight_grads(att, branch, normed, logit_grad, scaled):
    return pl.pallas_call(
        shared_grads_kernel,
        out_shape=jax.ShapeDtypeStruct((8, 128, 1152), bf16),
        compiler_params=pltpu.CompilerParams(vmem_limit_bytes=VMEM_LIMIT),
        cost_estimate=pl.CostEstimate(
            flops=2 * TOK * WIDTH * 1280, bytes_accessed=5 << 20, transcendentals=0
        ),
    )(att, branch, normed, logit_grad, scaled)


def local(
    tokens,
    routes,
    cont_lengths,
    norm_attn,
    w_qkv,
    w_out,
    w_router,
    norm_ffn,
    w_gate_up,
    w_down,
    cotangent,
):
    seq_index = lax.axis_index("seq")
    places, blocks = relative_places(seq_index)
    rows = tokens[0]
    query_width = HEADS * HEAD_DIM
    kv_width = KV_HEADS * HEAD_DIM

    position, begin = group_layout(cont_lengths[0])
    begin = begin[None]
    table = rotary_table(position.astype(f32))
    kv_heads = lambda start: jnp.repeat(
        w_qkv[:, start : start + kv_width].reshape(8, KV_HEADS, HEAD_DIM), 2, axis=1
    )
    head_cols = jnp.concatenate(
        [
            w_qkv[:, :query_width].reshape(8, HEADS, HEAD_DIM),
            kv_heads(query_width),
            kv_heads(query_width + kv_width),
            jnp.broadcast_to(norm_attn[:, None, None], (8, HEADS, HEAD_DIM)),
        ],
        axis=2,
    ).transpose(1, 0, 2)
    head_cols = jnp.broadcast_to(head_cols[:, None], (HEADS, 8, 8, 256)).reshape(128, 8, 256)
    head_weights = lax.all_to_all(head_cols, BOTH, 0, 0, tiled=True).reshape(WIDTH, 256)
    gain_attn = head_weights[:, 192].astype(f32)[None]
    head_weights = jnp.where(jnp.arange(256)[None] < 192, head_weights, 0.0).astype(bf16)

    rows_near, rows_across = gather_near(rows)
    rows_near, _, table, head_weights = tie(rows_near, rows_across, table, head_weights)
    rows_near, rows_far = both_cores(rows_near), gather_far(rows_across)

    own_x = lax.axis_index("wshard") % 2
    expert_rows = jnp.concatenate([w_gate_up, w_down], axis=1)
    along_y = lambda t: lax.all_gather(t, "wshard", axis_index_groups=ALONG_Y, axis=0)
    experts, expert_rows = along_y(expert_rows), swap_x(expert_rows)

    qkv = project(places[:8], rows_near, head_weights, gain_attn, table, ())
    shared = jnp.concatenate(
        [w_out, w_router, norm_ffn[:, None], jnp.zeros((8, 95), bf16)], axis=1
    )
    shared, qkv = tie(shared, qkv)
    shared = lax.all_to_all(
        jnp.broadcast_to(shared[None], (128, 8, 1152)), BOTH, 0, 0, tiled=True
    ).reshape(WIDTH, 1152)
    routes_rows = jnp.pad(routes[0].T.astype(bf16), ((0, 8), (0, WIDTH - TOK)))
    upstream_rows = jnp.concatenate([cotangent[0], routes_rows], axis=0)
    rows_far, qkv, upstream_rows, expert_rows = tie(rows_far, qkv, upstream_rows, expert_rows)
    experts = [experts, along_y(expert_rows)]
    rows_far = both_cores(rows_far)
    grad_near = [upstream_rows] + [send(upstream_rows, 0, b) for b in (1, 3, 2)]
    qkv = project(places[8:], rows_far, head_weights, gain_attn, table, (qkv,))

    router_t = shared[:, WIDTH : WIDTH + EXPERTS].T
    gain_ffn = shared[:, WIDTH + EXPERTS].astype(f32)[None]
    attended_head, attended_t, lse = attend(qkv, begin)
    attended_head, shared = tie(attended_head, shared)
    attended = lax.all_to_all(attended_head, "seq", 0, 0, tiled=True)
    attended, grad_near = tie(attended, grad_near)
    grad_near = jnp.stack(grad_near)
    grad_rows = grad_near.reshape(-1, WIDTH)
    grad_far = [send(grad_rows[:EARLY], 1, 0)]
    hidden, normed_ffn = hidden_of(attended, shared, rows, gain_ffn)
    ffn_near, ffn_across = gather_near(normed_ffn)
    grad_rows, _ = tie(grad_rows, ffn_across)
    ffn_near, _, grad_far[0] = tie(ffn_near, ffn_across, grad_far[0])
    grad_far.append(send(grad_rows[EARLY:], 1, 0))
    grad_near = (grad_near, swap_cores(grad_near))
    ffn_near, ffn_far = both_cores(ffn_near), gather_far(ffn_across)
    own = jnp.stack([seq_index * 2, own_x])
    near = run_experts(0, own, ffn_near, grad_near, experts, router_t, ())
    near_terms = sum_along_z(*near[:2])
    ffn_far = both_cores(ffn_far)
    grad_far = jnp.concatenate(grad_far, axis=0).reshape(grad_near[0].shape)
    grad_far = (grad_far, swap_cores(grad_far))
    far = run_experts(1, own, ffn_far, grad_far, experts, router_t, near[2:])
    far, near_terms = tie(far, near_terms)
    moved, saved = far[2:4], far[4:]
    far_other, moved_other = tie(swap_cores(far[1]), moved[1])
    far_terms = send_along_z(chip_parts(far[0], far_other))
    expert_grads = expert_weight_grads(*saved)
    moved_other = swap_cores(moved_other)
    far_terms, expert_grads, moved_other = tie(far_terms, expert_grads, moved_other)
    crossed = send(add_low(*far_terms), 1, 0)
    by_x = [t.reshape(2, 4, TOK, WIDTH) for t in (moved[0], moved_other)]
    moved_parts = [add_low(by_x[0][:, i], by_x[1][:, i]) for i in range(4)]
    crossed, moved_parts = tie(crossed, moved_parts)

    expert_range = jnp.arange(EXPERTS, dtype=i32)
    chosen_here = jnp.any(routes[0].T[None] == expert_range[:, None, None], axis=1).astype(f32)
    hidden_grad, branch_grad, logit_grad, scaled_grad, attended_grad = hidden_back(
        near_terms, crossed, hidden, normed_ffn, chosen_here, router_t, cotangent[0], gain_ffn, shared
    )
    expert_grads = lax.psum_scatter(
        expert_grads.reshape(8, 2, 192, 1024),
        "wshard",
        axis_index_groups=ALONG_Y,
        scatter_dimension=0,
        tiled=True,
    )
    head_grad = lax.all_to_all(attended_grad, "seq", 0, 0, tiled=True)
    shared_grads = shared_weight_grads(attended, branch_grad, normed_ffn, logit_grad, scaled_grad)
    head_grad, shared_grads, moved_parts = tie(head_grad, shared_grads, moved_parts)
    moved_terms = [moved_parts[0]] + [
        send(moved_parts[i], 0, -b) for i, b in ((1, 1), (2, 3), (3, 2))
    ]

    shared_grads = lax.all_to_all(shared_grads, "wshard", 0, 0, tiled=True)
    projected_grad = attend_back(qkv, head_grad, attended_t, lse, begin, table)
    grad_head = head_weight_grad(places, rows_near, rows_far, gain_attn, projected_grad)
    shared_grads, grad_head, projected_grad, moved_terms = tie(
        shared_grads, grad_head, projected_grad, moved_terms
    )
    shared_grads = jnp.sum(shared_grads.astype(f32), axis=0)
    moved_crossed = add_low(*[t[1] for t in moved_terms])
    shared_grads, moved_crossed = tie(shared_grads, moved_crossed)
    moved_crossed = send(moved_crossed, 1, 0)
    far_part = project_back(places[8:], projected_grad, head_weights, shared_grads)
    near_part = project_back(places[:8], projected_grad, head_weights, shared_grads)
    far_parts = chip_parts(far_part[0], swap_cores(far_part[1]))
    near_parts = chip_parts(near_part[0], swap_cores(near_part[1]))
    far_parts, near_parts, grad_head = tie(far_parts, near_parts, grad_head)
    far_terms, moved_crossed, expert_grads = tie(
        send_along_z(far_parts), moved_crossed, expert_grads
    )
    near_terms = send_along_z(near_parts)
    grad_heads = lax.all_to_all(grad_head.reshape(128, 8, 256), BOTH, 0, 0, tiled=True)
    crossed = send(add_low(*far_terms), 1, 0)
    crossed, near_terms, grad_heads = tie(crossed, near_terms, grad_heads)
    kept = lax.dynamic_index_in_dim(expert_grads, own_x, 0, keepdims=False)
    sent = lax.dynamic_index_in_dim(expert_grads, 1 - own_x, 0, keepdims=False)
    expert_grads = kept.astype(f32) + swap_x(sent).astype(f32)
    total = lambda terms: sum([t.astype(f32) for t in terms])
    output = (hidden + total([t[0] for t in moved_terms] + [moved_crossed])).astype(bf16)
    last_sum = total(near_terms + [crossed])
    normed_grad, shared_grads = last_sum[:TOK], last_sum[TOK:]
    grad_heads = jnp.sum(grad_heads.reshape(16, 8, 8, 256).astype(f32), axis=1).transpose(1, 0, 2)
    kv_sum = lambda start: jnp.sum(
        grad_heads[:, :, start : start + HEAD_DIM].reshape(8, KV_HEADS, 2, HEAD_DIM), axis=2
    ).reshape(8, kv_width)
    grad_qkv = jnp.concatenate(
        [grad_heads[:, :, :HEAD_DIM].reshape(8, query_width), kv_sum(HEAD_DIM), kv_sum(2 * HEAD_DIM)],
        axis=1,
    )
    grad_norm_attn = jnp.sum(grad_qkv * w_qkv.astype(f32), axis=1) / norm_attn.astype(f32)
    inputs = rows.astype(f32)
    grad_input = hidden_grad + rms_pull(inputs, inverse_rms(inputs), gain_attn, normed_grad)
    return (
        output[None],
        grad_input[None],
        grad_norm_attn,
        grad_qkv,
        shared_grads[:8],
        shared_grads[8:, :EXPERTS],
        shared_grads[8:, EXPERTS],
        expert_grads[:, :128],
        expert_grads[:, 128:],
    )


def solution(mesh):
    return jax.shard_map(
        local,
        mesh=mesh,
        in_specs=(
            P("wshard", "seq", None),
            P("wshard", "seq", None),
            P("wshard", None),
            P(BOTH),
            P(BOTH, None),
            P(BOTH, None),
            P(BOTH, None),
            P(BOTH),
            P("seq", "wshard", None),
            P("seq", "wshard", None),
            P("wshard", "seq", None),
        ),
        out_specs=(
            P("wshard", "seq", None),
            P("wshard", "seq", None),
            P(BOTH),
            P(BOTH, None),
            P(BOTH, None),
            P(BOTH, None),
            P(BOTH),
            P("seq", "wshard", None),
            P("seq", "wshard", None),
        ),
        check_vma=False,
    )
```

```python
import jax
import jax.numpy as jnp
from jax import lax
from jax.experimental import pallas as pl
from jax.experimental.pallas import tpu as pltpu
from jax.sharding import PartitionSpec as P

HEADS = 16
KV_HEADS = 8
HEAD_DIM = 64
EXPERTS = 32
FF = 512
PROMPT = 2048
GROUP = 3584
TOK = 224
WIDTH = 1024
SLOTS = 72
STEP_ROWS = 4 * SLOTS
ALL_ROWS = 16 * SLOTS
BLOCK = 512
VMEM_LIMIT = 60 << 20
LAST = TOK + 16
EARLY = 352
PAY = TOK + 32

norm_eps = 1e-06
rope_base = 10000.0
masked_score = -1e30
BOTH = ("seq", "wshard")
NT = (((1,), (1,)), ((), ()))
TN = (((0,), (0,)), ((), ()))
f32 = jnp.float32
bf16 = jnp.bfloat16
i32 = jnp.int32


def place_of(x, z, core):
    return x * 8 + z * 2 + core


def shift_perm(a, b):
    return [
        (place_of(x, z, c), place_of(x ^ a, (z + b) % 4, c))
        for x in range(2)
        for z in range(4)
        for c in range(2)
    ]


CORE_PERM = [(i, i ^ 1) for i in range(16)]


def send(rows, a, b):
    return lax.ppermute(rows, "seq", shift_perm(a, b))


def swap_cores(rows):
    return lax.ppermute(rows, "seq", CORE_PERM)


def relative_places(seq_index):
    x, z, c = seq_index // 8, (seq_index // 2) % 4, seq_index % 2
    r = jnp.arange(16, dtype=i32)
    a, i, k = r // 8, (r // 2) % 4, r % 2
    shift = i ^ (i // 2)
    behind = (z - i) % 4
    places = (a ^ x) * 8 + ((z - shift) % 4) * 2 + (k ^ c)
    return places, (a ^ x) * 8 + (behind ^ (behind // 2)) * 2 + (k ^ c)


def gather_near(rows):
    return [rows] + [send(rows, 0, b) for b in (1, 3, 2)], send(rows, 1, 0)


def both_cores(parts):
    mine = jnp.stack(parts)
    return mine, swap_cores(mine)


def gather_far(across):
    return [across] + [send(across, 0, b) for b in (1, 3, 2)]


def add_low(*terms):
    return sum([t.astype(f32) for t in terms]).astype(bf16)


def sum_along_z(mine, other):
    return send_along_z(chip_parts(mine, swap_cores(other)))


def chip_parts(mine, got):
    return [add_low(mine[i], got[i]) for i in range(4)]


def send_along_z(parts):
    return [parts[0]] + [send(parts[i], 0, -b) for i, b in ((1, 1), (2, 3), (3, 2))]


def swap_x(rows):
    return lax.ppermute(rows, "wshard", [(w, w ^ 1) for w in range(8)])


ALONG_Y = [[y * 2 + x for y in range(4)] for x in range(2)]


def tie(*values):
    return lax.optimization_barrier(values)


def inverse_rms(values):
    return lax.rsqrt(jnp.mean(values * values, axis=-1, keepdims=True) + norm_eps)


def rms_pull(values, scale, gain, grad):
    scaled = grad * gain
    return scale * scaled - values * (scale * scale * scale) * jnp.mean(
        scaled * values, axis=-1, keepdims=True
    )


def group_layout(lengths):
    places = jnp.arange(GROUP, dtype=i32)
    ends = jnp.cumsum(lengths)
    starts = ends - lengths
    offset_in = places - PROMPT
    segment_id = jnp.sum((offset_in[:, None] >= ends[None, :]).astype(i32), axis=1)
    segment_hot = segment_id[:, None] == jnp.arange(lengths.shape[0], dtype=i32)[None, :]
    begin = jnp.sum(jnp.where(segment_hot, starts[None, :], 0), axis=1)
    inside = offset_in >= 0
    position = jnp.where(inside, PROMPT + offset_in - begin, places)
    return position, jnp.where(inside, PROMPT + begin, 0)


def rotary_table(position):
    half_dim = HEAD_DIM // 2
    inverse = rope_base ** (-((jnp.arange(2 * HEAD_DIM) % half_dim).astype(f32) * 2.0) / HEAD_DIM)
    back = jnp.where(jnp.arange(2 * HEAD_DIM) < HEAD_DIM, 0.0, 0.5 * jnp.pi).astype(f32)
    return jnp.cos(position[:, None] * inverse[None, :] - back[None, :])


def turn(values):
    half_dim = HEAD_DIM // 2
    return jnp.concatenate([-values[:, half_dim:], values[:, :half_dim]], axis=-1)


def turn_back(values):
    half_dim = HEAD_DIM // 2
    return jnp.concatenate([values[:, half_dim:], -values[:, :half_dim]], axis=-1)


def project_kernel(places, mine, other, w, gain, table, *refs):
    out = refs[-1]
    j = pl.program_id(0)

    if len(refs) > 1:

        @pl.when(j == 0)
        def _():
            out[...] = refs[0][...]

    for k, ref in enumerate((mine, other)):
        at = pl.ds(pl.multiple_of(places[2 * j + k] * TOK, TOK), TOK)
        rows = ref[0].astype(f32)
        normed = (rows * inverse_rms(rows) * gain[...]).astype(bf16)
        projected = jnp.dot(normed, w[...], preferred_element_type=f32)
        c, s = table[at, :HEAD_DIM], table[at, HEAD_DIM:]
        q, k, v = projected[:, :64], projected[:, 64:128], projected[:, 128:]
        q = (q * c + turn(q) * s).astype(bf16).astype(f32) * HEAD_DIM**-0.5
        out[at, :] = jnp.concatenate([q, k * c + turn(k) * s, v], axis=1).astype(bf16)


def project(places, gathered, w, gain, table, before):
    chip = pl.BlockSpec((1, TOK, WIDTH), lambda j, p: (j, 0, 0))
    whole = lambda *shape: pl.BlockSpec(shape, lambda j, p: (0,) * len(shape))
    return pl.pallas_call(
        project_kernel,
        grid_spec=pltpu.PrefetchScalarGridSpec(
            num_scalar_prefetch=1,
            grid=(4,),
            in_specs=[chip, chip, whole(WIDTH, 256), whole(1, WIDTH), whole(GROUP, 128)]
            + [whole(GROUP, 256)] * len(before),
            out_specs=whole(GROUP, 256),
        ),
        out_shape=jax.ShapeDtypeStruct((GROUP, 256), bf16),
        compiler_params=pltpu.CompilerParams(vmem_limit_bytes=VMEM_LIMIT),
        cost_estimate=pl.CostEstimate(
            flops=2 * 8 * TOK * WIDTH * 256, bytes_accessed=10 << 20, transcendentals=0
        ),
    )(places, *gathered, w, gain, table, *before)


def project_back_kernel(places, first, second, w, first_shared, second_shared, mine, other):
    del places
    for projected, shared, out in ((first, first_shared, mine), (second, second_shared, other)):
        out[0, :TOK, :] = lax.dot_general(
            projected[...], w[...], NT, preferred_element_type=f32
        ).astype(bf16)
        rest = jnp.concatenate([shared[:, WIDTH:], jnp.zeros((8, WIDTH - 128), f32)], axis=1)
        out[0, TOK:, :] = jnp.concatenate([shared[:, :WIDTH], rest], axis=0).astype(bf16)


def project_back(places, projected_grad, w, shared):
    chip = pl.BlockSpec((1, LAST, WIDTH), lambda j, p: (j, 0, 0))
    at = lambda k, rows, n: pl.BlockSpec((rows, n), lambda j, p: (p[2 * j + k], 0))
    part = jax.ShapeDtypeStruct((4, LAST, WIDTH), bf16)
    return pl.pallas_call(
        project_back_kernel,
        grid_spec=pltpu.PrefetchScalarGridSpec(
            num_scalar_prefetch=1,
            grid=(4,),
            in_specs=[
                at(0, TOK, 256),
                at(1, TOK, 256),
                pl.BlockSpec((WIDTH, 256), lambda j, p: (0, 0)),
                at(0, 8, 1152),
                at(1, 8, 1152),
            ],
            out_specs=[chip, chip],
        ),
        out_shape=[part, part],
        compiler_params=pltpu.CompilerParams(vmem_limit_bytes=VMEM_LIMIT),
        cost_estimate=pl.CostEstimate(
            flops=2 * 8 * TOK * WIDTH * 256, bytes_accessed=5 << 20, transcendentals=0
        ),
    )(places, projected_grad, projected_grad, w, shared, shared)


def head_grad_kernel(places, near_mine, near_other, far_mine, far_other, gain, first, second, out, total):
    del places
    j = pl.program_id(0)

    @pl.when(j == 0)
    def _():
        total[...] = jnp.zeros_like(total)

    for near, far, projected in ((near_mine, far_mine, first), (near_other, far_other, second)):
        rows = jnp.where(j < 4, near[0], far[0]).astype(f32)
        normed = (rows * inverse_rms(rows) * gain[...]).astype(bf16)
        total[...] += lax.dot_general(normed, projected[...], TN, preferred_element_type=f32)

    @pl.when(j == 7)
    def _():
        out[...] = total[...].astype(bf16)


def head_weight_grad(places, near, far, gain, projected_grad):
    near_chip = pl.BlockSpec((1, TOK, WIDTH), lambda j, p: (jnp.minimum(j, 3), 0, 0))
    far_chip = pl.BlockSpec((1, TOK, WIDTH), lambda j, p: (jnp.maximum(j - 4, 0), 0, 0))
    at = lambda k: pl.BlockSpec((TOK, 256), lambda j, p: (p[2 * j + k], 0))
    return pl.pallas_call(
        head_grad_kernel,
        grid_spec=pltpu.PrefetchScalarGridSpec(
            num_scalar_prefetch=1,
            grid=(8,),
            in_specs=[
                near_chip,
                near_chip,
                far_chip,
                far_chip,
                pl.BlockSpec((1, WIDTH), lambda j, p: (0, 0)),
                at(0),
                at(1),
            ],
            out_specs=pl.BlockSpec((WIDTH, 256), lambda j, p: (0, 0)),
            scratch_shapes=[pltpu.VMEM((WIDTH, 256), f32)],
        ),
        out_shape=jax.ShapeDtypeStruct((WIDTH, 256), bf16),
        compiler_params=pltpu.CompilerParams(vmem_limit_bytes=VMEM_LIMIT),
        cost_estimate=pl.CostEstimate(
            flops=2 * 16 * TOK * WIDTH * 256, bytes_accessed=10 << 20, transcendentals=0
        ),
    )(places, *near, *far, gain, projected_grad, projected_grad)


def tile_mask(scores, key_start, query_start, begin):
    keys = key_start + lax.broadcasted_iota(i32, scores.shape, 0)
    queries = query_start + lax.broadcasted_iota(i32, scores.shape, 1)
    return jnp.where((keys <= queries) & (keys >= begin), scores, masked_score)


def key_ranges(i):
    first = PROMPT // BLOCK
    return jnp.where(i > first, i - 1, i), jnp.minimum(i, first)


def attend_kernel(qkv_ref, begin_ref, o_ref, ot_ref, lse_ref, keys, vt):
    i = pl.program_id(0)
    here = pl.ds(pl.multiple_of(i * BLOCK, BLOCK), BLOCK)

    @pl.when(i == 0)
    def _():
        keys[...] = qkv_ref[:, 64:128]
        vt[...] = qkv_ref[:, 128:192].T

    q = qkv_ref[here, :64]
    begin = begin_ref[...]

    def tile(j, carry, masked, n=1):
        peak, total, out = carry
        start = pl.multiple_of(j * BLOCK, BLOCK)
        at = pl.ds(start, n * BLOCK)
        s = lax.dot_general(keys[at, :], q, NT, preferred_element_type=f32)
        if masked:
            s = tile_mask(s, start, i * BLOCK, begin)
        higher = jnp.maximum(peak, jnp.max(s, axis=0, keepdims=True))
        p = jnp.exp(s - higher)
        fade = jnp.exp(peak - higher)
        total = total * fade + jnp.sum(p, axis=0, keepdims=True)
        out = out * fade + jnp.dot(vt[:, at], p.astype(bf16), preferred_element_type=f32)
        return higher, total, out

    carry = (
        jnp.full((1, BLOCK), masked_score, f32),
        jnp.zeros((1, BLOCK), f32),
        jnp.zeros((HEAD_DIM, BLOCK), f32),
    )
    carry = tile(i, carry, True)
    window, shared = key_ranges(i)
    carry = lax.fori_loop(window, i, lambda j, c: tile(j, c, True), carry)
    pairs = shared // 2
    carry = lax.fori_loop(0, pairs, lambda j, c: tile(2 * j, c, False, 2), carry)
    peak, total, out = lax.fori_loop(2 * pairs, shared, lambda j, c: tile(j, c, False), carry)
    ot_ref[:, here] = out * (1.0 / total)
    lse_ref[...] = peak + jnp.log(total)

    @pl.when(i == GROUP // BLOCK - 1)
    def _():
        for b in range(16):
            o_ref[b] = ot_ref[:, b * TOK : (b + 1) * TOK].astype(bf16)


def attend(qkv, begin):
    whole = lambda *shape: pl.BlockSpec(shape, lambda i: (0,) * len(shape))
    cols = lambda n: pl.BlockSpec((n, BLOCK), lambda i: (0, i))
    return pl.pallas_call(
        attend_kernel,
        grid=(GROUP // BLOCK,),
        in_specs=[whole(GROUP, 256), cols(1)],
        out_specs=[whole(16, HEAD_DIM, TOK), whole(HEAD_DIM, GROUP), cols(1)],
        out_shape=[
            jax.ShapeDtypeStruct((16, HEAD_DIM, TOK), bf16),
            jax.ShapeDtypeStruct((HEAD_DIM, GROUP), f32),
            jax.ShapeDtypeStruct((1, GROUP), f32),
        ],
        scratch_shapes=[
            pltpu.VMEM((GROUP, HEAD_DIM), bf16),
            pltpu.VMEM((HEAD_DIM, GROUP), bf16),
        ],
        compiler_params=pltpu.CompilerParams(vmem_limit_bytes=VMEM_LIMIT),
        cost_estimate=pl.CostEstimate(
            flops=2 * 27 * BLOCK * BLOCK * 512, bytes_accessed=4 << 20, transcendentals=27 * BLOCK * BLOCK
        ),
    )(qkv, begin)


def attend_back_kernel(
    qkv_ref, g_ref, ot_ref, lse_ref, begin_ref, table, out_ref, keys, values, kt, gt, dq, dk, dv
):
    i = pl.program_id(0)
    here = pl.ds(pl.multiple_of(i * BLOCK, BLOCK), BLOCK)

    @pl.when(i == 0)
    def _():
        dk[...] = jnp.zeros_like(dk)
        dv[...] = jnp.zeros_like(dv)
        keys[...] = qkv_ref[:, 64:128]
        values[...] = qkv_ref[:, 128:192]
        kt[...] = qkv_ref[:, 64:128].T
        for b in range(16):
            gt[:, b * TOK : (b + 1) * TOK] = g_ref[b]

    q = qkv_ref[here, :64]
    g = gt[:, here]
    begin = begin_ref[...]
    lse = lse_ref[...]
    inner = jnp.sum(g.astype(f32) * ot_ref[...], axis=0, keepdims=True)

    def tile(j, dq, masked, n=1):
        start = pl.multiple_of(j * BLOCK, BLOCK)
        at = pl.ds(start, n * BLOCK)
        s = lax.dot_general(keys[at, :], q, NT, preferred_element_type=f32)
        if masked:
            s = tile_mask(s, start, i * BLOCK, begin)
        p = jnp.exp(s - lse)
        dp = jnp.dot(values[at, :], g, preferred_element_type=f32)
        ds = (p * (dp - inner)).astype(bf16)
        dv[at, :] += lax.dot_general(p.astype(bf16), g, NT, preferred_element_type=f32)
        dk[at, :] += jnp.dot(ds, q, preferred_element_type=f32)
        return dq + jnp.dot(kt[:, at], ds, preferred_element_type=f32)

    dqt = tile(i, jnp.zeros((HEAD_DIM, BLOCK), f32), True)
    window, shared = key_ranges(i)
    dqt = lax.fori_loop(window, i, lambda j, c: tile(j, c, True), dqt)
    pairs = shared // 2
    dqt = lax.fori_loop(0, pairs, lambda j, c: tile(2 * j, c, False, 2), dqt)
    dqt = lax.fori_loop(2 * pairs, shared, lambda j, c: tile(j, c, False), dqt)
    dq[here, :] = dqt.T * HEAD_DIM**-0.5

    @pl.when(i == GROUP // BLOCK - 1)
    def _():
        def back(b, _):
            at = pl.ds(pl.multiple_of(b * BLOCK, BLOCK), BLOCK)
            c, s = table[at, :HEAD_DIM], table[at, HEAD_DIM:]
            q, k = dq[at, :].astype(bf16).astype(f32), dk[at, :].astype(bf16).astype(f32)
            parts = [q * c + turn_back(q * s), k * c + turn_back(k * s), dv[at, :], jnp.zeros_like(q)]
            out_ref[at, :] = jnp.concatenate(parts, axis=1).astype(bf16)
            return 0

        lax.fori_loop(0, GROUP // BLOCK, back, 0)


def attend_back(qkv, g, ot, lse, begin, table):
    whole = lambda *shape: pl.BlockSpec(shape, lambda i: (0,) * len(shape))
    cols = lambda n: pl.BlockSpec((n, BLOCK), lambda i: (0, i))
    return pl.pallas_call(
        attend_back_kernel,
        grid=(GROUP // BLOCK,),
        in_specs=[
            whole(GROUP, 256),
            whole(16, HEAD_DIM, TOK),
            cols(HEAD_DIM),
            cols(1),
            cols(1),
            whole(GROUP, 128),
        ],
        out_specs=whole(GROUP, 256),
        out_shape=jax.ShapeDtypeStruct((GROUP, 256), bf16),
        scratch_shapes=[
            pltpu.VMEM((GROUP, HEAD_DIM), bf16),
            pltpu.VMEM((GROUP, HEAD_DIM), bf16),
            pltpu.VMEM((HEAD_DIM, GROUP), bf16),
            pltpu.VMEM((HEAD_DIM, GROUP), bf16),
            pltpu.VMEM((GROUP, HEAD_DIM), f32),
            pltpu.VMEM((GROUP, HEAD_DIM), f32),
            pltpu.VMEM((GROUP, HEAD_DIM), f32),
        ],
        compiler_params=pltpu.CompilerParams(vmem_limit_bytes=VMEM_LIMIT),
        cost_estimate=pl.CostEstimate(
            flops=5 * 27 * BLOCK * BLOCK * 512, bytes_accessed=8 << 20, transcendentals=27 * BLOCK * BLOCK
        ),
    )(qkv, g, ot, lse, begin, table)


def experts_kernel(
    own_ref, ffn_mine, ffn_other, g_mine, g_other, routes_mine, routes_other, router_ref, own_w, across_w, *refs
):
    routed_mine, routed_other, moved_mine, moved_other = refs[-10:-6]
    x_ref, dh_ref, act_ref, dy_ref, w_ref, sem = refs[-6:]
    own = own_ref[0]

    copies = [
        [
            pltpu.make_async_copy(shards.at[y, e], w_ref.at[e, 2 * y + (own_ref[1] ^ a)], sem.at[a, y, e])
            for a, shards in enumerate((own_w, across_w))
            for y in range(4)
        ]
        for e in range(2)
    ]

    @pl.when(pl.program_id(0) == 0)
    def _():
        for copy in copies[0] + copies[1]:
            copy.start()

    expert_rows = lax.broadcasted_iota(i32, (EXPERTS, TOK), 0)
    slot_rows = lax.broadcasted_iota(i32, (SLOTS, TOK), 0).astype(f32)
    upto = (
        lax.broadcasted_iota(i32, (TOK, TOK), 0) <= lax.broadcasted_iota(i32, (TOK, TOK), 1)
    ).astype(f32).astype(bf16)
    slot_cols = []
    gate_grads = [jnp.zeros((EXPERTS, WIDTH), f32) for _ in range(4)]
    payload_rows = lax.broadcasted_iota(i32, (EXPERTS, WIDTH), 0)
    gate_rows = [[], []]
    picks = [[], []]
    picked_rows = [[], []]
    picked_grads = [[], []]
    blocks = [(ffn_mine, g_mine, routes_mine, 0), (ffn_other, g_other, routes_other, 0)]
    blocks = blocks + [(*refs_of[:3], 1) for refs_of in blocks]
    for rows_ref, grads_ref, routes_ref, n in blocks:
        rows, grads = rows_ref[n], grads_ref[n]
        routes = routes_ref[n][:8, :TOK].astype(f32).astype(i32)
        chosen = expert_rows == routes[0:1]
        for j in range(1, 8):
            chosen = chosen | (expert_rows == routes[j : j + 1])
        named = [jnp.max((routes == own + e).astype(f32), axis=0, keepdims=True) for e in range(2)]
        named = jnp.concatenate(named + [jnp.zeros((6, TOK), f32)], axis=0)
        rank = jnp.dot(named.astype(bf16), upto, preferred_element_type=f32)
        slots = jnp.where(named > 0, rank - 1.0, -1.0)
        slot_cols.append(slots.T)
        logits = lax.dot_general(router_ref[...], rows, NT, preferred_element_type=f32)
        peak = jnp.max(jnp.where(chosen, logits, masked_score), axis=0, keepdims=True)
        raised = jnp.where(chosen, jnp.exp(jnp.minimum(logits - peak, 0.0)), 0.0)
        gates = raised / jnp.sum(raised, axis=0, keepdims=True)
        for e in range(2):
            gate_rows[e].append(
                jnp.sum(jnp.where(expert_rows == own + e, gates, 0.0), axis=0, keepdims=True)
            )
            picks[e].append((slots[e : e + 1] == slot_rows).astype(f32))
        low = jnp.concatenate([picks[0][-1], picks[1][-1]], axis=0).astype(bf16)
        for source, kept in ((rows, picked_rows), (grads, picked_grads)):
            both = jnp.dot(low, source, preferred_element_type=f32)
            kept[0].append(both[:SLOTS])
            kept[1].append(both[SLOTS:])
    moved, routed = [], []
    for e in range(2):

        @pl.when(pl.program_id(0) == 0)
        def _():
            for copy in copies[e]:
                copy.wait()

        w_gate_up = w_ref[e, :, :128, :].reshape(WIDTH, 2 * FF)
        w_down = w_ref[e, :, 128:, :].reshape(FF, WIDTH)
        x = jnp.concatenate(picked_rows[e], axis=0).astype(bf16)
        gate = jnp.concatenate(
            [jnp.sum(p * r, axis=1, keepdims=True) for p, r in zip(picks[e], gate_rows[e])], axis=0
        )
        grads = jnp.concatenate(picked_grads[e], axis=0)
        dy = (gate * grads).astype(bf16)
        mixed = jnp.dot(x, w_gate_up, preferred_element_type=f32)
        dact = lax.dot_general(dy, w_down, NT, preferred_element_type=f32)
        gate_part, up_part = mixed[:, :FF], mixed[:, FF:]
        sigma = 1.0 / (1.0 + jnp.exp(-gate_part))
        silu = gate_part * sigma
        act = (silu * up_part).astype(bf16)
        dh = jnp.concatenate(
            [dact * up_part * (sigma + silu * (1.0 - sigma)), dact * silu], axis=1
        ).astype(bf16)
        x_ref[e] = x
        dy_ref[e] = dy
        act_ref[e] = act
        dh_ref[e] = dh
        returned = jnp.dot(act, w_down, preferred_element_type=f32).astype(bf16).astype(f32)
        dgate = jnp.sum(returned * grads, axis=1, keepdims=True)
        for b in range(4):
            grad = jnp.sum(
                picks[e][b] * dgate[b * SLOTS : (b + 1) * SLOTS], axis=0, keepdims=True
            )
            high = grad.astype(bf16).astype(f32)
            gap = jnp.zeros((1, 256 - TOK), f32)
            wide = jnp.concatenate([high, gap, grad - high, gap, jnp.zeros((1, WIDTH - 512), f32)], axis=1)
            gate_grads[b] = gate_grads[b] + jnp.where(payload_rows == own + e, wide, 0.0)
        moved.append(gate * returned)
        routed.append(lax.dot_general(dh, w_gate_up, NT, preferred_element_type=f32))
    columns = lax.broadcasted_iota(i32, (TOK, 2 * SLOTS), 1).astype(f32)
    outs = [(routed_mine, moved_mine, 0), (routed_other, moved_other, 0), (routed_mine, moved_mine, 1), (routed_other, moved_other, 1)]
    for b, (routed_ref, moved_ref, n) in enumerate(outs):
        first, second = slot_cols[b][:, 0:1], slot_cols[b][:, 1:2]
        back = ((columns == first) | ((columns == second + SLOTS) & (second >= 0))).astype(f32).astype(bf16)
        at = slice(b * SLOTS, (b + 1) * SLOTS)
        for terms, ref in ((routed, routed_ref), (moved, moved_ref)):
            joined = jnp.concatenate([terms[0][at], terms[1][at]], axis=0).astype(bf16)
            ref[n, :TOK, :] = jnp.dot(back, joined, preferred_element_type=f32).astype(bf16)
        routed_ref[n, TOK:, :] = gate_grads[b].astype(bf16)


def run_experts(half, own, ffn, grads, weights, router, before):
    pair = pl.BlockSpec((2, TOK, WIDTH), lambda i, o: (i, 0, 0))
    pair_of_all = pl.BlockSpec((2, TOK, WIDTH), lambda i, o: (i + 2 * half, 0, 0))
    whole = lambda shape: pl.BlockSpec(shape, lambda i, o: (0,) * len(shape))
    routes = pl.BlockSpec((2, 16, 256), lambda i, o: (i, TOK // 16, 0))
    summed = pl.BlockSpec((2, PAY, WIDTH), lambda i, o: (i, 0, 0))
    kept = lambda n: pl.BlockSpec((2, STEP_ROWS, n), lambda i, o: (0, i + 2 * half, 0))
    part = jax.ShapeDtypeStruct((4, PAY, WIDTH), bf16)
    keep = lambda n: jax.ShapeDtypeStruct((2, ALL_ROWS, n), bf16)
    return pl.pallas_call(
        experts_kernel,
        grid_spec=pltpu.PrefetchScalarGridSpec(
            num_scalar_prefetch=1,
            grid=(2,),
            in_specs=[
                pair,
                pair,
                pair,
                pair,
                routes,
                routes,
                whole((EXPERTS, WIDTH)),
            ]
            + [pl.BlockSpec(memory_space=pl.ANY)] * (2 + len(before)),
            out_specs=[
                summed,
                summed,
                pair_of_all,
                pair_of_all,
                kept(WIDTH),
                kept(2 * FF),
                kept(FF),
                kept(WIDTH),
            ],
            scratch_shapes=[
                pltpu.VMEM((2, 8, 192, 1024), bf16),
                pltpu.SemaphoreType.DMA((2, 4, 2)),
            ],
        ),
        out_shape=[
            part,
            part,
            jax.ShapeDtypeStruct((8, TOK, WIDTH), bf16),
            jax.ShapeDtypeStruct((8, TOK, WIDTH), bf16),
            keep(WIDTH),
            keep(2 * FF),
            keep(FF),
            keep(WIDTH),
        ],
        input_output_aliases={10 + i: 2 + i for i in range(len(before))},
        compiler_params=pltpu.CompilerParams(vmem_limit_bytes=VMEM_LIMIT),
        cost_estimate=pl.CostEstimate(
            flops=14 << 30, bytes_accessed=24 << 20, transcendentals=8 * SLOTS * 2 * FF
        ),
    )(own, *ffn, *grads, *grads, router, *weights, *before)


def expert_grads_kernel(x_ref, dh_ref, act_ref, dy_ref, out_ref):
    up = lax.dot_general(x_ref[0], dh_ref[0], TN, preferred_element_type=f32)
    down = lax.dot_general(act_ref[0], dy_ref[0], TN, preferred_element_type=f32)
    out_ref[0, :, 0, :128, :] = up.astype(bf16).reshape(2, 128, 2 * FF)
    out_ref[0, :, 0, 128:, :] = down.astype(bf16).reshape(2, 64, WIDTH)


def expert_weight_grads(x, dh, act, dy):
    return pl.pallas_call(
        expert_grads_kernel,
        grid=(2, 4),
        in_specs=[
            pl.BlockSpec((1, ALL_ROWS, 256), lambda e, i: (e, 0, i)),
            pl.BlockSpec((1, ALL_ROWS, 2 * FF), lambda e, i: (e, 0, 0)),
            pl.BlockSpec((1, ALL_ROWS, 128), lambda e, i: (e, 0, i)),
            pl.BlockSpec((1, ALL_ROWS, WIDTH), lambda e, i: (e, 0, 0)),
        ],
        out_specs=pl.BlockSpec((1, 2, 1, 192, 1024), lambda e, i: (i, 0, e, 0, 0)),
        out_shape=jax.ShapeDtypeStruct((4, 2, 2, 192, 1024), bf16),
        compiler_params=pltpu.CompilerParams(vmem_limit_bytes=VMEM_LIMIT),
        cost_estimate=pl.CostEstimate(flops=8 << 30, bytes_accessed=14 << 20, transcendentals=0),
    )(x, dh, act, dy)


def hidden_kernel(att_ref, w_ref, rows_ref, gain_ref, hidden_ref, normed_ref):
    att = att_ref[...].reshape(WIDTH, TOK)
    hidden = rows_ref[...].astype(f32) + lax.dot_general(
        att, w_ref[:, :WIDTH], TN, preferred_element_type=f32
    )
    hidden_ref[...] = hidden
    normed_ref[...] = (hidden * inverse_rms(hidden) * gain_ref[...]).astype(bf16)


def hidden_of(attended, shared, rows, gain):
    return pl.pallas_call(
        hidden_kernel,
        out_shape=[
            jax.ShapeDtypeStruct((TOK, WIDTH), f32),
            jax.ShapeDtypeStruct((TOK, WIDTH), bf16),
        ],
        compiler_params=pltpu.CompilerParams(vmem_limit_bytes=VMEM_LIMIT),
        cost_estimate=pl.CostEstimate(
            flops=2 * TOK * WIDTH * WIDTH, bytes_accessed=5 << 20, transcendentals=0
        ),
    )(attended, shared, rows, gain)


def hidden_back_kernel(
    t0, t1, t2, t3, crossed, hidden_ref, normed_ref, chosen_ref, router_ref, g_ref, gain_ref,
    w_ref, hidden_grad_ref, branch_ref, logit_ref, scaled_ref, att_ref
):
    chosen = chosen_ref[...] > 0
    logits = lax.dot_general(router_ref[...], normed_ref[...], NT, preferred_element_type=f32)
    peak = jnp.max(jnp.where(chosen, logits, masked_score), axis=0, keepdims=True)
    raised = jnp.where(chosen, jnp.exp(jnp.minimum(logits - peak, 0.0)), 0.0)
    gates = raised / jnp.sum(raised, axis=0, keepdims=True)
    summed = t0[...].astype(f32)
    for term in (t1, t2, t3, crossed):
        summed = summed + term[...].astype(f32)
    gate_grad = summed[TOK:, :TOK] + summed[TOK:, 256 : 256 + TOK]
    logit_grad = gates * (gate_grad - jnp.sum(gates * gate_grad, axis=0, keepdims=True))
    logit_grad = logit_grad.astype(bf16)
    logit_ref[...] = logit_grad
    normed_grad = summed[:TOK] + lax.dot_general(
        logit_grad, router_ref[...], TN, preferred_element_type=f32
    )
    hidden = hidden_ref[...]
    scale = inverse_rms(hidden)
    scaled_ref[...] = (normed_grad * hidden * scale).astype(bf16)
    hidden_grad = g_ref[...].astype(f32) + rms_pull(hidden, scale, gain_ref[...], normed_grad)
    hidden_grad_ref[...] = hidden_grad
    branch = hidden_grad.astype(bf16)
    branch_ref[...] = branch
    att = lax.dot_general(w_ref[:, :WIDTH], branch, NT, preferred_element_type=f32)
    att_ref[...] = att.astype(bf16).reshape(HEADS, HEAD_DIM, TOK)


def hidden_back(terms, crossed, hidden, normed, chosen, router_t, g, gain, shared):
    wide = lambda t: jax.ShapeDtypeStruct((TOK, WIDTH), t)
    return pl.pallas_call(
        hidden_back_kernel,
        out_shape=[
            wide(f32),
            wide(bf16),
            jax.ShapeDtypeStruct((EXPERTS, TOK), bf16),
            wide(bf16),
            jax.ShapeDtypeStruct((HEADS, HEAD_DIM, TOK), bf16),
        ],
        compiler_params=pltpu.CompilerParams(vmem_limit_bytes=VMEM_LIMIT),
        cost_estimate=pl.CostEstimate(
            flops=2 * TOK * WIDTH * WIDTH, bytes_accessed=8 << 20, transcendentals=0
        ),
    )(*terms, crossed, hidden, normed, chosen, router_t, g, gain, shared)


def shared_grads_kernel(att_ref, branch_ref, normed_ref, logit_ref, scaled_ref, out_ref):
    over_tokens = (((0,), (1,)), ((), ()))
    logit = jnp.concatenate([logit_ref[...], jnp.zeros((96, TOK), bf16)], axis=0)
    ones = (lax.broadcasted_iota(i32, (128, TOK), 0) == EXPERTS).astype(f32).astype(bf16)
    att = att_ref[...].reshape(WIDTH, TOK)
    grads = [
        jnp.dot(att, branch_ref[...], preferred_element_type=f32),
        lax.dot_general(normed_ref[...], logit, over_tokens, preferred_element_type=f32)
        + lax.dot_general(scaled_ref[...], ones, over_tokens, preferred_element_type=f32),
    ]
    for w in range(8):
        for part, at in zip(grads, (slice(0, WIDTH), slice(WIDTH, None))):
            rows = [part[s * 64 + w * 8 : s * 64 + w * 8 + 8] for s in range(16)]
            out_ref[w, :, at] = jnp.concatenate(rows, axis=0).astype(bf16)


def shared_weight_grads(att, branch, normed, logit_grad, scaled):
    return pl.pallas_call(
        shared_grads_kernel,
        out_shape=jax.ShapeDtypeStruct((8, 128, 1152), bf16),
        compiler_params=pltpu.CompilerParams(vmem_limit_bytes=VMEM_LIMIT),
        cost_estimate=pl.CostEstimate(
            flops=2 * TOK * WIDTH * 1280, bytes_accessed=5 << 20, transcendentals=0
        ),
    )(att, branch, normed, logit_grad, scaled)


def local(
    tokens,
    routes,
    cont_lengths,
    norm_attn,
    w_qkv,
    w_out,
    w_router,
    norm_ffn,
    w_gate_up,
    w_down,
    cotangent,
):
    seq_index = lax.axis_index("seq")
    places, blocks = relative_places(seq_index)
    rows = tokens[0]
    query_width = HEADS * HEAD_DIM
    kv_width = KV_HEADS * HEAD_DIM

    position, begin = group_layout(cont_lengths[0])
    begin = begin[None]
    table = rotary_table(position.astype(f32))
    kv_heads = lambda start: jnp.repeat(
        w_qkv[:, start : start + kv_width].reshape(8, KV_HEADS, HEAD_DIM), 2, axis=1
    )
    head_cols = jnp.concatenate(
        [
            w_qkv[:, :query_width].reshape(8, HEADS, HEAD_DIM),
            kv_heads(query_width),
            kv_heads(query_width + kv_width),
            jnp.broadcast_to(norm_attn[:, None, None], (8, HEADS, HEAD_DIM)),
        ],
        axis=2,
    ).transpose(1, 0, 2)
    head_cols = jnp.broadcast_to(head_cols[:, None], (HEADS, 8, 8, 256)).reshape(128, 8, 256)
    head_weights = lax.all_to_all(head_cols, BOTH, 0, 0, tiled=True).reshape(WIDTH, 256)
    gain_attn = head_weights[:, 192].astype(f32)[None]
    head_weights = jnp.where(jnp.arange(256)[None] < 192, head_weights, 0.0).astype(bf16)

    rows_near, rows_across = gather_near(rows)
    rows_near, _, table, head_weights = tie(rows_near, rows_across, table, head_weights)
    rows_near, rows_far = both_cores(rows_near), gather_far(rows_across)

    own_x = lax.axis_index("wshard") % 2
    expert_rows = jnp.concatenate([w_gate_up, w_down], axis=1)
    along_y = lambda t: lax.all_gather(t, "wshard", axis_index_groups=ALONG_Y, axis=0)
    experts, expert_rows = along_y(expert_rows), swap_x(expert_rows)

    qkv = project(places[:8], rows_near, head_weights, gain_attn, table, ())
    shared = jnp.concatenate(
        [w_out, w_router, norm_ffn[:, None], jnp.zeros((8, 95), bf16)], axis=1
    )
    shared, qkv = tie(shared, qkv)
    shared = lax.all_to_all(
        jnp.broadcast_to(shared[None], (128, 8, 1152)), BOTH, 0, 0, tiled=True
    ).reshape(WIDTH, 1152)
    routes_rows = jnp.pad(routes[0].T.astype(bf16), ((0, 8), (0, WIDTH - TOK)))
    upstream_rows = jnp.concatenate([cotangent[0], routes_rows], axis=0)
    rows_far, qkv, upstream_rows, expert_rows = tie(rows_far, qkv, upstream_rows, expert_rows)
    experts = [experts, along_y(expert_rows)]
    rows_far = both_cores(rows_far)
    grad_near = [upstream_rows] + [send(upstream_rows, 0, b) for b in (1, 3, 2)]
    qkv = project(places[8:], rows_far, head_weights, gain_attn, table, (qkv,))

    router_t = shared[:, WIDTH : WIDTH + EXPERTS].T
    gain_ffn = shared[:, WIDTH + EXPERTS].astype(f32)[None]
    attended_head, attended_t, lse = attend(qkv, begin)
    attended_head, shared = tie(attended_head, shared)
    attended = lax.all_to_all(attended_head, "seq", 0, 0, tiled=True)
    attended, grad_near = tie(attended, grad_near)
    grad_near = jnp.stack(grad_near)
    grad_rows = grad_near.reshape(-1, WIDTH)
    grad_far = [send(grad_rows[:EARLY], 1, 0)]
    hidden, normed_ffn = hidden_of(attended, shared, rows, gain_ffn)
    ffn_near, ffn_across = gather_near(normed_ffn)
    grad_rows, _ = tie(grad_rows, ffn_across)
    ffn_near, _, grad_far[0] = tie(ffn_near, ffn_across, grad_far[0])
    grad_far.append(send(grad_rows[EARLY:], 1, 0))
    grad_near = (grad_near, swap_cores(grad_near))
    ffn_near, ffn_far = both_cores(ffn_near), gather_far(ffn_across)
    own = jnp.stack([seq_index * 2, own_x])
    near = run_experts(0, own, ffn_near, grad_near, experts, router_t, ())
    near_terms = sum_along_z(*near[:2])
    ffn_far = both_cores(ffn_far)
    grad_far = jnp.concatenate(grad_far, axis=0).reshape(grad_near[0].shape)
    grad_far = (grad_far, swap_cores(grad_far))
    far = run_experts(1, own, ffn_far, grad_far, experts, router_t, near[2:])
    far, near_terms = tie(far, near_terms)
    moved, saved = far[2:4], far[4:]
    far_other, moved_other = tie(swap_cores(far[1]), moved[1])
    far_terms = send_along_z(chip_parts(far[0], far_other))
    expert_grads = expert_weight_grads(*saved)
    moved_other = swap_cores(moved_other)
    far_terms, expert_grads, moved_other = tie(far_terms, expert_grads, moved_other)
    crossed = send(add_low(*far_terms), 1, 0)
    by_x = [t.reshape(2, 4, TOK, WIDTH) for t in (moved[0], moved_other)]
    moved_parts = [add_low(by_x[0][:, i], by_x[1][:, i]) for i in range(4)]
    crossed, moved_parts = tie(crossed, moved_parts)

    expert_range = jnp.arange(EXPERTS, dtype=i32)
    chosen_here = jnp.any(routes[0].T[None] == expert_range[:, None, None], axis=1).astype(f32)
    hidden_grad, branch_grad, logit_grad, scaled_grad, attended_grad = hidden_back(
        near_terms, crossed, hidden, normed_ffn, chosen_here, router_t, cotangent[0], gain_ffn, shared
    )
    expert_grads = lax.psum_scatter(
        expert_grads.reshape(8, 2, 192, 1024),
        "wshard",
        axis_index_groups=ALONG_Y,
        scatter_dimension=0,
        tiled=True,
    )
    head_grad = lax.all_to_all(attended_grad, "seq", 0, 0, tiled=True)
    shared_grads = shared_weight_grads(attended, branch_grad, normed_ffn, logit_grad, scaled_grad)
    head_grad, shared_grads, moved_parts = tie(head_grad, shared_grads, moved_parts)
    moved_terms = [moved_parts[0]] + [
        send(moved_parts[i], 0, -b) for i, b in ((1, 1), (2, 3), (3, 2))
    ]

    shared_grads = lax.all_to_all(shared_grads, "wshard", 0, 0, tiled=True)
    projected_grad = attend_back(qkv, head_grad, attended_t, lse, begin, table)
    grad_head = head_weight_grad(places, rows_near, rows_far, gain_attn, projected_grad)
    shared_grads, grad_head, projected_grad, moved_terms = tie(
        shared_grads, grad_head, projected_grad, moved_terms
    )
    shared_grads = jnp.sum(shared_grads.astype(f32), axis=0)
    moved_crossed = add_low(*[t[1] for t in moved_terms])
    shared_grads, moved_crossed = tie(shared_grads, moved_crossed)
    moved_crossed = send(moved_crossed, 1, 0)
    far_part = project_back(places[8:], projected_grad, head_weights, shared_grads)
    near_part = project_back(places[:8], projected_grad, head_weights, shared_grads)
    upper, lower = slice(0, TOK // 2), slice(TOK // 2, LAST)
    far_got, near_got = swap_cores(far_part[1]), swap_cores(near_part[1])
    far_upper = add_low(far_part[0][:, upper], far_got[:, upper])
    lower_parts = [
        jnp.stack(
            [
                add_low(near_part[0][i, lower], near_got[i, lower]),
                add_low(far_part[0][i, lower], far_got[i, lower]),
            ]
        )
        for i in range(4)
    ]
    far_upper, lower_parts, grad_head, moved_crossed = tie(
        far_upper, lower_parts, grad_head, moved_crossed
    )
    far_upper = send(far_upper, 1, 0)
    lower_terms = [lower_parts[0]] + [
        send(lower_parts[i], 0, -b) for i, b in ((1, 1), (2, 3), (3, 2))
    ]
    grad_heads = lax.all_to_all(grad_head.reshape(128, 8, 256), BOTH, 0, 0, tiled=True)
    far_upper, lower_terms, expert_grads = tie(far_upper, lower_terms, expert_grads)
    crossed = send(add_low(*[t[1] for t in lower_terms]), 1, 0)
    upper_parts = [
        add_low(near_part[0][i, upper], near_got[i, upper], far_upper[i]) for i in range(4)
    ]
    upper_terms = [upper_parts[0]] + [
        send(upper_parts[i], 0, -b) for i, b in ((1, 1), (2, 3), (3, 2))
    ]
    crossed, grad_heads = tie(crossed, grad_heads)
    kept = lax.dynamic_index_in_dim(expert_grads, own_x, 0, keepdims=False)
    sent = lax.dynamic_index_in_dim(expert_grads, 1 - own_x, 0, keepdims=False)
    expert_grads = kept.astype(f32) + swap_x(sent).astype(f32)
    total = lambda terms: sum([t.astype(f32) for t in terms])
    output = (hidden + total([t[0] for t in moved_terms] + [moved_crossed])).astype(bf16)
    last_sum = jnp.concatenate(
        [total(upper_terms), total([t[0] for t in lower_terms] + [crossed])], axis=0
    )
    normed_grad, shared_grads = last_sum[:TOK], last_sum[TOK:]
    grad_heads = jnp.sum(grad_heads.reshape(16, 8, 8, 256).astype(f32), axis=1).transpose(1, 0, 2)
    kv_sum = lambda start: jnp.sum(
        grad_heads[:, :, start : start + HEAD_DIM].reshape(8, KV_HEADS, 2, HEAD_DIM), axis=2
    ).reshape(8, kv_width)
    grad_qkv = jnp.concatenate(
        [grad_heads[:, :, :HEAD_DIM].reshape(8, query_width), kv_sum(HEAD_DIM), kv_sum(2 * HEAD_DIM)],
        axis=1,
    )
    grad_norm_attn = jnp.sum(grad_qkv * w_qkv.astype(f32), axis=1) / norm_attn.astype(f32)
    inputs = rows.astype(f32)
    grad_input = hidden_grad + rms_pull(inputs, inverse_rms(inputs), gain_attn, normed_grad)
    return (
        output[None],
        grad_input[None],
        grad_norm_attn,
        grad_qkv,
        shared_grads[:8],
        shared_grads[8:, :EXPERTS],
        shared_grads[8:, EXPERTS],
        expert_grads[:, :128],
        expert_grads[:, 128:],
    )


def solution(mesh):
    return jax.shard_map(
        local,
        mesh=mesh,
        in_specs=(
            P("wshard", "seq", None),
            P("wshard", "seq", None),
            P("wshard", None),
            P(BOTH),
            P(BOTH, None),
            P(BOTH, None),
            P(BOTH, None),
            P(BOTH),
            P("seq", "wshard", None),
            P("seq", "wshard", None),
            P("wshard", "seq", None),
        ),
        out_specs=(
            P("wshard", "seq", None),
            P("wshard", "seq", None),
            P(BOTH),
            P(BOTH, None),
            P(BOTH, None),
            P(BOTH, None),
            P(BOTH),
            P("seq", "wshard", None),
            P("seq", "wshard", None),
        ),
        check_vma=False,
    )
```

```python
import jax
import jax.numpy as jnp
from jax import lax
from jax.experimental import pallas as pl
from jax.experimental.pallas import tpu as pltpu
from jax.sharding import PartitionSpec as P

HEADS = 16
KV_HEADS = 8
HEAD_DIM = 64
EXPERTS = 32
FF = 512
PROMPT = 2048
GROUP = 3584
TOK = 224
WIDTH = 1024
SLOTS = 72
STEP_ROWS = 4 * SLOTS
ALL_ROWS = 16 * SLOTS
BLOCK = 512
VMEM_LIMIT = 60 << 20
LAST = TOK + 16
PAY = TOK + 32

norm_eps = 1e-06
rope_base = 10000.0
masked_score = -1e30
BOTH = ("seq", "wshard")
NT = (((1,), (1,)), ((), ()))
TN = (((0,), (0,)), ((), ()))
f32 = jnp.float32
bf16 = jnp.bfloat16
i32 = jnp.int32


def place_of(x, z, core):
    return x * 8 + z * 2 + core


def shift_perm(a, b):
    return [
        (place_of(x, z, c), place_of(x ^ a, (z + b) % 4, c))
        for x in range(2)
        for z in range(4)
        for c in range(2)
    ]


CORE_PERM = [(i, i ^ 1) for i in range(16)]


def send(rows, a, b):
    return lax.ppermute(rows, "seq", shift_perm(a, b))


def swap_cores(rows):
    return lax.ppermute(rows, "seq", CORE_PERM)


def relative_places(seq_index):
    x, z, c = seq_index // 8, (seq_index // 2) % 4, seq_index % 2
    r = jnp.arange(16, dtype=i32)
    a, i, k = r // 8, (r // 2) % 4, r % 2
    shift = i ^ (i // 2)
    behind = (z - i) % 4
    places = (a ^ x) * 8 + ((z - shift) % 4) * 2 + (k ^ c)
    return places, (a ^ x) * 8 + (behind ^ (behind // 2)) * 2 + (k ^ c)


def gather_near(rows):
    return [rows] + [send(rows, 0, b) for b in (1, 3, 2)], send(rows, 1, 0)


def both_cores(parts):
    mine = jnp.stack(parts)
    return mine, swap_cores(mine)


def gather_far(across):
    return [across] + [send(across, 0, b) for b in (1, 3, 2)]


def add_low(*terms):
    return sum([t.astype(f32) for t in terms]).astype(bf16)


def sum_along_z(mine, other):
    return send_along_z(chip_parts(mine, swap_cores(other)))


def chip_parts(mine, got):
    return [add_low(mine[i], got[i]) for i in range(4)]


def send_along_z(parts):
    return [parts[0]] + [send(parts[i], 0, -b) for i, b in ((1, 1), (2, 3), (3, 2))]


def swap_x(rows):
    return lax.ppermute(rows, "wshard", [(w, w ^ 1) for w in range(8)])


ALONG_Y = [[y * 2 + x for y in range(4)] for x in range(2)]


def tie(*values):
    return lax.optimization_barrier(values)


def inverse_rms(values):
    return lax.rsqrt(jnp.mean(values * values, axis=-1, keepdims=True) + norm_eps)


def rms_pull(values, scale, gain, grad):
    scaled = grad * gain
    return scale * scaled - values * (scale * scale * scale) * jnp.mean(
        scaled * values, axis=-1, keepdims=True
    )


def group_layout(lengths):
    places = jnp.arange(GROUP, dtype=i32)
    ends = jnp.cumsum(lengths)
    starts = ends - lengths
    offset_in = places - PROMPT
    segment_id = jnp.sum((offset_in[:, None] >= ends[None, :]).astype(i32), axis=1)
    segment_hot = segment_id[:, None] == jnp.arange(lengths.shape[0], dtype=i32)[None, :]
    begin = jnp.sum(jnp.where(segment_hot, starts[None, :], 0), axis=1)
    inside = offset_in >= 0
    position = jnp.where(inside, PROMPT + offset_in - begin, places)
    return position, jnp.where(inside, PROMPT + begin, 0)


def rotary_table(position):
    half_dim = HEAD_DIM // 2
    inverse = rope_base ** (-((jnp.arange(2 * HEAD_DIM) % half_dim).astype(f32) * 2.0) / HEAD_DIM)
    back = jnp.where(jnp.arange(2 * HEAD_DIM) < HEAD_DIM, 0.0, 0.5 * jnp.pi).astype(f32)
    return jnp.cos(position[:, None] * inverse[None, :] - back[None, :])


def turn(values):
    half_dim = HEAD_DIM // 2
    return jnp.concatenate([-values[:, half_dim:], values[:, :half_dim]], axis=-1)


def turn_back(values):
    half_dim = HEAD_DIM // 2
    return jnp.concatenate([values[:, half_dim:], -values[:, :half_dim]], axis=-1)


def project_kernel(places, mine, other, w, gain, table, *refs):
    out = refs[-1]
    j = pl.program_id(0)

    if len(refs) > 1:

        @pl.when(j == 0)
        def _():
            out[...] = refs[0][...]

    for k, ref in enumerate((mine, other)):
        at = pl.ds(pl.multiple_of(places[2 * j + k] * TOK, TOK), TOK)
        rows = ref[0].astype(f32)
        normed = (rows * inverse_rms(rows) * gain[...]).astype(bf16)
        projected = jnp.dot(normed, w[...], preferred_element_type=f32)
        c, s = table[at, :HEAD_DIM], table[at, HEAD_DIM:]
        q, k, v = projected[:, :64], projected[:, 64:128], projected[:, 128:]
        q = (q * c + turn(q) * s).astype(bf16).astype(f32) * HEAD_DIM**-0.5
        out[at, :] = jnp.concatenate([q, k * c + turn(k) * s, v], axis=1).astype(bf16)


def project(places, gathered, w, gain, table, before):
    chip = pl.BlockSpec((1, TOK, WIDTH), lambda j, p: (j, 0, 0))
    whole = lambda *shape: pl.BlockSpec(shape, lambda j, p: (0,) * len(shape))
    return pl.pallas_call(
        project_kernel,
        grid_spec=pltpu.PrefetchScalarGridSpec(
            num_scalar_prefetch=1,
            grid=(4,),
            in_specs=[chip, chip, whole(WIDTH, 256), whole(1, WIDTH), whole(GROUP, 128)]
            + [whole(GROUP, 256)] * len(before),
            out_specs=whole(GROUP, 256),
        ),
        out_shape=jax.ShapeDtypeStruct((GROUP, 256), bf16),
        compiler_params=pltpu.CompilerParams(vmem_limit_bytes=VMEM_LIMIT),
        cost_estimate=pl.CostEstimate(
            flops=2 * 8 * TOK * WIDTH * 256, bytes_accessed=10 << 20, transcendentals=0
        ),
    )(places, *gathered, w, gain, table, *before)


def project_back_kernel(places, first, second, w, first_shared, second_shared, mine, other):
    del places
    for projected, shared, out in ((first, first_shared, mine), (second, second_shared, other)):
        out[0, :TOK, :] = lax.dot_general(
            projected[...], w[...], NT, preferred_element_type=f32
        ).astype(bf16)
        rest = jnp.concatenate([shared[:, WIDTH:], jnp.zeros((8, WIDTH - 128), f32)], axis=1)
        out[0, TOK:, :] = jnp.concatenate([shared[:, :WIDTH], rest], axis=0).astype(bf16)


def project_back(places, projected_grad, w, shared):
    chip = pl.BlockSpec((1, LAST, WIDTH), lambda j, p: (j, 0, 0))
    at = lambda k, rows, n: pl.BlockSpec((rows, n), lambda j, p: (p[2 * j + k], 0))
    part = jax.ShapeDtypeStruct((4, LAST, WIDTH), bf16)
    return pl.pallas_call(
        project_back_kernel,
        grid_spec=pltpu.PrefetchScalarGridSpec(
            num_scalar_prefetch=1,
            grid=(4,),
            in_specs=[
                at(0, TOK, 256),
                at(1, TOK, 256),
                pl.BlockSpec((WIDTH, 256), lambda j, p: (0, 0)),
                at(0, 8, 1152),
                at(1, 8, 1152),
            ],
            out_specs=[chip, chip],
        ),
        out_shape=[part, part],
        compiler_params=pltpu.CompilerParams(vmem_limit_bytes=VMEM_LIMIT),
        cost_estimate=pl.CostEstimate(
            flops=2 * 8 * TOK * WIDTH * 256, bytes_accessed=5 << 20, transcendentals=0
        ),
    )(places, projected_grad, projected_grad, w, shared, shared)


def head_grad_kernel(places, near_mine, near_other, far_mine, far_other, gain, first, second, out, total):
    del places
    j = pl.program_id(0)

    @pl.when(j == 0)
    def _():
        total[...] = jnp.zeros_like(total)

    for near, far, projected in ((near_mine, far_mine, first), (near_other, far_other, second)):
        rows = jnp.where(j < 4, near[0], far[0]).astype(f32)
        normed = (rows * inverse_rms(rows) * gain[...]).astype(bf16)
        total[...] += lax.dot_general(normed, projected[...], TN, preferred_element_type=f32)

    @pl.when(j == 7)
    def _():
        out[...] = total[...].astype(bf16)


def head_weight_grad(places, near, far, gain, projected_grad):
    near_chip = pl.BlockSpec((1, TOK, WIDTH), lambda j, p: (jnp.minimum(j, 3), 0, 0))
    far_chip = pl.BlockSpec((1, TOK, WIDTH), lambda j, p: (jnp.maximum(j - 4, 0), 0, 0))
    at = lambda k: pl.BlockSpec((TOK, 256), lambda j, p: (p[2 * j + k], 0))
    return pl.pallas_call(
        head_grad_kernel,
        grid_spec=pltpu.PrefetchScalarGridSpec(
            num_scalar_prefetch=1,
            grid=(8,),
            in_specs=[
                near_chip,
                near_chip,
                far_chip,
                far_chip,
                pl.BlockSpec((1, WIDTH), lambda j, p: (0, 0)),
                at(0),
                at(1),
            ],
            out_specs=pl.BlockSpec((WIDTH, 256), lambda j, p: (0, 0)),
            scratch_shapes=[pltpu.VMEM((WIDTH, 256), f32)],
        ),
        out_shape=jax.ShapeDtypeStruct((WIDTH, 256), bf16),
        compiler_params=pltpu.CompilerParams(vmem_limit_bytes=VMEM_LIMIT),
        cost_estimate=pl.CostEstimate(
            flops=2 * 16 * TOK * WIDTH * 256, bytes_accessed=10 << 20, transcendentals=0
        ),
    )(places, *near, *far, gain, projected_grad, projected_grad)


def tile_mask(scores, key_start, query_start, begin):
    keys = key_start + lax.broadcasted_iota(i32, scores.shape, 0)
    queries = query_start + lax.broadcasted_iota(i32, scores.shape, 1)
    return jnp.where((keys <= queries) & (keys >= begin), scores, masked_score)


def key_ranges(i):
    first = PROMPT // BLOCK
    return jnp.where(i > first, i - 1, i), jnp.minimum(i, first)


def attend_kernel(qkv_ref, begin_ref, o_ref, ot_ref, lse_ref, keys, vt):
    i = pl.program_id(0)
    here = pl.ds(pl.multiple_of(i * BLOCK, BLOCK), BLOCK)

    @pl.when(i == 0)
    def _():
        keys[...] = qkv_ref[:, 64:128]
        vt[...] = qkv_ref[:, 128:192].T

    q = qkv_ref[here, :64]
    begin = begin_ref[...]

    def tile(j, carry, masked, n=1):
        peak, total, out = carry
        start = pl.multiple_of(j * BLOCK, BLOCK)
        at = pl.ds(start, n * BLOCK)
        s = lax.dot_general(keys[at, :], q, NT, preferred_element_type=f32)
        if masked:
            s = tile_mask(s, start, i * BLOCK, begin)
        higher = jnp.maximum(peak, jnp.max(s, axis=0, keepdims=True))
        p = jnp.exp(s - higher)
        fade = jnp.exp(peak - higher)
        total = total * fade + jnp.sum(p, axis=0, keepdims=True)
        out = out * fade + jnp.dot(vt[:, at], p.astype(bf16), preferred_element_type=f32)
        return higher, total, out

    carry = (
        jnp.full((1, BLOCK), masked_score, f32),
        jnp.zeros((1, BLOCK), f32),
        jnp.zeros((HEAD_DIM, BLOCK), f32),
    )
    carry = tile(i, carry, True)
    window, shared = key_ranges(i)
    carry = lax.fori_loop(window, i, lambda j, c: tile(j, c, True), carry)
    pairs = shared // 2
    carry = lax.fori_loop(0, pairs, lambda j, c: tile(2 * j, c, False, 2), carry)
    peak, total, out = lax.fori_loop(2 * pairs, shared, lambda j, c: tile(j, c, False), carry)
    ot_ref[:, here] = out * (1.0 / total)
    lse_ref[...] = peak + jnp.log(total)

    @pl.when(i == GROUP // BLOCK - 1)
    def _():
        for b in range(16):
            o_ref[b] = ot_ref[:, b * TOK : (b + 1) * TOK].astype(bf16)


def attend(qkv, begin):
    whole = lambda *shape: pl.BlockSpec(shape, lambda i: (0,) * len(shape))
    cols = lambda n: pl.BlockSpec((n, BLOCK), lambda i: (0, i))
    return pl.pallas_call(
        attend_kernel,
        grid=(GROUP // BLOCK,),
        in_specs=[whole(GROUP, 256), cols(1)],
        out_specs=[whole(16, HEAD_DIM, TOK), whole(HEAD_DIM, GROUP), cols(1)],
        out_shape=[
            jax.ShapeDtypeStruct((16, HEAD_DIM, TOK), bf16),
            jax.ShapeDtypeStruct((HEAD_DIM, GROUP), f32),
            jax.ShapeDtypeStruct((1, GROUP), f32),
        ],
        scratch_shapes=[
            pltpu.VMEM((GROUP, HEAD_DIM), bf16),
            pltpu.VMEM((HEAD_DIM, GROUP), bf16),
        ],
        compiler_params=pltpu.CompilerParams(vmem_limit_bytes=VMEM_LIMIT),
        cost_estimate=pl.CostEstimate(
            flops=2 * 27 * BLOCK * BLOCK * 512, bytes_accessed=4 << 20, transcendentals=27 * BLOCK * BLOCK
        ),
    )(qkv, begin)


def attend_back_kernel(
    qkv_ref, g_ref, ot_ref, lse_ref, begin_ref, table, out_ref, keys, values, kt, gt, dq, dk, dv
):
    i = pl.program_id(0)
    here = pl.ds(pl.multiple_of(i * BLOCK, BLOCK), BLOCK)

    @pl.when(i == 0)
    def _():
        dk[...] = jnp.zeros_like(dk)
        dv[...] = jnp.zeros_like(dv)
        keys[...] = qkv_ref[:, 64:128]
        values[...] = qkv_ref[:, 128:192]
        kt[...] = qkv_ref[:, 64:128].T
        for b in range(16):
            gt[:, b * TOK : (b + 1) * TOK] = g_ref[b]

    q = qkv_ref[here, :64]
    g = gt[:, here]
    begin = begin_ref[...]
    lse = lse_ref[...]
    inner = jnp.sum(g.astype(f32) * ot_ref[...], axis=0, keepdims=True)

    def tile(j, dq, masked, n=1):
        start = pl.multiple_of(j * BLOCK, BLOCK)
        at = pl.ds(start, n * BLOCK)
        s = lax.dot_general(keys[at, :], q, NT, preferred_element_type=f32)
        if masked:
            s = tile_mask(s, start, i * BLOCK, begin)
        p = jnp.exp(s - lse)
        dp = jnp.dot(values[at, :], g, preferred_element_type=f32)
        ds = (p * (dp - inner)).astype(bf16)
        dv[at, :] += lax.dot_general(p.astype(bf16), g, NT, preferred_element_type=f32)
        dk[at, :] += jnp.dot(ds, q, preferred_element_type=f32)
        return dq + jnp.dot(kt[:, at], ds, preferred_element_type=f32)

    dqt = tile(i, jnp.zeros((HEAD_DIM, BLOCK), f32), True)
    window, shared = key_ranges(i)
    dqt = lax.fori_loop(window, i, lambda j, c: tile(j, c, True), dqt)
    pairs = shared // 2
    dqt = lax.fori_loop(0, pairs, lambda j, c: tile(2 * j, c, False, 2), dqt)
    dqt = lax.fori_loop(2 * pairs, shared, lambda j, c: tile(j, c, False), dqt)
    dq[here, :] = dqt.T * HEAD_DIM**-0.5

    @pl.when(i == GROUP // BLOCK - 1)
    def _():
        def back(b, _):
            at = pl.ds(pl.multiple_of(b * BLOCK, BLOCK), BLOCK)
            c, s = table[at, :HEAD_DIM], table[at, HEAD_DIM:]
            q, k = dq[at, :].astype(bf16).astype(f32), dk[at, :].astype(bf16).astype(f32)
            parts = [q * c + turn_back(q * s), k * c + turn_back(k * s), dv[at, :], jnp.zeros_like(q)]
            out_ref[at, :] = jnp.concatenate(parts, axis=1).astype(bf16)
            return 0

        lax.fori_loop(0, GROUP // BLOCK, back, 0)


def attend_back(qkv, g, ot, lse, begin, table):
    whole = lambda *shape: pl.BlockSpec(shape, lambda i: (0,) * len(shape))
    cols = lambda n: pl.BlockSpec((n, BLOCK), lambda i: (0, i))
    return pl.pallas_call(
        attend_back_kernel,
        grid=(GROUP // BLOCK,),
        in_specs=[
            whole(GROUP, 256),
            whole(16, HEAD_DIM, TOK),
            cols(HEAD_DIM),
            cols(1),
            cols(1),
            whole(GROUP, 128),
        ],
        out_specs=whole(GROUP, 256),
        out_shape=jax.ShapeDtypeStruct((GROUP, 256), bf16),
        scratch_shapes=[
            pltpu.VMEM((GROUP, HEAD_DIM), bf16),
            pltpu.VMEM((GROUP, HEAD_DIM), bf16),
            pltpu.VMEM((HEAD_DIM, GROUP), bf16),
            pltpu.VMEM((HEAD_DIM, GROUP), bf16),
            pltpu.VMEM((GROUP, HEAD_DIM), f32),
            pltpu.VMEM((GROUP, HEAD_DIM), f32),
            pltpu.VMEM((GROUP, HEAD_DIM), f32),
        ],
        compiler_params=pltpu.CompilerParams(vmem_limit_bytes=VMEM_LIMIT),
        cost_estimate=pl.CostEstimate(
            flops=5 * 27 * BLOCK * BLOCK * 512, bytes_accessed=8 << 20, transcendentals=27 * BLOCK * BLOCK
        ),
    )(qkv, g, ot, lse, begin, table)


def experts_kernel(
    own_ref, ffn_mine, ffn_other, g_mine, g_other, routes_mine, routes_other, router_ref, own_w, across_w, *refs
):
    routed_mine, routed_other, moved_mine, moved_other = refs[-10:-6]
    x_ref, dh_ref, act_ref, dy_ref, w_ref, sem = refs[-6:]
    own = own_ref[0]

    copies = [
        [
            pltpu.make_async_copy(shards.at[y, e], w_ref.at[e, 2 * y + (own_ref[1] ^ a)], sem.at[a, y, e])
            for a, shards in enumerate((own_w, across_w))
            for y in range(4)
        ]
        for e in range(2)
    ]

    @pl.when(pl.program_id(0) == 0)
    def _():
        for copy in copies[0] + copies[1]:
            copy.start()

    expert_rows = lax.broadcasted_iota(i32, (EXPERTS, TOK), 0)
    slot_rows = lax.broadcasted_iota(i32, (SLOTS, TOK), 0).astype(f32)
    upto = (
        lax.broadcasted_iota(i32, (TOK, TOK), 0) <= lax.broadcasted_iota(i32, (TOK, TOK), 1)
    ).astype(f32).astype(bf16)
    slot_cols = []
    gate_grads = [jnp.zeros((EXPERTS, WIDTH), f32) for _ in range(4)]
    payload_rows = lax.broadcasted_iota(i32, (EXPERTS, WIDTH), 0)
    gate_rows = [[], []]
    picks = [[], []]
    picked_rows = [[], []]
    picked_grads = [[], []]
    blocks = [(ffn_mine, g_mine, routes_mine, 0), (ffn_other, g_other, routes_other, 0)]
    blocks = blocks + [(*refs_of[:3], 1) for refs_of in blocks]
    for rows_ref, grads_ref, routes_ref, n in blocks:
        rows, grads = rows_ref[n], grads_ref[n]
        routes = routes_ref[n][:8, :TOK].astype(f32).astype(i32)
        chosen = expert_rows == routes[0:1]
        for j in range(1, 8):
            chosen = chosen | (expert_rows == routes[j : j + 1])
        named = [jnp.max((routes == own + e).astype(f32), axis=0, keepdims=True) for e in range(2)]
        named = jnp.concatenate(named + [jnp.zeros((6, TOK), f32)], axis=0)
        rank = jnp.dot(named.astype(bf16), upto, preferred_element_type=f32)
        slots = jnp.where(named > 0, rank - 1.0, -1.0)
        slot_cols.append(slots.T)
        logits = lax.dot_general(router_ref[...], rows, NT, preferred_element_type=f32)
        peak = jnp.max(jnp.where(chosen, logits, masked_score), axis=0, keepdims=True)
        raised = jnp.where(chosen, jnp.exp(jnp.minimum(logits - peak, 0.0)), 0.0)
        gates = raised / jnp.sum(raised, axis=0, keepdims=True)
        for e in range(2):
            gate_rows[e].append(
                jnp.sum(jnp.where(expert_rows == own + e, gates, 0.0), axis=0, keepdims=True)
            )
            picks[e].append((slots[e : e + 1] == slot_rows).astype(f32))
        low = jnp.concatenate([picks[0][-1], picks[1][-1]], axis=0).astype(bf16)
        for source, kept in ((rows, picked_rows), (grads, picked_grads)):
            both = jnp.dot(low, source, preferred_element_type=f32)
            kept[0].append(both[:SLOTS])
            kept[1].append(both[SLOTS:])
    moved, routed = [], []
    for e in range(2):

        @pl.when(pl.program_id(0) == 0)
        def _():
            for copy in copies[e]:
                copy.wait()

        w_gate_up = w_ref[e, :, :128, :].reshape(WIDTH, 2 * FF)
        w_down = w_ref[e, :, 128:, :].reshape(FF, WIDTH)
        x = jnp.concatenate(picked_rows[e], axis=0).astype(bf16)
        gate = jnp.concatenate(
            [jnp.sum(p * r, axis=1, keepdims=True) for p, r in zip(picks[e], gate_rows[e])], axis=0
        )
        grads = jnp.concatenate(picked_grads[e], axis=0)
        dy = (gate * grads).astype(bf16)
        mixed = jnp.dot(x, w_gate_up, preferred_element_type=f32)
        dact = lax.dot_general(dy, w_down, NT, preferred_element_type=f32)
        gate_part, up_part = mixed[:, :FF], mixed[:, FF:]
        sigma = 1.0 / (1.0 + jnp.exp(-gate_part))
        silu = gate_part * sigma
        act = (silu * up_part).astype(bf16)
        dh = jnp.concatenate(
            [dact * up_part * (sigma + silu * (1.0 - sigma)), dact * silu], axis=1
        ).astype(bf16)
        x_ref[e] = x
        dy_ref[e] = dy
        act_ref[e] = act
        dh_ref[e] = dh
        returned = jnp.dot(act, w_down, preferred_element_type=f32).astype(bf16).astype(f32)
        dgate = jnp.sum(returned * grads, axis=1, keepdims=True)
        for b in range(4):
            grad = jnp.sum(
                picks[e][b] * dgate[b * SLOTS : (b + 1) * SLOTS], axis=0, keepdims=True
            )
            high = grad.astype(bf16).astype(f32)
            gap = jnp.zeros((1, 256 - TOK), f32)
            wide = jnp.concatenate([high, gap, grad - high, gap, jnp.zeros((1, WIDTH - 512), f32)], axis=1)
            gate_grads[b] = gate_grads[b] + jnp.where(payload_rows == own + e, wide, 0.0)
        moved.append(gate * returned)
        routed.append(lax.dot_general(dh, w_gate_up, NT, preferred_element_type=f32))
    columns = lax.broadcasted_iota(i32, (TOK, 2 * SLOTS), 1).astype(f32)
    outs = [(routed_mine, moved_mine, 0), (routed_other, moved_other, 0), (routed_mine, moved_mine, 1), (routed_other, moved_other, 1)]
    for b, (routed_ref, moved_ref, n) in enumerate(outs):
        first, second = slot_cols[b][:, 0:1], slot_cols[b][:, 1:2]
        back = ((columns == first) | ((columns == second + SLOTS) & (second >= 0))).astype(f32).astype(bf16)
        at = slice(b * SLOTS, (b + 1) * SLOTS)
        for terms, ref in ((routed, routed_ref), (moved, moved_ref)):
            joined = jnp.concatenate([terms[0][at], terms[1][at]], axis=0).astype(bf16)
            ref[n, :TOK, :] = jnp.dot(back, joined, preferred_element_type=f32).astype(bf16)
        routed_ref[n, TOK:, :] = gate_grads[b].astype(bf16)


def run_experts(half, own, ffn, grads, weights, router, before):
    pair = pl.BlockSpec((2, TOK, WIDTH), lambda i, o: (i, 0, 0))
    pair_of_all = pl.BlockSpec((2, TOK, WIDTH), lambda i, o: (i + 2 * half, 0, 0))
    whole = lambda shape: pl.BlockSpec(shape, lambda i, o: (0,) * len(shape))
    routes = pl.BlockSpec((2, 16, 256), lambda i, o: (i, TOK // 16, 0))
    summed = pl.BlockSpec((2, PAY, WIDTH), lambda i, o: (i, 0, 0))
    kept = lambda n: pl.BlockSpec((2, STEP_ROWS, n), lambda i, o: (0, i + 2 * half, 0))
    part = jax.ShapeDtypeStruct((4, PAY, WIDTH), bf16)
    keep = lambda n: jax.ShapeDtypeStruct((2, ALL_ROWS, n), bf16)
    return pl.pallas_call(
        experts_kernel,
        grid_spec=pltpu.PrefetchScalarGridSpec(
            num_scalar_prefetch=1,
            grid=(2,),
            in_specs=[
                pair,
                pair,
                pair,
                pair,
                routes,
                routes,
                whole((EXPERTS, WIDTH)),
            ]
            + [pl.BlockSpec(memory_space=pl.ANY)] * (2 + len(before)),
            out_specs=[
                summed,
                summed,
                pair_of_all,
                pair_of_all,
                kept(WIDTH),
                kept(2 * FF),
                kept(FF),
                kept(WIDTH),
            ],
            scratch_shapes=[
                pltpu.VMEM((2, 8, 192, 1024), bf16),
                pltpu.SemaphoreType.DMA((2, 4, 2)),
            ],
        ),
        out_shape=[
            part,
            part,
            jax.ShapeDtypeStruct((8, TOK, WIDTH), bf16),
            jax.ShapeDtypeStruct((8, TOK, WIDTH), bf16),
            keep(WIDTH),
            keep(2 * FF),
            keep(FF),
            keep(WIDTH),
        ],
        input_output_aliases={10 + i: 2 + i for i in range(len(before))},
        compiler_params=pltpu.CompilerParams(vmem_limit_bytes=VMEM_LIMIT),
        cost_estimate=pl.CostEstimate(
            flops=14 << 30, bytes_accessed=24 << 20, transcendentals=8 * SLOTS * 2 * FF
        ),
    )(own, *ffn, *grads, *grads, router, *weights, *before)


def expert_grads_kernel(x_ref, dh_ref, act_ref, dy_ref, out_ref):
    up = lax.dot_general(x_ref[0], dh_ref[0], TN, preferred_element_type=f32)
    down = lax.dot_general(act_ref[0], dy_ref[0], TN, preferred_element_type=f32)
    out_ref[0, :, 0, :128, :] = up.astype(bf16).reshape(2, 128, 2 * FF)
    out_ref[0, :, 0, 128:, :] = down.astype(bf16).reshape(2, 64, WIDTH)


def expert_weight_grads(x, dh, act, dy):
    return pl.pallas_call(
        expert_grads_kernel,
        grid=(2, 4),
        in_specs=[
            pl.BlockSpec((1, ALL_ROWS, 256), lambda e, i: (e, 0, i)),
            pl.BlockSpec((1, ALL_ROWS, 2 * FF), lambda e, i: (e, 0, 0)),
            pl.BlockSpec((1, ALL_ROWS, 128), lambda e, i: (e, 0, i)),
            pl.BlockSpec((1, ALL_ROWS, WIDTH), lambda e, i: (e, 0, 0)),
        ],
        out_specs=pl.BlockSpec((1, 2, 1, 192, 1024), lambda e, i: (i, 0, e, 0, 0)),
        out_shape=jax.ShapeDtypeStruct((4, 2, 2, 192, 1024), bf16),
        compiler_params=pltpu.CompilerParams(vmem_limit_bytes=VMEM_LIMIT),
        cost_estimate=pl.CostEstimate(flops=8 << 30, bytes_accessed=14 << 20, transcendentals=0),
    )(x, dh, act, dy)


def hidden_kernel(att_ref, w_ref, rows_ref, gain_ref, hidden_ref, normed_ref):
    att = att_ref[...].reshape(WIDTH, TOK)
    hidden = rows_ref[...].astype(f32) + lax.dot_general(
        att, w_ref[:, :WIDTH], TN, preferred_element_type=f32
    )
    hidden_ref[...] = hidden
    normed_ref[...] = (hidden * inverse_rms(hidden) * gain_ref[...]).astype(bf16)


def hidden_of(attended, shared, rows, gain):
    return pl.pallas_call(
        hidden_kernel,
        out_shape=[
            jax.ShapeDtypeStruct((TOK, WIDTH), f32),
            jax.ShapeDtypeStruct((TOK, WIDTH), bf16),
        ],
        compiler_params=pltpu.CompilerParams(vmem_limit_bytes=VMEM_LIMIT),
        cost_estimate=pl.CostEstimate(
            flops=2 * TOK * WIDTH * WIDTH, bytes_accessed=5 << 20, transcendentals=0
        ),
    )(attended, shared, rows, gain)


def hidden_back_kernel(
    t0, t1, t2, t3, crossed, hidden_ref, normed_ref, chosen_ref, router_ref, g_ref, gain_ref,
    w_ref, hidden_grad_ref, branch_ref, logit_ref, scaled_ref, att_ref
):
    chosen = chosen_ref[...] > 0
    logits = lax.dot_general(router_ref[...], normed_ref[...], NT, preferred_element_type=f32)
    peak = jnp.max(jnp.where(chosen, logits, masked_score), axis=0, keepdims=True)
    raised = jnp.where(chosen, jnp.exp(jnp.minimum(logits - peak, 0.0)), 0.0)
    gates = raised / jnp.sum(raised, axis=0, keepdims=True)
    summed = t0[...].astype(f32)
    for term in (t1, t2, t3, crossed):
        summed = summed + term[...].astype(f32)
    gate_grad = summed[TOK:, :TOK] + summed[TOK:, 256 : 256 + TOK]
    logit_grad = gates * (gate_grad - jnp.sum(gates * gate_grad, axis=0, keepdims=True))
    logit_grad = logit_grad.astype(bf16)
    logit_ref[...] = logit_grad
    normed_grad = summed[:TOK] + lax.dot_general(
        logit_grad, router_ref[...], TN, preferred_element_type=f32
    )
    hidden = hidden_ref[...]
    scale = inverse_rms(hidden)
    scaled_ref[...] = (normed_grad * hidden * scale).astype(bf16)
    hidden_grad = g_ref[...].astype(f32) + rms_pull(hidden, scale, gain_ref[...], normed_grad)
    hidden_grad_ref[...] = hidden_grad
    branch = hidden_grad.astype(bf16)
    branch_ref[...] = branch
    att = lax.dot_general(w_ref[:, :WIDTH], branch, NT, preferred_element_type=f32)
    att_ref[...] = att.astype(bf16).reshape(HEADS, HEAD_DIM, TOK)


def hidden_back(terms, crossed, hidden, normed, chosen, router_t, g, gain, shared):
    wide = lambda t: jax.ShapeDtypeStruct((TOK, WIDTH), t)
    return pl.pallas_call(
        hidden_back_kernel,
        out_shape=[
            wide(f32),
            wide(bf16),
            jax.ShapeDtypeStruct((EXPERTS, TOK), bf16),
            wide(bf16),
            jax.ShapeDtypeStruct((HEADS, HEAD_DIM, TOK), bf16),
        ],
        compiler_params=pltpu.CompilerParams(vmem_limit_bytes=VMEM_LIMIT),
        cost_estimate=pl.CostEstimate(
            flops=2 * TOK * WIDTH * WIDTH, bytes_accessed=8 << 20, transcendentals=0
        ),
    )(*terms, crossed, hidden, normed, chosen, router_t, g, gain, shared)


def shared_grads_kernel(att_ref, branch_ref, normed_ref, logit_ref, scaled_ref, out_ref):
    over_tokens = (((0,), (1,)), ((), ()))
    logit = jnp.concatenate([logit_ref[...], jnp.zeros((96, TOK), bf16)], axis=0)
    ones = (lax.broadcasted_iota(i32, (128, TOK), 0) == EXPERTS).astype(f32).astype(bf16)
    att = att_ref[...].reshape(WIDTH, TOK)
    grads = [
        jnp.dot(att, branch_ref[...], preferred_element_type=f32),
        lax.dot_general(normed_ref[...], logit, over_tokens, preferred_element_type=f32)
        + lax.dot_general(scaled_ref[...], ones, over_tokens, preferred_element_type=f32),
    ]
    for w in range(8):
        for part, at in zip(grads, (slice(0, WIDTH), slice(WIDTH, None))):
            rows = [part[s * 64 + w * 8 : s * 64 + w * 8 + 8] for s in range(16)]
            out_ref[w, :, at] = jnp.concatenate(rows, axis=0).astype(bf16)


def shared_weight_grads(att, branch, normed, logit_grad, scaled):
    return pl.pallas_call(
        shared_grads_kernel,
        out_shape=jax.ShapeDtypeStruct((8, 128, 1152), bf16),
        compiler_params=pltpu.CompilerParams(vmem_limit_bytes=VMEM_LIMIT),
        cost_estimate=pl.CostEstimate(
            flops=2 * TOK * WIDTH * 1280, bytes_accessed=5 << 20, transcendentals=0
        ),
    )(att, branch, normed, logit_grad, scaled)


def local(
    tokens,
    routes,
    cont_lengths,
    norm_attn,
    w_qkv,
    w_out,
    w_router,
    norm_ffn,
    w_gate_up,
    w_down,
    cotangent,
):
    seq_index = lax.axis_index("seq")
    places, blocks = relative_places(seq_index)
    rows = tokens[0]
    query_width = HEADS * HEAD_DIM
    kv_width = KV_HEADS * HEAD_DIM

    position, begin = group_layout(cont_lengths[0])
    begin = begin[None]
    table = rotary_table(position.astype(f32))
    kv_heads = lambda start: jnp.repeat(
        w_qkv[:, start : start + kv_width].reshape(8, KV_HEADS, HEAD_DIM), 2, axis=1
    )
    head_cols = jnp.concatenate(
        [
            w_qkv[:, :query_width].reshape(8, HEADS, HEAD_DIM),
            kv_heads(query_width),
            kv_heads(query_width + kv_width),
            jnp.broadcast_to(norm_attn[:, None, None], (8, HEADS, HEAD_DIM)),
        ],
        axis=2,
    ).transpose(1, 0, 2)
    head_cols = jnp.broadcast_to(head_cols[:, None], (HEADS, 8, 8, 256)).reshape(128, 8, 256)
    head_weights = lax.all_to_all(head_cols, BOTH, 0, 0, tiled=True).reshape(WIDTH, 256)
    gain_attn = head_weights[:, 192].astype(f32)[None]
    head_weights = jnp.where(jnp.arange(256)[None] < 192, head_weights, 0.0).astype(bf16)

    rows_near, rows_across = gather_near(rows)
    rows_near, _, table, head_weights = tie(rows_near, rows_across, table, head_weights)
    rows_near, rows_far = both_cores(rows_near), gather_far(rows_across)

    own_x = lax.axis_index("wshard") % 2
    expert_rows = jnp.concatenate([w_gate_up, w_down], axis=1)
    along_y = lambda t: lax.all_gather(t, "wshard", axis_index_groups=ALONG_Y, axis=0)
    experts, expert_rows = along_y(expert_rows), swap_x(expert_rows)

    qkv = project(places[:8], rows_near, head_weights, gain_attn, table, ())
    shared = jnp.concatenate(
        [w_out, w_router, norm_ffn[:, None], jnp.zeros((8, 95), bf16)], axis=1
    )
    shared, qkv = tie(shared, qkv)
    shared = lax.all_to_all(
        jnp.broadcast_to(shared[None], (128, 8, 1152)), BOTH, 0, 0, tiled=True
    ).reshape(WIDTH, 1152)
    routes_rows = jnp.pad(routes[0].T.astype(bf16), ((0, 8), (0, WIDTH - TOK)))
    upstream_rows = jnp.concatenate([cotangent[0], routes_rows], axis=0)
    rows_far, qkv, upstream_rows, expert_rows = tie(rows_far, qkv, upstream_rows, expert_rows)
    experts = [experts, along_y(expert_rows)]
    rows_far = both_cores(rows_far)
    grad_near = [upstream_rows] + [send(upstream_rows, 0, b) for b in (1, 3, 2)]
    qkv = project(places[8:], rows_far, head_weights, gain_attn, table, (qkv,))

    router_t = shared[:, WIDTH : WIDTH + EXPERTS].T
    gain_ffn = shared[:, WIDTH + EXPERTS].astype(f32)[None]
    attended_head, attended_t, lse = attend(qkv, begin)
    attended_head, shared = tie(attended_head, shared)
    attended = lax.all_to_all(attended_head, "seq", 0, 0, tiled=True)
    attended, grad_near = tie(attended, grad_near)
    grad_near = jnp.stack(grad_near)
    grad_far = [send(grad_near[:2], 1, 0)]
    hidden, normed_ffn = hidden_of(attended, shared, rows, gain_ffn)
    ffn_near, ffn_across = gather_near(normed_ffn)
    grad_near_mine, _ = tie(grad_near, ffn_across)
    ffn_near, _, grad_far[0] = tie(ffn_near, ffn_across, grad_far[0])
    grad_far.append(send(grad_near_mine[2:], 1, 0))
    grad_near = (grad_near, swap_cores(grad_near))
    ffn_near, ffn_far = both_cores(ffn_near), gather_far(ffn_across)
    own = jnp.stack([seq_index * 2, own_x])
    near = run_experts(0, own, ffn_near, grad_near, experts, router_t, ())
    near_terms = sum_along_z(*near[:2])
    ffn_far = both_cores(ffn_far)
    grad_far = jnp.concatenate(grad_far, axis=0)
    grad_far = (grad_far, swap_cores(grad_far))
    far = run_experts(1, own, ffn_far, grad_far, experts, router_t, near[2:])
    far, near_terms = tie(far, near_terms)
    moved, saved = far[2:4], far[4:]
    far_other, moved_other = tie(swap_cores(far[1]), moved[1])
    far_terms = send_along_z(chip_parts(far[0], far_other))
    expert_grads = expert_weight_grads(*saved)
    moved_other = swap_cores(moved_other)
    far_terms, expert_grads, moved_other = tie(far_terms, expert_grads, moved_other)
    crossed = send(add_low(*far_terms), 1, 0)
    by_x = [t.reshape(2, 4, TOK, WIDTH) for t in (moved[0], moved_other)]
    moved_parts = [add_low(by_x[0][:, i], by_x[1][:, i]) for i in range(4)]
    crossed, moved_parts = tie(crossed, moved_parts)

    expert_range = jnp.arange(EXPERTS, dtype=i32)
    chosen_here = jnp.any(routes[0].T[None] == expert_range[:, None, None], axis=1).astype(f32)
    hidden_grad, branch_grad, logit_grad, scaled_grad, attended_grad = hidden_back(
        near_terms, crossed, hidden, normed_ffn, chosen_here, router_t, cotangent[0], gain_ffn, shared
    )
    expert_grads = lax.psum_scatter(
        expert_grads.reshape(8, 2, 192, 1024),
        "wshard",
        axis_index_groups=ALONG_Y,
        scatter_dimension=0,
        tiled=True,
    )
    head_grad = lax.all_to_all(attended_grad, "seq", 0, 0, tiled=True)
    shared_grads = shared_weight_grads(attended, branch_grad, normed_ffn, logit_grad, scaled_grad)
    head_grad, shared_grads, moved_parts = tie(head_grad, shared_grads, moved_parts)
    moved_terms = [moved_parts[0]] + [
        send(moved_parts[i], 0, -b) for i, b in ((1, 1), (2, 3), (3, 2))
    ]

    shared_grads = lax.all_to_all(shared_grads, "wshard", 0, 0, tiled=True)
    projected_grad = attend_back(qkv, head_grad, attended_t, lse, begin, table)
    shared_grads = jnp.sum(shared_grads.astype(f32), axis=0)
    far_part = project_back(places[8:], projected_grad, head_weights, shared_grads)
    near_part = project_back(places[:8], projected_grad, head_weights, shared_grads)
    far_parts = chip_parts(far_part[0], swap_cores(far_part[1]))
    near_part, moved_terms = tie(near_part, moved_terms)
    near_parts = chip_parts(near_part[0], swap_cores(near_part[1]))
    far_parts, near_parts, projected_grad, moved_terms = tie(
        far_parts, near_parts, projected_grad, moved_terms
    )
    far_terms, expert_grads = tie(send_along_z(far_parts), expert_grads)
    near_terms = send_along_z(near_parts)
    moved_crossed = send(add_low(*[t[1] for t in moved_terms]), 1, 0)
    grad_head = head_weight_grad(places, rows_near, rows_far, gain_attn, projected_grad)
    grad_heads = lax.all_to_all(grad_head.reshape(128, 8, 256), BOTH, 0, 0, tiled=True)
    crossed = send(add_low(*far_terms), 1, 0)
    crossed, near_terms, grad_heads = tie(crossed, near_terms, grad_heads)
    kept = lax.dynamic_index_in_dim(expert_grads, own_x, 0, keepdims=False)
    sent = lax.dynamic_index_in_dim(expert_grads, 1 - own_x, 0, keepdims=False)
    expert_grads = kept.astype(f32) + swap_x(sent).astype(f32)
    total = lambda terms: sum([t.astype(f32) for t in terms])
    output = (hidden + total([t[0] for t in moved_terms] + [moved_crossed])).astype(bf16)
    last_sum = total(near_terms + [crossed])
    normed_grad, shared_grads = last_sum[:TOK], last_sum[TOK:]
    grad_heads = jnp.sum(grad_heads.reshape(16, 8, 8, 256).astype(f32), axis=1).transpose(1, 0, 2)
    kv_sum = lambda start: jnp.sum(
        grad_heads[:, :, start : start + HEAD_DIM].reshape(8, KV_HEADS, 2, HEAD_DIM), axis=2
    ).reshape(8, kv_width)
    grad_qkv = jnp.concatenate(
        [grad_heads[:, :, :HEAD_DIM].reshape(8, query_width), kv_sum(HEAD_DIM), kv_sum(2 * HEAD_DIM)],
        axis=1,
    )
    grad_norm_attn = jnp.sum(grad_qkv * w_qkv.astype(f32), axis=1) / norm_attn.astype(f32)
    inputs = rows.astype(f32)
    grad_input = hidden_grad + rms_pull(inputs, inverse_rms(inputs), gain_attn, normed_grad)
    return (
        output[None],
        grad_input[None],
        grad_norm_attn,
        grad_qkv,
        shared_grads[:8],
        shared_grads[8:, :EXPERTS],
        shared_grads[8:, EXPERTS],
        expert_grads[:, :128],
        expert_grads[:, 128:],
    )


def solution(mesh):
    return jax.shard_map(
        local,
        mesh=mesh,
        in_specs=(
            P("wshard", "seq", None),
            P("wshard", "seq", None),
            P("wshard", None),
            P(BOTH),
            P(BOTH, None),
            P(BOTH, None),
            P(BOTH, None),
            P(BOTH),
            P("seq", "wshard", None),
            P("seq", "wshard", None),
            P("wshard", "seq", None),
        ),
        out_specs=(
            P("wshard", "seq", None),
            P("wshard", "seq", None),
            P(BOTH),
            P(BOTH, None),
            P(BOTH, None),
            P(BOTH, None),
            P(BOTH),
            P("seq", "wshard", None),
            P("seq", "wshard", None),
        ),
        check_vma=False,
    )
```
